32 devices in a mesh: section: 2 (over core), dp: 4 (over z), tensor: 4 (over y, x).
Axes of the slice: x: 2, y: 2, z: 4, core: 2. Of those that a mesh axis runs over, the one named last changes fastest.
Arguments:
- hidden: bfloat16 [2, 2, 4, 1024, 768], P('section', None, 'dp', 'tensor'), may hold values from -6 to 6
- cotangent: bfloat16 [2, 2, 4, 1024, 768], P('section', None, 'dp', 'tensor'), may hold values from -6 to 6
- segments: int32 [2, 2, 4, 1024], P(None, None, 'dp'), may hold values from 0 to 7, as said below
- sa_qkv: bfloat16 [2, 768, 3, 768], P('section', 'dp', None, 'tensor'), may hold values from -0.21875 to 0.21875
- sa_out: bfloat16 [2, 768, 768], P('section', 'dp', 'tensor'), may hold values from -1.75 to 1.75
- cross_one: bfloat16 [2, 768, 768], P('section', 'dp', 'tensor'), may hold values from -0.21875 to 0.21875
- cross_two: bfloat16 [2, 768, 768], P('section', 'dp', 'tensor'), may hold values from -0.625 to 0.625
- ffn_in: bfloat16 [2, 768, 3072], P('section', 'dp', 'tensor'), may hold values from -0.21875 to 0.21875
- ffn_out: bfloat16 [2, 3072, 768], P('section', 'tensor', 'dp'), may hold values from -0.109375 to 0.109375
- norm_gain: float32 [2, 3, 768], P('section'), may hold values from 0.5 to 1.5
- norm_bias: float32 [2, 3, 768], P('section'), may hold values from -1.2 to 1.2
Outputs:
- hidden_out: bfloat16 [2, 2, 4, 1024, 768], P('section', None, 'dp', 'tensor')
- hidden_grad: float32 [2, 2, 4, 1024, 768], P('section', None, 'dp', 'tensor')
- grad_sa_qkv: float32 [2, 768, 3, 768], P('section', 'dp', None, 'tensor')
- grad_sa_out: float32 [2, 768, 768], P('section', 'dp', 'tensor')
- grad_cross_one: float32 [2, 768, 768], P('section', 'dp', 'tensor')
- grad_cross_two: float32 [2, 768, 768], P('section', 'dp', 'tensor')
- grad_ffn_in: float32 [2, 768, 3072], P('section', 'dp', 'tensor')
- grad_ffn_out: float32 [2, 3072, 768], P('section', 'tensor', 'dp')
- grad_norm_gain: float32 [2, 3, 768], P('section', None, ('dp', 'tensor'))
- grad_norm_bias: float32 [2, 3, 768], P('section', None, ('dp', 'tensor'))
The draws below stay inside these ranges and needn't reach their ends.
Inputs may be any that keep to these rules, and one draw needn't show every extreme that they name: Ids in each row start at 0 and rise by one at each of 7 boundaries, so every row holds all 8 segments, and target segment j pairs with source segment j; no boundary lies between positions 256 and 768 inclusive.
All inputs are finite; a program needn't handle non-finite values.
Results may differ from the reference program's by a relative error of at most 0.028.
Values may be sent and summed in bfloat16 or wider, within the bound.
No kernel may reach another device: no remote copies, remote signals or barrier semaphores. Data moves between devices by JAX's collectives and lax.ppermute only.
A program may use at most 256 MiB of HBM per device.

```python
import jax
import jax.numpy as jnp
from jax import lax

D = 768
HDIM = 64
FF = 3072
SEQ = 1024
SEGS = 8
MICRO = 2
ROWS = 4


def draw_segments(key, part):
    key = jax.random.fold_in(key, 7)
    row_total = 2 * MICRO * ROWS
    places = jnp.arange(1, SEQ, dtype=jnp.int32)
    allowed = jnp.logical_or(places <= SEQ // 4 - 1, places >= 3 * SEQ // 4 + 1)
    scores = jax.random.randint(key, (row_total, SEQ - 1), 0, 1 << 20, dtype=jnp.int32) * SEQ + places[None, :]
    scores = jnp.where(allowed[None, :], scores, -1)
    _, picked = lax.top_k(scores, SEGS - 1)
    marks = jnp.sum(jax.nn.one_hot(picked, SEQ - 1, dtype=jnp.int32), axis=1)
    rising = jnp.cumsum(marks, axis=1, dtype=jnp.int32)
    segment_ids = jnp.concatenate([jnp.zeros((row_total, 1), jnp.int32), rising], axis=1)
    return segment_ids.reshape(2, MICRO, ROWS, SEQ)


def shard_levels(key, dims, cuts, least, top_value):
    loudness, own = 1.0, jax.random.fold_in(key, 6)
    for axis_at, shards_of in cuts:
        steps = jnp.exp(jax.random.uniform(jax.random.fold_in(own, axis_at), (shards_of,), jnp.float32, least / len(cuts), top_value / len(cuts)))
        loudness = loudness * jnp.repeat(steps, dims[axis_at] // shards_of).reshape([-1 if axis == axis_at else 1 for axis in range(len(dims))])
    return loudness


def bell_draw(stream_key, dims, deviation, most, split=(), kind=jnp.bfloat16):
    entries = jax.random.normal(stream_key, dims, jnp.float32) * deviation
    if len(split) > 0:
        entries = shard_levels(stream_key, dims, split, -0.22, 0.18) * entries
    return jnp.clip(entries, min=-most, max=most).astype(kind)


def setup_inputs(seed: int = 0) -> dict:
    seeds = jax.random.split(jax.random.key(seed), 12)
    hidden = bell_draw(seeds[0], (2, MICRO, ROWS, SEQ, D), 1.0, 6.0, ((0, 2), (2, 4), (3, 4)))
    cotangent = bell_draw(seeds[1], (2, MICRO, ROWS, SEQ, D), 1.0, 6.0, ((0, 2), (2, 4), (3, 4)))
    segments = draw_segments(jax.random.fold_in(seeds[11], 71), 0)
    sa_qkv = bell_draw(seeds[3], (2, D, 3, D), D ** -0.5, 0.21875, ((0, 2), (1, 4), (3, 4)))
    sa_out = bell_draw(seeds[4], (2, D, D), (D // 64) ** -0.5, 1.75, ((0, 2), (1, 4), (2, 4)))
    cross_one = bell_draw(seeds[5], (2, D, D), D ** -0.5, 0.21875, ((0, 2), (1, 4), (2, 4)))
    cross_two = bell_draw(seeds[6], (2, D, D), (D // 8) ** -0.5, 0.625, ((0, 2), (1, 4), (2, 4)))
    ffn_in = bell_draw(seeds[7], (2, D, FF), D ** -0.5, 0.21875, ((0, 2), (1, 4), (2, 4)))
    ffn_out = bell_draw(seeds[8], (2, FF, D), FF ** -0.5, 0.109375, ((0, 2), (1, 4), (2, 4)))
    norm_gain = jnp.clip(1.0 + 0.1 * jax.random.normal(seeds[9], (2, 3, D), jnp.float32), 0.5, 1.5)
    norm_bias = bell_draw(seeds[10], (2, 3, D), 0.2, 1.2, ((0, 2),), jnp.float32)
    return {"hidden": hidden, "cotangent": cotangent, "segments": segments, "sa_qkv": sa_qkv, "sa_out": sa_out, "cross_one": cross_one, "cross_two": cross_two, "ffn_in": ffn_in, "ffn_out": ffn_out, "norm_gain": norm_gain, "norm_bias": norm_bias}


@jax.custom_vjp
def low(v):
    return lax.optimization_barrier(v.astype(jnp.bfloat16)).astype(jnp.float32)

@jax.custom_vjp
def low_back(v):
    return v

def low_keep(v):
    return (low(v), None)

def low_pass(kept, grad):
    return (grad,)

def back_keep(v):
    return (v, None)

def back_low(kept, grad):
    return (low(grad),)
low.defvjp(low_keep, low_pass)
low_back.defvjp(back_keep, back_low)
MASKED_SCORE = -1e+30
NORM_EPS = 1e-05
PRECISE = lax.Precision.HIGHEST

def layer_norm(values, gain_row, bias_row):
    average = lax.optimization_barrier(jnp.mean(values, axis=-1, keepdims=True))
    centered = values - average
    variance = lax.optimization_barrier(jnp.mean(centered * centered, axis=-1, keepdims=True))
    return centered * lax.rsqrt(variance + NORM_EPS) * gain_row + bias_row

def split_heads(flat_rows):
    return flat_rows.reshape(flat_rows.shape[0], flat_rows.shape[1] // HDIM, HDIM)

def attend(queries, key_rows, value_rows, query_seg, key_seg, causal):
    scores = jnp.einsum('qhd,khd->hqk', split_heads(queries), split_heads(key_rows), precision=PRECISE) * HDIM ** (-0.5)
    scores = low_back(scores)
    allowed = query_seg[:, None] == key_seg[None, :]
    if causal:
        positions = jnp.arange(query_seg.shape[0])
        allowed = jnp.logical_and(allowed, positions[None, :] <= positions[:, None])
    scores = jnp.where(allowed[None], scores, MASKED_SCORE)
    highest = lax.optimization_barrier(jnp.max(scores, axis=-1, keepdims=True))
    weights = jnp.exp(scores - highest)
    weights_low = low(weights / lax.optimization_barrier(jnp.sum(weights, axis=-1, keepdims=True)))
    context = jnp.einsum('hqk,khd->qhd', weights_low, split_heads(value_rows), precision=PRECISE)
    return low(low_back(context.reshape(queries.shape[0], queries.shape[1])))

def rounded_out(inputs, weight, form):
    return low(low_back(jnp.einsum(form, inputs, weight, precision=PRECISE)))

def self_block(inputs, w_qkv, w_out, segment, causal):
    packed = rounded_out(low(inputs), w_qkv, 'sd,dtc->stc')
    context = attend(packed[:, 0], packed[:, 1], packed[:, 2], segment, segment, causal)
    return low_back(jnp.einsum('sc,ec->se', context, w_out, precision=PRECISE))

def feed_forward(inputs, w_in, w_back):
    inner_pre = low_back(jnp.einsum('sd,df->sf', low(inputs), w_in, precision=PRECISE))
    active = low(jax.nn.gelu(inner_pre, approximate=False))
    return low_back(jnp.einsum('sf,fd->sd', active, w_back, precision=PRECISE))

def row_pair(params, source, target, source_seg, target_seg):
    w_qkv, w_out, w_one, w_two, w_in, w_back, gains, biases = params
    normed_in = layer_norm(source, gains[0, 0], biases[0, 0])
    enc_mid = layer_norm(normed_in + self_block(normed_in, w_qkv[0], w_out[0], source_seg, False), gains[0, 1], biases[0, 1])
    encoded = layer_norm(enc_mid + feed_forward(enc_mid, w_in[0], w_back[0]), gains[0, 2], biases[0, 2])
    memory = low(encoded)
    key_rows = rounded_out(memory, w_one[0], 'sd,dc->sc')
    value_rows = rounded_out(memory, w_two[0], 'sd,dc->sc')
    dec_self = layer_norm(target + self_block(target, w_qkv[1], w_out[1], target_seg, True), gains[1, 0], biases[1, 0])
    queries = rounded_out(low(dec_self), w_one[1], 'sd,dc->sc')
    context = attend(queries, key_rows, value_rows, target_seg, source_seg, False)
    cross_out = low_back(jnp.einsum('sc,ec->se', context, w_two[1], precision=PRECISE))
    dec_cross = layer_norm(dec_self + cross_out, gains[1, 1], biases[1, 1])
    decoded = layer_norm(dec_cross + feed_forward(dec_cross, w_in[1], w_back[1]), gains[1, 2], biases[1, 2])
    return (encoded, decoded)

def reference(hidden, cotangent, segments, sa_qkv, sa_out, cross_one, cross_two, ffn_in, ffn_out, norm_gain, norm_bias):
    pair_count = MICRO * ROWS
    params = (sa_qkv.astype(jnp.float32), sa_out.astype(jnp.float32), cross_one.astype(jnp.float32), cross_two.astype(jnp.float32), ffn_in.astype(jnp.float32), ffn_out.astype(jnp.float32), norm_gain.astype(jnp.float32), norm_bias.astype(jnp.float32))
    source = hidden[0].astype(jnp.float32).reshape(pair_count, SEQ, D)
    target = hidden[1].astype(jnp.float32).reshape(pair_count, SEQ, D)
    source_seg = segments[0].reshape(pair_count, SEQ)
    target_seg = segments[1].reshape(pair_count, SEQ)

    def forward(param_set, source_rows, target_rows):

        def scan_step(running, row_item):
            return (running, row_pair(param_set, row_item[0], row_item[1], row_item[2], row_item[3]))
        _, outputs = lax.scan(jax.checkpoint(scan_step), jnp.zeros((), jnp.float32), (source_rows, target_rows, source_seg, target_seg))
        return outputs
    outputs, pullback = jax.vjp(forward, params, source, target)
    cotangents = (cotangent[0].astype(jnp.float32).reshape(pair_count, SEQ, D), cotangent[1].astype(jnp.float32).reshape(pair_count, SEQ, D))
    grad_set, d_source, d_target = pullback(cotangents)
    out_shape = (MICRO, ROWS, SEQ, D)
    hidden_out = jnp.stack([outputs[0].reshape(out_shape), outputs[1].reshape(out_shape)]).astype(jnp.bfloat16)
    hidden_grad = jnp.stack([d_source.reshape(out_shape), d_target.reshape(out_shape)])
    return (hidden_out, hidden_grad, grad_set[0], grad_set[1], grad_set[2], grad_set[3], grad_set[4], grad_set[5], grad_set[6], grad_set[7])
```

```python
import functools

import jax
import jax.numpy as jnp
from jax import lax
from jax.experimental import pallas as pl
from jax.experimental.pallas import tpu as pltpu
from jax.sharding import Mesh
from jax.sharding import PartitionSpec as P

HDIM = 64
LANES = 128
MASKED = -1e30
NORM_EPS = 1e-05
VMEM_BYTES = 56 * 1024 * 1024

SEG_LANES = 8
PART_LANE = 12

HEADS = ((0, 1, 2, 0, 0), (0, 1, 2, 1, 1), (1, 3, 0, 0, 1))


def mul(a, b):
    return jnp.dot(a, b, preferred_element_type=jnp.float32)


def mul_nt(a, b):
    return lax.dot_general(a, b, (((1,), (1,)), ((), ())), preferred_element_type=jnp.float32)


def mul_tn(a, b):
    return lax.dot_general(a, b, (((0,), (0,)), ((), ())), preferred_element_type=jnp.float32)


def tile_of(values, index):
    return values[:, index * LANES : (index + 1) * LANES]


def lane_ids(rows):
    return lax.broadcasted_iota(jnp.int32, (rows, LANES), 1)


def half_mask(rows, half):
    lanes = lane_ids(rows)
    return lanes >= HDIM if half else lanes < HDIM


def in_parts(base, column):
    lanes = lane_ids(base.shape[0])
    high = column.astype(jnp.bfloat16).astype(jnp.float32)
    rest = column - high
    middle = rest.astype(jnp.bfloat16).astype(jnp.float32)
    low = rest - middle
    parts = jnp.where(
        lanes == PART_LANE,
        high,
        jnp.where(lanes == PART_LANE + 1, middle, jnp.where(lanes == PART_LANE + 2, low, base)),
    )
    return parts.astype(jnp.bfloat16)


def with_triangle(scores, tri, at):
    size = tri.shape[1]
    pieces = []
    if at > 0:
        pieces.append(scores[:, : at * size])
    pieces.append(scores[:, at * size : (at + 1) * size] + tri)
    pieces.append(scores[:, (at + 1) * size :])
    return jnp.concatenate(pieces, axis=1)


def attend_kernel(causal, xq_ref, xkv_ref, a_ref, qx_ref, kx_ref, tri_ref, o_ref, q_ref, kv_ref, c_ref, l_ref):
    block = pl.program_id(0)
    q_ref[0] = mul(xq_ref[...], a_ref[0, :, : 2 * LANES]).astype(jnp.bfloat16)
    kv_ref[0] = mul(xkv_ref[...], a_ref[0, :, LANES : 5 * LANES]).astype(jnp.bfloat16)
    rows = tri_ref.shape[0]
    ones = jnp.ones((kv_ref.shape[1], LANES), jnp.bfloat16)
    for part in range(q_ref.shape[1] // rows):
        at = slice(part * rows, (part + 1) * rows)
        contexts = []
        totals = jnp.zeros((rows, LANES), jnp.float32)
        for head, (q_tile, k_tile, v_tile, q_half, v_half) in enumerate(HEADS):
            queries = q_ref[0, at, q_tile * LANES : (q_tile + 1) * LANES] * 0.125
            queries = jnp.where(half_mask(rows, q_half), queries, 0).astype(jnp.bfloat16)
            keys = kv_ref[0, :, k_tile * LANES : (k_tile + 1) * LANES]
            values = kv_ref[0, :, v_tile * LANES : (v_tile + 1) * LANES]
            scores = mul_nt(
                jnp.concatenate([queries, qx_ref[at, :]], axis=1),
                jnp.concatenate([keys, kx_ref[...]], axis=1),
            )
            if causal:
                scores = with_triangle(scores, tri_ref[...], part)
            highest = jnp.max(scores, axis=1, keepdims=True)
            weights = jnp.exp(scores - highest).astype(jnp.bfloat16)
            full = mul(weights, jnp.concatenate([values, ones], axis=1))
            sums = full[:, LANES:]
            contexts.append(full[:, :LANES] / sums)
            totals = jnp.where(lane_ids(rows) == head, highest + jnp.log(sums), totals)
        low = half_mask(rows, 0)
        c_ref[0, at, :LANES] = jnp.where(low, 0, contexts[2]).astype(jnp.bfloat16)
        c_ref[0, at, LANES:] = jnp.where(low, contexts[0], contexts[1]).astype(jnp.bfloat16)
        l_ref[0, at, :] = totals
    out = mul_nt(c_ref[0], a_ref[0, :, 4 * LANES :])

    @pl.when(block == 0)
    def _():
        o_ref[...] = out

    @pl.when(block > 0)
    def _():
        o_ref[...] += out


def attend_back_kernel(
    causal,
    do_ref,
    xq_ref,
    xkv_ref,
    a_ref,
    q_ref,
    kv_ref,
    c_ref,
    l_ref,
    qx_ref,
    kx_ref,
    tri_ref,
    dxq_ref,
    dxkv_ref,
    da_ref,
    dkv_ref,
    dq_ref,
):
    block = pl.program_id(0)
    rows = tri_ref.shape[0]
    d_context = mul(do_ref[...], a_ref[0, :, 4 * LANES :]).astype(jnp.bfloat16)
    for part in range(q_ref.shape[1] // rows):
        at = slice(part * rows, (part + 1) * rows)
        d_queries = []
        for head, (q_tile, k_tile, v_tile, q_half, v_half) in enumerate(HEADS):
            c_tile = 0 if head == 2 else 1
            queries = q_ref[0, at, q_tile * LANES : (q_tile + 1) * LANES] * 0.125
            queries = jnp.where(half_mask(rows, q_half), queries, 0).astype(jnp.bfloat16)
            keys = kv_ref[0, :, k_tile * LANES : (k_tile + 1) * LANES]
            values = kv_ref[0, :, v_tile * LANES : (v_tile + 1) * LANES]
            d_rows = jnp.where(
                half_mask(rows, v_half), d_context[at, c_tile * LANES : (c_tile + 1) * LANES], 0
            ).astype(jnp.bfloat16)
            context = c_ref[0, at, c_tile * LANES : (c_tile + 1) * LANES].astype(jnp.float32)
            inner = jnp.sum(d_rows.astype(jnp.float32) * context, axis=1, keepdims=True)
            total = l_ref[0, at, head : head + 1]
            scores = mul_nt(
                jnp.concatenate([queries, in_parts(qx_ref[at, :].astype(jnp.float32), -total)], axis=1),
                jnp.concatenate([keys, kx_ref[...]], axis=1),
            )
            if causal:
                scores = with_triangle(scores, tri_ref[...], part)
            probs = jnp.exp(scores)
            d_probs = mul_nt(
                jnp.concatenate([d_rows, in_parts(jnp.zeros((rows, LANES), jnp.float32), -inner)], axis=1),
                jnp.concatenate([values, kx_ref[...]], axis=1),
            )
            d_scores = (probs * d_probs).astype(jnp.bfloat16)
            d_values = mul_tn(probs.astype(jnp.bfloat16), d_rows)
            d_keys = mul_tn(d_scores, queries)
            d_queries.append(mul(d_scores, keys) * 0.125)
            first = part == 0
            k_at = slice(k_tile * LANES, (k_tile + 1) * LANES)
            v_at = slice(v_tile * LANES, (v_tile + 1) * LANES)
            if first and head != 1:
                dkv_ref[:, k_at] = d_keys
                dkv_ref[:, v_at] = d_values
            else:
                dkv_ref[:, k_at] += d_keys
                dkv_ref[:, v_at] += d_values
        low = half_mask(rows, 0)
        dq_ref[at, :LANES] = jnp.where(low, d_queries[0], d_queries[1]).astype(jnp.bfloat16)
        dq_ref[at, LANES:] = jnp.where(low, d_queries[2], 0).astype(jnp.bfloat16)
    d_pair = dkv_ref[...].astype(jnp.bfloat16)
    d_query = dq_ref[...]
    d_xq = mul_nt(d_query, a_ref[0, :, : 2 * LANES])
    d_xkv = mul_nt(d_pair, a_ref[0, :, LANES : 5 * LANES])

    @pl.when(block == 0)
    def _():
        dxq_ref[...] = d_xq
        dxkv_ref[...] = d_xkv

    @pl.when(block > 0)
    def _():
        dxq_ref[...] += d_xq
        dxkv_ref[...] += d_xkv

    grad_q = mul_tn(xq_ref[...], d_query)
    grad_kv = mul_tn(xkv_ref[...], d_pair)
    grad_o = mul_tn(do_ref[...], c_ref[0])
    da_ref[0, :, :LANES] = grad_q[:, :LANES].astype(jnp.bfloat16)
    da_ref[0, :, LANES : 2 * LANES] = (grad_q[:, LANES:] + grad_kv[:, :LANES]).astype(jnp.bfloat16)
    da_ref[0, :, 2 * LANES : 4 * LANES] = grad_kv[:, LANES : 3 * LANES].astype(jnp.bfloat16)
    da_ref[0, :, 4 * LANES : 5 * LANES] = (grad_kv[:, 3 * LANES :] + grad_o[:, :LANES]).astype(jnp.bfloat16)
    da_ref[0, :, 5 * LANES :] = grad_o[:, LANES:].astype(jnp.bfloat16)


def whole(shape):
    return pl.BlockSpec(shape, lambda j: (0,) * len(shape))


def per_block(shape):
    return pl.BlockSpec((1,) + shape, lambda j: (j,) + (0,) * len(shape))


PARAMS = pltpu.CompilerParams(vmem_limit_bytes=VMEM_BYTES)


def attend(xq, xkv, packed, extras, causal):
    rows, width = xq.shape
    keys = xkv.shape[0]
    blocks = packed.shape[0]
    qx, kx, tri = extras
    shape = jax.ShapeDtypeStruct
    return pl.pallas_call(
        functools.partial(attend_kernel, causal),
        grid=(blocks,),
        in_specs=[
            whole((rows, width)),
            whole((keys, width)),
            per_block(packed.shape[1:]),
            whole(qx.shape),
            whole(kx.shape),
            whole(tri.shape),
        ],
        out_specs=[
            whole((rows, width)),
            per_block((rows, 2 * LANES)),
            per_block((keys, 4 * LANES)),
            per_block((rows, 2 * LANES)),
            per_block((rows, LANES)),
        ],
        out_shape=[
            shape((rows, width), jnp.float32),
            shape((blocks, rows, 2 * LANES), jnp.bfloat16),
            shape((blocks, keys, 4 * LANES), jnp.bfloat16),
            shape((blocks, rows, 2 * LANES), jnp.bfloat16),
            shape((blocks, rows, LANES), jnp.float32),
        ],
        compiler_params=PARAMS,
        name="attend_self" if causal else "attend_cross",
    )(xq, xkv, packed, qx, kx, tri)


def attend_back(d_out, xq, xkv, packed, kept, extras, causal):
    rows, width = xq.shape
    keys = xkv.shape[0]
    blocks = packed.shape[0]
    qx, kx, tri = extras
    shape = jax.ShapeDtypeStruct
    return pl.pallas_call(
        functools.partial(attend_back_kernel, causal),
        grid=(blocks,),
        in_specs=[
            whole((rows, width)),
            whole((rows, width)),
            whole((keys, width)),
            per_block(packed.shape[1:]),
            per_block((rows, 2 * LANES)),
            per_block((keys, 4 * LANES)),
            per_block((rows, 2 * LANES)),
            per_block((rows, LANES)),
            whole(qx.shape),
            whole(kx.shape),
            whole(tri.shape),
        ],
        out_specs=[
            whole((rows, width)),
            whole((keys, width)),
            per_block(packed.shape[1:]),
        ],
        out_shape=[
            shape((rows, width), jnp.float32),
            shape((keys, width), jnp.float32),
            shape(packed.shape, jnp.bfloat16),
        ],
        scratch_shapes=[
            pltpu.VMEM((keys, 4 * LANES), jnp.float32),
            pltpu.VMEM((rows, 2 * LANES), jnp.bfloat16),
        ],
        compiler_params=PARAMS,
        name="attend_self_back" if causal else "attend_cross_back",
    )(d_out, xq, xkv, packed, *kept, qx, kx, tri)


def ffn_kernel(x_ref, f1_ref, f2_ref, z_ref, g_ref, slope_ref):
    block = pl.program_id(0)
    inner = mul(x_ref[...], f1_ref[0])
    spread = 0.5 * (1.0 + lax.erf(inner * (0.5**0.5)))
    bell = jnp.exp(-0.5 * inner * inner) * 0.3989422804014327
    active = (inner * spread).astype(jnp.bfloat16)
    g_ref[0] = active
    slope_ref[0] = (spread + inner * bell).astype(jnp.bfloat16)
    out = mul_nt(active, f2_ref[0])

    @pl.when(block == 0)
    def _():
        z_ref[...] = out

    @pl.when(block > 0)
    def _():
        z_ref[...] += out


def ffn(x, first, second):
    rows, width = x.shape
    blocks, _, units = first.shape
    shape = jax.ShapeDtypeStruct
    return pl.pallas_call(
        ffn_kernel,
        grid=(blocks,),
        in_specs=[whole((rows, width)), per_block(first.shape[1:]), per_block(second.shape[1:])],
        out_specs=[whole((rows, width)), per_block((rows, units)), per_block((rows, units))],
        out_shape=[
            shape((rows, width), jnp.float32),
            shape((blocks, rows, units), jnp.bfloat16),
            shape((blocks, rows, units), jnp.bfloat16),
        ],
        compiler_params=PARAMS,
        name="ffn",
    )(x, first, second)


def ffn_back_kernel(dz_ref, f1_ref, f2_ref, slope_ref, dx_ref, dh_ref):
    block = pl.program_id(0)
    d_active = mul(dz_ref[...], f2_ref[0])
    d_inner = (d_active * slope_ref[0].astype(jnp.float32)).astype(jnp.bfloat16)
    dh_ref[0] = d_inner
    out = mul_nt(d_inner, f1_ref[0])

    @pl.when(block == 0)
    def _():
        dx_ref[...] = out

    @pl.when(block > 0)
    def _():
        dx_ref[...] += out


def ffn_back(dz, first, second, slope):
    rows, width = dz.shape
    blocks, _, units = first.shape
    shape = jax.ShapeDtypeStruct
    return pl.pallas_call(
        ffn_back_kernel,
        grid=(blocks,),
        in_specs=[
            whole((rows, width)),
            per_block(first.shape[1:]),
            per_block(second.shape[1:]),
            per_block((rows, units)),
        ],
        out_specs=[whole((rows, width)), per_block((rows, units))],
        out_shape=[
            shape((rows, width), jnp.float32),
            shape((blocks, rows, units), jnp.bfloat16),
        ],
        compiler_params=PARAMS,
        name="ffn_back",
    )(dz, first, second, slope)


def ffn_grads_kernel(x_ref, dz_ref, g_ref, dh_ref, d1_ref, d2_ref):
    d1_ref[0] = mul_tn(x_ref[...], dh_ref[0]).astype(jnp.bfloat16)
    d2_ref[0] = mul_tn(dz_ref[...], g_ref[0]).astype(jnp.bfloat16)


def ffn_grads(x, dz, active, d_inner):
    rows, width = x.shape
    blocks, _, units = active.shape
    out = jax.ShapeDtypeStruct((blocks, width, units), jnp.bfloat16)
    return pl.pallas_call(
        ffn_grads_kernel,
        grid=(blocks,),
        in_specs=[
            whole((rows, width)),
            whole((rows, width)),
            per_block((rows, units)),
            per_block((rows, units)),
        ],
        out_specs=[per_block((width, units)), per_block((width, units))],
        out_shape=[out, out],
        compiler_params=PARAMS,
        name="ffn_grads",
    )(x, dz, active, d_inner)


def layer_norm(values, gain_row, bias_row):
    average = jnp.mean(values, axis=-1, keepdims=True)
    centered = values - average
    variance = jnp.mean(centered * centered, axis=-1, keepdims=True)
    return centered * lax.rsqrt(variance + NORM_EPS) * gain_row + bias_row


def norm_back(values, gain_row, bias_row, upstream):
    _, pullback = jax.vjp(layer_norm, values, gain_row, bias_row)
    return pullback(upstream)


def low(values):
    return values.astype(jnp.bfloat16)


SWAP = [(0, 0), (1, 2), (2, 1), (3, 3)]
PAIR = [(0, 1), (1, 0)]


def swapped(x):
    return lax.ppermute(x, ("section", "tx"), SWAP)


def over_y(x):
    return lax.ppermute(x, "ty", PAIR)


def over_cores(x):
    return lax.ppermute(x, "section", PAIR)


def in_order(x, flag, axis):
    return jnp.where(flag == 1, jnp.flip(x, axis), x)


def pack_heads(query, key, value, out):
    pair = 2 * HDIM
    return jnp.concatenate(
        [
            query,
            value[:, pair:],
            key[:, :pair],
            value[:, :pair],
            key[:, pair:],
            out[:, pair:],
            out[:, :pair],
        ],
        axis=1,
    )


def unpack_heads(packed):
    part = [packed[:, at * HDIM : (at + 1) * HDIM] for at in range(12)]
    query = jnp.concatenate(part[0:3], axis=1)
    key = jnp.concatenate([part[4], part[5], part[8]], axis=1)
    value = jnp.concatenate([part[6], part[7], part[3]], axis=1)
    out = jnp.concatenate([part[10], part[11], part[9]], axis=1)
    return query, key, value, out


def spread(shard):
    own = lax.all_gather(shard, "dp", axis=0, tiled=True)
    pair = jnp.stack([own, over_y(own)])
    return jnp.concatenate([pair, over_cores(pair)], axis=0)


def collected(blocks):
    pair = low(blocks[:2].astype(jnp.float32) + over_cores(blocks[2:]).astype(jnp.float32))
    own = low(pair[0].astype(jnp.float32) + over_y(pair[1]).astype(jnp.float32))
    return lax.psum_scatter(own, "dp", scatter_dimension=0, tiled=True)


def body(
    hidden,
    cotangent,
    segments,
    sa_qkv,
    sa_out,
    cross_one,
    cross_two,
    ffn_in,
    ffn_out,
    norm_gain,
    norm_bias,
):
    core = lax.axis_index("section")
    y_at = lax.axis_index("ty")
    on_encoder = lax.axis_index("tx") == 0
    quarter = hidden.shape[3]

    def pick(first, second):
        return jnp.where(on_encoder, first, second)

    def rows_in(x):
        both = in_order(swapped(x[0, :, 0]), y_at, 0)
        return jnp.concatenate([both[0], over_y(both[1])], axis=0)

    def rows_out(x):
        both = jnp.stack([x[:quarter], over_y(x[quarter:])])
        return swapped(in_order(both, y_at, 0))[None, :, None]

    norms = swapped(jnp.concatenate([norm_gain[0], norm_bias[0]], axis=0))
    gains, biases = norms[:3], norms[3:]
    rows_here = rows_in(hidden)
    rows_all = jnp.concatenate([rows_here, over_cores(rows_here)], axis=0)
    cot = rows_in(cotangent).astype(jnp.float32)

    packed_self = pack_heads(sa_qkv[0, :, 0], sa_qkv[0, :, 1], sa_qkv[0, :, 2], sa_out[0])
    cross_low = jnp.concatenate([cross_one[0], cross_two[0]], axis=1)
    w_self = spread(swapped(packed_self))
    w_first = spread(swapped(ffn_in[0]))
    w_second = spread(swapped(ffn_out[0].T))
    width = cross_one.shape[2]
    pair_kv = lax.ppermute(cross_low, ("section", "tx"), [(0, 1), (1, 3)])
    pair_qo = lax.ppermute(cross_low, ("section", "tx"), [(2, 1), (3, 3)])
    packed_cross = pack_heads(pair_qo[:, :width], pair_kv[:, :width], pair_kv[:, width:], pair_qo[:, width:])
    w_cross = spread(packed_cross)

    both_segments = in_order(segments[:, :, 0], y_at, 1)[:, 0]
    ordered = both_segments.reshape(2, 2, 2, quarter)
    ordered = in_order(in_order(ordered, y_at, 1), core, 2).transpose(0, 2, 1, 3).reshape(2, 4 * quarter)
    source_seg, target_seg = ordered[0], ordered[1]
    self_seg = pick(source_seg, target_seg)
    places = jnp.arange(4)
    quarter_of = jnp.repeat(2 * ((places % 2) ^ y_at) + ((places // 2) ^ core), quarter)
    lanes = jnp.arange(LANES)[None, :]

    def key_extras(seg):
        differs = jnp.logical_and(lanes < SEG_LANES, seg[:, None] != lanes)
        later = jnp.logical_and(
            jnp.logical_and(lanes >= SEG_LANES, lanes < PART_LANE),
            quarter_of[:, None] > lanes - SEG_LANES,
        )
        part = jnp.logical_and(lanes >= PART_LANE, lanes < PART_LANE + 3)
        return jnp.where(differs | later | part, 1.0, 0.0).astype(jnp.bfloat16)

    def query_extras(seg, causal):
        seg, at = seg[: 2 * quarter], quarter_of[: 2 * quarter]
        same = seg[:, None] == lanes
        here = jnp.logical_and(at[:, None] + SEG_LANES == lanes, causal)
        return jnp.where(same | here, MASKED, 0.0).astype(jnp.bfloat16)

    at_row = jnp.arange(quarter)
    later_key = jnp.logical_and(at_row[None, :] > at_row[:, None], jnp.logical_not(on_encoder))
    tri = jnp.where(later_key, MASKED, 0.0).astype(jnp.float32)
    self_extras = (query_extras(self_seg, jnp.logical_not(on_encoder)), key_extras(self_seg), tri)
    cross_extras = (query_extras(target_seg, False), key_extras(source_seg), tri)

    start = rows_all.astype(jnp.float32)
    start = pick(layer_norm(start, gains[0], biases[0]), start)
    start_here = start[: 2 * quarter]
    start_low = low(start)
    self_gain, self_bias = pick(gains[1], gains[0]), pick(biases[1], biases[0])
    self_out, *kept_self = attend(start_low[: 2 * quarter], start_low, w_self, self_extras, True)
    self_total = start_here + self_out
    middle = layer_norm(self_total, self_gain, self_bias)
    middle_low = low(middle)

    enc_out, enc_active, enc_slope = ffn(middle_low, w_first, w_second)
    enc_total = middle + enc_out
    encoded = low(layer_norm(enc_total, gains[2], biases[2]))
    memory_here = lax.ppermute(encoded, "tx", [(0, 1)])
    memory = jnp.concatenate([memory_here, over_cores(memory_here)], axis=0)

    cross_out, *kept_cross = attend(middle_low, memory, w_cross, cross_extras, False)
    cross_total = middle + cross_out
    after = layer_norm(cross_total, gains[1], biases[1])
    after_low = low(after)
    dec_out, dec_active, dec_slope = ffn(after_low, w_first, w_second)
    dec_total = after + dec_out
    decoded = low(layer_norm(dec_total, gains[2], biases[2]))
    hidden_out = rows_out(pick(encoded, decoded))

    d_dec_total, dec_gain_c, dec_bias_c = norm_back(dec_total, gains[2], biases[2], cot)
    d_dec_low = low(d_dec_total)
    d_after, dec_inner = ffn_back(d_dec_low, w_first, w_second, dec_slope)
    d_cross_total, dec_gain_b, dec_bias_b = norm_back(
        cross_total, gains[1], biases[1], d_dec_total + d_after
    )
    d_middle_part, d_memory, grad_cross = attend_back(
        low(d_cross_total), middle_low, memory, w_cross, kept_cross, cross_extras, False
    )
    d_memory_here = d_memory[: 2 * quarter] + over_cores(low(d_memory[2 * quarter :])).astype(jnp.float32)
    d_encoded = lax.ppermute(low(d_memory_here), "tx", [(1, 0)]).astype(jnp.float32) + cot

    d_enc_total, enc_gain_c, enc_bias_c = norm_back(enc_total, gains[2], biases[2], d_encoded)
    d_enc_low = low(d_enc_total)
    d_enc_middle, enc_inner = ffn_back(d_enc_low, w_first, w_second, enc_slope)
    grad_first, grad_second = ffn_grads(
        pick(middle_low, after_low),
        pick(d_enc_low, d_dec_low),
        pick(enc_active, dec_active),
        pick(enc_inner, dec_inner),
    )

    d_middle = pick(d_enc_total + d_enc_middle, d_cross_total + d_middle_part)
    d_self_total, gain_s, bias_s = norm_back(self_total, self_gain, self_bias, d_middle)
    d_start_q, d_start_kv, grad_self = attend_back(
        low(d_self_total), start_low[: 2 * quarter], start_low, w_self, kept_self, self_extras, True
    )
    d_start = d_self_total + d_start_q + d_start_kv[: 2 * quarter]
    d_start = d_start + over_cores(low(d_start_kv[2 * quarter :])).astype(jnp.float32)
    d_source, gain_a, bias_a = norm_back(
        rows_here.astype(jnp.float32), gains[0], biases[0], d_start
    )
    hidden_grad = rows_out(low(pick(d_source, d_start))).astype(jnp.float32)

    share_cross = collected(grad_cross)
    share_first = swapped(collected(grad_first)).astype(jnp.float32)
    share_second = swapped(collected(grad_second)).astype(jnp.float32).T
    share_self = swapped(collected(grad_self)).astype(jnp.float32)
    g_query, g_key, g_value, g_out = unpack_heads(share_self)
    grad_qkv = jnp.stack([g_query, g_key, g_value], axis=1)
    c_query, c_key, c_value, c_out = unpack_heads(share_cross)
    for_enc = lax.ppermute(jnp.concatenate([c_key, c_value], axis=1), ("section", "tx"), [(1, 0), (3, 1)])
    for_dec = lax.ppermute(jnp.concatenate([c_query, c_out], axis=1), ("section", "tx"), [(1, 2), (3, 3)])
    cross = jnp.where(core == 0, for_enc, for_dec).astype(jnp.float32)

    norm_sums = jnp.stack(
        [
            pick(gain_a, gain_s),
            pick(gain_s, dec_gain_b),
            pick(enc_gain_c, dec_gain_c),
            pick(bias_a, bias_s),
            pick(bias_s, dec_bias_b),
            pick(enc_bias_c, dec_bias_c),
        ]
    )
    dp_count = lax.axis_size("dp")
    pieces = norm_sums.reshape(6, dp_count, 2, 2, -1)
    pieces = in_order(in_order(pieces, y_at, 2), core, 3)
    pieces = pieces[:, :, :, 0] + over_cores(pieces[:, :, :, 1])
    pieces = pieces[:, :, 0] + over_y(pieces[:, :, 1])
    mine = lax.psum_scatter(pieces, "dp", scatter_dimension=1, tiled=True)[:, 0]
    norm_shares = swapped(mine)
    return (
        hidden_out,
        hidden_grad,
        grad_qkv[None],
        g_out[None],
        cross[None, :, :width],
        cross[None, :, width:],
        share_first[None],
        share_second[None],
        norm_shares[None, :3],
        norm_shares[None, 3:],
    )


def solution(mesh):
    _, dp_count, tensor_count = mesh.devices.shape
    split = Mesh(
        mesh.devices.reshape(2, dp_count, tensor_count // 2, 2), ("section", "dp", "ty", "tx")
    )
    tensor = ("ty", "tx")
    rows = P("section", None, "dp", tensor, None)
    in_specs = (
        rows,
        rows,
        P(None, None, "dp", None),
        P("section", "dp", None, tensor),
        P("section", "dp", tensor),
        P("section", "dp", tensor),
        P("section", "dp", tensor),
        P("section", "dp", tensor),
        P("section", tensor, "dp"),
        P("section", None, None),
        P("section", None, None),
    )
    out_specs = (
        rows,
        rows,
        P("section", "dp", None, tensor),
        P("section", "dp", tensor),
        P("section", "dp", tensor),
        P("section", "dp", tensor),
        P("section", "dp", tensor),
        P("section", tensor, "dp"),
        P("section", None, ("dp",) + tensor),
        P("section", None, ("dp",) + tensor),
    )
    return jax.shard_map(body, mesh=split, in_specs=in_specs, out_specs=out_specs, check_vma=False)
```

```python
import functools

import jax
import jax.numpy as jnp
from jax import lax
from jax.experimental import pallas as pl
from jax.experimental.pallas import tpu as pltpu
from jax.sharding import Mesh
from jax.sharding import PartitionSpec as P

HDIM = 64
LANES = 128
MASKED = -1e30
NORM_EPS = 1e-05
VMEM_BYTES = 56 * 1024 * 1024

SEG_LANES = 8
PART_LANE = 12

HEADS = ((0, 1, 2, 0, 0), (0, 1, 2, 1, 1), (1, 3, 0, 0, 1))


def mul(a, b):
    return jnp.dot(a, b, preferred_element_type=jnp.float32)


def mul_nt(a, b):
    return lax.dot_general(a, b, (((1,), (1,)), ((), ())), preferred_element_type=jnp.float32)


def mul_tn(a, b):
    return lax.dot_general(a, b, (((0,), (0,)), ((), ())), preferred_element_type=jnp.float32)


def tile_of(values, index):
    return values[:, index * LANES : (index + 1) * LANES]


def lane_ids(rows):
    return lax.broadcasted_iota(jnp.int32, (rows, LANES), 1)


def half_mask(rows, half):
    lanes = lane_ids(rows)
    return lanes >= HDIM if half else lanes < HDIM


def in_parts(base, column):
    lanes = lane_ids(base.shape[0])
    high = column.astype(jnp.bfloat16).astype(jnp.float32)
    rest = column - high
    middle = rest.astype(jnp.bfloat16).astype(jnp.float32)
    low = rest - middle
    parts = jnp.where(
        lanes == PART_LANE,
        high,
        jnp.where(lanes == PART_LANE + 1, middle, jnp.where(lanes == PART_LANE + 2, low, base)),
    )
    return parts.astype(jnp.bfloat16)


def with_triangle(scores, tri, at):
    size = tri.shape[1]
    pieces = []
    if at > 0:
        pieces.append(scores[:, : at * size])
    pieces.append(scores[:, at * size : (at + 1) * size] + tri)
    pieces.append(scores[:, (at + 1) * size :])
    return jnp.concatenate(pieces, axis=1)


def assemble(core, half, own_refs, peer_refs, w_ref):
    mine = pl.multiple_of(core * half, half)
    other = pl.multiple_of((1 - core) * half, half)
    for part, (own_ref, peer_ref) in enumerate(zip(own_refs, peer_refs)):
        width = own_ref.shape[2]
        columns = slice(part * width, (part + 1) * width)
        w_ref[pl.ds(mine, half), columns] = own_ref[0]
        w_ref[pl.ds(other, half), columns] = peer_ref[0]


def hand_out(core, half, g_ref, keep_refs, send_refs):
    mine = pl.multiple_of(core * half, half)
    other = pl.multiple_of((1 - core) * half, half)
    for part, (keep_ref, send_ref) in enumerate(zip(keep_refs, send_refs)):
        width = keep_ref.shape[2]
        columns = slice(part * width, (part + 1) * width)
        keep_ref[0] = g_ref[pl.ds(mine, half), columns]
        send_ref[0] = g_ref[pl.ds(other, half), columns]


def scaled_queries(q_ref, at, q_tile, q_half):
    queries = q_ref[0, at, q_tile * LANES : (q_tile + 1) * LANES] * 0.125
    return jnp.where(half_mask(queries.shape[0], q_half), queries, 0).astype(jnp.bfloat16)


def units_of(total, rows):
    return [
        (slice(part * rows, (part + 1) * rows), part, head)
        for part in range(total // rows)
        for head in range(len(HEADS))
    ]


def attend_kernel(causal, core_ref, xq_ref, xkv_ref, *refs):
    own_refs, peer_refs = refs[:3], refs[3:6]
    qx_ref, kx_ref, tri_ref, o_ref, q_ref, kv_ref, c_ref, l_ref, w_ref = refs[6:]
    block = pl.program_id(0)
    assemble(core_ref[0], own_refs[0].shape[1], own_refs, peer_refs, w_ref)
    q_ref[0] = mul(xq_ref[...], w_ref[:, : 2 * LANES]).astype(jnp.bfloat16)
    kv_ref[0] = mul(xkv_ref[...], w_ref[:, LANES : 5 * LANES]).astype(jnp.bfloat16)
    rows = tri_ref.shape[0]
    low = half_mask(rows, 0)

    def scores_of(at, part, head):
        q_tile, k_tile, _, q_half, _ = HEADS[head]
        keys = kv_ref[0, :, k_tile * LANES : (k_tile + 1) * LANES]
        scores = mul_nt(
            jnp.concatenate([scaled_queries(q_ref, at, q_tile, q_half), qx_ref[at, :]], axis=1),
            jnp.concatenate([keys, kx_ref[...]], axis=1),
        )
        return with_triangle(scores, tri_ref[...], part) if causal else scores

    units = units_of(q_ref.shape[1], rows)
    ahead = scores_of(*units[0])
    contexts, totals = [], None
    for index, (at, part, head) in enumerate(units):
        scores = ahead
        if index + 1 < len(units):
            ahead = scores_of(*units[index + 1])
        v_tile = HEADS[head][2]
        values = kv_ref[0, :, v_tile * LANES : (v_tile + 1) * LANES]
        highest = jnp.max(scores, axis=1, keepdims=True)
        weights = jnp.exp(scores - highest)
        sums = jnp.sum(weights, axis=1, keepdims=True)
        contexts.append(mul(weights.astype(jnp.bfloat16), values) / sums)
        logs = jnp.broadcast_to(highest + jnp.log(sums), (rows, LANES))
        totals = logs if head == 0 else jnp.where(lane_ids(rows) == head, logs, totals)
        if head == len(HEADS) - 1:
            c_ref[0, at, :LANES] = jnp.where(low, 0, contexts[2]).astype(jnp.bfloat16)
            c_ref[0, at, LANES:] = jnp.where(low, contexts[0], contexts[1]).astype(jnp.bfloat16)
            l_ref[0, at, :] = totals
            contexts = []
    out = mul_nt(c_ref[0], w_ref[:, 4 * LANES :])

    @pl.when(block == 0)
    def _():
        o_ref[...] = out

    @pl.when(block > 0)
    def _():
        o_ref[...] += out


def attend_back_kernel(causal, core_ref, do_ref, xq_ref, xkv_ref, *refs):
    own_refs, peer_refs = refs[:3], refs[3:6]
    q_ref, kv_ref, c_ref, l_ref, qx_ref, kx_ref, tri_ref, dxq_ref, dxkv_ref = refs[6:15]
    keep_refs, send_refs = refs[15:18], refs[18:21]
    w_ref, dkv_ref, dq_ref, g_ref = refs[21:]
    block = pl.program_id(0)
    rows = tri_ref.shape[0]
    half = own_refs[0].shape[1]
    assemble(core_ref[0], half, own_refs, peer_refs, w_ref)
    d_context = mul(do_ref[...], w_ref[:, 4 * LANES :]).astype(jnp.bfloat16)
    low = half_mask(rows, 0)

    def products_of(at, part, head):
        q_tile, k_tile, v_tile, q_half, v_half = HEADS[head]
        c_tile = 0 if head == 2 else 1
        keys = kv_ref[0, :, k_tile * LANES : (k_tile + 1) * LANES]
        values = kv_ref[0, :, v_tile * LANES : (v_tile + 1) * LANES]
        queries = scaled_queries(q_ref, at, q_tile, q_half)
        d_rows = jnp.where(half_mask(rows, v_half), tile_of(d_context[at], c_tile), 0).astype(jnp.bfloat16)
        total = l_ref[0, at, head : head + 1]
        scores = mul_nt(
            jnp.concatenate([queries, in_parts(qx_ref[at, :].astype(jnp.float32), -total)], axis=1),
            jnp.concatenate([keys, kx_ref[...]], axis=1),
        )
        if causal:
            scores = with_triangle(scores, tri_ref[...], part)
        return scores, mul_nt(d_rows, values), queries, d_rows, keys

    units = units_of(q_ref.shape[1], rows)
    ahead = products_of(*units[0])
    d_queries = []
    for index, (at, part, head) in enumerate(units):
        scores, d_probs, queries, d_rows, keys = ahead
        if index + 1 < len(units):
            ahead = products_of(*units[index + 1])
        _, k_tile, v_tile, _, _ = HEADS[head]
        probs = jnp.exp(scores)
        inner = jnp.sum(probs * d_probs, axis=1, keepdims=True)
        d_scores = (probs * (d_probs - inner)).astype(jnp.bfloat16)
        d_values = mul_tn(probs.astype(jnp.bfloat16), d_rows)
        d_keys = mul_tn(d_scores, queries)
        d_queries.append(mul(d_scores, keys) * 0.125)
        k_at = slice(k_tile * LANES, (k_tile + 1) * LANES)
        v_at = slice(v_tile * LANES, (v_tile + 1) * LANES)
        if part == 0 and head != 1:
            dkv_ref[:, k_at] = d_keys
            dkv_ref[:, v_at] = d_values
        else:
            dkv_ref[:, k_at] += d_keys
            dkv_ref[:, v_at] += d_values
        if head == len(HEADS) - 1:
            dq_ref[at, :LANES] = jnp.where(low, d_queries[0], d_queries[1]).astype(jnp.bfloat16)
            dq_ref[at, LANES:] = jnp.where(low, d_queries[2], 0).astype(jnp.bfloat16)
            d_queries = []
    d_pair = dkv_ref[...].astype(jnp.bfloat16)
    d_query = dq_ref[...]
    d_xq = mul_nt(d_query, w_ref[:, : 2 * LANES])
    d_xkv = mul_nt(d_pair, w_ref[:, LANES : 5 * LANES])

    @pl.when(block == 0)
    def _():
        dxq_ref[...] = d_xq
        dxkv_ref[...] = d_xkv

    @pl.when(block > 0)
    def _():
        dxq_ref[...] += d_xq
        dxkv_ref[...] += d_xkv

    grad_q = mul_tn(xq_ref[...], d_query)
    grad_kv = mul_tn(xkv_ref[...], d_pair)
    grad_o = mul_tn(do_ref[...], c_ref[0])
    g_ref[:, :LANES] = grad_q[:, :LANES].astype(jnp.bfloat16)
    g_ref[:, LANES : 2 * LANES] = (grad_q[:, LANES:] + grad_kv[:, :LANES]).astype(jnp.bfloat16)
    g_ref[:, 2 * LANES : 4 * LANES] = grad_kv[:, LANES : 3 * LANES].astype(jnp.bfloat16)
    g_ref[:, 4 * LANES : 5 * LANES] = (grad_kv[:, 3 * LANES :] + grad_o[:, :LANES]).astype(jnp.bfloat16)
    g_ref[:, 5 * LANES :] = grad_o[:, LANES:].astype(jnp.bfloat16)
    hand_out(core_ref[0], half, g_ref, keep_refs, send_refs)


def whole(shape):
    return pl.BlockSpec(shape, lambda j: (0,) * len(shape))


def per_block(shape):
    return pl.BlockSpec((1,) + shape, lambda j: (j,) + (0,) * len(shape))


FLAG = pl.BlockSpec(memory_space=pltpu.SMEM)
PARAMS = pltpu.CompilerParams(vmem_limit_bytes=VMEM_BYTES)
shape = jax.ShapeDtypeStruct


def attend(core, xq, xkv, weights, extras, causal):
    rows, width = xq.shape
    keys = xkv.shape[0]
    blocks = weights[0].shape[0]
    qx, kx, tri = extras
    return pl.pallas_call(
        functools.partial(attend_kernel, causal),
        grid=(blocks,),
        in_specs=[FLAG, whole((rows, width)), whole((keys, width))]
        + [per_block(part.shape[1:]) for part in weights]
        + [whole(qx.shape), whole(kx.shape), whole(tri.shape)],
        out_specs=[
            whole((rows, width)),
            per_block((rows, 2 * LANES)),
            per_block((keys, 4 * LANES)),
            per_block((rows, 2 * LANES)),
            per_block((rows, LANES)),
        ],
        out_shape=[
            shape((rows, width), jnp.float32),
            shape((blocks, rows, 2 * LANES), jnp.bfloat16),
            shape((blocks, keys, 4 * LANES), jnp.bfloat16),
            shape((blocks, rows, 2 * LANES), jnp.bfloat16),
            shape((blocks, rows, LANES), jnp.float32),
        ],
        scratch_shapes=[pltpu.VMEM((width, 6 * LANES), jnp.bfloat16)],
        compiler_params=PARAMS,
        name="attend_self" if causal else "attend_cross",
    )(core, xq, xkv, *weights, qx, kx, tri)


def attend_back(core, d_out, xq, xkv, weights, kept, extras, causal):
    rows, width = xq.shape
    keys = xkv.shape[0]
    blocks = weights[0].shape[0]
    qx, kx, tri = extras
    out = pl.pallas_call(
        functools.partial(attend_back_kernel, causal),
        grid=(blocks,),
        in_specs=[FLAG, whole((rows, width)), whole((rows, width)), whole((keys, width))]
        + [per_block(part.shape[1:]) for part in weights]
        + [
            per_block((rows, 2 * LANES)),
            per_block((keys, 4 * LANES)),
            per_block((rows, 2 * LANES)),
            per_block((rows, LANES)),
            whole(qx.shape),
            whole(kx.shape),
            whole(tri.shape),
        ],
        out_specs=[whole((rows, width)), whole((keys, width))]
        + [per_block(part.shape[1:]) for part in weights],
        out_shape=[shape((rows, width), jnp.float32), shape((keys, width), jnp.float32)]
        + [shape(part.shape, jnp.bfloat16) for part in weights],
        scratch_shapes=[
            pltpu.VMEM((width, 6 * LANES), jnp.bfloat16),
            pltpu.VMEM((keys, 4 * LANES), jnp.float32),
            pltpu.VMEM((rows, 2 * LANES), jnp.bfloat16),
            pltpu.VMEM((width, 6 * LANES), jnp.bfloat16),
        ],
        compiler_params=PARAMS,
        name="attend_self_back" if causal else "attend_cross_back",
    )(core, d_out, xq, xkv, *weights, *kept, qx, kx, tri)
    return out[0], out[1], out[2:5], out[5:8]


def ffn_kernel(core_ref, x_ref, *refs):
    own_refs, peer_refs = refs[:3], refs[3:6]
    z_ref, g_ref, slope_ref, w_ref = refs[6:]
    block = pl.program_id(0)
    assemble(core_ref[0], own_refs[0].shape[1], own_refs, peer_refs, w_ref)
    units = own_refs[0].shape[2] // 2
    out = 0.0
    for part in range(3):
        at = 2 * units * part
        inner = mul(x_ref[...], w_ref[:, at : at + units])
        spread = 0.5 * (1.0 + lax.erf(inner * (0.5**0.5)))
        bell = jnp.exp(-0.5 * inner * inner) * 0.3989422804014327
        active = (inner * spread).astype(jnp.bfloat16)
        columns = slice(units * part, units * (part + 1))
        g_ref[0, :, columns] = active
        slope_ref[0, :, columns] = (spread + inner * bell).astype(jnp.bfloat16)
        out = out + mul_nt(active, w_ref[:, at + units : at + 2 * units])

    @pl.when(block == 0)
    def _():
        z_ref[...] = out

    @pl.when(block > 0)
    def _():
        z_ref[...] += out


def ffn(core, x, weights):
    rows, width = x.shape
    blocks, _, columns = weights[0].shape
    units = 3 * columns // 2
    return pl.pallas_call(
        ffn_kernel,
        grid=(blocks,),
        in_specs=[FLAG, whole((rows, width))] + [per_block(part.shape[1:]) for part in weights],
        out_specs=[whole((rows, width)), per_block((rows, units)), per_block((rows, units))],
        out_shape=[
            shape((rows, width), jnp.float32),
            shape((blocks, rows, units), jnp.bfloat16),
            shape((blocks, rows, units), jnp.bfloat16),
        ],
        scratch_shapes=[pltpu.VMEM((width, 3 * columns), jnp.bfloat16)],
        compiler_params=PARAMS,
        name="ffn",
    )(core, x, *weights)


def ffn_back_kernel(core_ref, dz_ref, *refs):
    own_refs, peer_refs = refs[:3], refs[3:6]
    slope_ref, dx_ref, dh_ref, w_ref = refs[6:]
    block = pl.program_id(0)
    assemble(core_ref[0], own_refs[0].shape[1], own_refs, peer_refs, w_ref)
    units = own_refs[0].shape[2] // 2
    out = 0.0
    for part in range(3):
        at = 2 * units * part
        columns = slice(units * part, units * (part + 1))
        d_active = mul(dz_ref[...], w_ref[:, at + units : at + 2 * units])
        d_inner = (d_active * slope_ref[0, :, columns].astype(jnp.float32)).astype(jnp.bfloat16)
        dh_ref[0, :, columns] = d_inner
        out = out + mul_nt(d_inner, w_ref[:, at : at + units])

    @pl.when(block == 0)
    def _():
        dx_ref[...] = out

    @pl.when(block > 0)
    def _():
        dx_ref[...] += out


def ffn_back(core, dz, weights, slope):
    rows, width = dz.shape
    blocks, _, columns = weights[0].shape
    units = 3 * columns // 2
    return pl.pallas_call(
        ffn_back_kernel,
        grid=(blocks,),
        in_specs=[FLAG, whole((rows, width))]
        + [per_block(part.shape[1:]) for part in weights]
        + [per_block((rows, units))],
        out_specs=[whole((rows, width)), per_block((rows, units))],
        out_shape=[
            shape((rows, width), jnp.float32),
            shape((blocks, rows, units), jnp.bfloat16),
        ],
        scratch_shapes=[pltpu.VMEM((width, 3 * columns), jnp.bfloat16)],
        compiler_params=PARAMS,
        name="ffn_back",
    )(core, dz, *weights, slope)


def ffn_grads_kernel(core_ref, x_ref, dz_ref, g_ref, dh_ref, *refs):
    keep_refs, send_refs, w_ref = refs[:3], refs[3:6], refs[6]
    units = keep_refs[0].shape[2] // 2
    for part in range(3):
        at = 2 * units * part
        columns = slice(units * part, units * (part + 1))
        w_ref[:, at : at + units] = mul_tn(x_ref[...], dh_ref[0, :, columns]).astype(jnp.bfloat16)
        w_ref[:, at + units : at + 2 * units] = mul_tn(dz_ref[...], g_ref[0, :, columns]).astype(jnp.bfloat16)
    hand_out(core_ref[0], keep_refs[0].shape[1], w_ref, keep_refs, send_refs)


def ffn_grads(core, x, dz, active, d_inner, like):
    rows, width = x.shape
    blocks, _, units = active.shape
    out = pl.pallas_call(
        ffn_grads_kernel,
        grid=(blocks,),
        in_specs=[
            FLAG,
            whole((rows, width)),
            whole((rows, width)),
            per_block((rows, units)),
            per_block((rows, units)),
        ],
        out_specs=[per_block(part.shape[1:]) for part in like],
        out_shape=[shape(part.shape, jnp.bfloat16) for part in like],
        scratch_shapes=[pltpu.VMEM((width, 2 * units), jnp.bfloat16)],
        compiler_params=PARAMS,
        name="ffn_grads",
    )(core, x, dz, active, d_inner)
    return out[:3], out[3:]


def layer_norm(values, gain_row, bias_row):
    average = jnp.mean(values, axis=-1, keepdims=True)
    centered = values - average
    variance = jnp.mean(centered * centered, axis=-1, keepdims=True)
    return centered * lax.rsqrt(variance + NORM_EPS) * gain_row + bias_row


def norm_back(values, gain_row, bias_row, upstream):
    _, pullback = jax.vjp(layer_norm, values, gain_row, bias_row)
    return pullback(upstream)


def low(values):
    return values.astype(jnp.bfloat16)


SWAP = [(0, 0), (1, 2), (2, 1), (3, 3)]
PAIR = [(0, 1), (1, 0)]


def swapped(x, axis="zh"):
    return lax.ppermute(x, ("section", axis), SWAP)


def over(x, axis):
    return lax.ppermute(x, axis, PAIR)


def in_order(x, flag, axis):
    return jnp.where(flag == 1, jnp.flip(x, axis), x)


def pack_heads(query, key, value, out):
    pair = 2 * HDIM
    return jnp.concatenate(
        [
            query,
            value[:, pair:],
            key[:, :pair],
            value[:, :pair],
            key[:, pair:],
            out[:, pair:],
            out[:, :pair],
        ],
        axis=1,
    )


def unpack_heads(packed):
    part = [packed[:, at * HDIM : (at + 1) * HDIM] for at in range(12)]
    query = jnp.concatenate(part[0:3], axis=1)
    key = jnp.concatenate([part[4], part[5], part[8]], axis=1)
    value = jnp.concatenate([part[6], part[7], part[3]], axis=1)
    out = jnp.concatenate([part[10], part[11], part[9]], axis=1)
    return query, key, value, out


def in_turns(count, first):
    groups = [["tx"], ["ty"], ["z%d" % at for at in range(count)]]
    return sum(groups[first:] + groups[:first], [])


def dim_of(axis):
    return {"ty": 0, "tx": 1}.get(axis, 2 + int(axis[1:]) if axis[0] == "z" else 0)


def spread(shard, count, first):
    x = shard.reshape((1,) * (2 + count) + shard.shape)
    for axis in in_turns(count, first):
        both = jnp.concatenate([x, over(x, axis)], axis=dim_of(axis))
        x = both if axis[0] == "t" else in_order(both, lax.axis_index(axis), dim_of(axis))
    x = x.reshape(4, -1, shard.shape[1])
    return x, over(x, "section")


def plus(first, second):
    return low(first.astype(jnp.float32) + second.astype(jnp.float32))


def collected(keep, send, count, first):
    x = plus(keep, over(send, "section"))
    x = x.reshape((2, 2) + (2,) * count + (-1, x.shape[2]))
    for axis in in_turns(count, first):
        dim = dim_of(axis)
        both = x if axis[0] == "t" else in_order(x, lax.axis_index(axis), dim)
        mine, other = jnp.split(both, 2, axis=dim)
        x = plus(mine, over(other, axis))
    return x.reshape(x.shape[-2:])


def body(
    count,
    hidden,
    cotangent,
    segments,
    sa_qkv,
    sa_out,
    cross_one,
    cross_two,
    ffn_in,
    ffn_out,
    norm_gain,
    norm_bias,
):
    core = lax.axis_index("section")
    core_flag = core.reshape(1)
    x_at, y_at, zh_at = lax.axis_index("tx"), lax.axis_index("ty"), lax.axis_index("zh")
    on_encoder = zh_at == 0
    quarter = hidden.shape[3]

    def pick(first, second):
        return jnp.where(on_encoder, first, second)

    def rows_in(x):
        both = in_order(swapped(x[0, :, 0]), x_at, 0)
        both = in_order(jnp.stack([both[0], over(both[1], "tx")]), x_at, 0)
        return swapped(both.reshape(2 * quarter, -1), "ty")

    def rows_out(x):
        both = in_order(swapped(x, "ty").reshape(2, quarter, -1), x_at, 0)
        both = in_order(jnp.stack([both[0], over(both[1], "tx")]), x_at, 0)
        return swapped(both)[None, :, None]

    packed_self = pack_heads(sa_qkv[0, :, 0], sa_qkv[0, :, 1], sa_qkv[0, :, 2], sa_out[0])
    first, second = ffn_in[0], ffn_out[0].T
    step = first.shape[1] // 3
    packed_ffn = jnp.concatenate(
        [side[:, step * at : step * (at + 1)] for at in range(3) for side in (first, second)], axis=1
    )
    cross_low = jnp.concatenate([cross_one[0], cross_two[0]], axis=1)

    def gathered(packed):
        width = packed.shape[1] // 3
        parts = [spread(packed[:, width * at : width * (at + 1)], count, at) for at in range(3)]
        return [own for own, _ in parts] + [peer for _, peer in parts]

    w_self = gathered(swapped(packed_self))

    rows_here = rows_in(hidden)
    rows_all = jnp.concatenate([rows_here, over(rows_here, "section")], axis=0)
    norms = swapped(jnp.concatenate([norm_gain[0], norm_bias[0]], axis=0))
    gains, biases = norms[:3], norms[3:]
    seg_own = segments[:, :, 0].astype(jnp.float32)
    seg_here = jnp.where(y_at == zh_at, seg_own, over(seg_own, "zh")).astype(jnp.int32)
    w_ffn = gathered(swapped(packed_ffn))

    width = cross_one.shape[2]
    pair_kv = lax.ppermute(cross_low, ("section", "zh"), [(0, 1), (1, 3)])
    pair_qo = lax.ppermute(cross_low, ("section", "zh"), [(2, 1), (3, 3)])
    packed_cross = pack_heads(pair_qo[:, :width], pair_kv[:, :width], pair_kv[:, width:], pair_qo[:, width:])
    w_cross = gathered(packed_cross)
    cot = rows_in(cotangent).astype(jnp.float32)

    both_segments = in_order(seg_here, x_at, 1)[:, 0]
    ordered = in_order(both_segments.reshape(2, 2, 2 * quarter), core, 1).reshape(2, 4 * quarter)
    source_seg, target_seg = ordered[0], ordered[1]
    self_seg = pick(source_seg, target_seg)
    places = jnp.arange(4)
    quarter_of = jnp.repeat(2 * ((places // 2) ^ core) + places % 2, quarter)
    lanes = jnp.arange(LANES)[None, :]

    def key_extras(seg):
        differs = jnp.logical_and(lanes < SEG_LANES, seg[:, None] != lanes)
        later = jnp.logical_and(
            jnp.logical_and(lanes >= SEG_LANES, lanes < PART_LANE),
            quarter_of[:, None] > lanes - SEG_LANES,
        )
        part = jnp.logical_and(lanes >= PART_LANE, lanes < PART_LANE + 3)
        return jnp.where(differs | later | part, 1.0, 0.0).astype(jnp.bfloat16)

    def query_extras(seg, causal):
        seg, at = seg[: 2 * quarter], quarter_of[: 2 * quarter]
        same = seg[:, None] == lanes
        here = jnp.logical_and(at[:, None] + SEG_LANES == lanes, causal)
        return jnp.where(same | here, MASKED, 0.0).astype(jnp.bfloat16)

    at_row = jnp.arange(quarter)
    later_key = jnp.logical_and(at_row[None, :] > at_row[:, None], jnp.logical_not(on_encoder))
    tri = jnp.where(later_key, MASKED, 0.0).astype(jnp.float32)
    self_extras = (query_extras(self_seg, jnp.logical_not(on_encoder)), key_extras(self_seg), tri)
    cross_extras = (query_extras(target_seg, False), key_extras(source_seg), tri)

    start = rows_all.astype(jnp.float32)
    start = pick(layer_norm(start, gains[0], biases[0]), start)
    start_here = start[: 2 * quarter]
    start_low = low(start)
    self_gain, self_bias = pick(gains[1], gains[0]), pick(biases[1], biases[0])
    self_out, *kept_self = attend(core_flag, start_low[: 2 * quarter], start_low, w_self, self_extras, True)
    self_total = start_here + self_out
    middle = layer_norm(self_total, self_gain, self_bias)
    middle_low = low(middle)

    enc_out, enc_active, enc_slope = ffn(core_flag, middle_low, w_ffn)
    enc_total = middle + enc_out
    encoded = low(layer_norm(enc_total, gains[2], biases[2]))
    memory_here = lax.ppermute(encoded, "zh", [(0, 1)])
    memory = jnp.concatenate([memory_here, over(memory_here, "section")], axis=0)

    cross_out, *kept_cross = attend(core_flag, middle_low, memory, w_cross, cross_extras, False)
    cross_total = middle + cross_out
    after = layer_norm(cross_total, gains[1], biases[1])
    after_low = low(after)
    dec_out, dec_active, dec_slope = ffn(core_flag, after_low, w_ffn)
    dec_total = after + dec_out
    decoded = low(layer_norm(dec_total, gains[2], biases[2]))
    hidden_out = rows_out(pick(encoded, decoded))

    d_dec_total, dec_gain_c, dec_bias_c = norm_back(dec_total, gains[2], biases[2], cot)
    d_dec_low = low(d_dec_total)
    d_after, dec_inner = ffn_back(core_flag, d_dec_low, w_ffn, dec_slope)
    d_cross_total, dec_gain_b, dec_bias_b = norm_back(
        cross_total, gains[1], biases[1], d_dec_total + d_after
    )
    d_middle_part, d_memory, cross_keep, cross_send = attend_back(
        core_flag, low(d_cross_total), middle_low, memory, w_cross, kept_cross, cross_extras, False
    )
    d_memory_here = d_memory[: 2 * quarter] + over(low(d_memory[2 * quarter :]), "section").astype(jnp.float32)
    d_encoded = lax.ppermute(low(d_memory_here), "zh", [(1, 0)]).astype(jnp.float32) + cot

    d_enc_total, enc_gain_c, enc_bias_c = norm_back(enc_total, gains[2], biases[2], d_encoded)
    d_enc_low = low(d_enc_total)
    d_enc_middle, enc_inner = ffn_back(core_flag, d_enc_low, w_ffn, enc_slope)
    ffn_keep, ffn_send = ffn_grads(
        core_flag,
        pick(middle_low, after_low),
        pick(d_enc_low, d_dec_low),
        pick(enc_active, dec_active),
        pick(enc_inner, dec_inner),
        w_ffn,
    )

    d_middle = pick(d_enc_total + d_enc_middle, d_cross_total + d_middle_part)
    d_self_total, gain_s, bias_s = norm_back(self_total, self_gain, self_bias, d_middle)
    d_start_q, d_start_kv, self_keep, self_send = attend_back(
        core_flag, low(d_self_total), start_low[: 2 * quarter], start_low, w_self, kept_self, self_extras, True
    )
    d_start = d_self_total + d_start_q + d_start_kv[: 2 * quarter]
    d_start = d_start + over(low(d_start_kv[2 * quarter :]), "section").astype(jnp.float32)
    d_source, gain_a, bias_a = norm_back(
        rows_here.astype(jnp.float32), gains[0], biases[0], d_start
    )
    hidden_grad = rows_out(low(pick(d_source, d_start))).astype(jnp.float32)

    def summed(keep, send):
        return jnp.concatenate([collected(keep[at], send[at], count, at) for at in range(3)], axis=1)

    share_cross = summed(cross_keep, cross_send)
    share_ffn = swapped(summed(ffn_keep, ffn_send)).astype(jnp.float32)
    share_self = swapped(summed(self_keep, self_send)).astype(jnp.float32)
    share_first = jnp.concatenate([share_ffn[:, 2 * at * step : (2 * at + 1) * step] for at in range(3)], axis=1)
    share_second = jnp.concatenate(
        [share_ffn[:, (2 * at + 1) * step : (2 * at + 2) * step] for at in range(3)], axis=1
    ).T
    g_query, g_key, g_value, g_out = unpack_heads(share_self)
    grad_qkv = jnp.stack([g_query, g_key, g_value], axis=1)
    c_query, c_key, c_value, c_out = unpack_heads(share_cross)
    for_enc = lax.ppermute(jnp.concatenate([c_key, c_value], axis=1), ("section", "zh"), [(1, 0), (3, 1)])
    for_dec = lax.ppermute(jnp.concatenate([c_query, c_out], axis=1), ("section", "zh"), [(1, 2), (3, 3)])
    cross = jnp.where(core == 0, for_enc, for_dec).astype(jnp.float32)

    norm_sums = jnp.stack(
        [
            pick(gain_a, gain_s),
            pick(gain_s, dec_gain_b),
            pick(enc_gain_c, dec_gain_c),
            pick(bias_a, bias_s),
            pick(bias_s, dec_bias_b),
            pick(enc_bias_c, dec_bias_c),
        ]
    )
    pieces = norm_sums.reshape((6, 2) + (2,) * count + (2, 2, -1))
    for axis, at in [("section", core)] + [
        (name, lax.axis_index(name)) for name in ["z%d" % z for z in range(count)] + ["ty", "tx"]
    ]:
        pieces = in_order(pieces, at, 1)
        pieces = pieces[:, 0] + over(pieces[:, 1], axis)
    norm_shares = swapped(pieces)
    return (
        hidden_out,
        hidden_grad,
        grad_qkv[None],
        g_out[None],
        cross[None, :, :width],
        cross[None, :, width:],
        share_first[None],
        share_second[None],
        norm_shares[None, :3],
        norm_shares[None, 3:],
    )


def solution(mesh):
    _, dp_count, _ = mesh.devices.shape
    count = (dp_count // 2).bit_length() - 1
    dp = ("zh",) + tuple("z%d" % at for at in range(count))
    tensor = ("ty", "tx")
    split = Mesh(mesh.devices.reshape((2, 2) + (2,) * count + (2, 2)), ("section",) + dp + tensor)
    rows = P("section", None, dp, tensor, None)
    in_specs = (
        rows,
        rows,
        P(None, None, dp, None),
        P("section", dp, None, tensor),
        P("section", dp, tensor),
        P("section", dp, tensor),
        P("section", dp, tensor),
        P("section", dp, tensor),
        P("section", tensor, dp),
        P("section", None, None),
        P("section", None, None),
    )
    out_specs = (
        rows,
        rows,
        P("section", dp, None, tensor),
        P("section", dp, tensor),
        P("section", dp, tensor),
        P("section", dp, tensor),
        P("section", dp, tensor),
        P("section", tensor, dp),
        P("section", None, dp + tensor),
        P("section", None, dp + tensor),
    )
    return jax.shard_map(
        functools.partial(body, count), mesh=split, in_specs=in_specs, out_specs=out_specs, check_vma=False
    )
```

```python
import functools

import jax
import jax.numpy as jnp
from jax import lax
from jax.experimental import pallas as pl
from jax.experimental.pallas import tpu as pltpu
from jax.sharding import Mesh
from jax.sharding import PartitionSpec as P

HDIM = 64
LANES = 128
MASKED = -1e30
NORM_EPS = 1e-05
VMEM_BYTES = 56 * 1024 * 1024

SEG_LANES = 8
PART_LANE = 12

PARTS = 2
HEADS = ((0, 1, 2, 0, 0), (0, 1, 2, 1, 1), (1, 3, 0, 0, 1))


def mul(a, b):
    return jnp.dot(a, b, preferred_element_type=jnp.float32)


def mul_nt(a, b):
    return lax.dot_general(a, b, (((1,), (1,)), ((), ())), preferred_element_type=jnp.float32)


def mul_tn(a, b):
    return lax.dot_general(a, b, (((0,), (0,)), ((), ())), preferred_element_type=jnp.float32)


def tile_of(values, index):
    return values[:, index * LANES : (index + 1) * LANES]


def lane_ids(rows):
    return lax.broadcasted_iota(jnp.int32, (rows, LANES), 1)


def half_mask(rows, half):
    lanes = lane_ids(rows)
    return lanes >= HDIM if half else lanes < HDIM


def in_parts(base, column):
    lanes = lane_ids(base.shape[0])
    high = column.astype(jnp.bfloat16).astype(jnp.float32)
    rest = column - high
    middle = rest.astype(jnp.bfloat16).astype(jnp.float32)
    low = rest - middle
    parts = jnp.where(
        lanes == PART_LANE,
        high,
        jnp.where(lanes == PART_LANE + 1, middle, jnp.where(lanes == PART_LANE + 2, low, base)),
    )
    return parts.astype(jnp.bfloat16)


def with_triangle(scores, tri, at):
    size = tri.shape[1]
    pieces = []
    if at > 0:
        pieces.append(scores[:, : at * size])
    pieces.append(scores[:, at * size : (at + 1) * size] + tri)
    pieces.append(scores[:, (at + 1) * size :])
    return jnp.concatenate(pieces, axis=1)


def assemble(core, half, own_refs, peer_refs, w_ref):
    mine = pl.multiple_of(core * half, half)
    other = pl.multiple_of((1 - core) * half, half)
    for part, (own_ref, peer_ref) in enumerate(zip(own_refs, peer_refs)):
        width = own_ref.shape[2]
        columns = slice(part * width, (part + 1) * width)
        w_ref[pl.ds(mine, half), columns] = own_ref[0]
        w_ref[pl.ds(other, half), columns] = peer_ref[0]


def hand_out(core, half, g_ref, keep_refs, send_refs):
    mine = pl.multiple_of(core * half, half)
    other = pl.multiple_of((1 - core) * half, half)
    for part, (keep_ref, send_ref) in enumerate(zip(keep_refs, send_refs)):
        width = keep_ref.shape[2]
        columns = slice(part * width, (part + 1) * width)
        keep_ref[0] = g_ref[pl.ds(mine, half), columns]
        send_ref[0] = g_ref[pl.ds(other, half), columns]


def scaled_queries(q_ref, at, q_tile, q_half):
    queries = q_ref[0, at, q_tile * LANES : (q_tile + 1) * LANES] * 0.125
    return jnp.where(half_mask(queries.shape[0], q_half), queries, 0).astype(jnp.bfloat16)


def units_of(total, rows):
    return [
        (slice(part * rows, (part + 1) * rows), part, head)
        for part in range(total // rows)
        for head in range(len(HEADS))
    ]


def attend_kernel(causal, core_ref, xq_ref, xkv_ref, *refs):
    own_refs, peer_refs = refs[:PARTS], refs[PARTS : 2 * PARTS]
    qx_ref, kx_ref, tri_ref, o_ref, q_ref, kv_ref, c_ref, l_ref, w_ref = refs[2 * PARTS :]
    block = pl.program_id(0)
    assemble(core_ref[0], own_refs[0].shape[1], own_refs, peer_refs, w_ref)
    q_ref[0] = mul(xq_ref[...], w_ref[:, : 2 * LANES]).astype(jnp.bfloat16)
    kv_ref[0] = mul(xkv_ref[...], w_ref[:, LANES : 5 * LANES]).astype(jnp.bfloat16)
    rows = tri_ref.shape[0]
    low = half_mask(rows, 0)

    def scores_of(at, part, head):
        q_tile, k_tile, _, q_half, _ = HEADS[head]
        keys = kv_ref[0, :, k_tile * LANES : (k_tile + 1) * LANES]
        scores = mul_nt(
            jnp.concatenate([scaled_queries(q_ref, at, q_tile, q_half), qx_ref[at, :]], axis=1),
            jnp.concatenate([keys, kx_ref[...]], axis=1),
        )
        return with_triangle(scores, tri_ref[...], part) if causal else scores

    units = units_of(q_ref.shape[1], rows)
    ahead = scores_of(*units[0])
    contexts, totals = [], None
    for index, (at, part, head) in enumerate(units):
        scores = ahead
        if index + 1 < len(units):
            ahead = scores_of(*units[index + 1])
        v_tile = HEADS[head][2]
        values = kv_ref[0, :, v_tile * LANES : (v_tile + 1) * LANES]
        highest = jnp.max(scores, axis=1, keepdims=True)
        weights = jnp.exp(scores - highest)
        sums = jnp.sum(weights, axis=1, keepdims=True)
        contexts.append(mul(weights.astype(jnp.bfloat16), values) / sums)
        logs = jnp.broadcast_to(highest + jnp.log(sums), (rows, LANES))
        totals = logs if head == 0 else jnp.where(lane_ids(rows) == head, logs, totals)
        if head == len(HEADS) - 1:
            c_ref[0, at, :LANES] = jnp.where(low, 0, contexts[2]).astype(jnp.bfloat16)
            c_ref[0, at, LANES:] = jnp.where(low, contexts[0], contexts[1]).astype(jnp.bfloat16)
            l_ref[0, at, :] = totals
            contexts = []
    out = mul_nt(c_ref[0], w_ref[:, 4 * LANES :])

    @pl.when(block == 0)
    def _():
        o_ref[...] = out

    @pl.when(block > 0)
    def _():
        o_ref[...] += out


def attend_back_kernel(causal, core_ref, do_ref, xq_ref, xkv_ref, *refs):
    own_refs, peer_refs = refs[:PARTS], refs[PARTS : 2 * PARTS]
    q_ref, kv_ref, c_ref, l_ref, qx_ref, kx_ref, tri_ref, dxq_ref, dxkv_ref, *refs = refs[2 * PARTS :]
    keep_refs, send_refs = refs[:PARTS], refs[PARTS : 2 * PARTS]
    w_ref, dkv_ref, dq_ref, g_ref = refs[2 * PARTS :]
    block = pl.program_id(0)
    rows = tri_ref.shape[0]
    half = own_refs[0].shape[1]
    assemble(core_ref[0], half, own_refs, peer_refs, w_ref)
    d_context = mul(do_ref[...], w_ref[:, 4 * LANES :]).astype(jnp.bfloat16)
    low = half_mask(rows, 0)

    def products_of(at, part, head):
        q_tile, k_tile, v_tile, q_half, v_half = HEADS[head]
        c_tile = 0 if head == 2 else 1
        keys = kv_ref[0, :, k_tile * LANES : (k_tile + 1) * LANES]
        values = kv_ref[0, :, v_tile * LANES : (v_tile + 1) * LANES]
        queries = scaled_queries(q_ref, at, q_tile, q_half)
        d_rows = jnp.where(half_mask(rows, v_half), tile_of(d_context[at], c_tile), 0).astype(jnp.bfloat16)
        total = l_ref[0, at, head : head + 1]
        scores = mul_nt(
            jnp.concatenate([queries, in_parts(qx_ref[at, :].astype(jnp.float32), -total)], axis=1),
            jnp.concatenate([keys, kx_ref[...]], axis=1),
        )
        if causal:
            scores = with_triangle(scores, tri_ref[...], part)
        return scores, mul_nt(d_rows, values), queries, d_rows, keys

    units = units_of(q_ref.shape[1], rows)
    ahead = products_of(*units[0])
    d_queries = []
    for index, (at, part, head) in enumerate(units):
        scores, d_probs, queries, d_rows, keys = ahead
        if index + 1 < len(units):
            ahead = products_of(*units[index + 1])
        _, k_tile, v_tile, _, _ = HEADS[head]
        probs = jnp.exp(scores)
        inner = jnp.sum(probs * d_probs, axis=1, keepdims=True)
        d_scores = (probs * (d_probs - inner)).astype(jnp.bfloat16)
        d_values = mul_tn(probs.astype(jnp.bfloat16), d_rows)
        d_keys = mul_tn(d_scores, queries)
        d_queries.append(mul(d_scores, keys) * 0.125)
        k_at = slice(k_tile * LANES, (k_tile + 1) * LANES)
        v_at = slice(v_tile * LANES, (v_tile + 1) * LANES)
        if part == 0 and head != 1:
            dkv_ref[:, k_at] = d_keys
            dkv_ref[:, v_at] = d_values
        else:
            dkv_ref[:, k_at] += d_keys
            dkv_ref[:, v_at] += d_values
        if head == len(HEADS) - 1:
            dq_ref[at, :LANES] = jnp.where(low, d_queries[0], d_queries[1]).astype(jnp.bfloat16)
            dq_ref[at, LANES:] = jnp.where(low, d_queries[2], 0).astype(jnp.bfloat16)
            d_queries = []
    d_pair = dkv_ref[...].astype(jnp.bfloat16)
    d_query = dq_ref[...]
    d_xq = mul_nt(d_query, w_ref[:, : 2 * LANES])
    d_xkv = mul_nt(d_pair, w_ref[:, LANES : 5 * LANES])

    @pl.when(block == 0)
    def _():
        dxq_ref[...] = d_xq
        dxkv_ref[...] = d_xkv

    @pl.when(block > 0)
    def _():
        dxq_ref[...] += d_xq
        dxkv_ref[...] += d_xkv

    grad_q = mul_tn(xq_ref[...], d_query)
    grad_kv = mul_tn(xkv_ref[...], d_pair)
    grad_o = mul_tn(do_ref[...], c_ref[0])
    g_ref[:, :LANES] = grad_q[:, :LANES].astype(jnp.bfloat16)
    g_ref[:, LANES : 2 * LANES] = (grad_q[:, LANES:] + grad_kv[:, :LANES]).astype(jnp.bfloat16)
    g_ref[:, 2 * LANES : 4 * LANES] = grad_kv[:, LANES : 3 * LANES].astype(jnp.bfloat16)
    g_ref[:, 4 * LANES : 5 * LANES] = (grad_kv[:, 3 * LANES :] + grad_o[:, :LANES]).astype(jnp.bfloat16)
    g_ref[:, 5 * LANES :] = grad_o[:, LANES:].astype(jnp.bfloat16)
    hand_out(core_ref[0], half, g_ref, keep_refs, send_refs)


def whole(shape):
    return pl.BlockSpec(shape, lambda j: (0,) * len(shape))


def per_block(shape):
    return pl.BlockSpec((1,) + shape, lambda j: (j,) + (0,) * len(shape))


FLAG = pl.BlockSpec(memory_space=pltpu.SMEM)
PARAMS = pltpu.CompilerParams(vmem_limit_bytes=VMEM_BYTES)
shape = jax.ShapeDtypeStruct


def cost(micros, moved):
    return pl.CostEstimate(flops=int(micros * 1.15e9), bytes_accessed=int(moved), transcendentals=0)


def attend(core, xq, xkv, weights, extras, causal):
    rows, width = xq.shape
    keys = xkv.shape[0]
    blocks = weights[0].shape[0]
    qx, kx, tri = extras
    return pl.pallas_call(
        functools.partial(attend_kernel, causal),
        grid=(blocks,),
        in_specs=[FLAG, whole((rows, width)), whole((keys, width))]
        + [per_block(part.shape[1:]) for part in weights]
        + [whole(qx.shape), whole(kx.shape), whole(tri.shape)],
        out_specs=[
            whole((rows, width)),
            per_block((rows, 2 * LANES)),
            per_block((keys, 4 * LANES)),
            per_block((rows, 2 * LANES)),
            per_block((rows, LANES)),
        ],
        out_shape=[
            shape((rows, width), jnp.float32),
            shape((blocks, rows, 2 * LANES), jnp.bfloat16),
            shape((blocks, keys, 4 * LANES), jnp.bfloat16),
            shape((blocks, rows, 2 * LANES), jnp.bfloat16),
            shape((blocks, rows, LANES), jnp.float32),
        ],
        scratch_shapes=[pltpu.VMEM((width, 6 * LANES), jnp.bfloat16)],
        compiler_params=PARAMS,
        cost_estimate=cost(20, 24 * 2**20),
        name="attend_self" if causal else "attend_cross",
    )(core, xq, xkv, *weights, qx, kx, tri)


def attend_back(core, d_out, xq, xkv, weights, kept, extras, causal):
    rows, width = xq.shape
    keys = xkv.shape[0]
    blocks = weights[0].shape[0]
    qx, kx, tri = extras
    out = pl.pallas_call(
        functools.partial(attend_back_kernel, causal),
        grid=(blocks,),
        in_specs=[FLAG, whole((rows, width)), whole((rows, width)), whole((keys, width))]
        + [per_block(part.shape[1:]) for part in weights]
        + [
            per_block((rows, 2 * LANES)),
            per_block((keys, 4 * LANES)),
            per_block((rows, 2 * LANES)),
            per_block((rows, LANES)),
            whole(qx.shape),
            whole(kx.shape),
            whole(tri.shape),
        ],
        out_specs=[whole((rows, width)), whole((keys, width))]
        + [per_block(part.shape[1:]) for part in weights],
        out_shape=[shape((rows, width), jnp.float32), shape((keys, width), jnp.float32)]
        + [shape(part.shape, jnp.bfloat16) for part in weights],
        scratch_shapes=[
            pltpu.VMEM((width, 6 * LANES), jnp.bfloat16),
            pltpu.VMEM((keys, 4 * LANES), jnp.float32),
            pltpu.VMEM((rows, 2 * LANES), jnp.bfloat16),
            pltpu.VMEM((width, 6 * LANES), jnp.bfloat16),
        ],
        compiler_params=PARAMS,
        cost_estimate=cost(40, 24 * 2**20),
        name="attend_self_back" if causal else "attend_cross_back",
    )(core, d_out, xq, xkv, *weights, *kept, qx, kx, tri)
    return out[0], out[1], out[2 : 2 + PARTS], out[2 + PARTS :]


def ffn_kernel(core_ref, x_ref, *refs):
    own_refs, peer_refs = refs[:PARTS], refs[PARTS : 2 * PARTS]
    z_ref, g_ref, slope_ref, w_ref = refs[2 * PARTS :]
    block = pl.program_id(0)
    assemble(core_ref[0], own_refs[0].shape[1], own_refs, peer_refs, w_ref)
    units = own_refs[0].shape[2]
    inner = mul(x_ref[...], w_ref[:, :units])
    spread = 0.5 * (1.0 + lax.erf(inner * (0.5**0.5)))
    bell = jnp.exp(-0.5 * inner * inner) * 0.3989422804014327
    active = (inner * spread).astype(jnp.bfloat16)
    g_ref[0] = active
    slope_ref[0] = (spread + inner * bell).astype(jnp.bfloat16)
    out = mul_nt(active, w_ref[:, units:])

    @pl.when(block == 0)
    def _():
        z_ref[...] = out

    @pl.when(block > 0)
    def _():
        z_ref[...] += out


def ffn(core, x, weights):
    rows, width = x.shape
    blocks, _, units = weights[0].shape
    return pl.pallas_call(
        ffn_kernel,
        grid=(blocks,),
        in_specs=[FLAG, whole((rows, width))] + [per_block(part.shape[1:]) for part in weights],
        out_specs=[whole((rows, width)), per_block((rows, units)), per_block((rows, units))],
        out_shape=[
            shape((rows, width), jnp.float32),
            shape((blocks, rows, units), jnp.bfloat16),
            shape((blocks, rows, units), jnp.bfloat16),
        ],
        scratch_shapes=[pltpu.VMEM((width, 2 * units), jnp.bfloat16)],
        compiler_params=PARAMS,
        cost_estimate=cost(12, rows * units * blocks * 16),
        name="ffn",
    )(core, x, *weights)


def ffn_back_kernel(core_ref, dz_ref, *refs):
    own_refs, peer_refs = refs[:PARTS], refs[PARTS : 2 * PARTS]
    slope_ref, dx_ref, dh_ref, w_ref = refs[2 * PARTS :]
    block = pl.program_id(0)
    assemble(core_ref[0], own_refs[0].shape[1], own_refs, peer_refs, w_ref)
    units = own_refs[0].shape[2]
    d_active = mul(dz_ref[...], w_ref[:, units:])
    d_inner = (d_active * slope_ref[0].astype(jnp.float32)).astype(jnp.bfloat16)
    dh_ref[0] = d_inner
    out = mul_nt(d_inner, w_ref[:, :units])

    @pl.when(block == 0)
    def _():
        dx_ref[...] = out

    @pl.when(block > 0)
    def _():
        dx_ref[...] += out


def ffn_back(core, dz, weights, slope):
    rows, width = dz.shape
    blocks, _, units = weights[0].shape
    return pl.pallas_call(
        ffn_back_kernel,
        grid=(blocks,),
        in_specs=[FLAG, whole((rows, width))]
        + [per_block(part.shape[1:]) for part in weights]
        + [per_block((rows, units))],
        out_specs=[whole((rows, width)), per_block((rows, units))],
        out_shape=[
            shape((rows, width), jnp.float32),
            shape((blocks, rows, units), jnp.bfloat16),
        ],
        scratch_shapes=[pltpu.VMEM((width, 2 * units), jnp.bfloat16)],
        compiler_params=PARAMS,
        cost_estimate=cost(12, rows * units * blocks * 12),
        name="ffn_back",
    )(core, dz, *weights, slope)


def ffn_grads_kernel(core_ref, x_ref, dz_ref, g_ref, dh_ref, *refs):
    keep_refs, send_refs, w_ref = refs[:PARTS], refs[PARTS : 2 * PARTS], refs[2 * PARTS]
    units = keep_refs[0].shape[2]
    w_ref[:, :units] = mul_tn(x_ref[...], dh_ref[0]).astype(jnp.bfloat16)
    w_ref[:, units:] = mul_tn(dz_ref[...], g_ref[0]).astype(jnp.bfloat16)
    hand_out(core_ref[0], keep_refs[0].shape[1], w_ref, keep_refs, send_refs)


def ffn_grads(core, x, dz, active, d_inner, like):
    rows, width = x.shape
    blocks, _, units = active.shape
    out = pl.pallas_call(
        ffn_grads_kernel,
        grid=(blocks,),
        in_specs=[
            FLAG,
            whole((rows, width)),
            whole((rows, width)),
            per_block((rows, units)),
            per_block((rows, units)),
        ],
        out_specs=[per_block(part.shape[1:]) for part in like],
        out_shape=[shape(part.shape, jnp.bfloat16) for part in like],
        scratch_shapes=[pltpu.VMEM((width, 2 * units), jnp.bfloat16)],
        compiler_params=PARAMS,
        cost_estimate=cost(10, rows * units * blocks * 16),
        name="ffn_grads",
    )(core, x, dz, active, d_inner)
    return out[:PARTS], out[PARTS:]


def layer_norm(values, gain_row, bias_row):
    average = jnp.mean(values, axis=-1, keepdims=True)
    centered = values - average
    variance = jnp.mean(centered * centered, axis=-1, keepdims=True)
    return centered * lax.rsqrt(variance + NORM_EPS) * gain_row + bias_row


def norm_back(values, gain_row, bias_row, upstream):
    _, pullback = jax.vjp(layer_norm, values, gain_row, bias_row)
    return pullback(upstream)


def low(values):
    return values.astype(jnp.bfloat16)


SWAP = [(0, 0), (1, 2), (2, 1), (3, 3)]
PAIR = [(0, 1), (1, 0)]


def swapped(x, axis="zh"):
    return lax.ppermute(x, ("section", axis), SWAP)


def to_work(other):
    return [
        (8 * s + 4 * z + 2 * y + x, 8 * y + 4 * s + 2 * z + (x ^ other))
        for s in (0, 1)
        for z in (0, 1)
        for y in (0, 1)
        for x in (0, 1)
    ]


def to_home(other):
    return [(work, home) for home, work in to_work(other)]


def over(x, axis):
    return lax.ppermute(x, axis, PAIR)


def in_order(x, flag, axis):
    return jnp.where(flag == 1, jnp.flip(x, axis), x)


def pack_heads(query, key, value, out):
    pair = 2 * HDIM
    return jnp.concatenate(
        [
            query,
            value[:, pair:],
            key[:, :pair],
            value[:, :pair],
            key[:, pair:],
            out[:, pair:],
            out[:, :pair],
        ],
        axis=1,
    )


def unpack_heads(packed):
    part = [packed[:, at * HDIM : (at + 1) * HDIM] for at in range(12)]
    query = jnp.concatenate(part[0:3], axis=1)
    key = jnp.concatenate([part[4], part[5], part[8]], axis=1)
    value = jnp.concatenate([part[6], part[7], part[3]], axis=1)
    out = jnp.concatenate([part[10], part[11], part[9]], axis=1)
    return query, key, value, out


def after(x, *earlier):
    return lax.optimization_barrier((x,) + earlier)[0]


DIAGONAL = [(0, 3), (1, 2), (2, 1), (3, 0)]


def over_diagonal(x):
    return lax.ppermute(x, ("ty", "tx"), DIAGONAL)


def plane_gathered(x):
    return jnp.stack([x, over(x, "tx"), over(x, "ty"), over_diagonal(x)])


def plane_summed(x):
    first, second, third, fourth = (x[at] for at in range(4))
    terms = [first, over(second, "tx"), over(third, "ty"), over_diagonal(fourth)]
    return low(sum(term.astype(jnp.float32) for term in terms))


def rows_gathered(x, count):
    for at in reversed(range(count)):
        axis = "z%d" % at
        both = in_order(jnp.stack([x, over(x, axis)], axis=-3), lax.axis_index(axis), x.ndim - 2)
        x = both.reshape(x.shape[:-2] + (2 * x.shape[-2], x.shape[-1]))
    return x


def rows_summed(x, count):
    for at in range(count):
        axis = "z%d" % at
        halves = x.reshape(x.shape[:-2] + (2, x.shape[-2] // 2, x.shape[-1]))
        halves = in_order(halves, lax.axis_index(axis), x.ndim - 2)
        x = plus(halves[..., 0, :, :], over(halves[..., 1, :, :], axis))
    return x


def spread(packed, count):
    first, second = jnp.split(packed, 2, axis=1)
    own = [plane_gathered(rows_gathered(first, count)), rows_gathered(plane_gathered(second), count)]
    return own + [over(part, "section") for part in own]


def plus(first, second):
    return low(first.astype(jnp.float32) + second.astype(jnp.float32))


def collected(keep, send, count):
    first, second = (plus(mine, over(other, "section")) for mine, other in zip(keep, send))
    parts = [rows_summed(plane_summed(first), count), plane_summed(rows_summed(second, count))]
    return jnp.concatenate(parts, axis=1)


def body(
    count,
    hidden,
    cotangent,
    segments,
    sa_qkv,
    sa_out,
    cross_one,
    cross_two,
    ffn_in,
    ffn_out,
    norm_gain,
    norm_bias,
):
    core = lax.axis_index("section")
    core_flag = core.reshape(1)
    x_at, y_at, zh_at = lax.axis_index("tx"), lax.axis_index("ty"), lax.axis_index("zh")
    on_encoder = zh_at == 0
    quarter = hidden.shape[3]

    def pick(first, second):
        return jnp.where(on_encoder, first, second)

    def rows_in(x):
        mine, other = in_order(x[0, :, 0], x_at, 0)
        whole_axes = ("section", "zh", "ty", "tx")
        both = [lax.ppermute(mine, whole_axes, to_work(0)), lax.ppermute(other, whole_axes, to_work(1))]
        return in_order(jnp.stack(both), x_at, 0).reshape(2 * quarter, -1)

    def rows_out(x):
        mine, other = in_order(x.reshape(2, quarter, -1), x_at, 0)
        whole_axes = ("section", "zh", "ty", "tx")
        both = [lax.ppermute(mine, whole_axes, to_home(0)), lax.ppermute(other, whole_axes, to_home(1))]
        return in_order(jnp.stack(both), x_at, 0)[None, :, None]

    packed_self = pack_heads(sa_qkv[0, :, 0], sa_qkv[0, :, 1], sa_qkv[0, :, 2], sa_out[0])
    with jax.named_scope("self_weights"):
        w_self = spread(swapped(packed_self), count)
    with jax.named_scope("hidden_in"):
        rows_here = rows_in(hidden)
        rows_all = jnp.concatenate([rows_here, over(rows_here, "section")], axis=0)
    with jax.named_scope("norms_in"):
        norms = swapped(jnp.concatenate([norm_gain[0], norm_bias[0]], axis=0))
        gains, biases = norms[:3], norms[3:]
        seg_own = segments[:, :, 0].astype(jnp.float32)
        seg_here = jnp.where(y_at == zh_at, seg_own, over(seg_own, "zh")).astype(jnp.int32)
    with jax.named_scope("ffn_weights"):
        packed_ffn = jnp.concatenate([ffn_in[0], ffn_out[0].T], axis=1)
        w_ffn = spread(swapped(packed_ffn), count)
    units = ffn_in.shape[2]
    width = cross_one.shape[2]

    both_segments = in_order(seg_here, x_at, 1)[:, 0]
    ordered = in_order(both_segments.reshape(2, 2, 2 * quarter), core, 1).reshape(2, 4 * quarter)
    source_seg, target_seg = ordered[0], ordered[1]
    self_seg = pick(source_seg, target_seg)
    places = jnp.arange(4)
    quarter_of = jnp.repeat(2 * ((places // 2) ^ core) + places % 2, quarter)
    lanes = jnp.arange(LANES)[None, :]

    def key_extras(seg):
        differs = jnp.logical_and(lanes < SEG_LANES, seg[:, None] != lanes)
        later = jnp.logical_and(
            jnp.logical_and(lanes >= SEG_LANES, lanes < PART_LANE),
            quarter_of[:, None] > lanes - SEG_LANES,
        )
        part = jnp.logical_and(lanes >= PART_LANE, lanes < PART_LANE + 3)
        return jnp.where(differs | later | part, 1.0, 0.0).astype(jnp.bfloat16)

    def query_extras(seg, causal):
        seg, at = seg[: 2 * quarter], quarter_of[: 2 * quarter]
        same = seg[:, None] == lanes
        here = jnp.logical_and(at[:, None] + SEG_LANES == lanes, causal)
        return jnp.where(same | here, MASKED, 0.0).astype(jnp.bfloat16)

    at_row = jnp.arange(quarter)
    later_key = jnp.logical_and(at_row[None, :] > at_row[:, None], jnp.logical_not(on_encoder))
    tri = jnp.where(later_key, MASKED, 0.0).astype(jnp.float32)
    self_extras = (query_extras(self_seg, jnp.logical_not(on_encoder)), key_extras(self_seg), tri)
    cross_extras = (query_extras(target_seg, False), key_extras(source_seg), tri)

    start = rows_all.astype(jnp.float32)
    start = pick(layer_norm(start, gains[0], biases[0]), start)
    start_here = start[: 2 * quarter]
    start_low = low(start)
    self_gain, self_bias = pick(gains[1], gains[0]), pick(biases[1], biases[0])
    with jax.named_scope("cotangent_in"):
        cot = rows_in(after(cotangent, rows_all)).astype(jnp.float32)
    self_out, *kept_self = attend(core_flag, start_low[: 2 * quarter], start_low, w_self, self_extras, True)
    self_total = start_here + self_out
    middle = layer_norm(self_total, self_gain, self_bias)
    middle_low = low(middle)

    with jax.named_scope("cross_weights"):
        cross_low = after(jnp.concatenate([cross_one[0], cross_two[0]], axis=1), middle_low)
        pair_kv = lax.ppermute(cross_low, ("section", "zh"), [(0, 1), (1, 3)])
        pair_qo = lax.ppermute(cross_low, ("section", "zh"), [(2, 1), (3, 3)])
        w_cross = spread(
            pack_heads(pair_qo[:, :width], pair_kv[:, :width], pair_kv[:, width:], pair_qo[:, width:]), count
        )

    enc_out, enc_active, enc_slope = ffn(core_flag, middle_low, w_ffn)
    enc_total = middle + enc_out
    encoded = low(layer_norm(enc_total, gains[2], biases[2]))
    with jax.named_scope("memory"):
        memory_here = lax.ppermute(encoded, "zh", [(0, 1)])
        memory = jnp.concatenate([memory_here, over(memory_here, "section")], axis=0)

    cross_out, *kept_cross = attend(core_flag, middle_low, memory, w_cross, cross_extras, False)
    cross_total = middle + cross_out
    crossed = layer_norm(cross_total, gains[1], biases[1])
    crossed_low = low(crossed)
    dec_out, dec_active, dec_slope = ffn(core_flag, crossed_low, w_ffn)
    dec_total = crossed + dec_out
    decoded = low(layer_norm(dec_total, gains[2], biases[2]))
    with jax.named_scope("hidden_out"):
        hidden_out = rows_out(pick(encoded, decoded))

    d_dec_total, dec_gain_c, dec_bias_c = norm_back(dec_total, gains[2], biases[2], cot)
    d_dec_low = low(d_dec_total)
    d_after, dec_inner = ffn_back(core_flag, d_dec_low, w_ffn, dec_slope)
    d_cross_total, dec_gain_b, dec_bias_b = norm_back(
        cross_total, gains[1], biases[1], d_dec_total + d_after
    )
    d_middle_part, d_memory, cross_keep, cross_send = attend_back(
        core_flag, low(d_cross_total), middle_low, memory, w_cross, kept_cross, cross_extras, False
    )
    with jax.named_scope("d_memory"):
        d_memory_here = d_memory[: 2 * quarter] + over(low(d_memory[2 * quarter :]), "section").astype(jnp.float32)
        d_encoded = lax.ppermute(low(d_memory_here), "zh", [(1, 0)]).astype(jnp.float32) + cot
    with jax.named_scope("cross_sums"):
        share_cross = collected(cross_keep, cross_send, count)

    d_enc_total, enc_gain_c, enc_bias_c = norm_back(enc_total, gains[2], biases[2], d_encoded)
    d_enc_low = low(d_enc_total)
    d_enc_middle, enc_inner = ffn_back(core_flag, d_enc_low, w_ffn, enc_slope)
    ffn_keep, ffn_send = ffn_grads(
        core_flag,
        pick(middle_low, crossed_low),
        pick(d_enc_low, d_dec_low),
        pick(enc_active, dec_active),
        pick(enc_inner, dec_inner),
        w_ffn,
    )

    d_middle = pick(d_enc_total + d_enc_middle, d_cross_total + d_middle_part)
    d_self_total, gain_s, bias_s = norm_back(self_total, self_gain, self_bias, d_middle)
    d_start_q, d_start_kv, self_keep, self_send = attend_back(
        core_flag, after(low(d_self_total), *ffn_keep), start_low[: 2 * quarter], start_low, w_self, kept_self, self_extras, True
    )
    d_start = d_self_total + d_start_q + d_start_kv[: 2 * quarter]
    with jax.named_scope("d_start"):
        d_start = d_start + over(low(d_start_kv[2 * quarter :]), "section").astype(jnp.float32)
    d_source, gain_a, bias_a = norm_back(
        rows_here.astype(jnp.float32), gains[0], biases[0], d_start
    )
    with jax.named_scope("hidden_grad"):
        hidden_grad = rows_out(low(pick(d_source, d_start))).astype(jnp.float32)

    with jax.named_scope("ffn_sums"):
        share_ffn = swapped(collected(ffn_keep, ffn_send, count)).astype(jnp.float32)
    share_first, share_second = share_ffn[:, :units], share_ffn[:, units:].T
    with jax.named_scope("self_sums"):
        share_self = swapped(collected(self_keep, self_send, count)).astype(jnp.float32)
    g_query, g_key, g_value, g_out = unpack_heads(share_self)
    grad_qkv = jnp.stack([g_query, g_key, g_value], axis=1)
    c_query, c_key, c_value, c_out = unpack_heads(share_cross)
    for_enc = lax.ppermute(jnp.concatenate([c_key, c_value], axis=1), ("section", "zh"), [(1, 0), (3, 1)])
    for_dec = lax.ppermute(jnp.concatenate([c_query, c_out], axis=1), ("section", "zh"), [(1, 2), (3, 3)])
    cross = jnp.where(core == 0, for_enc, for_dec).astype(jnp.float32)

    norm_sums = jnp.stack(
        [
            pick(gain_a, gain_s),
            pick(gain_s, dec_gain_b),
            pick(enc_gain_c, dec_gain_c),
            pick(bias_a, bias_s),
            pick(bias_s, dec_bias_b),
            pick(enc_bias_c, dec_bias_c),
        ]
    )
    pieces = norm_sums.reshape((6, 2) + (2,) * count + (2, 2, -1))
    for axis, at in [("section", core)] + [
        (name, lax.axis_index(name)) for name in ["z%d" % z for z in range(count)] + ["ty", "tx"]
    ]:
        pieces = in_order(pieces, at, 1)
        pieces = pieces[:, 0] + over(pieces[:, 1], axis)
    norm_shares = swapped(pieces)
    return (
        hidden_out,
        hidden_grad,
        grad_qkv[None],
        g_out[None],
        cross[None, :, :width],
        cross[None, :, width:],
        share_first[None],
        share_second[None],
        norm_shares[None, :3],
        norm_shares[None, 3:],
    )


def solution(mesh):
    _, dp_count, _ = mesh.devices.shape
    count = (dp_count // 2).bit_length() - 1
    dp = ("zh",) + tuple("z%d" % at for at in range(count))
    tensor = ("ty", "tx")
    split = Mesh(mesh.devices.reshape((2, 2) + (2,) * count + (2, 2)), ("section",) + dp + tensor)
    rows = P("section", None, dp, tensor, None)
    in_specs = (
        rows,
        rows,
        P(None, None, dp, None),
        P("section", dp, None, tensor),
        P("section", dp, tensor),
        P("section", dp, tensor),
        P("section", dp, tensor),
        P("section", dp, tensor),
        P("section", tensor, dp),
        P("section", None, None),
        P("section", None, None),
    )
    out_specs = (
        rows,
        rows,
        P("section", dp, None, tensor),
        P("section", dp, tensor),
        P("section", dp, tensor),
        P("section", dp, tensor),
        P("section", dp, tensor),
        P("section", tensor, dp),
        P("section", None, dp + tensor),
        P("section", None, dp + tensor),
    )
    return jax.shard_map(
        functools.partial(body, count), mesh=split, in_specs=in_specs, out_specs=out_specs, check_vma=False
    )
```

```python
import functools

import jax
import jax.numpy as jnp
from jax import lax
from jax.experimental import pallas as pl
from jax.experimental.pallas import tpu as pltpu
from jax.sharding import Mesh
from jax.sharding import PartitionSpec as P

HDIM = 64
LANES = 128
MASKED = -1e30
NORM_EPS = 1e-05
VMEM_BYTES = 56 * 1024 * 1024

SEG_LANES = 8
PART_LANE = 12

PARTS = 2
HEADS = ((0, 1, 2, 0, 0), (0, 1, 2, 1, 1), (1, 3, 0, 0, 1))


def mul(a, b):
    return jnp.dot(a, b, preferred_element_type=jnp.float32)


def mul_nt(a, b):
    return lax.dot_general(a, b, (((1,), (1,)), ((), ())), preferred_element_type=jnp.float32)


def mul_tn(a, b):
    return lax.dot_general(a, b, (((0,), (0,)), ((), ())), preferred_element_type=jnp.float32)


def tile_of(values, index):
    return values[:, index * LANES : (index + 1) * LANES]


def lane_ids(rows):
    return lax.broadcasted_iota(jnp.int32, (rows, LANES), 1)


def half_mask(rows, half):
    lanes = lane_ids(rows)
    return lanes >= HDIM if half else lanes < HDIM


def in_parts(base, column):
    lanes = lane_ids(base.shape[0])
    high = column.astype(jnp.bfloat16).astype(jnp.float32)
    rest = column - high
    middle = rest.astype(jnp.bfloat16).astype(jnp.float32)
    low = rest - middle
    parts = jnp.where(
        lanes == PART_LANE,
        high,
        jnp.where(lanes == PART_LANE + 1, middle, jnp.where(lanes == PART_LANE + 2, low, base)),
    )
    return parts.astype(jnp.bfloat16)


def with_triangle(scores, tri, at):
    size = tri.shape[1]
    pieces = []
    if at > 0:
        pieces.append(scores[:, : at * size])
    pieces.append(scores[:, at * size : (at + 1) * size] + tri)
    pieces.append(scores[:, (at + 1) * size :])
    return jnp.concatenate(pieces, axis=1)


def assemble(core, half, own_refs, peer_refs, w_ref):
    mine = pl.multiple_of(core * half, half)
    other = pl.multiple_of((1 - core) * half, half)
    for part, (own_ref, peer_ref) in enumerate(zip(own_refs, peer_refs)):
        width = own_ref.shape[2]
        columns = slice(part * width, (part + 1) * width)
        w_ref[pl.ds(mine, half), columns] = own_ref[0]
        w_ref[pl.ds(other, half), columns] = peer_ref[0]


def hand_out(core, half, g_ref, keep_refs, send_refs):
    mine = pl.multiple_of(core * half, half)
    other = pl.multiple_of((1 - core) * half, half)
    for part, (keep_ref, send_ref) in enumerate(zip(keep_refs, send_refs)):
        width = keep_ref.shape[2]
        columns = slice(part * width, (part + 1) * width)
        keep_ref[0] = g_ref[pl.ds(mine, half), columns]
        send_ref[0] = g_ref[pl.ds(other, half), columns]


def scaled_queries(q_ref, at, q_tile, q_half):
    queries = q_ref[0, at, q_tile * LANES : (q_tile + 1) * LANES] * 0.125
    return jnp.where(half_mask(queries.shape[0], q_half), queries, 0).astype(jnp.bfloat16)


def units_of(total, rows):
    return [
        (slice(part * rows, (part + 1) * rows), part, head)
        for part in range(total // rows)
        for head in range(len(HEADS))
    ]


def attend_kernel(causal, core_ref, xq_ref, xkv_ref, *refs):
    own_refs, peer_refs = refs[:1], refs[1:2]
    qx_ref, kx_ref, tri_ref, o_ref, q_ref, kv_ref, c_ref, l_ref, w_ref = refs[2:]
    block = pl.program_id(0)
    assemble(core_ref[0], own_refs[0].shape[1], own_refs, peer_refs, w_ref)
    q_ref[0] = mul(xq_ref[...], w_ref[:, : 2 * LANES]).astype(jnp.bfloat16)
    kv_ref[0] = mul(xkv_ref[...], w_ref[:, LANES : 5 * LANES]).astype(jnp.bfloat16)
    rows = tri_ref.shape[0]
    low = half_mask(rows, 0)

    def scores_of(at, part, head):
        q_tile, k_tile, _, q_half, _ = HEADS[head]
        keys = kv_ref[0, :, k_tile * LANES : (k_tile + 1) * LANES]
        scores = mul_nt(
            jnp.concatenate([scaled_queries(q_ref, at, q_tile, q_half), qx_ref[at, :]], axis=1),
            jnp.concatenate([keys, kx_ref[...]], axis=1),
        )
        return with_triangle(scores, tri_ref[...], part) if causal else scores

    units = units_of(q_ref.shape[1], rows)
    ahead = scores_of(*units[0])
    contexts, totals = [], None
    for index, (at, part, head) in enumerate(units):
        scores = ahead
        if index + 1 < len(units):
            ahead = scores_of(*units[index + 1])
        v_tile = HEADS[head][2]
        values = kv_ref[0, :, v_tile * LANES : (v_tile + 1) * LANES]
        highest = jnp.max(scores, axis=1, keepdims=True)
        weights = jnp.exp(scores - highest)
        sums = jnp.sum(weights, axis=1, keepdims=True)
        contexts.append(mul(weights.astype(jnp.bfloat16), values) / sums)
        logs = jnp.broadcast_to(highest + jnp.log(sums), (rows, LANES))
        totals = logs if head == 0 else jnp.where(lane_ids(rows) == head, logs, totals)
        if head == len(HEADS) - 1:
            c_ref[0, at, :LANES] = jnp.where(low, 0, contexts[2]).astype(jnp.bfloat16)
            c_ref[0, at, LANES:] = jnp.where(low, contexts[0], contexts[1]).astype(jnp.bfloat16)
            l_ref[0, at, :] = totals
            contexts = []
    out = mul_nt(c_ref[0], w_ref[:, 4 * LANES :])

    @pl.when(block == 0)
    def _():
        o_ref[...] = out

    @pl.when(block > 0)
    def _():
        o_ref[...] += out


def attend_back_kernel(causal, core_ref, do_ref, xq_ref, xkv_ref, *refs):
    own_refs, peer_refs = refs[:1], refs[1:2]
    q_ref, kv_ref, c_ref, l_ref, qx_ref, kx_ref, tri_ref, dq_ref, dkv_ref, *refs = refs[2:]
    keep_refs, send_refs = refs[:1], refs[1:2]
    w_ref, sum_ref, g_ref = refs[2:]
    rows = tri_ref.shape[0]
    half = own_refs[0].shape[1]
    assemble(core_ref[0], half, own_refs, peer_refs, w_ref)
    d_context = mul(do_ref[...], w_ref[:, 4 * LANES :]).astype(jnp.bfloat16)
    low = half_mask(rows, 0)

    def products_of(at, part, head):
        q_tile, k_tile, v_tile, q_half, v_half = HEADS[head]
        c_tile = 0 if head == 2 else 1
        keys = kv_ref[0, :, k_tile * LANES : (k_tile + 1) * LANES]
        values = kv_ref[0, :, v_tile * LANES : (v_tile + 1) * LANES]
        queries = scaled_queries(q_ref, at, q_tile, q_half)
        d_rows = jnp.where(half_mask(rows, v_half), tile_of(d_context[at], c_tile), 0).astype(jnp.bfloat16)
        total = l_ref[0, at, head : head + 1]
        scores = mul_nt(
            jnp.concatenate([queries, in_parts(qx_ref[at, :].astype(jnp.float32), -total)], axis=1),
            jnp.concatenate([keys, kx_ref[...]], axis=1),
        )
        if causal:
            scores = with_triangle(scores, tri_ref[...], part)
        return scores, mul_nt(d_rows, values), queries, d_rows, keys

    units = units_of(q_ref.shape[1], rows)
    ahead = products_of(*units[0])
    d_queries = []
    for index, (at, part, head) in enumerate(units):
        scores, d_probs, queries, d_rows, keys = ahead
        if index + 1 < len(units):
            ahead = products_of(*units[index + 1])
        _, k_tile, v_tile, _, _ = HEADS[head]
        probs = jnp.exp(scores)
        inner = jnp.sum(probs * d_probs, axis=1, keepdims=True)
        d_scores = (probs * (d_probs - inner)).astype(jnp.bfloat16)
        d_values = mul_tn(probs.astype(jnp.bfloat16), d_rows)
        d_keys = mul_tn(d_scores, queries)
        d_queries.append(mul(d_scores, keys) * 0.125)
        k_at = slice(k_tile * LANES, (k_tile + 1) * LANES)
        v_at = slice(v_tile * LANES, (v_tile + 1) * LANES)
        if part == 0 and head != 1:
            sum_ref[:, k_at] = d_keys
            sum_ref[:, v_at] = d_values
        else:
            sum_ref[:, k_at] += d_keys
            sum_ref[:, v_at] += d_values
        if head == len(HEADS) - 1:
            dq_ref[0, at, :LANES] = jnp.where(low, d_queries[0], d_queries[1]).astype(jnp.bfloat16)
            dq_ref[0, at, LANES:] = jnp.where(low, d_queries[2], 0).astype(jnp.bfloat16)
            d_queries = []
    dkv_ref[0] = sum_ref[...].astype(jnp.bfloat16)
    grad_q = mul_tn(xq_ref[...], dq_ref[0])
    grad_kv = mul_tn(xkv_ref[...], dkv_ref[0])
    grad_o = mul_tn(do_ref[...], c_ref[0])
    g_ref[:, :LANES] = grad_q[:, :LANES].astype(jnp.bfloat16)
    g_ref[:, LANES : 2 * LANES] = (grad_q[:, LANES:] + grad_kv[:, :LANES]).astype(jnp.bfloat16)
    g_ref[:, 2 * LANES : 4 * LANES] = grad_kv[:, LANES : 3 * LANES].astype(jnp.bfloat16)
    g_ref[:, 4 * LANES : 5 * LANES] = (grad_kv[:, 3 * LANES :] + grad_o[:, :LANES]).astype(jnp.bfloat16)
    g_ref[:, 5 * LANES :] = grad_o[:, LANES:].astype(jnp.bfloat16)
    hand_out(core_ref[0], half, g_ref, keep_refs, send_refs)


def attend_inputs_kernel(count, core_ref, *refs):
    own_refs, peer_refs = refs[:1], refs[1:2]
    dq_refs, dkv_refs = refs[2 : 2 + count], refs[2 + count : 2 + 2 * count]
    dxq_ref, dxkv_ref, w_ref = refs[2 + 2 * count :]
    block = pl.program_id(0)
    assemble(core_ref[0], own_refs[0].shape[1], own_refs, peer_refs, w_ref)

    for at in range(count):

        @pl.when(block == at)
        def _():
            d_xq = mul_nt(dq_refs[at][0], w_ref[:, : 2 * LANES])
            d_xkv = mul_nt(dkv_refs[at][0], w_ref[:, LANES : 5 * LANES])
            dxq_ref[...] = d_xq if at == 0 else dxq_ref[...] + d_xq
            dxkv_ref[...] = d_xkv if at == 0 else dxkv_ref[...] + d_xkv


def whole(shape):
    return pl.BlockSpec(shape, lambda j: (0,) * len(shape))


def per_block(shape):
    return pl.BlockSpec((1,) + shape, lambda j: (j,) + (0,) * len(shape))


FLAG = pl.BlockSpec(memory_space=pltpu.SMEM)
PARAMS = pltpu.CompilerParams(vmem_limit_bytes=VMEM_BYTES)
shape = jax.ShapeDtypeStruct


def cost(micros, moved):
    return pl.CostEstimate(flops=int(micros * 1.15e9), bytes_accessed=int(moved), transcendentals=0)


def attend(core, xq, xkv, weights, extras, causal):
    rows, width = xq.shape
    keys = xkv.shape[0]
    blocks = weights[0].shape[0]
    qx, kx, tri = extras
    return pl.pallas_call(
        functools.partial(attend_kernel, causal),
        grid=(blocks,),
        in_specs=[FLAG, whole((rows, width)), whole((keys, width))]
        + [per_block(part.shape[1:]) for part in weights]
        + [whole(qx.shape), whole(kx.shape), whole(tri.shape)],
        out_specs=[
            whole((rows, width)),
            per_block((rows, 2 * LANES)),
            per_block((keys, 4 * LANES)),
            per_block((rows, 2 * LANES)),
            per_block((rows, LANES)),
        ],
        out_shape=[
            shape((rows, width), jnp.float32),
            shape((blocks, rows, 2 * LANES), jnp.bfloat16),
            shape((blocks, keys, 4 * LANES), jnp.bfloat16),
            shape((blocks, rows, 2 * LANES), jnp.bfloat16),
            shape((blocks, rows, LANES), jnp.float32),
        ],
        scratch_shapes=[pltpu.VMEM((width, 6 * LANES), jnp.bfloat16)],
        compiler_params=PARAMS,
        cost_estimate=cost(20, 24 * 2**20),
        name="attend_self" if causal else "attend_cross",
    )(core, xq, xkv, *weights, qx, kx, tri)


def attend_back(core, d_out, xq, xkv, weights, kept, extras, causal, first, count):
    rows, width = xq.shape
    keys = xkv.shape[0]
    qx, kx, tri = extras

    def block_of(of):
        return pl.BlockSpec((1,) + of, lambda j: (first + j,) + (0,) * len(of))

    grads = [shape((count,) + part.shape[1:], jnp.bfloat16) for part in weights]
    out = pl.pallas_call(
        functools.partial(attend_back_kernel, causal),
        grid=(count,),
        in_specs=[FLAG, whole((rows, width)), whole((rows, width)), whole((keys, width))]
        + [block_of(part.shape[1:]) for part in weights]
        + [
            block_of((rows, 2 * LANES)),
            block_of((keys, 4 * LANES)),
            block_of((rows, 2 * LANES)),
            block_of((rows, LANES)),
            whole(qx.shape),
            whole(kx.shape),
            whole(tri.shape),
        ],
        out_specs=[per_block((rows, 2 * LANES)), per_block((keys, 4 * LANES))]
        + [per_block(part.shape[1:]) for part in weights],
        out_shape=[
            shape((count, rows, 2 * LANES), jnp.bfloat16),
            shape((count, keys, 4 * LANES), jnp.bfloat16),
        ]
        + grads,
        scratch_shapes=[
            pltpu.VMEM((width, 6 * LANES), jnp.bfloat16),
            pltpu.VMEM((keys, 4 * LANES), jnp.float32),
            pltpu.VMEM((width, 6 * LANES), jnp.bfloat16),
        ],
        compiler_params=PARAMS,
        cost_estimate=cost(10 * count, 6 * 2**20 * count),
        name="attend_self_back" if causal else "attend_cross_back",
    )(core, d_out, xq, xkv, *weights, *kept, qx, kx, tri)
    return out[0], out[1], out[2:3], out[3:]


def attend_inputs(core, weights, d_queries, d_pairs):
    blocks, half, _ = weights[0].shape
    width = 2 * half
    rows, keys = d_queries[0].shape[1], d_pairs[0].shape[1]
    return pl.pallas_call(
        functools.partial(attend_inputs_kernel, blocks),
        grid=(blocks,),
        in_specs=[FLAG]
        + [per_block(part.shape[1:]) for part in weights]
        + [whole(part.shape) for part in d_queries + d_pairs],
        out_specs=[whole((rows, width)), whole((keys, width))],
        out_shape=[shape((rows, width), jnp.float32), shape((keys, width), jnp.float32)],
        scratch_shapes=[pltpu.VMEM((width, 6 * LANES), jnp.bfloat16)],
        compiler_params=PARAMS,
        cost_estimate=cost(5, 12 * 2**20),
        name="attend_inputs",
    )(core, *weights, *d_queries, *d_pairs)


def ffn_kernel(core_ref, x_ref, *refs):
    own_refs, peer_refs = refs[:PARTS], refs[PARTS : 2 * PARTS]
    z_ref, g_ref, slope_ref, w_ref = refs[2 * PARTS :]
    block = pl.program_id(0)
    assemble(core_ref[0], own_refs[0].shape[1], own_refs, peer_refs, w_ref)
    units = own_refs[0].shape[2]
    inner = mul(x_ref[...], w_ref[:, :units])
    spread = 0.5 * (1.0 + lax.erf(inner * (0.5**0.5)))
    bell = jnp.exp(-0.5 * inner * inner) * 0.3989422804014327
    active = (inner * spread).astype(jnp.bfloat16)
    g_ref[0] = active
    slope_ref[0] = (spread + inner * bell).astype(jnp.bfloat16)
    out = mul_nt(active, w_ref[:, units:])

    @pl.when(block == 0)
    def _():
        z_ref[...] = out

    @pl.when(block > 0)
    def _():
        z_ref[...] += out


def ffn(core, x, weights):
    rows, width = x.shape
    blocks, _, units = weights[0].shape
    return pl.pallas_call(
        ffn_kernel,
        grid=(blocks,),
        in_specs=[FLAG, whole((rows, width))] + [per_block(part.shape[1:]) for part in weights],
        out_specs=[whole((rows, width)), per_block((rows, units)), per_block((rows, units))],
        out_shape=[
            shape((rows, width), jnp.float32),
            shape((blocks, rows, units), jnp.bfloat16),
            shape((blocks, rows, units), jnp.bfloat16),
        ],
        scratch_shapes=[pltpu.VMEM((width, 2 * units), jnp.bfloat16)],
        compiler_params=PARAMS,
        cost_estimate=cost(12, rows * units * blocks * 16),
        name="ffn",
    )(core, x, *weights)


def ffn_back_kernel(core_ref, dz_ref, *refs):
    own_refs, peer_refs = refs[:PARTS], refs[PARTS : 2 * PARTS]
    slope_ref, dx_ref, dh_ref, w_ref = refs[2 * PARTS :]
    block = pl.program_id(0)
    assemble(core_ref[0], own_refs[0].shape[1], own_refs, peer_refs, w_ref)
    units = own_refs[0].shape[2]
    d_active = mul(dz_ref[...], w_ref[:, units:])
    d_inner = (d_active * slope_ref[0].astype(jnp.float32)).astype(jnp.bfloat16)
    dh_ref[0] = d_inner
    out = mul_nt(d_inner, w_ref[:, :units])

    @pl.when(block == 0)
    def _():
        dx_ref[...] = out

    @pl.when(block > 0)
    def _():
        dx_ref[...] += out


def ffn_back(core, dz, weights, slope):
    rows, width = dz.shape
    blocks, _, units = weights[0].shape
    return pl.pallas_call(
        ffn_back_kernel,
        grid=(blocks,),
        in_specs=[FLAG, whole((rows, width))]
        + [per_block(part.shape[1:]) for part in weights]
        + [per_block((rows, units))],
        out_specs=[whole((rows, width)), per_block((rows, units))],
        out_shape=[
            shape((rows, width), jnp.float32),
            shape((blocks, rows, units), jnp.bfloat16),
        ],
        scratch_shapes=[pltpu.VMEM((width, 2 * units), jnp.bfloat16)],
        compiler_params=PARAMS,
        cost_estimate=cost(12, rows * units * blocks * 12),
        name="ffn_back",
    )(core, dz, *weights, slope)


def ffn_grad_kernel(core_ref, left_ref, right_ref, keep_ref, send_ref, g_ref):
    half = keep_ref.shape[1]
    g_ref[...] = mul_tn(left_ref[...], right_ref[0]).astype(jnp.bfloat16)
    hand_out(core_ref[0], half, g_ref, (keep_ref,), (send_ref,))


def ffn_grad(core, left, right, like):
    rows, width = left.shape
    blocks, _, units = right.shape
    return pl.pallas_call(
        ffn_grad_kernel,
        grid=(blocks,),
        in_specs=[FLAG, whole((rows, width)), per_block((rows, units))],
        out_specs=[per_block(like.shape[1:])] * 2,
        out_shape=[shape(like.shape, jnp.bfloat16)] * 2,
        scratch_shapes=[pltpu.VMEM((width, units), jnp.bfloat16)],
        compiler_params=PARAMS,
        cost_estimate=cost(5, rows * units * blocks * 8),
        name="ffn_grad",
    )(core, left, right)


def layer_norm(values, gain_row, bias_row):
    average = jnp.mean(values, axis=-1, keepdims=True)
    centered = values - average
    variance = jnp.mean(centered * centered, axis=-1, keepdims=True)
    return centered * lax.rsqrt(variance + NORM_EPS) * gain_row + bias_row


def norm_back(values, gain_row, bias_row, upstream):
    _, pullback = jax.vjp(layer_norm, values, gain_row, bias_row)
    return pullback(upstream)


def low(values):
    return values.astype(jnp.bfloat16)


SWAP = [(0, 0), (1, 2), (2, 1), (3, 3)]


def swapped(x, axis="zh"):
    return lax.ppermute(x, ("section", axis), SWAP)


def over(x, *axes, decoder=False):
    count = 2 ** len(axes)
    if decoder and axes == ("section",):
        return lax.ppermute(x, ("section", "zh"), [(1, 3), (3, 1)])
    if decoder:
        return lax.ppermute(x, ("zh",) + axes, [(count + at, 2 * count - 1 - at) for at in range(count)])
    return lax.ppermute(x, axes, [(at, count - 1 - at) for at in range(count)])


def to_work(other):
    return [
        (8 * s + 4 * z + 2 * y + x, 8 * y + 4 * s + 2 * z + (x ^ other))
        for s in (0, 1)
        for z in (0, 1)
        for y in (0, 1)
        for x in (0, 1)
    ]


def to_home(other):
    return [(work, home) for home, work in to_work(other)]


def in_order(x, flag, axis):
    return jnp.where(flag == 1, jnp.flip(x, axis), x)


def pack_heads(query, key, value, out):
    pair = 2 * HDIM
    return jnp.concatenate(
        [
            query,
            value[:, pair:],
            key[:, :pair],
            value[:, :pair],
            key[:, pair:],
            out[:, pair:],
            out[:, :pair],
        ],
        axis=1,
    )


def unpack_heads(packed):
    part = [packed[:, at * HDIM : (at + 1) * HDIM] for at in range(12)]
    query = jnp.concatenate(part[0:3], axis=1)
    key = jnp.concatenate([part[4], part[5], part[8]], axis=1)
    value = jnp.concatenate([part[6], part[7], part[3]], axis=1)
    out = jnp.concatenate([part[10], part[11], part[9]], axis=1)
    return query, key, value, out


def after(x, *earlier):
    return lax.optimization_barrier((x,) + earlier)[0]


def plane_gathered(x, **only):
    return jnp.stack([x, over(x, "tx", **only), over(x, "ty", **only), over(x, "ty", "tx", **only)])


def plane_summed(x, **only):
    terms = [x[0], over(x[1], "tx", **only), over(x[2], "ty", **only), over(x[3], "ty", "tx", **only)]
    return low(sum(term.astype(jnp.float32) for term in terms))


def rows_gathered(x, count, **only):
    for at in reversed(range(count)):
        axis = "z%d" % at
        both = in_order(jnp.stack([x, over(x, axis, **only)], axis=-3), lax.axis_index(axis), x.ndim - 2)
        x = both.reshape(x.shape[:-2] + (2 * x.shape[-2], x.shape[-1]))
    return x


def rows_summed(x, count, **only):
    for at in range(count):
        axis = "z%d" % at
        halves = x.reshape(x.shape[:-2] + (2, x.shape[-2] // 2, x.shape[-1]))
        halves = in_order(halves, lax.axis_index(axis), x.ndim - 2)
        x = plus(halves[..., 0, :, :], over(halves[..., 1, :, :], axis, **only))
    return x


def plus(first, second):
    return low(first.astype(jnp.float32) + second.astype(jnp.float32))


def from_cores(keep, send, **only):
    return plus(keep, over(send, "section", **only))


def body(
    count,
    hidden,
    cotangent,
    segments,
    sa_qkv,
    sa_out,
    cross_one,
    cross_two,
    ffn_in,
    ffn_out,
    norm_gain,
    norm_bias,
):
    core = lax.axis_index("section")
    core_flag = core.reshape(1)
    x_at, y_at, zh_at = lax.axis_index("tx"), lax.axis_index("ty"), lax.axis_index("zh")
    on_encoder = zh_at == 0
    quarter = hidden.shape[3]

    def pick(first, second):
        return jnp.where(on_encoder, first, second)

    def rows_in(x):
        mine, other = in_order(x[0, :, 0], x_at, 0)
        whole_axes = ("section", "zh", "ty", "tx")
        both = [lax.ppermute(mine, whole_axes, to_work(0)), lax.ppermute(other, whole_axes, to_work(1))]
        return in_order(jnp.stack(both), x_at, 0).reshape(2 * quarter, -1)

    def rows_out(x):
        mine, other = in_order(x.reshape(2, quarter, -1), x_at, 0)
        whole_axes = ("section", "zh", "ty", "tx")
        both = [lax.ppermute(mine, whole_axes, to_home(0)), lax.ppermute(other, whole_axes, to_home(1))]
        return in_order(jnp.stack(both), x_at, 0)[None, :, None]

    packed_self = pack_heads(sa_qkv[0, :, 0], sa_qkv[0, :, 1], sa_qkv[0, :, 2], sa_out[0])
    packed_ffn = jnp.concatenate([ffn_in[0], ffn_out[0].T], axis=1)
    with jax.named_scope("norms_in"):
        norms = swapped(jnp.concatenate([norm_gain[0], norm_bias[0]], axis=0))
        gains, biases = norms[:3], norms[3:]
        seg_own = segments[:, :, 0].astype(jnp.float32)
        seg_here = jnp.where(y_at == zh_at, seg_own, over(seg_own, "zh")).astype(jnp.int32)
    with jax.named_scope("self_weights"):
        shard_self = swapped(packed_self)
        plane_self = plane_gathered(shard_self)
    with jax.named_scope("hidden_in"):
        moved = in_order(swapped(after(hidden[0, :, 0], shard_self)), x_at, 0)
    with jax.named_scope("ffn_weights"):
        shard_ffn = swapped(after(packed_ffn, moved))
    with jax.named_scope("self_weights"):
        own_self = rows_gathered(after(plane_self, shard_ffn), count)
    with jax.named_scope("hidden_in"):
        moved = after(moved, plane_self)
        moved = in_order(jnp.stack([moved[0], over(moved[1], "tx")]), x_at, 0)
        rows_here = swapped(moved.reshape(2 * quarter, -1), "ty")
    with jax.named_scope("ffn_weights"):
        ffn_second = plane_gathered(after(shard_ffn[:, ffn_in.shape[2] :], rows_here))
        ffn_first = rows_gathered(after(shard_ffn[:, : ffn_in.shape[2]], own_self), count)
    with jax.named_scope("self_weights"):
        w_self = [own_self, over(own_self, "section")]
    with jax.named_scope("hidden_in"):
        rows_all = jnp.concatenate([rows_here, over(rows_here, "section")], axis=0)
    with jax.named_scope("ffn_weights"):
        own_ffn = [plane_gathered(ffn_first), rows_gathered(ffn_second, count)]
        w_ffn = own_ffn + [over(part, "section") for part in own_ffn]
    units = ffn_in.shape[2]
    width = cross_one.shape[2]

    both_segments = in_order(seg_here, x_at, 1)[:, 0]
    ordered = in_order(both_segments.reshape(2, 2, 2 * quarter), core, 1).reshape(2, 4 * quarter)
    source_seg, target_seg = ordered[0], ordered[1]
    self_seg = pick(source_seg, target_seg)
    places = jnp.arange(4)
    quarter_of = jnp.repeat(2 * ((places // 2) ^ core) + places % 2, quarter)
    lanes = jnp.arange(LANES)[None, :]

    def key_extras(seg):
        differs = jnp.logical_and(lanes < SEG_LANES, seg[:, None] != lanes)
        later = jnp.logical_and(
            jnp.logical_and(lanes >= SEG_LANES, lanes < PART_LANE),
            quarter_of[:, None] > lanes - SEG_LANES,
        )
        part = jnp.logical_and(lanes >= PART_LANE, lanes < PART_LANE + 3)
        return jnp.where(differs | later | part, 1.0, 0.0).astype(jnp.bfloat16)

    def query_extras(seg, causal):
        seg, at = seg[: 2 * quarter], quarter_of[: 2 * quarter]
        same = seg[:, None] == lanes
        here = jnp.logical_and(at[:, None] + SEG_LANES == lanes, causal)
        return jnp.where(same | here, MASKED, 0.0).astype(jnp.bfloat16)

    at_row = jnp.arange(quarter)
    later_key = jnp.logical_and(at_row[None, :] > at_row[:, None], jnp.logical_not(on_encoder))
    tri = jnp.where(later_key, MASKED, 0.0).astype(jnp.float32)
    self_extras = (query_extras(self_seg, jnp.logical_not(on_encoder)), key_extras(self_seg), tri)
    cross_extras = (query_extras(target_seg, False), key_extras(source_seg), tri)

    start = rows_all.astype(jnp.float32)
    start = pick(layer_norm(start, gains[0], biases[0]), start)
    start_here = start[: 2 * quarter]
    start_low = low(start)
    self_gain, self_bias = pick(gains[1], gains[0]), pick(biases[1], biases[0])
    self_out, *kept_self = attend(
        core_flag, start_low[: 2 * quarter], after(start_low, ffn_first, ffn_second), w_self, self_extras, True
    )
    self_total = start_here + self_out
    middle = layer_norm(self_total, self_gain, self_bias)
    middle_low = low(middle)

    with jax.named_scope("cross_weights"):
        cross_low = after(jnp.concatenate([cross_one[0], cross_two[0]], axis=1), middle_low)
        pair_kv = lax.ppermute(cross_low, ("section", "zh"), [(0, 1), (1, 3)])
        pair_qo = lax.ppermute(cross_low, ("section", "zh"), [(2, 1), (3, 3)])
        packed = pack_heads(pair_qo[:, :width], pair_kv[:, :width], pair_kv[:, width:], pair_qo[:, width:])
        own_cross = rows_gathered(plane_gathered(packed, decoder=True), count, decoder=True)
        w_cross = [own_cross, over(own_cross, "section", decoder=True)]

    enc_out, enc_active, enc_slope = ffn(core_flag, middle_low, w_ffn)
    enc_total = middle + enc_out
    encoded = low(layer_norm(enc_total, gains[2], biases[2]))
    with jax.named_scope("memory"):
        memory_here = lax.ppermute(encoded, "zh", [(0, 1)])
        memory = jnp.concatenate([memory_here, over(memory_here, "section", decoder=True)], axis=0)
    with jax.named_scope("cotangent_in"):
        cot = rows_in(after(cotangent, memory)).astype(jnp.float32)

    cross_out, *kept_cross = attend(core_flag, middle_low, memory, w_cross, cross_extras, False)
    cross_total = middle + cross_out
    crossed = layer_norm(cross_total, gains[1], biases[1])
    crossed_low = low(crossed)
    dec_out, dec_active, dec_slope = ffn(core_flag, crossed_low, w_ffn)
    dec_total = crossed + dec_out
    decoded = low(layer_norm(dec_total, gains[2], biases[2]))

    d_dec_total, dec_gain_c, dec_bias_c = norm_back(dec_total, gains[2], biases[2], cot)
    d_dec_low = low(d_dec_total)
    d_after, dec_inner = ffn_back(core_flag, d_dec_low, w_ffn, dec_slope)
    d_cross_total, dec_gain_b, dec_bias_b = norm_back(
        cross_total, gains[1], biases[1], d_dec_total + d_after
    )
    d_queries, d_pairs, cross_keep, cross_send = attend_back(
        core_flag, low(d_cross_total), middle_low, memory, w_cross, kept_cross, cross_extras, False, 0, 4
    )
    d_middle_part, d_memory = attend_inputs(core_flag, w_cross, [d_queries[at : at + 1] for at in range(4)], [d_pairs[at : at + 1] for at in range(4)])
    with jax.named_scope("d_memory"):
        d_memory_here = d_memory[: 2 * quarter] + over(
            low(d_memory[2 * quarter :]), "section", decoder=True
        ).astype(jnp.float32)
        d_memory_low = low(d_memory_here)
        d_encoded = lax.ppermute(d_memory_low, "zh", [(1, 0)]).astype(jnp.float32) + cot
    with jax.named_scope("cross_sums"):
        cross_sum = from_cores(after(cross_keep[0], d_memory_low), after(cross_send[0], d_memory_low), decoder=True)
        cross_plane = plane_summed(cross_sum, decoder=True)
        share_cross = rows_summed(cross_plane, count, decoder=True)

    d_enc_total, enc_gain_c, enc_bias_c = norm_back(enc_total, gains[2], biases[2], d_encoded)
    d_enc_low = low(d_enc_total)
    second_keep, second_send = ffn_grad(
        core_flag, after(pick(d_enc_low, d_dec_low), cross_sum), pick(enc_active, dec_active), w_ffn[1]
    )
    with jax.named_scope("ffn_sums"):
        second_sum = from_cores(second_keep, second_send)
    d_enc_middle, enc_inner = ffn_back(core_flag, after(d_enc_low, second_keep), w_ffn, enc_slope)
    first_keep, first_send = ffn_grad(
        core_flag, after(pick(middle_low, crossed_low), second_sum, cross_plane), pick(enc_inner, dec_inner), w_ffn[0]
    )
    with jax.named_scope("ffn_sums"):
        second_rows = rows_summed(second_sum, count)
        first_sum = from_cores(first_keep, first_send)
        first_plane = plane_summed(first_sum)
        first_share = rows_summed(first_plane, count)
        second_share = plane_summed(after(second_rows, first_plane))
    with jax.named_scope("hidden_out"):
        hidden_out = rows_out(after(pick(encoded, decoded), first_plane))

    d_middle = pick(d_enc_total + d_enc_middle, d_cross_total + d_middle_part)
    d_self_total, gain_s, bias_s = norm_back(self_total, self_gain, self_bias, d_middle)
    d_self_low = low(d_self_total)
    earlier = {1: (first_keep,), 2: (first_sum,), 3: (second_rows,), 0: (first_plane,)}
    pieces, self_sums = {}, {}
    for at in (1, 2, 3, 0):
        d_queries, d_pairs, keep, send = attend_back(
            core_flag,
            after(d_self_low, *earlier[at]),
            start_low[: 2 * quarter],
            start_low,
            w_self,
            kept_self,
            self_extras,
            True,
            at,
            1,
        )
        pieces[at] = (d_queries, d_pairs)
        with jax.named_scope("self_sums"):
            self_sums[at] = from_cores(keep[0], send[0])
    d_start_q, d_start_kv = attend_inputs(
        core_flag, w_self, [pieces[at][0] for at in range(4)], [pieces[at][1] for at in range(4)]
    )
    d_start = d_self_total + d_start_q + d_start_kv[: 2 * quarter]
    with jax.named_scope("d_start"):
        d_start = d_start + over(low(d_start_kv[2 * quarter :]), "section").astype(jnp.float32)
    d_source, gain_a, bias_a = norm_back(
        rows_here.astype(jnp.float32), gains[0], biases[0], d_start
    )
    with jax.named_scope("hidden_grad"):
        hidden_grad = rows_out(low(pick(d_source, d_start))).astype(jnp.float32)

    with jax.named_scope("self_sums"):
        both = after(jnp.concatenate([self_sums[at] for at in range(4)], axis=0), second_share)
        columns = both.shape[2] // 2
        share_self = [
            rows_summed(plane_summed(both[:, :, :columns]), count),
            plane_summed(rows_summed(both[:, :, columns:], count)),
        ]
        share_self = swapped(jnp.concatenate(share_self, axis=1)).astype(jnp.float32)
    with jax.named_scope("ffn_sums"):
        share_ffn = swapped(jnp.concatenate([first_share, second_share], axis=1)).astype(jnp.float32)
    share_first, share_second = share_ffn[:, :units], share_ffn[:, units:].T
    g_query, g_key, g_value, g_out = unpack_heads(share_self)
    grad_qkv = jnp.stack([g_query, g_key, g_value], axis=1)
    c_query, c_key, c_value, c_out = unpack_heads(share_cross)
    for_enc = lax.ppermute(jnp.concatenate([c_key, c_value], axis=1), ("section", "zh"), [(1, 0), (3, 1)])
    for_dec = lax.ppermute(jnp.concatenate([c_query, c_out], axis=1), ("section", "zh"), [(1, 2), (3, 3)])
    cross = jnp.where(core == 0, for_enc, for_dec).astype(jnp.float32)

    norm_sums = jnp.stack(
        [
            pick(gain_a, gain_s),
            pick(gain_s, dec_gain_b),
            pick(enc_gain_c, dec_gain_c),
            pick(bias_a, bias_s),
            pick(bias_s, dec_bias_b),
            pick(enc_bias_c, dec_bias_c),
        ]
    )
    pieces = norm_sums.reshape((6, 2) + (2,) * count + (2, 2, -1))
    for axis, at in [("section", core)] + [
        (name, lax.axis_index(name)) for name in ["z%d" % z for z in range(count)] + ["ty", "tx"]
    ]:
        pieces = in_order(pieces, at, 1)
        pieces = pieces[:, 0] + over(pieces[:, 1], axis)
    norm_shares = swapped(pieces)
    return (
        hidden_out,
        hidden_grad,
        grad_qkv[None],
        g_out[None],
        cross[None, :, :width],
        cross[None, :, width:],
        share_first[None],
        share_second[None],
        norm_shares[None, :3],
        norm_shares[None, 3:],
    )


def solution(mesh):
    _, dp_count, _ = mesh.devices.shape
    count = (dp_count // 2).bit_length() - 1
    dp = ("zh",) + tuple("z%d" % at for at in range(count))
    tensor = ("ty", "tx")
    split = Mesh(mesh.devices.reshape((2, 2) + (2,) * count + (2, 2)), ("section",) + dp + tensor)
    rows = P("section", None, dp, tensor, None)
    in_specs = (
        rows,
        rows,
        P(None, None, dp, None),
        P("section", dp, None, tensor),
        P("section", dp, tensor),
        P("section", dp, tensor),
        P("section", dp, tensor),
        P("section", dp, tensor),
        P("section", tensor, dp),
        P("section", None, None),
        P("section", None, None),
    )
    out_specs = (
        rows,
        rows,
        P("section", dp, None, tensor),
        P("section", dp, tensor),
        P("section", dp, tensor),
        P("section", dp, tensor),
        P("section", dp, tensor),
        P("section", tensor, dp),
        P("section", None, dp + tensor),
        P("section", None, dp + tensor),
    )
    return jax.shard_map(
        functools.partial(body, count), mesh=split, in_specs=in_specs, out_specs=out_specs, check_vma=False
    )
```

```python
import functools

import jax
import jax.numpy as jnp
from jax import lax
from jax.experimental import pallas as pl
from jax.experimental.pallas import tpu as pltpu
from jax.sharding import Mesh
from jax.sharding import PartitionSpec as P

HDIM = 64
LANES = 128
MASKED = -1e30
NORM_EPS = 1e-05
VMEM_BYTES = 56 * 1024 * 1024

SEG_LANES = 8
PART_LANE = 12

PARTS = 2
HEADS = ((0, 1, 2, 0, 0), (0, 1, 2, 1, 1), (1, 3, 0, 0, 1))


def mul(a, b):
    return jnp.dot(a, b, preferred_element_type=jnp.float32)


def mul_nt(a, b):
    return lax.dot_general(a, b, (((1,), (1,)), ((), ())), preferred_element_type=jnp.float32)


def mul_tn(a, b):
    return lax.dot_general(a, b, (((0,), (0,)), ((), ())), preferred_element_type=jnp.float32)


def tile_of(values, index):
    return values[:, index * LANES : (index + 1) * LANES]


def lane_ids(rows):
    return lax.broadcasted_iota(jnp.int32, (rows, LANES), 1)


def half_mask(rows, half):
    lanes = lane_ids(rows)
    return lanes >= HDIM if half else lanes < HDIM


def in_parts(base, column):
    lanes = lane_ids(base.shape[0])
    high = column.astype(jnp.bfloat16).astype(jnp.float32)
    rest = column - high
    middle = rest.astype(jnp.bfloat16).astype(jnp.float32)
    low = rest - middle
    parts = jnp.where(
        lanes == PART_LANE,
        high,
        jnp.where(lanes == PART_LANE + 1, middle, jnp.where(lanes == PART_LANE + 2, low, base)),
    )
    return parts.astype(jnp.bfloat16)


def with_triangle(scores, tri, at):
    size = tri.shape[1]
    pieces = []
    if at > 0:
        pieces.append(scores[:, : at * size])
    pieces.append(scores[:, at * size : (at + 1) * size] + tri)
    pieces.append(scores[:, (at + 1) * size :])
    return jnp.concatenate(pieces, axis=1)


def places(core, block):
    return [pl.multiple_of((1 - core) * block, block), pl.multiple_of((2 + core) * block, block)]


def assemble(flag_ref, own_refs, peer_refs, w_ref):
    core, block = flag_ref[0], own_refs[0].shape[1] // 2
    for holder, refs in ((core, own_refs), (1 - core, peer_refs)):
        for part, ref in enumerate(refs):
            width = ref.shape[2]
            for at, place in enumerate(places(holder, block)):
                w_ref[pl.ds(place, block), part * width : (part + 1) * width] = ref[0, at * block : (at + 1) * block]


def hand_out(flag_ref, g_ref, keep_ref, send_ref):
    core, block = flag_ref[0], keep_ref.shape[1] // 2
    for holder, ref in ((core, keep_ref), (1 - core, send_ref)):
        for at, place in enumerate(places(holder, block)):
            ref[0, at * block : (at + 1) * block] = g_ref[pl.ds(place, block), :]


def where_active(kernel):
    def guarded(flag_ref, *refs):
        @pl.when(flag_ref[1] == 1)
        def _():
            kernel(flag_ref, *refs)

    return guarded


def scaled_queries(q_ref, at, q_tile, q_half):
    queries = q_ref[0, at, q_tile * LANES : (q_tile + 1) * LANES] * 0.125
    return jnp.where(half_mask(queries.shape[0], q_half), queries, 0).astype(jnp.bfloat16)


def units_of(total, rows):
    return [
        (slice(part * rows, (part + 1) * rows), part, head)
        for part in range(total // rows)
        for head in range(len(HEADS))
    ]


def attend_kernel(causal, flag_ref, xq_ref, xkv_ref, *refs):
    own_refs, peer_refs = refs[:1], refs[1:2]
    qx_ref, kx_ref, tri_ref, o_ref, q_ref, kv_ref, c_ref, l_ref, w_ref = refs[2:]
    block = pl.program_id(0)
    assemble(flag_ref, own_refs, peer_refs, w_ref)
    q_ref[0] = mul(xq_ref[...], w_ref[:, : 2 * LANES]).astype(jnp.bfloat16)
    kv_ref[0] = mul(xkv_ref[...], w_ref[:, LANES : 5 * LANES]).astype(jnp.bfloat16)
    rows = tri_ref.shape[0]
    low = half_mask(rows, 0)

    def scores_of(at, part, head):
        q_tile, k_tile, _, q_half, _ = HEADS[head]
        keys = kv_ref[0, :, k_tile * LANES : (k_tile + 1) * LANES]
        scores = mul_nt(
            jnp.concatenate([scaled_queries(q_ref, at, q_tile, q_half), qx_ref[at, :]], axis=1),
            jnp.concatenate([keys, kx_ref[...]], axis=1),
        )
        return with_triangle(scores, tri_ref[...], part) if causal else scores

    units = units_of(q_ref.shape[1], rows)
    ahead = scores_of(*units[0])
    contexts, totals = [], None
    for index, (at, part, head) in enumerate(units):
        scores = ahead
        if index + 1 < len(units):
            ahead = scores_of(*units[index + 1])
        v_tile = HEADS[head][2]
        values = kv_ref[0, :, v_tile * LANES : (v_tile + 1) * LANES]
        highest = jnp.max(scores, axis=1, keepdims=True)
        weights = jnp.exp(scores - highest)
        sums = jnp.sum(weights, axis=1, keepdims=True)
        contexts.append(mul(weights.astype(jnp.bfloat16), values) / sums)
        logs = jnp.broadcast_to(highest + jnp.log(sums), (rows, LANES))
        totals = logs if head == 0 else jnp.where(lane_ids(rows) == head, logs, totals)
        if head == len(HEADS) - 1:
            c_ref[0, at, :LANES] = jnp.where(low, 0, contexts[2]).astype(jnp.bfloat16)
            c_ref[0, at, LANES:] = jnp.where(low, contexts[0], contexts[1]).astype(jnp.bfloat16)
            l_ref[0, at, :] = totals
            contexts = []
    out = mul_nt(c_ref[0], w_ref[:, 4 * LANES :])

    @pl.when(block == 0)
    def _():
        o_ref[...] = out

    @pl.when(block > 0)
    def _():
        o_ref[...] += out


def attend_back_kernel(causal, flag_ref, do_ref, xq_ref, xkv_ref, *refs):
    own_refs, peer_refs = refs[:1], refs[1:2]
    q_ref, kv_ref, c_ref, l_ref, qx_ref, kx_ref, tri_ref, dq_ref, dkv_ref, *refs = refs[2:]
    keep_ref, send_ref, w_ref, sum_ref, g_ref = refs
    rows = tri_ref.shape[0]
    assemble(flag_ref, own_refs, peer_refs, w_ref)
    d_context = mul(do_ref[...], w_ref[:, 4 * LANES :]).astype(jnp.bfloat16)
    low = half_mask(rows, 0)

    def products_of(at, part, head):
        q_tile, k_tile, v_tile, q_half, v_half = HEADS[head]
        c_tile = 0 if head == 2 else 1
        keys = kv_ref[0, :, k_tile * LANES : (k_tile + 1) * LANES]
        values = kv_ref[0, :, v_tile * LANES : (v_tile + 1) * LANES]
        queries = scaled_queries(q_ref, at, q_tile, q_half)
        d_rows = jnp.where(half_mask(rows, v_half), tile_of(d_context[at], c_tile), 0).astype(jnp.bfloat16)
        total = l_ref[0, at, head : head + 1]
        scores = mul_nt(
            jnp.concatenate([queries, in_parts(qx_ref[at, :].astype(jnp.float32), -total)], axis=1),
            jnp.concatenate([keys, kx_ref[...]], axis=1),
        )
        if causal:
            scores = with_triangle(scores, tri_ref[...], part)
        return scores, mul_nt(d_rows, values), queries, d_rows, keys

    units = units_of(q_ref.shape[1], rows)
    ahead = products_of(*units[0])
    d_queries = []
    for index, (at, part, head) in enumerate(units):
        scores, d_probs, queries, d_rows, keys = ahead
        if index + 1 < len(units):
            ahead = products_of(*units[index + 1])
        _, k_tile, v_tile, _, _ = HEADS[head]
        probs = jnp.exp(scores)
        inner = jnp.sum(probs * d_probs, axis=1, keepdims=True)
        d_scores = (probs * (d_probs - inner)).astype(jnp.bfloat16)
        d_values = mul_tn(probs.astype(jnp.bfloat16), d_rows)
        d_keys = mul_tn(d_scores, queries)
        d_queries.append(mul(d_scores, keys) * 0.125)
        k_at = slice(k_tile * LANES, (k_tile + 1) * LANES)
        v_at = slice(v_tile * LANES, (v_tile + 1) * LANES)
        if part == 0 and head != 1:
            sum_ref[:, k_at] = d_keys
            sum_ref[:, v_at] = d_values
        else:
            sum_ref[:, k_at] += d_keys
            sum_ref[:, v_at] += d_values
        if head == len(HEADS) - 1:
            dq_ref[0, at, :LANES] = jnp.where(low, d_queries[0], d_queries[1]).astype(jnp.bfloat16)
            dq_ref[0, at, LANES:] = jnp.where(low, d_queries[2], 0).astype(jnp.bfloat16)
            d_queries = []
    dkv_ref[0] = sum_ref[...].astype(jnp.bfloat16)
    grad_q = mul_tn(xq_ref[...], dq_ref[0])
    grad_kv = mul_tn(xkv_ref[...], dkv_ref[0])
    grad_o = mul_tn(do_ref[...], c_ref[0])
    g_ref[:, :LANES] = grad_q[:, :LANES].astype(jnp.bfloat16)
    g_ref[:, LANES : 2 * LANES] = (grad_q[:, LANES:] + grad_kv[:, :LANES]).astype(jnp.bfloat16)
    g_ref[:, 2 * LANES : 4 * LANES] = grad_kv[:, LANES : 3 * LANES].astype(jnp.bfloat16)
    g_ref[:, 4 * LANES : 5 * LANES] = (grad_kv[:, 3 * LANES :] + grad_o[:, :LANES]).astype(jnp.bfloat16)
    g_ref[:, 5 * LANES :] = grad_o[:, LANES:].astype(jnp.bfloat16)
    hand_out(flag_ref, g_ref, keep_ref, send_ref)


def attend_inputs_kernel(count, flag_ref, *refs):
    own_refs, peer_refs = refs[:1], refs[1:2]
    dq_refs, dkv_refs = refs[2 : 2 + count], refs[2 + count : 2 + 2 * count]
    dxq_ref, dxkv_ref, w_ref = refs[2 + 2 * count :]
    block = pl.program_id(0)
    assemble(flag_ref, own_refs, peer_refs, w_ref)

    for at in range(count):

        @pl.when(block == at)
        def _():
            d_xq = mul_nt(dq_refs[at][0], w_ref[:, : 2 * LANES])
            d_xkv = mul_nt(dkv_refs[at][0], w_ref[:, LANES : 5 * LANES])
            dxq_ref[...] = d_xq if at == 0 else dxq_ref[...] + d_xq
            dxkv_ref[...] = d_xkv if at == 0 else dxkv_ref[...] + d_xkv


def whole(shape):
    return pl.BlockSpec(shape, lambda j, flag: (0,) * len(shape))


def per_block(shape, first=0, gate=1):
    return pl.BlockSpec((1,) + shape, lambda j, flag: (first + j * flag[gate],) + (0,) * len(shape))


shape = jax.ShapeDtypeStruct


def call(kernel, name, micros, moved, grid, in_specs, out_specs, out_shape, scratch, *operands):
    return pl.pallas_call(
        where_active(kernel),
        grid_spec=pltpu.PrefetchScalarGridSpec(
            num_scalar_prefetch=1,
            grid=(grid,),
            in_specs=in_specs,
            out_specs=out_specs,
            scratch_shapes=scratch,
        ),
        out_shape=out_shape,
        compiler_params=pltpu.CompilerParams(vmem_limit_bytes=VMEM_BYTES),
        cost_estimate=cost(micros, moved),
        name=name,
    )(*operands)


def cost(micros, moved):
    return pl.CostEstimate(flops=int(micros * 1.15e9), bytes_accessed=int(moved), transcendentals=0)


def attend(flag, xq, xkv, weights, extras, causal):
    rows, width = xq.shape
    keys = xkv.shape[0]
    blocks = weights[0].shape[0]
    return call(
        functools.partial(attend_kernel, causal),
        "attend_self" if causal else "attend_cross",
        20,
        24 * 2**20,
        blocks,
        [whole((rows, width)), whole((keys, width))]
        + [per_block(part.shape[1:]) for part in weights]
        + [whole(extra.shape) for extra in extras],
        [
            whole((rows, width)),
            per_block((rows, 2 * LANES)),
            per_block((keys, 4 * LANES)),
            per_block((rows, 2 * LANES)),
            per_block((rows, LANES)),
        ],
        [
            shape((rows, width), jnp.float32),
            shape((blocks, rows, 2 * LANES), jnp.bfloat16),
            shape((blocks, keys, 4 * LANES), jnp.bfloat16),
            shape((blocks, rows, 2 * LANES), jnp.bfloat16),
            shape((blocks, rows, LANES), jnp.float32),
        ],
        [pltpu.VMEM((width, 6 * LANES), jnp.bfloat16)],
        flag,
        xq,
        xkv,
        *weights,
        *extras,
    )


def attend_back(flag, d_out, xq, xkv, weights, kept, extras, causal, first, count):
    rows, width = xq.shape
    keys = xkv.shape[0]
    return call(
        functools.partial(attend_back_kernel, causal),
        "attend_self_back" if causal else "attend_cross_back",
        10 * count,
        6 * 2**20 * count,
        count,
        [whole((rows, width)), whole((rows, width)), whole((keys, width))]
        + [per_block(part.shape[1:], first) for part in weights]
        + [
            per_block((rows, 2 * LANES), first),
            per_block((keys, 4 * LANES), first),
            per_block((rows, 2 * LANES), first),
            per_block((rows, LANES), first),
        ]
        + [whole(extra.shape) for extra in extras],
        [per_block((rows, 2 * LANES)), per_block((keys, 4 * LANES))]
        + [per_block(part.shape[1:]) for part in weights],
        [
            shape((count, rows, 2 * LANES), jnp.bfloat16),
            shape((count, keys, 4 * LANES), jnp.bfloat16),
        ]
        + [shape((count,) + part.shape[1:], jnp.bfloat16) for part in weights],
        [
            pltpu.VMEM((width, 6 * LANES), jnp.bfloat16),
            pltpu.VMEM((keys, 4 * LANES), jnp.float32),
            pltpu.VMEM((width, 6 * LANES), jnp.bfloat16),
        ],
        flag,
        d_out,
        xq,
        xkv,
        *weights,
        *kept,
        *extras,
    )


def attend_inputs(flag, weights, d_queries, d_pairs):
    blocks, half, _ = weights[0].shape
    width = 2 * half
    rows, keys = d_queries[0].shape[1], d_pairs[0].shape[1]
    return call(
        functools.partial(attend_inputs_kernel, len(d_queries)),
        "attend_inputs",
        8,
        12 * 2**20,
        blocks,
        [per_block(part.shape[1:]) for part in weights]
        + [whole(part.shape) for part in d_queries + d_pairs],
        [whole((rows, width)), whole((keys, width))],
        [shape((rows, width), jnp.float32), shape((keys, width), jnp.float32)],
        [pltpu.VMEM((width, 6 * LANES), jnp.bfloat16)],
        flag,
        *weights,
        *d_queries,
        *d_pairs,
    )


def ffn_kernel(flag_ref, x_ref, *refs):
    own_refs, peer_refs = refs[:PARTS], refs[PARTS : 2 * PARTS]
    z_ref, g_ref, slope_ref, w_ref = refs[2 * PARTS :]
    block = pl.program_id(0)
    assemble(flag_ref, own_refs, peer_refs, w_ref)
    units = own_refs[0].shape[2]
    inner = mul(x_ref[...], w_ref[:, :units])
    spread = 0.5 * (1.0 + lax.erf(inner * (0.5**0.5)))
    bell = jnp.exp(-0.5 * inner * inner) * 0.3989422804014327
    active = (inner * spread).astype(jnp.bfloat16)
    g_ref[0] = active
    slope_ref[0] = (spread + inner * bell).astype(jnp.bfloat16)
    out = mul_nt(active, w_ref[:, units:])

    @pl.when(block == 0)
    def _():
        z_ref[...] = out

    @pl.when(block > 0)
    def _():
        z_ref[...] += out


def ffn(flag, x, weights):
    rows, width = x.shape
    blocks, _, units = weights[0].shape
    return call(
        ffn_kernel,
        "ffn",
        12,
        rows * units * blocks * 16,
        blocks,
        [whole((rows, width))] + [per_block(part.shape[1:]) for part in weights],
        [whole((rows, width)), per_block((rows, units)), per_block((rows, units))],
        [
            shape((rows, width), jnp.float32),
            shape((blocks, rows, units), jnp.bfloat16),
            shape((blocks, rows, units), jnp.bfloat16),
        ],
        [pltpu.VMEM((width, 2 * units), jnp.bfloat16)],
        flag,
        x,
        *weights,
    )


def ffn_back_kernel(flag_ref, dz_ref, *refs):
    own_refs, peer_refs = refs[:PARTS], refs[PARTS : 2 * PARTS]
    slope_ref, dx_ref, dh_ref, w_ref = refs[2 * PARTS :]
    block = pl.program_id(0)
    assemble(flag_ref, own_refs, peer_refs, w_ref)
    units = own_refs[0].shape[2]
    d_active = mul(dz_ref[...], w_ref[:, units:])
    d_inner = (d_active * slope_ref[0].astype(jnp.float32)).astype(jnp.bfloat16)
    dh_ref[0] = d_inner
    out = mul_nt(d_inner, w_ref[:, :units])

    @pl.when(block == 0)
    def _():
        dx_ref[...] = out

    @pl.when(block > 0)
    def _():
        dx_ref[...] += out


def ffn_back(flag, dz, weights, slope):
    rows, width = dz.shape
    blocks, _, units = weights[0].shape
    return call(
        ffn_back_kernel,
        "ffn_back",
        12,
        rows * units * blocks * 12,
        blocks,
        [whole((rows, width))] + [per_block(part.shape[1:]) for part in weights] + [per_block((rows, units))],
        [whole((rows, width)), per_block((rows, units))],
        [
            shape((rows, width), jnp.float32),
            shape((blocks, rows, units), jnp.bfloat16),
        ],
        [pltpu.VMEM((width, 2 * units), jnp.bfloat16)],
        flag,
        dz,
        *weights,
        slope,
    )


def ffn_grad_kernel(flag_ref, left_ref, enc_ref, dec_ref, keep_ref, send_ref, g_ref):
    right = jnp.where(flag_ref[2] == 1, enc_ref[0], dec_ref[0])
    g_ref[...] = mul_tn(left_ref[...], right).astype(jnp.bfloat16)
    hand_out(flag_ref, g_ref, keep_ref, send_ref)


def ffn_grad(flag, left, enc_right, dec_right, like):
    rows, width = left.shape
    blocks, _, units = enc_right.shape
    return call(
        ffn_grad_kernel,
        "ffn_grad",
        6,
        rows * units * blocks * 8,
        blocks,
        [whole((rows, width)), per_block((rows, units), 0, 2), per_block((rows, units), 0, 3)],
        [per_block(like.shape[1:])] * 2,
        [shape(like.shape, jnp.bfloat16)] * 2,
        [pltpu.VMEM((width, units), jnp.bfloat16)],
        flag,
        left,
        enc_right,
        dec_right,
    )


def layer_norm(values, gain_row, bias_row):
    average = jnp.mean(values, axis=-1, keepdims=True)
    centered = values - average
    variance = jnp.mean(centered * centered, axis=-1, keepdims=True)
    return centered * lax.rsqrt(variance + NORM_EPS) * gain_row + bias_row


def norm_back(values, gain_row, bias_row, upstream):
    _, pullback = jax.vjp(layer_norm, values, gain_row, bias_row)
    return pullback(upstream)


def low(values):
    return values.astype(jnp.bfloat16)


def axes_of(count):
    return ("section", "zh", "zl") + tuple("e%d" % at for at in range(count)) + ("ty", "tx")


def layer_of(place):
    return 1 ^ place["zh"] ^ place["zl"]


def moved(x, names, to):
    names = [name for name in axes_of(8) if name in names]

    def index(place):
        return sum(place[name] << (len(names) - 1 - at) for at, name in enumerate(names))

    pairs = []
    for source in range(2 ** len(names)):
        place = {name: source >> (len(names) - 1 - at) & 1 for at, name in enumerate(names)}
        target = to(place)
        if target is not None:
            pairs.append((source, index(target)))
    return lax.ppermute(x, tuple(names), pairs)


def over(x, *axes, layer=None):
    def to(place):
        if layer is not None and layer_of(place) != layer:
            return None
        return {**place, **{axis: 1 - place[axis] for axis in axes}}

    return moved(x, axes if layer is None else axes + Z, to)


Z = ("zh", "zl")


def swapped(x):
    def to(place):
        if place["section"] == layer_of(place):
            return place
        return {"section": 1 - place["section"], "zh": place["zh"], "zl": 1 - place["zl"]}

    return moved(x, ("section",) + Z, to)


def turned(x):
    return moved(x, ("section", "ty"), lambda place: {"section": place["ty"], "ty": place["section"]})


def sent_home(x, other):
    def to(place):
        return {
            "section": layer_of(place),
            "zh": place["zh"],
            "zl": 1 ^ place["zh"] ^ place["ty"],
            "ty": place["section"],
            "tx": place["tx"] ^ other,
        }

    return moved(x, ("section",) + Z + ("ty", "tx"), to)


def cross_in(x, layer):
    def to(place):
        if place["section"] != layer:
            return None
        return {"section": layer_of(place), "zh": place["zh"], "zl": place["zh"]}

    return moved(x, ("section",) + Z, to)


def cross_out(x, layer):
    def to(place):
        if layer_of(place) != 1:
            return None
        return {"section": layer, "zh": place["zh"], "zl": 1 ^ place["zh"] ^ place["section"]}

    return moved(x, ("section",) + Z, to)


def in_order(x, flag, axis):
    return jnp.where(flag == 1, jnp.flip(x, axis), x)


def pack_heads(query, key, value, out):
    pair = 2 * HDIM
    return jnp.concatenate(
        [
            query,
            value[:, pair:],
            key[:, :pair],
            value[:, :pair],
            key[:, pair:],
            out[:, pair:],
            out[:, :pair],
        ],
        axis=1,
    )


def unpack_heads(packed):
    part = [packed[:, at * HDIM : (at + 1) * HDIM] for at in range(12)]
    query = jnp.concatenate(part[0:3], axis=1)
    key = jnp.concatenate([part[4], part[5], part[8]], axis=1)
    value = jnp.concatenate([part[6], part[7], part[3]], axis=1)
    out = jnp.concatenate([part[10], part[11], part[9]], axis=1)
    return query, key, value, out


def after(x, *earlier):
    return lax.optimization_barrier((x,) + earlier)[0]


def plane_gathered(x, **only):
    return jnp.stack([x, over(x, "tx", **only), over(x, "ty", **only), over(x, "ty", "tx", **only)])


def plane_summed(x, **only):
    terms = [x[0], over(x[1], "tx", **only), over(x[2], "ty", **only), over(x[3], "ty", "tx", **only)]
    return low(sum(term.astype(jnp.float32) for term in terms))


def rows_gathered(x, count, **only):
    for axes in [("e%d" % at,) for at in reversed(range(count))] + [Z]:
        both = in_order(jnp.stack([x, over(x, *axes, **only)], axis=-3), lax.axis_index(axes[0]), x.ndim - 2)
        x = both.reshape(x.shape[:-2] + (2 * x.shape[-2], x.shape[-1]))
    return x


def rows_summed(x, count, **only):
    for axes in [Z] + [("e%d" % at,) for at in range(count)]:
        halves = x.reshape(x.shape[:-2] + (2, x.shape[-2] // 2, x.shape[-1]))
        halves = in_order(halves, lax.axis_index(axes[0]), x.ndim - 2)
        x = plus(halves[..., 0, :, :], over(halves[..., 1, :, :], *axes, **only))
    return x


def plus(first, second):
    return low(first.astype(jnp.float32) + second.astype(jnp.float32))


def from_cores(keep, send, **only):
    return plus(keep, over(send, "section", **only))


def body(
    count,
    hidden,
    cotangent,
    segments,
    sa_qkv,
    sa_out,
    cross_one,
    cross_two,
    ffn_in,
    ffn_out,
    norm_gain,
    norm_bias,
):
    core = lax.axis_index("section")
    x_at, y_at, zh_at, zl_at = (lax.axis_index(name) for name in ("tx", "ty", "zh", "zl"))
    layer = 1 ^ zh_at ^ zl_at
    on_encoder = layer == 0
    quarter = hidden.shape[3]
    enc_flag = jnp.stack([core, 1 - layer, 1 - layer, layer])
    dec_flag = jnp.stack([core, layer, 1 - layer, layer])
    flag = jnp.stack([core, jnp.ones_like(core), 1 - layer, layer])

    def pick(first, second):
        return jnp.where(on_encoder, first, second)

    def of_one_row(x):
        both = in_order(x[0, :, 0], x_at, 0)
        return in_order(jnp.stack([both[0], over(both[1], "tx")]), x_at, 0).reshape(2 * quarter, -1)

    def rows_out(x):
        mine, other = in_order(x.reshape(2, quarter, -1), x_at, 0)
        return in_order(jnp.stack([sent_home(mine, 0), sent_home(other, 1)]), x_at, 0)[None, :, None]

    units = ffn_in.shape[2]
    width = cross_one.shape[2]
    packed_self = pack_heads(sa_qkv[0, :, 0], sa_qkv[0, :, 1], sa_qkv[0, :, 2], sa_out[0])
    packed_ffn = jnp.concatenate([ffn_in[0], ffn_out[0].T], axis=1)
    with jax.named_scope("norms_in"):
        norms = swapped(jnp.concatenate([norm_gain[0], norm_bias[0]], axis=0))
        gains, biases = norms[:3], norms[3:]
        seg_own = segments[:, :, 0].astype(jnp.float32)
        seg_here = jnp.where(zl_at == 1 ^ zh_at ^ y_at, seg_own, over(seg_own, "zl")).astype(jnp.int32)
    with jax.named_scope("hidden_in"):
        one_row = of_one_row(hidden)
    with jax.named_scope("self_weights"):
        shard_self = swapped(packed_self)
    with jax.named_scope("ffn_weights"):
        shard_ffn = swapped(after(packed_ffn, shard_self))
        shard_first, shard_second = shard_ffn[:, :units], shard_ffn[:, units:]

    def both_rows(x):
        for_enc = rows_gathered(x, count, layer=0)
        return pick(for_enc, rows_gathered(after(x, for_enc), count, layer=1))

    with jax.named_scope("self_weights"):
        rows_self = both_rows(shard_self)
    with jax.named_scope("hidden_in"):
        one_row = swapped(after(one_row, shard_ffn))
    with jax.named_scope("self_weights"):
        own_self = plane_gathered(rows_self)
    with jax.named_scope("ffn_weights"):
        rows_first = both_rows(after(shard_first, rows_self))
    with jax.named_scope("hidden_in"):
        rows_here = turned(after(one_row, own_self))
        rows_all = jnp.concatenate([rows_here, over(rows_here, "section")], axis=0)
    with jax.named_scope("self_weights"):
        w_self = [own_self, over(own_self, "section")]
    with jax.named_scope("ffn_weights"):
        plane_second = plane_gathered(after(shard_second, rows_here))
        own_second = both_rows(plane_second)
        own_first = plane_gathered(after(rows_first, plane_second))
        w_ffn = [own_first, own_second]
        w_ffn = w_ffn + [over(part, "section") for part in w_ffn]

    both_segments = in_order(seg_here, x_at, 1)[:, 0]
    ordered = in_order(both_segments.reshape(2, 2, 2 * quarter), core, 1).reshape(2, 4 * quarter)
    source_seg, target_seg = ordered[0], ordered[1]
    self_seg = pick(source_seg, target_seg)
    parts = jnp.arange(4)
    quarter_of = jnp.repeat(2 * ((parts // 2) ^ core) + parts % 2, quarter)
    lanes = jnp.arange(LANES)[None, :]

    def key_extras(seg):
        differs = jnp.logical_and(lanes < SEG_LANES, seg[:, None] != lanes)
        later = jnp.logical_and(
            jnp.logical_and(lanes >= SEG_LANES, lanes < PART_LANE),
            quarter_of[:, None] > lanes - SEG_LANES,
        )
        part = jnp.logical_and(lanes >= PART_LANE, lanes < PART_LANE + 3)
        return jnp.where(differs | later | part, 1.0, 0.0).astype(jnp.bfloat16)

    def query_extras(seg, causal):
        seg, at = seg[: 2 * quarter], quarter_of[: 2 * quarter]
        same = seg[:, None] == lanes
        here = jnp.logical_and(at[:, None] + SEG_LANES == lanes, causal)
        return jnp.where(same | here, MASKED, 0.0).astype(jnp.bfloat16)

    at_row = jnp.arange(quarter)
    later_key = jnp.logical_and(at_row[None, :] > at_row[:, None], jnp.logical_not(on_encoder))
    tri = jnp.where(later_key, MASKED, 0.0).astype(jnp.float32)
    self_extras = (query_extras(self_seg, jnp.logical_not(on_encoder)), key_extras(self_seg), tri)
    cross_extras = (query_extras(target_seg, False), key_extras(source_seg), tri)

    start = rows_all.astype(jnp.float32)
    start = pick(layer_norm(start, gains[0], biases[0]), start)
    start_here = start[: 2 * quarter]
    start_low = low(start)
    self_gain, self_bias = pick(gains[1], gains[0]), pick(biases[1], biases[0])
    with jax.named_scope("cotangent_in"):
        cot_row = of_one_row(after(cotangent, plane_second))
    self_out, *kept_self = attend(
        flag, start_low[: 2 * quarter], after(start_low, plane_second), w_self, self_extras, True
    )
    self_total = start_here + self_out
    middle = layer_norm(self_total, self_gain, self_bias)
    middle_low = low(middle)

    with jax.named_scope("cotangent_in"):
        cot_row = swapped(after(cot_row, middle_low))
    with jax.named_scope("cross_weights"):
        cross_low = after(jnp.concatenate([cross_one[0], cross_two[0]], axis=1), middle_low)
        pair_kv, pair_qo = cross_in(cross_low, 0), cross_in(cross_low, 1)
        packed = pack_heads(pair_qo[:, :width], pair_kv[:, :width], pair_kv[:, width:], pair_qo[:, width:])
        own_cross = plane_gathered(rows_gathered(packed, count, layer=1), layer=1)
        w_cross = [own_cross, over(own_cross, "section", layer=1)]

    enc_out, enc_active, enc_slope = ffn(enc_flag, middle_low, w_ffn)
    enc_total = middle + enc_out
    encoded = low(layer_norm(enc_total, gains[2], biases[2]))

    def across(x, layer):
        return moved(x, Z, lambda place: {**place, "zl": 1 - place["zl"]} if layer_of(place) == layer else None)

    with jax.named_scope("memory"):
        memory_here = across(encoded, 0)
        memory = jnp.concatenate([memory_here, over(memory_here, "section", layer=1)], axis=0)
    with jax.named_scope("cotangent_in"):
        cot = turned(after(cot_row, encoded)).astype(jnp.float32)

    cross_out_rows, *kept_cross = attend(dec_flag, middle_low, memory, w_cross, cross_extras, False)
    cross_total = middle + cross_out_rows
    crossed = layer_norm(cross_total, gains[1], biases[1])
    crossed_low = low(crossed)
    dec_out, dec_active, dec_slope = ffn(dec_flag, crossed_low, w_ffn)
    dec_total = crossed + dec_out
    decoded = low(layer_norm(dec_total, gains[2], biases[2]))

    d_dec_total, dec_gain_c, dec_bias_c = norm_back(dec_total, gains[2], biases[2], cot)
    d_dec_low = low(d_dec_total)
    d_after, dec_inner = ffn_back(dec_flag, d_dec_low, w_ffn, dec_slope)
    d_cross_total, dec_gain_b, dec_bias_b = norm_back(
        cross_total, gains[1], biases[1], d_dec_total + d_after
    )
    d_queries, d_pairs, cross_keep, cross_send = attend_back(
        dec_flag, low(d_cross_total), middle_low, memory, w_cross, kept_cross, cross_extras, False, 0, 4
    )
    d_middle_part, d_memory = attend_inputs(
        dec_flag,
        w_cross,
        [d_queries[at : at + 1] for at in range(4)],
        [d_pairs[at : at + 1] for at in range(4)],
    )
    with jax.named_scope("d_memory"):
        d_memory_here = d_memory[: 2 * quarter] + over(
            low(d_memory[2 * quarter :]), "section", layer=1
        ).astype(jnp.float32)
        d_memory_low = low(d_memory_here)
        d_encoded = across(d_memory_low, 1).astype(jnp.float32) + cot
    with jax.named_scope("cross_sums"):
        cross_sum = from_cores(after(cross_keep, d_memory_low), after(cross_send, d_memory_low), layer=1)

    d_enc_total, enc_gain_c, enc_bias_c = norm_back(enc_total, gains[2], biases[2], d_encoded)
    d_enc_low = low(d_enc_total)
    second_keep, second_send = ffn_grad(
        flag, after(pick(d_enc_low, d_dec_low), cross_sum), enc_active, dec_active, w_ffn[1]
    )
    with jax.named_scope("ffn_sums"):
        second_sum = from_cores(second_keep, second_send)
    d_enc_middle, enc_inner = ffn_back(enc_flag, after(d_enc_low, second_keep), w_ffn, enc_slope)
    with jax.named_scope("cross_sums"):
        cross_plane = plane_summed(after(cross_sum, second_sum), layer=1)
    first_keep, first_send = ffn_grad(
        flag, after(pick(middle_low, crossed_low), second_sum), enc_inner, dec_inner, w_ffn[0]
    )
    with jax.named_scope("ffn_sums"):
        second_rows = rows_summed(second_sum, count)
        first_sum = from_cores(first_keep, first_send)
        first_plane = plane_summed(after(first_sum, cross_plane))
        first_share = rows_summed(first_plane, count)
        second_share = plane_summed(after(second_rows, first_plane))
    with jax.named_scope("cross_sums"):
        share_cross = rows_summed(after(cross_plane, first_plane), count, layer=1)

    d_middle = pick(d_enc_total + d_enc_middle, d_cross_total + d_middle_part)
    d_self_total, gain_s, bias_s = norm_back(self_total, self_gain, self_bias, d_middle)
    d_self_low = low(d_self_total)
    earlier = {1: (first_keep,), 2: (first_sum,), 3: (second_rows,), 0: (first_plane,)}
    pieces, self_sums = {}, {}
    for at in (1, 2, 3, 0):
        d_queries, d_pairs, keep, send = attend_back(
            flag,
            after(d_self_low, *earlier[at]),
            start_low[: 2 * quarter],
            start_low,
            w_self,
            kept_self,
            self_extras,
            True,
            at,
            1,
        )
        pieces[at] = (d_queries, d_pairs)
        with jax.named_scope("self_sums"):
            self_sums[at] = from_cores(keep, send)
    d_start_q, d_start_kv = attend_inputs(
        flag, w_self, [pieces[at][0] for at in range(4)], [pieces[at][1] for at in range(4)]
    )
    d_start = d_self_total + d_start_q + d_start_kv[: 2 * quarter]
    with jax.named_scope("d_start"):
        d_start = d_start + over(low(d_start_kv[2 * quarter :]), "section").astype(jnp.float32)
    d_source, gain_a, bias_a = norm_back(
        rows_here.astype(jnp.float32), gains[0], biases[0], d_start
    )
    with jax.named_scope("hidden_out"):
        hidden_out = rows_out(after(pick(encoded, decoded), pieces[0][0]))
    with jax.named_scope("hidden_grad"):
        hidden_grad = rows_out(low(pick(d_source, d_start))).astype(jnp.float32)

    with jax.named_scope("self_sums"):
        both = after(jnp.concatenate([self_sums[at] for at in range(4)], axis=0), second_share)
        columns = both.shape[2] // 2
        share_self = [
            rows_summed(plane_summed(both[:, :, :columns]), count),
            plane_summed(rows_summed(both[:, :, columns:], count)),
        ]
        share_self = swapped(jnp.concatenate(share_self, axis=1)).astype(jnp.float32)
    with jax.named_scope("ffn_sums"):
        share_ffn = swapped(jnp.concatenate([first_share, second_share], axis=1)).astype(jnp.float32)
    share_first, share_second = share_ffn[:, :units], share_ffn[:, units:].T
    g_query, g_key, g_value, g_out = unpack_heads(share_self)
    grad_qkv = jnp.stack([g_query, g_key, g_value], axis=1)
    c_query, c_key, c_value, c_out = unpack_heads(share_cross)
    with jax.named_scope("cross_out"):
        for_enc = cross_out(jnp.concatenate([c_key, c_value], axis=1), 0)
        for_dec = cross_out(jnp.concatenate([c_query, c_out], axis=1), 1)
    cross = jnp.where(core == 0, for_enc, for_dec).astype(jnp.float32)

    norm_sums = jnp.stack(
        [
            pick(gain_a, gain_s),
            pick(gain_s, dec_gain_b),
            pick(enc_gain_c, dec_gain_c),
            pick(bias_a, bias_s),
            pick(bias_s, dec_bias_b),
            pick(enc_bias_c, dec_bias_c),
        ]
    )
    sums = norm_sums.reshape((6, 2, 2) + (2,) * count + (2, 2, -1))
    sums = jnp.stack(
        [jnp.stack([sums[:, 0, 1], sums[:, 1, 0]], axis=1), jnp.stack([sums[:, 0, 0], sums[:, 1, 1]], axis=1)], axis=1
    )
    for axes in [("section",), Z] + [("e%d" % at,) for at in range(count)] + [("ty",), ("tx",)]:
        sums = in_order(sums, lax.axis_index(axes[0]), 1)
        sums = sums[:, 0] + over(sums[:, 1], *axes)
    norm_shares = swapped(sums)
    return (
        hidden_out,
        hidden_grad,
        grad_qkv[None],
        g_out[None],
        cross[None, :, :width],
        cross[None, :, width:],
        share_first[None],
        share_second[None],
        norm_shares[None, :3],
        norm_shares[None, 3:],
    )


def solution(mesh):
    _, dp_count, _ = mesh.devices.shape
    count = dp_count.bit_length() - 3
    names = axes_of(count)
    dp, tensor = names[1:-2], names[-2:]
    split = Mesh(mesh.devices.reshape((2,) * len(names)), names)
    rows = P("section", None, dp, tensor, None)
    in_specs = (
        rows,
        rows,
        P(None, None, dp, None),
        P("section", dp, None, tensor),
        P("section", dp, tensor),
        P("section", dp, tensor),
        P("section", dp, tensor),
        P("section", dp, tensor),
        P("section", tensor, dp),
        P("section", None, None),
        P("section", None, None),
    )
    out_specs = (
        rows,
        rows,
        P("section", dp, None, tensor),
        P("section", dp, tensor),
        P("section", dp, tensor),
        P("section", dp, tensor),
        P("section", dp, tensor),
        P("section", tensor, dp),
        P("section", None, dp + tensor),
        P("section", None, dp + tensor),
    )
    return jax.shard_map(
        functools.partial(body, count), mesh=split, in_specs=in_specs, out_specs=out_specs, check_vma=False
    )
```

```python
import functools

import jax
import jax.numpy as jnp
from jax import lax
from jax.experimental import pallas as pl
from jax.experimental.pallas import tpu as pltpu
from jax.sharding import Mesh
from jax.sharding import PartitionSpec as P

HDIM = 64
LANES = 128
MASKED = -1e30
NORM_EPS = 1e-05
VMEM_BYTES = 56 * 1024 * 1024

SEG_LANES = 8
PART_LANE = 12

PARTS = 2
HEADS = ((0, 1, 2, 0, 0), (0, 1, 2, 1, 1), (1, 3, 0, 0, 1))


def mul(a, b):
    return jnp.dot(a, b, preferred_element_type=jnp.float32)


def mul_nt(a, b):
    return lax.dot_general(a, b, (((1,), (1,)), ((), ())), preferred_element_type=jnp.float32)


def mul_tn(a, b):
    return lax.dot_general(a, b, (((0,), (0,)), ((), ())), preferred_element_type=jnp.float32)


def tile_of(values, index):
    return values[:, index * LANES : (index + 1) * LANES]


def lane_ids(rows):
    return lax.broadcasted_iota(jnp.int32, (rows, LANES), 1)


def half_mask(rows, half):
    lanes = lane_ids(rows)
    return lanes >= HDIM if half else lanes < HDIM


def in_parts(base, column):
    lanes = lane_ids(base.shape[0])
    high = column.astype(jnp.bfloat16).astype(jnp.float32)
    rest = column - high
    middle = rest.astype(jnp.bfloat16).astype(jnp.float32)
    low = rest - middle
    parts = jnp.where(
        lanes == PART_LANE,
        high,
        jnp.where(lanes == PART_LANE + 1, middle, jnp.where(lanes == PART_LANE + 2, low, base)),
    )
    return parts.astype(jnp.bfloat16)


def with_triangle(scores, tri, at):
    size = tri.shape[1]
    pieces = []
    if at > 0:
        pieces.append(scores[:, : at * size])
    pieces.append(scores[:, at * size : (at + 1) * size] + tri)
    pieces.append(scores[:, (at + 1) * size :])
    return jnp.concatenate(pieces, axis=1)


def places(core, block):
    return [pl.multiple_of((1 - core) * block, block), pl.multiple_of((2 + core) * block, block)]


def assemble(flag_ref, own_refs, peer_refs, w_ref):
    core, block = flag_ref[0], own_refs[0].shape[1] // 2
    for holder, refs in ((core, own_refs), (1 - core, peer_refs)):
        for part, ref in enumerate(refs):
            width = ref.shape[2]
            for at, place in enumerate(places(holder, block)):
                w_ref[pl.ds(place, block), part * width : (part + 1) * width] = ref[0, at * block : (at + 1) * block]


def hand_out(flag_ref, g_ref, keep_ref, send_ref):
    core, block = flag_ref[0], keep_ref.shape[1] // 2
    for holder, ref in ((core, keep_ref), (1 - core, send_ref)):
        for at, place in enumerate(places(holder, block)):
            ref[0, at * block : (at + 1) * block] = g_ref[pl.ds(place, block), :]


def where_active(kernel):
    def guarded(flag_ref, *refs):
        @pl.when(flag_ref[1] == 1)
        def _():
            kernel(flag_ref, *refs)

    return guarded


def scaled_queries(q_ref, at, q_tile, q_half):
    queries = q_ref[0, at, q_tile * LANES : (q_tile + 1) * LANES] * 0.125
    return jnp.where(half_mask(queries.shape[0], q_half), queries, 0).astype(jnp.bfloat16)


def units_of(total, rows):
    return [
        (slice(part * rows, (part + 1) * rows), part, head)
        for part in range(total // rows)
        for head in range(len(HEADS))
    ]


def attend_kernel(causal, flag_ref, xq_ref, xkv_ref, *refs):
    own_refs, peer_refs = refs[:1], refs[1:2]
    qx_ref, kx_ref, tri_ref, o_ref, q_ref, kv_ref, c_ref, l_ref, w_ref = refs[2:]
    block = pl.program_id(0)
    assemble(flag_ref, own_refs, peer_refs, w_ref)
    q_ref[0] = mul(xq_ref[...], w_ref[:, : 2 * LANES]).astype(jnp.bfloat16)
    kv_ref[0] = mul(xkv_ref[...], w_ref[:, LANES : 5 * LANES]).astype(jnp.bfloat16)
    rows = tri_ref.shape[0]
    low = half_mask(rows, 0)

    def scores_of(at, part, head):
        q_tile, k_tile, _, q_half, _ = HEADS[head]
        keys = kv_ref[0, :, k_tile * LANES : (k_tile + 1) * LANES]
        scores = mul_nt(
            jnp.concatenate([scaled_queries(q_ref, at, q_tile, q_half), qx_ref[at, :]], axis=1),
            jnp.concatenate([keys, kx_ref[...]], axis=1),
        )
        return with_triangle(scores, tri_ref[...], part) if causal else scores

    units = units_of(q_ref.shape[1], rows)
    ahead = scores_of(*units[0])
    contexts, totals = [], None
    for index, (at, part, head) in enumerate(units):
        scores = ahead
        if index + 1 < len(units):
            ahead = scores_of(*units[index + 1])
        v_tile = HEADS[head][2]
        values = kv_ref[0, :, v_tile * LANES : (v_tile + 1) * LANES]
        highest = jnp.max(scores, axis=1, keepdims=True)
        weights = jnp.exp(scores - highest)
        sums = jnp.sum(weights, axis=1, keepdims=True)
        contexts.append(mul(weights.astype(jnp.bfloat16), values) / sums)
        logs = jnp.broadcast_to(highest + jnp.log(sums), (rows, LANES))
        totals = logs if head == 0 else jnp.where(lane_ids(rows) == head, logs, totals)
        if head == len(HEADS) - 1:
            c_ref[0, at, :LANES] = jnp.where(low, 0, contexts[2]).astype(jnp.bfloat16)
            c_ref[0, at, LANES:] = jnp.where(low, contexts[0], contexts[1]).astype(jnp.bfloat16)
            l_ref[0, at, :] = totals
            contexts = []
    out = mul_nt(c_ref[0], w_ref[:, 4 * LANES :])

    @pl.when(block == 0)
    def _():
        o_ref[...] = out

    @pl.when(block > 0)
    def _():
        o_ref[...] += out


def attend_back_kernel(causal, flag_ref, do_ref, xq_ref, xkv_ref, *refs):
    own_refs, peer_refs = refs[:1], refs[1:2]
    q_ref, kv_ref, c_ref, l_ref, qx_ref, kx_ref, tri_ref, dxq_ref, dxkv_ref, *refs = refs[2:]
    keep_ref, send_ref, w_ref, sum_ref, dq_ref, dkv_ref, g_ref = refs
    rows = tri_ref.shape[0]
    assemble(flag_ref, own_refs, peer_refs, w_ref)
    d_context = mul(do_ref[...], w_ref[:, 4 * LANES :]).astype(jnp.bfloat16)
    low = half_mask(rows, 0)

    def products_of(at, part, head):
        q_tile, k_tile, v_tile, q_half, v_half = HEADS[head]
        c_tile = 0 if head == 2 else 1
        keys = kv_ref[0, :, k_tile * LANES : (k_tile + 1) * LANES]
        values = kv_ref[0, :, v_tile * LANES : (v_tile + 1) * LANES]
        queries = scaled_queries(q_ref, at, q_tile, q_half)
        d_rows = jnp.where(half_mask(rows, v_half), tile_of(d_context[at], c_tile), 0).astype(jnp.bfloat16)
        total = l_ref[0, at, head : head + 1]
        scores = mul_nt(
            jnp.concatenate([queries, in_parts(qx_ref[at, :].astype(jnp.float32), -total)], axis=1),
            jnp.concatenate([keys, kx_ref[...]], axis=1),
        )
        if causal:
            scores = with_triangle(scores, tri_ref[...], part)
        return scores, mul_nt(d_rows, values), queries, d_rows, keys

    units = units_of(q_ref.shape[1], rows)
    ahead = products_of(*units[0])
    d_queries = []
    for index, (at, part, head) in enumerate(units):
        scores, d_probs, queries, d_rows, keys = ahead
        if index + 1 < len(units):
            ahead = products_of(*units[index + 1])
        _, k_tile, v_tile, _, _ = HEADS[head]
        probs = jnp.exp(scores)
        inner = jnp.sum(probs * d_probs, axis=1, keepdims=True)
        d_scores = (probs * (d_probs - inner)).astype(jnp.bfloat16)
        d_values = mul_tn(probs.astype(jnp.bfloat16), d_rows)
        d_keys = mul_tn(d_scores, queries)
        d_queries.append(mul(d_scores, keys) * 0.125)
        k_at = slice(k_tile * LANES, (k_tile + 1) * LANES)
        v_at = slice(v_tile * LANES, (v_tile + 1) * LANES)
        if part == 0 and head != 1:
            sum_ref[:, k_at] = d_keys
            sum_ref[:, v_at] = d_values
        else:
            sum_ref[:, k_at] += d_keys
            sum_ref[:, v_at] += d_values
        if head == len(HEADS) - 1:
            dq_ref[at, :LANES] = jnp.where(low, d_queries[0], d_queries[1]).astype(jnp.bfloat16)
            dq_ref[at, LANES:] = jnp.where(low, d_queries[2], 0).astype(jnp.bfloat16)
            d_queries = []
    dkv_ref[...] = sum_ref[...].astype(jnp.bfloat16)
    d_xq = mul_nt(dq_ref[...], w_ref[:, : 2 * LANES])
    d_xkv = mul_nt(dkv_ref[...], w_ref[:, LANES : 5 * LANES])

    @pl.when(pl.program_id(0) == 0)
    def _():
        dxq_ref[...] = d_xq
        dxkv_ref[...] = d_xkv

    @pl.when(pl.program_id(0) > 0)
    def _():
        dxq_ref[...] += d_xq
        dxkv_ref[...] += d_xkv

    grad_q = mul_tn(xq_ref[...], dq_ref[...])
    grad_kv = mul_tn(xkv_ref[...], dkv_ref[...])
    grad_o = mul_tn(do_ref[...], c_ref[0])
    g_ref[:, :LANES] = grad_q[:, :LANES].astype(jnp.bfloat16)
    g_ref[:, LANES : 2 * LANES] = (grad_q[:, LANES:] + grad_kv[:, :LANES]).astype(jnp.bfloat16)
    g_ref[:, 2 * LANES : 4 * LANES] = grad_kv[:, LANES : 3 * LANES].astype(jnp.bfloat16)
    g_ref[:, 4 * LANES : 5 * LANES] = (grad_kv[:, 3 * LANES :] + grad_o[:, :LANES]).astype(jnp.bfloat16)
    g_ref[:, 5 * LANES :] = grad_o[:, LANES:].astype(jnp.bfloat16)
    hand_out(flag_ref, g_ref, keep_ref, send_ref)


def whole(shape):
    return pl.BlockSpec(shape, lambda j, flag: (0,) * len(shape))


def per_block(shape, first=0, gate=1):
    return pl.BlockSpec((1,) + shape, lambda j, flag: (first + j * flag[gate],) + (0,) * len(shape))


shape = jax.ShapeDtypeStruct


def call(kernel, name, micros, moved, grid, in_specs, out_specs, out_shape, scratch, *operands):
    return pl.pallas_call(
        where_active(kernel),
        grid_spec=pltpu.PrefetchScalarGridSpec(
            num_scalar_prefetch=1,
            grid=(grid,),
            in_specs=in_specs,
            out_specs=out_specs,
            scratch_shapes=scratch,
        ),
        out_shape=out_shape,
        compiler_params=pltpu.CompilerParams(vmem_limit_bytes=VMEM_BYTES),
        cost_estimate=cost(micros, moved),
        name=name,
    )(*operands)


def cost(micros, moved):
    return pl.CostEstimate(flops=int(micros * 1.15e9), bytes_accessed=int(moved), transcendentals=0)


def attend(flag, xq, xkv, weights, extras, causal):
    rows, width = xq.shape
    keys = xkv.shape[0]
    blocks = weights[0].shape[0]
    return call(
        functools.partial(attend_kernel, causal),
        "attend_self" if causal else "attend_cross",
        20,
        24 * 2**20,
        blocks,
        [whole((rows, width)), whole((keys, width))]
        + [per_block(part.shape[1:]) for part in weights]
        + [whole(extra.shape) for extra in extras],
        [
            whole((rows, width)),
            per_block((rows, 2 * LANES)),
            per_block((keys, 4 * LANES)),
            per_block((rows, 2 * LANES)),
            per_block((rows, LANES)),
        ],
        [
            shape((rows, width), jnp.float32),
            shape((blocks, rows, 2 * LANES), jnp.bfloat16),
            shape((blocks, keys, 4 * LANES), jnp.bfloat16),
            shape((blocks, rows, 2 * LANES), jnp.bfloat16),
            shape((blocks, rows, LANES), jnp.float32),
        ],
        [pltpu.VMEM((width, 6 * LANES), jnp.bfloat16)],
        flag,
        xq,
        xkv,
        *weights,
        *extras,
    )


def attend_back(flag, d_out, xq, xkv, weights, kept, extras, causal):
    rows, width = xq.shape
    keys = xkv.shape[0]
    blocks = weights[0].shape[0]
    return call(
        functools.partial(attend_back_kernel, causal),
        "attend_self_back" if causal else "attend_cross_back",
        40,
        24 * 2**20,
        blocks,
        [whole((rows, width)), whole((rows, width)), whole((keys, width))]
        + [per_block(part.shape[1:]) for part in weights]
        + [
            per_block((rows, 2 * LANES)),
            per_block((keys, 4 * LANES)),
            per_block((rows, 2 * LANES)),
            per_block((rows, LANES)),
        ]
        + [whole(extra.shape) for extra in extras],
        [whole((rows, width)), whole((keys, width))] + [per_block(part.shape[1:]) for part in weights],
        [shape((rows, width), jnp.float32), shape((keys, width), jnp.float32)]
        + [shape(part.shape, jnp.bfloat16) for part in weights],
        [
            pltpu.VMEM((width, 6 * LANES), jnp.bfloat16),
            pltpu.VMEM((keys, 4 * LANES), jnp.float32),
            pltpu.VMEM((rows, 2 * LANES), jnp.bfloat16),
            pltpu.VMEM((keys, 4 * LANES), jnp.bfloat16),
            pltpu.VMEM((width, 6 * LANES), jnp.bfloat16),
        ],
        flag,
        d_out,
        xq,
        xkv,
        *weights,
        *kept,
        *extras,
    )


CHUNK = 256


def ffn_kernel(flag_ref, x_ref, *refs):
    own_refs, peer_refs = refs[:PARTS], refs[PARTS : 2 * PARTS]
    z_ref, g_ref, slope_ref, w_ref = refs[2 * PARTS :]
    block = pl.program_id(0)
    assemble(flag_ref, own_refs, peer_refs, w_ref)
    units = own_refs[0].shape[2]

    def inner_of(at):
        return mul(x_ref[...], w_ref[:, at : at + CHUNK])

    ahead = inner_of(0)
    out = 0.0
    for at in range(0, units, CHUNK):
        inner = ahead
        if at + CHUNK < units:
            ahead = inner_of(at + CHUNK)
        spread = 0.5 * (1.0 + lax.erf(inner * (0.5**0.5)))
        bell = jnp.exp(-0.5 * inner * inner) * 0.3989422804014327
        active = (inner * spread).astype(jnp.bfloat16)
        g_ref[0, :, at : at + CHUNK] = active
        slope_ref[0, :, at : at + CHUNK] = (spread + inner * bell).astype(jnp.bfloat16)
        out = out + mul_nt(active, w_ref[:, units + at : units + at + CHUNK])

    @pl.when(block == 0)
    def _():
        z_ref[...] = out

    @pl.when(block > 0)
    def _():
        z_ref[...] += out


def ffn(flag, x, weights):
    rows, width = x.shape
    blocks, _, units = weights[0].shape
    return call(
        ffn_kernel,
        "ffn",
        12,
        rows * units * blocks * 16,
        blocks,
        [whole((rows, width))] + [per_block(part.shape[1:]) for part in weights],
        [whole((rows, width)), per_block((rows, units)), per_block((rows, units))],
        [
            shape((rows, width), jnp.float32),
            shape((blocks, rows, units), jnp.bfloat16),
            shape((blocks, rows, units), jnp.bfloat16),
        ],
        [pltpu.VMEM((width, 2 * units), jnp.bfloat16)],
        flag,
        x,
        *weights,
    )


def ffn_back_kernel(flag_ref, dz_ref, *refs):
    own_refs, peer_refs = refs[:PARTS], refs[PARTS : 2 * PARTS]
    slope_ref, dx_ref, dh_ref, w_ref = refs[2 * PARTS :]
    block = pl.program_id(0)
    assemble(flag_ref, own_refs, peer_refs, w_ref)
    units = own_refs[0].shape[2]
    d_active = mul(dz_ref[...], w_ref[:, units:])
    d_inner = (d_active * slope_ref[0].astype(jnp.float32)).astype(jnp.bfloat16)
    dh_ref[0] = d_inner
    out = mul_nt(d_inner, w_ref[:, :units])

    @pl.when(block == 0)
    def _():
        dx_ref[...] = out

    @pl.when(block > 0)
    def _():
        dx_ref[...] += out


def ffn_back(flag, dz, weights, slope):
    rows, width = dz.shape
    blocks, _, units = weights[0].shape
    return call(
        ffn_back_kernel,
        "ffn_back",
        12,
        rows * units * blocks * 12,
        blocks,
        [whole((rows, width))] + [per_block(part.shape[1:]) for part in weights] + [per_block((rows, units))],
        [whole((rows, width)), per_block((rows, units))],
        [
            shape((rows, width), jnp.float32),
            shape((blocks, rows, units), jnp.bfloat16),
        ],
        [pltpu.VMEM((width, 2 * units), jnp.bfloat16)],
        flag,
        dz,
        *weights,
        slope,
    )


def ffn_grad_kernel(flag_ref, left_ref, enc_ref, dec_ref, keep_ref, send_ref, g_ref):
    right = jnp.where(flag_ref[2] == 1, enc_ref[0], dec_ref[0])
    g_ref[...] = mul_tn(left_ref[...], right).astype(jnp.bfloat16)
    hand_out(flag_ref, g_ref, keep_ref, send_ref)


def ffn_grad(flag, left, enc_right, dec_right, like):
    rows, width = left.shape
    blocks, _, units = enc_right.shape
    return call(
        ffn_grad_kernel,
        "ffn_grad",
        6,
        rows * units * blocks * 8,
        blocks,
        [whole((rows, width)), per_block((rows, units), 0, 2), per_block((rows, units), 0, 3)],
        [per_block(like.shape[1:])] * 2,
        [shape(like.shape, jnp.bfloat16)] * 2,
        [pltpu.VMEM((width, units), jnp.bfloat16)],
        flag,
        left,
        enc_right,
        dec_right,
    )


def layer_norm(values, gain_row, bias_row):
    average = jnp.mean(values, axis=-1, keepdims=True)
    centered = values - average
    variance = jnp.mean(centered * centered, axis=-1, keepdims=True)
    return centered * lax.rsqrt(variance + NORM_EPS) * gain_row + bias_row


def norm_back(values, gain_row, bias_row, upstream):
    _, pullback = jax.vjp(layer_norm, values, gain_row, bias_row)
    return pullback(upstream)


def low(values):
    return values.astype(jnp.bfloat16)


def axes_of(count):
    return ("section", "zh", "zl") + tuple("e%d" % at for at in range(count)) + ("ty", "tx")


def layer_of(place):
    return 1 ^ place["zh"] ^ place["zl"]


def moved(x, names, to):
    names = [name for name in axes_of(8) if name in names]

    def index(place):
        return sum(place[name] << (len(names) - 1 - at) for at, name in enumerate(names))

    pairs = []
    for source in range(2 ** len(names)):
        place = {name: source >> (len(names) - 1 - at) & 1 for at, name in enumerate(names)}
        target = to(place)
        if target is not None:
            pairs.append((source, index(target)))
    return lax.ppermute(x, tuple(names), pairs)


def over(x, *axes, layer=None):
    def to(place):
        if layer is not None and layer_of(place) != layer:
            return None
        return {**place, **{axis: 1 - place[axis] for axis in axes}}

    return moved(x, axes if layer is None else axes + Z, to)


Z = ("zh", "zl")


def swapped(x):
    def to(place):
        if place["section"] == layer_of(place):
            return place
        return {"section": 1 - place["section"], "zh": place["zh"], "zl": 1 - place["zl"]}

    return moved(x, ("section",) + Z, to)


def turned(x):
    return moved(x, ("section", "ty"), lambda place: {"section": place["ty"], "ty": place["section"]})


def sent_home(x, other):
    def to(place):
        return {
            "section": layer_of(place),
            "zh": place["zh"],
            "zl": 1 ^ place["zh"] ^ place["ty"],
            "ty": place["section"],
            "tx": place["tx"] ^ other,
        }

    return moved(x, ("section",) + Z + ("ty", "tx"), to)


def cross_in(x, layer):
    def to(place):
        if place["section"] != layer:
            return None
        return {"section": layer_of(place), "zh": place["zh"], "zl": place["zh"]}

    return moved(x, ("section",) + Z, to)


def cross_out(x, layer):
    def to(place):
        if layer_of(place) != 1:
            return None
        return {"section": layer, "zh": place["zh"], "zl": 1 ^ place["zh"] ^ place["section"]}

    return moved(x, ("section",) + Z, to)


def in_order(x, flag, axis):
    return jnp.where(flag == 1, jnp.flip(x, axis), x)


def pack_heads(query, key, value, out):
    pair = 2 * HDIM
    return jnp.concatenate(
        [
            query,
            value[:, pair:],
            key[:, :pair],
            value[:, :pair],
            key[:, pair:],
            out[:, pair:],
            out[:, :pair],
        ],
        axis=1,
    )


def unpack_heads(packed):
    part = [packed[:, at * HDIM : (at + 1) * HDIM] for at in range(12)]
    query = jnp.concatenate(part[0:3], axis=1)
    key = jnp.concatenate([part[4], part[5], part[8]], axis=1)
    value = jnp.concatenate([part[6], part[7], part[3]], axis=1)
    out = jnp.concatenate([part[10], part[11], part[9]], axis=1)
    return query, key, value, out


def after(x, *earlier):
    return lax.optimization_barrier((x,) + earlier)[0]


def plane_gathered(x, until=(), **only):
    parts = [x, over(x, "tx", **only), over(x, "ty", **only), over(x, "ty", "tx", **only)]
    return jnp.stack([after(part, *until) for part in parts])


def plane_summed(x, **only):
    terms = [x[0], over(x[1], "tx", **only), over(x[2], "ty", **only), over(x[3], "ty", "tx", **only)]
    return low(sum(term.astype(jnp.float32) for term in terms))


def rows_gathered(x, count, until=(), **only):
    for axes in [("e%d" % at,) for at in reversed(range(count))] + [Z]:
        parts = [after(part, *until) for part in (x, over(x, *axes, **only))]
        both = in_order(jnp.stack(parts, axis=-3), lax.axis_index(axes[0]), x.ndim - 2)
        x = both.reshape(x.shape[:-2] + (2 * x.shape[-2], x.shape[-1]))
    return x


def rows_summed(x, count, **only):
    for axes in [Z] + [("e%d" % at,) for at in range(count)]:
        halves = x.reshape(x.shape[:-2] + (2, x.shape[-2] // 2, x.shape[-1]))
        halves = in_order(halves, lax.axis_index(axes[0]), x.ndim - 2)
        x = plus(halves[..., 0, :, :], over(halves[..., 1, :, :], *axes, **only))
    return x


def plus(first, second):
    return low(first.astype(jnp.float32) + second.astype(jnp.float32))


def from_cores(keep, send, **only):
    return plus(keep, over(send, "section", **only))


def body(
    count,
    hidden,
    cotangent,
    segments,
    sa_qkv,
    sa_out,
    cross_one,
    cross_two,
    ffn_in,
    ffn_out,
    norm_gain,
    norm_bias,
):
    core = lax.axis_index("section")
    x_at, y_at, zh_at, zl_at = (lax.axis_index(name) for name in ("tx", "ty", "zh", "zl"))
    layer = 1 ^ zh_at ^ zl_at
    on_encoder = layer == 0
    quarter = hidden.shape[3]
    enc_flag = jnp.stack([core, 1 - layer, 1 - layer, layer])
    dec_flag = jnp.stack([core, layer, 1 - layer, layer])
    flag = jnp.stack([core, jnp.ones_like(core), 1 - layer, layer])

    def pick(first, second):
        return jnp.where(on_encoder, first, second)

    def of_one_row(x):
        both = in_order(x[0, :, 0], x_at, 0)
        return in_order(jnp.stack([both[0], over(both[1], "tx")]), x_at, 0).reshape(2 * quarter, -1)

    def rows_out(x):
        mine, other = in_order(x.reshape(2, quarter, -1), x_at, 0)
        return in_order(jnp.stack([sent_home(mine, 0), sent_home(other, 1)]), x_at, 0)[None, :, None]

    units = ffn_in.shape[2]
    width = cross_one.shape[2]
    packed_self = pack_heads(sa_qkv[0, :, 0], sa_qkv[0, :, 1], sa_qkv[0, :, 2], sa_out[0])
    packed_ffn = jnp.concatenate([ffn_in[0], ffn_out[0].T], axis=1)
    with jax.named_scope("norms_in"):
        norms = swapped(jnp.concatenate([norm_gain[0], norm_bias[0]], axis=0))
        gains, biases = norms[:3], norms[3:]
        seg_own = segments[:, :, 0].astype(jnp.float32)
        seg_here = jnp.where(zl_at == 1 ^ zh_at ^ y_at, seg_own, over(seg_own, "zl")).astype(jnp.int32)
    with jax.named_scope("hidden_in"):
        one_row = of_one_row(hidden)
    with jax.named_scope("self_weights"):
        shard_self = swapped(packed_self)
    with jax.named_scope("ffn_weights"):
        shard_ffn = swapped(after(packed_ffn, shard_self))
        shard_first, shard_second = shard_ffn[:, :units], shard_ffn[:, units:]

    def both_rows(x):
        for_enc = rows_gathered(x, count, layer=0)
        return pick(for_enc, rows_gathered(after(x, for_enc), count, layer=1))

    with jax.named_scope("self_weights"):
        rows_self = both_rows(shard_self)
    with jax.named_scope("hidden_in"):
        rows_here = turned(swapped(after(one_row, shard_ffn)))
        rows_all = jnp.concatenate([rows_here, over(rows_here, "section")], axis=0)
    with jax.named_scope("self_weights"):
        own_self = plane_gathered(after(rows_self, rows_here))
        w_self = [own_self, over(own_self, "section")]
    with jax.named_scope("cross_weights"):
        cross_low = after(jnp.concatenate([cross_one[0], cross_two[0]], axis=1), rows_here)
        pair_kv, pair_qo = cross_in(cross_low, 0), cross_in(cross_low, 1)
        packed = pack_heads(pair_qo[:, :width], pair_kv[:, :width], pair_kv[:, width:], pair_qo[:, width:])
    with jax.named_scope("ffn_weights"):
        rows_first = both_rows(after(shard_first, rows_self))
        plane_second = plane_gathered(after(shard_second, own_self))
    both_segments = in_order(seg_here, x_at, 1)[:, 0]
    ordered = in_order(both_segments.reshape(2, 2, 2 * quarter), core, 1).reshape(2, 4 * quarter)
    source_seg, target_seg = ordered[0], ordered[1]
    self_seg = pick(source_seg, target_seg)
    parts = jnp.arange(4)
    quarter_of = jnp.repeat(2 * ((parts // 2) ^ core) + parts % 2, quarter)
    lanes = jnp.arange(LANES)[None, :]

    def key_extras(seg):
        differs = jnp.logical_and(lanes < SEG_LANES, seg[:, None] != lanes)
        later = jnp.logical_and(
            jnp.logical_and(lanes >= SEG_LANES, lanes < PART_LANE),
            quarter_of[:, None] > lanes - SEG_LANES,
        )
        part = jnp.logical_and(lanes >= PART_LANE, lanes < PART_LANE + 3)
        return jnp.where(differs | later | part, 1.0, 0.0).astype(jnp.bfloat16)

    def query_extras(seg, causal):
        seg, at = seg[: 2 * quarter], quarter_of[: 2 * quarter]
        same = seg[:, None] == lanes
        here = jnp.logical_and(at[:, None] + SEG_LANES == lanes, causal)
        return jnp.where(same | here, MASKED, 0.0).astype(jnp.bfloat16)

    at_row = jnp.arange(quarter)
    later_key = jnp.logical_and(at_row[None, :] > at_row[:, None], jnp.logical_not(on_encoder))
    tri = jnp.where(later_key, MASKED, 0.0).astype(jnp.float32)
    self_extras = (query_extras(self_seg, jnp.logical_not(on_encoder)), key_extras(self_seg), tri)
    cross_extras = (query_extras(target_seg, False), key_extras(source_seg), tri)

    start = rows_all.astype(jnp.float32)
    start = pick(layer_norm(start, gains[0], biases[0]), start)
    start_here = start[: 2 * quarter]
    start_low = low(start)
    self_gain, self_bias = pick(gains[1], gains[0]), pick(biases[1], biases[0])
    self_out, *kept_self = attend(
        flag, start_low[: 2 * quarter], after(start_low, plane_second), w_self, self_extras, True
    )
    with jax.named_scope("ffn_weights"):
        own_first = plane_gathered(after(rows_first, plane_second), until=(self_out,))
        own_second = pick(
            rows_gathered(plane_second, count, until=(self_out,), layer=0),
            rows_gathered(plane_second, count, until=(self_out,), layer=1),
        )
        w_ffn = [own_first, own_second]
        w_ffn = w_ffn + [over(part, "section") for part in w_ffn]
    with jax.named_scope("cotangent_in"):
        cot_row = of_one_row(after(cotangent, self_out))
    self_total = start_here + self_out
    middle = layer_norm(self_total, self_gain, self_bias)
    middle_low = low(middle)

    with jax.named_scope("cross_weights"):
        rows_cross = rows_gathered(after(packed, plane_second), count, until=(self_out,), layer=1)
        own_cross = plane_gathered(rows_cross, layer=1)
        w_cross = [own_cross, over(own_cross, "section", layer=1)]

    enc_out, enc_active, enc_slope = ffn(enc_flag, middle_low, w_ffn)
    enc_total = middle + enc_out
    encoded = low(layer_norm(enc_total, gains[2], biases[2]))

    def across(x, layer):
        return moved(x, Z, lambda place: {**place, "zl": 1 - place["zl"]} if layer_of(place) == layer else None)

    with jax.named_scope("memory"):
        memory_here = across(encoded, 0)
        memory = jnp.concatenate([memory_here, over(memory_here, "section", layer=1)], axis=0)
    with jax.named_scope("cotangent_in"):
        cot = turned(swapped(after(cot_row, memory_here))).astype(jnp.float32)

    cross_out_rows, *kept_cross = attend(dec_flag, middle_low, memory, w_cross, cross_extras, False)
    cross_total = middle + cross_out_rows
    crossed = layer_norm(cross_total, gains[1], biases[1])
    crossed_low = low(crossed)
    dec_out, dec_active, dec_slope = ffn(dec_flag, crossed_low, w_ffn)
    dec_total = crossed + dec_out
    decoded = low(layer_norm(dec_total, gains[2], biases[2]))

    d_dec_total, dec_gain_c, dec_bias_c = norm_back(dec_total, gains[2], biases[2], cot)
    d_dec_low = low(d_dec_total)
    d_after, dec_inner = ffn_back(dec_flag, d_dec_low, w_ffn, dec_slope)
    d_cross_total, dec_gain_b, dec_bias_b = norm_back(
        cross_total, gains[1], biases[1], d_dec_total + d_after
    )
    d_middle_part, d_memory, cross_keep, cross_send = attend_back(
        dec_flag, low(d_cross_total), middle_low, memory, w_cross, kept_cross, cross_extras, False
    )
    with jax.named_scope("d_memory"):
        d_memory_here = d_memory[: 2 * quarter] + over(
            low(d_memory[2 * quarter :]), "section", layer=1
        ).astype(jnp.float32)
        d_memory_low = low(d_memory_here)
        d_encoded = across(d_memory_low, 1).astype(jnp.float32) + cot
    with jax.named_scope("cross_sums"):
        cross_sum = from_cores(after(cross_keep, d_memory_low), after(cross_send, d_memory_low), layer=1)
        cross_plane = plane_summed(cross_sum, layer=1)
        share_cross = rows_summed(cross_plane, count, layer=1)

    d_enc_total, enc_gain_c, enc_bias_c = norm_back(enc_total, gains[2], biases[2], d_encoded)
    d_enc_low = low(d_enc_total)
    second_keep, second_send = ffn_grad(
        flag, after(pick(d_enc_low, d_dec_low), cross_sum), enc_active, dec_active, w_ffn[1]
    )
    with jax.named_scope("ffn_sums"):
        second_sum = from_cores(second_keep, second_send)
    with jax.named_scope("hidden_out"):
        hidden_out = rows_out(after(pick(encoded, decoded), second_keep))
    d_enc_middle, enc_inner = ffn_back(enc_flag, after(d_enc_low, second_keep), w_ffn, enc_slope)
    with jax.named_scope("ffn_sums"):
        second_plane = plane_summed(after(second_sum, hidden_out))
    first_keep, first_send = ffn_grad(
        flag, after(pick(middle_low, crossed_low), second_sum), enc_inner, dec_inner, w_ffn[0]
    )
    with jax.named_scope("ffn_sums"):
        first_sum = from_cores(first_keep, first_send)
        first_plane = plane_summed(after(first_sum, second_plane))
        second_share = rows_summed(second_plane, count)
        first_share = rows_summed(first_plane, count)

    d_middle = pick(d_enc_total + d_enc_middle, d_cross_total + d_middle_part)
    d_self_total, gain_s, bias_s = norm_back(self_total, self_gain, self_bias, d_middle)
    d_start_q, d_start_kv, self_keep, self_send = attend_back(
        flag,
        after(low(d_self_total), first_sum, second_plane),
        start_low[: 2 * quarter],
        start_low,
        w_self,
        kept_self,
        self_extras,
        True,
    )
    d_start = d_self_total + d_start_q + d_start_kv[: 2 * quarter]
    with jax.named_scope("d_start"):
        d_start = d_start + over(low(d_start_kv[2 * quarter :]), "section").astype(jnp.float32)
    d_source, gain_a, bias_a = norm_back(
        rows_here.astype(jnp.float32), gains[0], biases[0], d_start
    )
    with jax.named_scope("hidden_grad"):
        hidden_grad = rows_out(low(pick(d_source, d_start))).astype(jnp.float32)

    with jax.named_scope("self_sums"):
        both = from_cores(self_keep, self_send)
        columns = both.shape[2] // 2
        share_self = [
            rows_summed(plane_summed(both[:, :, :columns]), count),
            plane_summed(rows_summed(both[:, :, columns:], count)),
        ]
        share_self = swapped(jnp.concatenate(share_self, axis=1)).astype(jnp.float32)
    with jax.named_scope("ffn_sums"):
        share_ffn = swapped(jnp.concatenate([first_share, second_share], axis=1)).astype(jnp.float32)
    share_first, share_second = share_ffn[:, :units], share_ffn[:, units:].T
    g_query, g_key, g_value, g_out = unpack_heads(share_self)
    grad_qkv = jnp.stack([g_query, g_key, g_value], axis=1)
    c_query, c_key, c_value, c_out = unpack_heads(share_cross)
    with jax.named_scope("cross_out"):
        for_enc = cross_out(jnp.concatenate([c_key, c_value], axis=1), 0)
        for_dec = cross_out(jnp.concatenate([c_query, c_out], axis=1), 1)
    cross = jnp.where(core == 0, for_enc, for_dec).astype(jnp.float32)

    norm_sums = jnp.stack(
        [
            pick(gain_a, gain_s),
            pick(gain_s, dec_gain_b),
            pick(enc_gain_c, dec_gain_c),
            pick(bias_a, bias_s),
            pick(bias_s, dec_bias_b),
            pick(enc_bias_c, dec_bias_c),
        ]
    )
    sides = jnp.arange(2)
    held, outer, inner = core ^ sides[:, None], zh_at ^ sides[None, :], jnp.zeros((1,), jnp.int32)
    for at in range(count):
        inner = (2 * inner[:, None] + (lax.axis_index("e%d" % at) ^ sides)[None, :]).reshape(-1)
    row_block = (2 * outer + (1 ^ outer ^ held)) * 2**count
    column_block = (2 * (y_at ^ sides)[:, None] + (x_at ^ sides)[None, :]).reshape(-1)
    order = (row_block[:, :, None] + inner) [..., None] * 4 + column_block
    sums = jnp.take(norm_sums.reshape(6, 2 ** (count + 4), -1), order.reshape(-1), axis=1)
    sums = sums.reshape((6, 2, 2) + (2,) * count + (2, 2, -1))
    for axes in [("section",), Z] + [("e%d" % at,) for at in range(count)] + [("ty",), ("tx",)]:
        sums = sums[:, 0] + over(sums[:, 1], *axes)
    norm_shares = swapped(sums)
    return (
        hidden_out,
        hidden_grad,
        grad_qkv[None],
        g_out[None],
        cross[None, :, :width],
        cross[None, :, width:],
        share_first[None],
        share_second[None],
        norm_shares[None, :3],
        norm_shares[None, 3:],
    )


def solution(mesh):
    _, dp_count, _ = mesh.devices.shape
    count = dp_count.bit_length() - 3
    names = axes_of(count)
    dp, tensor = names[1:-2], names[-2:]
    split = Mesh(mesh.devices.reshape((2,) * len(names)), names)
    rows = P("section", None, dp, tensor, None)
    in_specs = (
        rows,
        rows,
        P(None, None, dp, None),
        P("section", dp, None, tensor),
        P("section", dp, tensor),
        P("section", dp, tensor),
        P("section", dp, tensor),
        P("section", dp, tensor),
        P("section", tensor, dp),
        P("section", None, None),
        P("section", None, None),
    )
    out_specs = (
        rows,
        rows,
        P("section", dp, None, tensor),
        P("section", dp, tensor),
        P("section", dp, tensor),
        P("section", dp, tensor),
        P("section", dp, tensor),
        P("section", tensor, dp),
        P("section", None, dp + tensor),
        P("section", None, dp + tensor),
    )
    return jax.shard_map(
        functools.partial(body, count), mesh=split, in_specs=in_specs, out_specs=out_specs, check_vma=False
    )
```

```python
import functools

import jax
import jax.numpy as jnp
from jax import lax
from jax.experimental import pallas as pl
from jax.experimental.pallas import tpu as pltpu
from jax.sharding import Mesh
from jax.sharding import PartitionSpec as P

HDIM = 64
LANES = 128
MASKED = -1e30
NORM_EPS = 1e-05
VMEM_BYTES = 56 * 1024 * 1024

SEG_LANES = 8
PART_LANE = 12

PARTS = 2
HEADS = ((0, 1, 2, 0, 0), (0, 1, 2, 1, 1), (1, 3, 0, 0, 1))


def mul(a, b):
    return jnp.dot(a, b, preferred_element_type=jnp.float32)


def mul_nt(a, b):
    return lax.dot_general(a, b, (((1,), (1,)), ((), ())), preferred_element_type=jnp.float32)


def mul_tn(a, b):
    return lax.dot_general(a, b, (((0,), (0,)), ((), ())), preferred_element_type=jnp.float32)


def tile_of(values, index):
    return values[:, index * LANES : (index + 1) * LANES]


def lane_ids(rows):
    return lax.broadcasted_iota(jnp.int32, (rows, LANES), 1)


def half_mask(rows, half):
    lanes = lane_ids(rows)
    return lanes >= HDIM if half else lanes < HDIM


def in_parts(base, column):
    lanes = lane_ids(base.shape[0])
    high = column.astype(jnp.bfloat16).astype(jnp.float32)
    rest = column - high
    middle = rest.astype(jnp.bfloat16).astype(jnp.float32)
    low = rest - middle
    parts = jnp.where(
        lanes == PART_LANE,
        high,
        jnp.where(lanes == PART_LANE + 1, middle, jnp.where(lanes == PART_LANE + 2, low, base)),
    )
    return parts.astype(jnp.bfloat16)


def with_triangle(scores, tri, at):
    size = tri.shape[1]
    pieces = []
    if at > 0:
        pieces.append(scores[:, : at * size])
    pieces.append(scores[:, at * size : (at + 1) * size] + tri)
    pieces.append(scores[:, (at + 1) * size :])
    return jnp.concatenate(pieces, axis=1)


def places(core, block):
    return [pl.multiple_of((1 - core) * block, block), pl.multiple_of((2 + core) * block, block)]


def assemble(flag_ref, own_refs, peer_refs, w_ref):
    core, block = flag_ref[0], own_refs[0].shape[1] // 2
    for holder, refs in ((core, own_refs), (1 - core, peer_refs)):
        for part, ref in enumerate(refs):
            width = ref.shape[2]
            for at, place in enumerate(places(holder, block)):
                w_ref[pl.ds(place, block), part * width : (part + 1) * width] = ref[0, at * block : (at + 1) * block]


def hand_out(flag_ref, g_ref, keep_ref, send_ref):
    core, block = flag_ref[0], keep_ref.shape[1] // 2
    for holder, ref in ((core, keep_ref), (1 - core, send_ref)):
        for at, place in enumerate(places(holder, block)):
            ref[0, at * block : (at + 1) * block] = g_ref[pl.ds(place, block), :]


def where_active(kernel):
    def guarded(flag_ref, *refs):
        @pl.when(flag_ref[1] == 1)
        def _():
            kernel(flag_ref, *refs)

    return guarded


def scaled_queries(q_ref, at, q_tile, q_half):
    queries = q_ref[0, at, q_tile * LANES : (q_tile + 1) * LANES] * 0.125
    return jnp.where(half_mask(queries.shape[0], q_half), queries, 0).astype(jnp.bfloat16)


def units_of(total, rows):
    return [
        (slice(part * rows, (part + 1) * rows), part, head)
        for part in range(total // rows)
        for head in range(len(HEADS))
    ]


def attend_kernel(causal, flag_ref, xq_ref, xkv_ref, *refs):
    own_refs, peer_refs = refs[:1], refs[1:2]
    qx_ref, kx_ref, tri_ref, o_ref, q_ref, kv_ref, c_ref, l_ref, w_ref = refs[2:]
    block = pl.program_id(0)
    assemble(flag_ref, own_refs, peer_refs, w_ref)
    q_ref[0] = mul(xq_ref[...], w_ref[:, : 2 * LANES]).astype(jnp.bfloat16)
    kv_ref[0] = mul(xkv_ref[...], w_ref[:, LANES : 5 * LANES]).astype(jnp.bfloat16)
    rows = tri_ref.shape[0]
    low = half_mask(rows, 0)

    def scores_of(at, part, head):
        q_tile, k_tile, _, q_half, _ = HEADS[head]
        keys = kv_ref[0, :, k_tile * LANES : (k_tile + 1) * LANES]
        scores = mul_nt(
            jnp.concatenate([scaled_queries(q_ref, at, q_tile, q_half), qx_ref[at, :]], axis=1),
            jnp.concatenate([keys, kx_ref[...]], axis=1),
        )
        return with_triangle(scores, tri_ref[...], part) if causal else scores

    units = units_of(q_ref.shape[1], rows)
    ahead = scores_of(*units[0])
    contexts, totals = [], None
    for index, (at, part, head) in enumerate(units):
        scores = ahead
        if index + 1 < len(units):
            ahead = scores_of(*units[index + 1])
        v_tile = HEADS[head][2]
        values = kv_ref[0, :, v_tile * LANES : (v_tile + 1) * LANES]
        highest = jnp.max(scores, axis=1, keepdims=True)
        weights = jnp.exp(scores - highest)
        sums = jnp.sum(weights, axis=1, keepdims=True)
        contexts.append(mul(weights.astype(jnp.bfloat16), values) / sums)
        logs = jnp.broadcast_to(highest + jnp.log(sums), (rows, LANES))
        totals = logs if head == 0 else jnp.where(lane_ids(rows) == head, logs, totals)
        if head == len(HEADS) - 1:
            c_ref[0, at, :LANES] = jnp.where(low, 0, contexts[2]).astype(jnp.bfloat16)
            c_ref[0, at, LANES:] = jnp.where(low, contexts[0], contexts[1]).astype(jnp.bfloat16)
            l_ref[0, at, :] = totals
            contexts = []
    out = mul_nt(c_ref[0], w_ref[:, 4 * LANES :])

    @pl.when(block == 0)
    def _():
        o_ref[...] = out

    @pl.when(block > 0)
    def _():
        o_ref[...] += out


def attend_back_kernel(causal, flag_ref, do_ref, xq_ref, xkv_ref, *refs):
    own_refs, peer_refs = refs[:1], refs[1:2]
    q_ref, kv_ref, c_ref, l_ref, qx_ref, kx_ref, tri_ref, dxq_ref, dxkv_ref, *refs = refs[2:]
    keep_ref, send_ref, w_ref, sum_ref, dq_ref, dkv_ref, g_ref = refs
    rows = tri_ref.shape[0]
    assemble(flag_ref, own_refs, peer_refs, w_ref)
    d_context = mul(do_ref[...], w_ref[:, 4 * LANES :]).astype(jnp.bfloat16)
    low = half_mask(rows, 0)

    def products_of(at, part, head):
        q_tile, k_tile, v_tile, q_half, v_half = HEADS[head]
        c_tile = 0 if head == 2 else 1
        keys = kv_ref[0, :, k_tile * LANES : (k_tile + 1) * LANES]
        values = kv_ref[0, :, v_tile * LANES : (v_tile + 1) * LANES]
        queries = scaled_queries(q_ref, at, q_tile, q_half)
        d_rows = jnp.where(half_mask(rows, v_half), tile_of(d_context[at], c_tile), 0).astype(jnp.bfloat16)
        total = l_ref[0, at, head : head + 1]
        scores = mul_nt(
            jnp.concatenate([queries, in_parts(qx_ref[at, :].astype(jnp.float32), -total)], axis=1),
            jnp.concatenate([keys, kx_ref[...]], axis=1),
        )
        if causal:
            scores = with_triangle(scores, tri_ref[...], part)
        return scores, mul_nt(d_rows, values), queries, d_rows, keys

    units = units_of(q_ref.shape[1], rows)
    ahead = products_of(*units[0])
    d_queries = []
    for index, (at, part, head) in enumerate(units):
        scores, d_probs, queries, d_rows, keys = ahead
        if index + 1 < len(units):
            ahead = products_of(*units[index + 1])
        _, k_tile, v_tile, _, _ = HEADS[head]
        probs = jnp.exp(scores)
        inner = jnp.sum(probs * d_probs, axis=1, keepdims=True)
        d_scores = (probs * (d_probs - inner)).astype(jnp.bfloat16)
        d_values = mul_tn(probs.astype(jnp.bfloat16), d_rows)
        d_keys = mul_tn(d_scores, queries)
        d_queries.append(mul(d_scores, keys) * 0.125)
        k_at = slice(k_tile * LANES, (k_tile + 1) * LANES)
        v_at = slice(v_tile * LANES, (v_tile + 1) * LANES)
        if part == 0 and head != 1:
            sum_ref[:, k_at] = d_keys
            sum_ref[:, v_at] = d_values
        else:
            sum_ref[:, k_at] += d_keys
            sum_ref[:, v_at] += d_values
        if head == len(HEADS) - 1:
            dq_ref[at, :LANES] = jnp.where(low, d_queries[0], d_queries[1]).astype(jnp.bfloat16)
            dq_ref[at, LANES:] = jnp.where(low, d_queries[2], 0).astype(jnp.bfloat16)
            d_queries = []
    dkv_ref[...] = sum_ref[...].astype(jnp.bfloat16)
    d_xq = mul_nt(dq_ref[...], w_ref[:, : 2 * LANES])
    d_xkv = mul_nt(dkv_ref[...], w_ref[:, LANES : 5 * LANES])

    @pl.when(pl.program_id(0) == 0)
    def _():
        dxq_ref[...] = d_xq
        dxkv_ref[...] = d_xkv

    @pl.when(pl.program_id(0) > 0)
    def _():
        dxq_ref[...] += d_xq
        dxkv_ref[...] += d_xkv

    grad_q = mul_tn(xq_ref[...], dq_ref[...])
    grad_kv = mul_tn(xkv_ref[...], dkv_ref[...])
    grad_o = mul_tn(do_ref[...], c_ref[0])
    g_ref[:, :LANES] = grad_q[:, :LANES].astype(jnp.bfloat16)
    g_ref[:, LANES : 2 * LANES] = (grad_q[:, LANES:] + grad_kv[:, :LANES]).astype(jnp.bfloat16)
    g_ref[:, 2 * LANES : 4 * LANES] = grad_kv[:, LANES : 3 * LANES].astype(jnp.bfloat16)
    g_ref[:, 4 * LANES : 5 * LANES] = (grad_kv[:, 3 * LANES :] + grad_o[:, :LANES]).astype(jnp.bfloat16)
    g_ref[:, 5 * LANES :] = grad_o[:, LANES:].astype(jnp.bfloat16)
    hand_out(flag_ref, g_ref, keep_ref, send_ref)


def whole(shape):
    return pl.BlockSpec(shape, lambda j, flag: (0,) * len(shape))


def per_block(shape, first=0, gate=1):
    return pl.BlockSpec((1,) + shape, lambda j, flag: (first + j * flag[gate],) + (0,) * len(shape))


shape = jax.ShapeDtypeStruct


def call(kernel, name, micros, moved, grid, in_specs, out_specs, out_shape, scratch, *operands):
    return pl.pallas_call(
        where_active(kernel),
        grid_spec=pltpu.PrefetchScalarGridSpec(
            num_scalar_prefetch=1,
            grid=(grid,),
            in_specs=in_specs,
            out_specs=out_specs,
            scratch_shapes=scratch,
        ),
        out_shape=out_shape,
        compiler_params=pltpu.CompilerParams(vmem_limit_bytes=VMEM_BYTES),
        cost_estimate=cost(micros, moved),
        name=name,
    )(*operands)


def cost(micros, moved):
    return pl.CostEstimate(flops=int(micros * 1.15e9), bytes_accessed=int(moved), transcendentals=0)


def attend(flag, xq, xkv, weights, extras, causal):
    rows, width = xq.shape
    keys = xkv.shape[0]
    blocks = weights[0].shape[0]
    return call(
        functools.partial(attend_kernel, causal),
        "attend_self" if causal else "attend_cross",
        20,
        24 * 2**20,
        blocks,
        [whole((rows, width)), whole((keys, width))]
        + [per_block(part.shape[1:]) for part in weights]
        + [whole(extra.shape) for extra in extras],
        [
            whole((rows, width)),
            per_block((rows, 2 * LANES)),
            per_block((keys, 4 * LANES)),
            per_block((rows, 2 * LANES)),
            per_block((rows, LANES)),
        ],
        [
            shape((rows, width), jnp.float32),
            shape((blocks, rows, 2 * LANES), jnp.bfloat16),
            shape((blocks, keys, 4 * LANES), jnp.bfloat16),
            shape((blocks, rows, 2 * LANES), jnp.bfloat16),
            shape((blocks, rows, LANES), jnp.float32),
        ],
        [pltpu.VMEM((width, 6 * LANES), jnp.bfloat16)],
        flag,
        xq,
        xkv,
        *weights,
        *extras,
    )


def attend_back(flag, d_out, xq, xkv, weights, kept, extras, causal, first, count):
    rows, width = xq.shape
    keys = xkv.shape[0]
    return call(
        functools.partial(attend_back_kernel, causal),
        "attend_self_back" if causal else "attend_cross_back",
        10 * count,
        6 * 2**20 * count,
        count,
        [whole((rows, width)), whole((rows, width)), whole((keys, width))]
        + [per_block(part.shape[1:], first) for part in weights]
        + [
            per_block((rows, 2 * LANES), first),
            per_block((keys, 4 * LANES), first),
            per_block((rows, 2 * LANES), first),
            per_block((rows, LANES), first),
        ]
        + [whole(extra.shape) for extra in extras],
        [whole((rows, width)), whole((keys, width))] + [per_block(part.shape[1:]) for part in weights],
        [shape((rows, width), jnp.float32), shape((keys, width), jnp.float32)]
        + [shape((count,) + part.shape[1:], jnp.bfloat16) for part in weights],
        [
            pltpu.VMEM((width, 6 * LANES), jnp.bfloat16),
            pltpu.VMEM((keys, 4 * LANES), jnp.float32),
            pltpu.VMEM((rows, 2 * LANES), jnp.bfloat16),
            pltpu.VMEM((keys, 4 * LANES), jnp.bfloat16),
            pltpu.VMEM((width, 6 * LANES), jnp.bfloat16),
        ],
        flag,
        d_out,
        xq,
        xkv,
        *weights,
        *kept,
        *extras,
    )


def ffn_kernel(flag_ref, x_ref, *refs):
    own_refs, peer_refs = refs[:PARTS], refs[PARTS : 2 * PARTS]
    z_ref, g_ref, slope_ref, w_ref = refs[2 * PARTS :]
    block = pl.program_id(0)
    assemble(flag_ref, own_refs, peer_refs, w_ref)
    units = own_refs[0].shape[2]
    inner = mul(x_ref[...], w_ref[:, :units])
    spread = 0.5 * (1.0 + lax.erf(inner * (0.5**0.5)))
    bell = jnp.exp(-0.5 * inner * inner) * 0.3989422804014327
    active = (inner * spread).astype(jnp.bfloat16)
    g_ref[0] = active
    slope_ref[0] = (spread + inner * bell).astype(jnp.bfloat16)
    out = mul_nt(active, w_ref[:, units:])

    @pl.when(block == 0)
    def _():
        z_ref[...] = out

    @pl.when(block > 0)
    def _():
        z_ref[...] += out


def ffn(flag, x, weights):
    rows, width = x.shape
    blocks, _, units = weights[0].shape
    return call(
        ffn_kernel,
        "ffn",
        12,
        rows * units * blocks * 16,
        blocks,
        [whole((rows, width))] + [per_block(part.shape[1:]) for part in weights],
        [whole((rows, width)), per_block((rows, units)), per_block((rows, units))],
        [
            shape((rows, width), jnp.float32),
            shape((blocks, rows, units), jnp.bfloat16),
            shape((blocks, rows, units), jnp.bfloat16),
        ],
        [pltpu.VMEM((width, 2 * units), jnp.bfloat16)],
        flag,
        x,
        *weights,
    )


def ffn_back_kernel(flag_ref, dz_ref, *refs):
    own_refs, peer_refs = refs[:PARTS], refs[PARTS : 2 * PARTS]
    slope_ref, dx_ref, dh_ref, w_ref = refs[2 * PARTS :]
    block = pl.program_id(0)
    assemble(flag_ref, own_refs, peer_refs, w_ref)
    units = own_refs[0].shape[2]
    d_active = mul(dz_ref[...], w_ref[:, units:])
    d_inner = (d_active * slope_ref[0].astype(jnp.float32)).astype(jnp.bfloat16)
    dh_ref[0] = d_inner
    out = mul_nt(d_inner, w_ref[:, :units])

    @pl.when(block == 0)
    def _():
        dx_ref[...] = out

    @pl.when(block > 0)
    def _():
        dx_ref[...] += out


def ffn_back(flag, dz, weights, slope):
    rows, width = dz.shape
    blocks, _, units = weights[0].shape
    return call(
        ffn_back_kernel,
        "ffn_back",
        12,
        rows * units * blocks * 12,
        blocks,
        [whole((rows, width))] + [per_block(part.shape[1:]) for part in weights] + [per_block((rows, units))],
        [whole((rows, width)), per_block((rows, units))],
        [
            shape((rows, width), jnp.float32),
            shape((blocks, rows, units), jnp.bfloat16),
        ],
        [pltpu.VMEM((width, 2 * units), jnp.bfloat16)],
        flag,
        dz,
        *weights,
        slope,
    )


def ffn_grad_kernel(flag_ref, left_ref, enc_ref, dec_ref, keep_ref, send_ref, g_ref):
    right = jnp.where(flag_ref[2] == 1, enc_ref[0], dec_ref[0])
    g_ref[...] = mul_tn(left_ref[...], right).astype(jnp.bfloat16)
    hand_out(flag_ref, g_ref, keep_ref, send_ref)


def ffn_grad(flag, left, enc_right, dec_right, like):
    rows, width = left.shape
    blocks, _, units = enc_right.shape
    return call(
        ffn_grad_kernel,
        "ffn_grad",
        6,
        rows * units * blocks * 8,
        blocks,
        [whole((rows, width)), per_block((rows, units), 0, 2), per_block((rows, units), 0, 3)],
        [per_block(like.shape[1:])] * 2,
        [shape(like.shape, jnp.bfloat16)] * 2,
        [pltpu.VMEM((width, units), jnp.bfloat16)],
        flag,
        left,
        enc_right,
        dec_right,
    )


def layer_norm(values, gain_row, bias_row):
    average = jnp.mean(values, axis=-1, keepdims=True)
    centered = values - average
    variance = jnp.mean(centered * centered, axis=-1, keepdims=True)
    return centered * lax.rsqrt(variance + NORM_EPS) * gain_row + bias_row


def norm_back(values, gain_row, bias_row, upstream):
    _, pullback = jax.vjp(layer_norm, values, gain_row, bias_row)
    return pullback(upstream)


def low(values):
    return values.astype(jnp.bfloat16)


def axes_of(count):
    return ("section", "zh", "zl") + tuple("e%d" % at for at in range(count)) + ("ty", "tx")


def layer_of(place):
    return 1 ^ place["zh"] ^ place["zl"]


def moved(x, names, to):
    names = [name for name in axes_of(8) if name in names]

    def index(place):
        return sum(place[name] << (len(names) - 1 - at) for at, name in enumerate(names))

    pairs = []
    for source in range(2 ** len(names)):
        place = {name: source >> (len(names) - 1 - at) & 1 for at, name in enumerate(names)}
        target = to(place)
        if target is not None:
            pairs.append((source, index(target)))
    return lax.ppermute(x, tuple(names), pairs)


def over(x, *axes, layer=None):
    def to(place):
        if layer is not None and layer_of(place) != layer:
            return None
        return {**place, **{axis: 1 - place[axis] for axis in axes}}

    return moved(x, axes if layer is None else axes + Z, to)


Z = ("zh", "zl")


def swapped(x):
    def to(place):
        if place["section"] == layer_of(place):
            return place
        return {"section": 1 - place["section"], "zh": place["zh"], "zl": 1 - place["zl"]}

    return moved(x, ("section",) + Z, to)


def turned(x):
    return moved(x, ("section", "ty"), lambda place: {"section": place["ty"], "ty": place["section"]})


def sent_home(x, other):
    def to(place):
        return {
            "section": layer_of(place),
            "zh": place["zh"],
            "zl": 1 ^ place["zh"] ^ place["ty"],
            "ty": place["section"],
            "tx": place["tx"] ^ other,
        }

    return moved(x, ("section",) + Z + ("ty", "tx"), to)


def cross_in(x, layer):
    def to(place):
        if place["section"] != layer:
            return None
        return {"section": layer_of(place), "zh": place["zh"], "zl": place["zh"]}

    return moved(x, ("section",) + Z, to)


def cross_out(x, layer):
    def to(place):
        if layer_of(place) != 1:
            return None
        return {"section": layer, "zh": place["zh"], "zl": 1 ^ place["zh"] ^ place["section"]}

    return moved(x, ("section",) + Z, to)


def in_order(x, flag, axis):
    return jnp.where(flag == 1, jnp.flip(x, axis), x)


def pack_heads(query, key, value, out):
    pair = 2 * HDIM
    return jnp.concatenate(
        [
            query,
            value[:, pair:],
            key[:, :pair],
            value[:, :pair],
            key[:, pair:],
            out[:, pair:],
            out[:, :pair],
        ],
        axis=1,
    )


def unpack_heads(packed):
    part = [packed[:, at * HDIM : (at + 1) * HDIM] for at in range(12)]
    query = jnp.concatenate(part[0:3], axis=1)
    key = jnp.concatenate([part[4], part[5], part[8]], axis=1)
    value = jnp.concatenate([part[6], part[7], part[3]], axis=1)
    out = jnp.concatenate([part[10], part[11], part[9]], axis=1)
    return query, key, value, out


def after(x, *earlier):
    return lax.optimization_barrier((x,) + earlier)[0]


def plane_gathered(x, until=(), **only):
    parts = [x, over(x, "tx", **only), over(x, "ty", **only), over(x, "ty", "tx", **only)]
    return jnp.stack([after(part, *until) for part in parts])


def plane_summed(x, until=(), **only):
    terms = [x[0], over(x[1], "tx", **only), over(x[2], "ty", **only), over(x[3], "ty", "tx", **only)]
    terms = [after(term, *until) for term in terms]
    return low(sum(term.astype(jnp.float32) for term in terms))


def rows_gathered(x, count, until=(), **only):
    for axes in [("e%d" % at,) for at in reversed(range(count))] + [Z]:
        parts = [after(part, *until) for part in (x, over(x, *axes, **only))]
        both = in_order(jnp.stack(parts, axis=-3), lax.axis_index(axes[0]), x.ndim - 2)
        x = both.reshape(x.shape[:-2] + (2 * x.shape[-2], x.shape[-1]))
    return x


def rows_summed(x, count, until=(), **only):
    for axes in [Z] + [("e%d" % at,) for at in range(count)]:
        halves = x.reshape(x.shape[:-2] + (2, x.shape[-2] // 2, x.shape[-1]))
        halves = in_order(halves, lax.axis_index(axes[0]), x.ndim - 2)
        x = plus(halves[..., 0, :, :], after(over(halves[..., 1, :, :], *axes, **only), *until))
    return x


def plus(first, second):
    return low(first.astype(jnp.float32) + second.astype(jnp.float32))


def from_cores(keep, send, **only):
    return plus(keep, over(send, "section", **only))


def body(
    count,
    hidden,
    cotangent,
    segments,
    sa_qkv,
    sa_out,
    cross_one,
    cross_two,
    ffn_in,
    ffn_out,
    norm_gain,
    norm_bias,
):
    core = lax.axis_index("section")
    x_at, y_at, zh_at, zl_at = (lax.axis_index(name) for name in ("tx", "ty", "zh", "zl"))
    layer = 1 ^ zh_at ^ zl_at
    on_encoder = layer == 0
    quarter = hidden.shape[3]
    enc_flag = jnp.stack([core, 1 - layer, 1 - layer, layer])
    dec_flag = jnp.stack([core, layer, 1 - layer, layer])
    flag = jnp.stack([core, jnp.ones_like(core), 1 - layer, layer])

    def pick(first, second):
        return jnp.where(on_encoder, first, second)

    def of_one_row(x):
        both = in_order(x[0, :, 0], x_at, 0)
        return in_order(jnp.stack([both[0], over(both[1], "tx")]), x_at, 0).reshape(2 * quarter, -1)

    def rows_out(x, *until):
        mine, other = in_order(x.reshape(2, quarter, -1), x_at, 0)
        both = [after(sent_home(mine, 0), *until), after(sent_home(other, 1), *until)]
        return in_order(jnp.stack(both), x_at, 0)[None, :, None]

    units = ffn_in.shape[2]
    width = cross_one.shape[2]
    packed_self = pack_heads(sa_qkv[0, :, 0], sa_qkv[0, :, 1], sa_qkv[0, :, 2], sa_out[0])
    packed_ffn = jnp.concatenate([ffn_in[0], ffn_out[0].T], axis=1)
    with jax.named_scope("norms_in"):
        norms = swapped(jnp.concatenate([norm_gain[0], norm_bias[0]], axis=0))
        gains, biases = norms[:3], norms[3:]
        seg_own = segments[:, :, 0].astype(jnp.float32)
        seg_here = jnp.where(zl_at == 1 ^ zh_at ^ y_at, seg_own, over(seg_own, "zl")).astype(jnp.int32)
    with jax.named_scope("hidden_in"):
        one_row = of_one_row(hidden)
    with jax.named_scope("self_weights"):
        shard_self = swapped(packed_self)
    with jax.named_scope("hidden_in"):
        one_row = swapped(after(one_row, shard_self))
    with jax.named_scope("ffn_weights"):
        shard_ffn = swapped(after(packed_ffn, one_row))
        shard_first, shard_second = shard_ffn[:, :units], shard_ffn[:, units:]

    def both_rows(x):
        for_enc = rows_gathered(x, count, layer=0)
        return pick(for_enc, rows_gathered(after(x, for_enc), count, layer=1))

    with jax.named_scope("self_weights"):
        rows_self = both_rows(shard_self)
        own_self = plane_gathered(rows_self)
        w_self = [own_self, over(own_self, "section")]
    with jax.named_scope("hidden_in"):
        rows_here = turned(one_row)
        rows_all = jnp.concatenate([rows_here, over(rows_here, "section")], axis=0)
    with jax.named_scope("cross_weights"):
        cross_low = after(jnp.concatenate([cross_one[0], cross_two[0]], axis=1), own_self)
        pair_kv, pair_qo = cross_in(cross_low, 0), cross_in(cross_low, 1)
        packed = pack_heads(pair_qo[:, :width], pair_kv[:, :width], pair_kv[:, width:], pair_qo[:, width:])
    with jax.named_scope("ffn_weights"):
        rows_first = both_rows(after(shard_first, rows_self))
        plane_second = plane_gathered(after(shard_second, own_self))

    both_segments = in_order(seg_here, x_at, 1)[:, 0]
    ordered = in_order(both_segments.reshape(2, 2, 2 * quarter), core, 1).reshape(2, 4 * quarter)
    source_seg, target_seg = ordered[0], ordered[1]
    self_seg = pick(source_seg, target_seg)
    parts = jnp.arange(4)
    quarter_of = jnp.repeat(2 * ((parts // 2) ^ core) + parts % 2, quarter)
    lanes = jnp.arange(LANES)[None, :]

    def key_extras(seg):
        differs = jnp.logical_and(lanes < SEG_LANES, seg[:, None] != lanes)
        later = jnp.logical_and(
            jnp.logical_and(lanes >= SEG_LANES, lanes < PART_LANE),
            quarter_of[:, None] > lanes - SEG_LANES,
        )
        part = jnp.logical_and(lanes >= PART_LANE, lanes < PART_LANE + 3)
        return jnp.where(differs | later | part, 1.0, 0.0).astype(jnp.bfloat16)

    def query_extras(seg, causal):
        seg, at = seg[: 2 * quarter], quarter_of[: 2 * quarter]
        same = seg[:, None] == lanes
        here = jnp.logical_and(at[:, None] + SEG_LANES == lanes, causal)
        return jnp.where(same | here, MASKED, 0.0).astype(jnp.bfloat16)

    at_row = jnp.arange(quarter)
    later_key = jnp.logical_and(at_row[None, :] > at_row[:, None], jnp.logical_not(on_encoder))
    tri = jnp.where(later_key, MASKED, 0.0).astype(jnp.float32)
    self_extras = (query_extras(self_seg, jnp.logical_not(on_encoder)), key_extras(self_seg), tri)
    cross_extras = (query_extras(target_seg, False), key_extras(source_seg), tri)

    start = rows_all.astype(jnp.float32)
    start = pick(layer_norm(start, gains[0], biases[0]), start)
    start_here = start[: 2 * quarter]
    start_low = low(start)
    self_gain, self_bias = pick(gains[1], gains[0]), pick(biases[1], biases[0])
    self_out, *kept_self = attend(
        flag, start_low[: 2 * quarter], after(start_low, plane_second), w_self, self_extras, True
    )
    with jax.named_scope("ffn_weights"):
        own_first = plane_gathered(after(rows_first, plane_second), until=(self_out,))
        enc_second = rows_gathered(plane_second, count, until=(self_out,), layer=0)
        peer_first = over(own_first, "section")
        w_enc = [own_first, enc_second, peer_first, over(enc_second, "section", layer=0)]
    with jax.named_scope("cotangent_in"):
        cot_row = of_one_row(after(cotangent, self_out))
    self_total = start_here + self_out
    middle = layer_norm(self_total, self_gain, self_bias)
    middle_low = low(middle)

    with jax.named_scope("cross_weights"):
        rows_cross = rows_gathered(after(packed, plane_second), count, until=(self_out,), layer=1)
        own_cross = plane_gathered(rows_cross, layer=1)
        w_cross = [own_cross, over(own_cross, "section", layer=1)]

    enc_out, enc_active, enc_slope = ffn(enc_flag, middle_low, w_enc)
    enc_total = middle + enc_out
    encoded = low(layer_norm(enc_total, gains[2], biases[2]))
    with jax.named_scope("ffn_weights"):
        dec_second = rows_gathered(after(plane_second, self_out), count, until=(encoded,), layer=1)
        w_dec = [own_first, dec_second, peer_first, over(dec_second, "section", layer=1)]

    def across(x, layer):
        return moved(x, Z, lambda place: {**place, "zl": 1 - place["zl"]} if layer_of(place) == layer else None)

    with jax.named_scope("memory"):
        memory_here = across(encoded, 0)
        memory = jnp.concatenate([memory_here, over(memory_here, "section", layer=1)], axis=0)
    with jax.named_scope("cotangent_in"):
        cot = turned(swapped(after(cot_row, memory_here))).astype(jnp.float32)

    cross_out_rows, *kept_cross = attend(dec_flag, middle_low, memory, w_cross, cross_extras, False)
    cross_total = middle + cross_out_rows
    crossed = layer_norm(cross_total, gains[1], biases[1])
    crossed_low = low(crossed)
    dec_out, dec_active, dec_slope = ffn(dec_flag, crossed_low, w_dec)
    dec_total = crossed + dec_out
    decoded = low(layer_norm(dec_total, gains[2], biases[2]))

    d_dec_total, dec_gain_c, dec_bias_c = norm_back(dec_total, gains[2], biases[2], cot)
    d_dec_low = low(d_dec_total)
    d_after, dec_inner = ffn_back(dec_flag, d_dec_low, w_dec, dec_slope)
    d_cross_total, dec_gain_b, dec_bias_b = norm_back(
        cross_total, gains[1], biases[1], d_dec_total + d_after
    )
    d_middle_part, d_memory, cross_keep, cross_send = attend_back(
        dec_flag, low(d_cross_total), middle_low, memory, w_cross, kept_cross, cross_extras, False, 0, 4
    )
    with jax.named_scope("hidden_out"):
        hidden_out = rows_out(after(pick(encoded, decoded), d_after), d_middle_part)
    with jax.named_scope("d_memory"):
        d_memory = after(d_memory, hidden_out)
        d_memory_here = d_memory[: 2 * quarter] + over(
            low(d_memory[2 * quarter :]), "section", layer=1
        ).astype(jnp.float32)
        d_memory_low = low(d_memory_here)
        d_encoded = across(d_memory_low, 1).astype(jnp.float32) + cot
    with jax.named_scope("cross_sums"):
        cross_sum = from_cores(after(cross_keep, d_memory_low), after(cross_send, d_memory_low), layer=1)

    d_enc_total, enc_gain_c, enc_bias_c = norm_back(enc_total, gains[2], biases[2], d_encoded)
    d_enc_low = low(d_enc_total)
    second_keep, second_send = ffn_grad(
        flag, pick(d_enc_low, d_dec_low), enc_active, dec_active, own_first
    )
    with jax.named_scope("ffn_sums"):
        second_sum = from_cores(second_keep, second_send)
    with jax.named_scope("cross_sums"):
        cross_plane = plane_summed(cross_sum, until=(second_sum,), layer=1)
    d_enc_middle, enc_inner = ffn_back(enc_flag, after(d_enc_low, second_keep), w_enc, enc_slope)
    with jax.named_scope("ffn_sums"):
        second_plane = plane_summed(second_sum)
    first_keep, first_send = ffn_grad(
        flag, after(pick(middle_low, crossed_low), second_sum), enc_inner, dec_inner, own_first
    )
    with jax.named_scope("ffn_sums"):
        first_sum = from_cores(first_keep, first_send)

    d_middle = pick(d_enc_total + d_enc_middle, d_cross_total + d_middle_part)
    d_self_total, gain_s, bias_s = norm_back(self_total, self_gain, self_bias, d_middle)
    halves = []
    for first, earlier in ((0, (first_keep,)), (2, (first_sum, second_plane))):
        halves.append(
            attend_back(
                flag,
                after(low(d_self_total), *earlier),
                start_low[: 2 * quarter],
                start_low,
                w_self,
                kept_self,
                self_extras,
                True,
                first,
                2,
            )
        )
    d_start_q = halves[0][0] + halves[1][0]
    with jax.named_scope("cross_sums"):
        share_cross = rows_summed(after(cross_plane, d_start_q), count, layer=1)
    with jax.named_scope("ffn_sums"):
        first_plane = plane_summed(after(first_sum, second_plane), until=(halves[1][0],))
        second_share = rows_summed(second_plane, count, until=(halves[1][0],))
    with jax.named_scope("self_sums"):
        self_sum = jnp.concatenate([from_cores(keep, send) for _, _, keep, send in halves], axis=0)
    with jax.named_scope("d_start"):
        d_start_kv = after(halves[0][1], first_plane, second_share) + halves[1][1]
        d_start = d_self_total + d_start_q + d_start_kv[: 2 * quarter]
        d_start = d_start + over(low(d_start_kv[2 * quarter :]), "section").astype(jnp.float32)
    d_source, gain_a, bias_a = norm_back(
        rows_here.astype(jnp.float32), gains[0], biases[0], d_start
    )

    norm_sums = jnp.stack(
        [
            pick(gain_a, gain_s),
            pick(gain_s, dec_gain_b),
            pick(enc_gain_c, dec_gain_c),
            pick(bias_a, bias_s),
            pick(bias_s, dec_bias_b),
            pick(enc_bias_c, dec_bias_c),
        ]
    )
    shards = 2**count
    sides = jnp.arange(2)
    held, outer = core ^ sides[:, None], sides[None, :]
    row_block = ((2 * outer + (1 ^ outer ^ held)) * shards)[:, :, None] + jnp.arange(shards)
    column_block = (2 * (y_at ^ sides)[:, None] + (x_at ^ sides)[None, :]).reshape(-1)
    order = (row_block.reshape(2, -1)[:, None, :] + 0) * 4 + column_block[:, None]
    norm_sums = jnp.take(norm_sums.reshape(6, 8 * 2 * shards, -1), order.reshape(-1), axis=1)
    norm_sums = norm_sums.reshape(6, 2, 4, 2 * shards, -1)
    with jax.named_scope("norm_sums"):
        norm_sums = norm_sums[:, 0] + over(norm_sums[:, 1], "section")
    norm_rows = low(norm_sums.transpose(1, 2, 0, 3).reshape(4, 2 * shards, 1, -1))
    norm_width = norm_rows.shape[3]

    with jax.named_scope("self_sums"):
        pad = ((0, 0), (0, 0), (0, 15), (0, self_sum.shape[2] - norm_width))
        both = jnp.concatenate(
            [self_sum.reshape(4, 2 * shards, -1, self_sum.shape[2]), jnp.pad(norm_rows, pad)], axis=2
        )
        self_plane = plane_summed(both.reshape(4, -1, self_sum.shape[2]))
        share_self = swapped(rows_summed(self_plane, count)).astype(jnp.float32)
    norm_shares = share_self[-16, :norm_width].reshape(6, -1)
    share_self = share_self[:-16]
    with jax.named_scope("ffn_sums"):
        first_share = rows_summed(first_plane, count)
        share_ffn = swapped(jnp.concatenate([first_share, second_share], axis=1)).astype(jnp.float32)
    share_first, share_second = share_ffn[:, :units], share_ffn[:, units:].T
    with jax.named_scope("hidden_grad"):
        hidden_grad = rows_out(after(low(pick(d_source, d_start)), self_plane)).astype(jnp.float32)
    g_query, g_key, g_value, g_out = unpack_heads(share_self)
    grad_qkv = jnp.stack([g_query, g_key, g_value], axis=1)
    c_query, c_key, c_value, c_out = unpack_heads(share_cross)
    with jax.named_scope("cross_out"):
        for_enc = cross_out(jnp.concatenate([c_key, c_value], axis=1), 0)
        for_dec = cross_out(jnp.concatenate([c_query, c_out], axis=1), 1)
    cross = jnp.where(core == 0, for_enc, for_dec).astype(jnp.float32)

    return (
        hidden_out,
        hidden_grad,
        grad_qkv[None],
        g_out[None],
        cross[None, :, :width],
        cross[None, :, width:],
        share_first[None],
        share_second[None],
        norm_shares[None, :3],
        norm_shares[None, 3:],
    )


def solution(mesh):
    _, dp_count, _ = mesh.devices.shape
    count = dp_count.bit_length() - 3
    names = axes_of(count)
    dp, tensor = names[1:-2], names[-2:]
    split = Mesh(mesh.devices.reshape((2,) * len(names)), names)
    rows = P("section", None, dp, tensor, None)
    in_specs = (
        rows,
        rows,
        P(None, None, dp, None),
        P("section", dp, None, tensor),
        P("section", dp, tensor),
        P("section", dp, tensor),
        P("section", dp, tensor),
        P("section", dp, tensor),
        P("section", tensor, dp),
        P("section", None, None),
        P("section", None, None),
    )
    out_specs = (
        rows,
        rows,
        P("section", dp, None, tensor),
        P("section", dp, tensor),
        P("section", dp, tensor),
        P("section", dp, tensor),
        P("section", dp, tensor),
        P("section", tensor, dp),
        P("section", None, dp + tensor),
        P("section", None, dp + tensor),
    )
    return jax.shard_map(
        functools.partial(body, count), mesh=split, in_specs=in_specs, out_specs=out_specs, check_vma=False
    )
```

```python
import functools

import jax
import jax.numpy as jnp
from jax import lax
from jax.experimental import pallas as pl
from jax.experimental.pallas import tpu as pltpu
from jax.sharding import Mesh
from jax.sharding import PartitionSpec as P

HDIM = 64
LANES = 128
MASKED = -1e30
NORM_EPS = 1e-05
VMEM_BYTES = 56 * 1024 * 1024

SEG_LANES = 8
PART_LANE = 12

PARTS = 2
HEADS = ((0, 1, 2, 0, 0), (0, 1, 2, 1, 1), (1, 3, 0, 0, 1))


def mul(a, b):
    return jnp.dot(a, b, preferred_element_type=jnp.float32)


def mul_nt(a, b):
    return lax.dot_general(a, b, (((1,), (1,)), ((), ())), preferred_element_type=jnp.float32)


def mul_tn(a, b):
    return lax.dot_general(a, b, (((0,), (0,)), ((), ())), preferred_element_type=jnp.float32)


def tile_of(values, index):
    return values[:, index * LANES : (index + 1) * LANES]


def lane_ids(rows):
    return lax.broadcasted_iota(jnp.int32, (rows, LANES), 1)


def half_mask(rows, half):
    lanes = lane_ids(rows)
    return lanes >= HDIM if half else lanes < HDIM


def places(core, block):
    return [pl.multiple_of((1 - core) * block, block), pl.multiple_of((2 + core) * block, block)]


def assemble(flag_ref, own_refs, peer_refs, w_ref):
    core, block = flag_ref[0], own_refs[0].shape[1] // 2
    for holder, refs in ((core, own_refs), (1 - core, peer_refs)):
        for part, ref in enumerate(refs):
            width = ref.shape[2]
            for at, place in enumerate(places(holder, block)):
                w_ref[pl.ds(place, block), part * width : (part + 1) * width] = ref[0, at * block : (at + 1) * block]


def hand_out(flag_ref, g_ref, keep_ref, send_ref):
    core, block = flag_ref[0], keep_ref.shape[1] // 2
    for holder, ref in ((core, keep_ref), (1 - core, send_ref)):
        for at, place in enumerate(places(holder, block)):
            ref[0, at * block : (at + 1) * block] = g_ref[pl.ds(place, block), :]


def where_active(kernel):
    def guarded(flag_ref, *refs):
        @pl.when(flag_ref[1] == 1)
        def _():
            kernel(flag_ref, *refs)

    return guarded


CHUNK = 256


def in_chunks(total):
    return [slice(at, at + CHUNK) for at in range(0, total, CHUNK)]


def attend_kernel(causal, flag_ref, xq_ref, xkv_ref, *refs):
    own_refs, peer_refs = refs[:1], refs[1:2]
    qx_ref, kxt_ref, tri_ref, o_ref, q_ref, kv_ref, c_ref, l_ref, w_ref, kt_ref, s_ref = refs[2:]
    block = pl.program_id(0)
    assemble(flag_ref, own_refs, peer_refs, w_ref)
    rows, keys = xq_ref.shape[0], xkv_ref.shape[0]
    q_ref[0] = mul(xq_ref[...], w_ref[:, : 2 * LANES]).astype(jnp.bfloat16)
    kv_ref[0] = mul(xkv_ref[...], w_ref[:, LANES : 5 * LANES]).astype(jnp.bfloat16)
    kt_ref[:LANES] = kv_ref[0, :, LANES : 2 * LANES].T
    kt_ref[LANES:] = kv_ref[0, :, 3 * LANES :].T
    low = half_mask(rows, 0)
    chunks = in_chunks(keys)

    def queries_of(head):
        q_tile, _, _, q_half, _ = HEADS[head]
        queries = q_ref[0, :, q_tile * LANES : (q_tile + 1) * LANES] * 0.125
        queries = jnp.where(half_mask(rows, q_half), queries, 0).astype(jnp.bfloat16)
        return jnp.concatenate([queries, qx_ref[...]], axis=1)

    def scores_of(head, queries, index):
        at = chunks[index]
        first = LANES if head == 2 else 0
        scores = mul(queries, jnp.concatenate([kt_ref[first : first + LANES, at], kxt_ref[:, at]], axis=0))
        if causal and index * CHUNK < rows:
            parts = [scores[part] for part in in_chunks(rows)]
            parts[index] = parts[index] + tri_ref[...]
            scores = jnp.concatenate(parts, axis=0)
        s_ref[head % 2, :, at] = scores
        return jnp.maximum(scores[:, :LANES], scores[:, LANES:])

    queries = queries_of(0)
    tops = scores_of(0, queries, 0)
    for index in range(1, len(chunks)):
        tops = jnp.maximum(tops, scores_of(0, queries, index))
    contexts = []
    totals = jnp.zeros((rows, LANES), jnp.float32)
    for head in range(len(HEADS)):
        highest = jnp.max(tops, axis=1, keepdims=True)
        more = head + 1 < len(HEADS)
        if more:
            queries = queries_of(head + 1)
        v_tile = HEADS[head][2]
        sums, context, tops = 0.0, 0.0, None
        for index, at in enumerate(chunks):
            if more:
                top = scores_of(head + 1, queries, index)
                tops = top if tops is None else jnp.maximum(tops, top)
            weights = jnp.exp(s_ref[head % 2, :, at] - highest)
            sums = sums + (weights[:, :LANES] + weights[:, LANES:])
            context = context + mul(
                weights.astype(jnp.bfloat16), kv_ref[0, at, v_tile * LANES : (v_tile + 1) * LANES]
            )
        sums = jnp.sum(sums, axis=1, keepdims=True)
        contexts.append(context / sums)
        totals = jnp.where(lane_ids(rows) == head, highest + jnp.log(sums), totals)
    c_ref[0, :, :LANES] = jnp.where(low, 0, contexts[2])
    c_ref[0, :, LANES:] = jnp.where(low, contexts[0], contexts[1])
    l_ref[0] = totals
    out = mul_nt(c_ref[0].astype(jnp.bfloat16), w_ref[:, 4 * LANES :])

    @pl.when(block == 0)
    def _():
        o_ref[...] = out

    @pl.when(block > 0)
    def _():
        o_ref[...] += out


EXTRAS = 16


def with_extras(rows, base, constant):
    at = lax.broadcasted_iota(jnp.int32, base.shape, 0)
    high = constant.astype(jnp.bfloat16).astype(jnp.float32)
    rest = constant - high
    middle = rest.astype(jnp.bfloat16).astype(jnp.float32)
    extras = jnp.where(
        at == PART_LANE,
        high,
        jnp.where(at == PART_LANE + 1, middle, jnp.where(at == PART_LANE + 2, rest - middle, base)),
    )
    blank = jnp.zeros((LANES - EXTRAS, base.shape[1]), jnp.bfloat16)
    return jnp.concatenate([rows, extras.astype(jnp.bfloat16), blank], axis=0)


def attend_back_kernel(causal, flag_ref, do_ref, xq_ref, xkv_ref, *refs):
    own_refs, peer_refs = refs[:1], refs[1:2]
    q_ref, kv_ref, c_ref, l_ref, qxt_ref, kx_ref, tri_ref, dxq_ref, dxkv_ref, *refs = refs[2:]
    keep_ref, send_ref, w_ref, sum_ref, dq_ref, dkv_ref, g_ref, kt_ref, xqt_ref, xkvt_ref, dot_ref = refs
    rows, keys = xq_ref.shape[0], xkv_ref.shape[0]
    assemble(flag_ref, own_refs, peer_refs, w_ref)

    @pl.when(pl.program_id(0) == 0)
    def _():
        xqt_ref[...] = xq_ref[...].T
        xkvt_ref[...] = xkv_ref[...].T
        dot_ref[...] = do_ref[...].T

    d_context = mul(do_ref[...], w_ref[:, 4 * LANES :]).astype(jnp.bfloat16)
    d_context_t = d_context.T
    kt_ref[:LANES] = kv_ref[0, :, LANES : 2 * LANES].T
    kt_ref[LANES:] = kv_ref[0, :, 3 * LANES :].T
    queries_low = (q_ref[0] * 0.125).astype(jnp.bfloat16)
    queries_t = queries_low.T
    lanes = lane_ids(rows)
    constants = l_ref[0]
    for head, (_, _, _, _, v_half) in enumerate(HEADS):
        c_tile = 0 if head == 2 else 1
        product = tile_of(d_context, c_tile).astype(jnp.float32) * tile_of(c_ref[0], c_tile)
        product = jnp.where(half_mask(rows, v_half), product, 0)
        constants = jnp.where(lanes == 3 + head, jnp.sum(product, axis=1, keepdims=True), constants)
    constants_t = constants.T
    upper = lax.broadcasted_iota(jnp.int32, (LANES, rows), 0) < HDIM
    chunks = in_chunks(keys)

    def operands_of(head):
        q_tile, _, _, q_half, v_half = HEADS[head]
        c_tile = 0 if head == 2 else 1
        tile_q = slice(q_tile * LANES, (q_tile + 1) * LANES)
        tile_c = slice(c_tile * LANES, (c_tile + 1) * LANES)
        queries = jnp.where(half_mask(rows, q_half), queries_low[:, tile_q], 0).astype(jnp.bfloat16)
        d_rows = jnp.where(half_mask(rows, v_half), d_context[:, tile_c], 0).astype(jnp.bfloat16)
        for_scores = jnp.where(upper == (q_half == 0), queries_t[tile_q], 0).astype(jnp.bfloat16)
        for_probs = jnp.where(upper == (v_half == 0), d_context_t[tile_c], 0).astype(jnp.bfloat16)
        for_scores = with_extras(for_scores, qxt_ref[...].astype(jnp.float32), -constants_t[head : head + 1])
        for_probs = with_extras(
            for_probs, jnp.zeros((EXTRAS, rows), jnp.float32), -constants_t[3 + head : 4 + head]
        )
        return queries, d_rows, for_scores, for_probs

    def products_of(head, index, operands):
        _, k_tile, v_tile, _, _ = HEADS[head]
        at = chunks[index]
        scores = mul(
            jnp.concatenate([kv_ref[0, at, k_tile * LANES : (k_tile + 1) * LANES], kx_ref[at]], axis=1), operands[2]
        )
        if causal and index * CHUNK < rows:
            parts = [scores[:, part] for part in in_chunks(rows)]
            parts[index] = parts[index] + tri_ref[...]
            scores = jnp.concatenate(parts, axis=1)
        d_probs = mul(
            jnp.concatenate([kv_ref[0, at, v_tile * LANES : (v_tile + 1) * LANES], kx_ref[at]], axis=1), operands[3]
        )
        return scores, d_probs

    steps = [(head, index) for head in range(len(HEADS)) for index in range(len(chunks))]
    operands = operands_of(0)
    ahead = products_of(0, 0, operands)
    d_queries = []
    for step, (head, index) in enumerate(steps):
        scores, d_probs = ahead
        queries, d_rows = operands[:2]
        if step + 1 < len(steps):
            if steps[step + 1][0] != head:
                operands = operands_of(head + 1)
            ahead = products_of(*steps[step + 1], operands)
        _, k_tile, v_tile, _, _ = HEADS[head]
        at = chunks[index]
        probs = jnp.exp(scores)
        d_scores = (probs * d_probs).astype(jnp.bfloat16)
        d_values = mul(probs.astype(jnp.bfloat16), d_rows)
        d_keys = mul(d_scores, queries)
        first = LANES if head == 2 else 0
        d_query = mul(kt_ref[first : first + LANES, at], d_scores)
        if index == 0:
            d_queries.append(d_query)
        else:
            d_queries[-1] = d_queries[-1] + d_query
        k_at = slice(k_tile * LANES, (k_tile + 1) * LANES)
        v_at = slice(v_tile * LANES, (v_tile + 1) * LANES)
        if head != 1:
            sum_ref[at, k_at] = d_keys
            sum_ref[at, v_at] = d_values
        else:
            sum_ref[at, k_at] += d_keys
            sum_ref[at, v_at] += d_values
    pair = (jnp.where(upper, d_queries[0], d_queries[1]) * 0.125).astype(jnp.bfloat16)
    single = (jnp.where(upper, d_queries[2], 0) * 0.125).astype(jnp.bfloat16)
    dq_ref[:, :LANES] = pair.T
    dq_ref[:, LANES:] = single.T
    dkv_ref[...] = sum_ref[...].astype(jnp.bfloat16)
    d_xq = mul_nt(dq_ref[...], w_ref[:, : 2 * LANES])
    d_xkv = mul_nt(dkv_ref[...], w_ref[:, LANES : 5 * LANES])

    @pl.when(pl.program_id(0) == 0)
    def _():
        dxq_ref[...] = d_xq
        dxkv_ref[...] = d_xkv

    @pl.when(pl.program_id(0) > 0)
    def _():
        dxq_ref[...] += d_xq
        dxkv_ref[...] += d_xkv

    grad_q = mul(xqt_ref[...], dq_ref[...])
    grad_kv = mul(xkvt_ref[...], dkv_ref[...])
    grad_o = mul(dot_ref[...], c_ref[0].astype(jnp.bfloat16))
    g_ref[:, :LANES] = grad_q[:, :LANES].astype(jnp.bfloat16)
    g_ref[:, LANES : 2 * LANES] = (grad_q[:, LANES:] + grad_kv[:, :LANES]).astype(jnp.bfloat16)
    g_ref[:, 2 * LANES : 4 * LANES] = grad_kv[:, LANES : 3 * LANES].astype(jnp.bfloat16)
    g_ref[:, 4 * LANES : 5 * LANES] = (grad_kv[:, 3 * LANES :] + grad_o[:, :LANES]).astype(jnp.bfloat16)
    g_ref[:, 5 * LANES :] = grad_o[:, LANES:].astype(jnp.bfloat16)
    hand_out(flag_ref, g_ref, keep_ref, send_ref)


def whole(shape):
    return pl.BlockSpec(shape, lambda j, flag: (0,) * len(shape))


def per_block(shape, first=0, gate=1):
    return pl.BlockSpec((1,) + shape, lambda j, flag: (first + j * flag[gate],) + (0,) * len(shape))


shape = jax.ShapeDtypeStruct


def call(kernel, name, micros, moved, grid, in_specs, out_specs, out_shape, scratch, *operands):
    return pl.pallas_call(
        where_active(kernel),
        grid_spec=pltpu.PrefetchScalarGridSpec(
            num_scalar_prefetch=1,
            grid=(grid,),
            in_specs=in_specs,
            out_specs=out_specs,
            scratch_shapes=scratch,
        ),
        out_shape=out_shape,
        compiler_params=pltpu.CompilerParams(vmem_limit_bytes=VMEM_BYTES),
        cost_estimate=cost(micros, moved),
        name=name,
    )(*operands)


def cost(micros, moved):
    return pl.CostEstimate(flops=int(micros * 1.15e9), bytes_accessed=int(moved), transcendentals=0)


def attend(flag, xq, xkv, weights, extras, causal):
    rows, width = xq.shape
    keys = xkv.shape[0]
    blocks = weights[0].shape[0]
    return call(
        functools.partial(attend_kernel, causal),
        "attend_self" if causal else "attend_cross",
        20,
        24 * 2**20,
        blocks,
        [whole((rows, width)), whole((keys, width))]
        + [per_block(part.shape[1:]) for part in weights]
        + [whole(extra.shape) for extra in extras],
        [
            whole((rows, width)),
            per_block((rows, 2 * LANES)),
            per_block((keys, 4 * LANES)),
            per_block((rows, 2 * LANES)),
            per_block((rows, LANES)),
        ],
        [
            shape((rows, width), jnp.float32),
            shape((blocks, rows, 2 * LANES), jnp.bfloat16),
            shape((blocks, keys, 4 * LANES), jnp.bfloat16),
            shape((blocks, rows, 2 * LANES), jnp.float32),
            shape((blocks, rows, LANES), jnp.float32),
        ],
        [
            pltpu.VMEM((width, 6 * LANES), jnp.bfloat16),
            pltpu.VMEM((2 * LANES, keys), jnp.bfloat16),
            pltpu.VMEM((2, rows, keys), jnp.float32),
        ],
        flag,
        xq,
        xkv,
        *weights,
        *extras,
    )


def attend_back(flag, d_out, xq, xkv, weights, kept, extras, causal, first, count):
    rows, width = xq.shape
    keys = xkv.shape[0]
    return call(
        functools.partial(attend_back_kernel, causal),
        "attend_self_back" if causal else "attend_cross_back",
        10 * count,
        6 * 2**20 * count,
        count,
        [whole((rows, width)), whole((rows, width)), whole((keys, width))]
        + [per_block(part.shape[1:], first) for part in weights]
        + [
            per_block((rows, 2 * LANES), first),
            per_block((keys, 4 * LANES), first),
            per_block((rows, 2 * LANES), first),
            per_block((rows, LANES), first),
        ]
        + [whole(extra.shape) for extra in extras],
        [whole((rows, width)), whole((keys, width))] + [per_block(part.shape[1:]) for part in weights],
        [shape((rows, width), jnp.float32), shape((keys, width), jnp.float32)]
        + [shape((count,) + part.shape[1:], jnp.bfloat16) for part in weights],
        [
            pltpu.VMEM((width, 6 * LANES), jnp.bfloat16),
            pltpu.VMEM((keys, 4 * LANES), jnp.float32),
            pltpu.VMEM((rows, 2 * LANES), jnp.bfloat16),
            pltpu.VMEM((keys, 4 * LANES), jnp.bfloat16),
            pltpu.VMEM((width, 6 * LANES), jnp.bfloat16),
            pltpu.VMEM((2 * LANES, keys), jnp.bfloat16),
            pltpu.VMEM((width, rows), jnp.bfloat16),
            pltpu.VMEM((width, keys), jnp.bfloat16),
            pltpu.VMEM((width, rows), jnp.bfloat16),
        ],
        flag,
        d_out,
        xq,
        xkv,
        *weights,
        *kept,
        *extras,
    )


def ffn_kernel(flag_ref, x_ref, *refs):
    own_refs, peer_refs = refs[:PARTS], refs[PARTS : 2 * PARTS]
    z_ref, g_ref, slope_ref, w_ref = refs[2 * PARTS :]
    block = pl.program_id(0)
    assemble(flag_ref, own_refs, peer_refs, w_ref)
    units = own_refs[0].shape[2]
    inner = mul(x_ref[...], w_ref[:, :units])
    spread = 0.5 * (1.0 + lax.erf(inner * (0.5**0.5)))
    bell = jnp.exp(-0.5 * inner * inner) * 0.3989422804014327
    active = (inner * spread).astype(jnp.bfloat16)
    g_ref[0] = active
    slope_ref[0] = (spread + inner * bell).astype(jnp.bfloat16)
    out = mul_nt(active, w_ref[:, units:])

    @pl.when(block == 0)
    def _():
        z_ref[...] = out

    @pl.when(block > 0)
    def _():
        z_ref[...] += out


def ffn(flag, x, weights):
    rows, width = x.shape
    blocks, _, units = weights[0].shape
    return call(
        ffn_kernel,
        "ffn",
        12,
        rows * units * blocks * 16,
        blocks,
        [whole((rows, width))] + [per_block(part.shape[1:]) for part in weights],
        [whole((rows, width)), per_block((rows, units)), per_block((rows, units))],
        [
            shape((rows, width), jnp.float32),
            shape((blocks, rows, units), jnp.bfloat16),
            shape((blocks, rows, units), jnp.bfloat16),
        ],
        [pltpu.VMEM((width, 2 * units), jnp.bfloat16)],
        flag,
        x,
        *weights,
    )


def ffn_back_kernel(flag_ref, dz_ref, *refs):
    own_refs, peer_refs = refs[:PARTS], refs[PARTS : 2 * PARTS]
    slope_ref, dx_ref, dh_ref, w_ref = refs[2 * PARTS :]
    block = pl.program_id(0)
    assemble(flag_ref, own_refs, peer_refs, w_ref)
    units = own_refs[0].shape[2]
    d_active = mul(dz_ref[...], w_ref[:, units:])
    d_inner = (d_active * slope_ref[0].astype(jnp.float32)).astype(jnp.bfloat16)
    dh_ref[0] = d_inner
    out = mul_nt(d_inner, w_ref[:, :units])

    @pl.when(block == 0)
    def _():
        dx_ref[...] = out

    @pl.when(block > 0)
    def _():
        dx_ref[...] += out


def ffn_back(flag, dz, weights, slope):
    rows, width = dz.shape
    blocks, _, units = weights[0].shape
    return call(
        ffn_back_kernel,
        "ffn_back",
        12,
        rows * units * blocks * 12,
        blocks,
        [whole((rows, width))] + [per_block(part.shape[1:]) for part in weights] + [per_block((rows, units))],
        [whole((rows, width)), per_block((rows, units))],
        [
            shape((rows, width), jnp.float32),
            shape((blocks, rows, units), jnp.bfloat16),
        ],
        [pltpu.VMEM((width, 2 * units), jnp.bfloat16)],
        flag,
        dz,
        *weights,
        slope,
    )


def ffn_grad_kernel(flag_ref, left_ref, enc_ref, dec_ref, keep_ref, send_ref, g_ref, left_t_ref):
    @pl.when(pl.program_id(0) == 0)
    def _():
        left_t_ref[...] = left_ref[...].T

    right = jnp.where(flag_ref[2] == 1, enc_ref[0], dec_ref[0])
    g_ref[...] = mul(left_t_ref[...], right).astype(jnp.bfloat16)
    hand_out(flag_ref, g_ref, keep_ref, send_ref)


def ffn_grad(flag, left, enc_right, dec_right, like):
    rows, width = left.shape
    blocks, _, units = enc_right.shape
    return call(
        ffn_grad_kernel,
        "ffn_grad",
        6,
        rows * units * blocks * 8,
        blocks,
        [whole((rows, width)), per_block((rows, units), 0, 2), per_block((rows, units), 0, 3)],
        [per_block(like.shape[1:])] * 2,
        [shape(like.shape, jnp.bfloat16)] * 2,
        [pltpu.VMEM((width, units), jnp.bfloat16), pltpu.VMEM((width, rows), jnp.bfloat16)],
        flag,
        left,
        enc_right,
        dec_right,
    )


def layer_norm(values, gain_row, bias_row):
    average = jnp.mean(values, axis=-1, keepdims=True)
    centered = values - average
    variance = jnp.mean(centered * centered, axis=-1, keepdims=True)
    return centered * lax.rsqrt(variance + NORM_EPS) * gain_row + bias_row


def norm_back(values, gain_row, bias_row, upstream):
    _, pullback = jax.vjp(layer_norm, values, gain_row, bias_row)
    return pullback(upstream)


def low(values):
    return values.astype(jnp.bfloat16)


def axes_of(count):
    return ("section", "zh", "zl") + tuple("e%d" % at for at in range(count)) + ("ty", "tx")


def layer_of(place):
    return 1 ^ place["zh"] ^ place["zl"]


def moved(x, names, to):
    names = [name for name in axes_of(8) if name in names]

    def index(place):
        return sum(place[name] << (len(names) - 1 - at) for at, name in enumerate(names))

    pairs = []
    for source in range(2 ** len(names)):
        place = {name: source >> (len(names) - 1 - at) & 1 for at, name in enumerate(names)}
        target = to(place)
        if target is not None:
            pairs.append((source, index(target)))
    return lax.ppermute(x, tuple(names), pairs)


def over(x, *axes, layer=None):
    def to(place):
        if layer is not None and layer_of(place) != layer:
            return None
        return {**place, **{axis: 1 - place[axis] for axis in axes}}

    return moved(x, axes if layer is None else axes + Z, to)


Z = ("zh", "zl")


def swapped(x):
    def to(place):
        if place["section"] == layer_of(place):
            return place
        return {"section": 1 - place["section"], "zh": place["zh"], "zl": 1 - place["zl"]}

    return moved(x, ("section",) + Z, to)


def turned(x):
    return moved(x, ("section", "ty"), lambda place: {"section": place["ty"], "ty": place["section"]})


def sent_home(x, other):
    def to(place):
        return {
            "section": layer_of(place),
            "zh": place["zh"],
            "zl": 1 ^ place["zh"] ^ place["ty"],
            "ty": place["section"],
            "tx": place["tx"] ^ other,
        }

    return moved(x, ("section",) + Z + ("ty", "tx"), to)


def cross_in(x, layer):
    def to(place):
        if place["section"] != layer:
            return None
        return {"section": layer_of(place), "zh": place["zh"], "zl": place["zh"]}

    return moved(x, ("section",) + Z, to)


def cross_out(x, layer):
    def to(place):
        if layer_of(place) != 1:
            return None
        return {"section": layer, "zh": place["zh"], "zl": 1 ^ place["zh"] ^ place["section"]}

    return moved(x, ("section",) + Z, to)


def in_order(x, flag, axis):
    return jnp.where(flag == 1, jnp.flip(x, axis), x)


def pack_heads(query, key, value, out):
    pair = 2 * HDIM
    return jnp.concatenate(
        [
            query,
            value[:, pair:],
            key[:, :pair],
            value[:, :pair],
            key[:, pair:],
            out[:, pair:],
            out[:, :pair],
        ],
        axis=1,
    )


def unpack_heads(packed):
    part = [packed[:, at * HDIM : (at + 1) * HDIM] for at in range(12)]
    query = jnp.concatenate(part[0:3], axis=1)
    key = jnp.concatenate([part[4], part[5], part[8]], axis=1)
    value = jnp.concatenate([part[6], part[7], part[3]], axis=1)
    out = jnp.concatenate([part[10], part[11], part[9]], axis=1)
    return query, key, value, out


def after(x, *earlier):
    return lax.optimization_barrier((x,) + earlier)[0]


def plane_gathered(x, until=(), **only):
    parts = [x, over(x, "tx", **only), over(x, "ty", **only), over(x, "ty", "tx", **only)]
    return jnp.stack([after(part, *until) for part in parts])


def plane_summed(x, until=(), **only):
    terms = [x[0], over(x[1], "tx", **only), over(x[2], "ty", **only), over(x[3], "ty", "tx", **only)]
    terms = [after(term, *until) for term in terms]
    return low(sum(term.astype(jnp.float32) for term in terms))


def rows_gathered(x, count, until=(), **only):
    for axes in [("e%d" % at,) for at in reversed(range(count))] + [Z]:
        parts = [after(part, *until) for part in (x, over(x, *axes, **only))]
        both = in_order(jnp.stack(parts, axis=-3), lax.axis_index(axes[0]), x.ndim - 2)
        x = both.reshape(x.shape[:-2] + (2 * x.shape[-2], x.shape[-1]))
    return x


def rows_summed(x, count, until=(), **only):
    for axes in [Z] + [("e%d" % at,) for at in range(count)]:
        halves = x.reshape(x.shape[:-2] + (2, x.shape[-2] // 2, x.shape[-1]))
        halves = in_order(halves, lax.axis_index(axes[0]), x.ndim - 2)
        x = plus(halves[..., 0, :, :], after(over(halves[..., 1, :, :], *axes, **only), *until))
    return x


def plus(first, second):
    return low(first.astype(jnp.float32) + second.astype(jnp.float32))


def from_cores(keep, send, **only):
    return plus(keep, over(send, "section", **only))


def body(
    count,
    hidden,
    cotangent,
    segments,
    sa_qkv,
    sa_out,
    cross_one,
    cross_two,
    ffn_in,
    ffn_out,
    norm_gain,
    norm_bias,
):
    core = lax.axis_index("section")
    x_at, y_at, zh_at, zl_at = (lax.axis_index(name) for name in ("tx", "ty", "zh", "zl"))
    layer = 1 ^ zh_at ^ zl_at
    on_encoder = layer == 0
    quarter = hidden.shape[3]
    enc_flag = jnp.stack([core, 1 - layer, 1 - layer, layer])
    dec_flag = jnp.stack([core, layer, 1 - layer, layer])
    flag = jnp.stack([core, jnp.ones_like(core), 1 - layer, layer])

    def pick(first, second):
        return jnp.where(on_encoder, first, second)

    def of_one_row(x):
        both = in_order(x[0, :, 0], x_at, 0)
        return in_order(jnp.stack([both[0], over(both[1], "tx")]), x_at, 0).reshape(2 * quarter, -1)

    def rows_out(x, *until):
        mine, other = in_order(x.reshape(2, quarter, -1), x_at, 0)
        both = [after(sent_home(mine, 0), *until), after(sent_home(other, 1), *until)]
        return in_order(jnp.stack(both), x_at, 0)[None, :, None]

    units = ffn_in.shape[2]
    width = cross_one.shape[2]
    packed_self = pack_heads(sa_qkv[0, :, 0], sa_qkv[0, :, 1], sa_qkv[0, :, 2], sa_out[0])
    packed_ffn = jnp.concatenate([ffn_in[0], ffn_out[0].T], axis=1)
    with jax.named_scope("norms_in"):
        norms = swapped(jnp.concatenate([norm_gain[0], norm_bias[0]], axis=0))
        gains, biases = norms[:3], norms[3:]
        seg_own = segments[:, :, 0].astype(jnp.float32)
        seg_here = jnp.where(zl_at == 1 ^ zh_at ^ y_at, seg_own, over(seg_own, "zl")).astype(jnp.int32)
    with jax.named_scope("hidden_in"):
        one_row = of_one_row(hidden)
    with jax.named_scope("self_weights"):
        shard_self = swapped(packed_self)
    with jax.named_scope("hidden_in"):
        one_row = swapped(after(one_row, shard_self))
    with jax.named_scope("ffn_weights"):
        shard_ffn = swapped(after(packed_ffn, one_row))
        shard_first, shard_second = shard_ffn[:, :units], shard_ffn[:, units:]

    def both_rows(x):
        for_enc = rows_gathered(x, count, layer=0)
        return pick(for_enc, rows_gathered(after(x, for_enc), count, layer=1))

    with jax.named_scope("self_weights"):
        rows_self = both_rows(shard_self)
        own_self = plane_gathered(rows_self)
        w_self = [own_self, over(own_self, "section")]
    with jax.named_scope("hidden_in"):
        rows_here = turned(one_row)
        rows_all = jnp.concatenate([rows_here, over(rows_here, "section")], axis=0)
    with jax.named_scope("cross_weights"):
        cross_low = after(jnp.concatenate([cross_one[0], cross_two[0]], axis=1), own_self)
        pair_kv, pair_qo = cross_in(cross_low, 0), cross_in(cross_low, 1)
        packed = pack_heads(pair_qo[:, :width], pair_kv[:, :width], pair_kv[:, width:], pair_qo[:, width:])
    with jax.named_scope("ffn_weights"):
        rows_first = both_rows(after(shard_first, rows_self))
        plane_second = plane_gathered(after(shard_second, own_self))

    both_segments = in_order(seg_here, x_at, 1)[:, 0]
    ordered = in_order(both_segments.reshape(2, 2, 2 * quarter), core, 1).reshape(2, 4 * quarter)
    source_seg, target_seg = ordered[0], ordered[1]
    self_seg = pick(source_seg, target_seg)
    parts = jnp.arange(4)
    quarter_of = jnp.repeat(2 * ((parts // 2) ^ core) + parts % 2, quarter)
    lanes = jnp.arange(LANES)[None, :]

    def key_extras(seg):
        differs = jnp.logical_and(lanes < SEG_LANES, seg[:, None] != lanes)
        later = jnp.logical_and(
            jnp.logical_and(lanes >= SEG_LANES, lanes < PART_LANE),
            quarter_of[:, None] > lanes - SEG_LANES,
        )
        part = jnp.logical_and(lanes >= PART_LANE, lanes < PART_LANE + 3)
        return jnp.where(differs | later | part, 1.0, 0.0).astype(jnp.bfloat16)

    def query_extras(seg, causal):
        seg, at = seg[: 2 * quarter], quarter_of[: 2 * quarter]
        same = seg[:, None] == lanes
        here = jnp.logical_and(at[:, None] + SEG_LANES == lanes, causal)
        return jnp.where(same | here, MASKED, 0.0).astype(jnp.bfloat16)

    at_row = jnp.arange(quarter)
    later_key = jnp.logical_and(at_row[None, :] > at_row[:, None], jnp.logical_not(on_encoder))
    tri = jnp.where(later_key, MASKED, 0.0).astype(jnp.float32)
    no_rows = jnp.logical_not(on_encoder)
    self_query, self_key = query_extras(self_seg, no_rows), key_extras(self_seg)
    cross_query, cross_key = query_extras(target_seg, False), key_extras(source_seg)
    self_extras, cross_extras = (self_query, self_key.T, tri), (cross_query, cross_key.T, tri)
    self_back = (self_query.T[:EXTRAS], self_key, tri.T)
    cross_back = (cross_query.T[:EXTRAS], cross_key, tri.T)

    start = rows_all.astype(jnp.float32)
    start = pick(layer_norm(start, gains[0], biases[0]), start)
    start_here = start[: 2 * quarter]
    start_low = low(start)
    self_gain, self_bias = pick(gains[1], gains[0]), pick(biases[1], biases[0])
    self_out, *kept_self = attend(
        flag, start_low[: 2 * quarter], after(start_low, plane_second), w_self, self_extras, True
    )
    with jax.named_scope("ffn_weights"):
        own_first = plane_gathered(after(rows_first, plane_second), until=(self_out,))
        enc_second = rows_gathered(plane_second, count, until=(self_out,), layer=0)
        peer_first = over(own_first, "section")
        w_enc = [own_first, enc_second, peer_first, over(enc_second, "section", layer=0)]
    with jax.named_scope("cotangent_in"):
        cot_row = of_one_row(after(cotangent, self_out))
    self_total = start_here + self_out
    middle = layer_norm(self_total, self_gain, self_bias)
    middle_low = low(middle)

    with jax.named_scope("cross_weights"):
        rows_cross = rows_gathered(after(packed, plane_second), count, until=(self_out,), layer=1)
        own_cross = plane_gathered(rows_cross, layer=1)
        w_cross = [own_cross, over(own_cross, "section", layer=1)]

    enc_out, enc_active, enc_slope = ffn(enc_flag, middle_low, w_enc)
    enc_total = middle + enc_out
    encoded = low(layer_norm(enc_total, gains[2], biases[2]))
    with jax.named_scope("ffn_weights"):
        dec_second = rows_gathered(after(plane_second, self_out), count, until=(encoded,), layer=1)
        w_dec = [own_first, dec_second, peer_first, over(dec_second, "section", layer=1)]

    def across(x, layer):
        return moved(x, Z, lambda place: {**place, "zl": 1 - place["zl"]} if layer_of(place) == layer else None)

    with jax.named_scope("memory"):
        memory_here = across(encoded, 0)
        memory = jnp.concatenate([memory_here, over(memory_here, "section", layer=1)], axis=0)
    with jax.named_scope("cotangent_in"):
        cot = turned(swapped(after(cot_row, memory_here))).astype(jnp.float32)

    cross_out_rows, *kept_cross = attend(dec_flag, middle_low, memory, w_cross, cross_extras, False)
    cross_total = middle + cross_out_rows
    crossed = layer_norm(cross_total, gains[1], biases[1])
    crossed_low = low(crossed)
    dec_out, dec_active, dec_slope = ffn(dec_flag, crossed_low, w_dec)
    dec_total = crossed + dec_out
    decoded = low(layer_norm(dec_total, gains[2], biases[2]))

    d_dec_total, dec_gain_c, dec_bias_c = norm_back(dec_total, gains[2], biases[2], cot)
    d_dec_low = low(d_dec_total)
    d_after, dec_inner = ffn_back(dec_flag, d_dec_low, w_dec, dec_slope)
    d_cross_total, dec_gain_b, dec_bias_b = norm_back(
        cross_total, gains[1], biases[1], d_dec_total + d_after
    )
    d_middle_part, d_memory, cross_keep, cross_send = attend_back(
        dec_flag, low(d_cross_total), middle_low, memory, w_cross, kept_cross, cross_back, False, 0, 4
    )
    with jax.named_scope("hidden_out"):
        hidden_out = rows_out(after(pick(encoded, decoded), d_after), d_middle_part)
    with jax.named_scope("d_memory"):
        d_memory = after(d_memory, hidden_out)
        d_memory_here = d_memory[: 2 * quarter] + over(
            low(d_memory[2 * quarter :]), "section", layer=1
        ).astype(jnp.float32)
        d_memory_low = low(d_memory_here)
        d_encoded = across(d_memory_low, 1).astype(jnp.float32) + cot
    with jax.named_scope("cross_sums"):
        cross_sum = from_cores(after(cross_keep, d_memory_low), after(cross_send, d_memory_low), layer=1)

    d_enc_total, enc_gain_c, enc_bias_c = norm_back(enc_total, gains[2], biases[2], d_encoded)
    d_enc_low = low(d_enc_total)
    second_keep, second_send = ffn_grad(
        flag, pick(d_enc_low, d_dec_low), enc_active, dec_active, own_first
    )
    with jax.named_scope("ffn_sums"):
        second_sum = from_cores(second_keep, second_send)
    with jax.named_scope("cross_sums"):
        cross_plane = plane_summed(cross_sum, until=(second_sum,), layer=1)
    d_enc_middle, enc_inner = ffn_back(enc_flag, after(d_enc_low, second_keep), w_enc, enc_slope)
    with jax.named_scope("ffn_sums"):
        second_plane = plane_summed(second_sum)
    first_keep, first_send = ffn_grad(
        flag, after(pick(middle_low, crossed_low), second_sum), enc_inner, dec_inner, own_first
    )
    with jax.named_scope("ffn_sums"):
        first_sum = from_cores(first_keep, first_send)

    d_middle = pick(d_enc_total + d_enc_middle, d_cross_total + d_middle_part)
    d_self_total, gain_s, bias_s = norm_back(self_total, self_gain, self_bias, d_middle)
    halves = []
    for first, earlier in ((0, (first_keep,)), (2, (first_sum, second_plane))):
        halves.append(
            attend_back(
                flag,
                after(low(d_self_total), *earlier),
                start_low[: 2 * quarter],
                start_low,
                w_self,
                kept_self,
                self_back,
                True,
                first,
                2,
            )
        )
    d_start_q = halves[0][0] + halves[1][0]
    with jax.named_scope("cross_sums"):
        share_cross = rows_summed(after(cross_plane, d_start_q), count, layer=1)
    with jax.named_scope("ffn_sums"):
        first_plane = plane_summed(after(first_sum, second_plane), until=(halves[1][0],))
        second_share = rows_summed(second_plane, count, until=(halves[1][0],))
    with jax.named_scope("self_sums"):
        self_sum = jnp.concatenate([from_cores(keep, send) for _, _, keep, send in halves], axis=0)
    with jax.named_scope("d_start"):
        d_start_kv = after(halves[0][1], first_plane, second_share) + halves[1][1]
        d_start = d_self_total + d_start_q + d_start_kv[: 2 * quarter]
        d_start = d_start + over(low(d_start_kv[2 * quarter :]), "section").astype(jnp.float32)
    d_source, gain_a, bias_a = norm_back(
        rows_here.astype(jnp.float32), gains[0], biases[0], d_start
    )

    norm_sums = jnp.stack(
        [
            pick(gain_a, gain_s),
            pick(gain_s, dec_gain_b),
            pick(enc_gain_c, dec_gain_c),
            pick(bias_a, bias_s),
            pick(bias_s, dec_bias_b),
            pick(enc_bias_c, dec_bias_c),
        ]
    )
    shards = 2**count
    sides = jnp.arange(2)
    held, outer = core ^ sides[:, None], sides[None, :]
    row_block = ((2 * outer + (1 ^ outer ^ held)) * shards)[:, :, None] + jnp.arange(shards)
    column_block = (2 * (y_at ^ sides)[:, None] + (x_at ^ sides)[None, :]).reshape(-1)
    order = (row_block.reshape(2, -1)[:, None, :] + 0) * 4 + column_block[:, None]
    norm_sums = jnp.take(norm_sums.reshape(6, 8 * 2 * shards, -1), order.reshape(-1), axis=1)
    norm_sums = norm_sums.reshape(6, 2, 4, 2 * shards, -1)
    with jax.named_scope("norm_sums"):
        norm_sums = norm_sums[:, 0] + over(norm_sums[:, 1], "section")
    norm_rows = low(norm_sums.transpose(1, 2, 0, 3).reshape(4, 2 * shards, 1, -1))
    norm_width = norm_rows.shape[3]

    with jax.named_scope("self_sums"):
        pad = ((0, 0), (0, 0), (0, 15), (0, self_sum.shape[2] - norm_width))
        both = jnp.concatenate(
            [self_sum.reshape(4, 2 * shards, -1, self_sum.shape[2]), jnp.pad(norm_rows, pad)], axis=2
        )
        self_plane = plane_summed(both.reshape(4, -1, self_sum.shape[2]))
        share_self = swapped(rows_summed(self_plane, count)).astype(jnp.float32)
    norm_shares = share_self[-16, :norm_width].reshape(6, -1)
    share_self = share_self[:-16]
    with jax.named_scope("ffn_sums"):
        first_share = rows_summed(first_plane, count)
        share_ffn = swapped(jnp.concatenate([first_share, second_share], axis=1)).astype(jnp.float32)
    share_first, share_second = share_ffn[:, :units], share_ffn[:, units:].T
    with jax.named_scope("hidden_grad"):
        hidden_grad = rows_out(after(low(pick(d_source, d_start)), self_plane)).astype(jnp.float32)
    g_query, g_key, g_value, g_out = unpack_heads(share_self)
    grad_qkv = jnp.stack([g_query, g_key, g_value], axis=1)
    c_query, c_key, c_value, c_out = unpack_heads(share_cross)
    with jax.named_scope("cross_out"):
        for_enc = cross_out(jnp.concatenate([c_key, c_value], axis=1), 0)
        for_dec = cross_out(jnp.concatenate([c_query, c_out], axis=1), 1)
    cross = jnp.where(core == 0, for_enc, for_dec).astype(jnp.float32)

    return (
        hidden_out,
        hidden_grad,
        grad_qkv[None],
        g_out[None],
        cross[None, :, :width],
        cross[None, :, width:],
        share_first[None],
        share_second[None],
        norm_shares[None, :3],
        norm_shares[None, 3:],
    )


def solution(mesh):
    _, dp_count, _ = mesh.devices.shape
    count = dp_count.bit_length() - 3
    names = axes_of(count)
    dp, tensor = names[1:-2], names[-2:]
    split = Mesh(mesh.devices.reshape((2,) * len(names)), names)
    rows = P("section", None, dp, tensor, None)
    in_specs = (
        rows,
        rows,
        P(None, None, dp, None),
        P("section", dp, None, tensor),
        P("section", dp, tensor),
        P("section", dp, tensor),
        P("section", dp, tensor),
        P("section", dp, tensor),
        P("section", tensor, dp),
        P("section", None, None),
        P("section", None, None),
    )
    out_specs = (
        rows,
        rows,
        P("section", dp, None, tensor),
        P("section", dp, tensor),
        P("section", dp, tensor),
        P("section", dp, tensor),
        P("section", dp, tensor),
        P("section", tensor, dp),
        P("section", None, dp + tensor),
        P("section", None, dp + tensor),
    )
    return jax.shard_map(
        functools.partial(body, count), mesh=split, in_specs=in_specs, out_specs=out_specs, check_vma=False
    )
```

```python
import functools

import jax
import jax.numpy as jnp
from jax import lax
from jax.experimental import pallas as pl
from jax.experimental.pallas import tpu as pltpu
from jax.sharding import Mesh
from jax.sharding import PartitionSpec as P

HDIM = 64
LANES = 128
MASKED = -1e30
NORM_EPS = 1e-05
VMEM_BYTES = 56 * 1024 * 1024

SEG_LANES = 8
PART_LANE = 12

PARTS = 2
HEADS = ((0, 1, 2, 0, 0), (0, 1, 2, 1, 1), (1, 3, 0, 0, 1))


def mul(a, b):
    return jnp.dot(a, b, preferred_element_type=jnp.float32)


def mul_nt(a, b):
    return lax.dot_general(a, b, (((1,), (1,)), ((), ())), preferred_element_type=jnp.float32)


def mul_tn(a, b):
    return lax.dot_general(a, b, (((0,), (0,)), ((), ())), preferred_element_type=jnp.float32)


def tile_of(values, index):
    return values[:, index * LANES : (index + 1) * LANES]


def lane_ids(rows):
    return lax.broadcasted_iota(jnp.int32, (rows, LANES), 1)


def half_mask(rows, half):
    lanes = lane_ids(rows)
    return lanes >= HDIM if half else lanes < HDIM


def in_parts(base, column):
    lanes = lane_ids(base.shape[0])
    high = column.astype(jnp.bfloat16).astype(jnp.float32)
    rest = column - high
    middle = rest.astype(jnp.bfloat16).astype(jnp.float32)
    low = rest - middle
    parts = jnp.where(
        lanes == PART_LANE,
        high,
        jnp.where(lanes == PART_LANE + 1, middle, jnp.where(lanes == PART_LANE + 2, low, base)),
    )
    return parts.astype(jnp.bfloat16)


def with_triangle(scores, tri, at):
    size = tri.shape[1]
    pieces = []
    if at > 0:
        pieces.append(scores[:, : at * size])
    pieces.append(scores[:, at * size : (at + 1) * size] + tri)
    pieces.append(scores[:, (at + 1) * size :])
    return jnp.concatenate(pieces, axis=1)


def places(core, block):
    return [pl.multiple_of((1 - core) * block, block), pl.multiple_of((2 + core) * block, block)]


def assemble(flag_ref, own_refs, peer_refs, w_ref):
    core, block = flag_ref[0], own_refs[0].shape[1] // 2
    for holder, refs in ((core, own_refs), (1 - core, peer_refs)):
        for part, ref in enumerate(refs):
            width = ref.shape[2]
            for at, place in enumerate(places(holder, block)):
                w_ref[pl.ds(place, block), part * width : (part + 1) * width] = ref[0, at * block : (at + 1) * block]


def hand_out(flag_ref, g_ref, keep_ref, send_ref):
    core, block = flag_ref[0], keep_ref.shape[1] // 2
    for holder, ref in ((core, keep_ref), (1 - core, send_ref)):
        for at, place in enumerate(places(holder, block)):
            ref[0, at * block : (at + 1) * block] = g_ref[pl.ds(place, block), :]


def where_active(kernel):
    def guarded(flag_ref, *refs):
        @pl.when(flag_ref[1] == 1)
        def _():
            kernel(flag_ref, *refs)

    return guarded


def scaled_queries(q_ref, at, q_tile, q_half):
    queries = q_ref[0, at, q_tile * LANES : (q_tile + 1) * LANES] * 0.125
    return jnp.where(half_mask(queries.shape[0], q_half), queries, 0).astype(jnp.bfloat16)


def units_of(total, rows):
    return [
        (slice(part * rows, (part + 1) * rows), part, head)
        for part in range(total // rows)
        for head in range(len(HEADS))
    ]


def attend_kernel(causal, flag_ref, xq_ref, xkv_ref, *refs):
    own_refs, peer_refs = refs[:1], refs[1:2]
    qx_ref, kx_ref, tri_ref, o_ref, q_ref, kv_ref, c_ref, l_ref, w_ref = refs[2:]
    block = pl.program_id(0)
    assemble(flag_ref, own_refs, peer_refs, w_ref)
    q_ref[0] = mul(xq_ref[...], w_ref[:, : 2 * LANES]).astype(jnp.bfloat16)
    kv_ref[0] = mul(xkv_ref[...], w_ref[:, LANES : 5 * LANES]).astype(jnp.bfloat16)
    rows = tri_ref.shape[0]
    low = half_mask(rows, 0)

    def scores_of(at, part, head):
        q_tile, k_tile, _, q_half, _ = HEADS[head]
        keys = kv_ref[0, :, k_tile * LANES : (k_tile + 1) * LANES]
        scores = mul_nt(
            jnp.concatenate([scaled_queries(q_ref, at, q_tile, q_half), qx_ref[at, :]], axis=1),
            jnp.concatenate([keys, kx_ref[...]], axis=1),
        )
        return with_triangle(scores, tri_ref[...], part) if causal else scores

    units = units_of(q_ref.shape[1], rows)
    ahead = scores_of(*units[0])
    contexts, totals = [], None
    for index, (at, part, head) in enumerate(units):
        scores = ahead
        if index + 1 < len(units):
            ahead = scores_of(*units[index + 1])
        v_tile = HEADS[head][2]
        values = kv_ref[0, :, v_tile * LANES : (v_tile + 1) * LANES]
        highest = jnp.max(scores, axis=1, keepdims=True)
        weights = jnp.exp(scores - highest)
        sums = jnp.sum(weights, axis=1, keepdims=True)
        contexts.append(mul(weights.astype(jnp.bfloat16), values) / sums)
        logs = jnp.broadcast_to(highest + jnp.log(sums), (rows, LANES))
        totals = logs if head == 0 else jnp.where(lane_ids(rows) == head, logs, totals)
        if head == len(HEADS) - 1:
            c_ref[0, at, :LANES] = jnp.where(low, 0, contexts[2]).astype(jnp.bfloat16)
            c_ref[0, at, LANES:] = jnp.where(low, contexts[0], contexts[1]).astype(jnp.bfloat16)
            l_ref[0, at, :] = totals
            contexts = []
    out = mul_nt(c_ref[0], w_ref[:, 4 * LANES :])

    @pl.when(block == 0)
    def _():
        o_ref[...] = out

    @pl.when(block > 0)
    def _():
        o_ref[...] += out


def attend_back_kernel(causal, flag_ref, do_ref, xq_ref, xkv_ref, *refs):
    own_refs, peer_refs = refs[:1], refs[1:2]
    q_ref, kv_ref, c_ref, l_ref, qx_ref, kx_ref, tri_ref, dxq_ref, dxkv_ref, *refs = refs[2:]
    keep_ref, send_ref, w_ref, sum_ref, dq_ref, dkv_ref, g_ref = refs
    rows = tri_ref.shape[0]
    assemble(flag_ref, own_refs, peer_refs, w_ref)
    d_context = mul(do_ref[...], w_ref[:, 4 * LANES :]).astype(jnp.bfloat16)
    low = half_mask(rows, 0)

    def products_of(at, part, head):
        q_tile, k_tile, v_tile, q_half, v_half = HEADS[head]
        c_tile = 0 if head == 2 else 1
        keys = kv_ref[0, :, k_tile * LANES : (k_tile + 1) * LANES]
        values = kv_ref[0, :, v_tile * LANES : (v_tile + 1) * LANES]
        queries = scaled_queries(q_ref, at, q_tile, q_half)
        d_rows = jnp.where(half_mask(rows, v_half), tile_of(d_context[at], c_tile), 0).astype(jnp.bfloat16)
        total = l_ref[0, at, head : head + 1]
        scores = mul_nt(
            jnp.concatenate([queries, in_parts(qx_ref[at, :].astype(jnp.float32), -total)], axis=1),
            jnp.concatenate([keys, kx_ref[...]], axis=1),
        )
        if causal:
            scores = with_triangle(scores, tri_ref[...], part)
        return scores, mul_nt(d_rows, values), queries, d_rows, keys

    units = units_of(q_ref.shape[1], rows)
    ahead = products_of(*units[0])
    d_queries = []
    for index, (at, part, head) in enumerate(units):
        scores, d_probs, queries, d_rows, keys = ahead
        if index + 1 < len(units):
            ahead = products_of(*units[index + 1])
        _, k_tile, v_tile, _, _ = HEADS[head]
        probs = jnp.exp(scores)
        inner = jnp.sum(probs * d_probs, axis=1, keepdims=True)
        d_scores = (probs * (d_probs - inner)).astype(jnp.bfloat16)
        d_values = mul_tn(probs.astype(jnp.bfloat16), d_rows)
        d_keys = mul_tn(d_scores, queries)
        d_queries.append(mul(d_scores, keys) * 0.125)
        k_at = slice(k_tile * LANES, (k_tile + 1) * LANES)
        v_at = slice(v_tile * LANES, (v_tile + 1) * LANES)
        if part == 0 and head != 1:
            sum_ref[:, k_at] = d_keys
            sum_ref[:, v_at] = d_values
        else:
            sum_ref[:, k_at] += d_keys
            sum_ref[:, v_at] += d_values
        if head == len(HEADS) - 1:
            dq_ref[at, :LANES] = jnp.where(low, d_queries[0], d_queries[1]).astype(jnp.bfloat16)
            dq_ref[at, LANES:] = jnp.where(low, d_queries[2], 0).astype(jnp.bfloat16)
            d_queries = []
    dkv_ref[...] = sum_ref[...].astype(jnp.bfloat16)
    d_xq = mul_nt(dq_ref[...], w_ref[:, : 2 * LANES])
    d_xkv = mul_nt(dkv_ref[...], w_ref[:, LANES : 5 * LANES])

    @pl.when(pl.program_id(0) == 0)
    def _():
        dxq_ref[...] = d_xq
        dxkv_ref[...] = d_xkv

    @pl.when(pl.program_id(0) > 0)
    def _():
        dxq_ref[...] += d_xq
        dxkv_ref[...] += d_xkv

    grad_q = mul_tn(xq_ref[...], dq_ref[...])
    grad_kv = mul_tn(xkv_ref[...], dkv_ref[...])
    grad_o = mul_tn(do_ref[...], c_ref[0])
    g_ref[:, :LANES] = grad_q[:, :LANES].astype(jnp.bfloat16)
    g_ref[:, LANES : 2 * LANES] = (grad_q[:, LANES:] + grad_kv[:, :LANES]).astype(jnp.bfloat16)
    g_ref[:, 2 * LANES : 4 * LANES] = grad_kv[:, LANES : 3 * LANES].astype(jnp.bfloat16)
    g_ref[:, 4 * LANES : 5 * LANES] = (grad_kv[:, 3 * LANES :] + grad_o[:, :LANES]).astype(jnp.bfloat16)
    g_ref[:, 5 * LANES :] = grad_o[:, LANES:].astype(jnp.bfloat16)
    hand_out(flag_ref, g_ref, keep_ref, send_ref)


def whole(shape):
    return pl.BlockSpec(shape, lambda j, flag: (0,) * len(shape))


def per_block(shape, first=0, gate=1):
    return pl.BlockSpec((1,) + shape, lambda j, flag: (first + j * flag[gate],) + (0,) * len(shape))


shape = jax.ShapeDtypeStruct


def call(kernel, name, micros, moved, grid, in_specs, out_specs, out_shape, scratch, *operands):
    return pl.pallas_call(
        where_active(kernel),
        grid_spec=pltpu.PrefetchScalarGridSpec(
            num_scalar_prefetch=1,
            grid=(grid,),
            in_specs=in_specs,
            out_specs=out_specs,
            scratch_shapes=scratch,
        ),
        out_shape=out_shape,
        compiler_params=pltpu.CompilerParams(vmem_limit_bytes=VMEM_BYTES),
        cost_estimate=cost(micros, moved),
        name=name,
    )(*operands)


def cost(micros, moved):
    return pl.CostEstimate(flops=int(micros * 1.15e9), bytes_accessed=int(moved), transcendentals=0)


def attend(flag, xq, xkv, weights, extras, causal, first, count):
    rows, width = xq.shape
    keys = xkv.shape[0]
    return call(
        functools.partial(attend_kernel, causal),
        "attend_self" if causal else "attend_cross",
        5 * count,
        6 * 2**20 * count,
        count,
        [whole((rows, width)), whole((keys, width))]
        + [per_block(part.shape[1:], first) for part in weights]
        + [whole(extra.shape) for extra in extras],
        [
            whole((rows, width)),
            per_block((rows, 2 * LANES)),
            per_block((keys, 4 * LANES)),
            per_block((rows, 2 * LANES)),
            per_block((rows, LANES)),
        ],
        [
            shape((rows, width), jnp.float32),
            shape((count, rows, 2 * LANES), jnp.bfloat16),
            shape((count, keys, 4 * LANES), jnp.bfloat16),
            shape((count, rows, 2 * LANES), jnp.bfloat16),
            shape((count, rows, LANES), jnp.float32),
        ],
        [pltpu.VMEM((width, 6 * LANES), jnp.bfloat16)],
        flag,
        xq,
        xkv,
        *weights,
        *extras,
    )


def attend_back(flag, d_out, xq, xkv, weights, kept, extras, causal, first, count):
    rows, width = xq.shape
    keys = xkv.shape[0]
    return call(
        functools.partial(attend_back_kernel, causal),
        "attend_self_back" if causal else "attend_cross_back",
        10 * count,
        6 * 2**20 * count,
        count,
        [whole((rows, width)), whole((rows, width)), whole((keys, width))]
        + [per_block(part.shape[1:], first) for part in weights]
        + [
            per_block((rows, 2 * LANES)),
            per_block((keys, 4 * LANES)),
            per_block((rows, 2 * LANES)),
            per_block((rows, LANES)),
        ]
        + [whole(extra.shape) for extra in extras],
        [whole((rows, width)), whole((keys, width))] + [per_block(part.shape[1:]) for part in weights],
        [shape((rows, width), jnp.float32), shape((keys, width), jnp.float32)]
        + [shape((count,) + part.shape[1:], jnp.bfloat16) for part in weights],
        [
            pltpu.VMEM((width, 6 * LANES), jnp.bfloat16),
            pltpu.VMEM((keys, 4 * LANES), jnp.float32),
            pltpu.VMEM((rows, 2 * LANES), jnp.bfloat16),
            pltpu.VMEM((keys, 4 * LANES), jnp.bfloat16),
            pltpu.VMEM((width, 6 * LANES), jnp.bfloat16),
        ],
        flag,
        d_out,
        xq,
        xkv,
        *weights,
        *kept,
        *extras,
    )


def ffn_kernel(flag_ref, x_ref, *refs):
    own_refs, peer_refs = refs[:PARTS], refs[PARTS : 2 * PARTS]
    z_ref, g_ref, slope_ref, w_ref = refs[2 * PARTS :]
    block = pl.program_id(0)
    assemble(flag_ref, own_refs, peer_refs, w_ref)
    units = own_refs[0].shape[2]
    inner = mul(x_ref[...], w_ref[:, :units])
    spread = 0.5 * (1.0 + lax.erf(inner * (0.5**0.5)))
    bell = jnp.exp(-0.5 * inner * inner) * 0.3989422804014327
    active = (inner * spread).astype(jnp.bfloat16)
    g_ref[0] = active
    slope_ref[0] = (spread + inner * bell).astype(jnp.bfloat16)
    out = mul_nt(active, w_ref[:, units:])

    @pl.when(block == 0)
    def _():
        z_ref[...] = out

    @pl.when(block > 0)
    def _():
        z_ref[...] += out


def ffn(flag, x, weights):
    rows, width = x.shape
    blocks, _, units = weights[0].shape
    return call(
        ffn_kernel,
        "ffn",
        12,
        rows * units * blocks * 16,
        blocks,
        [whole((rows, width))] + [per_block(part.shape[1:]) for part in weights],
        [whole((rows, width)), per_block((rows, units)), per_block((rows, units))],
        [
            shape((rows, width), jnp.float32),
            shape((blocks, rows, units), jnp.bfloat16),
            shape((blocks, rows, units), jnp.bfloat16),
        ],
        [pltpu.VMEM((width, 2 * units), jnp.bfloat16)],
        flag,
        x,
        *weights,
    )


def ffn_back_kernel(flag_ref, dz_ref, *refs):
    own_refs, peer_refs = refs[:PARTS], refs[PARTS : 2 * PARTS]
    slope_ref, dx_ref, dh_ref, w_ref = refs[2 * PARTS :]
    block = pl.program_id(0)
    assemble(flag_ref, own_refs, peer_refs, w_ref)
    units = own_refs[0].shape[2]
    d_active = mul(dz_ref[...], w_ref[:, units:])
    d_inner = (d_active * slope_ref[0].astype(jnp.float32)).astype(jnp.bfloat16)
    dh_ref[0] = d_inner
    out = mul_nt(d_inner, w_ref[:, :units])

    @pl.when(block == 0)
    def _():
        dx_ref[...] = out

    @pl.when(block > 0)
    def _():
        dx_ref[...] += out


def ffn_back(flag, dz, weights, slope):
    rows, width = dz.shape
    blocks, _, units = weights[0].shape
    return call(
        ffn_back_kernel,
        "ffn_back",
        12,
        rows * units * blocks * 12,
        blocks,
        [whole((rows, width))] + [per_block(part.shape[1:]) for part in weights] + [per_block((rows, units))],
        [whole((rows, width)), per_block((rows, units))],
        [
            shape((rows, width), jnp.float32),
            shape((blocks, rows, units), jnp.bfloat16),
        ],
        [pltpu.VMEM((width, 2 * units), jnp.bfloat16)],
        flag,
        dz,
        *weights,
        slope,
    )


def ffn_grad_kernel(flag_ref, left_ref, enc_ref, dec_ref, keep_ref, send_ref, g_ref):
    right = jnp.where(flag_ref[2] == 1, enc_ref[0], dec_ref[0])
    g_ref[...] = mul_tn(left_ref[...], right).astype(jnp.bfloat16)
    hand_out(flag_ref, g_ref, keep_ref, send_ref)


def ffn_grad(flag, left, enc_right, dec_right, like):
    rows, width = left.shape
    blocks, _, units = enc_right.shape
    return call(
        ffn_grad_kernel,
        "ffn_grad",
        6,
        rows * units * blocks * 8,
        blocks,
        [whole((rows, width)), per_block((rows, units), 0, 2), per_block((rows, units), 0, 3)],
        [per_block(like.shape[1:])] * 2,
        [shape(like.shape, jnp.bfloat16)] * 2,
        [pltpu.VMEM((width, units), jnp.bfloat16)],
        flag,
        left,
        enc_right,
        dec_right,
    )


def layer_norm(values, gain_row, bias_row):
    average = jnp.mean(values, axis=-1, keepdims=True)
    centered = values - average
    variance = jnp.mean(centered * centered, axis=-1, keepdims=True)
    return centered * lax.rsqrt(variance + NORM_EPS) * gain_row + bias_row


def norm_back(values, gain_row, bias_row, upstream):
    _, pullback = jax.vjp(layer_norm, values, gain_row, bias_row)
    return pullback(upstream)


def low(values):
    return values.astype(jnp.bfloat16)


def axes_of(count):
    return ("section", "zh", "zl") + tuple("e%d" % at for at in range(count)) + ("ty", "tx")


def layer_of(place):
    return 1 ^ place["zh"] ^ place["zl"]


def moved(x, names, to):
    names = [name for name in axes_of(8) if name in names]

    def index(place):
        return sum(place[name] << (len(names) - 1 - at) for at, name in enumerate(names))

    pairs = []
    for source in range(2 ** len(names)):
        place = {name: source >> (len(names) - 1 - at) & 1 for at, name in enumerate(names)}
        target = to(place)
        if target is not None:
            pairs.append((source, index(target)))
    return lax.ppermute(x, tuple(names), pairs)


def over(x, *axes, layer=None):
    def to(place):
        if layer is not None and layer_of(place) != layer:
            return None
        return {**place, **{axis: 1 - place[axis] for axis in axes}}

    return moved(x, axes if layer is None else axes + Z, to)


Z = ("zh", "zl")


def swapped(x):
    def to(place):
        if place["section"] == layer_of(place):
            return place
        return {"section": 1 - place["section"], "zh": place["zh"], "zl": 1 - place["zl"]}

    return moved(x, ("section",) + Z, to)


def turned(x):
    return moved(x, ("section", "ty"), lambda place: {"section": place["ty"], "ty": place["section"]})


def sent_home(x, other):
    def to(place):
        return {
            "section": layer_of(place),
            "zh": place["zh"],
            "zl": 1 ^ place["zh"] ^ place["ty"],
            "ty": place["section"],
            "tx": place["tx"] ^ other,
        }

    return moved(x, ("section",) + Z + ("ty", "tx"), to)


def cross_in(x, layer):
    def to(place):
        if place["section"] != layer:
            return None
        return {"section": layer_of(place), "zh": place["zh"], "zl": place["zh"]}

    return moved(x, ("section",) + Z, to)


def cross_out(x, layer):
    def to(place):
        if layer_of(place) != 1:
            return None
        return {"section": layer, "zh": place["zh"], "zl": 1 ^ place["zh"] ^ place["section"]}

    return moved(x, ("section",) + Z, to)


def in_order(x, flag, axis):
    return jnp.where(flag == 1, jnp.flip(x, axis), x)


def pack_heads(query, key, value, out):
    pair = 2 * HDIM
    return jnp.concatenate(
        [
            query,
            value[:, pair:],
            key[:, :pair],
            value[:, :pair],
            key[:, pair:],
            out[:, pair:],
            out[:, :pair],
        ],
        axis=1,
    )


def unpack_heads(packed):
    part = [packed[:, at * HDIM : (at + 1) * HDIM] for at in range(12)]
    query = jnp.concatenate(part[0:3], axis=1)
    key = jnp.concatenate([part[4], part[5], part[8]], axis=1)
    value = jnp.concatenate([part[6], part[7], part[3]], axis=1)
    out = jnp.concatenate([part[10], part[11], part[9]], axis=1)
    return query, key, value, out


def after(x, *earlier):
    return lax.optimization_barrier((x,) + earlier)[0]


def plane_gathered(x, until=(), **only):
    parts = [x, over(x, "tx", **only), over(x, "ty", **only), over(x, "ty", "tx", **only)]
    return jnp.stack([after(part, *until) for part in parts])


def plane_summed(x, until=(), **only):
    terms = [x[0], over(x[1], "tx", **only), over(x[2], "ty", **only), over(x[3], "ty", "tx", **only)]
    terms = [after(term, *until) for term in terms]
    return low(sum(term.astype(jnp.float32) for term in terms))


def rows_gathered(x, count, until=(), **only):
    for axes in [("e%d" % at,) for at in reversed(range(count))] + [Z]:
        parts = [after(part, *until) for part in (x, over(x, *axes, **only))]
        both = in_order(jnp.stack(parts, axis=-3), lax.axis_index(axes[0]), x.ndim - 2)
        x = both.reshape(x.shape[:-2] + (2 * x.shape[-2], x.shape[-1]))
    return x


def rows_summed(x, count, until=(), **only):
    for axes in [Z] + [("e%d" % at,) for at in range(count)]:
        halves = x.reshape(x.shape[:-2] + (2, x.shape[-2] // 2, x.shape[-1]))
        halves = in_order(halves, lax.axis_index(axes[0]), x.ndim - 2)
        x = plus(halves[..., 0, :, :], after(over(halves[..., 1, :, :], *axes, **only), *until))
    return x


def plus(first, second):
    return low(first.astype(jnp.float32) + second.astype(jnp.float32))


def from_cores(keep, send, **only):
    return plus(keep, over(send, "section", **only))


def body(
    count,
    hidden,
    cotangent,
    segments,
    sa_qkv,
    sa_out,
    cross_one,
    cross_two,
    ffn_in,
    ffn_out,
    norm_gain,
    norm_bias,
):
    core = lax.axis_index("section")
    x_at, y_at, zh_at, zl_at = (lax.axis_index(name) for name in ("tx", "ty", "zh", "zl"))
    layer = 1 ^ zh_at ^ zl_at
    on_encoder = layer == 0
    quarter = hidden.shape[3]
    enc_flag = jnp.stack([core, 1 - layer, 1 - layer, layer])
    dec_flag = jnp.stack([core, layer, 1 - layer, layer])
    flag = jnp.stack([core, jnp.ones_like(core), 1 - layer, layer])

    def pick(first, second):
        return jnp.where(on_encoder, first, second)

    def of_one_row(x):
        both = in_order(x[0, :, 0], x_at, 0)
        return in_order(jnp.stack([both[0], over(both[1], "tx")]), x_at, 0).reshape(2 * quarter, -1)

    def rows_out(x, *until):
        mine, other = in_order(x.reshape(2, quarter, -1), x_at, 0)
        both = [after(sent_home(mine, 0), *until), after(sent_home(other, 1), *until)]
        return in_order(jnp.stack(both), x_at, 0)[None, :, None]

    units = ffn_in.shape[2]
    width = cross_one.shape[2]
    packed_self = pack_heads(sa_qkv[0, :, 0], sa_qkv[0, :, 1], sa_qkv[0, :, 2], sa_out[0])
    packed_ffn = jnp.concatenate([ffn_in[0], ffn_out[0].T], axis=1)
    with jax.named_scope("norms_in"):
        norms = swapped(jnp.concatenate([norm_gain[0], norm_bias[0]], axis=0))
        gains, biases = norms[:3], norms[3:]
        seg_own = segments[:, :, 0].astype(jnp.float32)
        seg_here = jnp.where(zl_at == 1 ^ zh_at ^ y_at, seg_own, over(seg_own, "zl")).astype(jnp.int32)
    with jax.named_scope("hidden_in"):
        one_row = of_one_row(hidden)
    with jax.named_scope("self_weights"):
        shard_self = swapped(packed_self)
    with jax.named_scope("hidden_in"):
        one_row = swapped(after(one_row, shard_self))
    with jax.named_scope("ffn_weights"):
        shard_ffn = swapped(after(packed_ffn, one_row))
        shard_first, shard_second = shard_ffn[:, :units], shard_ffn[:, units:]

    def both_rows(x, later):
        for_enc = rows_gathered(x, count, layer=0)
        return pick(for_enc, rows_gathered(after(x, for_enc, later), count, layer=1))

    with jax.named_scope("self_weights"):
        rows_self = both_rows(shard_self, one_row)
        own_self = plane_gathered(rows_self)
        w_self = [own_self, over(own_self, "section")]
    with jax.named_scope("hidden_in"):
        rows_here = turned(one_row)
        rows_all = jnp.concatenate([rows_here, over(rows_here, "section")], axis=0)
    with jax.named_scope("cross_weights"):
        cross_low = after(jnp.concatenate([cross_one[0], cross_two[0]], axis=1), own_self)
        pair_kv, pair_qo = cross_in(cross_low, 0), cross_in(cross_low, 1)
        packed = pack_heads(pair_qo[:, :width], pair_kv[:, :width], pair_kv[:, width:], pair_qo[:, width:])
    with jax.named_scope("ffn_weights"):
        rows_first = both_rows(after(shard_first, rows_self), own_self)
        plane_second = plane_gathered(after(shard_second, own_self))

    both_segments = in_order(seg_here, x_at, 1)[:, 0]
    ordered = in_order(both_segments.reshape(2, 2, 2 * quarter), core, 1).reshape(2, 4 * quarter)
    source_seg, target_seg = ordered[0], ordered[1]
    self_seg = pick(source_seg, target_seg)
    parts = jnp.arange(4)
    quarter_of = jnp.repeat(2 * ((parts // 2) ^ core) + parts % 2, quarter)
    lanes = jnp.arange(LANES)[None, :]

    def key_extras(seg):
        differs = jnp.logical_and(lanes < SEG_LANES, seg[:, None] != lanes)
        later = jnp.logical_and(
            jnp.logical_and(lanes >= SEG_LANES, lanes < PART_LANE),
            quarter_of[:, None] > lanes - SEG_LANES,
        )
        part = jnp.logical_and(lanes >= PART_LANE, lanes < PART_LANE + 3)
        return jnp.where(differs | later | part, 1.0, 0.0).astype(jnp.bfloat16)

    def query_extras(seg, causal):
        seg, at = seg[: 2 * quarter], quarter_of[: 2 * quarter]
        same = seg[:, None] == lanes
        here = jnp.logical_and(at[:, None] + SEG_LANES == lanes, causal)
        return jnp.where(same | here, MASKED, 0.0).astype(jnp.bfloat16)

    at_row = jnp.arange(quarter)
    later_key = jnp.logical_and(at_row[None, :] > at_row[:, None], jnp.logical_not(on_encoder))
    tri = jnp.where(later_key, MASKED, 0.0).astype(jnp.float32)
    self_extras = (query_extras(self_seg, jnp.logical_not(on_encoder)), key_extras(self_seg), tri)
    cross_extras = (query_extras(target_seg, False), key_extras(source_seg), tri)

    start = rows_all.astype(jnp.float32)
    start = pick(layer_norm(start, gains[0], biases[0]), start)
    start_here = start[: 2 * quarter]
    start_low = low(start)
    self_gain, self_bias = pick(gains[1], gains[0]), pick(biases[1], biases[0])
    kept_self = []
    for first, earlier in ((0, ()), (2, (plane_second,))):
        kept_self.append(
            attend(flag, start_low[: 2 * quarter], after(start_low, *earlier), w_self, self_extras, True, first, 2)
        )
    self_out = kept_self[0][0] + kept_self[1][0]
    with jax.named_scope("ffn_weights"):
        own_first = plane_gathered(after(rows_first, plane_second), until=(kept_self[1][0],))
        enc_second = rows_gathered(plane_second, count, until=(kept_self[1][0],), layer=0)
        peer_first = over(own_first, "section")
        w_enc = [own_first, enc_second, peer_first, over(enc_second, "section", layer=0)]
    with jax.named_scope("cotangent_in"):
        cot_row = of_one_row(after(cotangent, self_out))
    self_total = start_here + self_out
    middle = layer_norm(self_total, self_gain, self_bias)
    middle_low = low(middle)

    enc_out, enc_active, enc_slope = ffn(enc_flag, middle_low, w_enc)
    enc_total = middle + enc_out
    encoded = low(layer_norm(enc_total, gains[2], biases[2]))
    with jax.named_scope("cross_weights"):
        rows_cross = rows_gathered(after(packed, plane_second), count, until=(kept_self[1][0],), layer=1)
        own_cross = plane_gathered(rows_cross, until=(encoded,), layer=1)
        w_cross = [own_cross, over(own_cross, "section", layer=1)]
    with jax.named_scope("ffn_weights"):
        dec_second = rows_gathered(after(plane_second, self_out), count, until=(encoded,), layer=1)
        w_dec = [own_first, dec_second, peer_first, over(dec_second, "section", layer=1)]

    def across(x, layer):
        return moved(x, Z, lambda place: {**place, "zl": 1 - place["zl"]} if layer_of(place) == layer else None)

    with jax.named_scope("memory"):
        memory_here = across(encoded, 0)
        memory = jnp.concatenate([memory_here, over(memory_here, "section", layer=1)], axis=0)
    with jax.named_scope("cotangent_in"):
        cot = turned(swapped(after(cot_row, memory_here))).astype(jnp.float32)

    cross_out_rows, *kept_cross = attend(dec_flag, middle_low, memory, w_cross, cross_extras, False, 0, 4)
    cross_total = middle + cross_out_rows
    crossed = layer_norm(cross_total, gains[1], biases[1])
    crossed_low = low(crossed)
    dec_out, dec_active, dec_slope = ffn(dec_flag, crossed_low, w_dec)
    dec_total = crossed + dec_out
    decoded = low(layer_norm(dec_total, gains[2], biases[2]))

    d_dec_total, dec_gain_c, dec_bias_c = norm_back(dec_total, gains[2], biases[2], cot)
    d_dec_low = low(d_dec_total)
    d_after, dec_inner = ffn_back(dec_flag, d_dec_low, w_dec, dec_slope)
    d_cross_total, dec_gain_b, dec_bias_b = norm_back(
        cross_total, gains[1], biases[1], d_dec_total + d_after
    )
    d_middle_part, d_memory, cross_keep, cross_send = attend_back(
        dec_flag, low(d_cross_total), middle_low, memory, w_cross, kept_cross, cross_extras, False, 0, 4
    )
    with jax.named_scope("hidden_out"):
        hidden_out = rows_out(after(pick(encoded, decoded), d_after), d_middle_part)
    with jax.named_scope("d_memory"):
        d_memory = after(d_memory, hidden_out)
        d_memory_here = d_memory[: 2 * quarter] + over(
            low(d_memory[2 * quarter :]), "section", layer=1
        ).astype(jnp.float32)
        d_memory_low = low(d_memory_here)
        d_encoded = across(d_memory_low, 1).astype(jnp.float32) + cot
    with jax.named_scope("cross_sums"):
        cross_sum = from_cores(after(cross_keep, d_memory_low), after(cross_send, d_memory_low), layer=1)
        cross_plane = plane_summed(cross_sum, layer=1)

    d_enc_total, enc_gain_c, enc_bias_c = norm_back(enc_total, gains[2], biases[2], d_encoded)
    d_enc_low = low(d_enc_total)
    second_keep, second_send = ffn_grad(
        flag, pick(d_enc_low, d_dec_low), enc_active, dec_active, own_first
    )
    with jax.named_scope("ffn_sums"):
        second_sum = from_cores(second_keep, second_send)
    d_enc_middle, enc_inner = ffn_back(enc_flag, after(d_enc_low, second_keep, cross_plane), w_enc, enc_slope)
    with jax.named_scope("ffn_sums"):
        second_plane = plane_summed(second_sum)
    first_keep, first_send = ffn_grad(
        flag, after(pick(middle_low, crossed_low), second_sum), enc_inner, dec_inner, own_first
    )
    with jax.named_scope("ffn_sums"):
        first_sum = from_cores(first_keep, first_send)

    d_middle = pick(d_enc_total + d_enc_middle, d_cross_total + d_middle_part)
    d_self_total, gain_s, bias_s = norm_back(self_total, self_gain, self_bias, d_middle)
    halves = []
    for first, earlier in ((0, (first_keep,)), (2, (first_sum, second_plane))):
        halves.append(
            attend_back(
                flag,
                after(low(d_self_total), *earlier),
                start_low[: 2 * quarter],
                start_low,
                w_self,
                kept_self[first // 2][1:],
                self_extras,
                True,
                first,
                2,
            )
        )
    d_start_q = halves[0][0] + halves[1][0]
    with jax.named_scope("cross_sums"):
        share_cross = rows_summed(after(cross_plane, d_start_q), count, layer=1)
    with jax.named_scope("ffn_sums"):
        first_plane = plane_summed(after(first_sum, second_plane), until=(halves[1][0],))
        second_share = rows_summed(second_plane, count, until=(halves[1][0],))
    with jax.named_scope("self_sums"):
        self_sum = jnp.concatenate([from_cores(keep, send) for _, _, keep, send in halves], axis=0)
    with jax.named_scope("d_start"):
        d_start_kv = after(halves[0][1], first_plane, second_share) + halves[1][1]
        d_start = d_self_total + d_start_q + d_start_kv[: 2 * quarter]
        d_start = d_start + over(low(d_start_kv[2 * quarter :]), "section").astype(jnp.float32)
    d_source, gain_a, bias_a = norm_back(
        rows_here.astype(jnp.float32), gains[0], biases[0], d_start
    )

    norm_sums = jnp.stack(
        [
            pick(gain_a, gain_s),
            pick(gain_s, dec_gain_b),
            pick(enc_gain_c, dec_gain_c),
            pick(bias_a, bias_s),
            pick(bias_s, dec_bias_b),
            pick(enc_bias_c, dec_bias_c),
        ]
    )
    shards = 2**count
    sides = jnp.arange(2)
    held, outer = core ^ sides[:, None], sides[None, :]
    row_block = ((2 * outer + (1 ^ outer ^ held)) * shards)[:, :, None] + jnp.arange(shards)
    column_block = (2 * (y_at ^ sides)[:, None] + (x_at ^ sides)[None, :]).reshape(-1)
    order = (row_block.reshape(2, -1)[:, None, :] + 0) * 4 + column_block[:, None]
    norm_sums = jnp.take(norm_sums.reshape(6, 8 * 2 * shards, -1), order.reshape(-1), axis=1)
    norm_sums = norm_sums.reshape(6, 2, 4, 2 * shards, -1)
    with jax.named_scope("norm_sums"):
        norm_sums = norm_sums[:, 0] + over(norm_sums[:, 1], "section")
    with jax.named_scope("self_sums"):
        self_plane = plane_summed(self_sum)
    with jax.named_scope("norm_sums"):
        norm_blocks = after(norm_sums.transpose(1, 2, 0, 3).reshape(4, 2 * shards, -1), self_plane)
        norm_plane = norm_blocks[0] + over(norm_blocks[1], "tx") + over(norm_blocks[2], "ty")
        norm_plane = norm_plane + over(norm_blocks[3], "ty", "tx")
    norm_width = norm_plane.shape[1]
    with jax.named_scope("self_sums"):
        pad = ((0, 0), (0, 15), (0, self_plane.shape[1] - norm_width))
        both = jnp.concatenate(
            [
                self_plane.reshape(2 * shards, -1, self_plane.shape[1]),
                jnp.pad(low(norm_plane)[:, None], pad),
            ],
            axis=1,
        )
        share_self = swapped(rows_summed(both.reshape(-1, self_plane.shape[1]), count)).astype(jnp.float32)
    norm_shares = share_self[-16, :norm_width].reshape(6, -1)
    share_self = share_self[:-16]
    with jax.named_scope("ffn_sums"):
        first_share = rows_summed(first_plane, count, until=(self_sum,))
        share_ffn = swapped(jnp.concatenate([first_share, second_share], axis=1)).astype(jnp.float32)
    share_first, share_second = share_ffn[:, :units], share_ffn[:, units:].T
    with jax.named_scope("hidden_grad"):
        hidden_grad = rows_out(after(low(pick(d_source, d_start)), self_plane)).astype(jnp.float32)
    g_query, g_key, g_value, g_out = unpack_heads(share_self)
    grad_qkv = jnp.stack([g_query, g_key, g_value], axis=1)
    c_query, c_key, c_value, c_out = unpack_heads(share_cross)
    with jax.named_scope("cross_out"):
        for_enc = cross_out(jnp.concatenate([c_key, c_value], axis=1), 0)
        for_dec = cross_out(jnp.concatenate([c_query, c_out], axis=1), 1)
    cross = jnp.where(core == 0, for_enc, for_dec).astype(jnp.float32)

    return (
        hidden_out,
        hidden_grad,
        grad_qkv[None],
        g_out[None],
        cross[None, :, :width],
        cross[None, :, width:],
        share_first[None],
        share_second[None],
        norm_shares[None, :3],
        norm_shares[None, 3:],
    )


def solution(mesh):
    _, dp_count, _ = mesh.devices.shape
    count = dp_count.bit_length() - 3
    names = axes_of(count)
    dp, tensor = names[1:-2], names[-2:]
    split = Mesh(mesh.devices.reshape((2,) * len(names)), names)
    rows = P("section", None, dp, tensor, None)
    in_specs = (
        rows,
        rows,
        P(None, None, dp, None),
        P("section", dp, None, tensor),
        P("section", dp, tensor),
        P("section", dp, tensor),
        P("section", dp, tensor),
        P("section", dp, tensor),
        P("section", tensor, dp),
        P("section", None, None),
        P("section", None, None),
    )
    out_specs = (
        rows,
        rows,
        P("section", dp, None, tensor),
        P("section", dp, tensor),
        P("section", dp, tensor),
        P("section", dp, tensor),
        P("section", dp, tensor),
        P("section", tensor, dp),
        P("section", None, dp + tensor),
        P("section", None, dp + tensor),
    )
    return jax.shard_map(
        functools.partial(body, count), mesh=split, in_specs=in_specs, out_specs=out_specs, check_vma=False
    )
```

```python
import functools

import jax
import jax.numpy as jnp
from jax import lax
from jax.experimental import pallas as pl
from jax.experimental.pallas import tpu as pltpu
from jax.sharding import Mesh
from jax.sharding import PartitionSpec as P

HDIM = 64
LANES = 128
MASKED = -1e30
NORM_EPS = 1e-05
VMEM_BYTES = 56 * 1024 * 1024

SEG_LANES = 8
PART_LANE = 12

PARTS = 2
TILE_ROWS = 256
HEADS = ((0, 1, 2, 0, 0), (0, 1, 2, 1, 1), (1, 3, 0, 0, 1))


def mul(a, b):
    return jnp.dot(a, b, preferred_element_type=jnp.float32)


def mul_nt(a, b):
    return lax.dot_general(a, b, (((1,), (1,)), ((), ())), preferred_element_type=jnp.float32)


def mul_tn(a, b):
    return lax.dot_general(a, b, (((0,), (0,)), ((), ())), preferred_element_type=jnp.float32)


def tile_of(values, index):
    return values[:, index * LANES : (index + 1) * LANES]


def lane_ids(rows):
    return lax.broadcasted_iota(jnp.int32, (rows, LANES), 1)


def half_mask(rows, half):
    lanes = lane_ids(rows)
    return lanes >= HDIM if half else lanes < HDIM


def in_parts(base, column):
    lanes = lane_ids(base.shape[0])
    high = column.astype(jnp.bfloat16).astype(jnp.float32)
    rest = column - high
    middle = rest.astype(jnp.bfloat16).astype(jnp.float32)
    low = rest - middle
    parts = jnp.where(
        lanes == PART_LANE,
        high,
        jnp.where(lanes == PART_LANE + 1, middle, jnp.where(lanes == PART_LANE + 2, low, base)),
    )
    return parts.astype(jnp.bfloat16)


def with_triangle(scores, tri, at):
    size = tri.shape[1]
    pieces = []
    if at > 0:
        pieces.append(scores[:, : at * size])
    pieces.append(scores[:, at * size : (at + 1) * size] + tri)
    pieces.append(scores[:, (at + 1) * size :])
    return jnp.concatenate(pieces, axis=1)


def places(core, block):
    return [pl.multiple_of((1 - core) * block, block), pl.multiple_of((2 + core) * block, block)]


def assemble(flag_ref, own_refs, peer_refs, w_ref):
    core, block = flag_ref[0], own_refs[0].shape[1] // 2
    for holder, refs in ((core, own_refs), (1 - core, peer_refs)):
        for part, ref in enumerate(refs):
            width = ref.shape[2]
            for at, place in enumerate(places(holder, block)):
                w_ref[pl.ds(place, block), part * width : (part + 1) * width] = ref[0, at * block : (at + 1) * block]


def hand_out(flag_ref, g_ref, keep_ref, send_ref):
    core, block = flag_ref[0], keep_ref.shape[1] // 2
    for holder, ref in ((core, keep_ref), (1 - core, send_ref)):
        for at, place in enumerate(places(holder, block)):
            ref[0, at * block : (at + 1) * block] = g_ref[pl.ds(place, block), :]


def where_active(kernel):
    def guarded(flag_ref, *refs):
        @pl.when(flag_ref[1] == 1)
        def _():
            kernel(flag_ref, *refs)

    return guarded


def scaled_queries(q_ref, at, q_tile, q_half):
    queries = q_ref[0, at, q_tile * LANES : (q_tile + 1) * LANES] * 0.125
    return jnp.where(half_mask(queries.shape[0], q_half), queries, 0).astype(jnp.bfloat16)


def units_of(total, rows):
    return [
        (slice(part * rows, (part + 1) * rows), part, head)
        for part in range(total // rows)
        for head in range(len(HEADS))
    ]


def attend_block(causal, xq_ref, xkv_ref, w_ref, qx_ref, kx_ref, tri_ref, q_ref, kv_ref, c_ref, l_ref):
    q_ref[0] = mul(xq_ref[...], w_ref[:, : 2 * LANES]).astype(jnp.bfloat16)
    kv_ref[0] = mul(xkv_ref[...], w_ref[:, LANES : 5 * LANES]).astype(jnp.bfloat16)
    rows = TILE_ROWS
    low = half_mask(rows, 0)

    def scores_of(at, part, head):
        q_tile, k_tile, _, q_half, _ = HEADS[head]
        keys = kv_ref[0, :, k_tile * LANES : (k_tile + 1) * LANES]
        scores = mul_nt(
            jnp.concatenate([scaled_queries(q_ref, at, q_tile, q_half), qx_ref[at, :]], axis=1),
            jnp.concatenate([keys, kx_ref[...]], axis=1),
        )
        return with_triangle(scores, tri_ref[...], part) if causal else scores

    units = units_of(q_ref.shape[1], rows)
    ahead = scores_of(*units[0])
    contexts, totals = [], None
    for index, (at, part, head) in enumerate(units):
        scores = ahead
        if index + 1 < len(units):
            ahead = scores_of(*units[index + 1])
        v_tile = HEADS[head][2]
        values = kv_ref[0, :, v_tile * LANES : (v_tile + 1) * LANES]
        highest = jnp.max(scores, axis=1, keepdims=True)
        weights = jnp.exp(scores - highest)
        sums = jnp.sum(weights, axis=1, keepdims=True)
        contexts.append(mul(weights.astype(jnp.bfloat16), values) / sums)
        logs = jnp.broadcast_to(highest + jnp.log(sums), (rows, LANES))
        totals = logs if head == 0 else jnp.where(lane_ids(rows) == head, logs, totals)
        if head == len(HEADS) - 1:
            c_ref[0, at, :LANES] = jnp.where(low, 0, contexts[2]).astype(jnp.bfloat16)
            c_ref[0, at, LANES:] = jnp.where(low, contexts[0], contexts[1]).astype(jnp.bfloat16)
            l_ref[0, at, :] = totals
            contexts = []
    return mul_nt(c_ref[0], w_ref[:, 4 * LANES :])


def attend_kernel(causal, flag_ref, xq_ref, xkv_ref, own_ref, peer_ref, qx_ref, kx_ref, tri_ref, o_ref, *refs):
    q_ref, kv_ref, c_ref, l_ref, w_ref = refs
    assemble(flag_ref, [own_ref], [peer_ref], w_ref)
    out = attend_block(causal, xq_ref, xkv_ref, w_ref, qx_ref, kx_ref, tri_ref, q_ref, kv_ref, c_ref, l_ref)
    add_up(pl.program_id(0) == 0, o_ref, out)


def add_up(first, ref, value):
    @pl.when(first)
    def _():
        ref[...] = value

    @pl.when(jnp.logical_not(first))
    def _():
        ref[...] += value


def attend_back_block(causal, do_ref, xq_ref, xkv_ref, w_ref, qx_ref, kx_ref, tri_ref, kept, work):
    q_ref, kv_ref, c_ref, l_ref = kept
    sum_ref, dq_ref, dkv_ref, g_ref = work
    rows = TILE_ROWS
    d_context = mul(do_ref[...], w_ref[:, 4 * LANES :]).astype(jnp.bfloat16)
    low = half_mask(rows, 0)

    def products_of(at, part, head):
        q_tile, k_tile, v_tile, q_half, v_half = HEADS[head]
        c_tile = 0 if head == 2 else 1
        keys = kv_ref[0, :, k_tile * LANES : (k_tile + 1) * LANES]
        values = kv_ref[0, :, v_tile * LANES : (v_tile + 1) * LANES]
        queries = scaled_queries(q_ref, at, q_tile, q_half)
        d_rows = jnp.where(half_mask(rows, v_half), tile_of(d_context[at], c_tile), 0).astype(jnp.bfloat16)
        total = l_ref[0, at, head : head + 1]
        scores = mul_nt(
            jnp.concatenate([queries, in_parts(qx_ref[at, :].astype(jnp.float32), -total)], axis=1),
            jnp.concatenate([keys, kx_ref[...]], axis=1),
        )
        if causal:
            scores = with_triangle(scores, tri_ref[...], part)
        return scores, mul_nt(d_rows, values), queries, d_rows, keys

    units = units_of(q_ref.shape[1], rows)
    ahead = products_of(*units[0])
    d_queries = []
    for index, (at, part, head) in enumerate(units):
        scores, d_probs, queries, d_rows, keys = ahead
        if index + 1 < len(units):
            ahead = products_of(*units[index + 1])
        _, k_tile, v_tile, _, _ = HEADS[head]
        probs = jnp.exp(scores)
        inner = jnp.sum(probs * d_probs, axis=1, keepdims=True)
        d_scores = (probs * (d_probs - inner)).astype(jnp.bfloat16)
        d_values = mul_tn(probs.astype(jnp.bfloat16), d_rows)
        d_keys = mul_tn(d_scores, queries)
        d_queries.append(mul(d_scores, keys) * 0.125)
        k_at = slice(k_tile * LANES, (k_tile + 1) * LANES)
        v_at = slice(v_tile * LANES, (v_tile + 1) * LANES)
        if part == 0 and head != 1:
            sum_ref[:, k_at] = d_keys
            sum_ref[:, v_at] = d_values
        else:
            sum_ref[:, k_at] += d_keys
            sum_ref[:, v_at] += d_values
        if head == len(HEADS) - 1:
            dq_ref[at, :LANES] = jnp.where(low, d_queries[0], d_queries[1]).astype(jnp.bfloat16)
            dq_ref[at, LANES:] = jnp.where(low, d_queries[2], 0).astype(jnp.bfloat16)
            d_queries = []
    dkv_ref[...] = sum_ref[...].astype(jnp.bfloat16)
    d_xq = mul_nt(dq_ref[...], w_ref[:, : 2 * LANES])
    d_xkv = mul_nt(dkv_ref[...], w_ref[:, LANES : 5 * LANES])

    grad_q = mul_tn(xq_ref[...], dq_ref[...])
    grad_kv = mul_tn(xkv_ref[...], dkv_ref[...])
    grad_o = mul_tn(do_ref[...], c_ref[0])
    g_ref[:, :LANES] = grad_q[:, :LANES].astype(jnp.bfloat16)
    g_ref[:, LANES : 2 * LANES] = (grad_q[:, LANES:] + grad_kv[:, :LANES]).astype(jnp.bfloat16)
    g_ref[:, 2 * LANES : 4 * LANES] = grad_kv[:, LANES : 3 * LANES].astype(jnp.bfloat16)
    g_ref[:, 4 * LANES : 5 * LANES] = (grad_kv[:, 3 * LANES :] + grad_o[:, :LANES]).astype(jnp.bfloat16)
    g_ref[:, 5 * LANES :] = grad_o[:, LANES:].astype(jnp.bfloat16)
    return d_xq, d_xkv


def attend_back_kernel(causal, flag_ref, do_ref, xq_ref, xkv_ref, own_ref, peer_ref, *refs):
    kept, (qx_ref, kx_ref, tri_ref, dxq_ref, dxkv_ref, keep_ref, send_ref, w_ref) = refs[:4], refs[4:12]
    work = refs[12:]
    assemble(flag_ref, [own_ref], [peer_ref], w_ref)
    d_xq, d_xkv = attend_back_block(
        causal, do_ref, xq_ref, xkv_ref, w_ref, qx_ref, kx_ref, tri_ref, kept, work
    )
    add_up(pl.program_id(0) == 0, dxq_ref, d_xq)
    add_up(pl.program_id(0) == 0, dxkv_ref, d_xkv)
    hand_out(flag_ref, work[3], keep_ref, send_ref)


def whole(shape):
    return pl.BlockSpec(shape, lambda j, flag: (0,) * len(shape))


def per_block(shape, first=0, gate=1):
    return pl.BlockSpec((1,) + shape, lambda j, flag: (first + j * flag[gate],) + (0,) * len(shape))


shape = jax.ShapeDtypeStruct


def call(kernel, name, micros, moved, grid, in_specs, out_specs, out_shape, scratch, *operands):
    return pl.pallas_call(
        where_active(kernel),
        grid_spec=pltpu.PrefetchScalarGridSpec(
            num_scalar_prefetch=1,
            grid=(grid,),
            in_specs=in_specs,
            out_specs=out_specs,
            scratch_shapes=scratch,
        ),
        out_shape=out_shape,
        compiler_params=pltpu.CompilerParams(vmem_limit_bytes=VMEM_BYTES),
        cost_estimate=cost(micros, moved),
        name=name,
    )(*operands)


def cost(micros, moved):
    return pl.CostEstimate(flops=int(micros * 1.15e9), bytes_accessed=int(moved), transcendentals=0)


def attend(flag, xq, xkv, weights, extras, causal):
    rows, width = xq.shape
    keys = xkv.shape[0]
    blocks = weights[0].shape[0]
    return call(
        functools.partial(attend_kernel, causal),
        "attend_self" if causal else "attend_cross",
        20,
        24 * 2**20,
        blocks,
        [whole((rows, width)), whole((keys, width))]
        + [per_block(part.shape[1:]) for part in weights]
        + [whole(extra.shape) for extra in extras],
        [
            whole((rows, width)),
            per_block((rows, 2 * LANES)),
            per_block((keys, 4 * LANES)),
            per_block((rows, 2 * LANES)),
            per_block((rows, LANES)),
        ],
        [
            shape((rows, width), jnp.float32),
            shape((blocks, rows, 2 * LANES), jnp.bfloat16),
            shape((blocks, keys, 4 * LANES), jnp.bfloat16),
            shape((blocks, rows, 2 * LANES), jnp.bfloat16),
            shape((blocks, rows, LANES), jnp.float32),
        ],
        [pltpu.VMEM((width, 6 * LANES), jnp.bfloat16)],
        flag,
        xq,
        xkv,
        *weights,
        *extras,
    )


def attend_back(flag, d_out, xq, xkv, weights, kept, extras, causal, first, count):
    rows, width = xq.shape
    keys = xkv.shape[0]
    return call(
        functools.partial(attend_back_kernel, causal),
        "attend_self_back" if causal else "attend_cross_back",
        10 * count,
        6 * 2**20 * count,
        count,
        [whole((rows, width)), whole((rows, width)), whole((keys, width))]
        + [per_block(part.shape[1:], first) for part in weights]
        + [
            per_block((rows, 2 * LANES), first),
            per_block((keys, 4 * LANES), first),
            per_block((rows, 2 * LANES), first),
            per_block((rows, LANES), first),
        ]
        + [whole(extra.shape) for extra in extras],
        [whole((rows, width)), whole((keys, width))] + [per_block(part.shape[1:]) for part in weights],
        [shape((rows, width), jnp.float32), shape((keys, width), jnp.float32)]
        + [shape((count,) + part.shape[1:], jnp.bfloat16) for part in weights],
        [
            pltpu.VMEM((width, 6 * LANES), jnp.bfloat16),
            pltpu.VMEM((keys, 4 * LANES), jnp.float32),
            pltpu.VMEM((rows, 2 * LANES), jnp.bfloat16),
            pltpu.VMEM((keys, 4 * LANES), jnp.bfloat16),
            pltpu.VMEM((width, 6 * LANES), jnp.bfloat16),
        ],
        flag,
        d_out,
        xq,
        xkv,
        *weights,
        *kept,
        *extras,
    )


def ffn_block(x_ref, w_ref, units, g_ref, slope_ref):
    inner = mul(x_ref[...], w_ref[:, :units])
    spread = 0.5 * (1.0 + lax.erf(inner * (0.5**0.5)))
    bell = jnp.exp(-0.5 * inner * inner) * 0.3989422804014327
    active = (inner * spread).astype(jnp.bfloat16)
    g_ref[0] = active
    slope_ref[0] = (spread + inner * bell).astype(jnp.bfloat16)
    return mul_nt(active, w_ref[:, units:])


def ffn_kernel(flag_ref, x_ref, *refs):
    own_refs, peer_refs = refs[:PARTS], refs[PARTS : 2 * PARTS]
    z_ref, g_ref, slope_ref, w_ref = refs[2 * PARTS :]
    assemble(flag_ref, own_refs, peer_refs, w_ref)
    out = ffn_block(x_ref, w_ref, own_refs[0].shape[2], g_ref, slope_ref)
    add_up(pl.program_id(0) == 0, z_ref, out)


def ffn(flag, x, weights):
    rows, width = x.shape
    blocks, _, units = weights[0].shape
    return call(
        ffn_kernel,
        "ffn",
        12,
        rows * units * blocks * 16,
        blocks,
        [whole((rows, width))] + [per_block(part.shape[1:]) for part in weights],
        [whole((rows, width)), per_block((rows, units)), per_block((rows, units))],
        [
            shape((rows, width), jnp.float32),
            shape((blocks, rows, units), jnp.bfloat16),
            shape((blocks, rows, units), jnp.bfloat16),
        ],
        [pltpu.VMEM((width, 2 * units), jnp.bfloat16)],
        flag,
        x,
        *weights,
    )


def ffn_back_block(dz_ref, w_ref, units, slope_ref, dh_ref):
    d_active = mul(dz_ref[...], w_ref[:, units:])
    d_inner = (d_active * slope_ref[0].astype(jnp.float32)).astype(jnp.bfloat16)
    dh_ref[0] = d_inner
    return mul_nt(d_inner, w_ref[:, :units])


def ffn_back_kernel(flag_ref, dz_ref, *refs):
    own_refs, peer_refs = refs[:PARTS], refs[PARTS : 2 * PARTS]
    slope_ref, dx_ref, dh_ref, w_ref = refs[2 * PARTS :]
    assemble(flag_ref, own_refs, peer_refs, w_ref)
    out = ffn_back_block(dz_ref, w_ref, own_refs[0].shape[2], slope_ref, dh_ref)
    add_up(pl.program_id(0) == 0, dx_ref, out)


def ffn_back(flag, dz, weights, slope):
    rows, width = dz.shape
    blocks, _, units = weights[0].shape
    return call(
        ffn_back_kernel,
        "ffn_back",
        12,
        rows * units * blocks * 12,
        blocks,
        [whole((rows, width))] + [per_block(part.shape[1:]) for part in weights] + [per_block((rows, units))],
        [whole((rows, width)), per_block((rows, units))],
        [
            shape((rows, width), jnp.float32),
            shape((blocks, rows, units), jnp.bfloat16),
        ],
        [pltpu.VMEM((width, 2 * units), jnp.bfloat16)],
        flag,
        dz,
        *weights,
        slope,
    )


def ffn_grad_kernel(flag_ref, left_ref, enc_ref, dec_ref, keep_ref, send_ref, g_ref):
    right = jnp.where(flag_ref[2] == 1, enc_ref[0], dec_ref[0])
    g_ref[...] = mul_tn(left_ref[...], right).astype(jnp.bfloat16)
    hand_out(flag_ref, g_ref, keep_ref, send_ref)


def ffn_grad(flag, left, enc_right, dec_right, like):
    rows, width = left.shape
    blocks, _, units = enc_right.shape
    return call(
        ffn_grad_kernel,
        "ffn_grad",
        6,
        rows * units * blocks * 8,
        blocks,
        [whole((rows, width)), per_block((rows, units), 0, 2), per_block((rows, units), 0, 3)],
        [per_block(like.shape[1:])] * 2,
        [shape(like.shape, jnp.bfloat16)] * 2,
        [pltpu.VMEM((width, units), jnp.bfloat16)],
        flag,
        left,
        enc_right,
        dec_right,
    )


def layer_norm(values, gain_row, bias_row):
    average = jnp.mean(values, axis=-1, keepdims=True)
    centered = values - average
    variance = jnp.mean(centered * centered, axis=-1, keepdims=True)
    return centered * lax.rsqrt(variance + NORM_EPS) * gain_row + bias_row


def norm_back(values, gain_row, bias_row, upstream):
    _, pullback = jax.vjp(layer_norm, values, gain_row, bias_row)
    return pullback(upstream)


def norm_parts(values):
    average = jnp.mean(values, axis=1, keepdims=True)
    centered = values - average
    scale = lax.rsqrt(jnp.mean(centered * centered, axis=1, keepdims=True) + NORM_EPS)
    return centered * scale, scale


def norm_gradients(values, gain_row, upstream):
    shaped, scale = norm_parts(values)
    inner = upstream * gain_row
    mean_inner = jnp.mean(inner, axis=1, keepdims=True)
    mean_product = jnp.mean(inner * shaped, axis=1, keepdims=True)
    d_values = scale * (inner - mean_inner - shaped * mean_product)
    d_gain = jnp.sum(upstream * shaped, axis=0, keepdims=True)
    return d_values, d_gain, jnp.sum(upstream, axis=0, keepdims=True)


def decoder_kernel(
    flag_ref,
    h1_ref,
    mem_ref,
    peer_mem_ref,
    cot_ref,
    qx_ref,
    kx_ref,
    norms_ref,
    own_ref,
    peer_ref,
    first_own_ref,
    second_own_ref,
    first_peer_ref,
    second_peer_ref,
    decoded_ref,
    crossed_ref,
    d_dec_ref,
    d_middle_ref,
    mine_ref,
    other_ref,
    sums_ref,
    active_ref,
    inner_ref,
    keep_ref,
    send_ref,
    xq_ref,
    xkv_ref,
    wx_ref,
    wf_ref,
    q_ref,
    kv_ref,
    c_ref,
    l_ref,
    slope_ref,
    out_ref,
    total_ref,
    crossed_full_ref,
    upstream_ref,
    do_ref,
    dxkv_ref,
    *work,
):
    step = pl.program_id(0)
    phase, at = step // 4, step % 4
    first, last = at == 0, at == 3
    rows = h1_ref.shape[0]
    units = first_own_ref.shape[2]
    gain = [norms_ref[row : row + 1, :] for row in range(3)]
    bias = [norms_ref[3 + row : 4 + row, :] for row in range(3)]

    def kept(block):
        return tuple(ref.at[pl.ds(block, 1)] for ref in (q_ref, kv_ref, c_ref, l_ref))

    @pl.when(step == 0)
    def _():
        xq_ref[...] = h1_ref[...].astype(jnp.bfloat16)
        xkv_ref[:rows] = mem_ref[...]
        xkv_ref[rows:] = peer_mem_ref[...]

    @pl.when(jnp.logical_or(phase == 0, phase == 3))
    def _():
        assemble(flag_ref, [own_ref], [peer_ref], wx_ref)

    @pl.when(jnp.logical_or(phase == 1, phase == 2))
    def _():
        assemble(flag_ref, [first_own_ref, second_own_ref], [first_peer_ref, second_peer_ref], wf_ref)

    @pl.when(phase == 0)
    def _():
        add_up(first, out_ref, attend_block(False, xq_ref, xkv_ref, wx_ref, qx_ref, kx_ref, None, *kept(at)))

    @pl.when(jnp.logical_and(phase == 0, last))
    def _():
        total = h1_ref[...] + out_ref[...]
        total_ref[...] = total
        crossed = norm_parts(total)[0] * gain[1] + bias[1]
        crossed_full_ref[...] = crossed
        crossed_ref[...] = crossed.astype(jnp.bfloat16)

    @pl.when(phase == 1)
    def _():
        add_up(first, out_ref, ffn_block(crossed_ref, wf_ref, units, active_ref, slope_ref.at[pl.ds(at, 1)]))

    @pl.when(jnp.logical_and(phase == 1, last))
    def _():
        total = crossed_full_ref[...] + out_ref[...]
        decoded_ref[...] = (norm_parts(total)[0] * gain[2] + bias[2]).astype(jnp.bfloat16)
        d_total, sums_ref[0:1, :], sums_ref[1:2, :] = norm_gradients(
            total, gain[2], cot_ref[...].astype(jnp.float32)
        )
        upstream_ref[...] = d_total
        d_dec_ref[...] = d_total.astype(jnp.bfloat16)

    @pl.when(phase == 2)
    def _():
        add_up(first, out_ref, ffn_back_block(d_dec_ref, wf_ref, units, slope_ref.at[pl.ds(3 - at, 1)], inner_ref))

    @pl.when(jnp.logical_and(phase == 2, last))
    def _():
        d_total, sums_ref[2:3, :], sums_ref[3:4, :] = norm_gradients(
            total_ref[...], gain[1], upstream_ref[...] + out_ref[...]
        )
        upstream_ref[...] = d_total
        do_ref[...] = d_total.astype(jnp.bfloat16)

    @pl.when(phase == 3)
    def _():
        d_xq, d_xkv = attend_back_block(
            False, do_ref, xq_ref, xkv_ref, wx_ref, qx_ref, kx_ref, None, kept(3 - at), work
        )
        add_up(first, out_ref, d_xq)
        add_up(first, dxkv_ref, d_xkv)
        hand_out(flag_ref, work[3], keep_ref, send_ref)

    @pl.when(jnp.logical_and(phase == 3, last))
    def _():
        d_middle_ref[...] = upstream_ref[...] + out_ref[...]
        mine_ref[...] = dxkv_ref[:rows]
        other_ref[...] = dxkv_ref[rows:].astype(jnp.bfloat16)


def decoder(flag, h1, mem, peer_mem, cot, extras, norms, cross, feed):
    rows, width = h1.shape
    blocks, half, _ = cross[0].shape
    units = feed[0].shape[2]
    keys = 2 * rows
    qx, kx = extras

    def at_step(of, in_phase):
        def index(j, flag):
            at = j % 4
            choice = [{"up": at, "down": 3 - at}.get(way, way) for way in in_phase]
            chosen = choice[3]
            for phase in (2, 1, 0):
                chosen = jnp.where(j // 4 == phase, choice[phase], chosen)
            return (chosen * flag[1],) + (0,) * len(of)

        return pl.BlockSpec((1,) + of, index)

    part = (half, cross[0].shape[2])
    full = shape((rows, width), jnp.float32)
    rounded = shape((rows, width), jnp.bfloat16)
    return call(
        decoder_kernel,
        "decoder",
        90,
        40 * 2**20,
        16,
        [whole(item.shape) for item in (h1, mem, peer_mem, cot, qx, kx, norms)]
        + [at_step(part, ("up", 3, 3, "down"))] * 2
        + [at_step((half, units), (0, "up", "down", 0))] * 4,
        [whole((rows, width))] * 6
        + [whole((8, width))]
        + [
            at_step((rows, units), (0, "up", 3, 3)),
            at_step((rows, units), (3, 3, "down", 0)),
            at_step(part, (3, 3, 3, "down")),
            at_step(part, (3, 3, 3, "down")),
        ],
        [rounded, rounded, rounded, full, full, rounded, shape((8, width), jnp.float32)]
        + [shape((blocks, rows, units), jnp.bfloat16)] * 2
        + [shape(cross[0].shape, jnp.bfloat16)] * 2,
        [
            pltpu.VMEM((rows, width), jnp.bfloat16),
            pltpu.VMEM((keys, width), jnp.bfloat16),
            pltpu.VMEM((width, 6 * LANES), jnp.bfloat16),
            pltpu.VMEM((width, 2 * units), jnp.bfloat16),
            pltpu.VMEM((blocks, rows, 2 * LANES), jnp.bfloat16),
            pltpu.VMEM((blocks, keys, 4 * LANES), jnp.bfloat16),
            pltpu.VMEM((blocks, rows, 2 * LANES), jnp.bfloat16),
            pltpu.VMEM((blocks, rows, LANES), jnp.float32),
            pltpu.VMEM((blocks, rows, units), jnp.bfloat16),
            pltpu.VMEM((rows, width), jnp.float32),
            pltpu.VMEM((rows, width), jnp.float32),
            pltpu.VMEM((rows, width), jnp.float32),
            pltpu.VMEM((rows, width), jnp.float32),
            pltpu.VMEM((rows, width), jnp.bfloat16),
            pltpu.VMEM((keys, width), jnp.float32),
            pltpu.VMEM((keys, 4 * LANES), jnp.float32),
            pltpu.VMEM((rows, 2 * LANES), jnp.bfloat16),
            pltpu.VMEM((keys, 4 * LANES), jnp.bfloat16),
            pltpu.VMEM((width, 6 * LANES), jnp.bfloat16),
        ],
        flag,
        h1,
        mem,
        peer_mem,
        cot,
        qx,
        kx,
        norms,
        *cross,
        *feed,
    )


def low(values):
    return values.astype(jnp.bfloat16)


def axes_of(count):
    return ("section", "zh", "zl") + tuple("e%d" % at for at in range(count)) + ("ty", "tx")


def layer_of(place):
    return 1 ^ place["zh"] ^ place["zl"]


def moved(x, names, to):
    names = [name for name in axes_of(8) if name in names]

    def index(place):
        return sum(place[name] << (len(names) - 1 - at) for at, name in enumerate(names))

    pairs = []
    for source in range(2 ** len(names)):
        place = {name: source >> (len(names) - 1 - at) & 1 for at, name in enumerate(names)}
        target = to(place)
        if target is not None:
            pairs.append((source, index(target)))
    return lax.ppermute(x, tuple(names), pairs)


def over(x, *axes, layer=None):
    def to(place):
        if layer is not None and layer_of(place) != layer:
            return None
        return {**place, **{axis: 1 - place[axis] for axis in axes}}

    return moved(x, axes if layer is None else axes + Z, to)


Z = ("zh", "zl")


def swapped(x):
    def to(place):
        if place["section"] == layer_of(place):
            return place
        return {"section": 1 - place["section"], "zh": place["zh"], "zl": 1 - place["zl"]}

    return moved(x, ("section",) + Z, to)


def turned(x):
    return moved(x, ("section", "ty"), lambda place: {"section": place["ty"], "ty": place["section"]})


def sent_home(x, other):
    def to(place):
        return {
            "section": layer_of(place),
            "zh": place["zh"],
            "zl": 1 ^ place["zh"] ^ place["ty"],
            "ty": place["section"],
            "tx": place["tx"] ^ other,
        }

    return moved(x, ("section",) + Z + ("ty", "tx"), to)


def cross_in(x, layer):
    def to(place):
        if place["section"] != layer:
            return None
        return {"section": layer_of(place), "zh": place["zh"], "zl": place["zh"]}

    return moved(x, ("section",) + Z, to)


def cross_out(x, layer):
    def to(place):
        if layer_of(place) != 1:
            return None
        return {"section": layer, "zh": place["zh"], "zl": 1 ^ place["zh"] ^ place["section"]}

    return moved(x, ("section",) + Z, to)


def in_order(x, flag, axis):
    return jnp.where(flag == 1, jnp.flip(x, axis), x)


def pack_heads(query, key, value, out):
    pair = 2 * HDIM
    return jnp.concatenate(
        [
            query,
            value[:, pair:],
            key[:, :pair],
            value[:, :pair],
            key[:, pair:],
            out[:, pair:],
            out[:, :pair],
        ],
        axis=1,
    )


def unpack_heads(packed):
    part = [packed[:, at * HDIM : (at + 1) * HDIM] for at in range(12)]
    query = jnp.concatenate(part[0:3], axis=1)
    key = jnp.concatenate([part[4], part[5], part[8]], axis=1)
    value = jnp.concatenate([part[6], part[7], part[3]], axis=1)
    out = jnp.concatenate([part[10], part[11], part[9]], axis=1)
    return query, key, value, out


def after(x, *earlier):
    return lax.optimization_barrier((x,) + earlier)[0]


def plane_gathered(x, until=(), **only):
    parts = [x, over(x, "tx", **only), over(x, "ty", **only), over(x, "ty", "tx", **only)]
    return jnp.stack([after(part, *until) for part in parts])


def plane_summed(x, until=(), **only):
    terms = [x[0], over(x[1], "tx", **only), over(x[2], "ty", **only), over(x[3], "ty", "tx", **only)]
    terms = [after(term, *until) for term in terms]
    return low(sum(term.astype(jnp.float32) for term in terms))


def rows_gathered(x, count, until=(), **only):
    for axes in [("e%d" % at,) for at in reversed(range(count))] + [Z]:
        parts = [after(part, *until) for part in (x, over(x, *axes, **only))]
        both = in_order(jnp.stack(parts, axis=-3), lax.axis_index(axes[0]), x.ndim - 2)
        x = both.reshape(x.shape[:-2] + (2 * x.shape[-2], x.shape[-1]))
    return x


def rows_summed(x, count, until=(), **only):
    for axes in [Z] + [("e%d" % at,) for at in range(count)]:
        halves = x.reshape(x.shape[:-2] + (2, x.shape[-2] // 2, x.shape[-1]))
        halves = in_order(halves, lax.axis_index(axes[0]), x.ndim - 2)
        x = plus(halves[..., 0, :, :], after(over(halves[..., 1, :, :], *axes, **only), *until))
    return x


def plus(first, second):
    return low(first.astype(jnp.float32) + second.astype(jnp.float32))


def from_cores(keep, send, **only):
    return plus(keep, over(send, "section", **only))


def body(
    count,
    hidden,
    cotangent,
    segments,
    sa_qkv,
    sa_out,
    cross_one,
    cross_two,
    ffn_in,
    ffn_out,
    norm_gain,
    norm_bias,
):
    core = lax.axis_index("section")
    x_at, y_at, zh_at, zl_at = (lax.axis_index(name) for name in ("tx", "ty", "zh", "zl"))
    layer = 1 ^ zh_at ^ zl_at
    on_encoder = layer == 0
    quarter = hidden.shape[3]
    enc_flag = jnp.stack([core, 1 - layer, 1 - layer, layer])
    dec_flag = jnp.stack([core, layer, 1 - layer, layer])
    flag = jnp.stack([core, jnp.ones_like(core), 1 - layer, layer])

    def pick(first, second):
        return jnp.where(on_encoder, first, second)

    def of_one_row(x):
        both = in_order(x[0, :, 0], x_at, 0)
        return in_order(jnp.stack([both[0], over(both[1], "tx")]), x_at, 0).reshape(2 * quarter, -1)

    def rows_out(x, *until):
        mine, other = in_order(x.reshape(2, quarter, -1), x_at, 0)
        both = [after(sent_home(mine, 0), *until), after(sent_home(other, 1), *until)]
        return in_order(jnp.stack(both), x_at, 0)[None, :, None]

    units = ffn_in.shape[2]
    width = cross_one.shape[2]
    packed_self = pack_heads(sa_qkv[0, :, 0], sa_qkv[0, :, 1], sa_qkv[0, :, 2], sa_out[0])
    packed_ffn = jnp.concatenate([ffn_in[0], ffn_out[0].T], axis=1)
    with jax.named_scope("norms_in"):
        norms = swapped(jnp.concatenate([norm_gain[0], norm_bias[0]], axis=0))
        gains, biases = norms[:3], norms[3:]
        seg_own = segments[:, :, 0].astype(jnp.float32)
        seg_here = jnp.where(zl_at == 1 ^ zh_at ^ y_at, seg_own, over(seg_own, "zl")).astype(jnp.int32)
    with jax.named_scope("hidden_in"):
        one_row = of_one_row(hidden)
    with jax.named_scope("self_weights"):
        shard_self = swapped(packed_self)
    with jax.named_scope("hidden_in"):
        one_row = swapped(after(one_row, shard_self))
    with jax.named_scope("ffn_weights"):
        shard_ffn = swapped(after(packed_ffn, one_row))
        shard_first, shard_second = shard_ffn[:, :units], shard_ffn[:, units:]

    def both_rows(x):
        for_enc = rows_gathered(x, count, layer=0)
        return pick(for_enc, rows_gathered(after(x, for_enc), count, layer=1))

    with jax.named_scope("self_weights"):
        rows_self = both_rows(shard_self)
        own_self = plane_gathered(rows_self)
        w_self = [own_self, over(own_self, "section")]
    with jax.named_scope("hidden_in"):
        rows_here = turned(one_row)
        rows_all = jnp.concatenate([rows_here, over(rows_here, "section")], axis=0)
    with jax.named_scope("cross_weights"):
        cross_low = after(jnp.concatenate([cross_one[0], cross_two[0]], axis=1), own_self)
        pair_kv, pair_qo = cross_in(cross_low, 0), cross_in(cross_low, 1)
        packed = pack_heads(pair_qo[:, :width], pair_kv[:, :width], pair_kv[:, width:], pair_qo[:, width:])
    with jax.named_scope("ffn_weights"):
        rows_first = both_rows(after(shard_first, rows_self))
        plane_second = plane_gathered(after(shard_second, own_self))

    both_segments = in_order(seg_here, x_at, 1)[:, 0]
    ordered = in_order(both_segments.reshape(2, 2, 2 * quarter), core, 1).reshape(2, 4 * quarter)
    source_seg, target_seg = ordered[0], ordered[1]
    self_seg = pick(source_seg, target_seg)
    parts = jnp.arange(4)
    quarter_of = jnp.repeat(2 * ((parts // 2) ^ core) + parts % 2, quarter)
    lanes = jnp.arange(LANES)[None, :]

    def key_extras(seg):
        differs = jnp.logical_and(lanes < SEG_LANES, seg[:, None] != lanes)
        later = jnp.logical_and(
            jnp.logical_and(lanes >= SEG_LANES, lanes < PART_LANE),
            quarter_of[:, None] > lanes - SEG_LANES,
        )
        part = jnp.logical_and(lanes >= PART_LANE, lanes < PART_LANE + 3)
        return jnp.where(differs | later | part, 1.0, 0.0).astype(jnp.bfloat16)

    def query_extras(seg, causal):
        seg, at = seg[: 2 * quarter], quarter_of[: 2 * quarter]
        same = seg[:, None] == lanes
        here = jnp.logical_and(at[:, None] + SEG_LANES == lanes, causal)
        return jnp.where(same | here, MASKED, 0.0).astype(jnp.bfloat16)

    at_row = jnp.arange(quarter)
    later_key = jnp.logical_and(at_row[None, :] > at_row[:, None], jnp.logical_not(on_encoder))
    tri = jnp.where(later_key, MASKED, 0.0).astype(jnp.float32)
    self_extras = (query_extras(self_seg, jnp.logical_not(on_encoder)), key_extras(self_seg), tri)
    cross_extras = (query_extras(target_seg, False), key_extras(source_seg), tri)

    start = rows_all.astype(jnp.float32)
    start = pick(layer_norm(start, gains[0], biases[0]), start)
    start_here = start[: 2 * quarter]
    start_low = low(start)
    self_gain, self_bias = pick(gains[1], gains[0]), pick(biases[1], biases[0])
    self_out, *kept_self = attend(
        flag, start_low[: 2 * quarter], after(start_low, plane_second), w_self, self_extras, True
    )
    with jax.named_scope("ffn_weights"):
        own_first = plane_gathered(after(rows_first, plane_second), until=(self_out,))
        enc_second = rows_gathered(plane_second, count, until=(self_out,), layer=0)
        peer_first = over(own_first, "section")
        w_enc = [own_first, enc_second, peer_first, over(enc_second, "section", layer=0)]
    with jax.named_scope("cotangent_in"):
        cot = turned(swapped(of_one_row(after(cotangent, self_out))))
    self_total = start_here + self_out
    middle = layer_norm(self_total, self_gain, self_bias)
    middle_low = low(middle)

    with jax.named_scope("cross_weights"):
        rows_cross = rows_gathered(after(packed, plane_second), count, until=(self_out,), layer=1)
        own_cross = plane_gathered(rows_cross, layer=1)
        w_cross = [own_cross, over(own_cross, "section", layer=1)]

    enc_out, enc_active, enc_slope = ffn(enc_flag, after(middle_low, cot), w_enc)
    enc_total = middle + enc_out
    encoded = low(layer_norm(enc_total, gains[2], biases[2]))
    with jax.named_scope("ffn_weights"):
        dec_second = rows_gathered(after(plane_second, self_out), count, until=(encoded,), layer=1)
        w_dec = [own_first, dec_second, peer_first, over(dec_second, "section", layer=1)]

    def across(x, layer):
        return moved(x, Z, lambda place: {**place, "zl": 1 - place["zl"]} if layer_of(place) == layer else None)

    with jax.named_scope("memory"):
        memory_here = across(encoded, 0)
        memory_peer = over(memory_here, "section", layer=1)

    (
        decoded,
        crossed_low,
        d_dec_low,
        d_middle_dec,
        d_memory_here,
        d_memory_other,
        dec_sums,
        dec_active,
        dec_inner,
        cross_keep,
        cross_send,
    ) = decoder(
        dec_flag, middle, memory_here, memory_peer, cot, cross_extras[:2], norms, w_cross, w_dec
    )
    with jax.named_scope("d_memory"):
        d_memory_here = d_memory_here + over(d_memory_other, "section", layer=1).astype(jnp.float32)
        d_memory_low = low(d_memory_here)
        arrived = across(d_memory_low, 1)
        d_encoded = arrived.astype(jnp.float32) + cot.astype(jnp.float32)
    with jax.named_scope("hidden_out"):
        hidden_out = rows_out(after(pick(encoded, decoded), arrived))
    with jax.named_scope("cross_sums"):
        cross_sum = from_cores(after(cross_keep, d_memory_low), after(cross_send, d_memory_low), layer=1)

    d_enc_total, enc_gain_c, enc_bias_c = norm_back(enc_total, gains[2], biases[2], d_encoded)
    d_enc_low = low(d_enc_total)
    second_keep, second_send = ffn_grad(
        flag, pick(d_enc_low, d_dec_low), enc_active, dec_active, own_first
    )
    with jax.named_scope("ffn_sums"):
        second_sum = from_cores(second_keep, second_send)
    with jax.named_scope("cross_sums"):
        cross_plane = plane_summed(cross_sum, until=(second_sum,), layer=1)
    d_enc_middle, enc_inner = ffn_back(enc_flag, after(d_enc_low, second_keep, hidden_out), w_enc, enc_slope)
    with jax.named_scope("ffn_sums"):
        second_plane = plane_summed(second_sum)
    first_keep, first_send = ffn_grad(
        flag, after(pick(middle_low, crossed_low), second_sum), enc_inner, dec_inner, own_first
    )
    with jax.named_scope("ffn_sums"):
        first_sum = from_cores(first_keep, first_send)

    d_middle = pick(d_enc_total + d_enc_middle, d_middle_dec)
    d_self_total, gain_s, bias_s = norm_back(self_total, self_gain, self_bias, d_middle)
    halves = []
    for first, earlier in ((0, (first_keep,)), (2, (first_sum, second_plane))):
        halves.append(
            attend_back(
                flag,
                after(low(d_self_total), *earlier),
                start_low[: 2 * quarter],
                start_low,
                w_self,
                kept_self,
                self_extras,
                True,
                first,
                2,
            )
        )
    d_start_q = halves[0][0] + halves[1][0]
    with jax.named_scope("cross_sums"):
        share_cross = rows_summed(after(cross_plane, d_start_q), count, layer=1)
    with jax.named_scope("ffn_sums"):
        first_plane = plane_summed(after(first_sum, second_plane), until=(halves[1][0],))
        second_share = rows_summed(second_plane, count, until=(halves[1][0],))
    with jax.named_scope("self_sums"):
        self_sum = jnp.concatenate([from_cores(keep, send) for _, _, keep, send in halves], axis=0)
    with jax.named_scope("d_start"):
        d_start_kv = after(halves[0][1], first_plane, second_share) + halves[1][1]
        d_start = d_self_total + d_start_q + d_start_kv[: 2 * quarter]
        d_start = d_start + over(low(d_start_kv[2 * quarter :]), "section").astype(jnp.float32)
    d_source, gain_a, bias_a = norm_back(
        rows_here.astype(jnp.float32), gains[0], biases[0], d_start
    )

    norm_sums = jnp.stack(
        [
            pick(gain_a, gain_s),
            pick(gain_s, dec_sums[2]),
            pick(enc_gain_c, dec_sums[0]),
            pick(bias_a, bias_s),
            pick(bias_s, dec_sums[3]),
            pick(enc_bias_c, dec_sums[1]),
        ]
    )
    shards = 2**count
    sides = jnp.arange(2)
    held, outer = core ^ sides[:, None], sides[None, :]
    row_block = ((2 * outer + (1 ^ outer ^ held)) * shards)[:, :, None] + jnp.arange(shards)
    column_block = (2 * (y_at ^ sides)[:, None] + (x_at ^ sides)[None, :]).reshape(-1)
    order = (row_block.reshape(2, -1)[:, None, :] + 0) * 4 + column_block[:, None]
    norm_sums = jnp.take(norm_sums.reshape(6, 8 * 2 * shards, -1), order.reshape(-1), axis=1)
    norm_sums = norm_sums.reshape(6, 2, 4, 2 * shards, -1)
    with jax.named_scope("norm_sums"):
        norm_sums = norm_sums[:, 0] + over(norm_sums[:, 1], "section")
    with jax.named_scope("self_sums"):
        self_plane = plane_summed(self_sum)
    with jax.named_scope("norm_sums"):
        norm_blocks = after(norm_sums.transpose(1, 2, 0, 3).reshape(4, 2 * shards, -1), self_plane)
        norm_plane = norm_blocks[0] + over(norm_blocks[1], "tx") + over(norm_blocks[2], "ty")
        norm_plane = norm_plane + over(norm_blocks[3], "ty", "tx")
    norm_width = norm_plane.shape[1]
    with jax.named_scope("self_sums"):
        pad = ((0, 0), (0, 15), (0, self_plane.shape[1] - norm_width))
        both = jnp.concatenate(
            [
                self_plane.reshape(2 * shards, -1, self_plane.shape[1]),
                jnp.pad(low(norm_plane)[:, None], pad),
            ],
            axis=1,
        )
        share_self = swapped(rows_summed(both.reshape(-1, self_plane.shape[1]), count)).astype(jnp.float32)
    norm_shares = share_self[-16, :norm_width].reshape(6, -1)
    share_self = share_self[:-16]
    with jax.named_scope("ffn_sums"):
        first_share = rows_summed(first_plane, count, until=(self_sum,))
        share_ffn = swapped(jnp.concatenate([first_share, second_share], axis=1)).astype(jnp.float32)
    share_first, share_second = share_ffn[:, :units], share_ffn[:, units:].T
    with jax.named_scope("hidden_grad"):
        hidden_grad = rows_out(after(low(pick(d_source, d_start)), self_plane)).astype(jnp.float32)
    g_query, g_key, g_value, g_out = unpack_heads(share_self)
    grad_qkv = jnp.stack([g_query, g_key, g_value], axis=1)
    c_query, c_key, c_value, c_out = unpack_heads(share_cross)
    with jax.named_scope("cross_out"):
        for_enc = cross_out(jnp.concatenate([c_key, c_value], axis=1), 0)
        for_dec = cross_out(jnp.concatenate([c_query, c_out], axis=1), 1)
    cross = jnp.where(core == 0, for_enc, for_dec).astype(jnp.float32)

    return (
        hidden_out,
        hidden_grad,
        grad_qkv[None],
        g_out[None],
        cross[None, :, :width],
        cross[None, :, width:],
        share_first[None],
        share_second[None],
        norm_shares[None, :3],
        norm_shares[None, 3:],
    )


def solution(mesh):
    _, dp_count, _ = mesh.devices.shape
    count = dp_count.bit_length() - 3
    names = axes_of(count)
    dp, tensor = names[1:-2], names[-2:]
    split = Mesh(mesh.devices.reshape((2,) * len(names)), names)
    rows = P("section", None, dp, tensor, None)
    in_specs = (
        rows,
        rows,
        P(None, None, dp, None),
        P("section", dp, None, tensor),
        P("section", dp, tensor),
        P("section", dp, tensor),
        P("section", dp, tensor),
        P("section", dp, tensor),
        P("section", tensor, dp),
        P("section", None, None),
        P("section", None, None),
    )
    out_specs = (
        rows,
        rows,
        P("section", dp, None, tensor),
        P("section", dp, tensor),
        P("section", dp, tensor),
        P("section", dp, tensor),
        P("section", dp, tensor),
        P("section", tensor, dp),
        P("section", None, dp + tensor),
        P("section", None, dp + tensor),
    )
    return jax.shard_map(
        functools.partial(body, count), mesh=split, in_specs=in_specs, out_specs=out_specs, check_vma=False
    )
```

```python
import functools

import jax
import jax.numpy as jnp
from jax import lax
from jax.experimental import pallas as pl
from jax.experimental.pallas import tpu as pltpu
from jax.sharding import Mesh
from jax.sharding import PartitionSpec as P

HDIM = 64
LANES = 128
MASKED = -1e30
NORM_EPS = 1e-05
VMEM_BYTES = 56 * 1024 * 1024

SEG_LANES = 8
PART_LANE = 12

PARTS = 2
TILE_ROWS = 256
HEADS = ((0, 1, 2, 0, 0), (0, 1, 2, 1, 1), (1, 3, 0, 0, 1))


def mul(a, b):
    return jnp.dot(a, b, preferred_element_type=jnp.float32)


def mul_nt(a, b):
    return lax.dot_general(a, b, (((1,), (1,)), ((), ())), preferred_element_type=jnp.float32)


def mul_tn(a, b):
    return lax.dot_general(a, b, (((0,), (0,)), ((), ())), preferred_element_type=jnp.float32)


def tile_of(values, index):
    return values[:, index * LANES : (index + 1) * LANES]


def lane_ids(rows):
    return lax.broadcasted_iota(jnp.int32, (rows, LANES), 1)


def half_mask(rows, half):
    lanes = lane_ids(rows)
    return lanes >= HDIM if half else lanes < HDIM


def in_parts(base, column):
    lanes = lane_ids(base.shape[0])
    high = column.astype(jnp.bfloat16).astype(jnp.float32)
    rest = column - high
    middle = rest.astype(jnp.bfloat16).astype(jnp.float32)
    low = rest - middle
    parts = jnp.where(
        lanes == PART_LANE,
        high,
        jnp.where(lanes == PART_LANE + 1, middle, jnp.where(lanes == PART_LANE + 2, low, base)),
    )
    return parts.astype(jnp.bfloat16)


def with_triangle(scores, tri, at):
    size = tri.shape[1]
    pieces = []
    if at > 0:
        pieces.append(scores[:, : at * size])
    pieces.append(scores[:, at * size : (at + 1) * size] + tri)
    pieces.append(scores[:, (at + 1) * size :])
    return jnp.concatenate(pieces, axis=1)


def places(core, block):
    return [pl.multiple_of((1 - core) * block, block), pl.multiple_of((2 + core) * block, block)]


def assemble(flag_ref, own_refs, peer_refs, w_ref):
    core, block = flag_ref[0], own_refs[0].shape[1] // 2
    for holder, refs in ((core, own_refs), (1 - core, peer_refs)):
        for part, ref in enumerate(refs):
            width = ref.shape[2]
            for at, place in enumerate(places(holder, block)):
                w_ref[pl.ds(place, block), part * width : (part + 1) * width] = ref[0, at * block : (at + 1) * block]


def hand_out(flag_ref, g_ref, keep_ref, send_ref):
    core, block = flag_ref[0], keep_ref.shape[1] // 2
    for holder, ref in ((core, keep_ref), (1 - core, send_ref)):
        for at, place in enumerate(places(holder, block)):
            ref[0, at * block : (at + 1) * block] = g_ref[pl.ds(place, block), :]


def where_active(kernel):
    def guarded(flag_ref, *refs):
        @pl.when(flag_ref[1] == 1)
        def _():
            kernel(flag_ref, *refs)

    return guarded


def scaled_queries(q_ref, at, q_tile, q_half):
    queries = q_ref[0, at, q_tile * LANES : (q_tile + 1) * LANES] * 0.125
    return jnp.where(half_mask(queries.shape[0], q_half), queries, 0).astype(jnp.bfloat16)


def units_of(total, rows):
    return [
        (slice(part * rows, (part + 1) * rows), part, head)
        for part in range(total // rows)
        for head in range(len(HEADS))
    ]


def attend_block(causal, xq_ref, xkv_ref, w_ref, qx_ref, kx_ref, tri_ref, q_ref, kv_ref, c_ref, l_ref):
    q_ref[0] = mul(xq_ref[...], w_ref[:, : 2 * LANES]).astype(jnp.bfloat16)
    kv_ref[0] = mul(xkv_ref[...], w_ref[:, LANES : 5 * LANES]).astype(jnp.bfloat16)
    rows = TILE_ROWS
    low = half_mask(rows, 0)

    def scores_of(at, part, head):
        q_tile, k_tile, _, q_half, _ = HEADS[head]
        keys = kv_ref[0, :, k_tile * LANES : (k_tile + 1) * LANES]
        scores = mul_nt(
            jnp.concatenate([scaled_queries(q_ref, at, q_tile, q_half), qx_ref[at, :]], axis=1),
            jnp.concatenate([keys, kx_ref[...]], axis=1),
        )
        return with_triangle(scores, tri_ref[...], part) if causal else scores

    units = units_of(q_ref.shape[1], rows)
    ahead = scores_of(*units[0])
    contexts, totals = [], None
    for index, (at, part, head) in enumerate(units):
        scores = ahead
        if index + 1 < len(units):
            ahead = scores_of(*units[index + 1])
        v_tile = HEADS[head][2]
        values = kv_ref[0, :, v_tile * LANES : (v_tile + 1) * LANES]
        highest = jnp.max(scores, axis=1, keepdims=True)
        weights = jnp.exp(scores - highest)
        sums = jnp.sum(weights, axis=1, keepdims=True)
        contexts.append(mul(weights.astype(jnp.bfloat16), values) / sums)
        logs = jnp.broadcast_to(highest + jnp.log(sums), (rows, LANES))
        totals = logs if head == 0 else jnp.where(lane_ids(rows) == head, logs, totals)
        if head == len(HEADS) - 1:
            c_ref[0, at, :LANES] = jnp.where(low, 0, contexts[2]).astype(jnp.bfloat16)
            c_ref[0, at, LANES:] = jnp.where(low, contexts[0], contexts[1]).astype(jnp.bfloat16)
            l_ref[0, at, :] = totals
            contexts = []
    return mul_nt(c_ref[0], w_ref[:, 4 * LANES :])


def attend_kernel(causal, flag_ref, xq_ref, xkv_ref, own_ref, peer_ref, qx_ref, kx_ref, tri_ref, o_ref, *refs):
    q_ref, kv_ref, c_ref, l_ref, w_ref = refs
    assemble(flag_ref, [own_ref], [peer_ref], w_ref)
    out = attend_block(causal, xq_ref, xkv_ref, w_ref, qx_ref, kx_ref, tri_ref, q_ref, kv_ref, c_ref, l_ref)
    add_up(pl.program_id(0) == 0, o_ref, out)


def add_up(first, ref, value):
    @pl.when(first)
    def _():
        ref[...] = value

    @pl.when(jnp.logical_not(first))
    def _():
        ref[...] += value


def attend_back_block(causal, do_ref, xq_ref, xkv_ref, w_ref, qx_ref, kx_ref, tri_ref, kept, work):
    q_ref, kv_ref, c_ref, l_ref = kept
    sum_ref, dq_ref, dkv_ref, g_ref = work
    rows = TILE_ROWS
    d_context = mul(do_ref[...], w_ref[:, 4 * LANES :]).astype(jnp.bfloat16)
    low = half_mask(rows, 0)

    def products_of(at, part, head):
        q_tile, k_tile, v_tile, q_half, v_half = HEADS[head]
        c_tile = 0 if head == 2 else 1
        keys = kv_ref[0, :, k_tile * LANES : (k_tile + 1) * LANES]
        values = kv_ref[0, :, v_tile * LANES : (v_tile + 1) * LANES]
        queries = scaled_queries(q_ref, at, q_tile, q_half)
        d_rows = jnp.where(half_mask(rows, v_half), tile_of(d_context[at], c_tile), 0).astype(jnp.bfloat16)
        total = l_ref[0, at, head : head + 1]
        scores = mul_nt(
            jnp.concatenate([queries, in_parts(qx_ref[at, :].astype(jnp.float32), -total)], axis=1),
            jnp.concatenate([keys, kx_ref[...]], axis=1),
        )
        if causal:
            scores = with_triangle(scores, tri_ref[...], part)
        return scores, mul_nt(d_rows, values), queries, d_rows, keys

    units = units_of(q_ref.shape[1], rows)
    ahead = products_of(*units[0])
    d_queries = []
    for index, (at, part, head) in enumerate(units):
        scores, d_probs, queries, d_rows, keys = ahead
        if index + 1 < len(units):
            ahead = products_of(*units[index + 1])
        _, k_tile, v_tile, _, _ = HEADS[head]
        probs = jnp.exp(scores)
        inner = jnp.sum(probs * d_probs, axis=1, keepdims=True)
        d_scores = (probs * (d_probs - inner)).astype(jnp.bfloat16)
        d_values = mul_tn(probs.astype(jnp.bfloat16), d_rows)
        d_keys = mul_tn(d_scores, queries)
        d_queries.append(mul(d_scores, keys) * 0.125)
        k_at = slice(k_tile * LANES, (k_tile + 1) * LANES)
        v_at = slice(v_tile * LANES, (v_tile + 1) * LANES)
        if part == 0 and head != 1:
            sum_ref[:, k_at] = d_keys
            sum_ref[:, v_at] = d_values
        else:
            sum_ref[:, k_at] += d_keys
            sum_ref[:, v_at] += d_values
        if head == len(HEADS) - 1:
            dq_ref[at, :LANES] = jnp.where(low, d_queries[0], d_queries[1]).astype(jnp.bfloat16)
            dq_ref[at, LANES:] = jnp.where(low, d_queries[2], 0).astype(jnp.bfloat16)
            d_queries = []
    dkv_ref[...] = sum_ref[...].astype(jnp.bfloat16)
    d_xq = mul_nt(dq_ref[...], w_ref[:, : 2 * LANES])
    d_xkv = mul_nt(dkv_ref[...], w_ref[:, LANES : 5 * LANES])

    grad_q = mul_tn(xq_ref[...], dq_ref[...])
    grad_kv = mul_tn(xkv_ref[...], dkv_ref[...])
    grad_o = mul_tn(do_ref[...], c_ref[0])
    g_ref[:, :LANES] = grad_q[:, :LANES].astype(jnp.bfloat16)
    g_ref[:, LANES : 2 * LANES] = (grad_q[:, LANES:] + grad_kv[:, :LANES]).astype(jnp.bfloat16)
    g_ref[:, 2 * LANES : 4 * LANES] = grad_kv[:, LANES : 3 * LANES].astype(jnp.bfloat16)
    g_ref[:, 4 * LANES : 5 * LANES] = (grad_kv[:, 3 * LANES :] + grad_o[:, :LANES]).astype(jnp.bfloat16)
    g_ref[:, 5 * LANES :] = grad_o[:, LANES:].astype(jnp.bfloat16)
    return d_xq, d_xkv


def attend_back_kernel(causal, flag_ref, do_ref, xq_ref, xkv_ref, own_ref, peer_ref, *refs):
    kept, (qx_ref, kx_ref, tri_ref, dxq_ref, dxkv_ref, keep_ref, send_ref, w_ref) = refs[:4], refs[4:12]
    work = refs[12:]
    assemble(flag_ref, [own_ref], [peer_ref], w_ref)
    d_xq, d_xkv = attend_back_block(
        causal, do_ref, xq_ref, xkv_ref, w_ref, qx_ref, kx_ref, tri_ref, kept, work
    )
    add_up(pl.program_id(0) == 0, dxq_ref, d_xq)
    add_up(pl.program_id(0) == 0, dxkv_ref, d_xkv)
    hand_out(flag_ref, work[3], keep_ref, send_ref)


def whole(shape):
    return pl.BlockSpec(shape, lambda j, flag: (0,) * len(shape))


def per_block(shape, first=0, gate=1):
    return pl.BlockSpec((1,) + shape, lambda j, flag: (first + j * flag[gate],) + (0,) * len(shape))


shape = jax.ShapeDtypeStruct


def call(kernel, name, micros, moved, grid, in_specs, out_specs, out_shape, scratch, *operands):
    return pl.pallas_call(
        where_active(kernel),
        grid_spec=pltpu.PrefetchScalarGridSpec(
            num_scalar_prefetch=1,
            grid=(grid,),
            in_specs=in_specs,
            out_specs=out_specs,
            scratch_shapes=scratch,
        ),
        out_shape=out_shape,
        compiler_params=pltpu.CompilerParams(vmem_limit_bytes=VMEM_BYTES),
        cost_estimate=cost(micros, moved),
        name=name,
    )(*operands)


def cost(micros, moved):
    return pl.CostEstimate(flops=int(micros * 1.15e9), bytes_accessed=int(moved), transcendentals=0)


def attend(flag, xq, xkv, weights, extras, causal):
    rows, width = xq.shape
    keys = xkv.shape[0]
    blocks = weights[0].shape[0]
    return call(
        functools.partial(attend_kernel, causal),
        "attend_self" if causal else "attend_cross",
        20,
        24 * 2**20,
        blocks,
        [whole((rows, width)), whole((keys, width))]
        + [per_block(part.shape[1:]) for part in weights]
        + [whole(extra.shape) for extra in extras],
        [
            whole((rows, width)),
            per_block((rows, 2 * LANES)),
            per_block((keys, 4 * LANES)),
            per_block((rows, 2 * LANES)),
            per_block((rows, LANES)),
        ],
        [
            shape((rows, width), jnp.float32),
            shape((blocks, rows, 2 * LANES), jnp.bfloat16),
            shape((blocks, keys, 4 * LANES), jnp.bfloat16),
            shape((blocks, rows, 2 * LANES), jnp.bfloat16),
            shape((blocks, rows, LANES), jnp.float32),
        ],
        [pltpu.VMEM((width, 6 * LANES), jnp.bfloat16)],
        flag,
        xq,
        xkv,
        *weights,
        *extras,
    )


def attend_back(flag, d_out, xq, xkv, weights, kept, extras, causal, first, count):
    rows, width = xq.shape
    keys = xkv.shape[0]
    return call(
        functools.partial(attend_back_kernel, causal),
        "attend_self_back" if causal else "attend_cross_back",
        10 * count,
        6 * 2**20 * count,
        count,
        [whole((rows, width)), whole((rows, width)), whole((keys, width))]
        + [per_block(part.shape[1:], first) for part in weights]
        + [
            per_block((rows, 2 * LANES), first),
            per_block((keys, 4 * LANES), first),
            per_block((rows, 2 * LANES), first),
            per_block((rows, LANES), first),
        ]
        + [whole(extra.shape) for extra in extras],
        [whole((rows, width)), whole((keys, width))] + [per_block(part.shape[1:]) for part in weights],
        [shape((rows, width), jnp.float32), shape((keys, width), jnp.float32)]
        + [shape((count,) + part.shape[1:], jnp.bfloat16) for part in weights],
        [
            pltpu.VMEM((width, 6 * LANES), jnp.bfloat16),
            pltpu.VMEM((keys, 4 * LANES), jnp.float32),
            pltpu.VMEM((rows, 2 * LANES), jnp.bfloat16),
            pltpu.VMEM((keys, 4 * LANES), jnp.bfloat16),
            pltpu.VMEM((width, 6 * LANES), jnp.bfloat16),
        ],
        flag,
        d_out,
        xq,
        xkv,
        *weights,
        *kept,
        *extras,
    )


def ffn_block(x_ref, w_ref, units, g_ref, slope_ref):
    inner = mul(x_ref[...], w_ref[:, :units])
    spread = 0.5 * (1.0 + lax.erf(inner * (0.5**0.5)))
    bell = jnp.exp(-0.5 * inner * inner) * 0.3989422804014327
    active = (inner * spread).astype(jnp.bfloat16)
    g_ref[0] = active
    slope_ref[0] = (spread + inner * bell).astype(jnp.bfloat16)
    return mul_nt(active, w_ref[:, units:])


def ffn_kernel(flag_ref, x_ref, *refs):
    own_refs, peer_refs = refs[:PARTS], refs[PARTS : 2 * PARTS]
    z_ref, g_ref, slope_ref, w_ref = refs[2 * PARTS :]
    assemble(flag_ref, own_refs, peer_refs, w_ref)
    out = ffn_block(x_ref, w_ref, own_refs[0].shape[2], g_ref, slope_ref)
    add_up(pl.program_id(0) == 0, z_ref, out)


def ffn(flag, x, weights):
    rows, width = x.shape
    blocks, _, units = weights[0].shape
    return call(
        ffn_kernel,
        "ffn",
        12,
        rows * units * blocks * 16,
        blocks,
        [whole((rows, width))] + [per_block(part.shape[1:]) for part in weights],
        [whole((rows, width)), per_block((rows, units)), per_block((rows, units))],
        [
            shape((rows, width), jnp.float32),
            shape((blocks, rows, units), jnp.bfloat16),
            shape((blocks, rows, units), jnp.bfloat16),
        ],
        [pltpu.VMEM((width, 2 * units), jnp.bfloat16)],
        flag,
        x,
        *weights,
    )


def ffn_back_block(dz_ref, w_ref, units, slope_ref, dh_ref):
    d_active = mul(dz_ref[...], w_ref[:, units:])
    d_inner = (d_active * slope_ref[0].astype(jnp.float32)).astype(jnp.bfloat16)
    dh_ref[0] = d_inner
    return mul_nt(d_inner, w_ref[:, :units])


def layer_norm(values, gain_row, bias_row):
    average = jnp.mean(values, axis=-1, keepdims=True)
    centered = values - average
    variance = jnp.mean(centered * centered, axis=-1, keepdims=True)
    return centered * lax.rsqrt(variance + NORM_EPS) * gain_row + bias_row


def norm_back(values, gain_row, bias_row, upstream):
    _, pullback = jax.vjp(layer_norm, values, gain_row, bias_row)
    return pullback(upstream)


def norm_parts(values):
    average = jnp.mean(values, axis=1, keepdims=True)
    centered = values - average
    scale = lax.rsqrt(jnp.mean(centered * centered, axis=1, keepdims=True) + NORM_EPS)
    return centered * scale, scale


def norm_gradients(values, gain_row, upstream):
    shaped, scale = norm_parts(values)
    inner = upstream * gain_row
    mean_inner = jnp.mean(inner, axis=1, keepdims=True)
    mean_product = jnp.mean(inner * shaped, axis=1, keepdims=True)
    d_values = scale * (inner - mean_inner - shaped * mean_product)
    d_gain = jnp.sum(upstream * shaped, axis=0, keepdims=True)
    return d_values, d_gain, jnp.sum(upstream, axis=0, keepdims=True)


def enc_out_back_kernel(
    flag_ref, arrived_a_ref, arrived_b_ref, cot_ref, total_ref, norms_ref, d_dec_ref, enc_ref, dec_ref, *refs
):
    d_total_ref, dz_ref, sums_ref, keep_ref, send_ref, g_ref, left_t_ref = refs

    @pl.when(jnp.logical_and(pl.program_id(0) == 0, flag_ref[2] == 1))
    def _():
        arrived = jnp.concatenate([arrived_a_ref[...], arrived_b_ref[...]], axis=0)
        upstream = arrived.astype(jnp.float32) + cot_ref[...].astype(jnp.float32)
        d_total, sums_ref[0:1, :], sums_ref[1:2, :] = norm_gradients(total_ref[...], norms_ref[2:3, :], upstream)
        d_total_ref[...] = d_total
        dz_ref[...] = d_total.astype(jnp.bfloat16)

    @pl.when(jnp.logical_and(pl.program_id(0) == 0, flag_ref[2] == 0))
    def _():
        dz_ref[...] = d_dec_ref[...]

    @pl.when(pl.program_id(0) == 0)
    def _():
        left_t_ref[...] = dz_ref[...].T

    right = jnp.where(flag_ref[2] == 1, enc_ref[0], dec_ref[0])
    g_ref[...] = mul(left_t_ref[...], right).astype(jnp.bfloat16)
    hand_out(flag_ref, g_ref, keep_ref, send_ref)


def enc_out_back(flag, arrived_a, arrived_b, cot, total, norms, d_dec, enc_active, dec_active, like):
    rows, width = cot.shape
    blocks, _, units = enc_active.shape
    full = shape((rows, width), jnp.float32)
    return call(
        enc_out_back_kernel,
        "enc_out_back",
        9,
        rows * units * blocks * 8,
        blocks,
        [whole(item.shape) for item in (arrived_a, arrived_b, cot, total, norms, d_dec)]
        + [per_block((rows, units), 0, 2), per_block((rows, units), 0, 3)],
        [whole((rows, width))] * 2 + [whole((8, width))] + [per_block(like.shape[1:])] * 2,
        [full, shape((rows, width), jnp.bfloat16), shape((8, width), jnp.float32)]
        + [shape(like.shape, jnp.bfloat16)] * 2,
        [pltpu.VMEM((width, units), jnp.bfloat16), pltpu.VMEM((width, rows), jnp.bfloat16)],
        flag,
        arrived_a,
        arrived_b,
        cot,
        total,
        norms,
        d_dec,
        enc_active,
        dec_active,
    )


def enc_in_back_kernel(
    flag_ref, dz_ref, d_enc_ref, d_middle_ref, total_ref, gain_ref, middle_ref, crossed_ref, *refs
):
    first_own_ref, second_own_ref, first_peer_ref, second_peer_ref, slope_ref, dec_inner_ref, *refs = refs
    d_total_ref, d_low_ref, sums_ref, keep_ref, send_ref, w_ref, inner_ref, out_ref, g_ref, left_t_ref = refs
    step = pl.program_id(0)
    phase, at = step // 4, step % 4
    on_encoder = flag_ref[2] == 1

    @pl.when(jnp.logical_and(phase == 0, on_encoder))
    def _():
        assemble(flag_ref, [first_own_ref, second_own_ref], [first_peer_ref, second_peer_ref], w_ref)
        out = ffn_back_block(
            dz_ref, w_ref, first_own_ref.shape[2], slope_ref, inner_ref.at[pl.ds(at, 1)]
        )
        add_up(at == 0, out_ref, out)

    @pl.when(step == 3)
    def _():
        upstream = jnp.where(on_encoder, d_enc_ref[...] + out_ref[...], d_middle_ref[...])
        d_total, sums_ref[0:1, :], sums_ref[1:2, :] = norm_gradients(total_ref[...], gain_ref[0:1, :], upstream)
        d_total_ref[...] = d_total
        d_low_ref[...] = d_total.astype(jnp.bfloat16)
        left_t_ref[...] = jnp.where(on_encoder, middle_ref[...], crossed_ref[...]).T

    @pl.when(phase == 1)
    def _():
        right = jnp.where(on_encoder, inner_ref[at], dec_inner_ref[0])
        g_ref[...] = mul(left_t_ref[...], right).astype(jnp.bfloat16)
        hand_out(flag_ref, g_ref, keep_ref, send_ref)


def enc_in_back(flag, dz, d_enc, d_middle, total, gain, middle, crossed, feed, slope, dec_inner):
    rows, width = dz.shape
    blocks, half, units = feed[0].shape
    full = shape((rows, width), jnp.float32)

    def at_step(of, low, high, gate):
        def index(j, flag):
            return (jnp.where(j < 4, j if low == "up" else low, j - 4 if high == "up" else high) * flag[gate],) + (
                0,
            ) * len(of)

        return pl.BlockSpec((1,) + of, index)

    return call(
        enc_in_back_kernel,
        "enc_in_back",
        19,
        rows * units * blocks * 20,
        8,
        [whole(item.shape) for item in (dz, d_enc, d_middle, total, gain, middle, crossed)]
        + [at_step((half, units), "up", 3, 2)] * 4
        + [at_step((rows, units), "up", 3, 2), at_step((rows, units), 0, "up", 3)],
        [whole((rows, width))] * 2 + [whole((8, width))] + [at_step((half, units), 0, "up", 1)] * 2,
        [full, shape((rows, width), jnp.bfloat16), shape((8, width), jnp.float32)]
        + [shape(feed[0].shape, jnp.bfloat16)] * 2,
        [
            pltpu.VMEM((width, 2 * units), jnp.bfloat16),
            pltpu.VMEM((blocks, rows, units), jnp.bfloat16),
            pltpu.VMEM((rows, width), jnp.float32),
            pltpu.VMEM((width, units), jnp.bfloat16),
            pltpu.VMEM((width, rows), jnp.bfloat16),
        ],
        flag,
        dz,
        d_enc,
        d_middle,
        total,
        gain,
        middle,
        crossed,
        *feed,
        slope,
        dec_inner,
    )


def decoder_kernel(
    flag_ref,
    h1_ref,
    mem_a_ref,
    mem_b_ref,
    peer_a_ref,
    peer_b_ref,
    cot_ref,
    qx_ref,
    kx_ref,
    norms_ref,
    own_ref,
    peer_ref,
    first_own_ref,
    second_own_ref,
    first_peer_ref,
    second_peer_ref,
    decoded_ref,
    crossed_ref,
    d_dec_ref,
    d_middle_ref,
    mine_ref,
    other_ref,
    sums_ref,
    active_ref,
    inner_ref,
    keep_ref,
    send_ref,
    xq_ref,
    xkv_ref,
    wx_ref,
    wf_ref,
    q_ref,
    kv_ref,
    c_ref,
    l_ref,
    slope_ref,
    out_ref,
    total_ref,
    crossed_full_ref,
    upstream_ref,
    do_ref,
    dxkv_ref,
    *work,
):
    step = pl.program_id(0)
    phase, at = step // 4, step % 4
    first, last = at == 0, at == 3
    rows = h1_ref.shape[0]
    units = first_own_ref.shape[2]
    gain = [norms_ref[row : row + 1, :] for row in range(3)]
    bias = [norms_ref[3 + row : 4 + row, :] for row in range(3)]

    def kept(block):
        return tuple(ref.at[pl.ds(block, 1)] for ref in (q_ref, kv_ref, c_ref, l_ref))

    @pl.when(step == 0)
    def _():
        xq_ref[...] = h1_ref[...].astype(jnp.bfloat16)
        for part, ref in enumerate((mem_a_ref, mem_b_ref, peer_a_ref, peer_b_ref)):
            xkv_ref[part * rows // 2 : (part + 1) * rows // 2] = ref[...]

    @pl.when(jnp.logical_or(phase == 0, phase == 3))
    def _():
        assemble(flag_ref, [own_ref], [peer_ref], wx_ref)

    @pl.when(jnp.logical_or(phase == 1, phase == 2))
    def _():
        assemble(flag_ref, [first_own_ref, second_own_ref], [first_peer_ref, second_peer_ref], wf_ref)

    @pl.when(phase == 0)
    def _():
        add_up(first, out_ref, attend_block(False, xq_ref, xkv_ref, wx_ref, qx_ref, kx_ref, None, *kept(at)))

    @pl.when(jnp.logical_and(phase == 0, last))
    def _():
        total = h1_ref[...] + out_ref[...]
        total_ref[...] = total
        crossed = norm_parts(total)[0] * gain[1] + bias[1]
        crossed_full_ref[...] = crossed
        crossed_ref[...] = crossed.astype(jnp.bfloat16)

    @pl.when(phase == 1)
    def _():
        add_up(first, out_ref, ffn_block(crossed_ref, wf_ref, units, active_ref, slope_ref.at[pl.ds(at, 1)]))

    @pl.when(jnp.logical_and(phase == 1, last))
    def _():
        total = crossed_full_ref[...] + out_ref[...]
        decoded_ref[...] = (norm_parts(total)[0] * gain[2] + bias[2]).astype(jnp.bfloat16)
        d_total, sums_ref[0:1, :], sums_ref[1:2, :] = norm_gradients(
            total, gain[2], cot_ref[...].astype(jnp.float32)
        )
        upstream_ref[...] = d_total
        d_dec_ref[...] = d_total.astype(jnp.bfloat16)

    @pl.when(phase == 2)
    def _():
        add_up(first, out_ref, ffn_back_block(d_dec_ref, wf_ref, units, slope_ref.at[pl.ds(3 - at, 1)], inner_ref))

    @pl.when(jnp.logical_and(phase == 2, last))
    def _():
        d_total, sums_ref[2:3, :], sums_ref[3:4, :] = norm_gradients(
            total_ref[...], gain[1], upstream_ref[...] + out_ref[...]
        )
        upstream_ref[...] = d_total
        do_ref[...] = d_total.astype(jnp.bfloat16)

    @pl.when(phase == 3)
    def _():
        d_xq, d_xkv = attend_back_block(
            False, do_ref, xq_ref, xkv_ref, wx_ref, qx_ref, kx_ref, None, kept(3 - at), work
        )
        add_up(first, out_ref, d_xq)
        add_up(first, dxkv_ref, d_xkv)
        hand_out(flag_ref, work[3], keep_ref, send_ref)

    @pl.when(jnp.logical_and(phase == 3, last))
    def _():
        d_middle_ref[...] = upstream_ref[...] + out_ref[...]
        mine_ref[...] = dxkv_ref[:rows]
        other_ref[...] = dxkv_ref[rows:].astype(jnp.bfloat16)


def decoder(flag, h1, memory, cot, extras, norms, cross, feed):
    rows, width = h1.shape
    blocks, half, _ = cross[0].shape
    units = feed[0].shape[2]
    keys = 2 * rows
    qx, kx = extras

    def at_step(of, in_phase):
        def index(j, flag):
            at = j % 4
            choice = [{"up": at, "down": 3 - at}.get(way, way) for way in in_phase]
            chosen = choice[3]
            for phase in (2, 1, 0):
                chosen = jnp.where(j // 4 == phase, choice[phase], chosen)
            return (chosen * flag[1],) + (0,) * len(of)

        return pl.BlockSpec((1,) + of, index)

    part = (half, cross[0].shape[2])
    full = shape((rows, width), jnp.float32)
    rounded = shape((rows, width), jnp.bfloat16)
    return call(
        decoder_kernel,
        "decoder",
        90,
        40 * 2**20,
        16,
        [whole(item.shape) for item in (h1, *memory, cot, qx, kx, norms)]
        + [at_step(part, ("up", 3, 3, "down"))] * 2
        + [at_step((half, units), (0, "up", "down", 0))] * 4,
        [whole((rows, width))] * 6
        + [whole((8, width))]
        + [
            at_step((rows, units), (0, "up", 3, 3)),
            at_step((rows, units), (3, 3, "down", 0)),
            at_step(part, (3, 3, 3, "down")),
            at_step(part, (3, 3, 3, "down")),
        ],
        [rounded, rounded, rounded, full, full, rounded, shape((8, width), jnp.float32)]
        + [shape((blocks, rows, units), jnp.bfloat16)] * 2
        + [shape(cross[0].shape, jnp.bfloat16)] * 2,
        [
            pltpu.VMEM((rows, width), jnp.bfloat16),
            pltpu.VMEM((keys, width), jnp.bfloat16),
            pltpu.VMEM((width, 6 * LANES), jnp.bfloat16),
            pltpu.VMEM((width, 2 * units), jnp.bfloat16),
            pltpu.VMEM((blocks, rows, 2 * LANES), jnp.bfloat16),
            pltpu.VMEM((blocks, keys, 4 * LANES), jnp.bfloat16),
            pltpu.VMEM((blocks, rows, 2 * LANES), jnp.bfloat16),
            pltpu.VMEM((blocks, rows, LANES), jnp.float32),
            pltpu.VMEM((blocks, rows, units), jnp.bfloat16),
            pltpu.VMEM((rows, width), jnp.float32),
            pltpu.VMEM((rows, width), jnp.float32),
            pltpu.VMEM((rows, width), jnp.float32),
            pltpu.VMEM((rows, width), jnp.float32),
            pltpu.VMEM((rows, width), jnp.bfloat16),
            pltpu.VMEM((keys, width), jnp.float32),
            pltpu.VMEM((keys, 4 * LANES), jnp.float32),
            pltpu.VMEM((rows, 2 * LANES), jnp.bfloat16),
            pltpu.VMEM((keys, 4 * LANES), jnp.bfloat16),
            pltpu.VMEM((width, 6 * LANES), jnp.bfloat16),
        ],
        flag,
        h1,
        *memory,
        cot,
        qx,
        kx,
        norms,
        *cross,
        *feed,
    )


def low(values):
    return values.astype(jnp.bfloat16)


def axes_of(count):
    return ("section", "zh", "zl") + tuple("e%d" % at for at in range(count)) + ("ty", "tx")


def layer_of(place):
    return 1 ^ place["zh"] ^ place["zl"]


def moved(x, names, to):
    names = [name for name in axes_of(8) if name in names]

    def index(place):
        return sum(place[name] << (len(names) - 1 - at) for at, name in enumerate(names))

    pairs = []
    for source in range(2 ** len(names)):
        place = {name: source >> (len(names) - 1 - at) & 1 for at, name in enumerate(names)}
        target = to(place)
        if target is not None:
            pairs.append((source, index(target)))
    return lax.ppermute(x, tuple(names), pairs)


def over(x, *axes, layer=None):
    def to(place):
        if layer is not None and layer_of(place) != layer:
            return None
        return {**place, **{axis: 1 - place[axis] for axis in axes}}

    return moved(x, axes if layer is None else axes + Z, to)


Z = ("zh", "zl")


def swapped(x):
    def to(place):
        if place["section"] == layer_of(place):
            return place
        return {"section": 1 - place["section"], "zh": place["zh"], "zl": 1 - place["zl"]}

    return moved(x, ("section",) + Z, to)


def turned(x):
    return moved(x, ("section", "ty"), lambda place: {"section": place["ty"], "ty": place["section"]})


def sent_home(x, other):
    def to(place):
        return {
            "section": layer_of(place),
            "zh": place["zh"],
            "zl": 1 ^ place["zh"] ^ place["ty"],
            "ty": place["section"],
            "tx": place["tx"] ^ other,
        }

    return moved(x, ("section",) + Z + ("ty", "tx"), to)


def cross_in(x, layer):
    def to(place):
        if place["section"] != layer:
            return None
        return {"section": layer_of(place), "zh": place["zh"], "zl": place["zh"]}

    return moved(x, ("section",) + Z, to)


def cross_out(x, layer):
    def to(place):
        if layer_of(place) != 1:
            return None
        return {"section": layer, "zh": place["zh"], "zl": 1 ^ place["zh"] ^ place["section"]}

    return moved(x, ("section",) + Z, to)


def in_order(x, flag, axis):
    return jnp.where(flag == 1, jnp.flip(x, axis), x)


def pack_heads(query, key, value, out):
    pair = 2 * HDIM
    return jnp.concatenate(
        [
            query,
            value[:, pair:],
            key[:, :pair],
            value[:, :pair],
            key[:, pair:],
            out[:, pair:],
            out[:, :pair],
        ],
        axis=1,
    )


def unpack_heads(packed):
    part = [packed[:, at * HDIM : (at + 1) * HDIM] for at in range(12)]
    query = jnp.concatenate(part[0:3], axis=1)
    key = jnp.concatenate([part[4], part[5], part[8]], axis=1)
    value = jnp.concatenate([part[6], part[7], part[3]], axis=1)
    out = jnp.concatenate([part[10], part[11], part[9]], axis=1)
    return query, key, value, out


def after(x, *earlier):
    return lax.optimization_barrier((x,) + earlier)[0]


def plane_gathered(x, until=(), **only):
    parts = [x, over(x, "tx", **only), over(x, "ty", **only), over(x, "ty", "tx", **only)]
    return jnp.stack([after(part, *until) for part in parts])


def plane_summed(x, until=(), raw=None, **only):
    terms = [x[0], over(x[1], "tx", **only), over(x[2], "ty", **only), over(x[3], "ty", "tx", **only)]
    if raw is not None:
        raw.extend(terms[1:])
    terms = [after(term, *until) for term in terms]
    return low(sum(term.astype(jnp.float32) for term in terms))


def rows_gathered(x, count, until=(), raw=None, **only):
    for axes in [("e%d" % at,) for at in reversed(range(count))] + [Z]:
        got = over(x, *axes, **only)
        if raw is not None:
            raw.append(got)
        parts = [after(part, *until) for part in (x, got)]
        both = in_order(jnp.stack(parts, axis=-3), lax.axis_index(axes[0]), x.ndim - 2)
        x = both.reshape(x.shape[:-2] + (2 * x.shape[-2], x.shape[-1]))
    return x


def rows_summed(x, count, until=(), raw=None, **only):
    for axes in [Z] + [("e%d" % at,) for at in range(count)]:
        halves = x.reshape(x.shape[:-2] + (2, x.shape[-2] // 2, x.shape[-1]))
        halves = in_order(halves, lax.axis_index(axes[0]), x.ndim - 2)
        got = over(halves[..., 1, :, :], *axes, **only)
        if raw is not None:
            raw.append(got)
        x = plus(halves[..., 0, :, :], after(got, *until))
    return x


def plus(first, second):
    return low(first.astype(jnp.float32) + second.astype(jnp.float32))


def from_cores(keep, send, raw=None, **only):
    got = over(send, "section", **only)
    if raw is not None:
        raw.append(got)
    return plus(keep, got)


def body(
    count,
    hidden,
    cotangent,
    segments,
    sa_qkv,
    sa_out,
    cross_one,
    cross_two,
    ffn_in,
    ffn_out,
    norm_gain,
    norm_bias,
):
    core = lax.axis_index("section")
    x_at, y_at, zh_at, zl_at = (lax.axis_index(name) for name in ("tx", "ty", "zh", "zl"))
    layer = 1 ^ zh_at ^ zl_at
    on_encoder = layer == 0
    quarter = hidden.shape[3]
    enc_flag = jnp.stack([core, 1 - layer, 1 - layer, layer])
    dec_flag = jnp.stack([core, layer, 1 - layer, layer])
    flag = jnp.stack([core, jnp.ones_like(core), 1 - layer, layer])

    def pick(first, second):
        return jnp.where(on_encoder, first, second)

    def of_one_row(x):
        both = in_order(x[0, :, 0], x_at, 0)
        return in_order(jnp.stack([both[0], over(both[1], "tx")]), x_at, 0).reshape(2 * quarter, -1)

    def rows_out(x, raw=None):
        mine, other = in_order(x.reshape(2, quarter, -1), x_at, 0)
        both = [sent_home(mine, 0), sent_home(other, 1)]
        if raw is not None:
            raw.extend(both)
        return in_order(jnp.stack(both), x_at, 0)[None, :, None]

    units = ffn_in.shape[2]
    width = cross_one.shape[2]
    packed_self = pack_heads(sa_qkv[0, :, 0], sa_qkv[0, :, 1], sa_qkv[0, :, 2], sa_out[0])
    packed_ffn = jnp.concatenate([ffn_in[0], ffn_out[0].T], axis=1)
    with jax.named_scope("norms_in"):
        norms = swapped(jnp.concatenate([norm_gain[0], norm_bias[0]], axis=0))
        gains, biases = norms[:3], norms[3:]
        seg_own = segments[:, :, 0].astype(jnp.float32)
        seg_here = jnp.where(zl_at == 1 ^ zh_at ^ y_at, seg_own, over(seg_own, "zl")).astype(jnp.int32)
    with jax.named_scope("hidden_in"):
        one_row = of_one_row(hidden)
    with jax.named_scope("self_weights"):
        shard_self = swapped(packed_self)
    with jax.named_scope("hidden_in"):
        one_row = swapped(after(one_row, shard_self))
    with jax.named_scope("ffn_weights"):
        shard_ffn = swapped(after(packed_ffn, one_row))
        shard_first, shard_second = shard_ffn[:, :units], shard_ffn[:, units:]

    def both_rows(x):
        for_enc = rows_gathered(x, count, layer=0)
        return pick(for_enc, rows_gathered(after(x, for_enc), count, layer=1))

    with jax.named_scope("self_weights"):
        rows_self = both_rows(shard_self)
        own_self = plane_gathered(rows_self)
        w_self = [own_self, over(own_self, "section")]
    with jax.named_scope("hidden_in"):
        rows_here = turned(one_row)
        rows_all = jnp.concatenate([rows_here, over(rows_here, "section")], axis=0)
    with jax.named_scope("cross_weights"):
        cross_low = after(jnp.concatenate([cross_one[0], cross_two[0]], axis=1), own_self)
        pair_kv, pair_qo = cross_in(cross_low, 0), cross_in(cross_low, 1)
        packed = pack_heads(pair_qo[:, :width], pair_kv[:, :width], pair_kv[:, width:], pair_qo[:, width:])
    with jax.named_scope("ffn_weights"):
        rows_first = both_rows(after(shard_first, rows_self))
        plane_second = plane_gathered(after(shard_second, own_self))

    both_segments = in_order(seg_here, x_at, 1)[:, 0]
    ordered = in_order(both_segments.reshape(2, 2, 2 * quarter), core, 1).reshape(2, 4 * quarter)
    source_seg, target_seg = ordered[0], ordered[1]
    self_seg = pick(source_seg, target_seg)
    parts = jnp.arange(4)
    quarter_of = jnp.repeat(2 * ((parts // 2) ^ core) + parts % 2, quarter)
    lanes = jnp.arange(LANES)[None, :]

    def key_extras(seg):
        differs = jnp.logical_and(lanes < SEG_LANES, seg[:, None] != lanes)
        later = jnp.logical_and(
            jnp.logical_and(lanes >= SEG_LANES, lanes < PART_LANE),
            quarter_of[:, None] > lanes - SEG_LANES,
        )
        part = jnp.logical_and(lanes >= PART_LANE, lanes < PART_LANE + 3)
        return jnp.where(differs | later | part, 1.0, 0.0).astype(jnp.bfloat16)

    def query_extras(seg, causal):
        seg, at = seg[: 2 * quarter], quarter_of[: 2 * quarter]
        same = seg[:, None] == lanes
        here = jnp.logical_and(at[:, None] + SEG_LANES == lanes, causal)
        return jnp.where(same | here, MASKED, 0.0).astype(jnp.bfloat16)

    at_row = jnp.arange(quarter)
    later_key = jnp.logical_and(at_row[None, :] > at_row[:, None], jnp.logical_not(on_encoder))
    tri = jnp.where(later_key, MASKED, 0.0).astype(jnp.float32)
    self_extras = (query_extras(self_seg, jnp.logical_not(on_encoder)), key_extras(self_seg), tri)
    cross_extras = (query_extras(target_seg, False), key_extras(source_seg), tri)

    start = rows_all.astype(jnp.float32)
    start = pick(layer_norm(start, gains[0], biases[0]), start)
    start_here = start[: 2 * quarter]
    start_low = low(start)
    self_gain, self_bias = pick(gains[1], gains[0]), pick(biases[1], biases[0])
    self_out, *kept_self = attend(
        flag, start_low[: 2 * quarter], after(start_low, plane_second), w_self, self_extras, True
    )
    with jax.named_scope("ffn_weights"):
        own_first = plane_gathered(after(rows_first, plane_second), until=(self_out,))
        enc_second = rows_gathered(plane_second, count, until=(self_out,), layer=0)
        peer_first = over(own_first, "section")
        w_enc = [own_first, enc_second, peer_first, over(enc_second, "section", layer=0)]
    raw_second = []
    with jax.named_scope("ffn_weights"):
        dec_second = rows_gathered(after(plane_second, self_out), count, raw=raw_second, layer=1)
    with jax.named_scope("cotangent_in"):
        cot = turned(swapped(of_one_row(after(cotangent, self_out))))
    self_total = start_here + self_out
    middle = layer_norm(self_total, self_gain, self_bias)
    middle_low = low(middle)

    enc_out, enc_active, enc_slope = ffn(enc_flag, after(middle_low, cot, *raw_second), w_enc)
    enc_total = middle + enc_out
    encoded = low(layer_norm(enc_total, gains[2], biases[2]))
    def across(x, layer):
        return moved(x, Z, lambda place: {**place, "zl": 1 - place["zl"]} if layer_of(place) == layer else None)

    with jax.named_scope("memory"):
        memory_here = [across(encoded[:quarter], 0), across(encoded[quarter:], 0)]
        memory_peer = [over(part, "section", layer=1) for part in memory_here]
    with jax.named_scope("cross_weights"):
        rows_cross = rows_gathered(after(packed, plane_second), count, until=(self_out,), layer=1)
        own_cross = plane_gathered(rows_cross, until=tuple(memory_here), layer=1)
        w_cross = [own_cross, over(own_cross, "section", layer=1)]
    with jax.named_scope("ffn_weights"):
        w_dec = [own_first, dec_second, peer_first, over(dec_second, "section", layer=1)]

    (
        decoded,
        crossed_low,
        d_dec_low,
        d_middle_dec,
        d_memory_here,
        d_memory_other,
        dec_sums,
        dec_active,
        dec_inner,
        cross_keep,
        cross_send,
    ) = decoder(
        dec_flag, middle, memory_here + memory_peer, cot, cross_extras[:2], norms, w_cross, w_dec
    )
    with jax.named_scope("d_memory"):
        d_memory_here = d_memory_here + over(d_memory_other, "section", layer=1).astype(jnp.float32)
        d_memory_low = low(d_memory_here)
        arrived = [across(d_memory_low[:quarter], 1), across(d_memory_low[quarter:], 1)]
    with jax.named_scope("cross_sums"):
        cross_sum = from_cores(after(cross_keep, arrived[0]), after(cross_send, arrived[0]), layer=1)
        raw_cross = []
        cross_plane = plane_summed(cross_sum, raw=raw_cross, layer=1)

    d_enc_total, dz_low, enc_sums, second_keep, second_send = enc_out_back(
        flag, *arrived, cot, enc_total, norms, after(d_dec_low, cross_sum), enc_active, dec_active, own_first
    )
    with jax.named_scope("ffn_sums"):
        second_sum = from_cores(after(second_keep, *raw_cross), after(second_send, *raw_cross))
    raw_hidden = []
    with jax.named_scope("hidden_out"):
        hidden_out = rows_out(after(pick(encoded, decoded), second_keep), raw_hidden)
    gain_row = jnp.broadcast_to(self_gain, (8, self_gain.shape[0]))
    d_self_total, d_self_low, self_norm, first_keep, first_send = enc_in_back(
        flag,
        after(dz_low, second_keep),
        d_enc_total,
        d_middle_dec,
        self_total,
        gain_row,
        middle_low,
        crossed_low,
        w_enc,
        enc_slope,
        dec_inner,
    )
    with jax.named_scope("ffn_sums"):
        gate = []
        second_plane = plane_summed(second_sum, raw=gate)
        first_sum = from_cores(after(first_keep, *raw_hidden), after(first_send, *raw_hidden), raw=gate)

    halves = []
    for first, earlier in ((0, ()), (2, gate)):
        halves.append(
            attend_back(
                flag,
                after(d_self_low, *earlier),
                start_low[: 2 * quarter],
                start_low,
                w_self,
                kept_self,
                self_extras,
                True,
                first,
                2,
            )
        )
    d_start_q = halves[0][0] + halves[1][0]
    with jax.named_scope("cross_sums"):
        share_cross = rows_summed(after(cross_plane, d_start_q), count, layer=1)
    with jax.named_scope("ffn_sums"):
        gate_later = []
        first_plane = plane_summed(after(first_sum, second_plane), raw=gate_later)
        second_share = rows_summed(second_plane, count, raw=gate_later)
    with jax.named_scope("self_sums"):
        (_, _, keep, send), (_, _, *later) = halves
        self_sum = [from_cores(after(keep, *gate), after(send, *gate), raw=gate_later)]
        self_sum.append(from_cores(*(after(part, *gate_later) for part in later)))
        self_sum = jnp.concatenate(self_sum, axis=0)
    with jax.named_scope("d_start"):
        d_start_kv = after(halves[0][1], *gate_later) + halves[1][1]
        d_start = d_self_total + d_start_q + d_start_kv[: 2 * quarter]
        d_start = d_start + over(low(d_start_kv[2 * quarter :]), "section").astype(jnp.float32)
    d_source, gain_a, bias_a = norm_back(
        rows_here.astype(jnp.float32), gains[0], biases[0], d_start
    )

    norm_sums = jnp.stack(
        [
            pick(gain_a, self_norm[0]),
            pick(self_norm[0], dec_sums[2]),
            pick(enc_sums[0], dec_sums[0]),
            pick(bias_a, self_norm[1]),
            pick(self_norm[1], dec_sums[3]),
            pick(enc_sums[1], dec_sums[1]),
        ]
    )
    shards = 2**count
    sides = jnp.arange(2)
    held, outer = core ^ sides[:, None], sides[None, :]
    row_block = ((2 * outer + (1 ^ outer ^ held)) * shards)[:, :, None] + jnp.arange(shards)
    column_block = (2 * (y_at ^ sides)[:, None] + (x_at ^ sides)[None, :]).reshape(-1)
    order = (row_block.reshape(2, -1)[:, None, :] + 0) * 4 + column_block[:, None]
    norm_sums = jnp.take(norm_sums.reshape(6, 8 * 2 * shards, -1), order.reshape(-1), axis=1)
    norm_sums = norm_sums.reshape(6, 2, 4, 2 * shards, -1)
    with jax.named_scope("norm_sums"):
        norm_sums = norm_sums[:, 0] + over(norm_sums[:, 1], "section")
    with jax.named_scope("self_sums"):
        self_plane = plane_summed(self_sum)
    with jax.named_scope("norm_sums"):
        norm_blocks = after(norm_sums.transpose(1, 2, 0, 3).reshape(4, 2 * shards, -1), self_plane)
        norm_plane = norm_blocks[0] + over(norm_blocks[1], "tx") + over(norm_blocks[2], "ty")
        norm_plane = norm_plane + over(norm_blocks[3], "ty", "tx")
    norm_width = norm_plane.shape[1]
    with jax.named_scope("self_sums"):
        pad = ((0, 0), (0, 15), (0, self_plane.shape[1] - norm_width))
        both = jnp.concatenate(
            [
                self_plane.reshape(2 * shards, -1, self_plane.shape[1]),
                jnp.pad(low(norm_plane)[:, None], pad),
            ],
            axis=1,
        )
        raw_self = []
        share_self = rows_summed(both.reshape(-1, self_plane.shape[1]), count, raw=raw_self)
        share_self = swapped(share_self).astype(jnp.float32)
    norm_shares = share_self[-16, :norm_width].reshape(6, -1)
    share_self = share_self[:-16]
    with jax.named_scope("ffn_sums"):
        first_share = rows_summed(after(first_plane, halves[1][0]), count, until=(self_sum,))
        share_ffn = swapped(jnp.concatenate([first_share, second_share], axis=1)).astype(jnp.float32)
    share_first, share_second = share_ffn[:, :units], share_ffn[:, units:].T
    with jax.named_scope("hidden_grad"):
        hidden_grad = rows_out(after(low(pick(d_source, d_start)), *raw_self)).astype(jnp.float32)
    g_query, g_key, g_value, g_out = unpack_heads(share_self)
    grad_qkv = jnp.stack([g_query, g_key, g_value], axis=1)
    c_query, c_key, c_value, c_out = unpack_heads(share_cross)
    with jax.named_scope("cross_out"):
        for_enc = cross_out(jnp.concatenate([c_key, c_value], axis=1), 0)
        for_dec = cross_out(jnp.concatenate([c_query, c_out], axis=1), 1)
    cross = jnp.where(core == 0, for_enc, for_dec).astype(jnp.float32)

    return (
        hidden_out,
        hidden_grad,
        grad_qkv[None],
        g_out[None],
        cross[None, :, :width],
        cross[None, :, width:],
        share_first[None],
        share_second[None],
        norm_shares[None, :3],
        norm_shares[None, 3:],
    )


def solution(mesh):
    _, dp_count, _ = mesh.devices.shape
    count = dp_count.bit_length() - 3
    names = axes_of(count)
    dp, tensor = names[1:-2], names[-2:]
    split = Mesh(mesh.devices.reshape((2,) * len(names)), names)
    rows = P("section", None, dp, tensor, None)
    in_specs = (
        rows,
        rows,
        P(None, None, dp, None),
        P("section", dp, None, tensor),
        P("section", dp, tensor),
        P("section", dp, tensor),
        P("section", dp, tensor),
        P("section", dp, tensor),
        P("section", tensor, dp),
        P("section", None, None),
        P("section", None, None),
    )
    out_specs = (
        rows,
        rows,
        P("section", dp, None, tensor),
        P("section", dp, tensor),
        P("section", dp, tensor),
        P("section", dp, tensor),
        P("section", dp, tensor),
        P("section", tensor, dp),
        P("section", None, dp + tensor),
        P("section", None, dp + tensor),
    )
    return jax.shard_map(
        functools.partial(body, count), mesh=split, in_specs=in_specs, out_specs=out_specs, check_vma=False
    )
```

```python
import functools

import jax
import jax.numpy as jnp
from jax import lax
from jax.experimental import pallas as pl
from jax.experimental.pallas import tpu as pltpu
from jax.sharding import Mesh
from jax.sharding import PartitionSpec as P

HDIM = 64
LANES = 128
MASKED = -1e30
NORM_EPS = 1e-05
VMEM_BYTES = 56 * 1024 * 1024

SEG_LANES = 8
PART_LANE = 12

PARTS = 2
TILE_ROWS = 256
HEADS = ((0, 1, 2, 0, 0), (0, 1, 2, 1, 1), (1, 3, 0, 0, 1))


def mul(a, b):
    return jnp.dot(a, b, preferred_element_type=jnp.float32)


def mul_nt(a, b):
    return lax.dot_general(a, b, (((1,), (1,)), ((), ())), preferred_element_type=jnp.float32)


def mul_tn(a, b):
    return lax.dot_general(a, b, (((0,), (0,)), ((), ())), preferred_element_type=jnp.float32)


def tile_of(values, index):
    return values[:, index * LANES : (index + 1) * LANES]


def lane_ids(rows):
    return lax.broadcasted_iota(jnp.int32, (rows, LANES), 1)


def half_mask(rows, half):
    lanes = lane_ids(rows)
    return lanes >= HDIM if half else lanes < HDIM


def in_parts(base, column):
    lanes = lane_ids(base.shape[0])
    high = column.astype(jnp.bfloat16).astype(jnp.float32)
    rest = column - high
    middle = rest.astype(jnp.bfloat16).astype(jnp.float32)
    low = rest - middle
    parts = jnp.where(
        lanes == PART_LANE,
        high,
        jnp.where(lanes == PART_LANE + 1, middle, jnp.where(lanes == PART_LANE + 2, low, base)),
    )
    return parts.astype(jnp.bfloat16)


def with_triangle(scores, tri, at):
    size = tri.shape[1]
    pieces = []
    if at > 0:
        pieces.append(scores[:, : at * size])
    pieces.append(scores[:, at * size : (at + 1) * size] + tri)
    pieces.append(scores[:, (at + 1) * size :])
    return jnp.concatenate(pieces, axis=1)


def places(core, block):
    return [pl.multiple_of((1 - core) * block, block), pl.multiple_of((2 + core) * block, block)]


def assemble(flag_ref, own_refs, peer_refs, w_ref):
    core, block = flag_ref[0], own_refs[0].shape[1] // 2
    for holder, refs in ((core, own_refs), (1 - core, peer_refs)):
        for part, ref in enumerate(refs):
            width = ref.shape[2]
            for at, place in enumerate(places(holder, block)):
                w_ref[pl.ds(place, block), part * width : (part + 1) * width] = ref[0, at * block : (at + 1) * block]


def hand_out(flag_ref, g_ref, keep_ref, send_ref):
    core, block = flag_ref[0], keep_ref.shape[1] // 2
    for holder, ref in ((core, keep_ref), (1 - core, send_ref)):
        for at, place in enumerate(places(holder, block)):
            ref[0, at * block : (at + 1) * block] = g_ref[pl.ds(place, block), :]


def where_active(kernel):
    def guarded(flag_ref, *refs):
        @pl.when(flag_ref[1] == 1)
        def _():
            kernel(flag_ref, *refs)

    return guarded


def scaled_queries(q_ref, at, q_tile, q_half):
    queries = q_ref[0, at, q_tile * LANES : (q_tile + 1) * LANES] * 0.125
    return jnp.where(half_mask(queries.shape[0], q_half), queries, 0).astype(jnp.bfloat16)


def units_of(total, rows):
    return [
        (slice(part * rows, (part + 1) * rows), part, head)
        for part in range(total // rows)
        for head in range(len(HEADS))
    ]


def attend_block(causal, xq_ref, xkv_ref, w_ref, qx_ref, kx_ref, tri_ref, q_ref, kv_ref, c_ref, l_ref):
    q_ref[0] = mul(xq_ref[...], w_ref[:, : 2 * LANES]).astype(jnp.bfloat16)
    kv_ref[0] = mul(xkv_ref[...], w_ref[:, LANES : 5 * LANES]).astype(jnp.bfloat16)
    rows = TILE_ROWS
    low = half_mask(rows, 0)

    def scores_of(at, part, head):
        q_tile, k_tile, _, q_half, _ = HEADS[head]
        keys = kv_ref[0, :, k_tile * LANES : (k_tile + 1) * LANES]
        scores = mul_nt(
            jnp.concatenate([scaled_queries(q_ref, at, q_tile, q_half), qx_ref[at, :]], axis=1),
            jnp.concatenate([keys, kx_ref[...]], axis=1),
        )
        return with_triangle(scores, tri_ref[...], part) if causal else scores

    units = units_of(q_ref.shape[1], rows)
    ahead = scores_of(*units[0])
    contexts, totals = [], None
    for index, (at, part, head) in enumerate(units):
        scores = ahead
        if index + 1 < len(units):
            ahead = scores_of(*units[index + 1])
        v_tile = HEADS[head][2]
        values = kv_ref[0, :, v_tile * LANES : (v_tile + 1) * LANES]
        highest = jnp.max(scores, axis=1, keepdims=True)
        weights = jnp.exp(scores - highest)
        sums = jnp.sum(weights, axis=1, keepdims=True)
        contexts.append(mul(weights.astype(jnp.bfloat16), values) / sums)
        logs = jnp.broadcast_to(highest + jnp.log(sums), (rows, LANES))
        totals = logs if head == 0 else jnp.where(lane_ids(rows) == head, logs, totals)
        if head == len(HEADS) - 1:
            c_ref[0, at, :LANES] = jnp.where(low, 0, contexts[2]).astype(jnp.bfloat16)
            c_ref[0, at, LANES:] = jnp.where(low, contexts[0], contexts[1]).astype(jnp.bfloat16)
            l_ref[0, at, :] = totals
            contexts = []
    return mul_nt(c_ref[0], w_ref[:, 4 * LANES :])


def attend_kernel(causal, flag_ref, xq_ref, xkv_ref, own_ref, peer_ref, qx_ref, kx_ref, tri_ref, o_ref, *refs):
    q_ref, kv_ref, c_ref, l_ref, w_ref = refs
    assemble(flag_ref, [own_ref], [peer_ref], w_ref)
    out = attend_block(causal, xq_ref, xkv_ref, w_ref, qx_ref, kx_ref, tri_ref, q_ref, kv_ref, c_ref, l_ref)
    add_up(pl.program_id(0) == 0, o_ref, out)


def add_up(first, ref, value):
    @pl.when(first)
    def _():
        ref[...] = value

    @pl.when(jnp.logical_not(first))
    def _():
        ref[...] += value


def attend_back_block(causal, do_ref, xq_ref, xkv_ref, w_ref, qx_ref, kx_ref, tri_ref, kept, work):
    q_ref, kv_ref, c_ref, l_ref = kept
    sum_ref, dq_ref, dkv_ref, g_ref = work
    rows = TILE_ROWS
    d_context = mul(do_ref[...], w_ref[:, 4 * LANES :]).astype(jnp.bfloat16)
    low = half_mask(rows, 0)

    def products_of(at, part, head):
        q_tile, k_tile, v_tile, q_half, v_half = HEADS[head]
        c_tile = 0 if head == 2 else 1
        keys = kv_ref[0, :, k_tile * LANES : (k_tile + 1) * LANES]
        values = kv_ref[0, :, v_tile * LANES : (v_tile + 1) * LANES]
        queries = scaled_queries(q_ref, at, q_tile, q_half)
        d_rows = jnp.where(half_mask(rows, v_half), tile_of(d_context[at], c_tile), 0).astype(jnp.bfloat16)
        total = l_ref[0, at, head : head + 1]
        scores = mul_nt(
            jnp.concatenate([queries, in_parts(qx_ref[at, :].astype(jnp.float32), -total)], axis=1),
            jnp.concatenate([keys, kx_ref[...]], axis=1),
        )
        if causal:
            scores = with_triangle(scores, tri_ref[...], part)
        return scores, mul_nt(d_rows, values), queries, d_rows, keys

    units = units_of(q_ref.shape[1], rows)
    ahead = products_of(*units[0])
    d_queries = []
    for index, (at, part, head) in enumerate(units):
        scores, d_probs, queries, d_rows, keys = ahead
        if index + 1 < len(units):
            ahead = products_of(*units[index + 1])
        _, k_tile, v_tile, _, _ = HEADS[head]
        probs = jnp.exp(scores)
        inner = jnp.sum(probs * d_probs, axis=1, keepdims=True)
        d_scores = (probs * (d_probs - inner)).astype(jnp.bfloat16)
        d_values = mul_tn(probs.astype(jnp.bfloat16), d_rows)
        d_keys = mul_tn(d_scores, queries)
        d_queries.append(mul(d_scores, keys) * 0.125)
        k_at = slice(k_tile * LANES, (k_tile + 1) * LANES)
        v_at = slice(v_tile * LANES, (v_tile + 1) * LANES)
        if part == 0 and head != 1:
            sum_ref[:, k_at] = d_keys
            sum_ref[:, v_at] = d_values
        else:
            sum_ref[:, k_at] += d_keys
            sum_ref[:, v_at] += d_values
        if head == len(HEADS) - 1:
            dq_ref[at, :LANES] = jnp.where(low, d_queries[0], d_queries[1]).astype(jnp.bfloat16)
            dq_ref[at, LANES:] = jnp.where(low, d_queries[2], 0).astype(jnp.bfloat16)
            d_queries = []
    dkv_ref[...] = sum_ref[...].astype(jnp.bfloat16)
    d_xq = mul_nt(dq_ref[...], w_ref[:, : 2 * LANES])
    d_xkv = mul_nt(dkv_ref[...], w_ref[:, LANES : 5 * LANES])

    grad_q = mul_tn(xq_ref[...], dq_ref[...])
    grad_kv = mul_tn(xkv_ref[...], dkv_ref[...])
    grad_o = mul_tn(do_ref[...], c_ref[0])
    g_ref[:, :LANES] = grad_q[:, :LANES].astype(jnp.bfloat16)
    g_ref[:, LANES : 2 * LANES] = (grad_q[:, LANES:] + grad_kv[:, :LANES]).astype(jnp.bfloat16)
    g_ref[:, 2 * LANES : 4 * LANES] = grad_kv[:, LANES : 3 * LANES].astype(jnp.bfloat16)
    g_ref[:, 4 * LANES : 5 * LANES] = (grad_kv[:, 3 * LANES :] + grad_o[:, :LANES]).astype(jnp.bfloat16)
    g_ref[:, 5 * LANES :] = grad_o[:, LANES:].astype(jnp.bfloat16)
    return d_xq, d_xkv


def attend_back_kernel(causal, flag_ref, do_ref, xq_ref, xkv_ref, own_ref, peer_ref, *refs):
    kept, (qx_ref, kx_ref, tri_ref, dxq_ref, dxkv_ref, keep_ref, send_ref, w_ref) = refs[:4], refs[4:12]
    work = refs[12:]
    assemble(flag_ref, [own_ref], [peer_ref], w_ref)
    d_xq, d_xkv = attend_back_block(
        causal, do_ref, xq_ref, xkv_ref, w_ref, qx_ref, kx_ref, tri_ref, kept, work
    )
    add_up(pl.program_id(0) == 0, dxq_ref, d_xq)
    add_up(pl.program_id(0) == 0, dxkv_ref, d_xkv)
    hand_out(flag_ref, work[3], keep_ref, send_ref)


def whole(shape):
    return pl.BlockSpec(shape, lambda j, flag: (0,) * len(shape))


def per_block(shape, first=0, gate=1):
    return pl.BlockSpec((1,) + shape, lambda j, flag: (first + j * flag[gate],) + (0,) * len(shape))


shape = jax.ShapeDtypeStruct


def call(kernel, name, micros, moved, grid, in_specs, out_specs, out_shape, scratch, *operands):
    return pl.pallas_call(
        where_active(kernel),
        grid_spec=pltpu.PrefetchScalarGridSpec(
            num_scalar_prefetch=1,
            grid=(grid,),
            in_specs=in_specs,
            out_specs=out_specs,
            scratch_shapes=scratch,
        ),
        out_shape=out_shape,
        compiler_params=pltpu.CompilerParams(vmem_limit_bytes=VMEM_BYTES),
        cost_estimate=cost(micros, moved),
        name=name,
    )(*operands)


def cost(micros, moved):
    return pl.CostEstimate(flops=int(micros * 1.15e9), bytes_accessed=int(moved), transcendentals=0)


def attend(flag, xq, xkv, weights, extras, causal):
    rows, width = xq.shape
    keys = xkv.shape[0]
    blocks = weights[0].shape[0]
    return call(
        functools.partial(attend_kernel, causal),
        "attend_self" if causal else "attend_cross",
        20,
        24 * 2**20,
        blocks,
        [whole((rows, width)), whole((keys, width))]
        + [per_block(part.shape[1:]) for part in weights]
        + [whole(extra.shape) for extra in extras],
        [
            whole((rows, width)),
            per_block((rows, 2 * LANES)),
            per_block((keys, 4 * LANES)),
            per_block((rows, 2 * LANES)),
            per_block((rows, LANES)),
        ],
        [
            shape((rows, width), jnp.float32),
            shape((blocks, rows, 2 * LANES), jnp.bfloat16),
            shape((blocks, keys, 4 * LANES), jnp.bfloat16),
            shape((blocks, rows, 2 * LANES), jnp.bfloat16),
            shape((blocks, rows, LANES), jnp.float32),
        ],
        [pltpu.VMEM((width, 6 * LANES), jnp.bfloat16)],
        flag,
        xq,
        xkv,
        *weights,
        *extras,
    )


def attend_back(flag, d_out, xq, xkv, weights, kept, extras, causal, first, count):
    rows, width = xq.shape
    keys = xkv.shape[0]
    return call(
        functools.partial(attend_back_kernel, causal),
        "attend_self_back" if causal else "attend_cross_back",
        10 * count,
        6 * 2**20 * count,
        count,
        [whole((rows, width)), whole((rows, width)), whole((keys, width))]
        + [per_block(part.shape[1:], first) for part in weights]
        + [
            per_block((rows, 2 * LANES), first),
            per_block((keys, 4 * LANES), first),
            per_block((rows, 2 * LANES), first),
            per_block((rows, LANES), first),
        ]
        + [whole(extra.shape) for extra in extras],
        [whole((rows, width)), whole((keys, width))] + [per_block(part.shape[1:]) for part in weights],
        [shape((rows, width), jnp.float32), shape((keys, width), jnp.float32)]
        + [shape((count,) + part.shape[1:], jnp.bfloat16) for part in weights],
        [
            pltpu.VMEM((width, 6 * LANES), jnp.bfloat16),
            pltpu.VMEM((keys, 4 * LANES), jnp.float32),
            pltpu.VMEM((rows, 2 * LANES), jnp.bfloat16),
            pltpu.VMEM((keys, 4 * LANES), jnp.bfloat16),
            pltpu.VMEM((width, 6 * LANES), jnp.bfloat16),
        ],
        flag,
        d_out,
        xq,
        xkv,
        *weights,
        *kept,
        *extras,
    )


def ffn_block(x_ref, w_ref, units, g_ref, slope_ref):
    inner = mul(x_ref[...], w_ref[:, :units])
    spread = 0.5 * (1.0 + lax.erf(inner * (0.5**0.5)))
    bell = jnp.exp(-0.5 * inner * inner) * 0.3989422804014327
    active = (inner * spread).astype(jnp.bfloat16)
    g_ref[0] = active
    slope_ref[0] = (spread + inner * bell).astype(jnp.bfloat16)
    return mul_nt(active, w_ref[:, units:])


def ffn_kernel(flag_ref, x_ref, *refs):
    own_refs, peer_refs = refs[:PARTS], refs[PARTS : 2 * PARTS]
    z_ref, g_ref, slope_ref, w_ref = refs[2 * PARTS :]
    assemble(flag_ref, own_refs, peer_refs, w_ref)
    out = ffn_block(x_ref, w_ref, own_refs[0].shape[2], g_ref, slope_ref)
    add_up(pl.program_id(0) == 0, z_ref, out)


def ffn(flag, x, weights):
    rows, width = x.shape
    blocks, _, units = weights[0].shape
    return call(
        ffn_kernel,
        "ffn",
        12,
        rows * units * blocks * 16,
        blocks,
        [whole((rows, width))] + [per_block(part.shape[1:]) for part in weights],
        [whole((rows, width)), per_block((rows, units)), per_block((rows, units))],
        [
            shape((rows, width), jnp.float32),
            shape((blocks, rows, units), jnp.bfloat16),
            shape((blocks, rows, units), jnp.bfloat16),
        ],
        [pltpu.VMEM((width, 2 * units), jnp.bfloat16)],
        flag,
        x,
        *weights,
    )


def ffn_back_block(dz_ref, w_ref, units, slope_ref, dh_ref):
    d_active = mul(dz_ref[...], w_ref[:, units:])
    d_inner = (d_active * slope_ref[0].astype(jnp.float32)).astype(jnp.bfloat16)
    dh_ref[0] = d_inner
    return mul_nt(d_inner, w_ref[:, :units])


def layer_norm(values, gain_row, bias_row):
    average = jnp.mean(values, axis=-1, keepdims=True)
    centered = values - average
    variance = jnp.mean(centered * centered, axis=-1, keepdims=True)
    return centered * lax.rsqrt(variance + NORM_EPS) * gain_row + bias_row


def norm_back(values, gain_row, bias_row, upstream):
    _, pullback = jax.vjp(layer_norm, values, gain_row, bias_row)
    return pullback(upstream)


def norm_parts(values):
    average = jnp.mean(values, axis=1, keepdims=True)
    centered = values - average
    scale = lax.rsqrt(jnp.mean(centered * centered, axis=1, keepdims=True) + NORM_EPS)
    return centered * scale, scale


def norm_gradients(values, gain_row, upstream):
    shaped, scale = norm_parts(values)
    inner = upstream * gain_row
    mean_inner = jnp.mean(inner, axis=1, keepdims=True)
    mean_product = jnp.mean(inner * shaped, axis=1, keepdims=True)
    d_values = scale * (inner - mean_inner - shaped * mean_product)
    d_gain = jnp.sum(upstream * shaped, axis=0, keepdims=True)
    return d_values, d_gain, jnp.sum(upstream, axis=0, keepdims=True)


def enc_out_back_kernel(
    flag_ref, arrived_ref, cot_ref, total_ref, norms_ref, d_dec_ref, enc_ref, dec_ref, *refs
):
    d_total_ref, dz_ref, sums_ref, keep_ref, send_ref, g_ref, left_t_ref = refs

    @pl.when(jnp.logical_and(pl.program_id(0) == 0, flag_ref[2] == 1))
    def _():
        upstream = arrived_ref[...].astype(jnp.float32) + cot_ref[...].astype(jnp.float32)
        d_total, sums_ref[0:1, :], sums_ref[1:2, :] = norm_gradients(total_ref[...], norms_ref[2:3, :], upstream)
        d_total_ref[...] = d_total
        dz_ref[...] = d_total.astype(jnp.bfloat16)

    @pl.when(jnp.logical_and(pl.program_id(0) == 0, flag_ref[2] == 0))
    def _():
        dz_ref[...] = d_dec_ref[...]

    @pl.when(pl.program_id(0) == 0)
    def _():
        left_t_ref[...] = dz_ref[...].T

    right = jnp.where(flag_ref[2] == 1, enc_ref[0], dec_ref[0])
    g_ref[...] = mul(left_t_ref[...], right).astype(jnp.bfloat16)
    hand_out(flag_ref, g_ref, keep_ref, send_ref)


def enc_out_back(flag, arrived, cot, total, norms, d_dec, enc_active, dec_active, like):
    rows, width = cot.shape
    blocks, _, units = enc_active.shape
    full = shape((rows, width), jnp.float32)
    return call(
        enc_out_back_kernel,
        "enc_out_back",
        9,
        rows * units * blocks * 8,
        blocks,
        [whole(item.shape) for item in (arrived, cot, total, norms, d_dec)]
        + [per_block((rows, units), 0, 2), per_block((rows, units), 0, 3)],
        [whole((rows, width))] * 2 + [whole((8, width))] + [per_block(like.shape[1:])] * 2,
        [full, shape((rows, width), jnp.bfloat16), shape((8, width), jnp.float32)]
        + [shape(like.shape, jnp.bfloat16)] * 2,
        [pltpu.VMEM((width, units), jnp.bfloat16), pltpu.VMEM((width, rows), jnp.bfloat16)],
        flag,
        arrived,
        cot,
        total,
        norms,
        d_dec,
        enc_active,
        dec_active,
    )


def enc_in_back_kernel(
    flag_ref, dz_ref, d_enc_ref, d_middle_ref, total_ref, gain_ref, middle_ref, crossed_ref, *refs
):
    first_own_ref, second_own_ref, first_peer_ref, second_peer_ref, slope_ref, dec_inner_ref, *refs = refs
    d_total_ref, d_low_ref, sums_ref, keep_ref, send_ref, w_ref, inner_ref, out_ref, g_ref, left_t_ref = refs
    step = pl.program_id(0)
    phase, at = step // 4, step % 4
    on_encoder = flag_ref[2] == 1

    @pl.when(jnp.logical_and(phase == 0, on_encoder))
    def _():
        assemble(flag_ref, [first_own_ref, second_own_ref], [first_peer_ref, second_peer_ref], w_ref)
        out = ffn_back_block(
            dz_ref, w_ref, first_own_ref.shape[2], slope_ref, inner_ref.at[pl.ds(at, 1)]
        )
        add_up(at == 0, out_ref, out)

    @pl.when(step == 3)
    def _():
        upstream = jnp.where(on_encoder, d_enc_ref[...] + out_ref[...], d_middle_ref[...])
        d_total, sums_ref[0:1, :], sums_ref[1:2, :] = norm_gradients(total_ref[...], gain_ref[0:1, :], upstream)
        d_total_ref[...] = d_total
        d_low_ref[...] = d_total.astype(jnp.bfloat16)
        left_t_ref[...] = jnp.where(on_encoder, middle_ref[...], crossed_ref[...]).T

    @pl.when(phase == 1)
    def _():
        right = jnp.where(on_encoder, inner_ref[at], dec_inner_ref[0])
        g_ref[...] = mul(left_t_ref[...], right).astype(jnp.bfloat16)
        hand_out(flag_ref, g_ref, keep_ref, send_ref)


def enc_in_back(flag, dz, d_enc, d_middle, total, gain, middle, crossed, feed, slope, dec_inner):
    rows, width = dz.shape
    blocks, half, units = feed[0].shape
    full = shape((rows, width), jnp.float32)

    def at_step(of, low, high, gate):
        def index(j, flag):
            return (jnp.where(j < 4, j if low == "up" else low, j - 4 if high == "up" else high) * flag[gate],) + (
                0,
            ) * len(of)

        return pl.BlockSpec((1,) + of, index)

    return call(
        enc_in_back_kernel,
        "enc_in_back",
        19,
        rows * units * blocks * 20,
        8,
        [whole(item.shape) for item in (dz, d_enc, d_middle, total, gain, middle, crossed)]
        + [at_step((half, units), "up", 3, 2)] * 4
        + [at_step((rows, units), "up", 3, 2), at_step((rows, units), 0, "up", 3)],
        [whole((rows, width))] * 2 + [whole((8, width))] + [at_step((half, units), 0, "up", 1)] * 2,
        [full, shape((rows, width), jnp.bfloat16), shape((8, width), jnp.float32)]
        + [shape(feed[0].shape, jnp.bfloat16)] * 2,
        [
            pltpu.VMEM((width, 2 * units), jnp.bfloat16),
            pltpu.VMEM((blocks, rows, units), jnp.bfloat16),
            pltpu.VMEM((rows, width), jnp.float32),
            pltpu.VMEM((width, units), jnp.bfloat16),
            pltpu.VMEM((width, rows), jnp.bfloat16),
        ],
        flag,
        dz,
        d_enc,
        d_middle,
        total,
        gain,
        middle,
        crossed,
        *feed,
        slope,
        dec_inner,
    )


def decoder_kernel(
    flag_ref,
    h1_ref,
    mem_a_ref,
    mem_b_ref,
    peer_a_ref,
    peer_b_ref,
    cot_ref,
    qx_ref,
    kx_ref,
    norms_ref,
    own_ref,
    peer_ref,
    first_own_ref,
    second_own_ref,
    first_peer_ref,
    second_peer_ref,
    decoded_ref,
    crossed_ref,
    d_dec_ref,
    d_middle_ref,
    mine_ref,
    other_ref,
    sums_ref,
    active_ref,
    inner_ref,
    keep_ref,
    send_ref,
    xq_ref,
    xkv_ref,
    wx_ref,
    wf_ref,
    q_ref,
    kv_ref,
    c_ref,
    l_ref,
    slope_ref,
    out_ref,
    total_ref,
    crossed_full_ref,
    upstream_ref,
    do_ref,
    dxkv_ref,
    *work,
):
    step = pl.program_id(0)
    phase, at = step // 4, step % 4
    first, last = at == 0, at == 3
    rows = h1_ref.shape[0]
    units = first_own_ref.shape[2]
    gain = [norms_ref[row : row + 1, :] for row in range(3)]
    bias = [norms_ref[3 + row : 4 + row, :] for row in range(3)]

    def kept(block):
        return tuple(ref.at[pl.ds(block, 1)] for ref in (q_ref, kv_ref, c_ref, l_ref))

    @pl.when(step == 0)
    def _():
        xq_ref[...] = h1_ref[...].astype(jnp.bfloat16)
        for part, ref in enumerate((mem_a_ref, mem_b_ref, peer_a_ref, peer_b_ref)):
            xkv_ref[part * rows // 2 : (part + 1) * rows // 2] = ref[...]

    @pl.when(jnp.logical_or(phase == 0, phase == 3))
    def _():
        assemble(flag_ref, [own_ref], [peer_ref], wx_ref)

    @pl.when(jnp.logical_or(phase == 1, phase == 2))
    def _():
        assemble(flag_ref, [first_own_ref, second_own_ref], [first_peer_ref, second_peer_ref], wf_ref)

    @pl.when(phase == 0)
    def _():
        add_up(first, out_ref, attend_block(False, xq_ref, xkv_ref, wx_ref, qx_ref, kx_ref, None, *kept(at)))

    @pl.when(jnp.logical_and(phase == 0, last))
    def _():
        total = h1_ref[...] + out_ref[...]
        total_ref[...] = total
        crossed = norm_parts(total)[0] * gain[1] + bias[1]
        crossed_full_ref[...] = crossed
        crossed_ref[...] = crossed.astype(jnp.bfloat16)

    @pl.when(phase == 1)
    def _():
        add_up(first, out_ref, ffn_block(crossed_ref, wf_ref, units, active_ref, slope_ref.at[pl.ds(at, 1)]))

    @pl.when(jnp.logical_and(phase == 1, last))
    def _():
        total = crossed_full_ref[...] + out_ref[...]
        decoded_ref[...] = (norm_parts(total)[0] * gain[2] + bias[2]).astype(jnp.bfloat16)
        d_total, sums_ref[0:1, :], sums_ref[1:2, :] = norm_gradients(
            total, gain[2], cot_ref[...].astype(jnp.float32)
        )
        upstream_ref[...] = d_total
        d_dec_ref[...] = d_total.astype(jnp.bfloat16)

    @pl.when(phase == 2)
    def _():
        add_up(first, out_ref, ffn_back_block(d_dec_ref, wf_ref, units, slope_ref.at[pl.ds(3 - at, 1)], inner_ref))

    @pl.when(jnp.logical_and(phase == 2, last))
    def _():
        d_total, sums_ref[2:3, :], sums_ref[3:4, :] = norm_gradients(
            total_ref[...], gain[1], upstream_ref[...] + out_ref[...]
        )
        upstream_ref[...] = d_total
        do_ref[...] = d_total.astype(jnp.bfloat16)

    @pl.when(phase == 3)
    def _():
        d_xq, d_xkv = attend_back_block(
            False, do_ref, xq_ref, xkv_ref, wx_ref, qx_ref, kx_ref, None, kept(3 - at), work
        )
        add_up(first, out_ref, d_xq)
        add_up(first, dxkv_ref, d_xkv)
        hand_out(flag_ref, work[3], keep_ref, send_ref)

    @pl.when(jnp.logical_and(phase == 3, last))
    def _():
        d_middle_ref[...] = upstream_ref[...] + out_ref[...]
        mine_ref[...] = dxkv_ref[:rows]
        other_ref[...] = dxkv_ref[rows:].astype(jnp.bfloat16)


def decoder(flag, h1, memory, cot, extras, norms, cross, feed):
    rows, width = h1.shape
    blocks, half, _ = cross[0].shape
    units = feed[0].shape[2]
    keys = 2 * rows
    qx, kx = extras

    def at_step(of, in_phase):
        def index(j, flag):
            at = j % 4
            choice = [{"up": at, "down": 3 - at}.get(way, way) for way in in_phase]
            chosen = choice[3]
            for phase in (2, 1, 0):
                chosen = jnp.where(j // 4 == phase, choice[phase], chosen)
            return (chosen * flag[1],) + (0,) * len(of)

        return pl.BlockSpec((1,) + of, index)

    part = (half, cross[0].shape[2])
    full = shape((rows, width), jnp.float32)
    rounded = shape((rows, width), jnp.bfloat16)
    return call(
        decoder_kernel,
        "decoder",
        90,
        40 * 2**20,
        16,
        [whole(item.shape) for item in (h1, *memory, cot, qx, kx, norms)]
        + [at_step(part, ("up", 3, 3, "down"))] * 2
        + [at_step((half, units), (0, "up", "down", 0))] * 4,
        [whole((rows, width))] * 6
        + [whole((8, width))]
        + [
            at_step((rows, units), (0, "up", 3, 3)),
            at_step((rows, units), (3, 3, "down", 0)),
            at_step(part, (3, 3, 3, "down")),
            at_step(part, (3, 3, 3, "down")),
        ],
        [rounded, rounded, rounded, full, full, rounded, shape((8, width), jnp.float32)]
        + [shape((blocks, rows, units), jnp.bfloat16)] * 2
        + [shape(cross[0].shape, jnp.bfloat16)] * 2,
        [
            pltpu.VMEM((rows, width), jnp.bfloat16),
            pltpu.VMEM((keys, width), jnp.bfloat16),
            pltpu.VMEM((width, 6 * LANES), jnp.bfloat16),
            pltpu.VMEM((width, 2 * units), jnp.bfloat16),
            pltpu.VMEM((blocks, rows, 2 * LANES), jnp.bfloat16),
            pltpu.VMEM((blocks, keys, 4 * LANES), jnp.bfloat16),
            pltpu.VMEM((blocks, rows, 2 * LANES), jnp.bfloat16),
            pltpu.VMEM((blocks, rows, LANES), jnp.float32),
            pltpu.VMEM((blocks, rows, units), jnp.bfloat16),
            pltpu.VMEM((rows, width), jnp.float32),
            pltpu.VMEM((rows, width), jnp.float32),
            pltpu.VMEM((rows, width), jnp.float32),
            pltpu.VMEM((rows, width), jnp.float32),
            pltpu.VMEM((rows, width), jnp.bfloat16),
            pltpu.VMEM((keys, width), jnp.float32),
            pltpu.VMEM((keys, 4 * LANES), jnp.float32),
            pltpu.VMEM((rows, 2 * LANES), jnp.bfloat16),
            pltpu.VMEM((keys, 4 * LANES), jnp.bfloat16),
            pltpu.VMEM((width, 6 * LANES), jnp.bfloat16),
        ],
        flag,
        h1,
        *memory,
        cot,
        qx,
        kx,
        norms,
        *cross,
        *feed,
    )


def low(values):
    return values.astype(jnp.bfloat16)


def axes_of(count):
    return ("section", "zh", "zl") + tuple("e%d" % at for at in range(count)) + ("ty", "tx")


def layer_of(place):
    return 1 ^ place["zh"] ^ place["zl"]


def moved(x, names, to):
    names = [name for name in axes_of(8) if name in names]

    def index(place):
        return sum(place[name] << (len(names) - 1 - at) for at, name in enumerate(names))

    pairs = []
    for source in range(2 ** len(names)):
        place = {name: source >> (len(names) - 1 - at) & 1 for at, name in enumerate(names)}
        target = to(place)
        if target is not None:
            pairs.append((source, index(target)))
    return lax.ppermute(x, tuple(names), pairs)


def over(x, *axes, layer=None):
    def to(place):
        if layer is not None and layer_of(place) != layer:
            return None
        return {**place, **{axis: 1 - place[axis] for axis in axes}}

    return moved(x, axes if layer is None else axes + Z, to)


Z = ("zh", "zl")


def swapped(x):
    def to(place):
        if place["section"] == layer_of(place):
            return place
        return {"section": 1 - place["section"], "zh": place["zh"], "zl": 1 - place["zl"]}

    return moved(x, ("section",) + Z, to)


def turned(x):
    return moved(x, ("section", "ty"), lambda place: {"section": place["ty"], "ty": place["section"]})


def sent_home(x, other):
    def to(place):
        return {
            "section": layer_of(place),
            "zh": place["zh"],
            "zl": 1 ^ place["zh"] ^ place["ty"],
            "ty": place["section"],
            "tx": place["tx"] ^ other,
        }

    return moved(x, ("section",) + Z + ("ty", "tx"), to)


def cross_in(x, layer):
    def to(place):
        if place["section"] != layer:
            return None
        return {"section": layer_of(place), "zh": place["zh"], "zl": place["zh"]}

    return moved(x, ("section",) + Z, to)


def cross_out(x, layer):
    def to(place):
        if layer_of(place) != 1:
            return None
        return {"section": layer, "zh": place["zh"], "zl": 1 ^ place["zh"] ^ place["section"]}

    return moved(x, ("section",) + Z, to)


def in_order(x, flag, axis):
    return jnp.where(flag == 1, jnp.flip(x, axis), x)


def pack_heads(query, key, value, out):
    pair = 2 * HDIM
    return jnp.concatenate(
        [
            query,
            value[:, pair:],
            key[:, :pair],
            value[:, :pair],
            key[:, pair:],
            out[:, pair:],
            out[:, :pair],
        ],
        axis=1,
    )


def unpack_heads(packed):
    part = [packed[:, at * HDIM : (at + 1) * HDIM] for at in range(12)]
    query = jnp.concatenate(part[0:3], axis=1)
    key = jnp.concatenate([part[4], part[5], part[8]], axis=1)
    value = jnp.concatenate([part[6], part[7], part[3]], axis=1)
    out = jnp.concatenate([part[10], part[11], part[9]], axis=1)
    return query, key, value, out


def after(x, *earlier):
    return lax.optimization_barrier((x,) + earlier)[0]


def plane_gathered(x, until=(), **only):
    parts = [x, over(x, "tx", **only), over(x, "ty", **only), over(x, "ty", "tx", **only)]
    return jnp.stack([after(part, *until) for part in parts])


def plane_summed(x, until=(), raw=None, **only):
    terms = [x[0], over(x[1], "tx", **only), over(x[2], "ty", **only), over(x[3], "ty", "tx", **only)]
    if raw is not None:
        raw.extend(terms[1:])
    terms = [after(term, *until) for term in terms]
    return low(sum(term.astype(jnp.float32) for term in terms))


def rows_gathered(x, count, until=(), raw=None, **only):
    for axes in [("e%d" % at,) for at in reversed(range(count))] + [Z]:
        got = over(x, *axes, **only)
        if raw is not None:
            raw.append(got)
        parts = [after(part, *until) for part in (x, got)]
        both = in_order(jnp.stack(parts, axis=-3), lax.axis_index(axes[0]), x.ndim - 2)
        x = both.reshape(x.shape[:-2] + (2 * x.shape[-2], x.shape[-1]))
    return x


def rows_summed(x, count, until=(), raw=None, **only):
    for axes in [Z] + [("e%d" % at,) for at in range(count)]:
        halves = x.reshape(x.shape[:-2] + (2, x.shape[-2] // 2, x.shape[-1]))
        halves = in_order(halves, lax.axis_index(axes[0]), x.ndim - 2)
        got = over(halves[..., 1, :, :], *axes, **only)
        if raw is not None:
            raw.append(got)
        x = plus(halves[..., 0, :, :], after(got, *until))
    return x


def plus(first, second):
    return low(first.astype(jnp.float32) + second.astype(jnp.float32))


def from_cores(keep, send, raw=None, **only):
    got = over(send, "section", **only)
    if raw is not None:
        raw.append(got)
    return plus(keep, got)


def body(
    count,
    hidden,
    cotangent,
    segments,
    sa_qkv,
    sa_out,
    cross_one,
    cross_two,
    ffn_in,
    ffn_out,
    norm_gain,
    norm_bias,
):
    core = lax.axis_index("section")
    x_at, y_at, zh_at, zl_at = (lax.axis_index(name) for name in ("tx", "ty", "zh", "zl"))
    layer = 1 ^ zh_at ^ zl_at
    on_encoder = layer == 0
    quarter = hidden.shape[3]
    enc_flag = jnp.stack([core, 1 - layer, 1 - layer, layer])
    dec_flag = jnp.stack([core, layer, 1 - layer, layer])
    flag = jnp.stack([core, jnp.ones_like(core), 1 - layer, layer])

    def pick(first, second):
        return jnp.where(on_encoder, first, second)

    def of_one_row(x):
        both = in_order(x[0, :, 0], x_at, 0)
        return in_order(jnp.stack([both[0], over(both[1], "tx")]), x_at, 0).reshape(2 * quarter, -1)

    def rows_out(x, raw=None):
        mine, other = in_order(x.reshape(2, quarter, -1), x_at, 0)
        both = [sent_home(mine, 0), sent_home(other, 1)]
        if raw is not None:
            raw.extend(both)
        return in_order(jnp.stack(both), x_at, 0)[None, :, None]

    units = ffn_in.shape[2]
    width = cross_one.shape[2]
    packed_self = pack_heads(sa_qkv[0, :, 0], sa_qkv[0, :, 1], sa_qkv[0, :, 2], sa_out[0])
    packed_ffn = jnp.concatenate([ffn_in[0], ffn_out[0].T], axis=1)
    with jax.named_scope("norms_in"):
        norms = swapped(jnp.concatenate([norm_gain[0], norm_bias[0]], axis=0))
        gains, biases = norms[:3], norms[3:]
        seg_own = segments[:, :, 0].astype(jnp.float32)
        seg_here = jnp.where(zl_at == 1 ^ zh_at ^ y_at, seg_own, over(seg_own, "zl")).astype(jnp.int32)
    with jax.named_scope("hidden_in"):
        one_row = of_one_row(hidden)
    with jax.named_scope("self_weights"):
        shard_self = swapped(packed_self)
    with jax.named_scope("hidden_in"):
        one_row = swapped(after(one_row, shard_self))
    with jax.named_scope("ffn_weights"):
        shard_ffn = swapped(after(packed_ffn, one_row))
        shard_first, shard_second = shard_ffn[:, :units], shard_ffn[:, units:]

    def both_rows(x):
        for_enc = rows_gathered(x, count, layer=0)
        return pick(for_enc, rows_gathered(after(x, for_enc), count, layer=1))

    with jax.named_scope("self_weights"):
        rows_self = both_rows(shard_self)
        own_self = plane_gathered(rows_self)
        w_self = [own_self, over(own_self, "section")]
    with jax.named_scope("hidden_in"):
        rows_here = turned(one_row)
        rows_all = jnp.concatenate([rows_here, over(rows_here, "section")], axis=0)
    with jax.named_scope("cross_weights"):
        cross_low = after(jnp.concatenate([cross_one[0], cross_two[0]], axis=1), own_self)
        pair_kv, pair_qo = cross_in(cross_low, 0), cross_in(cross_low, 1)
        packed = pack_heads(pair_qo[:, :width], pair_kv[:, :width], pair_kv[:, width:], pair_qo[:, width:])
    with jax.named_scope("ffn_weights"):
        rows_first = both_rows(after(shard_first, rows_self))
        plane_second = plane_gathered(after(shard_second, own_self))

    both_segments = in_order(seg_here, x_at, 1)[:, 0]
    ordered = in_order(both_segments.reshape(2, 2, 2 * quarter), core, 1).reshape(2, 4 * quarter)
    source_seg, target_seg = ordered[0], ordered[1]
    self_seg = pick(source_seg, target_seg)
    parts = jnp.arange(4)
    quarter_of = jnp.repeat(2 * ((parts // 2) ^ core) + parts % 2, quarter)
    lanes = jnp.arange(LANES)[None, :]

    def key_extras(seg):
        differs = jnp.logical_and(lanes < SEG_LANES, seg[:, None] != lanes)
        later = jnp.logical_and(
            jnp.logical_and(lanes >= SEG_LANES, lanes < PART_LANE),
            quarter_of[:, None] > lanes - SEG_LANES,
        )
        part = jnp.logical_and(lanes >= PART_LANE, lanes < PART_LANE + 3)
        return jnp.where(differs | later | part, 1.0, 0.0).astype(jnp.bfloat16)

    def query_extras(seg, causal):
        seg, at = seg[: 2 * quarter], quarter_of[: 2 * quarter]
        same = seg[:, None] == lanes
        here = jnp.logical_and(at[:, None] + SEG_LANES == lanes, causal)
        return jnp.where(same | here, MASKED, 0.0).astype(jnp.bfloat16)

    at_row = jnp.arange(quarter)
    later_key = jnp.logical_and(at_row[None, :] > at_row[:, None], jnp.logical_not(on_encoder))
    tri = jnp.where(later_key, MASKED, 0.0).astype(jnp.float32)
    self_extras = (query_extras(self_seg, jnp.logical_not(on_encoder)), key_extras(self_seg), tri)
    cross_extras = (query_extras(target_seg, False), key_extras(source_seg), tri)

    start = rows_all.astype(jnp.float32)
    start = pick(layer_norm(start, gains[0], biases[0]), start)
    start_here = start[: 2 * quarter]
    start_low = low(start)
    self_gain, self_bias = pick(gains[1], gains[0]), pick(biases[1], biases[0])
    with jax.named_scope("cotangent_in"):
        cot_row = swapped(of_one_row(after(cotangent, own_self)))
    self_out, *kept_self = attend(
        flag, start_low[: 2 * quarter], after(start_low, plane_second), w_self, self_extras, True
    )
    with jax.named_scope("ffn_weights"):
        own_first = plane_gathered(after(rows_first, plane_second), until=(self_out,))
        enc_second = rows_gathered(plane_second, count, until=(self_out,), layer=0)
        peer_first = over(own_first, "section")
        w_enc = [own_first, enc_second, peer_first, over(enc_second, "section", layer=0)]
    raw_second = []
    with jax.named_scope("ffn_weights"):
        dec_second = rows_gathered(after(plane_second, self_out), count, raw=raw_second, layer=1)
    with jax.named_scope("cotangent_in"):
        cot = turned(after(cot_row, self_out))
    self_total = start_here + after(self_out, *raw_second)
    middle = layer_norm(self_total, self_gain, self_bias)
    middle_low = low(middle)

    enc_out, enc_active, enc_slope = ffn(enc_flag, after(middle_low, cot), w_enc)
    enc_total = middle + enc_out
    encoded = low(layer_norm(enc_total, gains[2], biases[2]))
    def across(x, layer):
        return moved(x, Z, lambda place: {**place, "zl": 1 - place["zl"]} if layer_of(place) == layer else None)

    with jax.named_scope("memory"):
        memory_here = [across(encoded[:quarter], 0), across(encoded[quarter:], 0)]
        memory_peer = [over(part, "section", layer=1) for part in memory_here]
    with jax.named_scope("cross_weights"):
        rows_cross = rows_gathered(after(packed, plane_second), count, until=(self_out,), layer=1)
        own_cross = plane_gathered(rows_cross, until=tuple(memory_here), layer=1)
        w_cross = [own_cross, over(own_cross, "section", layer=1)]
    with jax.named_scope("ffn_weights"):
        w_dec = [own_first, dec_second, peer_first, over(dec_second, "section", layer=1)]

    (
        decoded,
        crossed_low,
        d_dec_low,
        d_middle_dec,
        d_memory_here,
        d_memory_other,
        dec_sums,
        dec_active,
        dec_inner,
        cross_keep,
        cross_send,
    ) = decoder(
        dec_flag, middle, memory_here + memory_peer, cot, cross_extras[:2], norms, w_cross, w_dec
    )
    with jax.named_scope("d_memory"):
        d_memory_here = d_memory_here + over(d_memory_other, "section", layer=1).astype(jnp.float32)
        d_memory_low = low(d_memory_here)
        arrived = across(d_memory_low, 1)
    with jax.named_scope("cross_sums"):
        cross_sum = from_cores(after(cross_keep, arrived), after(cross_send, arrived), layer=1)
        raw_cross = []
        cross_plane = plane_summed(cross_sum, raw=raw_cross, layer=1)

    d_enc_total, dz_low, enc_sums, second_keep, second_send = enc_out_back(
        flag, arrived, cot, enc_total, norms, d_dec_low, enc_active, dec_active, own_first
    )
    with jax.named_scope("ffn_sums"):
        raw_second_sum = []
        second_sum = from_cores(second_keep, second_send, raw=raw_second_sum)
    gain_row = jnp.broadcast_to(self_gain, (8, self_gain.shape[0]))
    d_self_total, d_self_low, self_norm, first_keep, first_send = enc_in_back(
        flag,
        after(dz_low, second_keep, cross_sum),
        d_enc_total,
        d_middle_dec,
        self_total,
        gain_row,
        middle_low,
        crossed_low,
        w_enc,
        enc_slope,
        dec_inner,
    )
    with jax.named_scope("ffn_sums"):
        gate = []
        second_plane = plane_summed(after(second_sum, d_self_low), raw=gate)
        first_sum = from_cores(after(first_keep, *raw_cross), after(first_send, *raw_cross), raw=gate)

    halves = []
    for first, earlier in ((0, ()), (2, gate)):
        halves.append(
            attend_back(
                flag,
                after(d_self_low, *earlier),
                start_low[: 2 * quarter],
                start_low,
                w_self,
                kept_self,
                self_extras,
                True,
                first,
                2,
            )
        )
    d_start_q = halves[0][0] + halves[1][0]
    with jax.named_scope("cross_sums"):
        share_cross = rows_summed(after(cross_plane, d_start_q), count, layer=1)
    with jax.named_scope("ffn_sums"):
        gate_later = []
        first_plane = plane_summed(after(first_sum, second_plane), raw=gate_later)
        second_share = rows_summed(second_plane, count, raw=gate_later)
    with jax.named_scope("self_sums"):
        (_, _, keep, send), (_, _, *later) = halves
        self_sum = [from_cores(after(keep, *gate), after(send, *gate), raw=gate_later)]
        raw_later = []
        self_sum.append(from_cores(*(after(part, *gate_later) for part in later), raw=raw_later))
        self_sum = jnp.concatenate(self_sum, axis=0)
    with jax.named_scope("hidden_out"):
        hidden_out = rows_out(after(pick(encoded, decoded), halves[1][0]))
    with jax.named_scope("d_start"):
        d_start_kv = after(halves[0][1], *raw_later) + halves[1][1]
        d_start = d_self_total + d_start_q + d_start_kv[: 2 * quarter]
        d_start = d_start + over(low(d_start_kv[2 * quarter :]), "section").astype(jnp.float32)
    d_source, gain_a, bias_a = norm_back(
        rows_here.astype(jnp.float32), gains[0], biases[0], d_start
    )

    norm_sums = jnp.stack(
        [
            pick(gain_a, self_norm[0]),
            pick(self_norm[0], dec_sums[2]),
            pick(enc_sums[0], dec_sums[0]),
            pick(bias_a, self_norm[1]),
            pick(self_norm[1], dec_sums[3]),
            pick(enc_sums[1], dec_sums[1]),
        ]
    )
    shards = 2**count
    sides = jnp.arange(2)
    held, outer = core ^ sides[:, None], sides[None, :]
    row_block = ((2 * outer + (1 ^ outer ^ held)) * shards)[:, :, None] + jnp.arange(shards)
    column_block = (2 * (y_at ^ sides)[:, None] + (x_at ^ sides)[None, :]).reshape(-1)
    order = (row_block.reshape(2, -1)[:, None, :] + 0) * 4 + column_block[:, None]
    norm_sums = jnp.take(norm_sums.reshape(6, 8 * 2 * shards, -1), order.reshape(-1), axis=1)
    norm_sums = norm_sums.reshape(6, 2, 4, 2 * shards, -1)
    with jax.named_scope("norm_sums"):
        norm_sums = norm_sums[:, 0] + over(norm_sums[:, 1], "section")
    with jax.named_scope("self_sums"):
        self_plane = plane_summed(self_sum)
    with jax.named_scope("norm_sums"):
        norm_blocks = after(norm_sums.transpose(1, 2, 0, 3).reshape(4, 2 * shards, -1), self_plane)
        norm_plane = norm_blocks[0] + over(norm_blocks[1], "tx") + over(norm_blocks[2], "ty")
        norm_plane = norm_plane + over(norm_blocks[3], "ty", "tx")
    norm_width = norm_plane.shape[1]
    with jax.named_scope("self_sums"):
        pad = ((0, 0), (0, 15), (0, self_plane.shape[1] - norm_width))
        both = jnp.concatenate(
            [
                self_plane.reshape(2 * shards, -1, self_plane.shape[1]),
                jnp.pad(low(norm_plane)[:, None], pad),
            ],
            axis=1,
        )
        raw_self = []
        share_self = rows_summed(both.reshape(-1, self_plane.shape[1]), count, raw=raw_self)
        share_self = swapped(share_self).astype(jnp.float32)
    norm_shares = share_self[-16, :norm_width].reshape(6, -1)
    share_self = share_self[:-16]
    with jax.named_scope("ffn_sums"):
        first_share = rows_summed(after(first_plane, *raw_later), count)
        share_ffn = swapped(jnp.concatenate([first_share, second_share], axis=1)).astype(jnp.float32)
    share_first, share_second = share_ffn[:, :units], share_ffn[:, units:].T
    with jax.named_scope("hidden_grad"):
        hidden_grad = rows_out(after(low(pick(d_source, d_start)), *raw_self)).astype(jnp.float32)
    g_query, g_key, g_value, g_out = unpack_heads(share_self)
    grad_qkv = jnp.stack([g_query, g_key, g_value], axis=1)
    c_query, c_key, c_value, c_out = unpack_heads(share_cross)
    with jax.named_scope("cross_out"):
        for_enc = cross_out(jnp.concatenate([c_key, c_value], axis=1), 0)
        for_dec = cross_out(jnp.concatenate([c_query, c_out], axis=1), 1)
    cross = jnp.where(core == 0, for_enc, for_dec).astype(jnp.float32)

    return (
        hidden_out,
        hidden_grad,
        grad_qkv[None],
        g_out[None],
        cross[None, :, :width],
        cross[None, :, width:],
        share_first[None],
        share_second[None],
        norm_shares[None, :3],
        norm_shares[None, 3:],
    )


def solution(mesh):
    _, dp_count, _ = mesh.devices.shape
    count = dp_count.bit_length() - 3
    names = axes_of(count)
    dp, tensor = names[1:-2], names[-2:]
    split = Mesh(mesh.devices.reshape((2,) * len(names)), names)
    rows = P("section", None, dp, tensor, None)
    in_specs = (
        rows,
        rows,
        P(None, None, dp, None),
        P("section", dp, None, tensor),
        P("section", dp, tensor),
        P("section", dp, tensor),
        P("section", dp, tensor),
        P("section", dp, tensor),
        P("section", tensor, dp),
        P("section", None, None),
        P("section", None, None),
    )
    out_specs = (
        rows,
        rows,
        P("section", dp, None, tensor),
        P("section", dp, tensor),
        P("section", dp, tensor),
        P("section", dp, tensor),
        P("section", dp, tensor),
        P("section", tensor, dp),
        P("section", None, dp + tensor),
        P("section", None, dp + tensor),
    )
    return jax.shard_map(
        functools.partial(body, count), mesh=split, in_specs=in_specs, out_specs=out_specs, check_vma=False
    )
```

```python
import functools

import jax
import jax.numpy as jnp
from jax import lax
from jax.experimental import pallas as pl
from jax.experimental.pallas import tpu as pltpu
from jax.sharding import Mesh
from jax.sharding import PartitionSpec as P

HDIM = 64
LANES = 128
MASKED = -1e30
NORM_EPS = 1e-05
VMEM_BYTES = 56 * 1024 * 1024

SEG_LANES = 8
PART_LANE = 12

PARTS = 2
TILE_ROWS = 256
HEADS = ((0, 1, 2, 0, 0), (0, 1, 2, 1, 1), (1, 3, 0, 0, 1))


def mul(a, b):
    return jnp.dot(a, b, preferred_element_type=jnp.float32)


def mul_nt(a, b):
    return lax.dot_general(a, b, (((1,), (1,)), ((), ())), preferred_element_type=jnp.float32)


def mul_tn(a, b):
    return lax.dot_general(a, b, (((0,), (0,)), ((), ())), preferred_element_type=jnp.float32)


def tile_of(values, index):
    return values[:, index * LANES : (index + 1) * LANES]


def lane_ids(rows):
    return lax.broadcasted_iota(jnp.int32, (rows, LANES), 1)


def half_mask(rows, half):
    lanes = lane_ids(rows)
    return lanes >= HDIM if half else lanes < HDIM


def in_parts(base, column):
    lanes = lane_ids(base.shape[0])
    high = column.astype(jnp.bfloat16).astype(jnp.float32)
    rest = column - high
    middle = rest.astype(jnp.bfloat16).astype(jnp.float32)
    low = rest - middle
    parts = jnp.where(
        lanes == PART_LANE,
        high,
        jnp.where(lanes == PART_LANE + 1, middle, jnp.where(lanes == PART_LANE + 2, low, base)),
    )
    return parts.astype(jnp.bfloat16)


def with_triangle(scores, tri, at):
    size = tri.shape[1]
    pieces = []
    if at > 0:
        pieces.append(scores[:, : at * size])
    pieces.append(scores[:, at * size : (at + 1) * size] + tri)
    pieces.append(scores[:, (at + 1) * size :])
    return jnp.concatenate(pieces, axis=1)


def places(core, block):
    return [pl.multiple_of((1 - core) * block, block), pl.multiple_of((2 + core) * block, block)]


def assemble(flag_ref, own_refs, peer_refs, w_ref):
    core, block = flag_ref[0], own_refs[0].shape[1] // 2
    for holder, refs in ((core, own_refs), (1 - core, peer_refs)):
        for part, ref in enumerate(refs):
            width = ref.shape[2]
            for at, place in enumerate(places(holder, block)):
                w_ref[pl.ds(place, block), part * width : (part + 1) * width] = ref[0, at * block : (at + 1) * block]


def hand_out(flag_ref, g_ref, keep_ref, send_ref):
    core, block = flag_ref[0], keep_ref.shape[1] // 2
    for holder, ref in ((core, keep_ref), (1 - core, send_ref)):
        for at, place in enumerate(places(holder, block)):
            ref[0, at * block : (at + 1) * block] = g_ref[pl.ds(place, block), :]


def where_active(kernel):
    def guarded(flag_ref, *refs):
        @pl.when(flag_ref[1] == 1)
        def _():
            kernel(flag_ref, *refs)

    return guarded


def scaled_queries(q_ref, at, q_tile, q_half):
    queries = q_ref[0, at, q_tile * LANES : (q_tile + 1) * LANES] * 0.125
    return jnp.where(half_mask(queries.shape[0], q_half), queries, 0).astype(jnp.bfloat16)


def units_of(total, rows):
    return [
        (slice(part * rows, (part + 1) * rows), part, head)
        for part in range(total // rows)
        for head in range(len(HEADS))
    ]


def attend_block(causal, xq_ref, xkv_ref, w_ref, qx_ref, kx_ref, tri_ref, q_ref, kv_ref, c_ref, l_ref):
    q_ref[0] = mul(xq_ref[...], w_ref[:, : 2 * LANES]).astype(jnp.bfloat16)
    kv_ref[0] = mul(xkv_ref[...], w_ref[:, LANES : 5 * LANES]).astype(jnp.bfloat16)
    rows = TILE_ROWS
    low = half_mask(rows, 0)

    def scores_of(at, part, head):
        q_tile, k_tile, _, q_half, _ = HEADS[head]
        keys = kv_ref[0, :, k_tile * LANES : (k_tile + 1) * LANES]
        scores = mul_nt(
            jnp.concatenate([scaled_queries(q_ref, at, q_tile, q_half), qx_ref[at, :]], axis=1),
            jnp.concatenate([keys, kx_ref[...]], axis=1),
        )
        return with_triangle(scores, tri_ref[...], part) if causal else scores

    units = units_of(q_ref.shape[1], rows)
    ahead = scores_of(*units[0])
    contexts, totals = [], None
    for index, (at, part, head) in enumerate(units):
        scores = ahead
        if index + 1 < len(units):
            ahead = scores_of(*units[index + 1])
        v_tile = HEADS[head][2]
        values = kv_ref[0, :, v_tile * LANES : (v_tile + 1) * LANES]
        highest = jnp.max(scores, axis=1, keepdims=True)
        weights = jnp.exp(scores - highest)
        sums = jnp.sum(weights, axis=1, keepdims=True)
        contexts.append(mul(weights.astype(jnp.bfloat16), values) / sums)
        logs = jnp.broadcast_to(highest + jnp.log(sums), (rows, LANES))
        totals = logs if head == 0 else jnp.where(lane_ids(rows) == head, logs, totals)
        if head == len(HEADS) - 1:
            c_ref[0, at, :LANES] = jnp.where(low, 0, contexts[2]).astype(jnp.bfloat16)
            c_ref[0, at, LANES:] = jnp.where(low, contexts[0], contexts[1]).astype(jnp.bfloat16)
            l_ref[0, at, :] = totals
            contexts = []
    return mul_nt(c_ref[0], w_ref[:, 4 * LANES :])


def attend_kernel(causal, flag_ref, xq_ref, xkv_ref, own_ref, peer_ref, qx_ref, kx_ref, tri_ref, o_ref, *refs):
    q_ref, kv_ref, c_ref, l_ref, w_ref = refs
    assemble(flag_ref, [own_ref], [peer_ref], w_ref)
    out = attend_block(causal, xq_ref, xkv_ref, w_ref, qx_ref, kx_ref, tri_ref, q_ref, kv_ref, c_ref, l_ref)
    add_up(pl.program_id(0) == 0, o_ref, out)


def add_up(first, ref, value):
    @pl.when(first)
    def _():
        ref[...] = value

    @pl.when(jnp.logical_not(first))
    def _():
        ref[...] += value


def attend_back_block(causal, do_ref, xq_ref, xkv_ref, w_ref, qx_ref, kx_ref, tri_ref, kept, work):
    q_ref, kv_ref, c_ref, l_ref = kept
    sum_ref, dq_ref, dkv_ref, g_ref = work
    rows = TILE_ROWS
    d_context = mul(do_ref[...], w_ref[:, 4 * LANES :]).astype(jnp.bfloat16)
    low = half_mask(rows, 0)

    def products_of(at, part, head):
        q_tile, k_tile, v_tile, q_half, v_half = HEADS[head]
        c_tile = 0 if head == 2 else 1
        keys = kv_ref[0, :, k_tile * LANES : (k_tile + 1) * LANES]
        values = kv_ref[0, :, v_tile * LANES : (v_tile + 1) * LANES]
        queries = scaled_queries(q_ref, at, q_tile, q_half)
        d_rows = jnp.where(half_mask(rows, v_half), tile_of(d_context[at], c_tile), 0).astype(jnp.bfloat16)
        total = l_ref[0, at, head : head + 1]
        scores = mul_nt(
            jnp.concatenate([queries, in_parts(qx_ref[at, :].astype(jnp.float32), -total)], axis=1),
            jnp.concatenate([keys, kx_ref[...]], axis=1),
        )
        if causal:
            scores = with_triangle(scores, tri_ref[...], part)
        return scores, mul_nt(d_rows, values), queries, d_rows, keys

    units = units_of(q_ref.shape[1], rows)
    ahead = products_of(*units[0])
    d_queries = []
    for index, (at, part, head) in enumerate(units):
        scores, d_probs, queries, d_rows, keys = ahead
        if index + 1 < len(units):
            ahead = products_of(*units[index + 1])
        _, k_tile, v_tile, _, _ = HEADS[head]
        probs = jnp.exp(scores)
        inner = jnp.sum(probs * d_probs, axis=1, keepdims=True)
        d_scores = (probs * (d_probs - inner)).astype(jnp.bfloat16)
        d_values = mul_tn(probs.astype(jnp.bfloat16), d_rows)
        d_keys = mul_tn(d_scores, queries)
        d_queries.append(mul(d_scores, keys) * 0.125)
        k_at = slice(k_tile * LANES, (k_tile + 1) * LANES)
        v_at = slice(v_tile * LANES, (v_tile + 1) * LANES)
        if part == 0 and head != 1:
            sum_ref[:, k_at] = d_keys
            sum_ref[:, v_at] = d_values
        else:
            sum_ref[:, k_at] += d_keys
            sum_ref[:, v_at] += d_values
        if head == len(HEADS) - 1:
            dq_ref[at, :LANES] = jnp.where(low, d_queries[0], d_queries[1]).astype(jnp.bfloat16)
            dq_ref[at, LANES:] = jnp.where(low, d_queries[2], 0).astype(jnp.bfloat16)
            d_queries = []
    dkv_ref[...] = sum_ref[...].astype(jnp.bfloat16)
    d_xq = mul_nt(dq_ref[...], w_ref[:, : 2 * LANES])
    d_xkv = mul_nt(dkv_ref[...], w_ref[:, LANES : 5 * LANES])

    grad_q = mul_tn(xq_ref[...], dq_ref[...])
    grad_kv = mul_tn(xkv_ref[...], dkv_ref[...])
    grad_o = mul_tn(do_ref[...], c_ref[0])
    g_ref[:, :LANES] = grad_q[:, :LANES].astype(jnp.bfloat16)
    g_ref[:, LANES : 2 * LANES] = (grad_q[:, LANES:] + grad_kv[:, :LANES]).astype(jnp.bfloat16)
    g_ref[:, 2 * LANES : 4 * LANES] = grad_kv[:, LANES : 3 * LANES].astype(jnp.bfloat16)
    g_ref[:, 4 * LANES : 5 * LANES] = (grad_kv[:, 3 * LANES :] + grad_o[:, :LANES]).astype(jnp.bfloat16)
    g_ref[:, 5 * LANES :] = grad_o[:, LANES:].astype(jnp.bfloat16)
    return d_xq, d_xkv


def attend_back_kernel(causal, flag_ref, do_ref, xq_ref, xkv_ref, own_ref, peer_ref, *refs):
    kept, (qx_ref, kx_ref, tri_ref, dxq_ref, dxkv_ref, keep_ref, send_ref, w_ref) = refs[:4], refs[4:12]
    work = refs[12:]
    assemble(flag_ref, [own_ref], [peer_ref], w_ref)
    d_xq, d_xkv = attend_back_block(
        causal, do_ref, xq_ref, xkv_ref, w_ref, qx_ref, kx_ref, tri_ref, kept, work
    )
    add_up(pl.program_id(0) == 0, dxq_ref, d_xq)
    add_up(pl.program_id(0) == 0, dxkv_ref, d_xkv)
    hand_out(flag_ref, work[3], keep_ref, send_ref)


def whole(shape):
    return pl.BlockSpec(shape, lambda j, flag: (0,) * len(shape))


def per_block(shape, first=0, gate=1):
    return pl.BlockSpec((1,) + shape, lambda j, flag: (first + j * flag[gate],) + (0,) * len(shape))


shape = jax.ShapeDtypeStruct


def call(kernel, name, micros, moved, grid, in_specs, out_specs, out_shape, scratch, *operands):
    return pl.pallas_call(
        where_active(kernel),
        grid_spec=pltpu.PrefetchScalarGridSpec(
            num_scalar_prefetch=1,
            grid=(grid,),
            in_specs=in_specs,
            out_specs=out_specs,
            scratch_shapes=scratch,
        ),
        out_shape=out_shape,
        compiler_params=pltpu.CompilerParams(vmem_limit_bytes=VMEM_BYTES),
        cost_estimate=cost(micros, moved),
        name=name,
    )(*operands)


def cost(micros, moved):
    return pl.CostEstimate(flops=int(micros * 1.15e9), bytes_accessed=int(moved), transcendentals=0)


def attend(flag, xq, xkv, weights, extras, causal):
    rows, width = xq.shape
    keys = xkv.shape[0]
    blocks = weights[0].shape[0]
    return call(
        functools.partial(attend_kernel, causal),
        "attend_self" if causal else "attend_cross",
        20,
        24 * 2**20,
        blocks,
        [whole((rows, width)), whole((keys, width))]
        + [per_block(part.shape[1:]) for part in weights]
        + [whole(extra.shape) for extra in extras],
        [
            whole((rows, width)),
            per_block((rows, 2 * LANES)),
            per_block((keys, 4 * LANES)),
            per_block((rows, 2 * LANES)),
            per_block((rows, LANES)),
        ],
        [
            shape((rows, width), jnp.float32),
            shape((blocks, rows, 2 * LANES), jnp.bfloat16),
            shape((blocks, keys, 4 * LANES), jnp.bfloat16),
            shape((blocks, rows, 2 * LANES), jnp.bfloat16),
            shape((blocks, rows, LANES), jnp.float32),
        ],
        [pltpu.VMEM((width, 6 * LANES), jnp.bfloat16)],
        flag,
        xq,
        xkv,
        *weights,
        *extras,
    )


def attend_back(flag, d_out, xq, xkv, weights, kept, extras, causal, first, count):
    rows, width = xq.shape
    keys = xkv.shape[0]
    return call(
        functools.partial(attend_back_kernel, causal),
        "attend_self_back" if causal else "attend_cross_back",
        10 * count,
        6 * 2**20 * count,
        count,
        [whole((rows, width)), whole((rows, width)), whole((keys, width))]
        + [per_block(part.shape[1:], first) for part in weights]
        + [
            per_block((rows, 2 * LANES), first),
            per_block((keys, 4 * LANES), first),
            per_block((rows, 2 * LANES), first),
            per_block((rows, LANES), first),
        ]
        + [whole(extra.shape) for extra in extras],
        [whole((rows, width)), whole((keys, width))] + [per_block(part.shape[1:]) for part in weights],
        [shape((rows, width), jnp.float32), shape((keys, width), jnp.float32)]
        + [shape((count,) + part.shape[1:], jnp.bfloat16) for part in weights],
        [
            pltpu.VMEM((width, 6 * LANES), jnp.bfloat16),
            pltpu.VMEM((keys, 4 * LANES), jnp.float32),
            pltpu.VMEM((rows, 2 * LANES), jnp.bfloat16),
            pltpu.VMEM((keys, 4 * LANES), jnp.bfloat16),
            pltpu.VMEM((width, 6 * LANES), jnp.bfloat16),
        ],
        flag,
        d_out,
        xq,
        xkv,
        *weights,
        *kept,
        *extras,
    )


def ffn_block(x_ref, w_ref, units, g_ref, slope_ref):
    inner = mul(x_ref[...], w_ref[:, :units])
    spread = 0.5 * (1.0 + lax.erf(inner * (0.5**0.5)))
    bell = jnp.exp(-0.5 * inner * inner) * 0.3989422804014327
    active = (inner * spread).astype(jnp.bfloat16)
    g_ref[0] = active
    slope_ref[0] = (spread + inner * bell).astype(jnp.bfloat16)
    return mul_nt(active, w_ref[:, units:])


def ffn_kernel(flag_ref, x_ref, *refs):
    own_refs, peer_refs = refs[:PARTS], refs[PARTS : 2 * PARTS]
    z_ref, g_ref, slope_ref, w_ref = refs[2 * PARTS :]
    assemble(flag_ref, own_refs, peer_refs, w_ref)
    out = ffn_block(x_ref, w_ref, own_refs[0].shape[2], g_ref, slope_ref)
    add_up(pl.program_id(0) == 0, z_ref, out)


def ffn(flag, x, weights):
    rows, width = x.shape
    blocks, _, units = weights[0].shape
    return call(
        ffn_kernel,
        "ffn",
        12,
        rows * units * blocks * 16,
        blocks,
        [whole((rows, width))] + [per_block(part.shape[1:]) for part in weights],
        [whole((rows, width)), per_block((rows, units)), per_block((rows, units))],
        [
            shape((rows, width), jnp.float32),
            shape((blocks, rows, units), jnp.bfloat16),
            shape((blocks, rows, units), jnp.bfloat16),
        ],
        [pltpu.VMEM((width, 2 * units), jnp.bfloat16)],
        flag,
        x,
        *weights,
    )


def ffn_back_block(dz_ref, w_ref, units, slope_ref, dh_ref):
    d_active = mul(dz_ref[...], w_ref[:, units:])
    d_inner = (d_active * slope_ref[0].astype(jnp.float32)).astype(jnp.bfloat16)
    dh_ref[0] = d_inner
    return mul_nt(d_inner, w_ref[:, :units])


def layer_norm(values, gain_row, bias_row):
    average = jnp.mean(values, axis=-1, keepdims=True)
    centered = values - average
    variance = jnp.mean(centered * centered, axis=-1, keepdims=True)
    return centered * lax.rsqrt(variance + NORM_EPS) * gain_row + bias_row


def norm_back(values, gain_row, bias_row, upstream):
    _, pullback = jax.vjp(layer_norm, values, gain_row, bias_row)
    return pullback(upstream)


def norm_parts(values):
    average = jnp.mean(values, axis=1, keepdims=True)
    centered = values - average
    scale = lax.rsqrt(jnp.mean(centered * centered, axis=1, keepdims=True) + NORM_EPS)
    return centered * scale, scale


def norm_gradients(values, gain_row, upstream):
    shaped, scale = norm_parts(values)
    inner = upstream * gain_row
    mean_inner = jnp.mean(inner, axis=1, keepdims=True)
    mean_product = jnp.mean(inner * shaped, axis=1, keepdims=True)
    d_values = scale * (inner - mean_inner - shaped * mean_product)
    d_gain = jnp.sum(upstream * shaped, axis=0, keepdims=True)
    return d_values, d_gain, jnp.sum(upstream, axis=0, keepdims=True)


def enc_out_back_kernel(
    flag_ref, arrived_ref, cot_ref, total_ref, norms_ref, d_dec_ref, enc_ref, dec_ref, *refs
):
    d_total_ref, dz_ref, sums_ref, keep_ref, send_ref, g_ref, left_t_ref = refs

    @pl.when(jnp.logical_and(pl.program_id(0) == 0, flag_ref[2] == 1))
    def _():
        upstream = arrived_ref[...].astype(jnp.float32) + cot_ref[...].astype(jnp.float32)
        d_total, sums_ref[0:1, :], sums_ref[1:2, :] = norm_gradients(total_ref[...], norms_ref[2:3, :], upstream)
        d_total_ref[...] = d_total
        dz_ref[...] = d_total.astype(jnp.bfloat16)

    @pl.when(jnp.logical_and(pl.program_id(0) == 0, flag_ref[2] == 0))
    def _():
        dz_ref[...] = d_dec_ref[...]

    @pl.when(pl.program_id(0) == 0)
    def _():
        left_t_ref[...] = dz_ref[...].T

    right = jnp.where(flag_ref[2] == 1, enc_ref[0], dec_ref[0])
    g_ref[...] = mul(left_t_ref[...], right).astype(jnp.bfloat16)
    hand_out(flag_ref, g_ref, keep_ref, send_ref)


def enc_out_back(flag, arrived, cot, total, norms, d_dec, enc_active, dec_active, like):
    rows, width = cot.shape
    blocks, _, units = enc_active.shape
    full = shape((rows, width), jnp.float32)
    return call(
        enc_out_back_kernel,
        "enc_out_back",
        9,
        rows * units * blocks * 8,
        blocks,
        [whole(item.shape) for item in (arrived, cot, total, norms, d_dec)]
        + [per_block((rows, units), 0, 2), per_block((rows, units), 0, 3)],
        [whole((rows, width))] * 2 + [whole((8, width))] + [per_block(like.shape[1:])] * 2,
        [full, shape((rows, width), jnp.bfloat16), shape((8, width), jnp.float32)]
        + [shape(like.shape, jnp.bfloat16)] * 2,
        [pltpu.VMEM((width, units), jnp.bfloat16), pltpu.VMEM((width, rows), jnp.bfloat16)],
        flag,
        arrived,
        cot,
        total,
        norms,
        d_dec,
        enc_active,
        dec_active,
    )


def enc_in_back_kernel(
    flag_ref, dz_ref, d_enc_ref, d_middle_ref, total_ref, gain_ref, middle_ref, crossed_ref, *refs
):
    first_own_ref, second_own_ref, first_peer_ref, second_peer_ref, slope_ref, dec_inner_ref, *refs = refs
    d_total_ref, d_low_ref, sums_ref, keep_ref, send_ref, w_ref, inner_ref, out_ref, g_ref, left_t_ref = refs
    step = pl.program_id(0)
    phase, at = step // 4, step % 4
    on_encoder = flag_ref[2] == 1

    @pl.when(jnp.logical_and(phase == 0, on_encoder))
    def _():
        assemble(flag_ref, [first_own_ref, second_own_ref], [first_peer_ref, second_peer_ref], w_ref)
        out = ffn_back_block(
            dz_ref, w_ref, first_own_ref.shape[2], slope_ref, inner_ref.at[pl.ds(at, 1)]
        )
        add_up(at == 0, out_ref, out)

    @pl.when(step == 3)
    def _():
        upstream = jnp.where(on_encoder, d_enc_ref[...] + out_ref[...], d_middle_ref[...])
        d_total, sums_ref[0:1, :], sums_ref[1:2, :] = norm_gradients(total_ref[...], gain_ref[0:1, :], upstream)
        d_total_ref[...] = d_total
        d_low_ref[...] = d_total.astype(jnp.bfloat16)
        left_t_ref[...] = jnp.where(on_encoder, middle_ref[...], crossed_ref[...]).T

    @pl.when(phase == 1)
    def _():
        right = jnp.where(on_encoder, inner_ref[at], dec_inner_ref[0])
        g_ref[...] = mul(left_t_ref[...], right).astype(jnp.bfloat16)
        hand_out(flag_ref, g_ref, keep_ref, send_ref)


def enc_in_back(flag, dz, d_enc, d_middle, total, gain, middle, crossed, feed, slope, dec_inner):
    rows, width = dz.shape
    blocks, half, units = feed[0].shape
    full = shape((rows, width), jnp.float32)

    def at_step(of, low, high, gate):
        def index(j, flag):
            return (jnp.where(j < 4, j if low == "up" else low, j - 4 if high == "up" else high) * flag[gate],) + (
                0,
            ) * len(of)

        return pl.BlockSpec((1,) + of, index)

    return call(
        enc_in_back_kernel,
        "enc_in_back",
        19,
        rows * units * blocks * 20,
        8,
        [whole(item.shape) for item in (dz, d_enc, d_middle, total, gain, middle, crossed)]
        + [at_step((half, units), "up", 3, 2)] * 4
        + [at_step((rows, units), "up", 3, 2), at_step((rows, units), 0, "up", 3)],
        [whole((rows, width))] * 2 + [whole((8, width))] + [at_step((half, units), 0, "up", 1)] * 2,
        [full, shape((rows, width), jnp.bfloat16), shape((8, width), jnp.float32)]
        + [shape(feed[0].shape, jnp.bfloat16)] * 2,
        [
            pltpu.VMEM((width, 2 * units), jnp.bfloat16),
            pltpu.VMEM((blocks, rows, units), jnp.bfloat16),
            pltpu.VMEM((rows, width), jnp.float32),
            pltpu.VMEM((width, units), jnp.bfloat16),
            pltpu.VMEM((width, rows), jnp.bfloat16),
        ],
        flag,
        dz,
        d_enc,
        d_middle,
        total,
        gain,
        middle,
        crossed,
        *feed,
        slope,
        dec_inner,
    )


def decoder_kernel(
    flag_ref,
    h1_ref,
    mem_a_ref,
    mem_b_ref,
    peer_a_ref,
    peer_b_ref,
    cot_ref,
    qx_ref,
    kx_ref,
    norms_ref,
    own_ref,
    peer_ref,
    first_own_ref,
    second_own_ref,
    first_peer_ref,
    second_peer_ref,
    decoded_ref,
    crossed_ref,
    d_dec_ref,
    d_middle_ref,
    mine_ref,
    other_ref,
    sums_ref,
    active_ref,
    inner_ref,
    keep_ref,
    send_ref,
    xq_ref,
    xkv_ref,
    wx_ref,
    wf_ref,
    q_ref,
    kv_ref,
    c_ref,
    l_ref,
    slope_ref,
    out_ref,
    total_ref,
    crossed_full_ref,
    upstream_ref,
    do_ref,
    dxkv_ref,
    *work,
):
    step = pl.program_id(0)
    phase, at = step // 4, step % 4
    first, last = at == 0, at == 3
    rows = h1_ref.shape[0]
    units = first_own_ref.shape[2]
    gain = [norms_ref[row : row + 1, :] for row in range(3)]
    bias = [norms_ref[3 + row : 4 + row, :] for row in range(3)]

    def kept(block):
        return tuple(ref.at[pl.ds(block, 1)] for ref in (q_ref, kv_ref, c_ref, l_ref))

    @pl.when(step == 0)
    def _():
        xq_ref[...] = h1_ref[...].astype(jnp.bfloat16)
        for part, ref in enumerate((mem_a_ref, mem_b_ref, peer_a_ref, peer_b_ref)):
            xkv_ref[part * rows // 2 : (part + 1) * rows // 2] = ref[...]

    @pl.when(jnp.logical_or(phase == 0, phase == 3))
    def _():
        assemble(flag_ref, [own_ref], [peer_ref], wx_ref)

    @pl.when(jnp.logical_or(phase == 1, phase == 2))
    def _():
        assemble(flag_ref, [first_own_ref, second_own_ref], [first_peer_ref, second_peer_ref], wf_ref)

    @pl.when(phase == 0)
    def _():
        add_up(first, out_ref, attend_block(False, xq_ref, xkv_ref, wx_ref, qx_ref, kx_ref, None, *kept(at)))

    @pl.when(jnp.logical_and(phase == 0, last))
    def _():
        total = h1_ref[...] + out_ref[...]
        total_ref[...] = total
        crossed = norm_parts(total)[0] * gain[1] + bias[1]
        crossed_full_ref[...] = crossed
        crossed_ref[...] = crossed.astype(jnp.bfloat16)

    @pl.when(phase == 1)
    def _():
        add_up(first, out_ref, ffn_block(crossed_ref, wf_ref, units, active_ref, slope_ref.at[pl.ds(at, 1)]))

    @pl.when(jnp.logical_and(phase == 1, last))
    def _():
        total = crossed_full_ref[...] + out_ref[...]
        decoded_ref[...] = (norm_parts(total)[0] * gain[2] + bias[2]).astype(jnp.bfloat16)
        d_total, sums_ref[0:1, :], sums_ref[1:2, :] = norm_gradients(
            total, gain[2], cot_ref[...].astype(jnp.float32)
        )
        upstream_ref[...] = d_total
        d_dec_ref[...] = d_total.astype(jnp.bfloat16)

    @pl.when(phase == 2)
    def _():
        add_up(first, out_ref, ffn_back_block(d_dec_ref, wf_ref, units, slope_ref.at[pl.ds(3 - at, 1)], inner_ref))

    @pl.when(jnp.logical_and(phase == 2, last))
    def _():
        d_total, sums_ref[2:3, :], sums_ref[3:4, :] = norm_gradients(
            total_ref[...], gain[1], upstream_ref[...] + out_ref[...]
        )
        upstream_ref[...] = d_total
        do_ref[...] = d_total.astype(jnp.bfloat16)

    @pl.when(phase == 3)
    def _():
        d_xq, d_xkv = attend_back_block(
            False, do_ref, xq_ref, xkv_ref, wx_ref, qx_ref, kx_ref, None, kept(3 - at), work
        )
        add_up(first, out_ref, d_xq)
        add_up(first, dxkv_ref, d_xkv)
        hand_out(flag_ref, work[3], keep_ref, send_ref)

    @pl.when(jnp.logical_and(phase == 3, last))
    def _():
        d_middle_ref[...] = upstream_ref[...] + out_ref[...]
        mine_ref[...] = dxkv_ref[:rows]
        other_ref[...] = dxkv_ref[rows:].astype(jnp.bfloat16)


def decoder(flag, h1, memory, cot, extras, norms, cross, feed):
    rows, width = h1.shape
    blocks, half, _ = cross[0].shape
    units = feed[0].shape[2]
    keys = 2 * rows
    qx, kx = extras

    def at_step(of, in_phase):
        def index(j, flag):
            at = j % 4
            choice = [{"up": at, "down": 3 - at}.get(way, way) for way in in_phase]
            chosen = choice[3]
            for phase in (2, 1, 0):
                chosen = jnp.where(j // 4 == phase, choice[phase], chosen)
            return (chosen * flag[1],) + (0,) * len(of)

        return pl.BlockSpec((1,) + of, index)

    part = (half, cross[0].shape[2])
    full = shape((rows, width), jnp.float32)
    rounded = shape((rows, width), jnp.bfloat16)
    return call(
        decoder_kernel,
        "decoder",
        90,
        40 * 2**20,
        16,
        [whole(item.shape) for item in (h1, *memory, cot, qx, kx, norms)]
        + [at_step(part, ("up", 3, 3, "down"))] * 2
        + [at_step((half, units), (0, "up", "down", 0))] * 4,
        [whole((rows, width))] * 6
        + [whole((8, width))]
        + [
            at_step((rows, units), (0, "up", 3, 3)),
            at_step((rows, units), (3, 3, "down", 0)),
            at_step(part, (3, 3, 3, "down")),
            at_step(part, (3, 3, 3, "down")),
        ],
        [rounded, rounded, rounded, full, full, rounded, shape((8, width), jnp.float32)]
        + [shape((blocks, rows, units), jnp.bfloat16)] * 2
        + [shape(cross[0].shape, jnp.bfloat16)] * 2,
        [
            pltpu.VMEM((rows, width), jnp.bfloat16),
            pltpu.VMEM((keys, width), jnp.bfloat16),
            pltpu.VMEM((width, 6 * LANES), jnp.bfloat16),
            pltpu.VMEM((width, 2 * units), jnp.bfloat16),
            pltpu.VMEM((blocks, rows, 2 * LANES), jnp.bfloat16),
            pltpu.VMEM((blocks, keys, 4 * LANES), jnp.bfloat16),
            pltpu.VMEM((blocks, rows, 2 * LANES), jnp.bfloat16),
            pltpu.VMEM((blocks, rows, LANES), jnp.float32),
            pltpu.VMEM((blocks, rows, units), jnp.bfloat16),
            pltpu.VMEM((rows, width), jnp.float32),
            pltpu.VMEM((rows, width), jnp.float32),
            pltpu.VMEM((rows, width), jnp.float32),
            pltpu.VMEM((rows, width), jnp.float32),
            pltpu.VMEM((rows, width), jnp.bfloat16),
            pltpu.VMEM((keys, width), jnp.float32),
            pltpu.VMEM((keys, 4 * LANES), jnp.float32),
            pltpu.VMEM((rows, 2 * LANES), jnp.bfloat16),
            pltpu.VMEM((keys, 4 * LANES), jnp.bfloat16),
            pltpu.VMEM((width, 6 * LANES), jnp.bfloat16),
        ],
        flag,
        h1,
        *memory,
        cot,
        qx,
        kx,
        norms,
        *cross,
        *feed,
    )


def low(values):
    return values.astype(jnp.bfloat16)


def axes_of(count):
    return ("section", "zh", "zl") + tuple("e%d" % at for at in range(count)) + ("ty", "tx")


def layer_of(place):
    return 1 ^ place["zh"] ^ place["zl"]


def moved(x, names, to):
    names = [name for name in axes_of(8) if name in names]

    def index(place):
        return sum(place[name] << (len(names) - 1 - at) for at, name in enumerate(names))

    pairs = []
    for source in range(2 ** len(names)):
        place = {name: source >> (len(names) - 1 - at) & 1 for at, name in enumerate(names)}
        target = to(place)
        if target is not None:
            pairs.append((source, index(target)))
    return lax.ppermute(x, tuple(names), pairs)


def over(x, *axes, layer=None):
    def to(place):
        if layer is not None and layer_of(place) != layer:
            return None
        return {**place, **{axis: 1 - place[axis] for axis in axes}}

    return moved(x, axes if layer is None else axes + Z, to)


Z = ("zh", "zl")


def swapped(x):
    def to(place):
        if place["section"] == layer_of(place):
            return place
        return {"section": 1 - place["section"], "zh": place["zh"], "zl": 1 - place["zl"]}

    return moved(x, ("section",) + Z, to)


def turned(x):
    return moved(x, ("section", "ty"), lambda place: {"section": place["ty"], "ty": place["section"]})


def sent_home(x, other):
    def to(place):
        return {
            "section": layer_of(place),
            "zh": place["zh"],
            "zl": 1 ^ place["zh"] ^ place["ty"],
            "ty": place["section"],
            "tx": place["tx"] ^ other,
        }

    return moved(x, ("section",) + Z + ("ty", "tx"), to)


def cross_in(x, layer):
    def to(place):
        if place["section"] != layer:
            return None
        return {"section": layer_of(place), "zh": place["zh"], "zl": place["zh"]}

    return moved(x, ("section",) + Z, to)


def cross_out(x, layer):
    def to(place):
        if layer_of(place) != 1:
            return None
        return {"section": layer, "zh": place["zh"], "zl": 1 ^ place["zh"] ^ place["section"]}

    return moved(x, ("section",) + Z, to)


def in_order(x, flag, axis):
    return jnp.where(flag == 1, jnp.flip(x, axis), x)


def pack_heads(query, key, value, out):
    pair = 2 * HDIM
    return jnp.concatenate(
        [
            query,
            value[:, pair:],
            key[:, :pair],
            value[:, :pair],
            key[:, pair:],
            out[:, pair:],
            out[:, :pair],
        ],
        axis=1,
    )


def unpack_heads(packed):
    part = [packed[:, at * HDIM : (at + 1) * HDIM] for at in range(12)]
    query = jnp.concatenate(part[0:3], axis=1)
    key = jnp.concatenate([part[4], part[5], part[8]], axis=1)
    value = jnp.concatenate([part[6], part[7], part[3]], axis=1)
    out = jnp.concatenate([part[10], part[11], part[9]], axis=1)
    return query, key, value, out


def after(x, *earlier):
    return lax.optimization_barrier((x,) + earlier)[0]


def plane_gathered(x, until=(), **only):
    parts = [x, over(x, "tx", **only), over(x, "ty", **only), over(x, "ty", "tx", **only)]
    return jnp.stack([after(part, *until) for part in parts])


def plane_summed(x, until=(), raw=None, **only):
    terms = [x[0], over(x[1], "tx", **only), over(x[2], "ty", **only), over(x[3], "ty", "tx", **only)]
    if raw is not None:
        raw.extend(terms[1:])
    terms = [after(term, *until) for term in terms]
    return low(sum(term.astype(jnp.float32) for term in terms))


def rows_gathered(x, count, until=(), raw=None, **only):
    for axes in [("e%d" % at,) for at in reversed(range(count))] + [Z]:
        got = over(x, *axes, **only)
        if raw is not None:
            raw.append(got)
        parts = [after(part, *until) for part in (x, got)]
        both = in_order(jnp.stack(parts, axis=-3), lax.axis_index(axes[0]), x.ndim - 2)
        x = both.reshape(x.shape[:-2] + (2 * x.shape[-2], x.shape[-1]))
    return x


def rows_summed(x, count, until=(), raw=None, **only):
    for axes in [Z] + [("e%d" % at,) for at in range(count)]:
        halves = x.reshape(x.shape[:-2] + (2, x.shape[-2] // 2, x.shape[-1]))
        halves = in_order(halves, lax.axis_index(axes[0]), x.ndim - 2)
        got = over(halves[..., 1, :, :], *axes, **only)
        if raw is not None:
            raw.append(got)
        x = plus(halves[..., 0, :, :], after(got, *until))
    return x


def plus(first, second):
    return low(first.astype(jnp.float32) + second.astype(jnp.float32))


def from_cores(keep, send, raw=None, **only):
    got = over(send, "section", **only)
    if raw is not None:
        raw.append(got)
    return plus(keep, got)


def body(
    count,
    hidden,
    cotangent,
    segments,
    sa_qkv,
    sa_out,
    cross_one,
    cross_two,
    ffn_in,
    ffn_out,
    norm_gain,
    norm_bias,
):
    core = lax.axis_index("section")
    x_at, y_at, zh_at, zl_at = (lax.axis_index(name) for name in ("tx", "ty", "zh", "zl"))
    layer = 1 ^ zh_at ^ zl_at
    on_encoder = layer == 0
    quarter = hidden.shape[3]
    enc_flag = jnp.stack([core, 1 - layer, 1 - layer, layer])
    dec_flag = jnp.stack([core, layer, 1 - layer, layer])
    flag = jnp.stack([core, jnp.ones_like(core), 1 - layer, layer])

    def pick(first, second):
        return jnp.where(on_encoder, first, second)

    def of_one_row(x):
        both = in_order(x[0, :, 0], x_at, 0)
        return in_order(jnp.stack([both[0], over(both[1], "tx")]), x_at, 0).reshape(2 * quarter, -1)

    def rows_out(x, raw=None):
        mine, other = in_order(x.reshape(2, quarter, -1), x_at, 0)
        both = [sent_home(mine, 0), sent_home(other, 1)]
        if raw is not None:
            raw.extend(both)
        return in_order(jnp.stack(both), x_at, 0)[None, :, None]

    units = ffn_in.shape[2]
    width = cross_one.shape[2]
    packed_self = pack_heads(sa_qkv[0, :, 0], sa_qkv[0, :, 1], sa_qkv[0, :, 2], sa_out[0])
    packed_ffn = jnp.concatenate([ffn_in[0], ffn_out[0].T], axis=1)
    with jax.named_scope("norms_in"):
        norms = swapped(jnp.concatenate([norm_gain[0], norm_bias[0]], axis=0))
        gains, biases = norms[:3], norms[3:]
        seg_own = segments[:, :, 0].astype(jnp.float32)
        seg_here = jnp.where(zl_at == 1 ^ zh_at ^ y_at, seg_own, over(seg_own, "zl")).astype(jnp.int32)
    with jax.named_scope("hidden_in"):
        one_row = of_one_row(jnp.concatenate([hidden, cotangent], axis=-1))
    with jax.named_scope("self_weights"):
        shard_self = swapped(packed_self)
    with jax.named_scope("hidden_in"):
        one_row = swapped(after(one_row, shard_self))
    with jax.named_scope("ffn_weights"):
        shard_ffn = swapped(after(packed_ffn, one_row))
        shard_first, shard_second = shard_ffn[:, :units], shard_ffn[:, units:]

    def both_rows(x):
        for_enc = rows_gathered(x, count, layer=0)
        return pick(for_enc, rows_gathered(after(x, for_enc), count, layer=1))

    with jax.named_scope("self_weights"):
        rows_self = both_rows(shard_self)
        own_self = plane_gathered(rows_self)
        w_self = [own_self, over(own_self, "section")]
    with jax.named_scope("hidden_in"):
        rows_here = turned(one_row)
        rows_here, cot = rows_here[:, : hidden.shape[-1]], rows_here[:, hidden.shape[-1] :]
        rows_all = jnp.concatenate([rows_here, over(rows_here, "section")], axis=0)
    with jax.named_scope("cross_weights"):
        cross_low = after(jnp.concatenate([cross_one[0], cross_two[0]], axis=1), own_self)
        pair_kv, pair_qo = cross_in(cross_low, 0), cross_in(cross_low, 1)
        packed = pack_heads(pair_qo[:, :width], pair_kv[:, :width], pair_kv[:, width:], pair_qo[:, width:])
    with jax.named_scope("ffn_weights"):
        rows_first = both_rows(after(shard_first, rows_self))
        plane_second = plane_gathered(after(shard_second, own_self))

    both_segments = in_order(seg_here, x_at, 1)[:, 0]
    ordered = in_order(both_segments.reshape(2, 2, 2 * quarter), core, 1).reshape(2, 4 * quarter)
    source_seg, target_seg = ordered[0], ordered[1]
    self_seg = pick(source_seg, target_seg)
    parts = jnp.arange(4)
    quarter_of = jnp.repeat(2 * ((parts // 2) ^ core) + parts % 2, quarter)
    lanes = jnp.arange(LANES)[None, :]

    def key_extras(seg):
        differs = jnp.logical_and(lanes < SEG_LANES, seg[:, None] != lanes)
        later = jnp.logical_and(
            jnp.logical_and(lanes >= SEG_LANES, lanes < PART_LANE),
            quarter_of[:, None] > lanes - SEG_LANES,
        )
        part = jnp.logical_and(lanes >= PART_LANE, lanes < PART_LANE + 3)
        return jnp.where(differs | later | part, 1.0, 0.0).astype(jnp.bfloat16)

    def query_extras(seg, causal):
        seg, at = seg[: 2 * quarter], quarter_of[: 2 * quarter]
        same = seg[:, None] == lanes
        here = jnp.logical_and(at[:, None] + SEG_LANES == lanes, causal)
        return jnp.where(same | here, MASKED, 0.0).astype(jnp.bfloat16)

    at_row = jnp.arange(quarter)
    later_key = jnp.logical_and(at_row[None, :] > at_row[:, None], jnp.logical_not(on_encoder))
    tri = jnp.where(later_key, MASKED, 0.0).astype(jnp.float32)
    self_extras = (query_extras(self_seg, jnp.logical_not(on_encoder)), key_extras(self_seg), tri)
    cross_extras = (query_extras(target_seg, False), key_extras(source_seg), tri)

    start = rows_all.astype(jnp.float32)
    start = pick(layer_norm(start, gains[0], biases[0]), start)
    start_here = start[: 2 * quarter]
    start_low = low(start)
    self_gain, self_bias = pick(gains[1], gains[0]), pick(biases[1], biases[0])
    raw_cross_rows = []
    with jax.named_scope("cross_weights"):
        rows_cross = rows_gathered(after(packed, plane_second), count, raw=raw_cross_rows, layer=1)
    self_out, *kept_self = attend(
        flag, start_low[: 2 * quarter], after(start_low, plane_second), w_self, self_extras, True
    )
    with jax.named_scope("ffn_weights"):
        own_first = plane_gathered(after(rows_first, plane_second), until=(self_out, *raw_cross_rows))
        enc_second = rows_gathered(plane_second, count, until=(self_out, *raw_cross_rows), layer=0)
        raw_second = []
        dec_second = rows_gathered(after(plane_second, self_out), count, raw=raw_second, layer=1)
        peer_first = over(own_first, "section")
        w_enc = [own_first, enc_second, peer_first, over(enc_second, "section", layer=0)]
    self_total = start_here + after(self_out, *raw_cross_rows)
    middle = layer_norm(self_total, self_gain, self_bias)
    middle_low = low(middle)

    enc_out, enc_active, enc_slope = ffn(enc_flag, after(middle_low, *raw_second), w_enc)
    enc_total = middle + enc_out
    encoded = low(layer_norm(enc_total, gains[2], biases[2]))
    def across(x, layer):
        return moved(x, Z, lambda place: {**place, "zl": 1 - place["zl"]} if layer_of(place) == layer else None)

    with jax.named_scope("memory"):
        memory_here = [across(encoded[:quarter], 0), across(encoded[quarter:], 0)]
        memory_peer = [over(part, "section", layer=1) for part in memory_here]
    with jax.named_scope("cross_weights"):
        own_cross = plane_gathered(after(rows_cross, *raw_second), until=tuple(memory_here), layer=1)
        w_cross = [own_cross, over(own_cross, "section", layer=1)]
    with jax.named_scope("ffn_weights"):
        w_dec = [own_first, dec_second, peer_first, over(dec_second, "section", layer=1)]

    (
        decoded,
        crossed_low,
        d_dec_low,
        d_middle_dec,
        d_memory_here,
        d_memory_other,
        dec_sums,
        dec_active,
        dec_inner,
        cross_keep,
        cross_send,
    ) = decoder(
        dec_flag, middle, memory_here + memory_peer, cot, cross_extras[:2], norms, w_cross, w_dec
    )
    with jax.named_scope("d_memory"):
        d_memory_here = d_memory_here + over(d_memory_other, "section", layer=1).astype(jnp.float32)
        d_memory_low = low(d_memory_here)
        arrived = across(d_memory_low, 1)
    with jax.named_scope("cross_sums"):
        cross_sum = from_cores(after(cross_keep, arrived), after(cross_send, arrived), layer=1)
        raw_cross = []
        cross_plane = plane_summed(cross_sum, raw=raw_cross, layer=1)

    d_enc_total, dz_low, enc_sums, second_keep, second_send = enc_out_back(
        flag, arrived, cot, enc_total, norms, d_dec_low, enc_active, dec_active, own_first
    )
    with jax.named_scope("ffn_sums"):
        raw_second_sum = []
        second_sum = from_cores(second_keep, second_send, raw=raw_second_sum)
    gain_row = jnp.broadcast_to(self_gain, (8, self_gain.shape[0]))
    d_self_total, d_self_low, self_norm, first_keep, first_send = enc_in_back(
        flag,
        after(dz_low, second_keep, cross_sum),
        d_enc_total,
        d_middle_dec,
        self_total,
        gain_row,
        middle_low,
        crossed_low,
        w_enc,
        enc_slope,
        dec_inner,
    )
    with jax.named_scope("ffn_sums"):
        gate = []
        second_plane = plane_summed(after(second_sum, d_self_low), raw=gate)
        first_sum = from_cores(after(first_keep, *raw_cross), after(first_send, *raw_cross), raw=gate)

    halves = []
    for first, earlier in ((0, ()), (2, gate)):
        halves.append(
            attend_back(
                flag,
                after(d_self_low, *earlier),
                start_low[: 2 * quarter],
                start_low,
                w_self,
                kept_self,
                self_extras,
                True,
                first,
                2,
            )
        )
    d_start_q = halves[0][0] + halves[1][0]
    with jax.named_scope("cross_sums"):
        share_cross = rows_summed(after(cross_plane, d_start_q), count, layer=1)
    with jax.named_scope("ffn_sums"):
        gate_later = []
        first_plane = plane_summed(after(first_sum, second_plane), raw=gate_later)
        second_share = rows_summed(second_plane, count, raw=gate_later)
    with jax.named_scope("self_sums"):
        (_, _, keep, send), (_, _, *later) = halves
        self_sum = [from_cores(after(keep, *gate), after(send, *gate), raw=gate_later)]
        raw_later = []
        self_sum.append(from_cores(*(after(part, *gate_later) for part in later), raw=raw_later))
        self_sum = jnp.concatenate(self_sum, axis=0)
    with jax.named_scope("d_start"):
        d_start_kv = after(halves[0][1], *raw_later) + halves[1][1]
        d_start = d_self_total + d_start_q + d_start_kv[: 2 * quarter]
        d_start = d_start + over(low(d_start_kv[2 * quarter :]), "section").astype(jnp.float32)
    d_source, gain_a, bias_a = norm_back(
        rows_here.astype(jnp.float32), gains[0], biases[0], d_start
    )

    rows_from = jnp.concatenate([enc_sums, self_norm, dec_sums, jnp.stack([gain_a, bias_a])], axis=0)
    enc_rows, dec_rows = jnp.array([24, 8, 0, 25, 9, 1]), jnp.array([8, 18, 16, 9, 19, 17])
    wanted = pick(enc_rows, dec_rows)[:, None] == jnp.arange(26)
    norm_sums = jnp.sum(jnp.where(wanted[:, :, None], rows_from[None], 0.0), axis=1)
    shards = 2**count
    sides = jnp.arange(2)
    held, outer = core ^ sides[:, None], sides[None, :]
    row_block = ((2 * outer + (1 ^ outer ^ held)) * shards)[:, :, None] + jnp.arange(shards)
    column_block = (2 * (y_at ^ sides)[:, None] + (x_at ^ sides)[None, :]).reshape(-1)
    order = (row_block.reshape(2, -1)[:, None, :] + 0) * 4 + column_block[:, None]
    norm_sums = jnp.take(norm_sums.reshape(6, 8 * 2 * shards, -1), order.reshape(-1), axis=1)
    norm_sums = norm_sums.reshape(6, 2, 4, 2 * shards, -1)
    with jax.named_scope("norm_sums"):
        norm_got = over(norm_sums[:, 1], "section")
        norm_sums = norm_sums[:, 0] + norm_got
    with jax.named_scope("self_sums"):
        self_plane = plane_summed(self_sum, until=(norm_got,))
    with jax.named_scope("norm_sums"):
        norm_blocks = after(norm_sums.transpose(1, 2, 0, 3).reshape(4, 2 * shards, -1), self_plane)
        norm_plane = norm_blocks[0] + over(norm_blocks[1], "tx") + over(norm_blocks[2], "ty")
        norm_plane = norm_plane + over(norm_blocks[3], "ty", "tx")
    norm_width = norm_plane.shape[1]
    with jax.named_scope("self_sums"):
        pad = ((0, 0), (0, 15), (0, self_plane.shape[1] - norm_width))
        both = jnp.concatenate(
            [
                self_plane.reshape(2 * shards, -1, self_plane.shape[1]),
                jnp.pad(low(norm_plane)[:, None], pad),
            ],
            axis=1,
        )
        raw_self = []
        share_self = rows_summed(both.reshape(-1, self_plane.shape[1]), count, raw=raw_self)
        share_self = swapped(share_self).astype(jnp.float32)
    norm_shares = share_self[-16, :norm_width].reshape(6, -1)
    share_self = share_self[:-16]
    with jax.named_scope("ffn_sums"):
        first_share = rows_summed(after(first_plane, *raw_later), count)
        share_ffn = swapped(jnp.concatenate([first_share, second_share], axis=1)).astype(jnp.float32)
    share_first, share_second = share_ffn[:, :units], share_ffn[:, units:].T
    with jax.named_scope("outputs"):
        outputs = jnp.concatenate([pick(encoded, decoded), low(pick(d_source, d_start))], axis=1)
        outputs = rows_out(after(outputs, *raw_self))
    hidden_out = outputs[..., : hidden.shape[-1]]
    hidden_grad = outputs[..., hidden.shape[-1] :].astype(jnp.float32)
    g_query, g_key, g_value, g_out = unpack_heads(share_self)
    grad_qkv = jnp.stack([g_query, g_key, g_value], axis=1)
    c_query, c_key, c_value, c_out = unpack_heads(share_cross)
    with jax.named_scope("cross_out"):
        for_enc = cross_out(jnp.concatenate([c_key, c_value], axis=1), 0)
        for_dec = cross_out(jnp.concatenate([c_query, c_out], axis=1), 1)
    cross = jnp.where(core == 0, for_enc, for_dec).astype(jnp.float32)

    return (
        hidden_out,
        hidden_grad,
        grad_qkv[None],
        g_out[None],
        cross[None, :, :width],
        cross[None, :, width:],
        share_first[None],
        share_second[None],
        norm_shares[None, :3],
        norm_shares[None, 3:],
    )


def solution(mesh):
    _, dp_count, _ = mesh.devices.shape
    count = dp_count.bit_length() - 3
    names = axes_of(count)
    dp, tensor = names[1:-2], names[-2:]
    split = Mesh(mesh.devices.reshape((2,) * len(names)), names)
    rows = P("section", None, dp, tensor, None)
    in_specs = (
        rows,
        rows,
        P(None, None, dp, None),
        P("section", dp, None, tensor),
        P("section", dp, tensor),
        P("section", dp, tensor),
        P("section", dp, tensor),
        P("section", dp, tensor),
        P("section", tensor, dp),
        P("section", None, None),
        P("section", None, None),
    )
    out_specs = (
        rows,
        rows,
        P("section", dp, None, tensor),
        P("section", dp, tensor),
        P("section", dp, tensor),
        P("section", dp, tensor),
        P("section", dp, tensor),
        P("section", tensor, dp),
        P("section", None, dp + tensor),
        P("section", None, dp + tensor),
    )
    return jax.shard_map(
        functools.partial(body, count), mesh=split, in_specs=in_specs, out_specs=out_specs, check_vma=False
    )
```

```python
import functools

import jax
import jax.numpy as jnp
from jax import lax
from jax.experimental import pallas as pl
from jax.experimental.pallas import tpu as pltpu
from jax.sharding import Mesh
from jax.sharding import PartitionSpec as P

HDIM = 64
LANES = 128
MASKED = -1e30
NORM_EPS = 1e-05
VMEM_BYTES = 60 * 1024 * 1024

SEG_LANES = 8
PART_LANE = 12

PARTS = 2
TILE_ROWS = 256
HEADS = ((0, 1, 2, 0, 0), (0, 1, 2, 1, 1), (1, 3, 0, 0, 1))


def mul(a, b):
    return jnp.dot(a, b, preferred_element_type=jnp.float32)


def mul_nt(a, b):
    return lax.dot_general(a, b, (((1,), (1,)), ((), ())), preferred_element_type=jnp.float32)


def mul_tn(a, b):
    return lax.dot_general(a, b, (((0,), (0,)), ((), ())), preferred_element_type=jnp.float32)


def tile_of(values, index):
    return values[:, index * LANES : (index + 1) * LANES]


def lane_ids(rows):
    return lax.broadcasted_iota(jnp.int32, (rows, LANES), 1)


def half_mask(rows, half):
    lanes = lane_ids(rows)
    return lanes >= HDIM if half else lanes < HDIM


def in_parts(base, column):
    lanes = lane_ids(base.shape[0])
    high = column.astype(jnp.bfloat16).astype(jnp.float32)
    rest = column - high
    middle = rest.astype(jnp.bfloat16).astype(jnp.float32)
    low = rest - middle
    parts = jnp.where(
        lanes == PART_LANE,
        high,
        jnp.where(lanes == PART_LANE + 1, middle, jnp.where(lanes == PART_LANE + 2, low, base)),
    )
    return parts.astype(jnp.bfloat16)


def with_triangle(scores, tri, at):
    size = tri.shape[1]
    pieces = []
    if at > 0:
        pieces.append(scores[:, : at * size])
    pieces.append(scores[:, at * size : (at + 1) * size] + tri)
    pieces.append(scores[:, (at + 1) * size :])
    return jnp.concatenate(pieces, axis=1)


def places(core, block):
    return [pl.multiple_of((1 - core) * block, block), pl.multiple_of((2 + core) * block, block)]


def assemble(flag_ref, own_refs, peer_refs, w_ref):
    core, block = flag_ref[0], own_refs[0].shape[1] // 2
    for holder, refs in ((core, own_refs), (1 - core, peer_refs)):
        for part, ref in enumerate(refs):
            width = ref.shape[2]
            for at, place in enumerate(places(holder, block)):
                w_ref[pl.ds(place, block), part * width : (part + 1) * width] = ref[0, at * block : (at + 1) * block]


def hand_out(flag_ref, g_ref, keep_ref, send_ref):
    core, block = flag_ref[0], keep_ref.shape[1] // 2
    for holder, ref in ((core, keep_ref), (1 - core, send_ref)):
        for at, place in enumerate(places(holder, block)):
            ref[0, at * block : (at + 1) * block] = g_ref[pl.ds(place, block), :]


def where_active(kernel):
    def guarded(flag_ref, *refs):
        @pl.when(flag_ref[1] == 1)
        def _():
            kernel(flag_ref, *refs)

    return guarded


def unit_of(index):
    part, head = index // 3, index % 3
    third = (head == 2).astype(jnp.int32)

    def tile(number):
        return pl.ds(pl.multiple_of(number * LANES, LANES), LANES)

    upper = (lane_ids(TILE_ROWS) >= HDIM).astype(jnp.int32)
    return {
        "part": part,
        "head": head,
        "at": pl.ds(pl.multiple_of(part * TILE_ROWS, TILE_ROWS), TILE_ROWS),
        "query": tile(third),
        "key": tile(1 + 2 * third),
        "value": tile(2 - 2 * third),
        "context": tile(1 - third),
        "query_lanes": upper == (head == 1).astype(jnp.int32),
        "value_lanes": upper == (head >= 1).astype(jnp.int32),
    }


def unit_queries(unit, q_ref):
    queries = q_ref[0, unit["at"], unit["query"]] * 0.125
    return jnp.where(unit["query_lanes"], queries, 0).astype(jnp.bfloat16)


def with_triangle(scores, tri_ref, part):
    size = tri_ref.shape[1]
    pieces = [
        scores[:, at * size : (at + 1) * size] + jnp.where(part == at, tri_ref[...], 0.0) for at in (0, 1)
    ]
    return jnp.concatenate(pieces + [scores[:, 2 * size :]], axis=1)


def attend_block(causal, xq_ref, xkv_ref, w_ref, qx_ref, kx_ref, tri_ref, q_ref, kv_ref, c_ref, l_ref):
    q_ref[0] = mul(xq_ref[...], w_ref[:, : 2 * LANES]).astype(jnp.bfloat16)
    kv_ref[0] = mul(xkv_ref[...], w_ref[:, LANES : 5 * LANES]).astype(jnp.bfloat16)
    c_ref[0, :, :LANES] = jnp.zeros((c_ref.shape[1], LANES), c_ref.dtype)

    def step(index, carry):
        unit = unit_of(index)
        at = unit["at"]
        scores = mul_nt(
            jnp.concatenate([unit_queries(unit, q_ref), qx_ref[at, :]], axis=1),
            jnp.concatenate([kv_ref[0, :, unit["key"]], kx_ref[...]], axis=1),
        )
        if causal:
            scores = with_triangle(scores, tri_ref, unit["part"])
        highest = jnp.max(scores, axis=1, keepdims=True)
        weights = jnp.exp(scores - highest)
        sums = jnp.sum(weights, axis=1, keepdims=True)
        context = mul(weights.astype(jnp.bfloat16), kv_ref[0, :, unit["value"]]) / sums
        held = c_ref[0, at, unit["context"]]
        c_ref[0, at, unit["context"]] = jnp.where(unit["value_lanes"], context.astype(held.dtype), held)
        logs = jnp.broadcast_to(highest + jnp.log(sums), (TILE_ROWS, LANES))
        l_ref[0, at, :] = jnp.where(lane_ids(TILE_ROWS) == unit["head"], logs, l_ref[0, at, :])
        return carry

    lax.fori_loop(0, 3 * (q_ref.shape[1] // TILE_ROWS), step, 0)
    return mul_nt(c_ref[0], w_ref[:, 4 * LANES :])


def attend_kernel(causal, flag_ref, xq_ref, xkv_ref, own_ref, peer_ref, qx_ref, kx_ref, tri_ref, o_ref, *refs):
    q_ref, kv_ref, c_ref, l_ref, w_ref = refs
    assemble(flag_ref, [own_ref], [peer_ref], w_ref)
    out = attend_block(causal, xq_ref, xkv_ref, w_ref, qx_ref, kx_ref, tri_ref, q_ref, kv_ref, c_ref, l_ref)
    add_up(pl.program_id(0) == 0, o_ref, out)


def add_up(first, ref, value):
    @pl.when(first)
    def _():
        ref[...] = value

    @pl.when(jnp.logical_not(first))
    def _():
        ref[...] += value


def attend_back_block(causal, do_ref, xq_ref, xkv_ref, w_ref, qx_ref, kx_ref, tri_ref, kept, work):
    q_ref, kv_ref, c_ref, l_ref = kept
    sum_ref, dq_ref, dkv_ref, g_ref, dc_ref = work
    dc_ref[...] = mul(do_ref[...], w_ref[:, 4 * LANES :]).astype(jnp.bfloat16)
    sum_ref[...] = jnp.zeros(sum_ref.shape, jnp.float32)
    dq_ref[...] = jnp.zeros(dq_ref.shape, jnp.bfloat16)

    def step(index, carry):
        unit = unit_of(index)
        at, key, value = unit["at"], unit["key"], unit["value"]
        queries = unit_queries(unit, q_ref)
        d_rows = jnp.where(unit["value_lanes"], dc_ref[at, unit["context"]], 0).astype(jnp.bfloat16)
        keys = kv_ref[0, :, key]
        total = jnp.where(lane_ids(TILE_ROWS) == unit["head"], l_ref[0, at, :], 0.0)
        total = jnp.sum(total, axis=1, keepdims=True)
        scores = mul_nt(
            jnp.concatenate([queries, in_parts(qx_ref[at, :].astype(jnp.float32), -total)], axis=1),
            jnp.concatenate([keys, kx_ref[...]], axis=1),
        )
        if causal:
            scores = with_triangle(scores, tri_ref, unit["part"])
        d_probs = mul_nt(d_rows, kv_ref[0, :, value])
        probs = jnp.exp(scores)
        inner = jnp.sum(probs * d_probs, axis=1, keepdims=True)
        d_scores = (probs * (d_probs - inner)).astype(jnp.bfloat16)
        sum_ref[:, value] += mul_tn(probs.astype(jnp.bfloat16), d_rows)
        sum_ref[:, key] += mul_tn(d_scores, queries)
        d_query = (mul(d_scores, keys) * 0.125).astype(jnp.bfloat16)
        dq_ref[at, unit["query"]] = jnp.where(unit["query_lanes"], d_query, dq_ref[at, unit["query"]])
        return carry

    lax.fori_loop(0, 3 * (q_ref.shape[1] // TILE_ROWS), step, 0)
    dkv_ref[...] = sum_ref[...].astype(jnp.bfloat16)
    d_xq = mul_nt(dq_ref[...], w_ref[:, : 2 * LANES])
    d_xkv = mul_nt(dkv_ref[...], w_ref[:, LANES : 5 * LANES])

    grad_q = mul_tn(xq_ref[...], dq_ref[...])
    grad_kv = mul_tn(xkv_ref[...], dkv_ref[...])
    grad_o = mul_tn(do_ref[...], c_ref[0])
    g_ref[:, :LANES] = grad_q[:, :LANES].astype(jnp.bfloat16)
    g_ref[:, LANES : 2 * LANES] = (grad_q[:, LANES:] + grad_kv[:, :LANES]).astype(jnp.bfloat16)
    g_ref[:, 2 * LANES : 4 * LANES] = grad_kv[:, LANES : 3 * LANES].astype(jnp.bfloat16)
    g_ref[:, 4 * LANES : 5 * LANES] = (grad_kv[:, 3 * LANES :] + grad_o[:, :LANES]).astype(jnp.bfloat16)
    g_ref[:, 5 * LANES :] = grad_o[:, LANES:].astype(jnp.bfloat16)
    return d_xq, d_xkv


def attend_back_kernel(causal, flag_ref, do_ref, xq_ref, xkv_ref, own_ref, peer_ref, *refs):
    kept, (qx_ref, kx_ref, tri_ref, dxq_ref, dxkv_ref, keep_ref, send_ref, w_ref) = refs[:4], refs[4:12]
    work = refs[12:]
    assemble(flag_ref, [own_ref], [peer_ref], w_ref)
    d_xq, d_xkv = attend_back_block(
        causal, do_ref, xq_ref, xkv_ref, w_ref, qx_ref, kx_ref, tri_ref, kept, work
    )
    add_up(pl.program_id(0) == 0, dxq_ref, d_xq)
    add_up(pl.program_id(0) == 0, dxkv_ref, d_xkv)
    hand_out(flag_ref, work[3], keep_ref, send_ref)


def whole(shape):
    return pl.BlockSpec(shape, lambda j, flag: (0,) * len(shape))


def held(shape):
    return pl.BlockSpec(shape, lambda j, flag: (0,) * len(shape), pipeline_mode=pl.Buffered(1))


def per_block(shape, first=0, gate=1):
    return pl.BlockSpec((1,) + shape, lambda j, flag: (first + j * flag[gate],) + (0,) * len(shape))


shape = jax.ShapeDtypeStruct


def call(kernel, name, micros, moved, grid, in_specs, out_specs, out_shape, scratch, *operands):
    return pl.pallas_call(
        where_active(kernel),
        grid_spec=pltpu.PrefetchScalarGridSpec(
            num_scalar_prefetch=1,
            grid=(grid,),
            in_specs=in_specs,
            out_specs=out_specs,
            scratch_shapes=scratch,
        ),
        out_shape=out_shape,
        compiler_params=pltpu.CompilerParams(vmem_limit_bytes=VMEM_BYTES),
        cost_estimate=cost(micros, moved),
        name=name,
    )(*operands)


def cost(micros, moved):
    return pl.CostEstimate(flops=int(micros * 1.15e9), bytes_accessed=int(moved), transcendentals=0)


def attend(flag, xq, xkv, weights, extras, causal):
    rows, width = xq.shape
    keys = xkv.shape[0]
    blocks = weights[0].shape[0]
    return call(
        functools.partial(attend_kernel, causal),
        "attend_self" if causal else "attend_cross",
        20,
        24 * 2**20,
        blocks,
        [held((rows, width)), held((keys, width))]
        + [per_block(part.shape[1:]) for part in weights]
        + [held(extra.shape) for extra in extras],
        [
            whole((rows, width)),
            per_block((rows, 2 * LANES)),
            per_block((keys, 4 * LANES)),
            per_block((rows, 2 * LANES)),
            per_block((rows, LANES)),
        ],
        [
            shape((rows, width), jnp.float32),
            shape((blocks, rows, 2 * LANES), jnp.bfloat16),
            shape((blocks, keys, 4 * LANES), jnp.bfloat16),
            shape((blocks, rows, 2 * LANES), jnp.bfloat16),
            shape((blocks, rows, LANES), jnp.float32),
        ],
        [pltpu.VMEM((width, 6 * LANES), jnp.bfloat16)],
        flag,
        xq,
        xkv,
        *weights,
        *extras,
    )


def attend_back(flag, d_out, xq, xkv, weights, kept, extras, causal, first, count):
    rows, width = xq.shape
    keys = xkv.shape[0]
    return call(
        functools.partial(attend_back_kernel, causal),
        "attend_self_back" if causal else "attend_cross_back",
        10 * count,
        6 * 2**20 * count,
        count,
        [held((rows, width)), held((rows, width)), held((keys, width))]
        + [per_block(part.shape[1:], first) for part in weights]
        + [
            per_block((rows, 2 * LANES), first),
            per_block((keys, 4 * LANES), first),
            per_block((rows, 2 * LANES), first),
            per_block((rows, LANES), first),
        ]
        + [held(extra.shape) for extra in extras],
        [whole((rows, width)), whole((keys, width))] + [per_block(part.shape[1:]) for part in weights],
        [shape((rows, width), jnp.float32), shape((keys, width), jnp.float32)]
        + [shape((count,) + part.shape[1:], jnp.bfloat16) for part in weights],
        [
            pltpu.VMEM((width, 6 * LANES), jnp.bfloat16),
            pltpu.VMEM((keys, 4 * LANES), jnp.float32),
            pltpu.VMEM((rows, 2 * LANES), jnp.bfloat16),
            pltpu.VMEM((keys, 4 * LANES), jnp.bfloat16),
            pltpu.VMEM((width, 6 * LANES), jnp.bfloat16),
            pltpu.VMEM((rows, 2 * LANES), jnp.bfloat16),
        ],
        flag,
        d_out,
        xq,
        xkv,
        *weights,
        *kept,
        *extras,
    )


def in_tiles(rows, work):
    def step(index, carry):
        work(pl.ds(pl.multiple_of(index * TILE_ROWS, TILE_ROWS), TILE_ROWS))
        return carry

    lax.fori_loop(0, rows // TILE_ROWS, step, 0)


def ffn_block(x_ref, w_ref, units, g_ref, slope_ref, first, out_ref):
    def tile(at):
        inner = mul(x_ref[at, :], w_ref[:, :units])
        spread = 0.5 * (1.0 + lax.erf(inner * (0.5**0.5)))
        bell = jnp.exp(-0.5 * inner * inner) * 0.3989422804014327
        active = (inner * spread).astype(jnp.bfloat16)
        g_ref[0, at, :] = active
        slope_ref[0, at, :] = (spread + inner * bell).astype(jnp.bfloat16)
        out = mul_nt(active, w_ref[:, units:])
        out_ref[at, :] = jnp.where(first, out, out_ref[at, :] + out)

    in_tiles(x_ref.shape[0], tile)


def ffn_kernel(flag_ref, x_ref, *refs):
    own_refs, peer_refs = refs[:PARTS], refs[PARTS : 2 * PARTS]
    z_ref, g_ref, slope_ref, w_ref = refs[2 * PARTS :]
    assemble(flag_ref, own_refs, peer_refs, w_ref)
    ffn_block(x_ref, w_ref, own_refs[0].shape[2], g_ref, slope_ref, pl.program_id(0) == 0, z_ref)


def feed_blocks(feed, index):
    half, units = feed[0].shape[1], feed[0].shape[2] // 2
    return [
        pl.BlockSpec((1, half, units), lambda j, flag, side=side: (index(j, flag), 0, side))
        for _ in feed
        for side in (0, 1)
    ]


def feed_operands(feed):
    return [part for part in feed for _ in (0, 1)]


def ffn(flag, x, feed):
    rows, width = x.shape
    blocks, units = feed[0].shape[0], feed[0].shape[2] // 2
    return call(
        ffn_kernel,
        "ffn",
        12,
        rows * units * blocks * 16,
        blocks,
        [held((rows, width))] + feed_blocks(feed, lambda j, flag: j * flag[1]),
        [whole((rows, width)), per_block((rows, units)), per_block((rows, units))],
        [
            shape((rows, width), jnp.float32),
            shape((blocks, rows, units), jnp.bfloat16),
            shape((blocks, rows, units), jnp.bfloat16),
        ],
        [pltpu.VMEM((width, 2 * units), jnp.bfloat16)],
        flag,
        x,
        *feed_operands(feed),
    )


def ffn_back_block(dz_ref, w_ref, units, slope_ref, dh_ref, first, out_ref):
    def tile(at):
        d_active = mul(dz_ref[at, :], w_ref[:, units:])
        d_inner = (d_active * slope_ref[0, at, :].astype(jnp.float32)).astype(jnp.bfloat16)
        dh_ref[0, at, :] = d_inner
        out = mul_nt(d_inner, w_ref[:, :units])
        out_ref[at, :] = jnp.where(first, out, out_ref[at, :] + out)

    in_tiles(dz_ref.shape[0], tile)


def layer_norm(values, gain_row, bias_row):
    average = jnp.mean(values, axis=-1, keepdims=True)
    centered = values - average
    variance = jnp.mean(centered * centered, axis=-1, keepdims=True)
    return centered * lax.rsqrt(variance + NORM_EPS) * gain_row + bias_row


def norm_back(values, gain_row, bias_row, upstream):
    _, pullback = jax.vjp(layer_norm, values, gain_row, bias_row)
    return pullback(upstream)


def norm_parts(values):
    average = jnp.mean(values, axis=1, keepdims=True)
    centered = values - average
    scale = lax.rsqrt(jnp.mean(centered * centered, axis=1, keepdims=True) + NORM_EPS)
    return centered * scale, scale


def norm_gradients(values, gain_row, upstream):
    shaped, scale = norm_parts(values)
    inner = upstream * gain_row
    mean_inner = jnp.mean(inner, axis=1, keepdims=True)
    mean_product = jnp.mean(inner * shaped, axis=1, keepdims=True)
    d_values = scale * (inner - mean_inner - shaped * mean_product)
    d_gain = jnp.sum(upstream * shaped, axis=0, keepdims=True)
    return d_values, d_gain, jnp.sum(upstream, axis=0, keepdims=True)


def enc_out_back_kernel(
    flag_ref, arrived_ref, cot_ref, total_ref, norms_ref, d_dec_ref, enc_ref, dec_ref, *refs
):
    d_total_ref, dz_ref, sums_ref, keep_ref, send_ref, g_ref, left_t_ref = refs

    @pl.when(jnp.logical_and(pl.program_id(0) == 0, flag_ref[2] == 1))
    def _():
        upstream = arrived_ref[...].astype(jnp.float32) + cot_ref[...].astype(jnp.float32)
        d_total, sums_ref[0:1, :], sums_ref[1:2, :] = norm_gradients(total_ref[...], norms_ref[2:3, :], upstream)
        d_total_ref[...] = d_total
        dz_ref[...] = d_total.astype(jnp.bfloat16)

    @pl.when(jnp.logical_and(pl.program_id(0) == 0, flag_ref[2] == 0))
    def _():
        dz_ref[...] = d_dec_ref[...]

    @pl.when(pl.program_id(0) == 0)
    def _():
        left_t_ref[...] = dz_ref[...].T

    right = jnp.where(flag_ref[2] == 1, enc_ref[0], dec_ref[0])
    g_ref[...] = mul(left_t_ref[...], right).astype(jnp.bfloat16)
    hand_out(flag_ref, g_ref, keep_ref, send_ref)


def enc_out_back(flag, arrived, cot, total, norms, d_dec, enc_active, dec_active, feed):
    rows, width = cot.shape
    blocks, _, units = enc_active.shape
    like = shape((blocks, feed[0].shape[1], units), jnp.bfloat16)
    full = shape((rows, width), jnp.float32)
    return call(
        enc_out_back_kernel,
        "enc_out_back",
        9,
        rows * units * blocks * 8,
        blocks,
        [held(item.shape) for item in (arrived, cot, total, norms, d_dec)]
        + [per_block((rows, units), 0, 2), per_block((rows, units), 0, 3)],
        [whole((rows, width))] * 2 + [whole((8, width))] + [per_block(like.shape[1:])] * 2,
        [full, shape((rows, width), jnp.bfloat16), shape((8, width), jnp.float32)]
        + [like] * 2,
        [pltpu.VMEM((width, units), jnp.bfloat16), pltpu.VMEM((width, rows), jnp.bfloat16)],
        flag,
        arrived,
        cot,
        total,
        norms,
        d_dec,
        enc_active,
        dec_active,
    )


def enc_in_back_kernel(
    flag_ref, dz_ref, d_enc_ref, d_middle_ref, total_ref, gain_ref, middle_ref, crossed_ref, *refs
):
    first_own_ref, second_own_ref, first_peer_ref, second_peer_ref, slope_ref, dec_inner_ref, *refs = refs
    d_total_ref, d_low_ref, sums_ref, keep_ref, send_ref, w_ref, inner_ref, out_ref, g_ref, left_t_ref = refs
    step = pl.program_id(0)
    phase, at = step // 4, step % 4
    on_encoder = flag_ref[2] == 1

    @pl.when(jnp.logical_and(phase == 0, on_encoder))
    def _():
        assemble(flag_ref, [first_own_ref, second_own_ref], [first_peer_ref, second_peer_ref], w_ref)
        ffn_back_block(
            dz_ref, w_ref, first_own_ref.shape[2], slope_ref, inner_ref.at[pl.ds(at, 1)], at == 0, out_ref
        )

    @pl.when(step == 3)
    def _():
        upstream = jnp.where(on_encoder, d_enc_ref[...] + out_ref[...], d_middle_ref[...])
        d_total, sums_ref[0:1, :], sums_ref[1:2, :] = norm_gradients(total_ref[...], gain_ref[0:1, :], upstream)
        d_total_ref[...] = d_total
        d_low_ref[...] = d_total.astype(jnp.bfloat16)
        left_t_ref[...] = jnp.where(on_encoder, middle_ref[...], crossed_ref[...]).T

    @pl.when(phase == 1)
    def _():
        right = jnp.where(on_encoder, inner_ref[at], dec_inner_ref[0])
        g_ref[...] = mul(left_t_ref[...], right).astype(jnp.bfloat16)
        hand_out(flag_ref, g_ref, keep_ref, send_ref)


def enc_in_back(flag, dz, d_enc, d_middle, total, gain, middle, crossed, feed, slope, dec_inner):
    rows, width = dz.shape
    blocks, half, units = feed[0].shape[0], feed[0].shape[1], feed[0].shape[2] // 2
    full = shape((rows, width), jnp.float32)

    def at_step(of, low, high, gate):
        def index(j, flag):
            return (jnp.where(j < 4, j if low == "up" else low, j - 4 if high == "up" else high) * flag[gate],) + (
                0,
            ) * len(of)

        return pl.BlockSpec((1,) + of, index)

    return call(
        enc_in_back_kernel,
        "enc_in_back",
        19,
        rows * units * blocks * 20,
        8,
        [held(item.shape) for item in (dz, d_enc, d_middle, total, gain, middle, crossed)]
        + feed_blocks(feed, lambda j, flag: jnp.where(j < 4, j, 3) * flag[2])
        + [at_step((rows, units), "up", 3, 2), at_step((rows, units), 0, "up", 3)],
        [whole((rows, width))] * 2 + [whole((8, width))] + [at_step((half, units), 0, "up", 1)] * 2,
        [full, shape((rows, width), jnp.bfloat16), shape((8, width), jnp.float32)]
        + [shape((blocks, half, units), jnp.bfloat16)] * 2,
        [
            pltpu.VMEM((width, 2 * units), jnp.bfloat16),
            pltpu.VMEM((blocks, rows, units), jnp.bfloat16),
            pltpu.VMEM((rows, width), jnp.float32),
            pltpu.VMEM((width, units), jnp.bfloat16),
            pltpu.VMEM((width, rows), jnp.bfloat16),
        ],
        flag,
        dz,
        d_enc,
        d_middle,
        total,
        gain,
        middle,
        crossed,
        *feed_operands(feed),
        slope,
        dec_inner,
    )


def decoder_kernel(
    flag_ref,
    h1_ref,
    mem_a_ref,
    mem_b_ref,
    peer_a_ref,
    peer_b_ref,
    cot_ref,
    qx_ref,
    kx_ref,
    norms_ref,
    own_ref,
    peer_ref,
    first_own_ref,
    second_own_ref,
    first_peer_ref,
    second_peer_ref,
    decoded_ref,
    crossed_ref,
    d_dec_ref,
    d_middle_ref,
    mine_ref,
    other_ref,
    sums_ref,
    active_ref,
    inner_ref,
    keep_ref,
    send_ref,
    xq_ref,
    xkv_ref,
    wx_ref,
    wf_ref,
    q_ref,
    kv_ref,
    c_ref,
    l_ref,
    slope_ref,
    out_ref,
    total_ref,
    do_ref,
    dxkv_ref,
    *work,
):
    step = pl.program_id(0)
    phase, at = step // 4, step % 4
    first, last = at == 0, at == 3
    rows = h1_ref.shape[0]
    units = first_own_ref.shape[2]
    gain = [norms_ref[row : row + 1, :] for row in range(3)]
    bias = [norms_ref[3 + row : 4 + row, :] for row in range(3)]

    def kept(block):
        return tuple(ref.at[pl.ds(block, 1)] for ref in (q_ref, kv_ref, c_ref, l_ref))

    @pl.when(step == 0)
    def _():
        xq_ref[...] = h1_ref[...].astype(jnp.bfloat16)
        for part, ref in enumerate((mem_a_ref, mem_b_ref, peer_a_ref, peer_b_ref)):
            xkv_ref[part * rows // 2 : (part + 1) * rows // 2] = ref[...]

    @pl.when(jnp.logical_or(phase == 0, phase == 3))
    def _():
        assemble(flag_ref, [own_ref], [peer_ref], wx_ref)

    @pl.when(jnp.logical_or(phase == 1, phase == 2))
    def _():
        assemble(flag_ref, [first_own_ref, second_own_ref], [first_peer_ref, second_peer_ref], wf_ref)

    @pl.when(phase == 0)
    def _():
        add_up(first, out_ref, attend_block(False, xq_ref, xkv_ref, wx_ref, qx_ref, kx_ref, None, *kept(at)))

    @pl.when(jnp.logical_and(phase == 0, last))
    def _():
        total = h1_ref[...] + out_ref[...]
        total_ref[...] = total
        crossed = norm_parts(total)[0] * gain[1] + bias[1]
        mine_ref[...] = crossed
        crossed_ref[...] = crossed.astype(jnp.bfloat16)

    @pl.when(phase == 1)
    def _():
        ffn_block(crossed_ref, wf_ref, units, active_ref, slope_ref.at[pl.ds(at, 1)], first, out_ref)

    @pl.when(jnp.logical_and(phase == 1, last))
    def _():
        total = mine_ref[...] + out_ref[...]
        decoded_ref[...] = (norm_parts(total)[0] * gain[2] + bias[2]).astype(jnp.bfloat16)
        d_total, sums_ref[0:1, :], sums_ref[1:2, :] = norm_gradients(
            total, gain[2], cot_ref[...].astype(jnp.float32)
        )
        d_middle_ref[...] = d_total
        d_dec_ref[...] = d_total.astype(jnp.bfloat16)

    @pl.when(phase == 2)
    def _():
        ffn_back_block(d_dec_ref, wf_ref, units, slope_ref.at[pl.ds(3 - at, 1)], inner_ref, first, out_ref)

    @pl.when(jnp.logical_and(phase == 2, last))
    def _():
        d_total, sums_ref[2:3, :], sums_ref[3:4, :] = norm_gradients(
            total_ref[...], gain[1], d_middle_ref[...] + out_ref[...]
        )
        d_middle_ref[...] = d_total
        do_ref[...] = d_total.astype(jnp.bfloat16)

    @pl.when(phase == 3)
    def _():
        d_xq, d_xkv = attend_back_block(
            False, do_ref, xq_ref, xkv_ref, wx_ref, qx_ref, kx_ref, None, kept(3 - at), work
        )
        add_up(first, out_ref, d_xq)
        add_up(first, dxkv_ref, d_xkv)
        hand_out(flag_ref, work[3], keep_ref, send_ref)

    @pl.when(jnp.logical_and(phase == 3, last))
    def _():
        d_middle_ref[...] += out_ref[...]
        mine_ref[...] = dxkv_ref[:rows]
        other_ref[...] = dxkv_ref[rows:].astype(jnp.bfloat16)


def decoder(flag, h1, memory, cot, extras, norms, cross, feed):
    rows, width = h1.shape
    blocks, half, _ = cross[0].shape
    units = feed[0].shape[2] // 2
    keys = 2 * rows
    qx, kx = extras

    def at_step(of, in_phase):
        def index(j, flag):
            at = j % 4
            choice = [{"up": at, "down": 3 - at}.get(way, way) for way in in_phase]
            chosen = choice[3]
            for phase in (2, 1, 0):
                chosen = jnp.where(j // 4 == phase, choice[phase], chosen)
            return (chosen * flag[1],) + (0,) * len(of)

        return pl.BlockSpec((1,) + of, index)

    part = (half, cross[0].shape[2])
    full = shape((rows, width), jnp.float32)
    rounded = shape((rows, width), jnp.bfloat16)
    return call(
        decoder_kernel,
        "decoder",
        90,
        40 * 2**20,
        16,
        [held(item.shape) for item in (h1, *memory, cot, qx, kx, norms)]
        + [at_step(part, ("up", 3, 3, "down"))] * 2
        + feed_blocks(feed, lambda j, flag: at_step((half, units), (0, "up", "down", 0)).index_map(j, flag)[0]),
        [whole((rows, width))] * 6
        + [whole((8, width))]
        + [
            at_step((rows, units), (0, "up", 3, 3)),
            at_step((rows, units), (3, 3, "down", 0)),
            at_step(part, (3, 3, 3, "down")),
            at_step(part, (3, 3, 3, "down")),
        ],
        [rounded, rounded, rounded, full, full, rounded, shape((8, width), jnp.float32)]
        + [shape((blocks, rows, units), jnp.bfloat16)] * 2
        + [shape(cross[0].shape, jnp.bfloat16)] * 2,
        [
            pltpu.VMEM((rows, width), jnp.bfloat16),
            pltpu.VMEM((keys, width), jnp.bfloat16),
            pltpu.VMEM((width, 6 * LANES), jnp.bfloat16),
            pltpu.VMEM((width, 2 * units), jnp.bfloat16),
            pltpu.VMEM((blocks, rows, 2 * LANES), jnp.bfloat16),
            pltpu.VMEM((blocks, keys, 4 * LANES), jnp.bfloat16),
            pltpu.VMEM((blocks, rows, 2 * LANES), jnp.bfloat16),
            pltpu.VMEM((blocks, rows, LANES), jnp.float32),
            pltpu.VMEM((blocks, rows, units), jnp.bfloat16),
            pltpu.VMEM((rows, width), jnp.float32),
            pltpu.VMEM((rows, width), jnp.float32),
            pltpu.VMEM((rows, width), jnp.bfloat16),
            pltpu.VMEM((keys, width), jnp.float32),
            pltpu.VMEM((keys, 4 * LANES), jnp.float32),
            pltpu.VMEM((rows, 2 * LANES), jnp.bfloat16),
            pltpu.VMEM((keys, 4 * LANES), jnp.bfloat16),
            pltpu.VMEM((width, 6 * LANES), jnp.bfloat16),
            pltpu.VMEM((rows, 2 * LANES), jnp.bfloat16),
        ],
        flag,
        h1,
        *memory,
        cot,
        qx,
        kx,
        norms,
        *cross,
        *feed_operands(feed),
    )


def low(values):
    return values.astype(jnp.bfloat16)


def axes_of(count):
    return ("section", "zh", "zl") + tuple("e%d" % at for at in range(count)) + ("ty", "tx")


def layer_of(place):
    return 1 ^ place["zh"] ^ place["zl"]


def moved(x, names, to):
    names = [name for name in axes_of(8) if name in names]

    def index(place):
        return sum(place[name] << (len(names) - 1 - at) for at, name in enumerate(names))

    pairs = []
    for source in range(2 ** len(names)):
        place = {name: source >> (len(names) - 1 - at) & 1 for at, name in enumerate(names)}
        target = to(place)
        if target is not None:
            pairs.append((source, index(target)))
    return lax.ppermute(x, tuple(names), pairs)


def over(x, *axes, layer=None):
    def to(place):
        if layer is not None and layer_of(place) != layer:
            return None
        return {**place, **{axis: 1 - place[axis] for axis in axes}}

    return moved(x, axes if layer is None else axes + Z, to)


Z = ("zh", "zl")


def swapped(x):
    def to(place):
        if place["section"] == layer_of(place):
            return place
        return {"section": 1 - place["section"], "zh": place["zh"], "zl": 1 - place["zl"]}

    return moved(x, ("section",) + Z, to)


def turned(x):
    return moved(x, ("section", "ty"), lambda place: {"section": place["ty"], "ty": place["section"]})


def sent_home(x, other):
    def to(place):
        return {
            "section": layer_of(place),
            "zh": place["zh"],
            "zl": 1 ^ place["zh"] ^ place["ty"],
            "ty": place["section"],
            "tx": place["tx"] ^ other,
        }

    return moved(x, ("section",) + Z + ("ty", "tx"), to)


def cross_in(x, layer):
    def to(place):
        if place["section"] != layer:
            return None
        return {"section": layer_of(place), "zh": place["zh"], "zl": place["zh"]}

    return moved(x, ("section",) + Z, to)


def cross_out(x, layer):
    def to(place):
        if layer_of(place) != 1:
            return None
        return {"section": layer, "zh": place["zh"], "zl": 1 ^ place["zh"] ^ place["section"]}

    return moved(x, ("section",) + Z, to)


def in_order(x, flag, axis):
    return jnp.where(flag == 1, jnp.flip(x, axis), x)


def pack_heads(query, key, value, out):
    pair = 2 * HDIM
    return jnp.concatenate(
        [
            query,
            value[:, pair:],
            key[:, :pair],
            value[:, :pair],
            key[:, pair:],
            out[:, pair:],
            out[:, :pair],
        ],
        axis=1,
    )


def unpack_heads(packed):
    part = [packed[:, at * HDIM : (at + 1) * HDIM] for at in range(12)]
    query = jnp.concatenate(part[0:3], axis=1)
    key = jnp.concatenate([part[4], part[5], part[8]], axis=1)
    value = jnp.concatenate([part[6], part[7], part[3]], axis=1)
    out = jnp.concatenate([part[10], part[11], part[9]], axis=1)
    return query, key, value, out


def after(x, *earlier):
    return lax.optimization_barrier((x,) + earlier)[0]


def plane_gathered(x, until=(), **only):
    parts = [x, over(x, "tx", **only), over(x, "ty", **only), over(x, "ty", "tx", **only)]
    return jnp.stack([after(part, *until) for part in parts])


def plane_summed(x, until=(), raw=None, **only):
    terms = [x[0], over(x[1], "tx", **only), over(x[2], "ty", **only), over(x[3], "ty", "tx", **only)]
    if raw is not None:
        raw.extend(terms[1:])
    terms = [after(term, *until) for term in terms]
    return low(sum(term.astype(jnp.float32) for term in terms))


def rows_gathered(x, count, until=(), raw=None, **only):
    for axes in [("e%d" % at,) for at in reversed(range(count))] + [Z]:
        got = over(x, *axes, **only)
        if raw is not None:
            raw.append(got)
        parts = [after(part, *until) for part in (x, got)]
        both = in_order(jnp.stack(parts, axis=-3), lax.axis_index(axes[0]), x.ndim - 2)
        x = both.reshape(x.shape[:-2] + (2 * x.shape[-2], x.shape[-1]))
    return x


def rows_summed(x, count, until=(), raw=None, **only):
    for axes in [Z] + [("e%d" % at,) for at in range(count)]:
        halves = x.reshape(x.shape[:-2] + (2, x.shape[-2] // 2, x.shape[-1]))
        halves = in_order(halves, lax.axis_index(axes[0]), x.ndim - 2)
        got = over(halves[..., 1, :, :], *axes, **only)
        if raw is not None:
            raw.append(got)
        x = plus(halves[..., 0, :, :], after(got, *until))
    return x


def plus(first, second):
    return low(first.astype(jnp.float32) + second.astype(jnp.float32))


def from_cores(keep, send, raw=None, **only):
    got = over(send, "section", **only)
    if raw is not None:
        raw.append(got)
    return plus(keep, got)


def body(
    count,
    hidden,
    cotangent,
    segments,
    sa_qkv,
    sa_out,
    cross_one,
    cross_two,
    ffn_in,
    ffn_out,
    norm_gain,
    norm_bias,
):
    core = lax.axis_index("section")
    x_at, y_at, zh_at, zl_at = (lax.axis_index(name) for name in ("tx", "ty", "zh", "zl"))
    layer = 1 ^ zh_at ^ zl_at
    on_encoder = layer == 0
    quarter = hidden.shape[3]
    enc_flag = jnp.stack([core, 1 - layer, 1 - layer, layer])
    dec_flag = jnp.stack([core, layer, 1 - layer, layer])
    flag = jnp.stack([core, jnp.ones_like(core), 1 - layer, layer])

    def pick(first, second):
        return jnp.where(on_encoder, first, second)

    def of_one_row(x):
        both = in_order(x[0, :, 0], x_at, 0)
        return in_order(jnp.stack([both[0], over(both[1], "tx")]), x_at, 0).reshape(2 * quarter, -1)

    def rows_out(x, raw=None):
        mine, other = in_order(x.reshape(2, quarter, -1), x_at, 0)
        both = [sent_home(mine, 0), sent_home(other, 1)]
        if raw is not None:
            raw.extend(both)
        return in_order(jnp.stack(both), x_at, 0)[None, :, None]

    units = ffn_in.shape[2]
    width = cross_one.shape[2]
    packed_self = pack_heads(sa_qkv[0, :, 0], sa_qkv[0, :, 1], sa_qkv[0, :, 2], sa_out[0])
    packed_ffn = jnp.concatenate([ffn_in[0], ffn_out[0].T], axis=1)
    with jax.named_scope("norms_in"):
        norms = swapped(jnp.concatenate([norm_gain[0], norm_bias[0]], axis=0))
        gains, biases = norms[:3], norms[3:]
        seg_own = segments[:, :, 0].astype(jnp.float32)
        seg_here = jnp.where(zl_at == 1 ^ zh_at ^ y_at, seg_own, over(seg_own, "zl")).astype(jnp.int32)
    with jax.named_scope("hidden_in"):
        one_row = of_one_row(jnp.concatenate([hidden, cotangent], axis=-1))
    with jax.named_scope("self_weights"):
        shard_self = swapped(packed_self)
    with jax.named_scope("hidden_in"):
        one_row = swapped(after(one_row, shard_self))
    with jax.named_scope("ffn_weights"):
        shard_ffn = swapped(after(packed_ffn, one_row))

    def both_rows(x):
        for_enc = rows_gathered(x, count, layer=0)
        return pick(for_enc, rows_gathered(after(x, for_enc), count, layer=1))

    with jax.named_scope("self_weights"):
        rows_self = both_rows(shard_self)
        own_self = plane_gathered(rows_self)
        w_self = [own_self, over(own_self, "section")]
    with jax.named_scope("hidden_in"):
        rows_here = turned(one_row)
        rows_here, cot = rows_here[:, : hidden.shape[-1]], rows_here[:, hidden.shape[-1] :]
        rows_all = jnp.concatenate([rows_here, over(rows_here, "section")], axis=0)
    with jax.named_scope("cross_weights"):
        cross_low = after(jnp.concatenate([cross_one[0], cross_two[0]], axis=1), own_self)
        pair_kv, pair_qo = cross_in(cross_low, 0), cross_in(cross_low, 1)
        packed = pack_heads(pair_qo[:, :width], pair_kv[:, :width], pair_kv[:, width:], pair_qo[:, width:])
    with jax.named_scope("ffn_weights"):
        rows_ffn = both_rows(after(shard_ffn, rows_self))

    both_segments = in_order(seg_here, x_at, 1)[:, 0]
    ordered = in_order(both_segments.reshape(2, 2, 2 * quarter), core, 1).reshape(2, 4 * quarter)
    source_seg, target_seg = ordered[0], ordered[1]
    self_seg = pick(source_seg, target_seg)
    parts = jnp.arange(4)
    quarter_of = jnp.repeat(2 * ((parts // 2) ^ core) + parts % 2, quarter)
    lanes = jnp.arange(LANES)[None, :]

    def key_extras(seg):
        differs = jnp.logical_and(lanes < SEG_LANES, seg[:, None] != lanes)
        later = jnp.logical_and(
            jnp.logical_and(lanes >= SEG_LANES, lanes < PART_LANE),
            quarter_of[:, None] > lanes - SEG_LANES,
        )
        part = jnp.logical_and(lanes >= PART_LANE, lanes < PART_LANE + 3)
        return jnp.where(differs | later | part, 1.0, 0.0).astype(jnp.bfloat16)

    def query_extras(seg, causal):
        seg, at = seg[: 2 * quarter], quarter_of[: 2 * quarter]
        same = seg[:, None] == lanes
        here = jnp.logical_and(at[:, None] + SEG_LANES == lanes, causal)
        return jnp.where(same | here, MASKED, 0.0).astype(jnp.bfloat16)

    at_row = jnp.arange(quarter)
    later_key = jnp.logical_and(at_row[None, :] > at_row[:, None], jnp.logical_not(on_encoder))
    tri = jnp.where(later_key, MASKED, 0.0).astype(jnp.float32)
    self_extras = (query_extras(self_seg, jnp.logical_not(on_encoder)), key_extras(self_seg), tri)
    cross_extras = (query_extras(target_seg, False), key_extras(source_seg), tri)

    start = rows_all.astype(jnp.float32)
    start = pick(layer_norm(start, gains[0], biases[0]), start)
    start_here = start[: 2 * quarter]
    start_low = low(start)
    self_gain, self_bias = pick(gains[1], gains[0]), pick(biases[1], biases[0])
    raw_cross_rows = []
    with jax.named_scope("cross_weights"):
        rows_cross = rows_gathered(after(packed, rows_ffn), count, raw=raw_cross_rows, layer=1)
    self_out, *kept_self = attend(
        flag, start_low[: 2 * quarter], start_low, w_self, self_extras, True
    )
    with jax.named_scope("ffn_weights"):
        own_ffn = plane_gathered(after(rows_ffn, own_self), until=(self_out, *raw_cross_rows))
        feed = [own_ffn, over(own_ffn, "section")]
    self_total = start_here + after(self_out, *raw_cross_rows)
    middle = layer_norm(self_total, self_gain, self_bias)
    middle_low = low(middle)

    enc_out, enc_active, enc_slope = ffn(enc_flag, middle_low, feed)
    enc_total = middle + enc_out
    encoded = low(layer_norm(enc_total, gains[2], biases[2]))
    def across(x, layer):
        return moved(x, Z, lambda place: {**place, "zl": 1 - place["zl"]} if layer_of(place) == layer else None)

    with jax.named_scope("memory"):
        memory_here = [across(encoded[:quarter], 0), across(encoded[quarter:], 0)]
        memory_peer = [over(part, "section", layer=1) for part in memory_here]
    with jax.named_scope("cross_weights"):
        own_cross = plane_gathered(after(rows_cross, feed[1]), until=tuple(memory_here), layer=1)
        w_cross = [own_cross, over(own_cross, "section", layer=1)]
    (
        decoded,
        crossed_low,
        d_dec_low,
        d_middle_dec,
        d_memory_here,
        d_memory_other,
        dec_sums,
        dec_active,
        dec_inner,
        cross_keep,
        cross_send,
    ) = decoder(
        dec_flag, middle, memory_here + memory_peer, cot, cross_extras[:2], norms, w_cross, feed
    )
    with jax.named_scope("d_memory"):
        d_memory_here = d_memory_here + over(d_memory_other, "section", layer=1).astype(jnp.float32)
        d_memory_low = low(d_memory_here)
        arrived = across(d_memory_low, 1)
    with jax.named_scope("cross_sums"):
        cross_sum = from_cores(after(cross_keep, arrived), after(cross_send, arrived), layer=1)
        raw_cross = []
        cross_plane = plane_summed(cross_sum, raw=raw_cross, layer=1)

    d_enc_total, dz_low, enc_sums, second_keep, second_send = enc_out_back(
        flag, arrived, cot, enc_total, norms, d_dec_low, enc_active, dec_active, feed
    )
    with jax.named_scope("ffn_sums"):
        raw_second_sum = []
        second_sum = from_cores(second_keep, second_send, raw=raw_second_sum)
    gain_row = jnp.broadcast_to(self_gain, (8, self_gain.shape[0]))
    d_self_total, d_self_low, self_norm, first_keep, first_send = enc_in_back(
        flag,
        after(dz_low, second_keep, cross_sum),
        d_enc_total,
        d_middle_dec,
        self_total,
        gain_row,
        middle_low,
        crossed_low,
        feed,
        enc_slope,
        dec_inner,
    )
    with jax.named_scope("ffn_sums"):
        gate = []
        second_plane = plane_summed(after(second_sum, d_self_low), raw=gate)
        first_sum = from_cores(after(first_keep, *raw_cross), after(first_send, *raw_cross), raw=gate)

    halves = []
    for first, earlier in ((0, ()), (2, gate)):
        halves.append(
            attend_back(
                flag,
                after(d_self_low, *earlier),
                start_low[: 2 * quarter],
                start_low,
                w_self,
                kept_self,
                self_extras,
                True,
                first,
                2,
            )
        )
    d_start_q = halves[0][0] + halves[1][0]
    with jax.named_scope("cross_sums"):
        share_cross = rows_summed(after(cross_plane, d_start_q), count, layer=1)
    with jax.named_scope("ffn_sums"):
        gate_later = []
        first_plane = plane_summed(after(first_sum, second_plane), raw=gate_later)
        second_share = rows_summed(second_plane, count, raw=gate_later)
    with jax.named_scope("self_sums"):
        (_, _, keep, send), (_, _, *later) = halves
        self_sum = [from_cores(after(keep, *gate), after(send, *gate), raw=gate_later)]
        raw_later = []
        self_sum.append(from_cores(*(after(part, *gate_later) for part in later), raw=raw_later))
        self_sum = jnp.concatenate(self_sum, axis=0)
    with jax.named_scope("d_start"):
        d_start_kv = after(halves[0][1], *raw_later) + halves[1][1]
        d_start = d_self_total + d_start_q + d_start_kv[: 2 * quarter]
        d_start = d_start + over(low(d_start_kv[2 * quarter :]), "section").astype(jnp.float32)
    d_source, gain_a, bias_a = norm_back(
        rows_here.astype(jnp.float32), gains[0], biases[0], d_start
    )

    rows_from = jnp.concatenate([enc_sums, self_norm, dec_sums, jnp.stack([gain_a, bias_a])], axis=0)
    enc_rows, dec_rows = jnp.array([24, 8, 0, 25, 9, 1]), jnp.array([8, 18, 16, 9, 19, 17])
    wanted = pick(enc_rows, dec_rows)[:, None] == jnp.arange(26)
    norm_sums = jnp.sum(jnp.where(wanted[:, :, None], rows_from[None], 0.0), axis=1)
    shards = 2**count
    sides = jnp.arange(2)
    held, outer = core ^ sides[:, None], sides[None, :]
    row_block = ((2 * outer + (1 ^ outer ^ held)) * shards)[:, :, None] + jnp.arange(shards)
    column_block = (2 * (y_at ^ sides)[:, None] + (x_at ^ sides)[None, :]).reshape(-1)
    order = (row_block.reshape(2, -1)[:, None, :] + 0) * 4 + column_block[:, None]
    norm_sums = jnp.take(norm_sums.reshape(6, 8 * 2 * shards, -1), order.reshape(-1), axis=1)
    norm_sums = norm_sums.reshape(6, 2, 4, 2 * shards, -1)
    with jax.named_scope("norm_sums"):
        norm_got = over(norm_sums[:, 1], "section")
        norm_sums = norm_sums[:, 0] + norm_got
    with jax.named_scope("self_sums"):
        self_plane = plane_summed(self_sum, until=(norm_got,))
    with jax.named_scope("norm_sums"):
        norm_blocks = after(norm_sums.transpose(1, 2, 0, 3).reshape(4, 2 * shards, -1), self_plane)
        norm_plane = norm_blocks[0] + over(norm_blocks[1], "tx") + over(norm_blocks[2], "ty")
        norm_plane = norm_plane + over(norm_blocks[3], "ty", "tx")
    norm_width = norm_plane.shape[1]
    with jax.named_scope("self_sums"):
        pad = ((0, 0), (0, 15), (0, self_plane.shape[1] - norm_width))
        both = jnp.concatenate(
            [
                self_plane.reshape(2 * shards, -1, self_plane.shape[1]),
                jnp.pad(low(norm_plane)[:, None], pad),
            ],
            axis=1,
        )
        raw_self = []
        share_self = rows_summed(both.reshape(-1, self_plane.shape[1]), count, raw=raw_self)
        share_self = swapped(share_self).astype(jnp.float32)
    norm_shares = share_self[-16, :norm_width].reshape(6, -1)
    share_self = share_self[:-16]
    with jax.named_scope("ffn_sums"):
        first_share = rows_summed(after(first_plane, *raw_later), count)
        share_ffn = swapped(jnp.concatenate([first_share, second_share], axis=1)).astype(jnp.float32)
    share_first, share_second = share_ffn[:, :units], share_ffn[:, units:].T
    with jax.named_scope("outputs"):
        outputs = jnp.concatenate([pick(encoded, decoded), low(pick(d_source, d_start))], axis=1)
        outputs = rows_out(after(outputs, *raw_self))
    hidden_out = outputs[..., : hidden.shape[-1]]
    hidden_grad = outputs[..., hidden.shape[-1] :].astype(jnp.float32)
    g_query, g_key, g_value, g_out = unpack_heads(share_self)
    grad_qkv = jnp.stack([g_query, g_key, g_value], axis=1)
    c_query, c_key, c_value, c_out = unpack_heads(share_cross)
    with jax.named_scope("cross_out"):
        for_enc = cross_out(jnp.concatenate([c_key, c_value], axis=1), 0)
        for_dec = cross_out(jnp.concatenate([c_query, c_out], axis=1), 1)
    cross = jnp.where(core == 0, for_enc, for_dec).astype(jnp.float32)

    return (
        hidden_out,
        hidden_grad,
        grad_qkv[None],
        g_out[None],
        cross[None, :, :width],
        cross[None, :, width:],
        share_first[None],
        share_second[None],
        norm_shares[None, :3],
        norm_shares[None, 3:],
    )


def solution(mesh):
    _, dp_count, _ = mesh.devices.shape
    count = dp_count.bit_length() - 3
    names = axes_of(count)
    dp, tensor = names[1:-2], names[-2:]
    split = Mesh(mesh.devices.reshape((2,) * len(names)), names)
    rows = P("section", None, dp, tensor, None)
    in_specs = (
        rows,
        rows,
        P(None, None, dp, None),
        P("section", dp, None, tensor),
        P("section", dp, tensor),
        P("section", dp, tensor),
        P("section", dp, tensor),
        P("section", dp, tensor),
        P("section", tensor, dp),
        P("section", None, None),
        P("section", None, None),
    )
    out_specs = (
        rows,
        rows,
        P("section", dp, None, tensor),
        P("section", dp, tensor),
        P("section", dp, tensor),
        P("section", dp, tensor),
        P("section", dp, tensor),
        P("section", tensor, dp),
        P("section", None, dp + tensor),
        P("section", None, dp + tensor),
    )
    return jax.shard_map(
        functools.partial(body, count), mesh=split, in_specs=in_specs, out_specs=out_specs, check_vma=False
    )
```

```python
import functools

import jax
import jax.numpy as jnp
from jax import lax
from jax.experimental import pallas as pl
from jax.experimental.pallas import tpu as pltpu
from jax.sharding import Mesh
from jax.sharding import PartitionSpec as P

HDIM = 64
LANES = 128
MASKED = -1e30
NORM_EPS = 1e-05
VMEM_BYTES = 56 * 1024 * 1024

SEG_LANES = 8
PART_LANE = 12

PARTS = 2
TILE_ROWS = 256
HEADS = ((0, 1, 2, 0, 0), (0, 1, 2, 1, 1), (1, 3, 0, 0, 1))


def mul(a, b):
    return jnp.dot(a, b, preferred_element_type=jnp.float32)


def mul_nt(a, b):
    return lax.dot_general(a, b, (((1,), (1,)), ((), ())), preferred_element_type=jnp.float32)


def mul_tn(a, b):
    return lax.dot_general(a, b, (((0,), (0,)), ((), ())), preferred_element_type=jnp.float32)


def tile_of(values, index):
    return values[:, index * LANES : (index + 1) * LANES]


def lane_ids(rows):
    return lax.broadcasted_iota(jnp.int32, (rows, LANES), 1)


def half_mask(rows, half):
    lanes = lane_ids(rows)
    return lanes >= HDIM if half else lanes < HDIM


def in_parts(base, column):
    lanes = lane_ids(base.shape[0])
    high = column.astype(jnp.bfloat16).astype(jnp.float32)
    rest = column - high
    middle = rest.astype(jnp.bfloat16).astype(jnp.float32)
    low = rest - middle
    parts = jnp.where(
        lanes == PART_LANE,
        high,
        jnp.where(lanes == PART_LANE + 1, middle, jnp.where(lanes == PART_LANE + 2, low, base)),
    )
    return parts.astype(jnp.bfloat16)


def with_triangle(scores, tri, at):
    size = tri.shape[1]
    pieces = []
    if at > 0:
        pieces.append(scores[:, : at * size])
    pieces.append(scores[:, at * size : (at + 1) * size] + tri)
    pieces.append(scores[:, (at + 1) * size :])
    return jnp.concatenate(pieces, axis=1)


def places(core, block):
    return [pl.multiple_of((1 - core) * block, block), pl.multiple_of((2 + core) * block, block)]


def assemble(flag_ref, own_refs, peer_refs, w_ref):
    core, block = flag_ref[0], own_refs[0].shape[1] // 2
    for holder, refs in ((core, own_refs), (1 - core, peer_refs)):
        for part, ref in enumerate(refs):
            width = ref.shape[2]
            for at, place in enumerate(places(holder, block)):
                w_ref[pl.ds(place, block), part * width : (part + 1) * width] = ref[0, at * block : (at + 1) * block]


def hand_out(flag_ref, g_ref, keep_ref, send_ref):
    core, block = flag_ref[0], keep_ref.shape[1] // 2
    for holder, ref in ((core, keep_ref), (1 - core, send_ref)):
        for at, place in enumerate(places(holder, block)):
            ref[0, at * block : (at + 1) * block] = g_ref[pl.ds(place, block), :]


def where_active(kernel):
    def guarded(flag_ref, *refs):
        @pl.when(flag_ref[1] == 1)
        def _():
            kernel(flag_ref, *refs)

    return guarded


def scaled_queries(q_ref, at, q_tile, q_half):
    queries = q_ref[0, at, q_tile * LANES : (q_tile + 1) * LANES] * 0.125
    return jnp.where(half_mask(queries.shape[0], q_half), queries, 0).astype(jnp.bfloat16)


def units_of(total, rows):
    return [
        (slice(part * rows, (part + 1) * rows), part, head)
        for part in range(total // rows)
        for head in range(len(HEADS))
    ]


def attend_block(causal, xq_ref, xkv_ref, w_ref, qx_ref, kx_ref, tri_ref, q_ref, kv_ref, c_ref, l_ref):
    q_ref[0] = mul(xq_ref[...], w_ref[:, : 2 * LANES]).astype(jnp.bfloat16)
    kv_ref[0] = mul(xkv_ref[...], w_ref[:, LANES : 5 * LANES]).astype(jnp.bfloat16)
    rows = TILE_ROWS
    low = half_mask(rows, 0)

    def scores_of(at, part, head):
        q_tile, k_tile, _, q_half, _ = HEADS[head]
        keys = kv_ref[0, :, k_tile * LANES : (k_tile + 1) * LANES]
        scores = mul_nt(
            jnp.concatenate([scaled_queries(q_ref, at, q_tile, q_half), qx_ref[at, :]], axis=1),
            jnp.concatenate([keys, kx_ref[...]], axis=1),
        )
        return with_triangle(scores, tri_ref[...], part) if causal else scores

    units = units_of(q_ref.shape[1], rows)
    ahead = scores_of(*units[0])
    contexts, totals = [], None
    for index, (at, part, head) in enumerate(units):
        scores = ahead
        if index + 1 < len(units):
            ahead = scores_of(*units[index + 1])
        v_tile = HEADS[head][2]
        values = kv_ref[0, :, v_tile * LANES : (v_tile + 1) * LANES]
        highest = jnp.max(scores, axis=1, keepdims=True)
        weights = jnp.exp(scores - highest)
        sums = jnp.sum(weights, axis=1, keepdims=True)
        contexts.append(mul(weights.astype(jnp.bfloat16), values) / sums)
        logs = jnp.broadcast_to(highest + jnp.log(sums), (rows, LANES))
        totals = logs if head == 0 else jnp.where(lane_ids(rows) == head, logs, totals)
        if head == len(HEADS) - 1:
            c_ref[0, at, :LANES] = jnp.where(low, 0, contexts[2]).astype(jnp.bfloat16)
            c_ref[0, at, LANES:] = jnp.where(low, contexts[0], contexts[1]).astype(jnp.bfloat16)
            l_ref[0, at, :] = totals
            contexts = []
    return mul_nt(c_ref[0], w_ref[:, 4 * LANES :])


def attend_kernel(causal, flag_ref, xq_ref, xkv_ref, own_ref, peer_ref, qx_ref, kx_ref, tri_ref, o_ref, *refs):
    q_ref, kv_ref, c_ref, l_ref, w_ref = refs
    assemble(flag_ref, [own_ref], [peer_ref], w_ref)
    out = attend_block(causal, xq_ref, xkv_ref, w_ref, qx_ref, kx_ref, tri_ref, q_ref, kv_ref, c_ref, l_ref)
    add_up(pl.program_id(0) == 0, o_ref, out)


def add_up(first, ref, value):
    @pl.when(first)
    def _():
        ref[...] = value

    @pl.when(jnp.logical_not(first))
    def _():
        ref[...] += value


def attend_back_block(causal, do_ref, xq_ref, xkv_ref, w_ref, qx_ref, kx_ref, tri_ref, kept, work):
    q_ref, kv_ref, c_ref, l_ref = kept
    sum_ref, dq_ref, dkv_ref, g_ref = work
    rows = TILE_ROWS
    d_context = mul(do_ref[...], w_ref[:, 4 * LANES :]).astype(jnp.bfloat16)
    low = half_mask(rows, 0)

    def products_of(at, part, head):
        q_tile, k_tile, v_tile, q_half, v_half = HEADS[head]
        c_tile = 0 if head == 2 else 1
        keys = kv_ref[0, :, k_tile * LANES : (k_tile + 1) * LANES]
        values = kv_ref[0, :, v_tile * LANES : (v_tile + 1) * LANES]
        queries = scaled_queries(q_ref, at, q_tile, q_half)
        d_rows = jnp.where(half_mask(rows, v_half), tile_of(d_context[at], c_tile), 0).astype(jnp.bfloat16)
        total = l_ref[0, at, head : head + 1]
        scores = mul_nt(
            jnp.concatenate([queries, in_parts(qx_ref[at, :].astype(jnp.float32), -total)], axis=1),
            jnp.concatenate([keys, kx_ref[...]], axis=1),
        )
        if causal:
            scores = with_triangle(scores, tri_ref[...], part)
        return scores, mul_nt(d_rows, values), queries, d_rows, keys

    units = units_of(q_ref.shape[1], rows)
    ahead = products_of(*units[0])
    d_queries = []
    for index, (at, part, head) in enumerate(units):
        scores, d_probs, queries, d_rows, keys = ahead
        if index + 1 < len(units):
            ahead = products_of(*units[index + 1])
        _, k_tile, v_tile, _, _ = HEADS[head]
        probs = jnp.exp(scores)
        inner = jnp.sum(probs * d_probs, axis=1, keepdims=True)
        d_scores = (probs * (d_probs - inner)).astype(jnp.bfloat16)
        d_values = mul_tn(probs.astype(jnp.bfloat16), d_rows)
        d_keys = mul_tn(d_scores, queries)
        d_queries.append(mul(d_scores, keys) * 0.125)
        k_at = slice(k_tile * LANES, (k_tile + 1) * LANES)
        v_at = slice(v_tile * LANES, (v_tile + 1) * LANES)
        if part == 0 and head != 1:
            sum_ref[:, k_at] = d_keys
            sum_ref[:, v_at] = d_values
        else:
            sum_ref[:, k_at] += d_keys
            sum_ref[:, v_at] += d_values
        if head == len(HEADS) - 1:
            dq_ref[at, :LANES] = jnp.where(low, d_queries[0], d_queries[1]).astype(jnp.bfloat16)
            dq_ref[at, LANES:] = jnp.where(low, d_queries[2], 0).astype(jnp.bfloat16)
            d_queries = []
    dkv_ref[...] = sum_ref[...].astype(jnp.bfloat16)
    d_xq = mul_nt(dq_ref[...], w_ref[:, : 2 * LANES])
    d_xkv = mul_nt(dkv_ref[...], w_ref[:, LANES : 5 * LANES])

    grad_q = mul_tn(xq_ref[...], dq_ref[...])
    grad_kv = mul_tn(xkv_ref[...], dkv_ref[...])
    grad_o = mul_tn(do_ref[...], c_ref[0])
    g_ref[:, :LANES] = grad_q[:, :LANES].astype(jnp.bfloat16)
    g_ref[:, LANES : 2 * LANES] = (grad_q[:, LANES:] + grad_kv[:, :LANES]).astype(jnp.bfloat16)
    g_ref[:, 2 * LANES : 4 * LANES] = grad_kv[:, LANES : 3 * LANES].astype(jnp.bfloat16)
    g_ref[:, 4 * LANES : 5 * LANES] = (grad_kv[:, 3 * LANES :] + grad_o[:, :LANES]).astype(jnp.bfloat16)
    g_ref[:, 5 * LANES :] = grad_o[:, LANES:].astype(jnp.bfloat16)
    return d_xq, d_xkv


def attend_back_kernel(causal, flag_ref, do_ref, xq_ref, xkv_ref, own_ref, peer_ref, *refs):
    kept, (qx_ref, kx_ref, tri_ref, dxq_ref, dxkv_ref, keep_ref, send_ref, w_ref) = refs[:4], refs[4:12]
    work = refs[12:]
    assemble(flag_ref, [own_ref], [peer_ref], w_ref)
    d_xq, d_xkv = attend_back_block(
        causal, do_ref, xq_ref, xkv_ref, w_ref, qx_ref, kx_ref, tri_ref, kept, work
    )
    add_up(pl.program_id(0) == 0, dxq_ref, d_xq)
    add_up(pl.program_id(0) == 0, dxkv_ref, d_xkv)
    hand_out(flag_ref, work[3], keep_ref, send_ref)


def whole(shape):
    return pl.BlockSpec(shape, lambda j, flag: (0,) * len(shape))


def held(shape):
    return pl.BlockSpec(shape, lambda j, flag: (0,) * len(shape), pipeline_mode=pl.Buffered(1))


def per_block(shape, first=0, gate=1):
    return pl.BlockSpec((1,) + shape, lambda j, flag: (first + j * flag[gate],) + (0,) * len(shape))


shape = jax.ShapeDtypeStruct


def call(kernel, name, micros, moved, grid, in_specs, out_specs, out_shape, scratch, *operands):
    return pl.pallas_call(
        where_active(kernel),
        grid_spec=pltpu.PrefetchScalarGridSpec(
            num_scalar_prefetch=1,
            grid=(grid,),
            in_specs=in_specs,
            out_specs=out_specs,
            scratch_shapes=scratch,
        ),
        out_shape=out_shape,
        compiler_params=pltpu.CompilerParams(vmem_limit_bytes=VMEM_BYTES),
        cost_estimate=cost(micros, moved),
        name=name,
    )(*operands)


def cost(micros, moved):
    return pl.CostEstimate(flops=int(micros * 1.15e9), bytes_accessed=int(moved), transcendentals=0)


def attend(flag, xq, xkv, weights, extras, causal):
    rows, width = xq.shape
    keys = xkv.shape[0]
    blocks = weights[0].shape[0]
    return call(
        functools.partial(attend_kernel, causal),
        "attend_self" if causal else "attend_cross",
        20,
        24 * 2**20,
        blocks,
        [held((rows, width)), held((keys, width))]
        + [per_block(part.shape[1:]) for part in weights]
        + [held(extra.shape) for extra in extras],
        [
            whole((rows, width)),
            per_block((rows, 2 * LANES)),
            per_block((keys, 4 * LANES)),
            per_block((rows, 2 * LANES)),
            per_block((rows, LANES)),
        ],
        [
            shape((rows, width), jnp.float32),
            shape((blocks, rows, 2 * LANES), jnp.bfloat16),
            shape((blocks, keys, 4 * LANES), jnp.bfloat16),
            shape((blocks, rows, 2 * LANES), jnp.bfloat16),
            shape((blocks, rows, LANES), jnp.float32),
        ],
        [pltpu.VMEM((width, 6 * LANES), jnp.bfloat16)],
        flag,
        xq,
        xkv,
        *weights,
        *extras,
    )


def attend_back(flag, d_out, xq, xkv, weights, kept, extras, causal, first, count):
    rows, width = xq.shape
    keys = xkv.shape[0]
    return call(
        functools.partial(attend_back_kernel, causal),
        "attend_self_back" if causal else "attend_cross_back",
        10 * count,
        6 * 2**20 * count,
        count,
        [held((rows, width)), held((rows, width)), held((keys, width))]
        + [per_block(part.shape[1:], first) for part in weights]
        + [
            per_block((rows, 2 * LANES), first),
            per_block((keys, 4 * LANES), first),
            per_block((rows, 2 * LANES), first),
            per_block((rows, LANES), first),
        ]
        + [held(extra.shape) for extra in extras],
        [whole((rows, width)), whole((keys, width))] + [per_block(part.shape[1:]) for part in weights],
        [shape((rows, width), jnp.float32), shape((keys, width), jnp.float32)]
        + [shape((count,) + part.shape[1:], jnp.bfloat16) for part in weights],
        [
            pltpu.VMEM((width, 6 * LANES), jnp.bfloat16),
            pltpu.VMEM((keys, 4 * LANES), jnp.float32),
            pltpu.VMEM((rows, 2 * LANES), jnp.bfloat16),
            pltpu.VMEM((keys, 4 * LANES), jnp.bfloat16),
            pltpu.VMEM((width, 6 * LANES), jnp.bfloat16),
        ],
        flag,
        d_out,
        xq,
        xkv,
        *weights,
        *kept,
        *extras,
    )


def ffn_block(x_ref, w_ref, units, g_ref, slope_ref, first, out_ref):
    inner = mul(x_ref[...], w_ref[:, :units])
    spread = 0.5 * (1.0 + lax.erf(inner * (0.5**0.5)))
    bell = jnp.exp(-0.5 * inner * inner) * 0.3989422804014327
    active = (inner * spread).astype(jnp.bfloat16)
    g_ref[0] = active
    slope_ref[0] = (spread + inner * bell).astype(jnp.bfloat16)
    add_up(first, out_ref, mul_nt(active, w_ref[:, units:]))


def ffn_kernel(flag_ref, x_ref, *refs):
    own_refs, peer_refs = refs[:PARTS], refs[PARTS : 2 * PARTS]
    z_ref, g_ref, slope_ref, w_ref = refs[2 * PARTS :]
    assemble(flag_ref, own_refs, peer_refs, w_ref)
    ffn_block(x_ref, w_ref, own_refs[0].shape[2], g_ref, slope_ref, pl.program_id(0) == 0, z_ref)


def feed_blocks(feed, index):
    half, units = feed[0].shape[1], feed[0].shape[2] // 2
    return [
        pl.BlockSpec((1, half, units), lambda j, flag, side=side: (index(j, flag), 0, side))
        for _ in feed
        for side in (0, 1)
    ]


def feed_operands(feed):
    return [part for part in feed for _ in (0, 1)]


def ffn(flag, x, feed):
    rows, width = x.shape
    blocks, units = feed[0].shape[0], feed[0].shape[2] // 2
    return call(
        ffn_kernel,
        "ffn",
        12,
        rows * units * blocks * 16,
        blocks,
        [held((rows, width))] + feed_blocks(feed, lambda j, flag: j * flag[1]),
        [whole((rows, width)), per_block((rows, units)), per_block((rows, units))],
        [
            shape((rows, width), jnp.float32),
            shape((blocks, rows, units), jnp.bfloat16),
            shape((blocks, rows, units), jnp.bfloat16),
        ],
        [pltpu.VMEM((width, 2 * units), jnp.bfloat16)],
        flag,
        x,
        *feed_operands(feed),
    )


def ffn_back_block(dz_ref, w_ref, units, slope_ref, dh_ref, first, out_ref):
    d_active = mul(dz_ref[...], w_ref[:, units:])
    d_inner = (d_active * slope_ref[0].astype(jnp.float32)).astype(jnp.bfloat16)
    dh_ref[0] = d_inner
    add_up(first, out_ref, mul_nt(d_inner, w_ref[:, :units]))


def layer_norm(values, gain_row, bias_row):
    average = jnp.mean(values, axis=-1, keepdims=True)
    centered = values - average
    variance = jnp.mean(centered * centered, axis=-1, keepdims=True)
    return centered * lax.rsqrt(variance + NORM_EPS) * gain_row + bias_row


def norm_back(values, gain_row, bias_row, upstream):
    _, pullback = jax.vjp(layer_norm, values, gain_row, bias_row)
    return pullback(upstream)


def norm_parts(values):
    average = jnp.mean(values, axis=1, keepdims=True)
    centered = values - average
    scale = lax.rsqrt(jnp.mean(centered * centered, axis=1, keepdims=True) + NORM_EPS)
    return centered * scale, scale


def norm_gradients(values, gain_row, upstream):
    shaped, scale = norm_parts(values)
    inner = upstream * gain_row
    mean_inner = jnp.mean(inner, axis=1, keepdims=True)
    mean_product = jnp.mean(inner * shaped, axis=1, keepdims=True)
    d_values = scale * (inner - mean_inner - shaped * mean_product)
    d_gain = jnp.sum(upstream * shaped, axis=0, keepdims=True)
    return d_values, d_gain, jnp.sum(upstream, axis=0, keepdims=True)


def enc_out_back_kernel(
    flag_ref, arrived_ref, cot_ref, total_ref, norms_ref, d_dec_ref, enc_ref, dec_ref, *refs
):
    d_total_ref, dz_ref, sums_ref, keep_ref, send_ref, g_ref, left_t_ref = refs

    @pl.when(jnp.logical_and(pl.program_id(0) == 0, flag_ref[2] == 1))
    def _():
        upstream = arrived_ref[...].astype(jnp.float32) + cot_ref[...].astype(jnp.float32)
        d_total, sums_ref[0:1, :], sums_ref[1:2, :] = norm_gradients(total_ref[...], norms_ref[2:3, :], upstream)
        d_total_ref[...] = d_total
        dz_ref[...] = d_total.astype(jnp.bfloat16)

    @pl.when(jnp.logical_and(pl.program_id(0) == 0, flag_ref[2] == 0))
    def _():
        dz_ref[...] = d_dec_ref[...]

    @pl.when(pl.program_id(0) == 0)
    def _():
        left_t_ref[...] = dz_ref[...].T

    right = jnp.where(flag_ref[2] == 1, enc_ref[0], dec_ref[0])
    g_ref[...] = mul(left_t_ref[...], right).astype(jnp.bfloat16)
    hand_out(flag_ref, g_ref, keep_ref, send_ref)


def enc_out_back(flag, arrived, cot, total, norms, d_dec, enc_active, dec_active, feed):
    rows, width = cot.shape
    blocks, _, units = enc_active.shape
    like = shape((blocks, feed[0].shape[1], units), jnp.bfloat16)
    full = shape((rows, width), jnp.float32)
    return call(
        enc_out_back_kernel,
        "enc_out_back",
        9,
        rows * units * blocks * 8,
        blocks,
        [held(item.shape) for item in (arrived, cot, total, norms, d_dec)]
        + [per_block((rows, units), 0, 2), per_block((rows, units), 0, 3)],
        [whole((rows, width))] * 2 + [whole((8, width))] + [per_block(like.shape[1:])] * 2,
        [full, shape((rows, width), jnp.bfloat16), shape((8, width), jnp.float32)]
        + [like] * 2,
        [pltpu.VMEM((width, units), jnp.bfloat16), pltpu.VMEM((width, rows), jnp.bfloat16)],
        flag,
        arrived,
        cot,
        total,
        norms,
        d_dec,
        enc_active,
        dec_active,
    )


def enc_in_back_kernel(
    flag_ref, dz_ref, d_enc_ref, d_middle_ref, total_ref, gain_ref, middle_ref, crossed_ref, *refs
):
    first_own_ref, second_own_ref, first_peer_ref, second_peer_ref, slope_ref, dec_inner_ref, *refs = refs
    d_total_ref, d_low_ref, sums_ref, keep_ref, send_ref, w_ref, inner_ref, out_ref, g_ref, left_t_ref = refs
    step = pl.program_id(0)
    phase, at = step // 4, step % 4
    on_encoder = flag_ref[2] == 1

    @pl.when(jnp.logical_and(phase == 0, on_encoder))
    def _():
        assemble(flag_ref, [first_own_ref, second_own_ref], [first_peer_ref, second_peer_ref], w_ref)
        ffn_back_block(
            dz_ref, w_ref, first_own_ref.shape[2], slope_ref, inner_ref.at[pl.ds(at, 1)], at == 0, out_ref
        )

    @pl.when(step == 3)
    def _():
        upstream = jnp.where(on_encoder, d_enc_ref[...] + out_ref[...], d_middle_ref[...])
        d_total, sums_ref[0:1, :], sums_ref[1:2, :] = norm_gradients(total_ref[...], gain_ref[0:1, :], upstream)
        d_total_ref[...] = d_total
        d_low_ref[...] = d_total.astype(jnp.bfloat16)
        left_t_ref[...] = jnp.where(on_encoder, middle_ref[...], crossed_ref[...]).T

    @pl.when(phase == 1)
    def _():
        right = jnp.where(on_encoder, inner_ref[at], dec_inner_ref[0])
        g_ref[...] = mul(left_t_ref[...], right).astype(jnp.bfloat16)
        hand_out(flag_ref, g_ref, keep_ref, send_ref)


def enc_in_back(flag, dz, d_enc, d_middle, total, gain, middle, crossed, feed, slope, dec_inner):
    rows, width = dz.shape
    blocks, half, units = feed[0].shape[0], feed[0].shape[1], feed[0].shape[2] // 2
    full = shape((rows, width), jnp.float32)

    def at_step(of, low, high, gate):
        def index(j, flag):
            return (jnp.where(j < 4, j if low == "up" else low, j - 4 if high == "up" else high) * flag[gate],) + (
                0,
            ) * len(of)

        return pl.BlockSpec((1,) + of, index)

    return call(
        enc_in_back_kernel,
        "enc_in_back",
        19,
        rows * units * blocks * 20,
        8,
        [held(item.shape) for item in (dz, d_enc, d_middle, total, gain, middle, crossed)]
        + feed_blocks(feed, lambda j, flag: jnp.where(j < 4, j, 3) * flag[2])
        + [at_step((rows, units), "up", 3, 2), at_step((rows, units), 0, "up", 3)],
        [whole((rows, width))] * 2 + [whole((8, width))] + [at_step((half, units), 0, "up", 1)] * 2,
        [full, shape((rows, width), jnp.bfloat16), shape((8, width), jnp.float32)]
        + [shape((blocks, half, units), jnp.bfloat16)] * 2,
        [
            pltpu.VMEM((width, 2 * units), jnp.bfloat16),
            pltpu.VMEM((blocks, rows, units), jnp.bfloat16),
            pltpu.VMEM((rows, width), jnp.float32),
            pltpu.VMEM((width, units), jnp.bfloat16),
            pltpu.VMEM((width, rows), jnp.bfloat16),
        ],
        flag,
        dz,
        d_enc,
        d_middle,
        total,
        gain,
        middle,
        crossed,
        *feed_operands(feed),
        slope,
        dec_inner,
    )


def decoder_kernel(
    flag_ref,
    h1_ref,
    mem_a_ref,
    mem_b_ref,
    peer_a_ref,
    peer_b_ref,
    cot_ref,
    qx_ref,
    kx_ref,
    norms_ref,
    own_ref,
    peer_ref,
    first_own_ref,
    second_own_ref,
    first_peer_ref,
    second_peer_ref,
    decoded_ref,
    crossed_ref,
    d_dec_ref,
    d_middle_ref,
    mine_ref,
    other_ref,
    sums_ref,
    active_ref,
    inner_ref,
    keep_ref,
    send_ref,
    xq_ref,
    xkv_ref,
    wx_ref,
    wf_ref,
    q_ref,
    kv_ref,
    c_ref,
    l_ref,
    slope_ref,
    out_ref,
    total_ref,
    do_ref,
    dxkv_ref,
    *work,
):
    step = pl.program_id(0)
    phase, at = step // 4, step % 4
    first, last = at == 0, at == 3
    rows = h1_ref.shape[0]
    units = first_own_ref.shape[2]
    gain = [norms_ref[row : row + 1, :] for row in range(3)]
    bias = [norms_ref[3 + row : 4 + row, :] for row in range(3)]

    def kept(block):
        return tuple(ref.at[pl.ds(block, 1)] for ref in (q_ref, kv_ref, c_ref, l_ref))

    @pl.when(step == 0)
    def _():
        xq_ref[...] = h1_ref[...].astype(jnp.bfloat16)
        for part, ref in enumerate((mem_a_ref, mem_b_ref, peer_a_ref, peer_b_ref)):
            xkv_ref[part * rows // 2 : (part + 1) * rows // 2] = ref[...]

    @pl.when(jnp.logical_or(phase == 0, phase == 3))
    def _():
        assemble(flag_ref, [own_ref], [peer_ref], wx_ref)

    @pl.when(jnp.logical_or(phase == 1, phase == 2))
    def _():
        assemble(flag_ref, [first_own_ref, second_own_ref], [first_peer_ref, second_peer_ref], wf_ref)

    @pl.when(phase == 0)
    def _():
        add_up(first, out_ref, attend_block(False, xq_ref, xkv_ref, wx_ref, qx_ref, kx_ref, None, *kept(at)))

    @pl.when(jnp.logical_and(phase == 0, last))
    def _():
        total = h1_ref[...] + out_ref[...]
        total_ref[...] = total
        crossed = norm_parts(total)[0] * gain[1] + bias[1]
        mine_ref[...] = crossed
        crossed_ref[...] = crossed.astype(jnp.bfloat16)

    @pl.when(phase == 1)
    def _():
        ffn_block(crossed_ref, wf_ref, units, active_ref, slope_ref.at[pl.ds(at, 1)], first, out_ref)

    @pl.when(jnp.logical_and(phase == 1, last))
    def _():
        total = mine_ref[...] + out_ref[...]
        decoded_ref[...] = (norm_parts(total)[0] * gain[2] + bias[2]).astype(jnp.bfloat16)
        d_total, sums_ref[0:1, :], sums_ref[1:2, :] = norm_gradients(
            total, gain[2], cot_ref[...].astype(jnp.float32)
        )
        d_middle_ref[...] = d_total
        d_dec_ref[...] = d_total.astype(jnp.bfloat16)

    @pl.when(phase == 2)
    def _():
        ffn_back_block(d_dec_ref, wf_ref, units, slope_ref.at[pl.ds(3 - at, 1)], inner_ref, first, out_ref)

    @pl.when(jnp.logical_and(phase == 2, last))
    def _():
        d_total, sums_ref[2:3, :], sums_ref[3:4, :] = norm_gradients(
            total_ref[...], gain[1], d_middle_ref[...] + out_ref[...]
        )
        d_middle_ref[...] = d_total
        do_ref[...] = d_total.astype(jnp.bfloat16)

    @pl.when(phase == 3)
    def _():
        d_xq, d_xkv = attend_back_block(
            False, do_ref, xq_ref, xkv_ref, wx_ref, qx_ref, kx_ref, None, kept(3 - at), work
        )
        add_up(first, out_ref, d_xq)
        add_up(first, dxkv_ref, d_xkv)
        hand_out(flag_ref, work[3], keep_ref, send_ref)

    @pl.when(jnp.logical_and(phase == 3, last))
    def _():
        d_middle_ref[...] += out_ref[...]
        mine_ref[...] = dxkv_ref[:rows]
        other_ref[...] = dxkv_ref[rows:].astype(jnp.bfloat16)


def decoder(flag, h1, memory, cot, extras, norms, cross, feed):
    rows, width = h1.shape
    blocks, half, _ = cross[0].shape
    units = feed[0].shape[2] // 2
    keys = 2 * rows
    qx, kx = extras

    def at_step(of, in_phase):
        def index(j, flag):
            at = j % 4
            choice = [{"up": at, "down": 3 - at}.get(way, way) for way in in_phase]
            chosen = choice[3]
            for phase in (2, 1, 0):
                chosen = jnp.where(j // 4 == phase, choice[phase], chosen)
            return (chosen * flag[1],) + (0,) * len(of)

        return pl.BlockSpec((1,) + of, index)

    part = (half, cross[0].shape[2])
    full = shape((rows, width), jnp.float32)
    rounded = shape((rows, width), jnp.bfloat16)
    return call(
        decoder_kernel,
        "decoder",
        90,
        40 * 2**20,
        16,
        [held(item.shape) for item in (h1, *memory, cot, qx, kx, norms)]
        + [at_step(part, ("up", 3, 3, "down"))] * 2
        + feed_blocks(feed, lambda j, flag: at_step((half, units), (0, "up", "down", 0)).index_map(j, flag)[0]),
        [whole((rows, width))] * 6
        + [whole((8, width))]
        + [
            at_step((rows, units), (0, "up", 3, 3)),
            at_step((rows, units), (3, 3, "down", 0)),
            at_step(part, (3, 3, 3, "down")),
            at_step(part, (3, 3, 3, "down")),
        ],
        [rounded, rounded, rounded, full, full, rounded, shape((8, width), jnp.float32)]
        + [shape((blocks, rows, units), jnp.bfloat16)] * 2
        + [shape(cross[0].shape, jnp.bfloat16)] * 2,
        [
            pltpu.VMEM((rows, width), jnp.bfloat16),
            pltpu.VMEM((keys, width), jnp.bfloat16),
            pltpu.VMEM((width, 6 * LANES), jnp.bfloat16),
            pltpu.VMEM((width, 2 * units), jnp.bfloat16),
            pltpu.VMEM((blocks, rows, 2 * LANES), jnp.bfloat16),
            pltpu.VMEM((blocks, keys, 4 * LANES), jnp.bfloat16),
            pltpu.VMEM((blocks, rows, 2 * LANES), jnp.bfloat16),
            pltpu.VMEM((blocks, rows, LANES), jnp.float32),
            pltpu.VMEM((blocks, rows, units), jnp.bfloat16),
            pltpu.VMEM((rows, width), jnp.float32),
            pltpu.VMEM((rows, width), jnp.float32),
            pltpu.VMEM((rows, width), jnp.bfloat16),
            pltpu.VMEM((keys, width), jnp.float32),
            pltpu.VMEM((keys, 4 * LANES), jnp.float32),
            pltpu.VMEM((rows, 2 * LANES), jnp.bfloat16),
            pltpu.VMEM((keys, 4 * LANES), jnp.bfloat16),
            pltpu.VMEM((width, 6 * LANES), jnp.bfloat16),
        ],
        flag,
        h1,
        *memory,
        cot,
        qx,
        kx,
        norms,
        *cross,
        *feed_operands(feed),
    )


def low(values):
    return values.astype(jnp.bfloat16)


def axes_of(count):
    return ("section", "zh", "zl") + tuple("e%d" % at for at in range(count)) + ("ty", "tx")


def layer_of(place):
    return 1 ^ place["zh"] ^ place["zl"]


def moved(x, names, to):
    names = [name for name in axes_of(8) if name in names]

    def index(place):
        return sum(place[name] << (len(names) - 1 - at) for at, name in enumerate(names))

    pairs = []
    for source in range(2 ** len(names)):
        place = {name: source >> (len(names) - 1 - at) & 1 for at, name in enumerate(names)}
        target = to(place)
        if target is not None:
            pairs.append((source, index(target)))
    return lax.ppermute(x, tuple(names), pairs)


def over(x, *axes, layer=None):
    def to(place):
        if layer is not None and layer_of(place) != layer:
            return None
        return {**place, **{axis: 1 - place[axis] for axis in axes}}

    return moved(x, axes if layer is None else axes + Z, to)


Z = ("zh", "zl")


def swapped(x):
    def to(place):
        if place["section"] == layer_of(place):
            return place
        return {"section": 1 - place["section"], "zh": place["zh"], "zl": 1 - place["zl"]}

    return moved(x, ("section",) + Z, to)


def turned(x):
    return moved(x, ("section", "ty"), lambda place: {"section": place["ty"], "ty": place["section"]})


def sent_home(x, other):
    def to(place):
        return {
            "section": layer_of(place),
            "zh": place["zh"],
            "zl": 1 ^ place["zh"] ^ place["ty"],
            "ty": place["section"],
            "tx": place["tx"] ^ other,
        }

    return moved(x, ("section",) + Z + ("ty", "tx"), to)


def cross_in(x, layer):
    def to(place):
        if place["section"] != layer:
            return None
        return {"section": layer_of(place), "zh": place["zh"], "zl": place["zh"]}

    return moved(x, ("section",) + Z, to)


def cross_out(x, layer):
    def to(place):
        if layer_of(place) != 1:
            return None
        return {"section": layer, "zh": place["zh"], "zl": 1 ^ place["zh"] ^ place["section"]}

    return moved(x, ("section",) + Z, to)


def in_order(x, flag, axis):
    return jnp.where(flag == 1, jnp.flip(x, axis), x)


def pack_heads(query, key, value, out):
    pair = 2 * HDIM
    return jnp.concatenate(
        [
            query,
            value[:, pair:],
            key[:, :pair],
            value[:, :pair],
            key[:, pair:],
            out[:, pair:],
            out[:, :pair],
        ],
        axis=1,
    )


def unpack_heads(packed):
    part = [packed[:, at * HDIM : (at + 1) * HDIM] for at in range(12)]
    query = jnp.concatenate(part[0:3], axis=1)
    key = jnp.concatenate([part[4], part[5], part[8]], axis=1)
    value = jnp.concatenate([part[6], part[7], part[3]], axis=1)
    out = jnp.concatenate([part[10], part[11], part[9]], axis=1)
    return query, key, value, out


def after(x, *earlier):
    return lax.optimization_barrier((x,) + earlier)[0]


def plane_gathered(x, until=(), **only):
    parts = [x, over(x, "tx", **only), over(x, "ty", **only), over(x, "ty", "tx", **only)]
    return jnp.stack([after(part, *until) for part in parts])


def plane_summed(x, until=(), raw=None, **only):
    terms = [x[0], over(x[1], "tx", **only), over(x[2], "ty", **only), over(x[3], "ty", "tx", **only)]
    if raw is not None:
        raw.extend(terms[1:])
    terms = [after(term, *until) for term in terms]
    return low(sum(term.astype(jnp.float32) for term in terms))


def rows_gathered(x, count, until=(), raw=None, **only):
    for axes in [("e%d" % at,) for at in reversed(range(count))] + [Z]:
        got = over(x, *axes, **only)
        if raw is not None:
            raw.append(got)
        parts = [after(part, *until) for part in (x, got)]
        both = in_order(jnp.stack(parts, axis=-3), lax.axis_index(axes[0]), x.ndim - 2)
        x = both.reshape(x.shape[:-2] + (2 * x.shape[-2], x.shape[-1]))
    return x


def rows_summed(x, count, until=(), raw=None, **only):
    for axes in [Z] + [("e%d" % at,) for at in range(count)]:
        halves = x.reshape(x.shape[:-2] + (2, x.shape[-2] // 2, x.shape[-1]))
        halves = in_order(halves, lax.axis_index(axes[0]), x.ndim - 2)
        got = over(halves[..., 1, :, :], *axes, **only)
        if raw is not None:
            raw.append(got)
        x = plus(halves[..., 0, :, :], after(got, *until))
    return x


def plus(first, second):
    return low(first.astype(jnp.float32) + second.astype(jnp.float32))


def from_cores(keep, send, raw=None, **only):
    got = over(send, "section", **only)
    if raw is not None:
        raw.append(got)
    return plus(keep, got)


def body(
    count,
    hidden,
    cotangent,
    segments,
    sa_qkv,
    sa_out,
    cross_one,
    cross_two,
    ffn_in,
    ffn_out,
    norm_gain,
    norm_bias,
):
    core = lax.axis_index("section")
    x_at, y_at, zh_at, zl_at = (lax.axis_index(name) for name in ("tx", "ty", "zh", "zl"))
    layer = 1 ^ zh_at ^ zl_at
    on_encoder = layer == 0
    quarter = hidden.shape[3]
    enc_flag = jnp.stack([core, 1 - layer, 1 - layer, layer])
    dec_flag = jnp.stack([core, layer, 1 - layer, layer])
    flag = jnp.stack([core, jnp.ones_like(core), 1 - layer, layer])

    def pick(first, second):
        return jnp.where(on_encoder, first, second)

    def of_one_row(x):
        both = in_order(x[0, :, 0], x_at, 0)
        return in_order(jnp.stack([both[0], over(both[1], "tx")]), x_at, 0).reshape(2 * quarter, -1)

    def rows_out(x, raw=None):
        mine, other = in_order(x.reshape(2, quarter, -1), x_at, 0)
        both = [sent_home(mine, 0), sent_home(other, 1)]
        if raw is not None:
            raw.extend(both)
        return in_order(jnp.stack(both), x_at, 0)[None, :, None]

    units = ffn_in.shape[2]
    width = cross_one.shape[2]
    packed_self = pack_heads(sa_qkv[0, :, 0], sa_qkv[0, :, 1], sa_qkv[0, :, 2], sa_out[0])
    packed_ffn = jnp.concatenate([ffn_in[0], ffn_out[0].T], axis=1)
    with jax.named_scope("norms_in"):
        norms = swapped(jnp.concatenate([norm_gain[0], norm_bias[0]], axis=0))
        gains, biases = norms[:3], norms[3:]
        seg_own = segments[:, :, 0].astype(jnp.float32)
        seg_here = jnp.where(zl_at == 1 ^ zh_at ^ y_at, seg_own, over(seg_own, "zl")).astype(jnp.int32)
    with jax.named_scope("hidden_in"):
        one_row = of_one_row(jnp.concatenate([hidden, cotangent], axis=-1))
    with jax.named_scope("self_weights"):
        shard_self = swapped(packed_self)
    with jax.named_scope("hidden_in"):
        one_row = swapped(after(one_row, shard_self))
    with jax.named_scope("ffn_weights"):
        shard_ffn = swapped(after(packed_ffn, one_row))

    def both_rows(x):
        for_enc = rows_gathered(x, count, layer=0)
        return pick(for_enc, rows_gathered(after(x, for_enc), count, layer=1))

    with jax.named_scope("self_weights"):
        rows_self = both_rows(shard_self)
        raw_ffn_rows = []
        rows_ffn_enc = rows_gathered(after(shard_ffn, rows_self), count, raw=raw_ffn_rows, layer=0)
        own_self = plane_gathered(rows_self, until=tuple(raw_ffn_rows))
        w_self = [own_self, over(own_self, "section")]
    with jax.named_scope("hidden_in"):
        rows_here = turned(one_row)
        rows_here, cot = rows_here[:, : hidden.shape[-1]], rows_here[:, hidden.shape[-1] :]
        rows_all = jnp.concatenate([rows_here, over(rows_here, "section")], axis=0)
    with jax.named_scope("cross_weights"):
        cross_low = after(jnp.concatenate([cross_one[0], cross_two[0]], axis=1), own_self)
        pair_kv, pair_qo = cross_in(cross_low, 0), cross_in(cross_low, 1)
        packed = pack_heads(pair_qo[:, :width], pair_kv[:, :width], pair_kv[:, width:], pair_qo[:, width:])
    with jax.named_scope("ffn_weights"):
        rows_ffn = pick(rows_ffn_enc, rows_gathered(after(shard_ffn, *raw_ffn_rows), count, layer=1))

    both_segments = in_order(seg_here, x_at, 1)[:, 0]
    ordered = in_order(both_segments.reshape(2, 2, 2 * quarter), core, 1).reshape(2, 4 * quarter)
    source_seg, target_seg = ordered[0], ordered[1]
    self_seg = pick(source_seg, target_seg)
    parts = jnp.arange(4)
    quarter_of = jnp.repeat(2 * ((parts // 2) ^ core) + parts % 2, quarter)
    lanes = jnp.arange(LANES)[None, :]

    def key_extras(seg):
        differs = jnp.logical_and(lanes < SEG_LANES, seg[:, None] != lanes)
        later = jnp.logical_and(
            jnp.logical_and(lanes >= SEG_LANES, lanes < PART_LANE),
            quarter_of[:, None] > lanes - SEG_LANES,
        )
        part = jnp.logical_and(lanes >= PART_LANE, lanes < PART_LANE + 3)
        return jnp.where(differs | later | part, 1.0, 0.0).astype(jnp.bfloat16)

    def query_extras(seg, causal):
        seg, at = seg[: 2 * quarter], quarter_of[: 2 * quarter]
        same = seg[:, None] == lanes
        here = jnp.logical_and(at[:, None] + SEG_LANES == lanes, causal)
        return jnp.where(same | here, MASKED, 0.0).astype(jnp.bfloat16)

    at_row = jnp.arange(quarter)
    later_key = jnp.logical_and(at_row[None, :] > at_row[:, None], jnp.logical_not(on_encoder))
    tri = jnp.where(later_key, MASKED, 0.0).astype(jnp.float32)
    self_extras = (query_extras(self_seg, jnp.logical_not(on_encoder)), key_extras(self_seg), tri)
    cross_extras = (query_extras(target_seg, False), key_extras(source_seg), tri)

    start = rows_all.astype(jnp.float32)
    start = pick(layer_norm(start, gains[0], biases[0]), start)
    start_here = start[: 2 * quarter]
    start_low = low(start)
    self_gain, self_bias = pick(gains[1], gains[0]), pick(biases[1], biases[0])
    raw_cross_rows = []
    with jax.named_scope("cross_weights"):
        rows_cross = rows_gathered(after(packed, rows_ffn), count, raw=raw_cross_rows, layer=1)
    self_out, *kept_self = attend(
        flag, start_low[: 2 * quarter], start_low, w_self, self_extras, True
    )
    with jax.named_scope("ffn_weights"):
        own_ffn = plane_gathered(after(rows_ffn, own_self), until=(self_out, *raw_cross_rows))
        feed = [own_ffn, over(own_ffn, "section")]
    self_total = start_here + after(self_out, *raw_cross_rows)
    middle = layer_norm(self_total, self_gain, self_bias)
    middle_low = low(middle)

    enc_out, enc_active, enc_slope = ffn(enc_flag, middle_low, feed)
    enc_total = middle + enc_out
    encoded = low(layer_norm(enc_total, gains[2], biases[2]))
    def across(x, layer):
        return moved(x, Z, lambda place: {**place, "zl": 1 - place["zl"]} if layer_of(place) == layer else None)

    with jax.named_scope("memory"):
        memory_here = [across(encoded[:quarter], 0), across(encoded[quarter:], 0)]
        memory_peer = [over(part, "section", layer=1) for part in memory_here]
    with jax.named_scope("cross_weights"):
        own_cross = plane_gathered(after(rows_cross, feed[1]), until=tuple(memory_here), layer=1)
        w_cross = [own_cross, over(own_cross, "section", layer=1)]
    (
        decoded,
        crossed_low,
        d_dec_low,
        d_middle_dec,
        d_memory_here,
        d_memory_other,
        dec_sums,
        dec_active,
        dec_inner,
        cross_keep,
        cross_send,
    ) = decoder(
        dec_flag, middle, memory_here + memory_peer, cot, cross_extras[:2], norms, w_cross, feed
    )
    with jax.named_scope("d_memory"):
        d_memory_here = d_memory_here + over(d_memory_other, "section", layer=1).astype(jnp.float32)
        d_memory_low = low(d_memory_here)
        arrived = across(d_memory_low, 1)
    with jax.named_scope("cross_sums"):
        cross_sum = from_cores(after(cross_keep, arrived), after(cross_send, arrived), layer=1)
        raw_cross = []
        cross_plane = plane_summed(cross_sum, raw=raw_cross, layer=1)

    d_enc_total, dz_low, enc_sums, second_keep, second_send = enc_out_back(
        flag, arrived, cot, enc_total, norms, d_dec_low, enc_active, dec_active, feed
    )
    with jax.named_scope("ffn_sums"):
        raw_second_sum = []
        second_sum = from_cores(second_keep, second_send, raw=raw_second_sum)
    gain_row = jnp.broadcast_to(self_gain, (8, self_gain.shape[0]))
    d_self_total, d_self_low, self_norm, first_keep, first_send = enc_in_back(
        flag,
        after(dz_low, second_keep, cross_sum),
        d_enc_total,
        d_middle_dec,
        self_total,
        gain_row,
        middle_low,
        crossed_low,
        feed,
        enc_slope,
        dec_inner,
    )
    with jax.named_scope("ffn_sums"):
        gate = []
        second_plane = plane_summed(after(second_sum, d_self_low), raw=gate)
        first_sum = from_cores(after(first_keep, *raw_cross), after(first_send, *raw_cross), raw=gate)

    halves = []
    for first, earlier in ((0, ()), (2, gate)):
        halves.append(
            attend_back(
                flag,
                after(d_self_low, *earlier),
                start_low[: 2 * quarter],
                start_low,
                w_self,
                kept_self,
                self_extras,
                True,
                first,
                2,
            )
        )
    d_start_q = halves[0][0] + halves[1][0]
    with jax.named_scope("cross_sums"):
        share_cross = rows_summed(after(cross_plane, d_start_q), count, layer=1)
    with jax.named_scope("ffn_sums"):
        gate_later = []
        first_plane = plane_summed(after(first_sum, second_plane), raw=gate_later)
        second_share = rows_summed(second_plane, count, raw=gate_later)
    with jax.named_scope("self_sums"):
        (_, _, keep, send), (_, _, *later) = halves
        self_sum = [from_cores(after(keep, *gate), after(send, *gate), raw=gate_later)]
        raw_later = []
        self_sum.append(from_cores(*(after(part, *gate_later) for part in later), raw=raw_later))
        self_sum = jnp.concatenate(self_sum, axis=0)
    with jax.named_scope("d_start"):
        d_start_kv = after(halves[0][1], *raw_later) + halves[1][1]
        d_start = d_self_total + d_start_q + d_start_kv[: 2 * quarter]
        d_start = d_start + over(low(d_start_kv[2 * quarter :]), "section").astype(jnp.float32)
    d_source, gain_a, bias_a = norm_back(
        rows_here.astype(jnp.float32), gains[0], biases[0], d_start
    )

    rows_from = jnp.concatenate([enc_sums, self_norm, dec_sums, jnp.stack([gain_a, bias_a])], axis=0)
    enc_rows, dec_rows = jnp.array([24, 8, 0, 25, 9, 1]), jnp.array([8, 18, 16, 9, 19, 17])
    wanted = pick(enc_rows, dec_rows)[:, None] == jnp.arange(26)
    norm_sums = jnp.sum(jnp.where(wanted[:, :, None], rows_from[None], 0.0), axis=1)
    shards = 2**count
    sides = jnp.arange(2)
    held, outer = core ^ sides[:, None], sides[None, :]
    row_block = ((2 * outer + (1 ^ outer ^ held)) * shards)[:, :, None] + jnp.arange(shards)
    column_block = (2 * (y_at ^ sides)[:, None] + (x_at ^ sides)[None, :]).reshape(-1)
    order = (row_block.reshape(2, -1)[:, None, :] + 0) * 4 + column_block[:, None]
    norm_sums = jnp.take(norm_sums.reshape(6, 8 * 2 * shards, -1), order.reshape(-1), axis=1)
    norm_sums = norm_sums.reshape(6, 2, 4, 2 * shards, -1)
    with jax.named_scope("norm_sums"):
        norm_got = over(norm_sums[:, 1], "section")
        norm_sums = norm_sums[:, 0] + norm_got
    with jax.named_scope("self_sums"):
        self_plane = plane_summed(self_sum, until=(norm_got,))
    with jax.named_scope("norm_sums"):
        norm_blocks = after(norm_sums.transpose(1, 2, 0, 3).reshape(4, 2 * shards, -1), self_plane)
        norm_plane = norm_blocks[0] + over(norm_blocks[1], "tx") + over(norm_blocks[2], "ty")
        norm_plane = norm_plane + over(norm_blocks[3], "ty", "tx")
    norm_width = norm_plane.shape[1]
    with jax.named_scope("self_sums"):
        pad = ((0, 0), (0, 15), (0, self_plane.shape[1] - norm_width))
        both = jnp.concatenate(
            [
                self_plane.reshape(2 * shards, -1, self_plane.shape[1]),
                jnp.pad(low(norm_plane)[:, None], pad),
            ],
            axis=1,
        )
        raw_self = []
        share_self = rows_summed(both.reshape(-1, self_plane.shape[1]), count, raw=raw_self)
        share_self = swapped(share_self).astype(jnp.float32)
    norm_shares = share_self[-16, :norm_width].reshape(6, -1)
    share_self = share_self[:-16]
    with jax.named_scope("ffn_sums"):
        first_share = rows_summed(after(first_plane, *raw_later), count)
        share_ffn = swapped(jnp.concatenate([first_share, second_share], axis=1)).astype(jnp.float32)
    share_first, share_second = share_ffn[:, :units], share_ffn[:, units:].T
    with jax.named_scope("outputs"):
        outputs = jnp.concatenate([pick(encoded, decoded), low(pick(d_source, d_start))], axis=1)
        outputs = rows_out(after(outputs, *raw_self))
    hidden_out = outputs[..., : hidden.shape[-1]]
    hidden_grad = outputs[..., hidden.shape[-1] :].astype(jnp.float32)
    g_query, g_key, g_value, g_out = unpack_heads(share_self)
    grad_qkv = jnp.stack([g_query, g_key, g_value], axis=1)
    c_query, c_key, c_value, c_out = unpack_heads(share_cross)
    with jax.named_scope("cross_out"):
        for_enc = cross_out(jnp.concatenate([c_key, c_value], axis=1), 0)
        for_dec = cross_out(jnp.concatenate([c_query, c_out], axis=1), 1)
    cross = jnp.where(core == 0, for_enc, for_dec).astype(jnp.float32)

    return (
        hidden_out,
        hidden_grad,
        grad_qkv[None],
        g_out[None],
        cross[None, :, :width],
        cross[None, :, width:],
        share_first[None],
        share_second[None],
        norm_shares[None, :3],
        norm_shares[None, 3:],
    )


def solution(mesh):
    _, dp_count, _ = mesh.devices.shape
    count = dp_count.bit_length() - 3
    names = axes_of(count)
    dp, tensor = names[1:-2], names[-2:]
    split = Mesh(mesh.devices.reshape((2,) * len(names)), names)
    rows = P("section", None, dp, tensor, None)
    in_specs = (
        rows,
        rows,
        P(None, None, dp, None),
        P("section", dp, None, tensor),
        P("section", dp, tensor),
        P("section", dp, tensor),
        P("section", dp, tensor),
        P("section", dp, tensor),
        P("section", tensor, dp),
        P("section", None, None),
        P("section", None, None),
    )
    out_specs = (
        rows,
        rows,
        P("section", dp, None, tensor),
        P("section", dp, tensor),
        P("section", dp, tensor),
        P("section", dp, tensor),
        P("section", dp, tensor),
        P("section", tensor, dp),
        P("section", None, dp + tensor),
        P("section", None, dp + tensor),
    )
    return jax.shard_map(
        functools.partial(body, count), mesh=split, in_specs=in_specs, out_specs=out_specs, check_vma=False
    )
```

```python
import functools

import jax
import jax.numpy as jnp
from jax import lax
from jax.experimental import pallas as pl
from jax.experimental.pallas import tpu as pltpu
from jax.sharding import Mesh
from jax.sharding import PartitionSpec as P

HDIM = 64
LANES = 128
MASKED = -1e30
NORM_EPS = 1e-05
VMEM_BYTES = 56 * 1024 * 1024

SEG_LANES = 8
PART_LANE = 12

PARTS = 2
TILE_ROWS = 256
HEADS = ((0, 1, 2, 0, 0), (0, 1, 2, 1, 1), (1, 3, 0, 0, 1))


def mul(a, b):
    return jnp.dot(a, b, preferred_element_type=jnp.float32)


def mul_nt(a, b):
    return lax.dot_general(a, b, (((1,), (1,)), ((), ())), preferred_element_type=jnp.float32)


def mul_tn(a, b):
    return lax.dot_general(a, b, (((0,), (0,)), ((), ())), preferred_element_type=jnp.float32)


def tile_of(values, index):
    return values[:, index * LANES : (index + 1) * LANES]


def lane_ids(rows):
    return lax.broadcasted_iota(jnp.int32, (rows, LANES), 1)


def half_mask(rows, half):
    lanes = lane_ids(rows)
    return lanes >= HDIM if half else lanes < HDIM


def in_parts(base, column):
    lanes = lane_ids(base.shape[0])
    high = column.astype(jnp.bfloat16).astype(jnp.float32)
    rest = column - high
    middle = rest.astype(jnp.bfloat16).astype(jnp.float32)
    low = rest - middle
    parts = jnp.where(
        lanes == PART_LANE,
        high,
        jnp.where(lanes == PART_LANE + 1, middle, jnp.where(lanes == PART_LANE + 2, low, base)),
    )
    return parts.astype(jnp.bfloat16)


def with_triangle(scores, tri, at):
    size = tri.shape[1]
    pieces = []
    if at > 0:
        pieces.append(scores[:, : at * size])
    pieces.append(scores[:, at * size : (at + 1) * size] + tri)
    pieces.append(scores[:, (at + 1) * size :])
    return jnp.concatenate(pieces, axis=1)


def places(core, block):
    return [pl.multiple_of((1 - core) * block, block), pl.multiple_of((2 + core) * block, block)]


def assemble(flag_ref, own_refs, peer_refs, w_ref):
    core, block = flag_ref[0], own_refs[0].shape[1] // 2
    for holder, refs in ((core, own_refs), (1 - core, peer_refs)):
        for part, ref in enumerate(refs):
            width = ref.shape[2]
            for at, place in enumerate(places(holder, block)):
                w_ref[pl.ds(place, block), part * width : (part + 1) * width] = ref[0, at * block : (at + 1) * block]


def hand_out(flag_ref, g_ref, keep_ref, send_ref):
    core, block = flag_ref[0], keep_ref.shape[1] // 2
    for holder, ref in ((core, keep_ref), (1 - core, send_ref)):
        for at, place in enumerate(places(holder, block)):
            ref[0, at * block : (at + 1) * block] = g_ref[pl.ds(place, block), :]


def where_active(kernel):
    def guarded(flag_ref, *refs):
        @pl.when(flag_ref[1] == 1)
        def _():
            kernel(flag_ref, *refs)

    return guarded


def scaled_queries(q_ref, at, q_tile, q_half):
    queries = q_ref[0, at, q_tile * LANES : (q_tile + 1) * LANES] * 0.125
    return jnp.where(half_mask(queries.shape[0], q_half), queries, 0).astype(jnp.bfloat16)


def units_of(total, rows):
    return [
        (slice(part * rows, (part + 1) * rows), part, head)
        for part in range(total // rows)
        for head in range(len(HEADS))
    ]


def attend_block(causal, xq_ref, xkv_ref, w_ref, qx_ref, kx_ref, tri_ref, q_ref, kv_ref, c_ref, l_ref):
    q_ref[0] = mul(xq_ref[...], w_ref[:, : 2 * LANES]).astype(jnp.bfloat16)
    kv_ref[0] = mul(xkv_ref[...], w_ref[:, LANES : 5 * LANES]).astype(jnp.bfloat16)
    rows = TILE_ROWS
    low = half_mask(rows, 0)

    def scores_of(at, part, head):
        q_tile, k_tile, _, q_half, _ = HEADS[head]
        keys = kv_ref[0, :, k_tile * LANES : (k_tile + 1) * LANES]
        scores = mul_nt(
            jnp.concatenate([scaled_queries(q_ref, at, q_tile, q_half), qx_ref[at, :]], axis=1),
            jnp.concatenate([keys, kx_ref[...]], axis=1),
        )
        return with_triangle(scores, tri_ref[...], part) if causal else scores

    units = units_of(q_ref.shape[1], rows)
    ahead = scores_of(*units[0])
    contexts, totals = [], None
    for index, (at, part, head) in enumerate(units):
        scores = ahead
        if index + 1 < len(units):
            ahead = scores_of(*units[index + 1])
        v_tile = HEADS[head][2]
        values = kv_ref[0, :, v_tile * LANES : (v_tile + 1) * LANES]
        highest = jnp.max(scores, axis=1, keepdims=True)
        weights = jnp.exp(scores - highest)
        sums = jnp.sum(weights, axis=1, keepdims=True)
        contexts.append(mul(weights.astype(jnp.bfloat16), values) / sums)
        logs = jnp.broadcast_to(highest + jnp.log(sums), (rows, LANES))
        totals = logs if head == 0 else jnp.where(lane_ids(rows) == head, logs, totals)
        if head == len(HEADS) - 1:
            c_ref[0, at, :LANES] = jnp.where(low, 0, contexts[2]).astype(jnp.bfloat16)
            c_ref[0, at, LANES:] = jnp.where(low, contexts[0], contexts[1]).astype(jnp.bfloat16)
            l_ref[0, at, :] = totals
            contexts = []
    return mul_nt(c_ref[0], w_ref[:, 4 * LANES :])


def attend_kernel(causal, flag_ref, xq_ref, xkv_ref, own_ref, peer_ref, qx_ref, kx_ref, tri_ref, o_ref, *refs):
    q_ref, kv_ref, c_ref, l_ref, w_ref = refs
    assemble(flag_ref, [own_ref], [peer_ref], w_ref)
    out = attend_block(causal, xq_ref, xkv_ref, w_ref, qx_ref, kx_ref, tri_ref, q_ref, kv_ref, c_ref, l_ref)
    add_up(pl.program_id(0) == 0, o_ref, out)


def add_up(first, ref, value):
    @pl.when(first)
    def _():
        ref[...] = value

    @pl.when(jnp.logical_not(first))
    def _():
        ref[...] += value


def attend_back_block(causal, do_ref, xq_ref, xkv_ref, w_ref, qx_ref, kx_ref, tri_ref, kept, work):
    q_ref, kv_ref, c_ref, l_ref = kept
    sum_ref, dq_ref, dkv_ref, g_ref = work
    rows = TILE_ROWS
    d_context = mul(do_ref[...], w_ref[:, 4 * LANES :]).astype(jnp.bfloat16)
    low = half_mask(rows, 0)

    def products_of(at, part, head):
        q_tile, k_tile, v_tile, q_half, v_half = HEADS[head]
        c_tile = 0 if head == 2 else 1
        keys = kv_ref[0, :, k_tile * LANES : (k_tile + 1) * LANES]
        values = kv_ref[0, :, v_tile * LANES : (v_tile + 1) * LANES]
        queries = scaled_queries(q_ref, at, q_tile, q_half)
        d_rows = jnp.where(half_mask(rows, v_half), tile_of(d_context[at], c_tile), 0).astype(jnp.bfloat16)
        total = l_ref[0, at, head : head + 1]
        scores = mul_nt(
            jnp.concatenate([queries, in_parts(qx_ref[at, :].astype(jnp.float32), -total)], axis=1),
            jnp.concatenate([keys, kx_ref[...]], axis=1),
        )
        if causal:
            scores = with_triangle(scores, tri_ref[...], part)
        return scores, mul_nt(d_rows, values), queries, d_rows, keys

    units = units_of(q_ref.shape[1], rows)
    ahead = products_of(*units[0])
    d_queries = []
    for index, (at, part, head) in enumerate(units):
        scores, d_probs, queries, d_rows, keys = ahead
        if index + 1 < len(units):
            ahead = products_of(*units[index + 1])
        _, k_tile, v_tile, _, _ = HEADS[head]
        probs = jnp.exp(scores)
        inner = jnp.sum(probs * d_probs, axis=1, keepdims=True)
        d_scores = (probs * (d_probs - inner)).astype(jnp.bfloat16)
        d_values = mul_tn(probs.astype(jnp.bfloat16), d_rows)
        d_keys = mul_tn(d_scores, queries)
        d_queries.append(mul(d_scores, keys) * 0.125)
        k_at = slice(k_tile * LANES, (k_tile + 1) * LANES)
        v_at = slice(v_tile * LANES, (v_tile + 1) * LANES)
        if part == 0 and head != 1:
            sum_ref[:, k_at] = d_keys
            sum_ref[:, v_at] = d_values
        else:
            sum_ref[:, k_at] += d_keys
            sum_ref[:, v_at] += d_values
        if head == len(HEADS) - 1:
            dq_ref[at, :LANES] = jnp.where(low, d_queries[0], d_queries[1]).astype(jnp.bfloat16)
            dq_ref[at, LANES:] = jnp.where(low, d_queries[2], 0).astype(jnp.bfloat16)
            d_queries = []
    dkv_ref[...] = sum_ref[...].astype(jnp.bfloat16)
    d_xq = mul_nt(dq_ref[...], w_ref[:, : 2 * LANES])
    d_xkv = mul_nt(dkv_ref[...], w_ref[:, LANES : 5 * LANES])

    grad_q = mul_tn(xq_ref[...], dq_ref[...])
    grad_kv = mul_tn(xkv_ref[...], dkv_ref[...])
    grad_o = mul_tn(do_ref[...], c_ref[0])
    g_ref[:, :LANES] = grad_q[:, :LANES].astype(jnp.bfloat16)
    g_ref[:, LANES : 2 * LANES] = (grad_q[:, LANES:] + grad_kv[:, :LANES]).astype(jnp.bfloat16)
    g_ref[:, 2 * LANES : 4 * LANES] = grad_kv[:, LANES : 3 * LANES].astype(jnp.bfloat16)
    g_ref[:, 4 * LANES : 5 * LANES] = (grad_kv[:, 3 * LANES :] + grad_o[:, :LANES]).astype(jnp.bfloat16)
    g_ref[:, 5 * LANES :] = grad_o[:, LANES:].astype(jnp.bfloat16)
    return d_xq, d_xkv


def attend_back_kernel(causal, flag_ref, do_ref, xq_ref, xkv_ref, own_ref, peer_ref, *refs):
    kept, (qx_ref, kx_ref, tri_ref, dxq_ref, dxkv_ref, keep_ref, send_ref, w_ref) = refs[:4], refs[4:12]
    work = refs[12:]
    assemble(flag_ref, [own_ref], [peer_ref], w_ref)
    d_xq, d_xkv = attend_back_block(
        causal, do_ref, xq_ref, xkv_ref, w_ref, qx_ref, kx_ref, tri_ref, kept, work
    )
    add_up(pl.program_id(0) == 0, dxq_ref, d_xq)
    add_up(pl.program_id(0) == 0, dxkv_ref, d_xkv)
    hand_out(flag_ref, work[3], keep_ref, send_ref)


def whole(shape):
    return pl.BlockSpec(shape, lambda j, flag: (0,) * len(shape))


def held(shape):
    return pl.BlockSpec(shape, lambda j, flag: (0,) * len(shape), pipeline_mode=pl.Buffered(1))


def per_block(shape, first=0, gate=1):
    return pl.BlockSpec((1,) + shape, lambda j, flag: (first + j * flag[gate],) + (0,) * len(shape))


shape = jax.ShapeDtypeStruct


def call(kernel, name, micros, moved, grid, in_specs, out_specs, out_shape, scratch, *operands):
    return pl.pallas_call(
        where_active(kernel),
        grid_spec=pltpu.PrefetchScalarGridSpec(
            num_scalar_prefetch=1,
            grid=(grid,),
            in_specs=in_specs,
            out_specs=out_specs,
            scratch_shapes=scratch,
        ),
        out_shape=out_shape,
        compiler_params=pltpu.CompilerParams(vmem_limit_bytes=VMEM_BYTES),
        cost_estimate=cost(micros, moved),
        name=name,
    )(*operands)


def cost(micros, moved):
    return pl.CostEstimate(flops=int(micros * 1.15e9), bytes_accessed=int(moved), transcendentals=0)


def attend(flag, xq, xkv, weights, extras, causal):
    rows, width = xq.shape
    keys = xkv.shape[0]
    blocks = weights[0].shape[0]
    return call(
        functools.partial(attend_kernel, causal),
        "attend_self" if causal else "attend_cross",
        20,
        24 * 2**20,
        blocks,
        [held((rows, width)), held((keys, width))]
        + [per_block(part.shape[1:]) for part in weights]
        + [held(extra.shape) for extra in extras],
        [
            whole((rows, width)),
            per_block((rows, 2 * LANES)),
            per_block((keys, 4 * LANES)),
            per_block((rows, 2 * LANES)),
            per_block((rows, LANES)),
        ],
        [
            shape((rows, width), jnp.float32),
            shape((blocks, rows, 2 * LANES), jnp.bfloat16),
            shape((blocks, keys, 4 * LANES), jnp.bfloat16),
            shape((blocks, rows, 2 * LANES), jnp.bfloat16),
            shape((blocks, rows, LANES), jnp.float32),
        ],
        [pltpu.VMEM((width, 6 * LANES), jnp.bfloat16)],
        flag,
        xq,
        xkv,
        *weights,
        *extras,
    )


def attend_back(flag, d_out, xq, xkv, weights, kept, extras, causal, first, count):
    rows, width = xq.shape
    keys = xkv.shape[0]
    return call(
        functools.partial(attend_back_kernel, causal),
        "attend_self_back" if causal else "attend_cross_back",
        10 * count,
        6 * 2**20 * count,
        count,
        [held((rows, width)), held((rows, width)), held((keys, width))]
        + [per_block(part.shape[1:], first) for part in weights]
        + [
            per_block((rows, 2 * LANES), first),
            per_block((keys, 4 * LANES), first),
            per_block((rows, 2 * LANES), first),
            per_block((rows, LANES), first),
        ]
        + [held(extra.shape) for extra in extras],
        [whole((rows, width)), whole((keys, width))] + [per_block(part.shape[1:]) for part in weights],
        [shape((rows, width), jnp.float32), shape((keys, width), jnp.float32)]
        + [shape((count,) + part.shape[1:], jnp.bfloat16) for part in weights],
        [
            pltpu.VMEM((width, 6 * LANES), jnp.bfloat16),
            pltpu.VMEM((keys, 4 * LANES), jnp.float32),
            pltpu.VMEM((rows, 2 * LANES), jnp.bfloat16),
            pltpu.VMEM((keys, 4 * LANES), jnp.bfloat16),
            pltpu.VMEM((width, 6 * LANES), jnp.bfloat16),
        ],
        flag,
        d_out,
        xq,
        xkv,
        *weights,
        *kept,
        *extras,
    )


def ffn_block(x_ref, w_ref, units, g_ref, slope_ref, first, out_ref):
    inner = mul(x_ref[...], w_ref[:, :units])
    spread = 0.5 * (1.0 + lax.erf(inner * (0.5**0.5)))
    bell = jnp.exp(-0.5 * inner * inner) * 0.3989422804014327
    active = (inner * spread).astype(jnp.bfloat16)
    g_ref[0] = active
    slope_ref[0] = (spread + inner * bell).astype(jnp.bfloat16)
    add_up(first, out_ref, mul_nt(active, w_ref[:, units:]))


def ffn_kernel(flag_ref, x_ref, *refs):
    own_refs, peer_refs = refs[:PARTS], refs[PARTS : 2 * PARTS]
    z_ref, g_ref, slope_ref, w_ref = refs[2 * PARTS :]
    assemble(flag_ref, own_refs, peer_refs, w_ref)
    ffn_block(x_ref, w_ref, own_refs[0].shape[2], g_ref, slope_ref, pl.program_id(0) == 0, z_ref)


def feed_blocks(feed, index):
    half, units = feed[0].shape[1], feed[0].shape[2] // 2
    return [
        pl.BlockSpec((1, half, units), lambda j, flag, side=side: (index(j, flag), 0, side))
        for _ in feed
        for side in (0, 1)
    ]


def feed_operands(feed):
    return [part for part in feed for _ in (0, 1)]


def ffn(flag, x, feed):
    rows, width = x.shape
    blocks, units = feed[0].shape[0], feed[0].shape[2] // 2
    return call(
        ffn_kernel,
        "ffn",
        12,
        rows * units * blocks * 16,
        blocks,
        [held((rows, width))] + feed_blocks(feed, lambda j, flag: j * flag[1]),
        [whole((rows, width)), per_block((rows, units)), per_block((rows, units))],
        [
            shape((rows, width), jnp.float32),
            shape((blocks, rows, units), jnp.bfloat16),
            shape((blocks, rows, units), jnp.bfloat16),
        ],
        [pltpu.VMEM((width, 2 * units), jnp.bfloat16)],
        flag,
        x,
        *feed_operands(feed),
    )


def ffn_back_block(dz_ref, w_ref, units, slope_ref, dh_ref, first, out_ref):
    d_active = mul(dz_ref[...], w_ref[:, units:])
    d_inner = (d_active * slope_ref[0].astype(jnp.float32)).astype(jnp.bfloat16)
    dh_ref[0] = d_inner
    add_up(first, out_ref, mul_nt(d_inner, w_ref[:, :units]))


def layer_norm(values, gain_row, bias_row):
    average = jnp.mean(values, axis=-1, keepdims=True)
    centered = values - average
    variance = jnp.mean(centered * centered, axis=-1, keepdims=True)
    return centered * lax.rsqrt(variance + NORM_EPS) * gain_row + bias_row


def norm_back(values, gain_row, bias_row, upstream):
    _, pullback = jax.vjp(layer_norm, values, gain_row, bias_row)
    return pullback(upstream)


def norm_parts(values):
    average = jnp.mean(values, axis=1, keepdims=True)
    centered = values - average
    scale = lax.rsqrt(jnp.mean(centered * centered, axis=1, keepdims=True) + NORM_EPS)
    return centered * scale, scale


def norm_gradients(values, gain_row, upstream):
    shaped, scale = norm_parts(values)
    inner = upstream * gain_row
    mean_inner = jnp.mean(inner, axis=1, keepdims=True)
    mean_product = jnp.mean(inner * shaped, axis=1, keepdims=True)
    d_values = scale * (inner - mean_inner - shaped * mean_product)
    d_gain = jnp.sum(upstream * shaped, axis=0, keepdims=True)
    return d_values, d_gain, jnp.sum(upstream, axis=0, keepdims=True)


def enc_out_back_kernel(
    flag_ref, arrived_ref, cot_ref, total_ref, norms_ref, d_dec_ref, enc_ref, dec_ref, *refs
):
    d_total_ref, dz_ref, sums_ref, keep_ref, send_ref, g_ref, left_t_ref = refs

    @pl.when(jnp.logical_and(pl.program_id(0) == 0, flag_ref[2] == 1))
    def _():
        upstream = arrived_ref[...].astype(jnp.float32) + cot_ref[...].astype(jnp.float32)
        d_total, sums_ref[0:1, :], sums_ref[1:2, :] = norm_gradients(total_ref[...], norms_ref[2:3, :], upstream)
        d_total_ref[...] = d_total
        dz_ref[...] = d_total.astype(jnp.bfloat16)

    @pl.when(jnp.logical_and(pl.program_id(0) == 0, flag_ref[2] == 0))
    def _():
        dz_ref[...] = d_dec_ref[...]

    @pl.when(pl.program_id(0) == 0)
    def _():
        left_t_ref[...] = dz_ref[...].T

    right = jnp.where(flag_ref[2] == 1, enc_ref[0], dec_ref[0])
    g_ref[...] = mul(left_t_ref[...], right).astype(jnp.bfloat16)
    hand_out(flag_ref, g_ref, keep_ref, send_ref)


def enc_out_back(flag, arrived, cot, total, norms, d_dec, enc_active, dec_active, feed):
    rows, width = cot.shape
    blocks, _, units = enc_active.shape
    like = shape((blocks, feed[0].shape[1], units), jnp.bfloat16)
    full = shape((rows, width), jnp.float32)
    return call(
        enc_out_back_kernel,
        "enc_out_back",
        9,
        rows * units * blocks * 8,
        blocks,
        [held(item.shape) for item in (arrived, cot, total, norms, d_dec)]
        + [per_block((rows, units), 0, 2), per_block((rows, units), 0, 3)],
        [whole((rows, width))] * 2 + [whole((8, width))] + [per_block(like.shape[1:])] * 2,
        [full, shape((rows, width), jnp.bfloat16), shape((8, width), jnp.float32)]
        + [like] * 2,
        [pltpu.VMEM((width, units), jnp.bfloat16), pltpu.VMEM((width, rows), jnp.bfloat16)],
        flag,
        arrived,
        cot,
        total,
        norms,
        d_dec,
        enc_active,
        dec_active,
    )


def enc_in_back_kernel(
    flag_ref, dz_ref, d_enc_ref, d_middle_ref, total_ref, gain_ref, middle_ref, crossed_ref, *refs
):
    first_own_ref, second_own_ref, first_peer_ref, second_peer_ref, slope_ref, dec_inner_ref, *refs = refs
    d_total_ref, d_low_ref, sums_ref, keep_ref, send_ref, w_ref, inner_ref, out_ref, g_ref, left_t_ref = refs
    step = pl.program_id(0)
    phase, at = step // 4, step % 4
    on_encoder = flag_ref[2] == 1

    @pl.when(jnp.logical_and(phase == 0, on_encoder))
    def _():
        assemble(flag_ref, [first_own_ref, second_own_ref], [first_peer_ref, second_peer_ref], w_ref)
        ffn_back_block(
            dz_ref, w_ref, first_own_ref.shape[2], slope_ref, inner_ref.at[pl.ds(at, 1)], at == 0, out_ref
        )

    @pl.when(step == 3)
    def _():
        upstream = jnp.where(on_encoder, d_enc_ref[...] + out_ref[...], d_middle_ref[...])
        d_total, sums_ref[0:1, :], sums_ref[1:2, :] = norm_gradients(total_ref[...], gain_ref[0:1, :], upstream)
        d_total_ref[...] = d_total
        d_low_ref[...] = d_total.astype(jnp.bfloat16)
        left_t_ref[...] = jnp.where(on_encoder, middle_ref[...], crossed_ref[...]).T

    @pl.when(phase == 1)
    def _():
        right = jnp.where(on_encoder, inner_ref[at], dec_inner_ref[0])
        g_ref[...] = mul(left_t_ref[...], right).astype(jnp.bfloat16)
        hand_out(flag_ref, g_ref, keep_ref, send_ref)


def enc_in_back(flag, dz, d_enc, d_middle, total, gain, middle, crossed, feed, slope, dec_inner):
    rows, width = dz.shape
    blocks, half, units = feed[0].shape[0], feed[0].shape[1], feed[0].shape[2] // 2
    full = shape((rows, width), jnp.float32)

    def at_step(of, low, high, gate):
        def index(j, flag):
            return (jnp.where(j < 4, j if low == "up" else low, j - 4 if high == "up" else high) * flag[gate],) + (
                0,
            ) * len(of)

        return pl.BlockSpec((1,) + of, index)

    return call(
        enc_in_back_kernel,
        "enc_in_back",
        19,
        rows * units * blocks * 20,
        8,
        [held(item.shape) for item in (dz, d_enc, d_middle, total, gain, middle, crossed)]
        + feed_blocks(feed, lambda j, flag: jnp.where(j < 4, j, 3) * flag[2])
        + [at_step((rows, units), "up", 3, 2), at_step((rows, units), 0, "up", 3)],
        [whole((rows, width))] * 2 + [whole((8, width))] + [at_step((half, units), 0, "up", 1)] * 2,
        [full, shape((rows, width), jnp.bfloat16), shape((8, width), jnp.float32)]
        + [shape((blocks, half, units), jnp.bfloat16)] * 2,
        [
            pltpu.VMEM((width, 2 * units), jnp.bfloat16),
            pltpu.VMEM((blocks, rows, units), jnp.bfloat16),
            pltpu.VMEM((rows, width), jnp.float32),
            pltpu.VMEM((width, units), jnp.bfloat16),
            pltpu.VMEM((width, rows), jnp.bfloat16),
        ],
        flag,
        dz,
        d_enc,
        d_middle,
        total,
        gain,
        middle,
        crossed,
        *feed_operands(feed),
        slope,
        dec_inner,
    )


def decoder_kernel(
    flag_ref,
    h1_ref,
    mem_a_ref,
    mem_b_ref,
    peer_a_ref,
    peer_b_ref,
    cot_ref,
    qx_ref,
    kx_ref,
    norms_ref,
    own_ref,
    peer_ref,
    first_own_ref,
    second_own_ref,
    first_peer_ref,
    second_peer_ref,
    decoded_ref,
    crossed_ref,
    d_dec_ref,
    d_middle_ref,
    mine_ref,
    other_ref,
    sums_ref,
    active_ref,
    inner_ref,
    keep_ref,
    send_ref,
    xq_ref,
    xkv_ref,
    wx_ref,
    wf_ref,
    q_ref,
    kv_ref,
    c_ref,
    l_ref,
    slope_ref,
    out_ref,
    total_ref,
    do_ref,
    dxkv_ref,
    *work,
):
    step = pl.program_id(0)
    phase, at = step // 4, step % 4
    first, last = at == 0, at == 3
    rows = h1_ref.shape[0]
    units = first_own_ref.shape[2]
    gain = [norms_ref[row : row + 1, :] for row in range(3)]
    bias = [norms_ref[3 + row : 4 + row, :] for row in range(3)]

    def kept(block):
        return tuple(ref.at[pl.ds(block, 1)] for ref in (q_ref, kv_ref, c_ref, l_ref))

    @pl.when(step == 0)
    def _():
        xq_ref[...] = h1_ref[...].astype(jnp.bfloat16)
        for part, ref in enumerate((mem_a_ref, mem_b_ref, peer_a_ref, peer_b_ref)):
            xkv_ref[part * rows // 2 : (part + 1) * rows // 2] = ref[...]

    @pl.when(jnp.logical_or(phase == 0, phase == 3))
    def _():
        assemble(flag_ref, [own_ref], [peer_ref], wx_ref)

    @pl.when(jnp.logical_or(phase == 1, phase == 2))
    def _():
        assemble(flag_ref, [first_own_ref, second_own_ref], [first_peer_ref, second_peer_ref], wf_ref)

    @pl.when(phase == 0)
    def _():
        add_up(first, out_ref, attend_block(False, xq_ref, xkv_ref, wx_ref, qx_ref, kx_ref, None, *kept(at)))

    @pl.when(jnp.logical_and(phase == 0, last))
    def _():
        total = h1_ref[...] + out_ref[...]
        total_ref[...] = total
        crossed = norm_parts(total)[0] * gain[1] + bias[1]
        mine_ref[...] = crossed
        crossed_ref[...] = crossed.astype(jnp.bfloat16)

    @pl.when(phase == 1)
    def _():
        ffn_block(crossed_ref, wf_ref, units, active_ref, slope_ref.at[pl.ds(at, 1)], first, out_ref)

    @pl.when(jnp.logical_and(phase == 1, last))
    def _():
        total = mine_ref[...] + out_ref[...]
        decoded_ref[...] = (norm_parts(total)[0] * gain[2] + bias[2]).astype(jnp.bfloat16)
        d_total, sums_ref[0:1, :], sums_ref[1:2, :] = norm_gradients(
            total, gain[2], cot_ref[...].astype(jnp.float32)
        )
        d_middle_ref[...] = d_total
        d_dec_ref[...] = d_total.astype(jnp.bfloat16)

    @pl.when(phase == 2)
    def _():
        ffn_back_block(d_dec_ref, wf_ref, units, slope_ref.at[pl.ds(3 - at, 1)], inner_ref, first, out_ref)

    @pl.when(jnp.logical_and(phase == 2, last))
    def _():
        d_total, sums_ref[2:3, :], sums_ref[3:4, :] = norm_gradients(
            total_ref[...], gain[1], d_middle_ref[...] + out_ref[...]
        )
        d_middle_ref[...] = d_total
        do_ref[...] = d_total.astype(jnp.bfloat16)

    @pl.when(phase == 3)
    def _():
        d_xq, d_xkv = attend_back_block(
            False, do_ref, xq_ref, xkv_ref, wx_ref, qx_ref, kx_ref, None, kept(3 - at), work
        )
        add_up(first, out_ref, d_xq)
        add_up(first, dxkv_ref, d_xkv)
        hand_out(flag_ref, work[3], keep_ref, send_ref)

    @pl.when(jnp.logical_and(phase == 3, last))
    def _():
        d_middle_ref[...] += out_ref[...]
        mine_ref[...] = dxkv_ref[:rows]
        other_ref[...] = dxkv_ref[rows:].astype(jnp.bfloat16)


def decoder(flag, h1, memory, cot, extras, norms, cross, feed):
    rows, width = h1.shape
    blocks, half, _ = cross[0].shape
    units = feed[0].shape[2] // 2
    keys = 2 * rows
    qx, kx = extras

    def at_step(of, in_phase):
        def index(j, flag):
            at = j % 4
            choice = [{"up": at, "down": 3 - at}.get(way, way) for way in in_phase]
            chosen = choice[3]
            for phase in (2, 1, 0):
                chosen = jnp.where(j // 4 == phase, choice[phase], chosen)
            return (chosen * flag[1],) + (0,) * len(of)

        return pl.BlockSpec((1,) + of, index)

    part = (half, cross[0].shape[2])
    full = shape((rows, width), jnp.float32)
    rounded = shape((rows, width), jnp.bfloat16)
    return call(
        decoder_kernel,
        "decoder",
        90,
        40 * 2**20,
        16,
        [held(item.shape) for item in (h1, *memory, cot, qx, kx, norms)]
        + [at_step(part, ("up", 3, 3, "down"))] * 2
        + feed_blocks(feed, lambda j, flag: at_step((half, units), (0, "up", "down", 0)).index_map(j, flag)[0]),
        [whole((rows, width))] * 6
        + [whole((8, width))]
        + [
            at_step((rows, units), (0, "up", 3, 3)),
            at_step((rows, units), (3, 3, "down", 0)),
            at_step(part, (3, 3, 3, "down")),
            at_step(part, (3, 3, 3, "down")),
        ],
        [rounded, rounded, rounded, full, full, rounded, shape((8, width), jnp.float32)]
        + [shape((blocks, rows, units), jnp.bfloat16)] * 2
        + [shape(cross[0].shape, jnp.bfloat16)] * 2,
        [
            pltpu.VMEM((rows, width), jnp.bfloat16),
            pltpu.VMEM((keys, width), jnp.bfloat16),
            pltpu.VMEM((width, 6 * LANES), jnp.bfloat16),
            pltpu.VMEM((width, 2 * units), jnp.bfloat16),
            pltpu.VMEM((blocks, rows, 2 * LANES), jnp.bfloat16),
            pltpu.VMEM((blocks, keys, 4 * LANES), jnp.bfloat16),
            pltpu.VMEM((blocks, rows, 2 * LANES), jnp.bfloat16),
            pltpu.VMEM((blocks, rows, LANES), jnp.float32),
            pltpu.VMEM((blocks, rows, units), jnp.bfloat16),
            pltpu.VMEM((rows, width), jnp.float32),
            pltpu.VMEM((rows, width), jnp.float32),
            pltpu.VMEM((rows, width), jnp.bfloat16),
            pltpu.VMEM((keys, width), jnp.float32),
            pltpu.VMEM((keys, 4 * LANES), jnp.float32),
            pltpu.VMEM((rows, 2 * LANES), jnp.bfloat16),
            pltpu.VMEM((keys, 4 * LANES), jnp.bfloat16),
            pltpu.VMEM((width, 6 * LANES), jnp.bfloat16),
        ],
        flag,
        h1,
        *memory,
        cot,
        qx,
        kx,
        norms,
        *cross,
        *feed_operands(feed),
    )


def low(values):
    return values.astype(jnp.bfloat16)


def axes_of(count):
    return ("section", "zh", "zl") + tuple("e%d" % at for at in range(count)) + ("ty", "tx")


def layer_of(place):
    return 1 ^ place["zh"] ^ place["zl"]


def moved(x, names, to):
    names = [name for name in axes_of(8) if name in names]

    def index(place):
        return sum(place[name] << (len(names) - 1 - at) for at, name in enumerate(names))

    pairs = []
    for source in range(2 ** len(names)):
        place = {name: source >> (len(names) - 1 - at) & 1 for at, name in enumerate(names)}
        target = to(place)
        if target is not None:
            pairs.append((source, index(target)))
    return lax.ppermute(x, tuple(names), pairs)


def over(x, *axes, layer=None):
    def to(place):
        if layer is not None and layer_of(place) != layer:
            return None
        return {**place, **{axis: 1 - place[axis] for axis in axes}}

    return moved(x, axes if layer is None else axes + Z, to)


Z = ("zh", "zl")


def swapped(x):
    def to(place):
        if place["section"] == layer_of(place):
            return place
        return {"section": 1 - place["section"], "zh": place["zh"], "zl": 1 - place["zl"]}

    return moved(x, ("section",) + Z, to)


def turned(x):
    return moved(x, ("section", "ty"), lambda place: {"section": place["ty"], "ty": place["section"]})


def sent_home(x, other):
    def to(place):
        return {
            "section": layer_of(place),
            "zh": place["zh"],
            "zl": 1 ^ place["zh"] ^ place["ty"],
            "ty": place["section"],
            "tx": place["tx"] ^ other,
        }

    return moved(x, ("section",) + Z + ("ty", "tx"), to)


def cross_in(x, layer):
    def to(place):
        if place["section"] != layer:
            return None
        return {"section": layer_of(place), "zh": place["zh"], "zl": place["zh"]}

    return moved(x, ("section",) + Z, to)


def cross_out(x, layer):
    def to(place):
        if layer_of(place) != 1:
            return None
        return {"section": layer, "zh": place["zh"], "zl": 1 ^ place["zh"] ^ place["section"]}

    return moved(x, ("section",) + Z, to)


def in_order(x, flag, axis):
    return jnp.where(flag == 1, jnp.flip(x, axis), x)


def pack_heads(query, key, value, out):
    pair = 2 * HDIM
    return jnp.concatenate(
        [
            query,
            value[:, pair:],
            key[:, :pair],
            value[:, :pair],
            key[:, pair:],
            out[:, pair:],
            out[:, :pair],
        ],
        axis=1,
    )


def unpack_heads(packed):
    part = [packed[:, at * HDIM : (at + 1) * HDIM] for at in range(12)]
    query = jnp.concatenate(part[0:3], axis=1)
    key = jnp.concatenate([part[4], part[5], part[8]], axis=1)
    value = jnp.concatenate([part[6], part[7], part[3]], axis=1)
    out = jnp.concatenate([part[10], part[11], part[9]], axis=1)
    return query, key, value, out


def after(x, *earlier):
    return lax.optimization_barrier((x,) + earlier)[0]


def plane_gathered(x, until=(), **only):
    parts = [x, over(x, "tx", **only), over(x, "ty", **only), over(x, "ty", "tx", **only)]
    return jnp.stack([after(part, *until) for part in parts])


def plane_summed(x, until=(), raw=None, **only):
    terms = [x[0], over(x[1], "tx", **only), over(x[2], "ty", **only), over(x[3], "ty", "tx", **only)]
    if raw is not None:
        raw.extend(terms[1:])
    terms = [after(term, *until) for term in terms]
    return low(sum(term.astype(jnp.float32) for term in terms))


def rows_gathered(x, count, until=(), raw=None, **only):
    for axes in [("e%d" % at,) for at in reversed(range(count))] + [Z]:
        got = over(x, *axes, **only)
        if raw is not None:
            raw.append(got)
        parts = [after(part, *until) for part in (x, got)]
        both = in_order(jnp.stack(parts, axis=-3), lax.axis_index(axes[0]), x.ndim - 2)
        x = both.reshape(x.shape[:-2] + (2 * x.shape[-2], x.shape[-1]))
    return x


def rows_summed(x, count, until=(), raw=None, **only):
    for axes in [Z] + [("e%d" % at,) for at in range(count)]:
        halves = x.reshape(x.shape[:-2] + (2, x.shape[-2] // 2, x.shape[-1]))
        halves = in_order(halves, lax.axis_index(axes[0]), x.ndim - 2)
        got = over(halves[..., 1, :, :], *axes, **only)
        if raw is not None:
            raw.append(got)
        x = plus(halves[..., 0, :, :], after(got, *until))
    return x


def plus(first, second):
    return low(first.astype(jnp.float32) + second.astype(jnp.float32))


def from_cores(keep, send, raw=None, **only):
    got = over(send, "section", **only)
    if raw is not None:
        raw.append(got)
    return plus(keep, got)


def body(
    count,
    hidden,
    cotangent,
    segments,
    sa_qkv,
    sa_out,
    cross_one,
    cross_two,
    ffn_in,
    ffn_out,
    norm_gain,
    norm_bias,
):
    core = lax.axis_index("section")
    x_at, y_at, zh_at, zl_at = (lax.axis_index(name) for name in ("tx", "ty", "zh", "zl"))
    layer = 1 ^ zh_at ^ zl_at
    on_encoder = layer == 0
    quarter = hidden.shape[3]
    enc_flag = jnp.stack([core, 1 - layer, 1 - layer, layer])
    dec_flag = jnp.stack([core, layer, 1 - layer, layer])
    flag = jnp.stack([core, jnp.ones_like(core), 1 - layer, layer])

    def pick(first, second):
        return jnp.where(on_encoder, first, second)

    def of_one_row(x):
        both = in_order(x[0, :, 0], x_at, 0)
        return in_order(jnp.stack([both[0], over(both[1], "tx")]), x_at, 0).reshape(2 * quarter, -1)

    def rows_out(x, raw=None):
        mine, other = in_order(x.reshape(2, quarter, -1), x_at, 0)
        both = [sent_home(mine, 0), sent_home(other, 1)]
        if raw is not None:
            raw.extend(both)
        return in_order(jnp.stack(both), x_at, 0)[None, :, None]

    units = ffn_in.shape[2]
    width = cross_one.shape[2]
    packed_self = pack_heads(sa_qkv[0, :, 0], sa_qkv[0, :, 1], sa_qkv[0, :, 2], sa_out[0])
    packed_ffn = jnp.concatenate([ffn_in[0], ffn_out[0].T], axis=1)
    with jax.named_scope("norms_in"):
        norms = swapped(jnp.concatenate([norm_gain[0], norm_bias[0]], axis=0))
        gains, biases = norms[:3], norms[3:]
        seg_own = segments[:, :, 0].astype(jnp.float32)
        seg_here = jnp.where(zl_at == 1 ^ zh_at ^ y_at, seg_own, over(seg_own, "zl")).astype(jnp.int32)
    with jax.named_scope("hidden_in"):
        one_row = of_one_row(jnp.concatenate([hidden, cotangent], axis=-1))
    with jax.named_scope("self_weights"):
        shard_self = swapped(packed_self)
    with jax.named_scope("hidden_in"):
        one_row = swapped(after(one_row, shard_self))
    with jax.named_scope("ffn_weights"):
        shard_ffn = swapped(after(packed_ffn, one_row))
    with jax.named_scope("cross_weights"):
        cross_low = after(jnp.concatenate([cross_one[0], cross_two[0]], axis=1), shard_ffn)
        pair_kv, pair_qo = cross_in(cross_low, 0), cross_in(cross_low, 1)

    def both_rows(x):
        for_enc = rows_gathered(x, count, layer=0)
        return pick(for_enc, rows_gathered(after(x, for_enc), count, layer=1))

    with jax.named_scope("self_weights"):
        rows_self = both_rows(shard_self)
        raw_ffn_rows = []
        rows_ffn_enc = rows_gathered(after(shard_ffn, rows_self), count, raw=raw_ffn_rows, layer=0)
        own_self = plane_gathered(rows_self, until=(*raw_ffn_rows, pair_kv, pair_qo))
        w_self = [own_self, over(own_self, "section")]
    with jax.named_scope("hidden_in"):
        rows_here = turned(one_row)
        rows_here, cot = rows_here[:, : hidden.shape[-1]], rows_here[:, hidden.shape[-1] :]
        rows_all = jnp.concatenate([rows_here, over(rows_here, "section")], axis=0)
    with jax.named_scope("cross_weights"):
        packed = pack_heads(pair_qo[:, :width], pair_kv[:, :width], pair_kv[:, width:], pair_qo[:, width:])
    with jax.named_scope("ffn_weights"):
        rows_ffn = pick(rows_ffn_enc, rows_gathered(after(shard_ffn, *raw_ffn_rows), count, layer=1))

    both_segments = in_order(seg_here, x_at, 1)[:, 0]
    ordered = in_order(both_segments.reshape(2, 2, 2 * quarter), core, 1).reshape(2, 4 * quarter)
    source_seg, target_seg = ordered[0], ordered[1]
    self_seg = pick(source_seg, target_seg)
    parts = jnp.arange(4)
    quarter_of = jnp.repeat(2 * ((parts // 2) ^ core) + parts % 2, quarter)
    lanes = jnp.arange(LANES)[None, :]

    def key_extras(seg):
        differs = jnp.logical_and(lanes < SEG_LANES, seg[:, None] != lanes)
        later = jnp.logical_and(
            jnp.logical_and(lanes >= SEG_LANES, lanes < PART_LANE),
            quarter_of[:, None] > lanes - SEG_LANES,
        )
        part = jnp.logical_and(lanes >= PART_LANE, lanes < PART_LANE + 3)
        return jnp.where(differs | later | part, 1.0, 0.0).astype(jnp.bfloat16)

    def query_extras(seg, causal):
        seg, at = seg[: 2 * quarter], quarter_of[: 2 * quarter]
        same = seg[:, None] == lanes
        here = jnp.logical_and(at[:, None] + SEG_LANES == lanes, causal)
        return jnp.where(same | here, MASKED, 0.0).astype(jnp.bfloat16)

    at_row = jnp.arange(quarter)
    later_key = jnp.logical_and(at_row[None, :] > at_row[:, None], jnp.logical_not(on_encoder))
    tri = jnp.where(later_key, MASKED, 0.0).astype(jnp.float32)
    self_extras = (query_extras(self_seg, jnp.logical_not(on_encoder)), key_extras(self_seg), tri)
    cross_extras = (query_extras(target_seg, False), key_extras(source_seg), tri)

    start = rows_all.astype(jnp.float32)
    start = pick(layer_norm(start, gains[0], biases[0]), start)
    start_here = start[: 2 * quarter]
    start_low = low(start)
    self_gain, self_bias = pick(gains[1], gains[0]), pick(biases[1], biases[0])
    raw_cross_rows = []
    with jax.named_scope("cross_weights"):
        rows_cross = rows_gathered(after(packed, rows_ffn), count, raw=raw_cross_rows, layer=1)
    self_out, *kept_self = attend(
        flag, start_low[: 2 * quarter], start_low, w_self, self_extras, True
    )
    with jax.named_scope("ffn_weights"):
        own_ffn = plane_gathered(after(rows_ffn, own_self), until=(self_out, *raw_cross_rows))
        feed = [own_ffn, over(own_ffn, "section")]
    self_total = start_here + after(self_out, *raw_cross_rows)
    middle = layer_norm(self_total, self_gain, self_bias)
    middle_low = low(middle)

    enc_out, enc_active, enc_slope = ffn(enc_flag, middle_low, feed)
    enc_total = middle + enc_out
    encoded = low(layer_norm(enc_total, gains[2], biases[2]))
    def across(x, layer):
        return moved(x, Z, lambda place: {**place, "zl": 1 - place["zl"]} if layer_of(place) == layer else None)

    with jax.named_scope("memory"):
        memory_here = [across(encoded[:quarter], 0), across(encoded[quarter:], 0)]
        memory_peer = [over(part, "section", layer=1) for part in memory_here]
    with jax.named_scope("cross_weights"):
        own_cross = plane_gathered(after(rows_cross, feed[1]), until=tuple(memory_here), layer=1)
        w_cross = [own_cross, over(own_cross, "section", layer=1)]
    (
        decoded,
        crossed_low,
        d_dec_low,
        d_middle_dec,
        d_memory_here,
        d_memory_other,
        dec_sums,
        dec_active,
        dec_inner,
        cross_keep,
        cross_send,
    ) = decoder(
        dec_flag, middle, memory_here + memory_peer, cot, cross_extras[:2], norms, w_cross, feed
    )
    with jax.named_scope("d_memory"):
        d_memory_here = d_memory_here + over(d_memory_other, "section", layer=1).astype(jnp.float32)
        d_memory_low = low(d_memory_here)
        arrived = across(d_memory_low, 1)
    with jax.named_scope("cross_sums"):
        cross_sum = from_cores(after(cross_keep, arrived), after(cross_send, arrived), layer=1)
        raw_cross = []
        cross_plane = plane_summed(cross_sum, raw=raw_cross, layer=1)

    d_enc_total, dz_low, enc_sums, second_keep, second_send = enc_out_back(
        flag, arrived, cot, enc_total, norms, d_dec_low, enc_active, dec_active, feed
    )
    with jax.named_scope("ffn_sums"):
        raw_second_sum = []
        second_sum = from_cores(second_keep, second_send, raw=raw_second_sum)
    gain_row = jnp.broadcast_to(self_gain, (8, self_gain.shape[0]))
    d_self_total, d_self_low, self_norm, first_keep, first_send = enc_in_back(
        flag,
        after(dz_low, second_keep, cross_sum),
        d_enc_total,
        d_middle_dec,
        self_total,
        gain_row,
        middle_low,
        crossed_low,
        feed,
        enc_slope,
        dec_inner,
    )
    with jax.named_scope("ffn_sums"):
        gate = []
        second_plane = plane_summed(after(second_sum, d_self_low), raw=gate)
        first_sum = from_cores(after(first_keep, *raw_cross), after(first_send, *raw_cross), raw=gate)

    halves = []
    for first, earlier in ((0, ()), (2, gate)):
        halves.append(
            attend_back(
                flag,
                after(d_self_low, *earlier),
                start_low[: 2 * quarter],
                start_low,
                w_self,
                kept_self,
                self_extras,
                True,
                first,
                2,
            )
        )
    d_start_q = halves[0][0] + halves[1][0]
    with jax.named_scope("cross_sums"):
        share_cross = rows_summed(after(cross_plane, d_start_q), count, layer=1)
    with jax.named_scope("ffn_sums"):
        gate_later = []
        first_plane = plane_summed(after(first_sum, second_plane), raw=gate_later)
        second_share = rows_summed(second_plane, count, raw=gate_later)
    with jax.named_scope("self_sums"):
        (_, _, keep, send), (_, _, *later) = halves
        self_sum = [from_cores(after(keep, *gate), after(send, *gate), raw=gate_later)]
        raw_later = []
        self_sum.append(from_cores(*(after(part, *gate_later) for part in later), raw=raw_later))
        self_sum = jnp.concatenate(self_sum, axis=0)
    with jax.named_scope("d_start"):
        d_start_kv = after(halves[0][1], *raw_later) + halves[1][1]
        d_start = d_self_total + d_start_q + d_start_kv[: 2 * quarter]
        d_start = d_start + over(low(d_start_kv[2 * quarter :]), "section").astype(jnp.float32)
    d_source, gain_a, bias_a = norm_back(
        rows_here.astype(jnp.float32), gains[0], biases[0], d_start
    )

    rows_from = jnp.concatenate([enc_sums, self_norm, dec_sums, jnp.stack([gain_a, bias_a])], axis=0)
    enc_rows, dec_rows = jnp.array([24, 8, 0, 25, 9, 1]), jnp.array([8, 18, 16, 9, 19, 17])
    wanted = pick(enc_rows, dec_rows)[:, None] == jnp.arange(26)
    norm_sums = jnp.sum(jnp.where(wanted[:, :, None], rows_from[None], 0.0), axis=1)
    shards = 2**count
    sides = jnp.arange(2)
    held, outer = core ^ sides[:, None], sides[None, :]
    row_block = ((2 * outer + (1 ^ outer ^ held)) * shards)[:, :, None] + jnp.arange(shards)
    column_block = (2 * (y_at ^ sides)[:, None] + (x_at ^ sides)[None, :]).reshape(-1)
    order = (row_block.reshape(2, -1)[:, None, :] + 0) * 4 + column_block[:, None]
    norm_sums = jnp.take(norm_sums.reshape(6, 8 * 2 * shards, -1), order.reshape(-1), axis=1)
    norm_sums = norm_sums.reshape(6, 2, 4, 2 * shards, -1)
    with jax.named_scope("norm_sums"):
        norm_got = over(norm_sums[:, 1], "section")
        norm_sums = norm_sums[:, 0] + norm_got
    with jax.named_scope("self_sums"):
        self_plane = plane_summed(self_sum, until=(norm_got,))
    with jax.named_scope("norm_sums"):
        norm_blocks = after(norm_sums.transpose(1, 2, 0, 3).reshape(4, 2 * shards, -1), self_plane)
        norm_plane = norm_blocks[0] + over(norm_blocks[1], "tx") + over(norm_blocks[2], "ty")
        norm_plane = norm_plane + over(norm_blocks[3], "ty", "tx")
    norm_width = norm_plane.shape[1]
    with jax.named_scope("self_sums"):
        pad = ((0, 0), (0, 15), (0, self_plane.shape[1] - norm_width))
        both = jnp.concatenate(
            [
                self_plane.reshape(2 * shards, -1, self_plane.shape[1]),
                jnp.pad(low(norm_plane)[:, None], pad),
            ],
            axis=1,
        )
        raw_self = []
        share_self = rows_summed(both.reshape(-1, self_plane.shape[1]), count, raw=raw_self)
        share_self = swapped(share_self).astype(jnp.float32)
    norm_shares = share_self[-16, :norm_width].reshape(6, -1)
    share_self = share_self[:-16]
    with jax.named_scope("ffn_sums"):
        first_share = rows_summed(after(first_plane, *raw_later), count)
        share_ffn = swapped(jnp.concatenate([first_share, second_share], axis=1)).astype(jnp.float32)
    share_first, share_second = share_ffn[:, :units], share_ffn[:, units:].T
    with jax.named_scope("outputs"):
        outputs = jnp.concatenate([pick(encoded, decoded), low(pick(d_source, d_start))], axis=1)
        outputs = rows_out(after(outputs, *raw_self))
    hidden_out = outputs[..., : hidden.shape[-1]]
    hidden_grad = outputs[..., hidden.shape[-1] :].astype(jnp.float32)
    g_query, g_key, g_value, g_out = unpack_heads(share_self)
    grad_qkv = jnp.stack([g_query, g_key, g_value], axis=1)
    c_query, c_key, c_value, c_out = unpack_heads(share_cross)
    with jax.named_scope("cross_out"):
        for_enc = cross_out(jnp.concatenate([c_key, c_value], axis=1), 0)
        for_dec = cross_out(jnp.concatenate([c_query, c_out], axis=1), 1)
    cross = jnp.where(core == 0, for_enc, for_dec).astype(jnp.float32)

    return (
        hidden_out,
        hidden_grad,
        grad_qkv[None],
        g_out[None],
        cross[None, :, :width],
        cross[None, :, width:],
        share_first[None],
        share_second[None],
        norm_shares[None, :3],
        norm_shares[None, 3:],
    )


def solution(mesh):
    _, dp_count, _ = mesh.devices.shape
    count = dp_count.bit_length() - 3
    names = axes_of(count)
    dp, tensor = names[1:-2], names[-2:]
    split = Mesh(mesh.devices.reshape((2,) * len(names)), names)
    rows = P("section", None, dp, tensor, None)
    in_specs = (
        rows,
        rows,
        P(None, None, dp, None),
        P("section", dp, None, tensor),
        P("section", dp, tensor),
        P("section", dp, tensor),
        P("section", dp, tensor),
        P("section", dp, tensor),
        P("section", tensor, dp),
        P("section", None, None),
        P("section", None, None),
    )
    out_specs = (
        rows,
        rows,
        P("section", dp, None, tensor),
        P("section", dp, tensor),
        P("section", dp, tensor),
        P("section", dp, tensor),
        P("section", dp, tensor),
        P("section", tensor, dp),
        P("section", None, dp + tensor),
        P("section", None, dp + tensor),
    )
    return jax.shard_map(
        functools.partial(body, count), mesh=split, in_specs=in_specs, out_specs=out_specs, check_vma=False
    )
```

```python
import functools

import jax
import jax.numpy as jnp
from jax import lax
from jax.experimental import pallas as pl
from jax.experimental.pallas import tpu as pltpu
from jax.sharding import Mesh
from jax.sharding import PartitionSpec as P

HDIM = 64
LANES = 128
MASKED = -1e30
NORM_EPS = 1e-05
VMEM_BYTES = 56 * 1024 * 1024

SEG_LANES = 8
PART_LANE = 12

PARTS = 2
TILE_ROWS = 256
HEADS = ((0, 1, 2, 0, 0), (0, 1, 2, 1, 1), (1, 3, 0, 0, 1))


def mul(a, b):
    return jnp.dot(a, b, preferred_element_type=jnp.float32)


def mul_nt(a, b):
    return lax.dot_general(a, b, (((1,), (1,)), ((), ())), preferred_element_type=jnp.float32)


def mul_tn(a, b):
    return lax.dot_general(a, b, (((0,), (0,)), ((), ())), preferred_element_type=jnp.float32)


def tile_of(values, index):
    return values[:, index * LANES : (index + 1) * LANES]


def lane_ids(rows):
    return lax.broadcasted_iota(jnp.int32, (rows, LANES), 1)


def half_mask(rows, half):
    lanes = lane_ids(rows)
    return lanes >= HDIM if half else lanes < HDIM


def in_parts(base, column):
    lanes = lane_ids(base.shape[0])
    high = column.astype(jnp.bfloat16).astype(jnp.float32)
    rest = column - high
    middle = rest.astype(jnp.bfloat16).astype(jnp.float32)
    low = rest - middle
    parts = jnp.where(
        lanes == PART_LANE,
        high,
        jnp.where(lanes == PART_LANE + 1, middle, jnp.where(lanes == PART_LANE + 2, low, base)),
    )
    return parts.astype(jnp.bfloat16)


def with_triangle(scores, tri, at):
    size = tri.shape[1]
    pieces = []
    if at > 0:
        pieces.append(scores[:, : at * size])
    pieces.append(scores[:, at * size : (at + 1) * size] + tri)
    pieces.append(scores[:, (at + 1) * size :])
    return jnp.concatenate(pieces, axis=1)


def places(core, block):
    return [pl.multiple_of((1 - core) * block, block), pl.multiple_of((2 + core) * block, block)]


def assemble(flag_ref, own_refs, peer_refs, w_ref):
    core, block = flag_ref[0], own_refs[0].shape[1] // 2
    for holder, refs in ((core, own_refs), (1 - core, peer_refs)):
        for part, ref in enumerate(refs):
            width = ref.shape[2]
            for at, place in enumerate(places(holder, block)):
                w_ref[pl.ds(place, block), part * width : (part + 1) * width] = ref[0, at * block : (at + 1) * block]


def hand_out(flag_ref, g_ref, keep_ref, send_ref):
    core, block = flag_ref[0], keep_ref.shape[1] // 2
    for holder, ref in ((core, keep_ref), (1 - core, send_ref)):
        for at, place in enumerate(places(holder, block)):
            ref[0, at * block : (at + 1) * block] = g_ref[pl.ds(place, block), :]


def where_active(kernel):
    def guarded(flag_ref, *refs):
        @pl.when(flag_ref[1] == 1)
        def _():
            kernel(flag_ref, *refs)

    return guarded


def scaled_queries(q_ref, at, q_tile, q_half):
    queries = q_ref[0, at, q_tile * LANES : (q_tile + 1) * LANES] * 0.125
    return jnp.where(half_mask(queries.shape[0], q_half), queries, 0).astype(jnp.bfloat16)


def units_of(total, rows):
    return [
        (slice(part * rows, (part + 1) * rows), part, head)
        for part in range(total // rows)
        for head in range(len(HEADS))
    ]


def attend_block(causal, xq_ref, xkv_ref, w_ref, qx_ref, kx_ref, tri_ref, q_ref, kv_ref, c_ref, l_ref):
    q_ref[0] = mul(xq_ref[...], w_ref[:, : 2 * LANES]).astype(jnp.bfloat16)
    kv_ref[0] = mul(xkv_ref[...], w_ref[:, LANES : 5 * LANES]).astype(jnp.bfloat16)
    rows = TILE_ROWS
    low = half_mask(rows, 0)

    def scores_of(at, part, head):
        q_tile, k_tile, _, q_half, _ = HEADS[head]
        keys = kv_ref[0, :, k_tile * LANES : (k_tile + 1) * LANES]
        scores = mul_nt(
            jnp.concatenate([scaled_queries(q_ref, at, q_tile, q_half), qx_ref[at, :]], axis=1),
            jnp.concatenate([keys, kx_ref[...]], axis=1),
        )
        return with_triangle(scores, tri_ref[...], part) if causal else scores

    units = units_of(q_ref.shape[1], rows)
    ahead = scores_of(*units[0])
    contexts, totals = [], None
    for index, (at, part, head) in enumerate(units):
        scores = ahead
        if index + 1 < len(units):
            ahead = scores_of(*units[index + 1])
        v_tile = HEADS[head][2]
        values = kv_ref[0, :, v_tile * LANES : (v_tile + 1) * LANES]
        highest = jnp.max(scores, axis=1, keepdims=True)
        weights = jnp.exp(scores - highest)
        sums = jnp.sum(weights, axis=1, keepdims=True)
        contexts.append(mul(weights.astype(jnp.bfloat16), values) / sums)
        logs = jnp.broadcast_to(highest + jnp.log(sums), (rows, LANES))
        totals = logs if head == 0 else jnp.where(lane_ids(rows) == head, logs, totals)
        if head == len(HEADS) - 1:
            c_ref[0, at, :LANES] = jnp.where(low, 0, contexts[2]).astype(jnp.bfloat16)
            c_ref[0, at, LANES:] = jnp.where(low, contexts[0], contexts[1]).astype(jnp.bfloat16)
            l_ref[0, at, :] = totals
            contexts = []
    return mul_nt(c_ref[0], w_ref[:, 4 * LANES :])


def attend_kernel(causal, flag_ref, xq_ref, xkv_ref, own_ref, peer_ref, qx_ref, kx_ref, tri_ref, o_ref, *refs):
    q_ref, kv_ref, c_ref, l_ref, w_ref = refs
    assemble(flag_ref, [own_ref], [peer_ref], w_ref)
    out = attend_block(causal, xq_ref, xkv_ref, w_ref, qx_ref, kx_ref, tri_ref, q_ref, kv_ref, c_ref, l_ref)
    add_up(pl.program_id(0) == 0, o_ref, out)


def add_up(first, ref, value):
    @pl.when(first)
    def _():
        ref[...] = value

    @pl.when(jnp.logical_not(first))
    def _():
        ref[...] += value


def attend_back_block(causal, do_ref, xq_ref, xkv_ref, w_ref, qx_ref, kx_ref, tri_ref, kept, work):
    q_ref, kv_ref, c_ref, l_ref = kept
    sum_ref, dq_ref, dkv_ref, g_ref = work
    rows = TILE_ROWS
    d_context = mul(do_ref[...], w_ref[:, 4 * LANES :]).astype(jnp.bfloat16)
    low = half_mask(rows, 0)

    def products_of(at, part, head):
        q_tile, k_tile, v_tile, q_half, v_half = HEADS[head]
        c_tile = 0 if head == 2 else 1
        keys = kv_ref[0, :, k_tile * LANES : (k_tile + 1) * LANES]
        values = kv_ref[0, :, v_tile * LANES : (v_tile + 1) * LANES]
        queries = scaled_queries(q_ref, at, q_tile, q_half)
        d_rows = jnp.where(half_mask(rows, v_half), tile_of(d_context[at], c_tile), 0).astype(jnp.bfloat16)
        total = l_ref[0, at, head : head + 1]
        scores = mul_nt(
            jnp.concatenate([queries, in_parts(qx_ref[at, :].astype(jnp.float32), -total)], axis=1),
            jnp.concatenate([keys, kx_ref[...]], axis=1),
        )
        if causal:
            scores = with_triangle(scores, tri_ref[...], part)
        return scores, mul_nt(d_rows, values), queries, d_rows, keys

    units = units_of(q_ref.shape[1], rows)
    ahead = products_of(*units[0])
    d_queries = []
    for index, (at, part, head) in enumerate(units):
        scores, d_probs, queries, d_rows, keys = ahead
        if index + 1 < len(units):
            ahead = products_of(*units[index + 1])
        _, k_tile, v_tile, _, _ = HEADS[head]
        probs = jnp.exp(scores)
        inner = jnp.sum(probs * d_probs, axis=1, keepdims=True)
        d_scores = (probs * (d_probs - inner)).astype(jnp.bfloat16)
        d_values = mul_tn(probs.astype(jnp.bfloat16), d_rows)
        d_keys = mul_tn(d_scores, queries)
        d_queries.append(mul(d_scores, keys) * 0.125)
        k_at = slice(k_tile * LANES, (k_tile + 1) * LANES)
        v_at = slice(v_tile * LANES, (v_tile + 1) * LANES)
        if part == 0 and head != 1:
            sum_ref[:, k_at] = d_keys
            sum_ref[:, v_at] = d_values
        else:
            sum_ref[:, k_at] += d_keys
            sum_ref[:, v_at] += d_values
        if head == len(HEADS) - 1:
            dq_ref[at, :LANES] = jnp.where(low, d_queries[0], d_queries[1]).astype(jnp.bfloat16)
            dq_ref[at, LANES:] = jnp.where(low, d_queries[2], 0).astype(jnp.bfloat16)
            d_queries = []
    dkv_ref[...] = sum_ref[...].astype(jnp.bfloat16)
    d_xq = mul_nt(dq_ref[...], w_ref[:, : 2 * LANES])
    d_xkv = mul_nt(dkv_ref[...], w_ref[:, LANES : 5 * LANES])

    grad_q = mul_tn(xq_ref[...], dq_ref[...])
    grad_kv = mul_tn(xkv_ref[...], dkv_ref[...])
    grad_o = mul_tn(do_ref[...], c_ref[0])
    g_ref[:, :LANES] = grad_q[:, :LANES].astype(jnp.bfloat16)
    g_ref[:, LANES : 2 * LANES] = (grad_q[:, LANES:] + grad_kv[:, :LANES]).astype(jnp.bfloat16)
    g_ref[:, 2 * LANES : 4 * LANES] = grad_kv[:, LANES : 3 * LANES].astype(jnp.bfloat16)
    g_ref[:, 4 * LANES : 5 * LANES] = (grad_kv[:, 3 * LANES :] + grad_o[:, :LANES]).astype(jnp.bfloat16)
    g_ref[:, 5 * LANES :] = grad_o[:, LANES:].astype(jnp.bfloat16)
    return d_xq, d_xkv


def attend_back_kernel(causal, flag_ref, do_ref, xq_ref, xkv_ref, own_ref, peer_ref, *refs):
    kept, (qx_ref, kx_ref, tri_ref, dxq_ref, dxkv_ref, keep_ref, send_ref, w_ref) = refs[:4], refs[4:12]
    work = refs[12:]
    assemble(flag_ref, [own_ref], [peer_ref], w_ref)
    d_xq, d_xkv = attend_back_block(
        causal, do_ref, xq_ref, xkv_ref, w_ref, qx_ref, kx_ref, tri_ref, kept, work
    )
    add_up(pl.program_id(0) == 0, dxq_ref, d_xq)
    add_up(pl.program_id(0) == 0, dxkv_ref, d_xkv)
    hand_out(flag_ref, work[3], keep_ref, send_ref)


def whole(shape):
    return pl.BlockSpec(shape, lambda j, flag: (0,) * len(shape))


def held(shape):
    return pl.BlockSpec(shape, lambda j, flag: (0,) * len(shape), pipeline_mode=pl.Buffered(1))


def per_block(shape, first=0, gate=1):
    return pl.BlockSpec((1,) + shape, lambda j, flag: (first + j * flag[gate],) + (0,) * len(shape))


shape = jax.ShapeDtypeStruct


def call(kernel, name, micros, moved, grid, in_specs, out_specs, out_shape, scratch, *operands):
    return pl.pallas_call(
        where_active(kernel),
        grid_spec=pltpu.PrefetchScalarGridSpec(
            num_scalar_prefetch=1,
            grid=(grid,),
            in_specs=in_specs,
            out_specs=out_specs,
            scratch_shapes=scratch,
        ),
        out_shape=out_shape,
        compiler_params=pltpu.CompilerParams(vmem_limit_bytes=VMEM_BYTES),
        cost_estimate=cost(micros, moved),
        name=name,
    )(*operands)


def cost(micros, moved):
    return pl.CostEstimate(flops=int(micros * 1.15e9), bytes_accessed=int(moved), transcendentals=0)


def attend(flag, xq, xkv, weights, extras, causal):
    rows, width = xq.shape
    keys = xkv.shape[0]
    blocks = weights[0].shape[0]
    return call(
        functools.partial(attend_kernel, causal),
        "attend_self" if causal else "attend_cross",
        20,
        24 * 2**20,
        blocks,
        [held((rows, width)), held((keys, width))]
        + [per_block(part.shape[1:]) for part in weights]
        + [held(extra.shape) for extra in extras],
        [
            whole((rows, width)),
            per_block((rows, 2 * LANES)),
            per_block((keys, 4 * LANES)),
            per_block((rows, 2 * LANES)),
            per_block((rows, LANES)),
        ],
        [
            shape((rows, width), jnp.float32),
            shape((blocks, rows, 2 * LANES), jnp.bfloat16),
            shape((blocks, keys, 4 * LANES), jnp.bfloat16),
            shape((blocks, rows, 2 * LANES), jnp.bfloat16),
            shape((blocks, rows, LANES), jnp.float32),
        ],
        [pltpu.VMEM((width, 6 * LANES), jnp.bfloat16)],
        flag,
        xq,
        xkv,
        *weights,
        *extras,
    )


def attend_back(flag, d_out, xq, xkv, weights, kept, extras, causal, first, count):
    rows, width = xq.shape
    keys = xkv.shape[0]
    return call(
        functools.partial(attend_back_kernel, causal),
        "attend_self_back" if causal else "attend_cross_back",
        10 * count,
        6 * 2**20 * count,
        count,
        [held((rows, width)), held((rows, width)), held((keys, width))]
        + [per_block(part.shape[1:], first) for part in weights]
        + [
            per_block((rows, 2 * LANES), first),
            per_block((keys, 4 * LANES), first),
            per_block((rows, 2 * LANES), first),
            per_block((rows, LANES), first),
        ]
        + [held(extra.shape) for extra in extras],
        [whole((rows, width)), whole((keys, width))] + [per_block(part.shape[1:]) for part in weights],
        [shape((rows, width), jnp.float32), shape((keys, width), jnp.float32)]
        + [shape((count,) + part.shape[1:], jnp.bfloat16) for part in weights],
        [
            pltpu.VMEM((width, 6 * LANES), jnp.bfloat16),
            pltpu.VMEM((keys, 4 * LANES), jnp.float32),
            pltpu.VMEM((rows, 2 * LANES), jnp.bfloat16),
            pltpu.VMEM((keys, 4 * LANES), jnp.bfloat16),
            pltpu.VMEM((width, 6 * LANES), jnp.bfloat16),
        ],
        flag,
        d_out,
        xq,
        xkv,
        *weights,
        *kept,
        *extras,
    )


def ffn_block(x_ref, w_ref, units, g_ref, slope_ref, first, out_ref):
    inner = mul(x_ref[...], w_ref[:, :units])
    spread = 0.5 * (1.0 + lax.erf(inner * (0.5**0.5)))
    bell = jnp.exp(-0.5 * inner * inner) * 0.3989422804014327
    active = (inner * spread).astype(jnp.bfloat16)
    g_ref[0] = active
    slope_ref[0] = (spread + inner * bell).astype(jnp.bfloat16)
    add_up(first, out_ref, mul_nt(active, w_ref[:, units:]))


def ffn_kernel(flag_ref, x_ref, *refs):
    own_refs, peer_refs = refs[:PARTS], refs[PARTS : 2 * PARTS]
    z_ref, g_ref, slope_ref, w_ref = refs[2 * PARTS :]
    assemble(flag_ref, own_refs, peer_refs, w_ref)
    ffn_block(x_ref, w_ref, own_refs[0].shape[2], g_ref, slope_ref, pl.program_id(0) == 0, z_ref)


def feed_blocks(feed, index):
    half, units = feed[0].shape[1], feed[0].shape[2] // 2
    return [
        pl.BlockSpec((1, half, units), lambda j, flag, side=side: (index(j, flag), 0, side))
        for _ in feed
        for side in (0, 1)
    ]


def feed_operands(feed):
    return [part for part in feed for _ in (0, 1)]


def ffn(flag, x, feed):
    rows, width = x.shape
    blocks, units = feed[0].shape[0], feed[0].shape[2] // 2
    return call(
        ffn_kernel,
        "ffn",
        12,
        rows * units * blocks * 16,
        blocks,
        [held((rows, width))] + feed_blocks(feed, lambda j, flag: j * flag[1]),
        [whole((rows, width)), per_block((rows, units)), per_block((rows, units))],
        [
            shape((rows, width), jnp.float32),
            shape((blocks, rows, units), jnp.bfloat16),
            shape((blocks, rows, units), jnp.bfloat16),
        ],
        [pltpu.VMEM((width, 2 * units), jnp.bfloat16)],
        flag,
        x,
        *feed_operands(feed),
    )


def ffn_back_block(dz_ref, w_ref, units, slope_ref, dh_ref, first, out_ref):
    d_active = mul(dz_ref[...], w_ref[:, units:])
    d_inner = (d_active * slope_ref[0].astype(jnp.float32)).astype(jnp.bfloat16)
    dh_ref[0] = d_inner
    add_up(first, out_ref, mul_nt(d_inner, w_ref[:, :units]))


def layer_norm(values, gain_row, bias_row):
    average = jnp.mean(values, axis=-1, keepdims=True)
    centered = values - average
    variance = jnp.mean(centered * centered, axis=-1, keepdims=True)
    return centered * lax.rsqrt(variance + NORM_EPS) * gain_row + bias_row


def norm_back(values, gain_row, bias_row, upstream):
    _, pullback = jax.vjp(layer_norm, values, gain_row, bias_row)
    return pullback(upstream)


def norm_parts(values):
    average = jnp.mean(values, axis=1, keepdims=True)
    centered = values - average
    scale = lax.rsqrt(jnp.mean(centered * centered, axis=1, keepdims=True) + NORM_EPS)
    return centered * scale, scale


def norm_gradients(values, gain_row, upstream):
    shaped, scale = norm_parts(values)
    inner = upstream * gain_row
    mean_inner = jnp.mean(inner, axis=1, keepdims=True)
    mean_product = jnp.mean(inner * shaped, axis=1, keepdims=True)
    d_values = scale * (inner - mean_inner - shaped * mean_product)
    d_gain = jnp.sum(upstream * shaped, axis=0, keepdims=True)
    return d_values, d_gain, jnp.sum(upstream, axis=0, keepdims=True)


def enc_out_back_kernel(
    flag_ref, arrived_ref, cot_ref, total_ref, norms_ref, d_dec_ref, enc_ref, dec_ref, *refs
):
    d_total_ref, dz_ref, sums_ref, keep_ref, send_ref, g_ref, left_t_ref = refs

    @pl.when(jnp.logical_and(pl.program_id(0) == 0, flag_ref[2] == 1))
    def _():
        upstream = arrived_ref[...].astype(jnp.float32) + cot_ref[...].astype(jnp.float32)
        d_total, sums_ref[0:1, :], sums_ref[1:2, :] = norm_gradients(total_ref[...], norms_ref[2:3, :], upstream)
        d_total_ref[...] = d_total
        dz_ref[...] = d_total.astype(jnp.bfloat16)

    @pl.when(jnp.logical_and(pl.program_id(0) == 0, flag_ref[2] == 0))
    def _():
        dz_ref[...] = d_dec_ref[...]

    @pl.when(pl.program_id(0) == 0)
    def _():
        left_t_ref[...] = dz_ref[...].T

    right = jnp.where(flag_ref[2] == 1, enc_ref[0], dec_ref[0])
    g_ref[...] = mul(left_t_ref[...], right).astype(jnp.bfloat16)
    hand_out(flag_ref, g_ref, keep_ref, send_ref)


def enc_out_back(flag, arrived, cot, total, norms, d_dec, enc_active, dec_active, feed):
    rows, width = cot.shape
    blocks, _, units = enc_active.shape
    like = shape((blocks, feed[0].shape[1], units), jnp.bfloat16)
    full = shape((rows, width), jnp.float32)
    return call(
        enc_out_back_kernel,
        "enc_out_back",
        9,
        rows * units * blocks * 8,
        blocks,
        [held(item.shape) for item in (arrived, cot, total, norms, d_dec)]
        + [per_block((rows, units), 0, 2), per_block((rows, units), 0, 3)],
        [whole((rows, width))] * 2 + [whole((8, width))] + [per_block(like.shape[1:])] * 2,
        [full, shape((rows, width), jnp.bfloat16), shape((8, width), jnp.float32)]
        + [like] * 2,
        [pltpu.VMEM((width, units), jnp.bfloat16), pltpu.VMEM((width, rows), jnp.bfloat16)],
        flag,
        arrived,
        cot,
        total,
        norms,
        d_dec,
        enc_active,
        dec_active,
    )


def enc_in_back_kernel(
    flag_ref, dz_ref, d_enc_ref, d_middle_ref, total_ref, gain_ref, middle_ref, crossed_ref, *refs
):
    first_own_ref, second_own_ref, first_peer_ref, second_peer_ref, slope_ref, dec_inner_ref, *refs = refs
    d_total_ref, d_low_ref, sums_ref, keep_ref, send_ref, w_ref, inner_ref, out_ref, g_ref, left_t_ref = refs
    step = pl.program_id(0)
    phase, at = step // 4, step % 4
    on_encoder = flag_ref[2] == 1

    @pl.when(jnp.logical_and(phase == 0, on_encoder))
    def _():
        assemble(flag_ref, [first_own_ref, second_own_ref], [first_peer_ref, second_peer_ref], w_ref)
        ffn_back_block(
            dz_ref, w_ref, first_own_ref.shape[2], slope_ref, inner_ref.at[pl.ds(at, 1)], at == 0, out_ref
        )

    @pl.when(step == 3)
    def _():
        upstream = jnp.where(on_encoder, d_enc_ref[...] + out_ref[...], d_middle_ref[...])
        d_total, sums_ref[0:1, :], sums_ref[1:2, :] = norm_gradients(total_ref[...], gain_ref[0:1, :], upstream)
        d_total_ref[...] = d_total
        d_low_ref[...] = d_total.astype(jnp.bfloat16)
        left_t_ref[...] = jnp.where(on_encoder, middle_ref[...], crossed_ref[...]).T

    @pl.when(phase == 1)
    def _():
        right = jnp.where(on_encoder, inner_ref[at], dec_inner_ref[0])
        g_ref[...] = mul(left_t_ref[...], right).astype(jnp.bfloat16)
        hand_out(flag_ref, g_ref, keep_ref, send_ref)


def enc_in_back(flag, dz, d_enc, d_middle, total, gain, middle, crossed, feed, slope, dec_inner):
    rows, width = dz.shape
    blocks, half, units = feed[0].shape[0], feed[0].shape[1], feed[0].shape[2] // 2
    full = shape((rows, width), jnp.float32)

    def at_step(of, low, high, gate):
        def index(j, flag):
            return (jnp.where(j < 4, j if low == "up" else low, j - 4 if high == "up" else high) * flag[gate],) + (
                0,
            ) * len(of)

        return pl.BlockSpec((1,) + of, index)

    return call(
        enc_in_back_kernel,
        "enc_in_back",
        19,
        rows * units * blocks * 20,
        8,
        [held(item.shape) for item in (dz, d_enc, d_middle, total, gain, middle, crossed)]
        + feed_blocks(feed, lambda j, flag: jnp.where(j < 4, j, 3) * flag[2])
        + [at_step((rows, units), "up", 3, 2), at_step((rows, units), 0, "up", 3)],
        [whole((rows, width))] * 2 + [whole((8, width))] + [at_step((half, units), 0, "up", 1)] * 2,
        [full, shape((rows, width), jnp.bfloat16), shape((8, width), jnp.float32)]
        + [shape((blocks, half, units), jnp.bfloat16)] * 2,
        [
            pltpu.VMEM((width, 2 * units), jnp.bfloat16),
            pltpu.VMEM((blocks, rows, units), jnp.bfloat16),
            pltpu.VMEM((rows, width), jnp.float32),
            pltpu.VMEM((width, units), jnp.bfloat16),
            pltpu.VMEM((width, rows), jnp.bfloat16),
        ],
        flag,
        dz,
        d_enc,
        d_middle,
        total,
        gain,
        middle,
        crossed,
        *feed_operands(feed),
        slope,
        dec_inner,
    )


def decoder_kernel(
    flag_ref,
    h1_ref,
    mem_a_ref,
    mem_b_ref,
    peer_a_ref,
    peer_b_ref,
    cot_ref,
    qx_ref,
    kx_ref,
    norms_ref,
    own_ref,
    peer_ref,
    first_own_ref,
    second_own_ref,
    first_peer_ref,
    second_peer_ref,
    decoded_ref,
    crossed_ref,
    d_dec_ref,
    d_middle_ref,
    mine_ref,
    other_ref,
    sums_ref,
    active_ref,
    inner_ref,
    keep_ref,
    send_ref,
    xq_ref,
    xkv_ref,
    wx_ref,
    wf_ref,
    q_ref,
    kv_ref,
    c_ref,
    l_ref,
    slope_ref,
    out_ref,
    total_ref,
    do_ref,
    dxkv_ref,
    *work,
):
    step = pl.program_id(0)
    phase, at = step // 4, step % 4
    first, last = at == 0, at == 3
    rows = h1_ref.shape[0]
    units = first_own_ref.shape[2]
    gain = [norms_ref[row : row + 1, :] for row in range(3)]
    bias = [norms_ref[3 + row : 4 + row, :] for row in range(3)]

    def kept(block):
        return tuple(ref.at[pl.ds(block, 1)] for ref in (q_ref, kv_ref, c_ref, l_ref))

    @pl.when(step == 0)
    def _():
        xq_ref[...] = h1_ref[...].astype(jnp.bfloat16)
        for part, ref in enumerate((mem_a_ref, mem_b_ref, peer_a_ref, peer_b_ref)):
            xkv_ref[part * rows // 2 : (part + 1) * rows // 2] = ref[...]

    @pl.when(jnp.logical_or(phase == 0, phase == 3))
    def _():
        assemble(flag_ref, [own_ref], [peer_ref], wx_ref)

    @pl.when(jnp.logical_or(phase == 1, phase == 2))
    def _():
        assemble(flag_ref, [first_own_ref, second_own_ref], [first_peer_ref, second_peer_ref], wf_ref)

    @pl.when(phase == 0)
    def _():
        add_up(first, out_ref, attend_block(False, xq_ref, xkv_ref, wx_ref, qx_ref, kx_ref, None, *kept(at)))

    @pl.when(jnp.logical_and(phase == 0, last))
    def _():
        total = h1_ref[...] + out_ref[...]
        total_ref[...] = total
        crossed = norm_parts(total)[0] * gain[1] + bias[1]
        mine_ref[...] = crossed
        crossed_ref[...] = crossed.astype(jnp.bfloat16)

    @pl.when(phase == 1)
    def _():
        ffn_block(crossed_ref, wf_ref, units, active_ref, slope_ref.at[pl.ds(at, 1)], first, out_ref)

    @pl.when(jnp.logical_and(phase == 1, last))
    def _():
        total = mine_ref[...] + out_ref[...]
        decoded_ref[...] = (norm_parts(total)[0] * gain[2] + bias[2]).astype(jnp.bfloat16)
        d_total, sums_ref[0:1, :], sums_ref[1:2, :] = norm_gradients(
            total, gain[2], cot_ref[...].astype(jnp.float32)
        )
        d_middle_ref[...] = d_total
        d_dec_ref[...] = d_total.astype(jnp.bfloat16)

    @pl.when(phase == 2)
    def _():
        ffn_back_block(d_dec_ref, wf_ref, units, slope_ref.at[pl.ds(3 - at, 1)], inner_ref, first, out_ref)

    @pl.when(jnp.logical_and(phase == 2, last))
    def _():
        d_total, sums_ref[2:3, :], sums_ref[3:4, :] = norm_gradients(
            total_ref[...], gain[1], d_middle_ref[...] + out_ref[...]
        )
        d_middle_ref[...] = d_total
        do_ref[...] = d_total.astype(jnp.bfloat16)

    @pl.when(phase == 3)
    def _():
        d_xq, d_xkv = attend_back_block(
            False, do_ref, xq_ref, xkv_ref, wx_ref, qx_ref, kx_ref, None, kept(3 - at), work
        )
        add_up(first, out_ref, d_xq)
        add_up(first, dxkv_ref, d_xkv)
        hand_out(flag_ref, work[3], keep_ref, send_ref)

    @pl.when(jnp.logical_and(phase == 3, last))
    def _():
        d_middle_ref[...] += out_ref[...]
        mine_ref[...] = dxkv_ref[:rows]
        other_ref[...] = dxkv_ref[rows:].astype(jnp.bfloat16)


def decoder(flag, h1, memory, cot, extras, norms, cross, feed):
    rows, width = h1.shape
    blocks, half, _ = cross[0].shape
    units = feed[0].shape[2] // 2
    keys = 2 * rows
    qx, kx = extras

    def at_step(of, in_phase):
        def index(j, flag):
            at = j % 4
            choice = [{"up": at, "down": 3 - at}.get(way, way) for way in in_phase]
            chosen = choice[3]
            for phase in (2, 1, 0):
                chosen = jnp.where(j // 4 == phase, choice[phase], chosen)
            return (chosen * flag[1],) + (0,) * len(of)

        return pl.BlockSpec((1,) + of, index)

    part = (half, cross[0].shape[2])
    full = shape((rows, width), jnp.float32)
    rounded = shape((rows, width), jnp.bfloat16)
    return call(
        decoder_kernel,
        "decoder",
        90,
        40 * 2**20,
        16,
        [held(item.shape) for item in (h1, *memory, cot, qx, kx, norms)]
        + [at_step(part, ("up", 3, 3, "down"))] * 2
        + feed_blocks(feed, lambda j, flag: at_step((half, units), (0, "up", "down", 0)).index_map(j, flag)[0]),
        [whole((rows, width))] * 6
        + [whole((8, width))]
        + [
            at_step((rows, units), (0, "up", 3, 3)),
            at_step((rows, units), (3, 3, "down", 0)),
            at_step(part, (3, 3, 3, "down")),
            at_step(part, (3, 3, 3, "down")),
        ],
        [rounded, rounded, rounded, full, full, rounded, shape((8, width), jnp.float32)]
        + [shape((blocks, rows, units), jnp.bfloat16)] * 2
        + [shape(cross[0].shape, jnp.bfloat16)] * 2,
        [
            pltpu.VMEM((rows, width), jnp.bfloat16),
            pltpu.VMEM((keys, width), jnp.bfloat16),
            pltpu.VMEM((width, 6 * LANES), jnp.bfloat16),
            pltpu.VMEM((width, 2 * units), jnp.bfloat16),
            pltpu.VMEM((blocks, rows, 2 * LANES), jnp.bfloat16),
            pltpu.VMEM((blocks, keys, 4 * LANES), jnp.bfloat16),
            pltpu.VMEM((blocks, rows, 2 * LANES), jnp.bfloat16),
            pltpu.VMEM((blocks, rows, LANES), jnp.float32),
            pltpu.VMEM((blocks, rows, units), jnp.bfloat16),
            pltpu.VMEM((rows, width), jnp.float32),
            pltpu.VMEM((rows, width), jnp.float32),
            pltpu.VMEM((rows, width), jnp.bfloat16),
            pltpu.VMEM((keys, width), jnp.float32),
            pltpu.VMEM((keys, 4 * LANES), jnp.float32),
            pltpu.VMEM((rows, 2 * LANES), jnp.bfloat16),
            pltpu.VMEM((keys, 4 * LANES), jnp.bfloat16),
            pltpu.VMEM((width, 6 * LANES), jnp.bfloat16),
        ],
        flag,
        h1,
        *memory,
        cot,
        qx,
        kx,
        norms,
        *cross,
        *feed_operands(feed),
    )


def low(values):
    return values.astype(jnp.bfloat16)


def axes_of(count):
    return ("section", "zh", "zl") + tuple("e%d" % at for at in range(count)) + ("ty", "tx")


def layer_of(place):
    return 1 ^ place["zh"] ^ place["zl"]


def moved(x, names, to):
    names = [name for name in axes_of(8) if name in names]

    def index(place):
        return sum(place[name] << (len(names) - 1 - at) for at, name in enumerate(names))

    pairs = []
    for source in range(2 ** len(names)):
        place = {name: source >> (len(names) - 1 - at) & 1 for at, name in enumerate(names)}
        target = to(place)
        if target is not None:
            pairs.append((source, index(target)))
    return lax.ppermute(x, tuple(names), pairs)


def over(x, *axes, layer=None):
    def to(place):
        if layer is not None and layer_of(place) != layer:
            return None
        return {**place, **{axis: 1 - place[axis] for axis in axes}}

    return moved(x, axes if layer is None else axes + Z, to)


Z = ("zh", "zl")


def swapped(x):
    def to(place):
        if place["section"] == layer_of(place):
            return place
        return {"section": 1 - place["section"], "zh": place["zh"], "zl": 1 - place["zl"]}

    return moved(x, ("section",) + Z, to)


def turned(x):
    return moved(x, ("section", "ty"), lambda place: {"section": place["ty"], "ty": place["section"]})


def sent_home(x, other):
    def to(place):
        return {
            "section": layer_of(place),
            "zh": place["zh"],
            "zl": 1 ^ place["zh"] ^ place["ty"],
            "ty": place["section"],
            "tx": place["tx"] ^ other,
        }

    return moved(x, ("section",) + Z + ("ty", "tx"), to)


def cross_in(x, layer):
    def to(place):
        if place["section"] != layer:
            return None
        return {"section": layer_of(place), "zh": place["zh"], "zl": place["zh"]}

    return moved(x, ("section",) + Z, to)


def cross_out(x, layer):
    def to(place):
        if layer_of(place) != 1:
            return None
        return {"section": layer, "zh": place["zh"], "zl": 1 ^ place["zh"] ^ place["section"]}

    return moved(x, ("section",) + Z, to)


def in_order(x, flag, axis):
    return jnp.where(flag == 1, jnp.flip(x, axis), x)


def pack_heads(query, key, value, out):
    pair = 2 * HDIM
    return jnp.concatenate(
        [
            query,
            value[:, pair:],
            key[:, :pair],
            value[:, :pair],
            key[:, pair:],
            out[:, pair:],
            out[:, :pair],
        ],
        axis=1,
    )


def unpack_heads(packed):
    part = [packed[:, at * HDIM : (at + 1) * HDIM] for at in range(12)]
    query = jnp.concatenate(part[0:3], axis=1)
    key = jnp.concatenate([part[4], part[5], part[8]], axis=1)
    value = jnp.concatenate([part[6], part[7], part[3]], axis=1)
    out = jnp.concatenate([part[10], part[11], part[9]], axis=1)
    return query, key, value, out


def after(x, *earlier):
    return lax.optimization_barrier((x,) + earlier)[0]


def plane_gathered(x, until=(), **only):
    parts = [x, over(x, "tx", **only), over(x, "ty", **only), over(x, "ty", "tx", **only)]
    return jnp.stack([after(part, *until) for part in parts])


def plane_summed(x, until=(), raw=None, **only):
    terms = [x[0], over(x[1], "tx", **only), over(x[2], "ty", **only), over(x[3], "ty", "tx", **only)]
    if raw is not None:
        raw.extend(terms[1:])
    terms = [after(term, *until) for term in terms]
    return low(sum(term.astype(jnp.float32) for term in terms))


def rows_gathered(x, count, until=(), raw=None, **only):
    for axes in [("e%d" % at,) for at in reversed(range(count))] + [Z]:
        got = over(x, *axes, **only)
        if raw is not None:
            raw.append(got)
        parts = [after(part, *until) for part in (x, got)]
        both = in_order(jnp.stack(parts, axis=-3), lax.axis_index(axes[0]), x.ndim - 2)
        x = both.reshape(x.shape[:-2] + (2 * x.shape[-2], x.shape[-1]))
    return x


def rows_summed(x, count, until=(), raw=None, **only):
    for axes in [Z] + [("e%d" % at,) for at in range(count)]:
        halves = x.reshape(x.shape[:-2] + (2, x.shape[-2] // 2, x.shape[-1]))
        halves = in_order(halves, lax.axis_index(axes[0]), x.ndim - 2)
        got = over(halves[..., 1, :, :], *axes, **only)
        if raw is not None:
            raw.append(got)
        x = plus(halves[..., 0, :, :], after(got, *until))
    return x


def plus(first, second):
    return low(first.astype(jnp.float32) + second.astype(jnp.float32))


def from_cores(keep, send, raw=None, **only):
    got = over(send, "section", **only)
    if raw is not None:
        raw.append(got)
    return plus(keep, got)


def body(
    count,
    hidden,
    cotangent,
    segments,
    sa_qkv,
    sa_out,
    cross_one,
    cross_two,
    ffn_in,
    ffn_out,
    norm_gain,
    norm_bias,
):
    core = lax.axis_index("section")
    x_at, y_at, zh_at, zl_at = (lax.axis_index(name) for name in ("tx", "ty", "zh", "zl"))
    layer = 1 ^ zh_at ^ zl_at
    on_encoder = layer == 0
    quarter = hidden.shape[3]
    enc_flag = jnp.stack([core, 1 - layer, 1 - layer, layer])
    dec_flag = jnp.stack([core, layer, 1 - layer, layer])
    flag = jnp.stack([core, jnp.ones_like(core), 1 - layer, layer])

    def pick(first, second):
        return jnp.where(on_encoder, first, second)

    def of_one_row(x):
        both = in_order(x[0, :, 0], x_at, 0)
        return in_order(jnp.stack([both[0], over(both[1], "tx")]), x_at, 0).reshape(2 * quarter, -1)

    def rows_out(x, raw=None):
        mine, other = in_order(x.reshape(2, quarter, -1), x_at, 0)
        both = [sent_home(mine, 0), sent_home(other, 1)]
        if raw is not None:
            raw.extend(both)
        return in_order(jnp.stack(both), x_at, 0)[None, :, None]

    units = ffn_in.shape[2]
    width = cross_one.shape[2]
    packed_self = pack_heads(sa_qkv[0, :, 0], sa_qkv[0, :, 1], sa_qkv[0, :, 2], sa_out[0])
    packed_ffn = jnp.concatenate([ffn_in[0], ffn_out[0].T], axis=1)
    with jax.named_scope("norms_in"):
        norms = swapped(jnp.concatenate([norm_gain[0], norm_bias[0]], axis=0))
        gains, biases = norms[:3], norms[3:]
        seg_own = segments[:, :, 0].astype(jnp.float32)
        seg_here = jnp.where(zl_at == 1 ^ zh_at ^ y_at, seg_own, over(seg_own, "zl")).astype(jnp.int32)
    with jax.named_scope("hidden_in"):
        one_row = of_one_row(jnp.concatenate([hidden, cotangent], axis=-1))
    with jax.named_scope("self_weights"):
        shard_self = swapped(packed_self)
    with jax.named_scope("cross_weights"):
        cross_low = after(jnp.concatenate([cross_one[0], cross_two[0]], axis=1), shard_self)
        pair_kv, pair_qo = cross_in(cross_low, 0), cross_in(cross_low, 1)
    with jax.named_scope("hidden_in"):
        one_row = swapped(after(one_row, pair_kv, pair_qo))
    with jax.named_scope("ffn_weights"):
        shard_ffn = swapped(after(packed_ffn, one_row))

    def both_rows(x):
        for_enc = rows_gathered(x, count, layer=0)
        return pick(for_enc, rows_gathered(after(x, for_enc), count, layer=1))

    with jax.named_scope("self_weights"):
        rows_self = both_rows(shard_self)
        raw_ffn_rows = []
        rows_ffn_enc = rows_gathered(after(shard_ffn, rows_self), count, raw=raw_ffn_rows, layer=0)
        own_self = plane_gathered(rows_self, until=tuple(raw_ffn_rows))
        w_self = [own_self, over(own_self, "section")]
    with jax.named_scope("hidden_in"):
        rows_here = turned(one_row)
        rows_here, cot = rows_here[:, : hidden.shape[-1]], rows_here[:, hidden.shape[-1] :]
        rows_all = jnp.concatenate([rows_here, over(rows_here, "section")], axis=0)
    with jax.named_scope("cross_weights"):
        packed = pack_heads(pair_qo[:, :width], pair_kv[:, :width], pair_kv[:, width:], pair_qo[:, width:])
    with jax.named_scope("ffn_weights"):
        rows_ffn = pick(rows_ffn_enc, rows_gathered(after(shard_ffn, *raw_ffn_rows), count, layer=1))

    both_segments = in_order(seg_here, x_at, 1)[:, 0]
    ordered = in_order(both_segments.reshape(2, 2, 2 * quarter), core, 1).reshape(2, 4 * quarter)
    source_seg, target_seg = ordered[0], ordered[1]
    self_seg = pick(source_seg, target_seg)
    parts = jnp.arange(4)
    quarter_of = jnp.repeat(2 * ((parts // 2) ^ core) + parts % 2, quarter)
    lanes = jnp.arange(LANES)[None, :]

    def key_extras(seg):
        differs = jnp.logical_and(lanes < SEG_LANES, seg[:, None] != lanes)
        later = jnp.logical_and(
            jnp.logical_and(lanes >= SEG_LANES, lanes < PART_LANE),
            quarter_of[:, None] > lanes - SEG_LANES,
        )
        part = jnp.logical_and(lanes >= PART_LANE, lanes < PART_LANE + 3)
        return jnp.where(differs | later | part, 1.0, 0.0).astype(jnp.bfloat16)

    def query_extras(seg, causal):
        seg, at = seg[: 2 * quarter], quarter_of[: 2 * quarter]
        same = seg[:, None] == lanes
        here = jnp.logical_and(at[:, None] + SEG_LANES == lanes, causal)
        return jnp.where(same | here, MASKED, 0.0).astype(jnp.bfloat16)

    at_row = jnp.arange(quarter)
    later_key = jnp.logical_and(at_row[None, :] > at_row[:, None], jnp.logical_not(on_encoder))
    tri = jnp.where(later_key, MASKED, 0.0).astype(jnp.float32)
    self_extras = (query_extras(self_seg, jnp.logical_not(on_encoder)), key_extras(self_seg), tri)
    cross_extras = (query_extras(target_seg, False), key_extras(source_seg), tri)

    start = rows_all.astype(jnp.float32)
    start = pick(layer_norm(start, gains[0], biases[0]), start)
    start_here = start[: 2 * quarter]
    start_low = low(start)
    self_gain, self_bias = pick(gains[1], gains[0]), pick(biases[1], biases[0])
    raw_cross_rows = []
    with jax.named_scope("cross_weights"):
        rows_cross = rows_gathered(after(packed, rows_ffn), count, raw=raw_cross_rows, layer=1)
    self_out, *kept_self = attend(
        flag, start_low[: 2 * quarter], start_low, w_self, self_extras, True
    )
    with jax.named_scope("ffn_weights"):
        own_ffn = plane_gathered(after(rows_ffn, own_self), until=(self_out, *raw_cross_rows))
        feed = [own_ffn, over(own_ffn, "section")]
    self_total = start_here + after(self_out, *raw_cross_rows)
    middle = layer_norm(self_total, self_gain, self_bias)
    middle_low = low(middle)

    enc_out, enc_active, enc_slope = ffn(enc_flag, middle_low, feed)
    enc_total = middle + enc_out
    encoded = low(layer_norm(enc_total, gains[2], biases[2]))
    def across(x, layer):
        return moved(x, Z, lambda place: {**place, "zl": 1 - place["zl"]} if layer_of(place) == layer else None)

    with jax.named_scope("memory"):
        memory_here = [across(encoded[:quarter], 0), across(encoded[quarter:], 0)]
        memory_peer = [over(part, "section", layer=1) for part in memory_here]
    with jax.named_scope("cross_weights"):
        own_cross = plane_gathered(after(rows_cross, feed[1]), until=tuple(memory_here), layer=1)
        w_cross = [own_cross, over(own_cross, "section", layer=1)]
    (
        decoded,
        crossed_low,
        d_dec_low,
        d_middle_dec,
        d_memory_here,
        d_memory_other,
        dec_sums,
        dec_active,
        dec_inner,
        cross_keep,
        cross_send,
    ) = decoder(
        dec_flag, middle, memory_here + memory_peer, cot, cross_extras[:2], norms, w_cross, feed
    )
    with jax.named_scope("d_memory"):
        d_memory_here = d_memory_here + over(d_memory_other, "section", layer=1).astype(jnp.float32)
        d_memory_low = low(d_memory_here)
        arrived = across(d_memory_low, 1)
    with jax.named_scope("cross_sums"):
        cross_sum = from_cores(after(cross_keep, arrived), after(cross_send, arrived), layer=1)
        raw_cross = []
        cross_plane = plane_summed(cross_sum, raw=raw_cross, layer=1)

    d_enc_total, dz_low, enc_sums, second_keep, second_send = enc_out_back(
        flag, arrived, cot, enc_total, norms, d_dec_low, enc_active, dec_active, feed
    )
    with jax.named_scope("ffn_sums"):
        raw_second_sum = []
        second_sum = from_cores(second_keep, second_send, raw=raw_second_sum)
    gain_row = jnp.broadcast_to(self_gain, (8, self_gain.shape[0]))
    d_self_total, d_self_low, self_norm, first_keep, first_send = enc_in_back(
        flag,
        after(dz_low, second_keep, cross_sum),
        d_enc_total,
        d_middle_dec,
        self_total,
        gain_row,
        middle_low,
        crossed_low,
        feed,
        enc_slope,
        dec_inner,
    )
    with jax.named_scope("ffn_sums"):
        gate = []
        second_plane = plane_summed(after(second_sum, d_self_low), raw=gate)
        first_sum = from_cores(after(first_keep, *raw_cross), after(first_send, *raw_cross), raw=gate)

    halves = []
    for first, earlier in ((0, ()), (2, gate)):
        halves.append(
            attend_back(
                flag,
                after(d_self_low, *earlier),
                start_low[: 2 * quarter],
                start_low,
                w_self,
                kept_self,
                self_extras,
                True,
                first,
                2,
            )
        )
    d_start_q = halves[0][0] + halves[1][0]
    with jax.named_scope("cross_sums"):
        share_cross = rows_summed(after(cross_plane, d_start_q), count, layer=1)
    with jax.named_scope("ffn_sums"):
        gate_later = []
        first_plane = plane_summed(after(first_sum, second_plane), raw=gate_later)
        second_share = rows_summed(second_plane, count, raw=gate_later)
    with jax.named_scope("self_sums"):
        (_, _, keep, send), (_, _, *later) = halves
        self_sum = [from_cores(after(keep, *gate), after(send, *gate), raw=gate_later)]
        raw_later = []
        self_sum.append(from_cores(*(after(part, *gate_later) for part in later), raw=raw_later))
        self_sum = jnp.concatenate(self_sum, axis=0)
    with jax.named_scope("d_start"):
        d_start_kv = after(halves[0][1], *raw_later) + halves[1][1]
        d_start = d_self_total + d_start_q + d_start_kv[: 2 * quarter]
        d_start = d_start + over(low(d_start_kv[2 * quarter :]), "section").astype(jnp.float32)
    d_source, gain_a, bias_a = norm_back(
        rows_here.astype(jnp.float32), gains[0], biases[0], d_start
    )

    rows_from = jnp.concatenate([enc_sums, self_norm, dec_sums, jnp.stack([gain_a, bias_a])], axis=0)
    enc_rows, dec_rows = jnp.array([24, 8, 0, 25, 9, 1]), jnp.array([8, 18, 16, 9, 19, 17])
    wanted = pick(enc_rows, dec_rows)[:, None] == jnp.arange(26)
    norm_sums = jnp.sum(jnp.where(wanted[:, :, None], rows_from[None], 0.0), axis=1)
    shards = 2**count
    sides = jnp.arange(2)
    held, outer = core ^ sides[:, None], sides[None, :]
    row_block = ((2 * outer + (1 ^ outer ^ held)) * shards)[:, :, None] + jnp.arange(shards)
    column_block = (2 * (y_at ^ sides)[:, None] + (x_at ^ sides)[None, :]).reshape(-1)
    order = (row_block.reshape(2, -1)[:, None, :] + 0) * 4 + column_block[:, None]
    norm_sums = jnp.take(norm_sums.reshape(6, 8 * 2 * shards, -1), order.reshape(-1), axis=1)
    norm_sums = norm_sums.reshape(6, 2, 4, 2 * shards, -1)
    with jax.named_scope("norm_sums"):
        norm_got = over(norm_sums[:, 1], "section")
        norm_sums = norm_sums[:, 0] + norm_got
    with jax.named_scope("self_sums"):
        self_plane = plane_summed(self_sum, until=(norm_got,))
    with jax.named_scope("norm_sums"):
        norm_blocks = after(norm_sums.transpose(1, 2, 0, 3).reshape(4, 2 * shards, -1), self_plane)
        norm_hops = [over(norm_blocks[1], "tx"), over(norm_blocks[2], "ty"), over(norm_blocks[3], "ty", "tx")]
        norm_plane = norm_blocks[0] + sum(norm_hops)
    norm_width = norm_plane.shape[1]
    with jax.named_scope("self_sums"):
        pad = ((0, 0), (0, 15), (0, self_plane.shape[1] - norm_width))
        both = jnp.concatenate(
            [
                self_plane.reshape(2 * shards, -1, self_plane.shape[1]),
                jnp.pad(low(norm_plane)[:, None], pad),
            ],
            axis=1,
        )
        raw_self = []
        share_self = rows_summed(both.reshape(-1, self_plane.shape[1]), count, raw=raw_self)
        share_self = swapped(share_self).astype(jnp.float32)
    norm_shares = share_self[-16, :norm_width].reshape(6, -1)
    share_self = share_self[:-16]
    with jax.named_scope("ffn_sums"):
        first_share = rows_summed(after(first_plane, *raw_later), count)
        share_ffn = swapped(jnp.concatenate([first_share, second_share], axis=1)).astype(jnp.float32)
    share_first, share_second = share_ffn[:, :units], share_ffn[:, units:].T
    with jax.named_scope("outputs"):
        outputs = jnp.concatenate([pick(encoded, decoded), low(pick(d_source, d_start))], axis=1)
        outputs = rows_out(after(outputs, *norm_hops))
    hidden_out = outputs[..., : hidden.shape[-1]]
    hidden_grad = outputs[..., hidden.shape[-1] :].astype(jnp.float32)
    g_query, g_key, g_value, g_out = unpack_heads(share_self)
    grad_qkv = jnp.stack([g_query, g_key, g_value], axis=1)
    c_query, c_key, c_value, c_out = unpack_heads(share_cross)
    with jax.named_scope("cross_out"):
        for_enc = cross_out(jnp.concatenate([c_key, c_value], axis=1), 0)
        for_dec = cross_out(jnp.concatenate([c_query, c_out], axis=1), 1)
    cross = jnp.where(core == 0, for_enc, for_dec).astype(jnp.float32)

    return (
        hidden_out,
        hidden_grad,
        grad_qkv[None],
        g_out[None],
        cross[None, :, :width],
        cross[None, :, width:],
        share_first[None],
        share_second[None],
        norm_shares[None, :3],
        norm_shares[None, 3:],
    )


def solution(mesh):
    _, dp_count, _ = mesh.devices.shape
    count = dp_count.bit_length() - 3
    names = axes_of(count)
    dp, tensor = names[1:-2], names[-2:]
    split = Mesh(mesh.devices.reshape((2,) * len(names)), names)
    rows = P("section", None, dp, tensor, None)
    in_specs = (
        rows,
        rows,
        P(None, None, dp, None),
        P("section", dp, None, tensor),
        P("section", dp, tensor),
        P("section", dp, tensor),
        P("section", dp, tensor),
        P("section", dp, tensor),
        P("section", tensor, dp),
        P("section", None, None),
        P("section", None, None),
    )
    out_specs = (
        rows,
        rows,
        P("section", dp, None, tensor),
        P("section", dp, tensor),
        P("section", dp, tensor),
        P("section", dp, tensor),
        P("section", dp, tensor),
        P("section", tensor, dp),
        P("section", None, dp + tensor),
        P("section", None, dp + tensor),
    )
    return jax.shard_map(
        functools.partial(body, count), mesh=split, in_specs=in_specs, out_specs=out_specs, check_vma=False
    )
```

```python
import functools

import jax
import jax.numpy as jnp
from jax import lax
from jax.experimental import pallas as pl
from jax.experimental.pallas import tpu as pltpu
from jax.sharding import Mesh
from jax.sharding import PartitionSpec as P

HDIM = 64
LANES = 128
MASKED = -1e30
NORM_EPS = 1e-05
VMEM_BYTES = 56 * 1024 * 1024

SEG_LANES = 8
PART_LANE = 12

PARTS = 2
TILE_ROWS = 256
HEADS = ((0, 1, 2, 0, 0), (0, 1, 2, 1, 1), (1, 3, 0, 0, 1))


def mul(a, b):
    return jnp.dot(a, b, preferred_element_type=jnp.float32)


def mul_nt(a, b):
    return lax.dot_general(a, b, (((1,), (1,)), ((), ())), preferred_element_type=jnp.float32)


def mul_tn(a, b):
    return lax.dot_general(a, b, (((0,), (0,)), ((), ())), preferred_element_type=jnp.float32)


def tile_of(values, index):
    return values[:, index * LANES : (index + 1) * LANES]


def lane_ids(rows):
    return lax.broadcasted_iota(jnp.int32, (rows, LANES), 1)


def half_mask(rows, half):
    lanes = lane_ids(rows)
    return lanes >= HDIM if half else lanes < HDIM


def in_parts(base, column):
    lanes = lane_ids(base.shape[0])
    high = column.astype(jnp.bfloat16).astype(jnp.float32)
    rest = column - high
    middle = rest.astype(jnp.bfloat16).astype(jnp.float32)
    low = rest - middle
    parts = jnp.where(
        lanes == PART_LANE,
        high,
        jnp.where(lanes == PART_LANE + 1, middle, jnp.where(lanes == PART_LANE + 2, low, base)),
    )
    return parts.astype(jnp.bfloat16)


def with_triangle(scores, tri, at):
    size = tri.shape[1]
    pieces = []
    if at > 0:
        pieces.append(scores[:, : at * size])
    pieces.append(scores[:, at * size : (at + 1) * size] + tri)
    pieces.append(scores[:, (at + 1) * size :])
    return jnp.concatenate(pieces, axis=1)


def places(core, block):
    return [pl.multiple_of((1 - core) * block, block), pl.multiple_of((2 + core) * block, block)]


def assemble(flag_ref, own_refs, peer_refs, w_ref):
    core, block = flag_ref[0], own_refs[0].shape[1] // 2
    for holder, refs in ((core, own_refs), (1 - core, peer_refs)):
        for part, ref in enumerate(refs):
            width = ref.shape[2]
            for at, place in enumerate(places(holder, block)):
                w_ref[pl.ds(place, block), part * width : (part + 1) * width] = ref[0, at * block : (at + 1) * block]


def hand_out(flag_ref, g_ref, keep_ref, send_ref):
    core, block = flag_ref[0], keep_ref.shape[1] // 2
    for holder, ref in ((core, keep_ref), (1 - core, send_ref)):
        for at, place in enumerate(places(holder, block)):
            ref[0, at * block : (at + 1) * block] = g_ref[pl.ds(place, block), :]


def where_active(kernel):
    def guarded(flag_ref, *refs):
        @pl.when(flag_ref[1] == 1)
        def _():
            kernel(flag_ref, *refs)

    return guarded


def scaled_queries(q_ref, at, q_tile, q_half):
    queries = q_ref[0, at, q_tile * LANES : (q_tile + 1) * LANES] * 0.125
    return jnp.where(half_mask(queries.shape[0], q_half), queries, 0).astype(jnp.bfloat16)


def units_of(total, rows):
    return [
        (slice(part * rows, (part + 1) * rows), part, head)
        for part in range(total // rows)
        for head in range(len(HEADS))
    ]


def attend_block(causal, xq_ref, xkv_ref, w_ref, qx_ref, kx_ref, tri_ref, q_ref, kv_ref, c_ref, l_ref):
    q_ref[0] = mul(xq_ref[...], w_ref[:, : 2 * LANES]).astype(jnp.bfloat16)
    kv_ref[0] = mul(xkv_ref[...], w_ref[:, LANES : 5 * LANES]).astype(jnp.bfloat16)
    rows = TILE_ROWS
    low = half_mask(rows, 0)

    def scores_of(at, part, head):
        q_tile, k_tile, _, q_half, _ = HEADS[head]
        keys = kv_ref[0, :, k_tile * LANES : (k_tile + 1) * LANES]
        scores = mul_nt(
            jnp.concatenate([scaled_queries(q_ref, at, q_tile, q_half), qx_ref[at, :]], axis=1),
            jnp.concatenate([keys, kx_ref[...]], axis=1),
        )
        return with_triangle(scores, tri_ref[...], part) if causal else scores

    units = units_of(q_ref.shape[1], rows)
    ahead = scores_of(*units[0])
    contexts, totals = [], None
    for index, (at, part, head) in enumerate(units):
        scores = ahead
        if index + 1 < len(units):
            ahead = scores_of(*units[index + 1])
        v_tile = HEADS[head][2]
        values = kv_ref[0, :, v_tile * LANES : (v_tile + 1) * LANES]
        highest = jnp.max(scores, axis=1, keepdims=True)
        weights = jnp.exp(scores - highest)
        sums = jnp.sum(weights, axis=1, keepdims=True)
        contexts.append(mul(weights.astype(jnp.bfloat16), values) / sums)
        logs = jnp.broadcast_to(highest + jnp.log(sums), (rows, LANES))
        totals = logs if head == 0 else jnp.where(lane_ids(rows) == head, logs, totals)
        if head == len(HEADS) - 1:
            c_ref[0, at, :LANES] = jnp.where(low, 0, contexts[2]).astype(jnp.bfloat16)
            c_ref[0, at, LANES:] = jnp.where(low, contexts[0], contexts[1]).astype(jnp.bfloat16)
            l_ref[0, at, :] = totals
            contexts = []
    return mul_nt(c_ref[0], w_ref[:, 4 * LANES :])


def attend_kernel(causal, flag_ref, xq_ref, xkv_ref, own_ref, peer_ref, qx_ref, kx_ref, tri_ref, o_ref, *refs):
    q_ref, kv_ref, c_ref, l_ref, w_ref = refs
    assemble(flag_ref, [own_ref], [peer_ref], w_ref)
    out = attend_block(causal, xq_ref, xkv_ref, w_ref, qx_ref, kx_ref, tri_ref, q_ref, kv_ref, c_ref, l_ref)
    add_up(pl.program_id(0) == 0, o_ref, out)


def add_up(first, ref, value):
    @pl.when(first)
    def _():
        ref[...] = value

    @pl.when(jnp.logical_not(first))
    def _():
        ref[...] += value


def attend_back_block(causal, do_ref, xq_ref, xkv_ref, w_ref, qx_ref, kx_ref, tri_ref, kept, work):
    q_ref, kv_ref, c_ref, l_ref = kept
    sum_ref, dq_ref, dkv_ref, g_ref = work
    rows = TILE_ROWS
    d_context = mul(do_ref[...], w_ref[:, 4 * LANES :]).astype(jnp.bfloat16)
    low = half_mask(rows, 0)

    def products_of(at, part, head):
        q_tile, k_tile, v_tile, q_half, v_half = HEADS[head]
        c_tile = 0 if head == 2 else 1
        keys = kv_ref[0, :, k_tile * LANES : (k_tile + 1) * LANES]
        values = kv_ref[0, :, v_tile * LANES : (v_tile + 1) * LANES]
        queries = scaled_queries(q_ref, at, q_tile, q_half)
        d_rows = jnp.where(half_mask(rows, v_half), tile_of(d_context[at], c_tile), 0).astype(jnp.bfloat16)
        total = l_ref[0, at, head : head + 1]
        scores = mul_nt(
            jnp.concatenate([queries, in_parts(qx_ref[at, :].astype(jnp.float32), -total)], axis=1),
            jnp.concatenate([keys, kx_ref[...]], axis=1),
        )
        if causal:
            scores = with_triangle(scores, tri_ref[...], part)
        return scores, mul_nt(d_rows, values), queries, d_rows, keys

    units = units_of(q_ref.shape[1], rows)
    ahead = products_of(*units[0])
    d_queries = []
    for index, (at, part, head) in enumerate(units):
        scores, d_probs, queries, d_rows, keys = ahead
        if index + 1 < len(units):
            ahead = products_of(*units[index + 1])
        _, k_tile, v_tile, _, _ = HEADS[head]
        probs = jnp.exp(scores)
        inner = jnp.sum(probs * d_probs, axis=1, keepdims=True)
        d_scores = (probs * (d_probs - inner)).astype(jnp.bfloat16)
        d_values = mul_tn(probs.astype(jnp.bfloat16), d_rows)
        d_keys = mul_tn(d_scores, queries)
        d_queries.append(mul(d_scores, keys) * 0.125)
        k_at = slice(k_tile * LANES, (k_tile + 1) * LANES)
        v_at = slice(v_tile * LANES, (v_tile + 1) * LANES)
        if part == 0 and head != 1:
            sum_ref[:, k_at] = d_keys
            sum_ref[:, v_at] = d_values
        else:
            sum_ref[:, k_at] += d_keys
            sum_ref[:, v_at] += d_values
        if head == len(HEADS) - 1:
            dq_ref[at, :LANES] = jnp.where(low, d_queries[0], d_queries[1]).astype(jnp.bfloat16)
            dq_ref[at, LANES:] = jnp.where(low, d_queries[2], 0).astype(jnp.bfloat16)
            d_queries = []
    dkv_ref[...] = sum_ref[...].astype(jnp.bfloat16)
    d_xq = mul_nt(dq_ref[...], w_ref[:, : 2 * LANES])
    d_xkv = mul_nt(dkv_ref[...], w_ref[:, LANES : 5 * LANES])

    grad_q = mul_tn(xq_ref[...], dq_ref[...])
    grad_kv = mul_tn(xkv_ref[...], dkv_ref[...])
    grad_o = mul_tn(do_ref[...], c_ref[0])
    g_ref[:, :LANES] = grad_q[:, :LANES].astype(jnp.bfloat16)
    g_ref[:, LANES : 2 * LANES] = (grad_q[:, LANES:] + grad_kv[:, :LANES]).astype(jnp.bfloat16)
    g_ref[:, 2 * LANES : 4 * LANES] = grad_kv[:, LANES : 3 * LANES].astype(jnp.bfloat16)
    g_ref[:, 4 * LANES : 5 * LANES] = (grad_kv[:, 3 * LANES :] + grad_o[:, :LANES]).astype(jnp.bfloat16)
    g_ref[:, 5 * LANES :] = grad_o[:, LANES:].astype(jnp.bfloat16)
    return d_xq, d_xkv


def attend_back_kernel(causal, flag_ref, do_ref, xq_ref, xkv_ref, own_ref, peer_ref, *refs):
    kept, (qx_ref, kx_ref, tri_ref, dxq_ref, dxkv_ref, keep_ref, send_ref, w_ref) = refs[:4], refs[4:12]
    work = refs[12:]
    assemble(flag_ref, [own_ref], [peer_ref], w_ref)
    d_xq, d_xkv = attend_back_block(
        causal, do_ref, xq_ref, xkv_ref, w_ref, qx_ref, kx_ref, tri_ref, kept, work
    )
    add_up(pl.program_id(0) == 0, dxq_ref, d_xq)
    add_up(pl.program_id(0) == 0, dxkv_ref, d_xkv)
    hand_out(flag_ref, work[3], keep_ref, send_ref)


def whole(shape):
    return pl.BlockSpec(shape, lambda j, flag: (0,) * len(shape))


def held(shape):
    return pl.BlockSpec(shape, lambda j, flag: (0,) * len(shape), pipeline_mode=pl.Buffered(1))


def per_block(shape, first=0, gate=1):
    return pl.BlockSpec((1,) + shape, lambda j, flag: (first + j * flag[gate],) + (0,) * len(shape))


shape = jax.ShapeDtypeStruct


def call(kernel, name, micros, moved, grid, in_specs, out_specs, out_shape, scratch, *operands):
    return pl.pallas_call(
        where_active(kernel),
        grid_spec=pltpu.PrefetchScalarGridSpec(
            num_scalar_prefetch=1,
            grid=(grid,),
            in_specs=in_specs,
            out_specs=out_specs,
            scratch_shapes=scratch,
        ),
        out_shape=out_shape,
        compiler_params=pltpu.CompilerParams(vmem_limit_bytes=VMEM_BYTES),
        cost_estimate=cost(micros, moved),
        name=name,
    )(*operands)


def cost(micros, moved):
    return pl.CostEstimate(flops=int(micros * 1.15e9), bytes_accessed=int(moved), transcendentals=0)


def attend(flag, xq, xkv, weights, extras, causal):
    rows, width = xq.shape
    keys = xkv.shape[0]
    blocks = weights[0].shape[0]
    return call(
        functools.partial(attend_kernel, causal),
        "attend_self" if causal else "attend_cross",
        20,
        24 * 2**20,
        blocks,
        [held((rows, width)), held((keys, width))]
        + [per_block(part.shape[1:]) for part in weights]
        + [held(extra.shape) for extra in extras],
        [
            whole((rows, width)),
            per_block((rows, 2 * LANES)),
            per_block((keys, 4 * LANES)),
            per_block((rows, 2 * LANES)),
            per_block((rows, LANES)),
        ],
        [
            shape((rows, width), jnp.float32),
            shape((blocks, rows, 2 * LANES), jnp.bfloat16),
            shape((blocks, keys, 4 * LANES), jnp.bfloat16),
            shape((blocks, rows, 2 * LANES), jnp.bfloat16),
            shape((blocks, rows, LANES), jnp.float32),
        ],
        [pltpu.VMEM((width, 6 * LANES), jnp.bfloat16)],
        flag,
        xq,
        xkv,
        *weights,
        *extras,
    )


def attend_back(flag, d_out, xq, xkv, weights, kept, extras, causal, first, count):
    rows, width = xq.shape
    keys = xkv.shape[0]
    return call(
        functools.partial(attend_back_kernel, causal),
        "attend_self_back" if causal else "attend_cross_back",
        10 * count,
        6 * 2**20 * count,
        count,
        [held((rows, width)), held((rows, width)), held((keys, width))]
        + [per_block(part.shape[1:], first) for part in weights]
        + [
            per_block((rows, 2 * LANES), first),
            per_block((keys, 4 * LANES), first),
            per_block((rows, 2 * LANES), first),
            per_block((rows, LANES), first),
        ]
        + [held(extra.shape) for extra in extras],
        [whole((rows, width)), whole((keys, width))] + [per_block(part.shape[1:]) for part in weights],
        [shape((rows, width), jnp.float32), shape((keys, width), jnp.float32)]
        + [shape((count,) + part.shape[1:], jnp.bfloat16) for part in weights],
        [
            pltpu.VMEM((width, 6 * LANES), jnp.bfloat16),
            pltpu.VMEM((keys, 4 * LANES), jnp.float32),
            pltpu.VMEM((rows, 2 * LANES), jnp.bfloat16),
            pltpu.VMEM((keys, 4 * LANES), jnp.bfloat16),
            pltpu.VMEM((width, 6 * LANES), jnp.bfloat16),
        ],
        flag,
        d_out,
        xq,
        xkv,
        *weights,
        *kept,
        *extras,
    )


def ffn_block(x_ref, w_ref, units, g_ref, slope_ref, first, out_ref):
    inner = mul(x_ref[...], w_ref[:, :units])
    spread = 0.5 * (1.0 + lax.erf(inner * (0.5**0.5)))
    bell = jnp.exp(-0.5 * inner * inner) * 0.3989422804014327
    active = (inner * spread).astype(jnp.bfloat16)
    g_ref[0] = active
    slope_ref[0] = (spread + inner * bell).astype(jnp.bfloat16)
    add_up(first, out_ref, mul_nt(active, w_ref[:, units:]))


def ffn_kernel(flag_ref, x_ref, *refs):
    own_refs, peer_refs = refs[:PARTS], refs[PARTS : 2 * PARTS]
    z_ref, g_ref, slope_ref, w_ref = refs[2 * PARTS :]
    assemble(flag_ref, own_refs, peer_refs, w_ref)
    ffn_block(x_ref, w_ref, own_refs[0].shape[2], g_ref, slope_ref, pl.program_id(0) == 0, z_ref)


def feed_blocks(feed, index):
    half, units = feed[0].shape[1], feed[0].shape[2] // 2
    return [
        pl.BlockSpec((1, half, units), lambda j, flag, side=side: (index(j, flag), 0, side))
        for _ in feed
        for side in (0, 1)
    ]


def feed_operands(feed):
    return [part for part in feed for _ in (0, 1)]


def ffn(flag, x, feed):
    rows, width = x.shape
    blocks, units = feed[0].shape[0], feed[0].shape[2] // 2
    return call(
        ffn_kernel,
        "ffn",
        12,
        rows * units * blocks * 16,
        blocks,
        [held((rows, width))] + feed_blocks(feed, lambda j, flag: j * flag[1]),
        [whole((rows, width)), per_block((rows, units)), per_block((rows, units))],
        [
            shape((rows, width), jnp.float32),
            shape((blocks, rows, units), jnp.bfloat16),
            shape((blocks, rows, units), jnp.bfloat16),
        ],
        [pltpu.VMEM((width, 2 * units), jnp.bfloat16)],
        flag,
        x,
        *feed_operands(feed),
    )


def ffn_back_block(dz_ref, w_ref, units, slope_ref, dh_ref, first, out_ref):
    d_active = mul(dz_ref[...], w_ref[:, units:])
    d_inner = (d_active * slope_ref[0].astype(jnp.float32)).astype(jnp.bfloat16)
    dh_ref[0] = d_inner
    add_up(first, out_ref, mul_nt(d_inner, w_ref[:, :units]))


def layer_norm(values, gain_row, bias_row):
    average = jnp.mean(values, axis=-1, keepdims=True)
    centered = values - average
    variance = jnp.mean(centered * centered, axis=-1, keepdims=True)
    return centered * lax.rsqrt(variance + NORM_EPS) * gain_row + bias_row


def norm_back(values, gain_row, bias_row, upstream):
    _, pullback = jax.vjp(layer_norm, values, gain_row, bias_row)
    return pullback(upstream)


def norm_parts(values):
    average = jnp.mean(values, axis=1, keepdims=True)
    centered = values - average
    scale = lax.rsqrt(jnp.mean(centered * centered, axis=1, keepdims=True) + NORM_EPS)
    return centered * scale, scale


def norm_gradients(values, gain_row, upstream):
    shaped, scale = norm_parts(values)
    inner = upstream * gain_row
    mean_inner = jnp.mean(inner, axis=1, keepdims=True)
    mean_product = jnp.mean(inner * shaped, axis=1, keepdims=True)
    d_values = scale * (inner - mean_inner - shaped * mean_product)
    d_gain = jnp.sum(upstream * shaped, axis=0, keepdims=True)
    return d_values, d_gain, jnp.sum(upstream, axis=0, keepdims=True)


def enc_out_back_kernel(
    flag_ref, arrived_ref, cot_ref, total_ref, norms_ref, d_dec_ref, enc_ref, dec_ref, *refs
):
    d_total_ref, dz_ref, sums_ref, keep_ref, send_ref, g_ref, left_t_ref = refs

    @pl.when(jnp.logical_and(pl.program_id(0) == 0, flag_ref[2] == 1))
    def _():
        upstream = arrived_ref[...].astype(jnp.float32) + cot_ref[...].astype(jnp.float32)
        d_total, sums_ref[0:1, :], sums_ref[1:2, :] = norm_gradients(total_ref[...], norms_ref[2:3, :], upstream)
        d_total_ref[...] = d_total
        dz_ref[...] = d_total.astype(jnp.bfloat16)

    @pl.when(jnp.logical_and(pl.program_id(0) == 0, flag_ref[2] == 0))
    def _():
        dz_ref[...] = d_dec_ref[...]

    @pl.when(pl.program_id(0) == 0)
    def _():
        left_t_ref[...] = dz_ref[...].T

    right = jnp.where(flag_ref[2] == 1, enc_ref[0], dec_ref[0])
    g_ref[...] = mul(left_t_ref[...], right).astype(jnp.bfloat16)
    hand_out(flag_ref, g_ref, keep_ref, send_ref)


def enc_out_back(flag, arrived, cot, total, norms, d_dec, enc_active, dec_active, feed):
    rows, width = cot.shape
    blocks, _, units = enc_active.shape
    like = shape((blocks, feed[0].shape[1], units), jnp.bfloat16)
    full = shape((rows, width), jnp.float32)
    return call(
        enc_out_back_kernel,
        "enc_out_back",
        9,
        rows * units * blocks * 8,
        blocks,
        [held(item.shape) for item in (arrived, cot, total, norms, d_dec)]
        + [per_block((rows, units), 0, 2), per_block((rows, units), 0, 3)],
        [whole((rows, width))] * 2 + [whole((8, width))] + [per_block(like.shape[1:])] * 2,
        [full, shape((rows, width), jnp.bfloat16), shape((8, width), jnp.float32)]
        + [like] * 2,
        [pltpu.VMEM((width, units), jnp.bfloat16), pltpu.VMEM((width, rows), jnp.bfloat16)],
        flag,
        arrived,
        cot,
        total,
        norms,
        d_dec,
        enc_active,
        dec_active,
    )


def enc_in_back_kernel(
    flag_ref, dz_ref, d_enc_ref, d_middle_ref, total_ref, gain_ref, middle_ref, crossed_ref, *refs
):
    first_own_ref, second_own_ref, first_peer_ref, second_peer_ref, slope_ref, dec_inner_ref, *refs = refs
    d_total_ref, d_low_ref, sums_ref, keep_ref, send_ref, w_ref, inner_ref, out_ref, g_ref, left_t_ref = refs
    step = pl.program_id(0)
    phase, at = step // 4, step % 4
    on_encoder = flag_ref[2] == 1

    @pl.when(jnp.logical_and(phase == 0, on_encoder))
    def _():
        assemble(flag_ref, [first_own_ref, second_own_ref], [first_peer_ref, second_peer_ref], w_ref)
        ffn_back_block(
            dz_ref, w_ref, first_own_ref.shape[2], slope_ref, inner_ref.at[pl.ds(at, 1)], at == 0, out_ref
        )

    @pl.when(step == 3)
    def _():
        upstream = jnp.where(on_encoder, d_enc_ref[...] + out_ref[...], d_middle_ref[...])
        d_total, sums_ref[0:1, :], sums_ref[1:2, :] = norm_gradients(total_ref[...], gain_ref[0:1, :], upstream)
        d_total_ref[...] = d_total
        d_low_ref[...] = d_total.astype(jnp.bfloat16)
        left_t_ref[...] = jnp.where(on_encoder, middle_ref[...], crossed_ref[...]).T

    @pl.when(phase == 1)
    def _():
        right = jnp.where(on_encoder, inner_ref[at], dec_inner_ref[0])
        g_ref[...] = mul(left_t_ref[...], right).astype(jnp.bfloat16)
        hand_out(flag_ref, g_ref, keep_ref, send_ref)


def enc_in_back(flag, dz, d_enc, d_middle, total, gain, middle, crossed, feed, slope, dec_inner):
    rows, width = dz.shape
    blocks, half, units = feed[0].shape[0], feed[0].shape[1], feed[0].shape[2] // 2
    full = shape((rows, width), jnp.float32)

    def at_step(of, low, high, gate):
        def index(j, flag):
            return (jnp.where(j < 4, j if low == "up" else low, j - 4 if high == "up" else high) * flag[gate],) + (
                0,
            ) * len(of)

        return pl.BlockSpec((1,) + of, index)

    return call(
        enc_in_back_kernel,
        "enc_in_back",
        19,
        rows * units * blocks * 20,
        8,
        [held(item.shape) for item in (dz, d_enc, d_middle, total, gain, middle, crossed)]
        + feed_blocks(feed, lambda j, flag: jnp.where(j < 4, j, 3) * flag[2])
        + [at_step((rows, units), "up", 3, 2), at_step((rows, units), 0, "up", 3)],
        [whole((rows, width))] * 2 + [whole((8, width))] + [at_step((half, units), 0, "up", 1)] * 2,
        [full, shape((rows, width), jnp.bfloat16), shape((8, width), jnp.float32)]
        + [shape((blocks, half, units), jnp.bfloat16)] * 2,
        [
            pltpu.VMEM((width, 2 * units), jnp.bfloat16),
            pltpu.VMEM((blocks, rows, units), jnp.bfloat16),
            pltpu.VMEM((rows, width), jnp.float32),
            pltpu.VMEM((width, units), jnp.bfloat16),
            pltpu.VMEM((width, rows), jnp.bfloat16),
        ],
        flag,
        dz,
        d_enc,
        d_middle,
        total,
        gain,
        middle,
        crossed,
        *feed_operands(feed),
        slope,
        dec_inner,
    )


def decoder_kernel(
    flag_ref,
    h1_ref,
    mem_a_ref,
    mem_b_ref,
    peer_a_ref,
    peer_b_ref,
    cot_ref,
    qx_ref,
    kx_ref,
    norms_ref,
    own_ref,
    peer_ref,
    first_own_ref,
    second_own_ref,
    first_peer_ref,
    second_peer_ref,
    decoded_ref,
    crossed_ref,
    d_dec_ref,
    d_middle_ref,
    mine_ref,
    other_ref,
    sums_ref,
    active_ref,
    inner_ref,
    keep_ref,
    send_ref,
    xq_ref,
    xkv_ref,
    wx_ref,
    wf_ref,
    q_ref,
    kv_ref,
    c_ref,
    l_ref,
    slope_ref,
    out_ref,
    total_ref,
    do_ref,
    dxkv_ref,
    *work,
):
    step = pl.program_id(0)
    phase, at = step // 4, step % 4
    first, last = at == 0, at == 3
    rows = h1_ref.shape[0]
    units = first_own_ref.shape[2]
    gain = [norms_ref[row : row + 1, :] for row in range(3)]
    bias = [norms_ref[3 + row : 4 + row, :] for row in range(3)]

    def kept(block):
        return tuple(ref.at[pl.ds(block, 1)] for ref in (q_ref, kv_ref, c_ref, l_ref))

    @pl.when(step == 0)
    def _():
        xq_ref[...] = h1_ref[...].astype(jnp.bfloat16)
        for part, ref in enumerate((mem_a_ref, mem_b_ref, peer_a_ref, peer_b_ref)):
            xkv_ref[part * rows // 2 : (part + 1) * rows // 2] = ref[...]

    @pl.when(jnp.logical_or(phase == 0, phase == 3))
    def _():
        assemble(flag_ref, [own_ref], [peer_ref], wx_ref)

    @pl.when(jnp.logical_or(phase == 1, phase == 2))
    def _():
        assemble(flag_ref, [first_own_ref, second_own_ref], [first_peer_ref, second_peer_ref], wf_ref)

    @pl.when(phase == 0)
    def _():
        add_up(first, out_ref, attend_block(False, xq_ref, xkv_ref, wx_ref, qx_ref, kx_ref, None, *kept(at)))

    @pl.when(jnp.logical_and(phase == 0, last))
    def _():
        total = h1_ref[...] + out_ref[...]
        total_ref[...] = total
        crossed = norm_parts(total)[0] * gain[1] + bias[1]
        mine_ref[...] = crossed
        crossed_ref[...] = crossed.astype(jnp.bfloat16)

    @pl.when(phase == 1)
    def _():
        ffn_block(crossed_ref, wf_ref, units, active_ref, slope_ref.at[pl.ds(at, 1)], first, out_ref)

    @pl.when(jnp.logical_and(phase == 1, last))
    def _():
        total = mine_ref[...] + out_ref[...]
        decoded_ref[...] = (norm_parts(total)[0] * gain[2] + bias[2]).astype(jnp.bfloat16)
        d_total, sums_ref[0:1, :], sums_ref[1:2, :] = norm_gradients(
            total, gain[2], cot_ref[...].astype(jnp.float32)
        )
        d_middle_ref[...] = d_total
        d_dec_ref[...] = d_total.astype(jnp.bfloat16)

    @pl.when(phase == 2)
    def _():
        ffn_back_block(d_dec_ref, wf_ref, units, slope_ref.at[pl.ds(3 - at, 1)], inner_ref, first, out_ref)

    @pl.when(jnp.logical_and(phase == 2, last))
    def _():
        d_total, sums_ref[2:3, :], sums_ref[3:4, :] = norm_gradients(
            total_ref[...], gain[1], d_middle_ref[...] + out_ref[...]
        )
        d_middle_ref[...] = d_total
        do_ref[...] = d_total.astype(jnp.bfloat16)

    @pl.when(phase == 3)
    def _():
        d_xq, d_xkv = attend_back_block(
            False, do_ref, xq_ref, xkv_ref, wx_ref, qx_ref, kx_ref, None, kept(3 - at), work
        )
        add_up(first, out_ref, d_xq)
        add_up(first, dxkv_ref, d_xkv)
        hand_out(flag_ref, work[3], keep_ref, send_ref)

    @pl.when(jnp.logical_and(phase == 3, last))
    def _():
        d_middle_ref[...] += out_ref[...]
        mine_ref[...] = dxkv_ref[:rows]
        other_ref[...] = dxkv_ref[rows:].astype(jnp.bfloat16)


def decoder(flag, h1, memory, cot, extras, norms, cross, feed):
    rows, width = h1.shape
    blocks, half, _ = cross[0].shape
    units = feed[0].shape[2] // 2
    keys = 2 * rows
    qx, kx = extras

    def at_step(of, in_phase):
        def index(j, flag):
            at = j % 4
            choice = [{"up": at, "down": 3 - at}.get(way, way) for way in in_phase]
            chosen = choice[3]
            for phase in (2, 1, 0):
                chosen = jnp.where(j // 4 == phase, choice[phase], chosen)
            return (chosen * flag[1],) + (0,) * len(of)

        return pl.BlockSpec((1,) + of, index)

    part = (half, cross[0].shape[2])
    full = shape((rows, width), jnp.float32)
    rounded = shape((rows, width), jnp.bfloat16)
    return call(
        decoder_kernel,
        "decoder",
        90,
        40 * 2**20,
        16,
        [held(item.shape) for item in (h1, *memory, cot, qx, kx, norms)]
        + [at_step(part, ("up", 3, 3, "down"))] * 2
        + feed_blocks(feed, lambda j, flag: at_step((half, units), (0, "up", "down", 0)).index_map(j, flag)[0]),
        [whole((rows, width))] * 6
        + [whole((8, width))]
        + [
            at_step((rows, units), (0, "up", 3, 3)),
            at_step((rows, units), (3, 3, "down", 0)),
            at_step(part, (3, 3, 3, "down")),
            at_step(part, (3, 3, 3, "down")),
        ],
        [rounded, rounded, rounded, full, full, rounded, shape((8, width), jnp.float32)]
        + [shape((blocks, rows, units), jnp.bfloat16)] * 2
        + [shape(cross[0].shape, jnp.bfloat16)] * 2,
        [
            pltpu.VMEM((rows, width), jnp.bfloat16),
            pltpu.VMEM((keys, width), jnp.bfloat16),
            pltpu.VMEM((width, 6 * LANES), jnp.bfloat16),
            pltpu.VMEM((width, 2 * units), jnp.bfloat16),
            pltpu.VMEM((blocks, rows, 2 * LANES), jnp.bfloat16),
            pltpu.VMEM((blocks, keys, 4 * LANES), jnp.bfloat16),
            pltpu.VMEM((blocks, rows, 2 * LANES), jnp.bfloat16),
            pltpu.VMEM((blocks, rows, LANES), jnp.float32),
            pltpu.VMEM((blocks, rows, units), jnp.bfloat16),
            pltpu.VMEM((rows, width), jnp.float32),
            pltpu.VMEM((rows, width), jnp.float32),
            pltpu.VMEM((rows, width), jnp.bfloat16),
            pltpu.VMEM((keys, width), jnp.float32),
            pltpu.VMEM((keys, 4 * LANES), jnp.float32),
            pltpu.VMEM((rows, 2 * LANES), jnp.bfloat16),
            pltpu.VMEM((keys, 4 * LANES), jnp.bfloat16),
            pltpu.VMEM((width, 6 * LANES), jnp.bfloat16),
        ],
        flag,
        h1,
        *memory,
        cot,
        qx,
        kx,
        norms,
        *cross,
        *feed_operands(feed),
    )


def low(values):
    return values.astype(jnp.bfloat16)


def axes_of(count):
    return ("section", "zh", "zl") + tuple("e%d" % at for at in range(count)) + ("ty", "tx")


def layer_of(place):
    return 1 ^ place["zh"] ^ place["zl"]


def moved(x, names, to):
    names = [name for name in axes_of(8) if name in names]

    def index(place):
        return sum(place[name] << (len(names) - 1 - at) for at, name in enumerate(names))

    pairs = []
    for source in range(2 ** len(names)):
        place = {name: source >> (len(names) - 1 - at) & 1 for at, name in enumerate(names)}
        target = to(place)
        if target is not None:
            pairs.append((source, index(target)))
    return lax.ppermute(x, tuple(names), pairs)


def over(x, *axes, layer=None):
    def to(place):
        if layer is not None and layer_of(place) != layer:
            return None
        return {**place, **{axis: 1 - place[axis] for axis in axes}}

    return moved(x, axes if layer is None else axes + Z, to)


Z = ("zh", "zl")


def swapped(x):
    def to(place):
        if place["section"] == layer_of(place):
            return place
        return {"section": 1 - place["section"], "zh": place["zh"], "zl": 1 - place["zl"]}

    return moved(x, ("section",) + Z, to)


def turned(x):
    return moved(x, ("section", "ty"), lambda place: {"section": place["ty"], "ty": place["section"]})


def sent_home(x, other):
    def to(place):
        return {
            "section": layer_of(place),
            "zh": place["zh"],
            "zl": 1 ^ place["zh"] ^ place["ty"],
            "ty": place["section"],
            "tx": place["tx"] ^ other,
        }

    return moved(x, ("section",) + Z + ("ty", "tx"), to)


def cross_in(x, layer):
    def to(place):
        if place["section"] != layer:
            return None
        return {"section": layer_of(place), "zh": place["zh"], "zl": place["zh"]}

    return moved(x, ("section",) + Z, to)


def cross_out(x, layer):
    def to(place):
        if layer_of(place) != 1:
            return None
        return {"section": layer, "zh": place["zh"], "zl": 1 ^ place["zh"] ^ place["section"]}

    return moved(x, ("section",) + Z, to)


def in_order(x, flag, axis):
    return jnp.where(flag == 1, jnp.flip(x, axis), x)


def pack_heads(query, key, value, out):
    pair = 2 * HDIM
    return jnp.concatenate(
        [
            query,
            value[:, pair:],
            key[:, :pair],
            value[:, :pair],
            key[:, pair:],
            out[:, pair:],
            out[:, :pair],
        ],
        axis=1,
    )


def unpack_heads(packed):
    part = [packed[:, at * HDIM : (at + 1) * HDIM] for at in range(12)]
    query = jnp.concatenate(part[0:3], axis=1)
    key = jnp.concatenate([part[4], part[5], part[8]], axis=1)
    value = jnp.concatenate([part[6], part[7], part[3]], axis=1)
    out = jnp.concatenate([part[10], part[11], part[9]], axis=1)
    return query, key, value, out


def after(x, *earlier):
    return lax.optimization_barrier((x,) + earlier)[0]


def plane_gathered(x, until=(), **only):
    parts = [x, over(x, "tx", **only), over(x, "ty", **only), over(x, "ty", "tx", **only)]
    return jnp.stack([after(part, *until) for part in parts])


def plane_summed(x, until=(), raw=None, **only):
    terms = [x[0], over(x[1], "tx", **only), over(x[2], "ty", **only), over(x[3], "ty", "tx", **only)]
    if raw is not None:
        raw.extend(terms[1:])
    terms = [after(term, *until) for term in terms]
    return low(sum(term.astype(jnp.float32) for term in terms))


def rows_gathered(x, count, until=(), raw=None, **only):
    for axes in [("e%d" % at,) for at in reversed(range(count))] + [Z]:
        got = over(x, *axes, **only)
        if raw is not None:
            raw.append(got)
        parts = [after(part, *until) for part in (x, got)]
        both = in_order(jnp.stack(parts, axis=-3), lax.axis_index(axes[0]), x.ndim - 2)
        x = both.reshape(x.shape[:-2] + (2 * x.shape[-2], x.shape[-1]))
    return x


def rows_summed(x, count, until=(), raw=None, **only):
    for axes in [Z] + [("e%d" % at,) for at in range(count)]:
        halves = x.reshape(x.shape[:-2] + (2, x.shape[-2] // 2, x.shape[-1]))
        halves = in_order(halves, lax.axis_index(axes[0]), x.ndim - 2)
        got = over(halves[..., 1, :, :], *axes, **only)
        if raw is not None:
            raw.append(got)
        x = plus(halves[..., 0, :, :], after(got, *until))
    return x


def plus(first, second):
    return low(first.astype(jnp.float32) + second.astype(jnp.float32))


def from_cores(keep, send, raw=None, **only):
    got = over(send, "section", **only)
    if raw is not None:
        raw.append(got)
    return plus(keep, got)


def body(
    count,
    hidden,
    cotangent,
    segments,
    sa_qkv,
    sa_out,
    cross_one,
    cross_two,
    ffn_in,
    ffn_out,
    norm_gain,
    norm_bias,
):
    core = lax.axis_index("section")
    x_at, y_at, zh_at, zl_at = (lax.axis_index(name) for name in ("tx", "ty", "zh", "zl"))
    layer = 1 ^ zh_at ^ zl_at
    on_encoder = layer == 0
    quarter = hidden.shape[3]
    enc_flag = jnp.stack([core, 1 - layer, 1 - layer, layer])
    dec_flag = jnp.stack([core, layer, 1 - layer, layer])
    flag = jnp.stack([core, jnp.ones_like(core), 1 - layer, layer])

    def pick(first, second):
        return jnp.where(on_encoder, first, second)

    def of_one_row(x):
        both = in_order(x[0, :, 0], x_at, 0)
        return in_order(jnp.stack([both[0], over(both[1], "tx")]), x_at, 0).reshape(2 * quarter, -1)

    def rows_out(x, raw=None):
        mine, other = in_order(x.reshape(2, quarter, -1), x_at, 0)
        both = [sent_home(mine, 0), sent_home(other, 1)]
        if raw is not None:
            raw.extend(both)
        return in_order(jnp.stack(both), x_at, 0)[None, :, None]

    units = ffn_in.shape[2]
    width = cross_one.shape[2]
    packed_self = pack_heads(sa_qkv[0, :, 0], sa_qkv[0, :, 1], sa_qkv[0, :, 2], sa_out[0])
    packed_ffn = jnp.concatenate([ffn_in[0], ffn_out[0].T], axis=1)
    with jax.named_scope("norms_in"):
        norms = swapped(jnp.concatenate([norm_gain[0], norm_bias[0]], axis=0))
        gains, biases = norms[:3], norms[3:]
        seg_own = segments[:, :, 0].astype(jnp.float32)
        seg_here = jnp.where(zl_at == 1 ^ zh_at ^ y_at, seg_own, over(seg_own, "zl")).astype(jnp.int32)
    with jax.named_scope("hidden_in"):
        one_row = of_one_row(jnp.concatenate([hidden, cotangent], axis=-1))
    with jax.named_scope("self_weights"):
        shard_self = swapped(packed_self)
    with jax.named_scope("hidden_in"):
        one_row = swapped(after(one_row, shard_self))
    with jax.named_scope("ffn_weights"):
        shard_ffn = swapped(after(packed_ffn, one_row))

    def both_rows(x):
        for_enc = rows_gathered(x, count, layer=0)
        return pick(for_enc, rows_gathered(after(x, for_enc), count, layer=1))

    with jax.named_scope("self_weights"):
        rows_self = both_rows(shard_self)
        raw_ffn_rows = []
        rows_ffn_enc = rows_gathered(after(shard_ffn, rows_self), count, raw=raw_ffn_rows, layer=0)
        own_self = plane_gathered(rows_self, until=tuple(raw_ffn_rows))
        w_self = [own_self, over(own_self, "section")]
    with jax.named_scope("hidden_in"):
        rows_here = turned(one_row)
        rows_here, cot = rows_here[:, : hidden.shape[-1]], rows_here[:, hidden.shape[-1] :]
        rows_all = jnp.concatenate([rows_here, over(rows_here, "section")], axis=0)
    with jax.named_scope("ffn_weights"):
        rows_ffn = pick(rows_ffn_enc, rows_gathered(after(shard_ffn, *raw_ffn_rows), count, layer=1))

    both_segments = in_order(seg_here, x_at, 1)[:, 0]
    ordered = in_order(both_segments.reshape(2, 2, 2 * quarter), core, 1).reshape(2, 4 * quarter)
    source_seg, target_seg = ordered[0], ordered[1]
    self_seg = pick(source_seg, target_seg)
    parts = jnp.arange(4)
    quarter_of = jnp.repeat(2 * ((parts // 2) ^ core) + parts % 2, quarter)
    lanes = jnp.arange(LANES)[None, :]

    def key_extras(seg):
        differs = jnp.logical_and(lanes < SEG_LANES, seg[:, None] != lanes)
        later = jnp.logical_and(
            jnp.logical_and(lanes >= SEG_LANES, lanes < PART_LANE),
            quarter_of[:, None] > lanes - SEG_LANES,
        )
        part = jnp.logical_and(lanes >= PART_LANE, lanes < PART_LANE + 3)
        return jnp.where(differs | later | part, 1.0, 0.0).astype(jnp.bfloat16)

    def query_extras(seg, causal):
        seg, at = seg[: 2 * quarter], quarter_of[: 2 * quarter]
        same = seg[:, None] == lanes
        here = jnp.logical_and(at[:, None] + SEG_LANES == lanes, causal)
        return jnp.where(same | here, MASKED, 0.0).astype(jnp.bfloat16)

    at_row = jnp.arange(quarter)
    later_key = jnp.logical_and(at_row[None, :] > at_row[:, None], jnp.logical_not(on_encoder))
    tri = jnp.where(later_key, MASKED, 0.0).astype(jnp.float32)
    self_extras = (query_extras(self_seg, jnp.logical_not(on_encoder)), key_extras(self_seg), tri)
    cross_extras = (query_extras(target_seg, False), key_extras(source_seg), tri)

    start = rows_all.astype(jnp.float32)
    start = pick(layer_norm(start, gains[0], biases[0]), start)
    start_here = start[: 2 * quarter]
    start_low = low(start)
    self_gain, self_bias = pick(gains[1], gains[0]), pick(biases[1], biases[0])
    self_out, *kept_self = attend(
        flag, start_low[: 2 * quarter], start_low, w_self, self_extras, True
    )
    raw_cross_rows = []
    with jax.named_scope("cross_weights"):
        cross_low = after(jnp.concatenate([cross_one[0], cross_two[0]], axis=1), self_out)
        pair_kv, pair_qo = cross_in(cross_low, 0), cross_in(cross_low, 1)
        packed = pack_heads(pair_qo[:, :width], pair_kv[:, :width], pair_kv[:, width:], pair_qo[:, width:])
        rows_cross = rows_gathered(packed, count, raw=raw_cross_rows, layer=1)
    with jax.named_scope("ffn_weights"):
        own_ffn = plane_gathered(after(rows_ffn, own_self), until=(self_out, pair_kv, pair_qo))
        feed = [own_ffn, over(after(own_ffn, *raw_cross_rows), "section")]
    self_total = start_here + self_out
    middle = layer_norm(self_total, self_gain, self_bias)
    middle_low = low(middle)

    enc_out, enc_active, enc_slope = ffn(enc_flag, middle_low, feed)
    enc_total = middle + enc_out
    encoded = low(layer_norm(enc_total, gains[2], biases[2]))
    def across(x, layer):
        return moved(x, Z, lambda place: {**place, "zl": 1 - place["zl"]} if layer_of(place) == layer else None)

    with jax.named_scope("memory"):
        memory_here = [across(encoded[:quarter], 0), across(encoded[quarter:], 0)]
        memory_peer = [over(part, "section", layer=1) for part in memory_here]
    with jax.named_scope("cross_weights"):
        own_cross = plane_gathered(after(rows_cross, feed[1]), until=tuple(memory_here), layer=1)
        w_cross = [own_cross, over(own_cross, "section", layer=1)]
    (
        decoded,
        crossed_low,
        d_dec_low,
        d_middle_dec,
        d_memory_here,
        d_memory_other,
        dec_sums,
        dec_active,
        dec_inner,
        cross_keep,
        cross_send,
    ) = decoder(
        dec_flag, middle, memory_here + memory_peer, cot, cross_extras[:2], norms, w_cross, feed
    )
    with jax.named_scope("d_memory"):
        d_memory_here = d_memory_here + over(d_memory_other, "section", layer=1).astype(jnp.float32)
        d_memory_low = low(d_memory_here)
        arrived = across(d_memory_low, 1)
    with jax.named_scope("cross_sums"):
        cross_sum = from_cores(after(cross_keep, arrived), after(cross_send, arrived), layer=1)
        raw_cross = []
        cross_plane = plane_summed(cross_sum, raw=raw_cross, layer=1)

    d_enc_total, dz_low, enc_sums, second_keep, second_send = enc_out_back(
        flag, arrived, cot, enc_total, norms, d_dec_low, enc_active, dec_active, feed
    )
    with jax.named_scope("ffn_sums"):
        raw_second_sum = []
        second_sum = from_cores(second_keep, second_send, raw=raw_second_sum)
    gain_row = jnp.broadcast_to(self_gain, (8, self_gain.shape[0]))
    d_self_total, d_self_low, self_norm, first_keep, first_send = enc_in_back(
        flag,
        after(dz_low, second_keep, cross_sum),
        d_enc_total,
        d_middle_dec,
        self_total,
        gain_row,
        middle_low,
        crossed_low,
        feed,
        enc_slope,
        dec_inner,
    )
    with jax.named_scope("ffn_sums"):
        gate = []
        second_plane = plane_summed(after(second_sum, d_self_low), raw=gate)
        first_sum = from_cores(after(first_keep, *raw_cross), after(first_send, *raw_cross), raw=gate)

    halves = []
    for first, earlier in ((0, ()), (2, gate)):
        halves.append(
            attend_back(
                flag,
                after(d_self_low, *earlier),
                start_low[: 2 * quarter],
                start_low,
                w_self,
                kept_self,
                self_extras,
                True,
                first,
                2,
            )
        )
    d_start_q = halves[0][0] + halves[1][0]
    with jax.named_scope("cross_sums"):
        share_cross = rows_summed(after(cross_plane, d_start_q), count, layer=1)
    with jax.named_scope("ffn_sums"):
        gate_later = []
        first_plane = plane_summed(after(first_sum, second_plane), raw=gate_later)
        second_share = rows_summed(second_plane, count, raw=gate_later)
    with jax.named_scope("self_sums"):
        (_, _, keep, send), (_, _, *later) = halves
        self_sum = [from_cores(after(keep, *gate), after(send, *gate), raw=gate_later)]
        raw_later = []
        self_sum.append(from_cores(*(after(part, *gate_later) for part in later), raw=raw_later))
        self_sum = jnp.concatenate(self_sum, axis=0)
    with jax.named_scope("d_start"):
        d_start_kv = after(halves[0][1], *raw_later) + halves[1][1]
        d_start = d_self_total + d_start_q + d_start_kv[: 2 * quarter]
        d_start = d_start + over(low(d_start_kv[2 * quarter :]), "section").astype(jnp.float32)
    d_source, gain_a, bias_a = norm_back(
        rows_here.astype(jnp.float32), gains[0], biases[0], d_start
    )

    rows_from = jnp.concatenate([enc_sums, self_norm, dec_sums, jnp.stack([gain_a, bias_a])], axis=0)
    enc_rows, dec_rows = jnp.array([24, 8, 0, 25, 9, 1]), jnp.array([8, 18, 16, 9, 19, 17])
    wanted = pick(enc_rows, dec_rows)[:, None] == jnp.arange(26)
    norm_sums = jnp.sum(jnp.where(wanted[:, :, None], rows_from[None], 0.0), axis=1)
    shards = 2**count
    sides = jnp.arange(2)
    held, outer = core ^ sides[:, None], sides[None, :]
    row_block = ((2 * outer + (1 ^ outer ^ held)) * shards)[:, :, None] + jnp.arange(shards)
    column_block = (2 * (y_at ^ sides)[:, None] + (x_at ^ sides)[None, :]).reshape(-1)
    order = (row_block.reshape(2, -1)[:, None, :] + 0) * 4 + column_block[:, None]
    norm_sums = jnp.take(norm_sums.reshape(6, 8 * 2 * shards, -1), order.reshape(-1), axis=1)
    norm_sums = norm_sums.reshape(6, 2, 4, 2 * shards, -1)
    with jax.named_scope("norm_sums"):
        norm_got = over(norm_sums[:, 1], "section")
        norm_sums = norm_sums[:, 0] + norm_got
    with jax.named_scope("self_sums"):
        self_plane = plane_summed(self_sum, until=(norm_got,))
    with jax.named_scope("norm_sums"):
        norm_blocks = after(norm_sums.transpose(1, 2, 0, 3).reshape(4, 2 * shards, -1), self_plane)
        norm_hops = [over(norm_blocks[1], "tx"), over(norm_blocks[2], "ty"), over(norm_blocks[3], "ty", "tx")]
        norm_plane = norm_blocks[0] + sum(norm_hops)
    norm_width = norm_plane.shape[1]
    with jax.named_scope("self_sums"):
        pad = ((0, 0), (0, 15), (0, self_plane.shape[1] - norm_width))
        both = jnp.concatenate(
            [
                self_plane.reshape(2 * shards, -1, self_plane.shape[1]),
                jnp.pad(low(norm_plane)[:, None], pad),
            ],
            axis=1,
        )
        raw_self = []
        share_self = rows_summed(both.reshape(-1, self_plane.shape[1]), count, raw=raw_self)
        share_self = swapped(share_self).astype(jnp.float32)
    norm_shares = share_self[-16, :norm_width].reshape(6, -1)
    share_self = share_self[:-16]
    with jax.named_scope("ffn_sums"):
        first_share = rows_summed(after(first_plane, *raw_later), count)
        share_ffn = swapped(jnp.concatenate([first_share, second_share], axis=1)).astype(jnp.float32)
    share_first, share_second = share_ffn[:, :units], share_ffn[:, units:].T
    g_query, g_key, g_value, g_out = unpack_heads(share_self)
    grad_qkv = jnp.stack([g_query, g_key, g_value], axis=1)
    c_query, c_key, c_value, c_out = unpack_heads(share_cross)
    with jax.named_scope("cross_out"):
        for_enc = cross_out(jnp.concatenate([c_key, c_value], axis=1), 0)
        for_dec = cross_out(jnp.concatenate([c_query, c_out], axis=1), 1)
    with jax.named_scope("outputs"):
        outputs = jnp.concatenate([pick(encoded, decoded), low(pick(d_source, d_start))], axis=1)
        outputs = rows_out(after(outputs, *norm_hops, for_enc, for_dec))
    hidden_out = outputs[..., : hidden.shape[-1]]
    hidden_grad = outputs[..., hidden.shape[-1] :].astype(jnp.float32)
    cross = jnp.where(core == 0, for_enc, for_dec).astype(jnp.float32)

    return (
        hidden_out,
        hidden_grad,
        grad_qkv[None],
        g_out[None],
        cross[None, :, :width],
        cross[None, :, width:],
        share_first[None],
        share_second[None],
        norm_shares[None, :3],
        norm_shares[None, 3:],
    )


def solution(mesh):
    _, dp_count, _ = mesh.devices.shape
    count = dp_count.bit_length() - 3
    names = axes_of(count)
    dp, tensor = names[1:-2], names[-2:]
    split = Mesh(mesh.devices.reshape((2,) * len(names)), names)
    rows = P("section", None, dp, tensor, None)
    in_specs = (
        rows,
        rows,
        P(None, None, dp, None),
        P("section", dp, None, tensor),
        P("section", dp, tensor),
        P("section", dp, tensor),
        P("section", dp, tensor),
        P("section", dp, tensor),
        P("section", tensor, dp),
        P("section", None, None),
        P("section", None, None),
    )
    out_specs = (
        rows,
        rows,
        P("section", dp, None, tensor),
        P("section", dp, tensor),
        P("section", dp, tensor),
        P("section", dp, tensor),
        P("section", dp, tensor),
        P("section", tensor, dp),
        P("section", None, dp + tensor),
        P("section", None, dp + tensor),
    )
    return jax.shard_map(
        functools.partial(body, count), mesh=split, in_specs=in_specs, out_specs=out_specs, check_vma=False
    )
```

```python
import functools

import jax
import jax.numpy as jnp
from jax import lax
from jax.experimental import pallas as pl
from jax.experimental.pallas import tpu as pltpu
from jax.sharding import Mesh
from jax.sharding import PartitionSpec as P

HDIM = 64
LANES = 128
MASKED = -1e30
NORM_EPS = 1e-05
VMEM_BYTES = 56 * 1024 * 1024

SEG_LANES = 8
PART_LANE = 12

PARTS = 2
TILE_ROWS = 256
HEADS = ((0, 1, 2, 0, 0), (0, 1, 2, 1, 1), (1, 3, 0, 0, 1))


def mul(a, b):
    return jnp.dot(a, b, preferred_element_type=jnp.float32)


def mul_nt(a, b):
    return lax.dot_general(a, b, (((1,), (1,)), ((), ())), preferred_element_type=jnp.float32)


def mul_tn(a, b):
    return lax.dot_general(a, b, (((0,), (0,)), ((), ())), preferred_element_type=jnp.float32)


def tile_of(values, index):
    return values[:, index * LANES : (index + 1) * LANES]


def lane_ids(rows):
    return lax.broadcasted_iota(jnp.int32, (rows, LANES), 1)


def half_mask(rows, half):
    lanes = lane_ids(rows)
    return lanes >= HDIM if half else lanes < HDIM


def in_parts(base, column):
    lanes = lane_ids(base.shape[0])
    high = column.astype(jnp.bfloat16).astype(jnp.float32)
    rest = column - high
    middle = rest.astype(jnp.bfloat16).astype(jnp.float32)
    low = rest - middle
    parts = jnp.where(
        lanes == PART_LANE,
        high,
        jnp.where(lanes == PART_LANE + 1, middle, jnp.where(lanes == PART_LANE + 2, low, base)),
    )
    return parts.astype(jnp.bfloat16)


def with_triangle(scores, tri, at):
    size = tri.shape[1]
    pieces = []
    if at > 0:
        pieces.append(scores[:, : at * size])
    pieces.append(scores[:, at * size : (at + 1) * size] + tri)
    pieces.append(scores[:, (at + 1) * size :])
    return jnp.concatenate(pieces, axis=1)


def places(core, block):
    return [pl.multiple_of((1 - core) * block, block), pl.multiple_of((2 + core) * block, block)]


def assemble(flag_ref, own_refs, peer_refs, w_ref):
    core, block = flag_ref[0], own_refs[0].shape[1] // 2
    for holder, refs in ((core, own_refs), (1 - core, peer_refs)):
        for part, ref in enumerate(refs):
            width = ref.shape[2]
            for at, place in enumerate(places(holder, block)):
                w_ref[pl.ds(place, block), part * width : (part + 1) * width] = ref[0, at * block : (at + 1) * block]


def hand_out(flag_ref, g_ref, keep_ref, send_ref):
    core, block = flag_ref[0], keep_ref.shape[1] // 2
    for holder, ref in ((core, keep_ref), (1 - core, send_ref)):
        for at, place in enumerate(places(holder, block)):
            ref[0, at * block : (at + 1) * block] = g_ref[pl.ds(place, block), :]


def where_active(kernel):
    def guarded(flag_ref, *refs):
        @pl.when(flag_ref[1] == 1)
        def _():
            kernel(flag_ref, *refs)

    return guarded


def scaled_queries(q_ref, at, q_tile, q_half):
    queries = q_ref[0, at, q_tile * LANES : (q_tile + 1) * LANES] * 0.125
    return jnp.where(half_mask(queries.shape[0], q_half), queries, 0).astype(jnp.bfloat16)


def units_of(total, rows):
    return [
        (slice(part * rows, (part + 1) * rows), part, head)
        for part in range(total // rows)
        for head in range(len(HEADS))
    ]


def attend_block(causal, xq_ref, xkv_ref, w_ref, qx_ref, kx_ref, tri_ref, q_ref, kv_ref, c_ref, l_ref):
    q_ref[0] = mul(xq_ref[...], w_ref[:, : 2 * LANES]).astype(jnp.bfloat16)
    kv_ref[0] = mul(xkv_ref[...], w_ref[:, LANES : 5 * LANES]).astype(jnp.bfloat16)
    rows = TILE_ROWS
    low = half_mask(rows, 0)

    def scores_of(at, part, head):
        q_tile, k_tile, _, q_half, _ = HEADS[head]
        keys = kv_ref[0, :, k_tile * LANES : (k_tile + 1) * LANES]
        scores = mul_nt(
            jnp.concatenate([scaled_queries(q_ref, at, q_tile, q_half), qx_ref[at, :]], axis=1),
            jnp.concatenate([keys, kx_ref[...]], axis=1),
        )
        return with_triangle(scores, tri_ref[...], part) if causal else scores

    units = units_of(q_ref.shape[1], rows)
    ahead = scores_of(*units[0])
    contexts, totals = [], None
    for index, (at, part, head) in enumerate(units):
        scores = ahead
        if index + 1 < len(units):
            ahead = scores_of(*units[index + 1])
        v_tile = HEADS[head][2]
        values = kv_ref[0, :, v_tile * LANES : (v_tile + 1) * LANES]
        highest = jnp.max(scores, axis=1, keepdims=True)
        weights = jnp.exp(scores - highest)
        sums = jnp.sum(weights, axis=1, keepdims=True)
        contexts.append(mul(weights.astype(jnp.bfloat16), values) / sums)
        logs = jnp.broadcast_to(highest + jnp.log(sums), (rows, LANES))
        totals = logs if head == 0 else jnp.where(lane_ids(rows) == head, logs, totals)
        if head == len(HEADS) - 1:
            c_ref[0, at, :LANES] = jnp.where(low, 0, contexts[2]).astype(jnp.bfloat16)
            c_ref[0, at, LANES:] = jnp.where(low, contexts[0], contexts[1]).astype(jnp.bfloat16)
            l_ref[0, at, :] = totals
            contexts = []
    return mul_nt(c_ref[0], w_ref[:, 4 * LANES :])


def attend_kernel(causal, flag_ref, xq_ref, xkv_ref, own_ref, peer_ref, qx_ref, kx_ref, tri_ref, o_ref, *refs):
    q_ref, kv_ref, c_ref, l_ref, w_ref = refs
    assemble(flag_ref, [own_ref], [peer_ref], w_ref)
    out = attend_block(causal, xq_ref, xkv_ref, w_ref, qx_ref, kx_ref, tri_ref, q_ref, kv_ref, c_ref, l_ref)
    add_up(pl.program_id(0) == 0, o_ref, out)


def add_up(first, ref, value):
    @pl.when(first)
    def _():
        ref[...] = value

    @pl.when(jnp.logical_not(first))
    def _():
        ref[...] += value


def attend_back_block(causal, do_ref, xq_ref, xkv_ref, w_ref, qx_ref, kx_ref, tri_ref, kept, work):
    q_ref, kv_ref, c_ref, l_ref = kept
    sum_ref, dq_ref, dkv_ref, g_ref = work
    rows = TILE_ROWS
    d_context = mul(do_ref[...], w_ref[:, 4 * LANES :]).astype(jnp.bfloat16)
    low = half_mask(rows, 0)

    def products_of(at, part, head):
        q_tile, k_tile, v_tile, q_half, v_half = HEADS[head]
        c_tile = 0 if head == 2 else 1
        keys = kv_ref[0, :, k_tile * LANES : (k_tile + 1) * LANES]
        values = kv_ref[0, :, v_tile * LANES : (v_tile + 1) * LANES]
        queries = scaled_queries(q_ref, at, q_tile, q_half)
        d_rows = jnp.where(half_mask(rows, v_half), tile_of(d_context[at], c_tile), 0).astype(jnp.bfloat16)
        total = l_ref[0, at, head : head + 1]
        scores = mul_nt(
            jnp.concatenate([queries, in_parts(qx_ref[at, :].astype(jnp.float32), -total)], axis=1),
            jnp.concatenate([keys, kx_ref[...]], axis=1),
        )
        if causal:
            scores = with_triangle(scores, tri_ref[...], part)
        return scores, mul_nt(d_rows, values), queries, d_rows, keys

    units = units_of(q_ref.shape[1], rows)
    ahead = products_of(*units[0])
    d_queries = []
    for index, (at, part, head) in enumerate(units):
        scores, d_probs, queries, d_rows, keys = ahead
        if index + 1 < len(units):
            ahead = products_of(*units[index + 1])
        _, k_tile, v_tile, _, _ = HEADS[head]
        probs = jnp.exp(scores)
        inner = jnp.sum(probs * d_probs, axis=1, keepdims=True)
        d_scores = (probs * (d_probs - inner)).astype(jnp.bfloat16)
        d_values = mul_tn(probs.astype(jnp.bfloat16), d_rows)
        d_keys = mul_tn(d_scores, queries)
        d_queries.append(mul(d_scores, keys) * 0.125)
        k_at = slice(k_tile * LANES, (k_tile + 1) * LANES)
        v_at = slice(v_tile * LANES, (v_tile + 1) * LANES)
        if part == 0 and head != 1:
            sum_ref[:, k_at] = d_keys
            sum_ref[:, v_at] = d_values
        else:
            sum_ref[:, k_at] += d_keys
            sum_ref[:, v_at] += d_values
        if head == len(HEADS) - 1:
            dq_ref[at, :LANES] = jnp.where(low, d_queries[0], d_queries[1]).astype(jnp.bfloat16)
            dq_ref[at, LANES:] = jnp.where(low, d_queries[2], 0).astype(jnp.bfloat16)
            d_queries = []
    dkv_ref[...] = sum_ref[...].astype(jnp.bfloat16)
    d_xq = mul_nt(dq_ref[...], w_ref[:, : 2 * LANES])
    d_xkv = mul_nt(dkv_ref[...], w_ref[:, LANES : 5 * LANES])

    grad_q = mul_tn(xq_ref[...], dq_ref[...])
    grad_kv = mul_tn(xkv_ref[...], dkv_ref[...])
    grad_o = mul_tn(do_ref[...], c_ref[0])
    g_ref[:, :LANES] = grad_q[:, :LANES].astype(jnp.bfloat16)
    g_ref[:, LANES : 2 * LANES] = (grad_q[:, LANES:] + grad_kv[:, :LANES]).astype(jnp.bfloat16)
    g_ref[:, 2 * LANES : 4 * LANES] = grad_kv[:, LANES : 3 * LANES].astype(jnp.bfloat16)
    g_ref[:, 4 * LANES : 5 * LANES] = (grad_kv[:, 3 * LANES :] + grad_o[:, :LANES]).astype(jnp.bfloat16)
    g_ref[:, 5 * LANES :] = grad_o[:, LANES:].astype(jnp.bfloat16)
    return d_xq, d_xkv


def attend_back_kernel(causal, flag_ref, do_ref, xq_ref, xkv_ref, own_ref, peer_ref, *refs):
    kept, (qx_ref, kx_ref, tri_ref, dxq_ref, dxkv_ref, keep_ref, send_ref, w_ref) = refs[:4], refs[4:12]
    work = refs[12:]
    assemble(flag_ref, [own_ref], [peer_ref], w_ref)
    d_xq, d_xkv = attend_back_block(
        causal, do_ref, xq_ref, xkv_ref, w_ref, qx_ref, kx_ref, tri_ref, kept, work
    )
    add_up(pl.program_id(0) == 0, dxq_ref, d_xq)
    add_up(pl.program_id(0) == 0, dxkv_ref, d_xkv)
    hand_out(flag_ref, work[3], keep_ref, send_ref)


def whole(shape):
    return pl.BlockSpec(shape, lambda j, flag: (0,) * len(shape))


def held(shape):
    return pl.BlockSpec(shape, lambda j, flag: (0,) * len(shape), pipeline_mode=pl.Buffered(1))


def per_block(shape, first=0, gate=1):
    return pl.BlockSpec((1,) + shape, lambda j, flag: (first + j * flag[gate],) + (0,) * len(shape))


shape = jax.ShapeDtypeStruct


def call(kernel, name, micros, moved, grid, in_specs, out_specs, out_shape, scratch, *operands):
    return pl.pallas_call(
        where_active(kernel),
        grid_spec=pltpu.PrefetchScalarGridSpec(
            num_scalar_prefetch=1,
            grid=(grid,),
            in_specs=in_specs,
            out_specs=out_specs,
            scratch_shapes=scratch,
        ),
        out_shape=out_shape,
        compiler_params=pltpu.CompilerParams(vmem_limit_bytes=VMEM_BYTES),
        cost_estimate=cost(micros, moved),
        name=name,
    )(*operands)


def cost(micros, moved):
    return pl.CostEstimate(flops=int(micros * 1.15e9), bytes_accessed=int(moved), transcendentals=0)


def attend(flag, xq, xkv, weights, extras, causal):
    rows, width = xq.shape
    keys = xkv.shape[0]
    blocks = weights[0].shape[0]
    return call(
        functools.partial(attend_kernel, causal),
        "attend_self" if causal else "attend_cross",
        20,
        24 * 2**20,
        blocks,
        [held((rows, width)), held((keys, width))]
        + [per_block(part.shape[1:]) for part in weights]
        + [held(extra.shape) for extra in extras],
        [
            whole((rows, width)),
            per_block((rows, 2 * LANES)),
            per_block((keys, 4 * LANES)),
            per_block((rows, 2 * LANES)),
            per_block((rows, LANES)),
        ],
        [
            shape((rows, width), jnp.float32),
            shape((blocks, rows, 2 * LANES), jnp.bfloat16),
            shape((blocks, keys, 4 * LANES), jnp.bfloat16),
            shape((blocks, rows, 2 * LANES), jnp.bfloat16),
            shape((blocks, rows, LANES), jnp.float32),
        ],
        [pltpu.VMEM((width, 6 * LANES), jnp.bfloat16)],
        flag,
        xq,
        xkv,
        *weights,
        *extras,
    )


def attend_back(flag, d_out, xq, xkv, weights, kept, extras, causal, first, count):
    rows, width = xq.shape
    keys = xkv.shape[0]
    return call(
        functools.partial(attend_back_kernel, causal),
        "attend_self_back" if causal else "attend_cross_back",
        10 * count,
        6 * 2**20 * count,
        count,
        [held((rows, width)), held((rows, width)), held((keys, width))]
        + [per_block(part.shape[1:], first) for part in weights]
        + [
            per_block((rows, 2 * LANES), first),
            per_block((keys, 4 * LANES), first),
            per_block((rows, 2 * LANES), first),
            per_block((rows, LANES), first),
        ]
        + [held(extra.shape) for extra in extras],
        [whole((rows, width)), whole((keys, width))] + [per_block(part.shape[1:]) for part in weights],
        [shape((rows, width), jnp.float32), shape((keys, width), jnp.float32)]
        + [shape((count,) + part.shape[1:], jnp.bfloat16) for part in weights],
        [
            pltpu.VMEM((width, 6 * LANES), jnp.bfloat16),
            pltpu.VMEM((keys, 4 * LANES), jnp.float32),
            pltpu.VMEM((rows, 2 * LANES), jnp.bfloat16),
            pltpu.VMEM((keys, 4 * LANES), jnp.bfloat16),
            pltpu.VMEM((width, 6 * LANES), jnp.bfloat16),
        ],
        flag,
        d_out,
        xq,
        xkv,
        *weights,
        *kept,
        *extras,
    )


def ffn_block(x_ref, w_ref, units, g_ref, slope_ref, first, out_ref):
    inner = mul(x_ref[...], w_ref[:, :units])
    spread = 0.5 * (1.0 + lax.erf(inner * (0.5**0.5)))
    bell = jnp.exp(-0.5 * inner * inner) * 0.3989422804014327
    active = (inner * spread).astype(jnp.bfloat16)
    g_ref[0] = active
    slope_ref[0] = (spread + inner * bell).astype(jnp.bfloat16)
    add_up(first, out_ref, mul_nt(active, w_ref[:, units:]))


def ffn_kernel(flag_ref, x_ref, *refs):
    own_refs, peer_refs = refs[:PARTS], refs[PARTS : 2 * PARTS]
    z_ref, g_ref, slope_ref, w_ref = refs[2 * PARTS :]
    assemble(flag_ref, own_refs, peer_refs, w_ref)
    ffn_block(x_ref, w_ref, own_refs[0].shape[2], g_ref, slope_ref, pl.program_id(0) == 0, z_ref)


def feed_blocks(feed, index):
    half, units = feed[0].shape[1], feed[0].shape[2] // 2
    return [
        pl.BlockSpec((1, half, units), lambda j, flag, side=side: (index(j, flag), 0, side))
        for _ in feed
        for side in (0, 1)
    ]


def feed_operands(feed):
    return [part for part in feed for _ in (0, 1)]


def ffn(flag, x, feed):
    rows, width = x.shape
    blocks, units = feed[0].shape[0], feed[0].shape[2] // 2
    return call(
        ffn_kernel,
        "ffn",
        12,
        rows * units * blocks * 16,
        blocks,
        [held((rows, width))] + feed_blocks(feed, lambda j, flag: j * flag[1]),
        [whole((rows, width)), per_block((rows, units)), per_block((rows, units))],
        [
            shape((rows, width), jnp.float32),
            shape((blocks, rows, units), jnp.bfloat16),
            shape((blocks, rows, units), jnp.bfloat16),
        ],
        [pltpu.VMEM((width, 2 * units), jnp.bfloat16)],
        flag,
        x,
        *feed_operands(feed),
    )


def ffn_back_block(dz_ref, w_ref, units, slope_ref, dh_ref, first, out_ref):
    d_active = mul(dz_ref[...], w_ref[:, units:])
    d_inner = (d_active * slope_ref[0].astype(jnp.float32)).astype(jnp.bfloat16)
    dh_ref[0] = d_inner
    add_up(first, out_ref, mul_nt(d_inner, w_ref[:, :units]))


def layer_norm(values, gain_row, bias_row):
    average = jnp.mean(values, axis=-1, keepdims=True)
    centered = values - average
    variance = jnp.mean(centered * centered, axis=-1, keepdims=True)
    return centered * lax.rsqrt(variance + NORM_EPS) * gain_row + bias_row


def norm_back(values, gain_row, bias_row, upstream):
    _, pullback = jax.vjp(layer_norm, values, gain_row, bias_row)
    return pullback(upstream)


def norm_parts(values):
    average = jnp.mean(values, axis=1, keepdims=True)
    centered = values - average
    scale = lax.rsqrt(jnp.mean(centered * centered, axis=1, keepdims=True) + NORM_EPS)
    return centered * scale, scale


def norm_gradients(values, gain_row, upstream):
    shaped, scale = norm_parts(values)
    inner = upstream * gain_row
    mean_inner = jnp.mean(inner, axis=1, keepdims=True)
    mean_product = jnp.mean(inner * shaped, axis=1, keepdims=True)
    d_values = scale * (inner - mean_inner - shaped * mean_product)
    d_gain = jnp.sum(upstream * shaped, axis=0, keepdims=True)
    return d_values, d_gain, jnp.sum(upstream, axis=0, keepdims=True)


def enc_out_back_kernel(
    flag_ref, arrived_ref, cot_ref, total_ref, norms_ref, d_dec_ref, enc_ref, dec_ref, *refs
):
    d_total_ref, dz_ref, sums_ref, keep_ref, send_ref, g_ref, left_t_ref = refs

    @pl.when(jnp.logical_and(pl.program_id(0) == 0, flag_ref[2] == 1))
    def _():
        upstream = arrived_ref[...].astype(jnp.float32) + cot_ref[...].astype(jnp.float32)
        d_total, sums_ref[0:1, :], sums_ref[1:2, :] = norm_gradients(total_ref[...], norms_ref[2:3, :], upstream)
        d_total_ref[...] = d_total
        dz_ref[...] = d_total.astype(jnp.bfloat16)

    @pl.when(jnp.logical_and(pl.program_id(0) == 0, flag_ref[2] == 0))
    def _():
        dz_ref[...] = d_dec_ref[...]

    @pl.when(pl.program_id(0) == 0)
    def _():
        left_t_ref[...] = dz_ref[...].T

    right = jnp.where(flag_ref[2] == 1, enc_ref[0], dec_ref[0])
    g_ref[...] = mul(left_t_ref[...], right).astype(jnp.bfloat16)
    hand_out(flag_ref, g_ref, keep_ref, send_ref)


def enc_out_back(flag, arrived, cot, total, norms, d_dec, enc_active, dec_active, feed):
    rows, width = cot.shape
    blocks, _, units = enc_active.shape
    like = shape((blocks, feed[0].shape[1], units), jnp.bfloat16)
    full = shape((rows, width), jnp.float32)
    return call(
        enc_out_back_kernel,
        "enc_out_back",
        9,
        rows * units * blocks * 8,
        blocks,
        [held(item.shape) for item in (arrived, cot, total, norms, d_dec)]
        + [per_block((rows, units), 0, 2), per_block((rows, units), 0, 3)],
        [whole((rows, width))] * 2 + [whole((8, width))] + [per_block(like.shape[1:])] * 2,
        [full, shape((rows, width), jnp.bfloat16), shape((8, width), jnp.float32)]
        + [like] * 2,
        [pltpu.VMEM((width, units), jnp.bfloat16), pltpu.VMEM((width, rows), jnp.bfloat16)],
        flag,
        arrived,
        cot,
        total,
        norms,
        d_dec,
        enc_active,
        dec_active,
    )


def enc_in_back_kernel(
    flag_ref, dz_ref, d_enc_ref, d_middle_ref, total_ref, gain_ref, middle_ref, crossed_ref, *refs
):
    first_own_ref, second_own_ref, first_peer_ref, second_peer_ref, slope_ref, dec_inner_ref, *refs = refs
    d_total_ref, d_low_ref, sums_ref, keep_ref, send_ref, w_ref, inner_ref, out_ref, g_ref, left_t_ref = refs
    step = pl.program_id(0)
    phase, at = step // 4, step % 4
    on_encoder = flag_ref[2] == 1

    @pl.when(jnp.logical_and(phase == 0, on_encoder))
    def _():
        assemble(flag_ref, [first_own_ref, second_own_ref], [first_peer_ref, second_peer_ref], w_ref)
        ffn_back_block(
            dz_ref, w_ref, first_own_ref.shape[2], slope_ref, inner_ref.at[pl.ds(at, 1)], at == 0, out_ref
        )

    @pl.when(step == 3)
    def _():
        upstream = jnp.where(on_encoder, d_enc_ref[...] + out_ref[...], d_middle_ref[...])
        d_total, sums_ref[0:1, :], sums_ref[1:2, :] = norm_gradients(total_ref[...], gain_ref[0:1, :], upstream)
        d_total_ref[...] = d_total
        d_low_ref[...] = d_total.astype(jnp.bfloat16)
        left_t_ref[...] = jnp.where(on_encoder, middle_ref[...], crossed_ref[...]).T

    @pl.when(phase == 1)
    def _():
        right = jnp.where(on_encoder, inner_ref[at], dec_inner_ref[0])
        g_ref[...] = mul(left_t_ref[...], right).astype(jnp.bfloat16)
        hand_out(flag_ref, g_ref, keep_ref, send_ref)


def enc_in_back(flag, dz, d_enc, d_middle, total, gain, middle, crossed, feed, slope, dec_inner):
    rows, width = dz.shape
    blocks, half, units = feed[0].shape[0], feed[0].shape[1], feed[0].shape[2] // 2
    full = shape((rows, width), jnp.float32)

    def at_step(of, low, high, gate):
        def index(j, flag):
            return (jnp.where(j < 4, j if low == "up" else low, j - 4 if high == "up" else high) * flag[gate],) + (
                0,
            ) * len(of)

        return pl.BlockSpec((1,) + of, index)

    return call(
        enc_in_back_kernel,
        "enc_in_back",
        19,
        rows * units * blocks * 20,
        8,
        [held(item.shape) for item in (dz, d_enc, d_middle, total, gain, middle, crossed)]
        + feed_blocks(feed, lambda j, flag: jnp.where(j < 4, j, 3) * flag[2])
        + [at_step((rows, units), "up", 3, 2), at_step((rows, units), 0, "up", 3)],
        [whole((rows, width))] * 2 + [whole((8, width))] + [at_step((half, units), 0, "up", 1)] * 2,
        [full, shape((rows, width), jnp.bfloat16), shape((8, width), jnp.float32)]
        + [shape((blocks, half, units), jnp.bfloat16)] * 2,
        [
            pltpu.VMEM((width, 2 * units), jnp.bfloat16),
            pltpu.VMEM((blocks, rows, units), jnp.bfloat16),
            pltpu.VMEM((rows, width), jnp.float32),
            pltpu.VMEM((width, units), jnp.bfloat16),
            pltpu.VMEM((width, rows), jnp.bfloat16),
        ],
        flag,
        dz,
        d_enc,
        d_middle,
        total,
        gain,
        middle,
        crossed,
        *feed_operands(feed),
        slope,
        dec_inner,
    )


def decoder_kernel(
    flag_ref,
    h1_ref,
    mem_a_ref,
    mem_b_ref,
    peer_a_ref,
    peer_b_ref,
    cot_ref,
    qx_ref,
    kx_ref,
    norms_ref,
    own_ref,
    peer_ref,
    first_own_ref,
    second_own_ref,
    first_peer_ref,
    second_peer_ref,
    decoded_ref,
    crossed_ref,
    d_dec_ref,
    d_middle_ref,
    mine_ref,
    other_ref,
    sums_ref,
    active_ref,
    inner_ref,
    keep_ref,
    send_ref,
    xq_ref,
    xkv_ref,
    wx_ref,
    wf_ref,
    q_ref,
    kv_ref,
    c_ref,
    l_ref,
    slope_ref,
    out_ref,
    total_ref,
    do_ref,
    dxkv_ref,
    *work,
):
    step = pl.program_id(0)
    phase, at = step // 4, step % 4
    first, last = at == 0, at == 3
    rows = h1_ref.shape[0]
    units = first_own_ref.shape[2]
    gain = [norms_ref[row : row + 1, :] for row in range(3)]
    bias = [norms_ref[3 + row : 4 + row, :] for row in range(3)]

    def kept(block):
        return tuple(ref.at[pl.ds(block, 1)] for ref in (q_ref, kv_ref, c_ref, l_ref))

    @pl.when(step == 0)
    def _():
        xq_ref[...] = h1_ref[...].astype(jnp.bfloat16)
        for part, ref in enumerate((mem_a_ref, mem_b_ref, peer_a_ref, peer_b_ref)):
            xkv_ref[part * rows // 2 : (part + 1) * rows // 2] = ref[...]

    @pl.when(jnp.logical_or(phase == 0, phase == 3))
    def _():
        assemble(flag_ref, [own_ref], [peer_ref], wx_ref)

    @pl.when(jnp.logical_or(phase == 1, phase == 2))
    def _():
        assemble(flag_ref, [first_own_ref, second_own_ref], [first_peer_ref, second_peer_ref], wf_ref)

    @pl.when(phase == 0)
    def _():
        add_up(first, out_ref, attend_block(False, xq_ref, xkv_ref, wx_ref, qx_ref, kx_ref, None, *kept(at)))

    @pl.when(jnp.logical_and(phase == 0, last))
    def _():
        total = h1_ref[...] + out_ref[...]
        total_ref[...] = total
        crossed = norm_parts(total)[0] * gain[1] + bias[1]
        mine_ref[...] = crossed
        crossed_ref[...] = crossed.astype(jnp.bfloat16)

    @pl.when(phase == 1)
    def _():
        ffn_block(crossed_ref, wf_ref, units, active_ref, slope_ref.at[pl.ds(at, 1)], first, out_ref)

    @pl.when(jnp.logical_and(phase == 1, last))
    def _():
        total = mine_ref[...] + out_ref[...]
        decoded_ref[...] = (norm_parts(total)[0] * gain[2] + bias[2]).astype(jnp.bfloat16)
        d_total, sums_ref[0:1, :], sums_ref[1:2, :] = norm_gradients(
            total, gain[2], cot_ref[...].astype(jnp.float32)
        )
        d_middle_ref[...] = d_total
        d_dec_ref[...] = d_total.astype(jnp.bfloat16)

    @pl.when(phase == 2)
    def _():
        ffn_back_block(d_dec_ref, wf_ref, units, slope_ref.at[pl.ds(3 - at, 1)], inner_ref, first, out_ref)

    @pl.when(jnp.logical_and(phase == 2, last))
    def _():
        d_total, sums_ref[2:3, :], sums_ref[3:4, :] = norm_gradients(
            total_ref[...], gain[1], d_middle_ref[...] + out_ref[...]
        )
        d_middle_ref[...] = d_total
        do_ref[...] = d_total.astype(jnp.bfloat16)

    @pl.when(phase == 3)
    def _():
        d_xq, d_xkv = attend_back_block(
            False, do_ref, xq_ref, xkv_ref, wx_ref, qx_ref, kx_ref, None, kept(3 - at), work
        )
        add_up(first, out_ref, d_xq)
        add_up(first, dxkv_ref, d_xkv)
        hand_out(flag_ref, work[3], keep_ref, send_ref)

    @pl.when(jnp.logical_and(phase == 3, last))
    def _():
        d_middle_ref[...] += out_ref[...]
        mine_ref[...] = dxkv_ref[:rows]
        other_ref[...] = dxkv_ref[rows:].astype(jnp.bfloat16)


def decoder(flag, h1, memory, cot, extras, norms, cross, feed):
    rows, width = h1.shape
    blocks, half, _ = cross[0].shape
    units = feed[0].shape[2] // 2
    keys = 2 * rows
    qx, kx = extras

    def at_step(of, in_phase):
        def index(j, flag):
            at = j % 4
            choice = [{"up": at, "down": 3 - at}.get(way, way) for way in in_phase]
            chosen = choice[3]
            for phase in (2, 1, 0):
                chosen = jnp.where(j // 4 == phase, choice[phase], chosen)
            return (chosen * flag[1],) + (0,) * len(of)

        return pl.BlockSpec((1,) + of, index)

    part = (half, cross[0].shape[2])
    full = shape((rows, width), jnp.float32)
    rounded = shape((rows, width), jnp.bfloat16)
    return call(
        decoder_kernel,
        "decoder",
        90,
        40 * 2**20,
        16,
        [held(item.shape) for item in (h1, *memory, cot, qx, kx, norms)]
        + [at_step(part, ("up", 3, 3, "down"))] * 2
        + feed_blocks(feed, lambda j, flag: at_step((half, units), (0, "up", "down", 0)).index_map(j, flag)[0]),
        [whole((rows, width))] * 6
        + [whole((8, width))]
        + [
            at_step((rows, units), (0, "up", 3, 3)),
            at_step((rows, units), (3, 3, "down", 0)),
            at_step(part, (3, 3, 3, "down")),
            at_step(part, (3, 3, 3, "down")),
        ],
        [rounded, rounded, rounded, full, full, rounded, shape((8, width), jnp.float32)]
        + [shape((blocks, rows, units), jnp.bfloat16)] * 2
        + [shape(cross[0].shape, jnp.bfloat16)] * 2,
        [
            pltpu.VMEM((rows, width), jnp.bfloat16),
            pltpu.VMEM((keys, width), jnp.bfloat16),
            pltpu.VMEM((width, 6 * LANES), jnp.bfloat16),
            pltpu.VMEM((width, 2 * units), jnp.bfloat16),
            pltpu.VMEM((blocks, rows, 2 * LANES), jnp.bfloat16),
            pltpu.VMEM((blocks, keys, 4 * LANES), jnp.bfloat16),
            pltpu.VMEM((blocks, rows, 2 * LANES), jnp.bfloat16),
            pltpu.VMEM((blocks, rows, LANES), jnp.float32),
            pltpu.VMEM((blocks, rows, units), jnp.bfloat16),
            pltpu.VMEM((rows, width), jnp.float32),
            pltpu.VMEM((rows, width), jnp.float32),
            pltpu.VMEM((rows, width), jnp.bfloat16),
            pltpu.VMEM((keys, width), jnp.float32),
            pltpu.VMEM((keys, 4 * LANES), jnp.float32),
            pltpu.VMEM((rows, 2 * LANES), jnp.bfloat16),
            pltpu.VMEM((keys, 4 * LANES), jnp.bfloat16),
            pltpu.VMEM((width, 6 * LANES), jnp.bfloat16),
        ],
        flag,
        h1,
        *memory,
        cot,
        qx,
        kx,
        norms,
        *cross,
        *feed_operands(feed),
    )


def low(values):
    return values.astype(jnp.bfloat16)


def axes_of(count):
    return ("section", "zh", "zl") + tuple("e%d" % at for at in range(count)) + ("ty", "tx")


def layer_of(place):
    return 1 ^ place["zh"] ^ place["zl"]


def moved(x, names, to):
    names = [name for name in axes_of(8) if name in names]

    def index(place):
        return sum(place[name] << (len(names) - 1 - at) for at, name in enumerate(names))

    pairs = []
    for source in range(2 ** len(names)):
        place = {name: source >> (len(names) - 1 - at) & 1 for at, name in enumerate(names)}
        target = to(place)
        if target is not None:
            pairs.append((source, index(target)))
    return lax.ppermute(x, tuple(names), pairs)


def over(x, *axes, layer=None):
    def to(place):
        if layer is not None and layer_of(place) != layer:
            return None
        return {**place, **{axis: 1 - place[axis] for axis in axes}}

    return moved(x, axes if layer is None else axes + Z, to)


Z = ("zh", "zl")


def swapped(x):
    def to(place):
        if place["section"] == layer_of(place):
            return place
        return {"section": 1 - place["section"], "zh": place["zh"], "zl": 1 - place["zl"]}

    return moved(x, ("section",) + Z, to)


def turned(x):
    return moved(x, ("section", "ty"), lambda place: {"section": place["ty"], "ty": place["section"]})


def sent_home(x, other):
    def to(place):
        return {
            "section": layer_of(place),
            "zh": place["zh"],
            "zl": 1 ^ place["zh"] ^ place["ty"],
            "ty": place["section"],
            "tx": place["tx"] ^ other,
        }

    return moved(x, ("section",) + Z + ("ty", "tx"), to)


def cross_in(x, layer):
    def to(place):
        if place["section"] != layer:
            return None
        return {"section": layer_of(place), "zh": place["zh"], "zl": place["zh"]}

    return moved(x, ("section",) + Z, to)


def cross_out(x, layer):
    def to(place):
        if layer_of(place) != 1:
            return None
        return {"section": layer, "zh": place["zh"], "zl": 1 ^ place["zh"] ^ place["section"]}

    return moved(x, ("section",) + Z, to)


def in_order(x, flag, axis):
    return jnp.where(flag == 1, jnp.flip(x, axis), x)


def pack_heads(query, key, value, out):
    pair = 2 * HDIM
    return jnp.concatenate(
        [
            query,
            value[:, pair:],
            key[:, :pair],
            value[:, :pair],
            key[:, pair:],
            out[:, pair:],
            out[:, :pair],
        ],
        axis=1,
    )


def unpack_heads(packed):
    part = [packed[:, at * HDIM : (at + 1) * HDIM] for at in range(12)]
    query = jnp.concatenate(part[0:3], axis=1)
    key = jnp.concatenate([part[4], part[5], part[8]], axis=1)
    value = jnp.concatenate([part[6], part[7], part[3]], axis=1)
    out = jnp.concatenate([part[10], part[11], part[9]], axis=1)
    return query, key, value, out


def after(x, *earlier):
    return lax.optimization_barrier((x,) + earlier)[0]


def plane_gathered(x, until=(), **only):
    parts = [x, over(x, "tx", **only), over(x, "ty", **only), over(x, "ty", "tx", **only)]
    return jnp.stack([after(part, *until) for part in parts])


def plane_summed(x, until=(), raw=None, **only):
    terms = [x[0], over(x[1], "tx", **only), over(x[2], "ty", **only), over(x[3], "ty", "tx", **only)]
    if raw is not None:
        raw.extend(terms[1:])
    terms = [after(term, *until) for term in terms]
    return low(sum(term.astype(jnp.float32) for term in terms))


def rows_gathered(x, count, until=(), raw=None, **only):
    for axes in [("e%d" % at,) for at in reversed(range(count))] + [Z]:
        got = over(x, *axes, **only)
        if raw is not None:
            raw.append(got)
        parts = [after(part, *until) for part in (x, got)]
        both = in_order(jnp.stack(parts, axis=-3), lax.axis_index(axes[0]), x.ndim - 2)
        x = both.reshape(x.shape[:-2] + (2 * x.shape[-2], x.shape[-1]))
    return x


def rows_summed(x, count, until=(), raw=None, **only):
    for axes in [Z] + [("e%d" % at,) for at in range(count)]:
        halves = x.reshape(x.shape[:-2] + (2, x.shape[-2] // 2, x.shape[-1]))
        halves = in_order(halves, lax.axis_index(axes[0]), x.ndim - 2)
        got = over(halves[..., 1, :, :], *axes, **only)
        if raw is not None:
            raw.append(got)
        x = plus(halves[..., 0, :, :], after(got, *until))
    return x


def plus(first, second):
    return low(first.astype(jnp.float32) + second.astype(jnp.float32))


def from_cores(keep, send, raw=None, **only):
    got = over(send, "section", **only)
    if raw is not None:
        raw.append(got)
    return plus(keep, got)


def body(
    count,
    hidden,
    cotangent,
    segments,
    sa_qkv,
    sa_out,
    cross_one,
    cross_two,
    ffn_in,
    ffn_out,
    norm_gain,
    norm_bias,
):
    core = lax.axis_index("section")
    x_at, y_at, zh_at, zl_at = (lax.axis_index(name) for name in ("tx", "ty", "zh", "zl"))
    layer = 1 ^ zh_at ^ zl_at
    on_encoder = layer == 0
    quarter = hidden.shape[3]
    enc_flag = jnp.stack([core, 1 - layer, 1 - layer, layer])
    dec_flag = jnp.stack([core, layer, 1 - layer, layer])
    flag = jnp.stack([core, jnp.ones_like(core), 1 - layer, layer])

    def pick(first, second):
        return jnp.where(on_encoder, first, second)

    def of_one_row(x):
        both = in_order(x[0, :, 0], x_at, 0)
        return in_order(jnp.stack([both[0], over(both[1], "tx")]), x_at, 0).reshape(2 * quarter, -1)

    def rows_out(x, raw=None):
        mine, other = in_order(x.reshape(2, quarter, -1), x_at, 0)
        both = [sent_home(mine, 0), sent_home(other, 1)]
        if raw is not None:
            raw.extend(both)
        return in_order(jnp.stack(both), x_at, 0)[None, :, None]

    units = ffn_in.shape[2]
    width = cross_one.shape[2]
    packed_self = pack_heads(sa_qkv[0, :, 0], sa_qkv[0, :, 1], sa_qkv[0, :, 2], sa_out[0])
    packed_ffn = jnp.concatenate([ffn_in[0], ffn_out[0].T], axis=1)
    with jax.named_scope("norms_in"):
        norms = swapped(jnp.concatenate([norm_gain[0], norm_bias[0]], axis=0))
        gains, biases = norms[:3], norms[3:]
        seg_own = segments[:, :, 0].astype(jnp.float32)
        seg_here = jnp.where(zl_at == 1 ^ zh_at ^ y_at, seg_own, over(seg_own, "zl")).astype(jnp.int32)
    with jax.named_scope("hidden_in"):
        one_row = of_one_row(jnp.concatenate([hidden, cotangent], axis=-1))
    with jax.named_scope("self_weights"):
        shard_self = swapped(packed_self)
    with jax.named_scope("hidden_in"):
        one_row = swapped(after(one_row, shard_self))
    with jax.named_scope("ffn_weights"):
        shard_ffn = swapped(after(packed_ffn, one_row))

    def both_rows(x):
        for_enc = rows_gathered(x, count, layer=0)
        return pick(for_enc, rows_gathered(after(x, for_enc), count, layer=1))

    with jax.named_scope("self_weights"):
        rows_self = both_rows(shard_self)
        raw_ffn_rows = []
        rows_ffn_enc = rows_gathered(after(shard_ffn, rows_self), count, raw=raw_ffn_rows, layer=0)
        own_self = plane_gathered(rows_self, until=tuple(raw_ffn_rows))
        w_self = [own_self, over(own_self, "section")]
    with jax.named_scope("hidden_in"):
        rows_here = turned(one_row)
        rows_here, cot = rows_here[:, : hidden.shape[-1]], rows_here[:, hidden.shape[-1] :]
        rows_all = jnp.concatenate([rows_here, over(rows_here, "section")], axis=0)
    with jax.named_scope("cross_weights"):
        cross_low = after(jnp.concatenate([cross_one[0], cross_two[0]], axis=1), own_self)
        pair_kv, pair_qo = cross_in(cross_low, 0), cross_in(cross_low, 1)
        packed = pack_heads(pair_qo[:, :width], pair_kv[:, :width], pair_kv[:, width:], pair_qo[:, width:])
    with jax.named_scope("ffn_weights"):
        rows_ffn = pick(rows_ffn_enc, rows_gathered(after(shard_ffn, *raw_ffn_rows), count, layer=1))

    both_segments = in_order(seg_here, x_at, 1)[:, 0]
    ordered = in_order(both_segments.reshape(2, 2, 2 * quarter), core, 1).reshape(2, 4 * quarter)
    source_seg, target_seg = ordered[0], ordered[1]
    self_seg = pick(source_seg, target_seg)
    parts = jnp.arange(4)
    quarter_of = jnp.repeat(2 * ((parts // 2) ^ core) + parts % 2, quarter)
    lanes = jnp.arange(LANES)[None, :]

    def key_extras(seg):
        differs = jnp.logical_and(lanes < SEG_LANES, seg[:, None] != lanes)
        later = jnp.logical_and(
            jnp.logical_and(lanes >= SEG_LANES, lanes < PART_LANE),
            quarter_of[:, None] > lanes - SEG_LANES,
        )
        part = jnp.logical_and(lanes >= PART_LANE, lanes < PART_LANE + 3)
        return jnp.where(differs | later | part, 1.0, 0.0).astype(jnp.bfloat16)

    def query_extras(seg, causal):
        seg, at = seg[: 2 * quarter], quarter_of[: 2 * quarter]
        same = seg[:, None] == lanes
        here = jnp.logical_and(at[:, None] + SEG_LANES == lanes, causal)
        return jnp.where(same | here, MASKED, 0.0).astype(jnp.bfloat16)

    at_row = jnp.arange(quarter)
    later_key = jnp.logical_and(at_row[None, :] > at_row[:, None], jnp.logical_not(on_encoder))
    tri = jnp.where(later_key, MASKED, 0.0).astype(jnp.float32)
    self_extras = (query_extras(self_seg, jnp.logical_not(on_encoder)), key_extras(self_seg), tri)
    cross_extras = (query_extras(target_seg, False), key_extras(source_seg), tri)

    start = rows_all.astype(jnp.float32)
    start = pick(layer_norm(start, gains[0], biases[0]), start)
    start_here = start[: 2 * quarter]
    start_low = low(start)
    self_gain, self_bias = pick(gains[1], gains[0]), pick(biases[1], biases[0])
    raw_cross_rows = []
    with jax.named_scope("cross_weights"):
        rows_cross = rows_gathered(after(packed, rows_ffn), count, raw=raw_cross_rows, layer=1)
    self_out, *kept_self = attend(
        flag, start_low[: 2 * quarter], start_low, w_self, self_extras, True
    )
    with jax.named_scope("ffn_weights"):
        own_ffn = plane_gathered(after(rows_ffn, own_self), until=(self_out, *raw_cross_rows))
        feed = [own_ffn, over(own_ffn, "section")]
    self_total = start_here + after(self_out, *raw_cross_rows)
    middle = layer_norm(self_total, self_gain, self_bias)
    middle_low = low(middle)

    enc_out, enc_active, enc_slope = ffn(enc_flag, middle_low, feed)
    enc_total = middle + enc_out
    encoded = low(layer_norm(enc_total, gains[2], biases[2]))
    def across(x, layer):
        return moved(x, Z, lambda place: {**place, "zl": 1 - place["zl"]} if layer_of(place) == layer else None)

    with jax.named_scope("memory"):
        memory_here = [across(encoded[:quarter], 0), across(encoded[quarter:], 0)]
        memory_peer = [over(part, "section", layer=1) for part in memory_here]
    with jax.named_scope("cross_weights"):
        own_cross = plane_gathered(after(rows_cross, feed[1]), until=tuple(memory_here), layer=1)
        w_cross = [own_cross, over(own_cross, "section", layer=1)]
    (
        decoded,
        crossed_low,
        d_dec_low,
        d_middle_dec,
        d_memory_here,
        d_memory_other,
        dec_sums,
        dec_active,
        dec_inner,
        cross_keep,
        cross_send,
    ) = decoder(
        dec_flag, middle, memory_here + memory_peer, cot, cross_extras[:2], norms, w_cross, feed
    )
    with jax.named_scope("d_memory"):
        d_memory_here = d_memory_here + over(d_memory_other, "section", layer=1).astype(jnp.float32)
        d_memory_low = low(d_memory_here)
        arrived = across(d_memory_low, 1)
    with jax.named_scope("cross_sums"):
        cross_sum = from_cores(after(cross_keep, arrived), after(cross_send, arrived), layer=1)
        raw_cross = []
        cross_plane = plane_summed(cross_sum, raw=raw_cross, layer=1)

    raw_hidden = []
    with jax.named_scope("hidden_out"):
        hidden_out = rows_out(after(pick(encoded, decoded), arrived), raw_hidden)

    d_enc_total, dz_low, enc_sums, second_keep, second_send = enc_out_back(
        flag, arrived, cot, enc_total, norms, d_dec_low, enc_active, dec_active, feed
    )
    with jax.named_scope("ffn_sums"):
        raw_second_sum = []
        second_sum = from_cores(
            after(second_keep, *raw_hidden), after(second_send, *raw_hidden), raw=raw_second_sum
        )
    gain_row = jnp.broadcast_to(self_gain, (8, self_gain.shape[0]))
    d_self_total, d_self_low, self_norm, first_keep, first_send = enc_in_back(
        flag,
        after(dz_low, second_keep, cross_sum),
        d_enc_total,
        d_middle_dec,
        self_total,
        gain_row,
        middle_low,
        crossed_low,
        feed,
        enc_slope,
        dec_inner,
    )
    with jax.named_scope("ffn_sums"):
        gate = []
        second_plane = plane_summed(after(second_sum, d_self_low), raw=gate)
        first_sum = from_cores(after(first_keep, *raw_cross), after(first_send, *raw_cross), raw=gate)

    halves = []
    for first, earlier in ((0, ()), (2, gate)):
        halves.append(
            attend_back(
                flag,
                after(d_self_low, *earlier),
                start_low[: 2 * quarter],
                start_low,
                w_self,
                kept_self,
                self_extras,
                True,
                first,
                2,
            )
        )
    d_start_q = halves[0][0] + halves[1][0]
    with jax.named_scope("cross_sums"):
        share_cross = rows_summed(after(cross_plane, d_start_q), count, layer=1)
    with jax.named_scope("ffn_sums"):
        gate_later = []
        first_plane = plane_summed(after(first_sum, second_plane), raw=gate_later)
        second_share = rows_summed(second_plane, count, raw=gate_later)
    with jax.named_scope("self_sums"):
        (_, _, keep, send), (_, _, *later) = halves
        self_sum = [from_cores(after(keep, *gate), after(send, *gate), raw=gate_later)]
        raw_later = []
        self_sum.append(from_cores(*(after(part, *gate_later) for part in later), raw=raw_later))
        self_sum = jnp.concatenate(self_sum, axis=0)
    with jax.named_scope("d_start"):
        d_start_kv = after(halves[0][1], *raw_later) + halves[1][1]
        d_start = d_self_total + d_start_q + d_start_kv[: 2 * quarter]
        d_start = d_start + over(low(d_start_kv[2 * quarter :]), "section").astype(jnp.float32)
    d_source, gain_a, bias_a = norm_back(
        rows_here.astype(jnp.float32), gains[0], biases[0], d_start
    )

    rows_from = jnp.concatenate([enc_sums, self_norm, dec_sums, jnp.stack([gain_a, bias_a])], axis=0)
    enc_rows, dec_rows = jnp.array([24, 8, 0, 25, 9, 1]), jnp.array([8, 18, 16, 9, 19, 17])
    wanted = pick(enc_rows, dec_rows)[:, None] == jnp.arange(26)
    norm_sums = jnp.sum(jnp.where(wanted[:, :, None], rows_from[None], 0.0), axis=1)
    shards = 2**count
    sides = jnp.arange(2)
    held, outer = core ^ sides[:, None], sides[None, :]
    row_block = ((2 * outer + (1 ^ outer ^ held)) * shards)[:, :, None] + jnp.arange(shards)
    column_block = (2 * (y_at ^ sides)[:, None] + (x_at ^ sides)[None, :]).reshape(-1)
    order = (row_block.reshape(2, -1)[:, None, :] + 0) * 4 + column_block[:, None]
    norm_sums = jnp.take(norm_sums.reshape(6, 8 * 2 * shards, -1), order.reshape(-1), axis=1)
    norm_sums = norm_sums.reshape(6, 2, 4, 2 * shards, -1)
    with jax.named_scope("norm_sums"):
        norm_got = over(norm_sums[:, 1], "section")
        norm_sums = norm_sums[:, 0] + norm_got
    with jax.named_scope("self_sums"):
        self_plane = plane_summed(self_sum, until=(norm_got,))
    with jax.named_scope("norm_sums"):
        norm_blocks = after(norm_sums.transpose(1, 2, 0, 3).reshape(4, 2 * shards, -1), self_plane)
        norm_plane = norm_blocks[0] + over(norm_blocks[1], "tx") + over(norm_blocks[2], "ty")
        norm_plane = norm_plane + over(norm_blocks[3], "ty", "tx")
    norm_width = norm_plane.shape[1]
    with jax.named_scope("self_sums"):
        pad = ((0, 0), (0, 15), (0, self_plane.shape[1] - norm_width))
        both = jnp.concatenate(
            [
                self_plane.reshape(2 * shards, -1, self_plane.shape[1]),
                jnp.pad(low(norm_plane)[:, None], pad),
            ],
            axis=1,
        )
        raw_self = []
        share_self = rows_summed(both.reshape(-1, self_plane.shape[1]), count, raw=raw_self)
        share_self = swapped(share_self).astype(jnp.float32)
    norm_shares = share_self[-16, :norm_width].reshape(6, -1)
    share_self = share_self[:-16]
    with jax.named_scope("ffn_sums"):
        first_share = rows_summed(after(first_plane, *raw_later), count)
        share_ffn = swapped(jnp.concatenate([first_share, second_share], axis=1)).astype(jnp.float32)
    share_first, share_second = share_ffn[:, :units], share_ffn[:, units:].T
    with jax.named_scope("hidden_grad"):
        hidden_grad = rows_out(after(low(pick(d_source, d_start)), *raw_self)).astype(jnp.float32)
    g_query, g_key, g_value, g_out = unpack_heads(share_self)
    grad_qkv = jnp.stack([g_query, g_key, g_value], axis=1)
    c_query, c_key, c_value, c_out = unpack_heads(share_cross)
    with jax.named_scope("cross_out"):
        for_enc = cross_out(jnp.concatenate([c_key, c_value], axis=1), 0)
        for_dec = cross_out(jnp.concatenate([c_query, c_out], axis=1), 1)
    cross = jnp.where(core == 0, for_enc, for_dec).astype(jnp.float32)

    return (
        hidden_out,
        hidden_grad,
        grad_qkv[None],
        g_out[None],
        cross[None, :, :width],
        cross[None, :, width:],
        share_first[None],
        share_second[None],
        norm_shares[None, :3],
        norm_shares[None, 3:],
    )


def solution(mesh):
    _, dp_count, _ = mesh.devices.shape
    count = dp_count.bit_length() - 3
    names = axes_of(count)
    dp, tensor = names[1:-2], names[-2:]
    split = Mesh(mesh.devices.reshape((2,) * len(names)), names)
    rows = P("section", None, dp, tensor, None)
    in_specs = (
        rows,
        rows,
        P(None, None, dp, None),
        P("section", dp, None, tensor),
        P("section", dp, tensor),
        P("section", dp, tensor),
        P("section", dp, tensor),
        P("section", dp, tensor),
        P("section", tensor, dp),
        P("section", None, None),
        P("section", None, None),
    )
    out_specs = (
        rows,
        rows,
        P("section", dp, None, tensor),
        P("section", dp, tensor),
        P("section", dp, tensor),
        P("section", dp, tensor),
        P("section", dp, tensor),
        P("section", tensor, dp),
        P("section", None, dp + tensor),
        P("section", None, dp + tensor),
    )
    return jax.shard_map(
        functools.partial(body, count), mesh=split, in_specs=in_specs, out_specs=out_specs, check_vma=False
    )
```

```python
import functools

import jax
import jax.numpy as jnp
from jax import lax
from jax.experimental import pallas as pl
from jax.experimental.pallas import tpu as pltpu
from jax.sharding import Mesh
from jax.sharding import PartitionSpec as P

HDIM = 64
LANES = 128
MASKED = -1e30
NORM_EPS = 1e-05
VMEM_BYTES = 56 * 1024 * 1024
SMALL_VMEM_BYTES = 42 * 1024 * 1024

SEG_LANES = 8
PART_LANE = 12

PARTS = 2
TILE_ROWS = 256
HEADS = ((0, 1, 2, 0, 0), (0, 1, 2, 1, 1), (1, 3, 0, 0, 1))


def mul(a, b):
    return jnp.dot(a, b, preferred_element_type=jnp.float32)


def mul_nt(a, b):
    return lax.dot_general(a, b, (((1,), (1,)), ((), ())), preferred_element_type=jnp.float32)


def mul_tn(a, b):
    return lax.dot_general(a, b, (((0,), (0,)), ((), ())), preferred_element_type=jnp.float32)


def tile_of(values, index):
    return values[:, index * LANES : (index + 1) * LANES]


def lane_ids(rows):
    return lax.broadcasted_iota(jnp.int32, (rows, LANES), 1)


def half_mask(rows, half):
    lanes = lane_ids(rows)
    return lanes >= HDIM if half else lanes < HDIM


def in_parts(base, column):
    lanes = lane_ids(base.shape[0])
    high = column.astype(jnp.bfloat16).astype(jnp.float32)
    rest = column - high
    middle = rest.astype(jnp.bfloat16).astype(jnp.float32)
    low = rest - middle
    parts = jnp.where(
        lanes == PART_LANE,
        high,
        jnp.where(lanes == PART_LANE + 1, middle, jnp.where(lanes == PART_LANE + 2, low, base)),
    )
    return parts.astype(jnp.bfloat16)


def with_triangle(scores, tri, at):
    size = tri.shape[1]
    pieces = []
    if at > 0:
        pieces.append(scores[:, : at * size])
    pieces.append(scores[:, at * size : (at + 1) * size] + tri)
    pieces.append(scores[:, (at + 1) * size :])
    return jnp.concatenate(pieces, axis=1)


def places(core, block):
    return [pl.multiple_of((1 - core) * block, block), pl.multiple_of((2 + core) * block, block)]


def assemble(flag_ref, own_refs, peer_refs, w_ref):
    core, block = flag_ref[0], own_refs[0].shape[1] // 2
    for holder, refs in ((core, own_refs), (1 - core, peer_refs)):
        for part, ref in enumerate(refs):
            width = ref.shape[2]
            for at, place in enumerate(places(holder, block)):
                w_ref[pl.ds(place, block), part * width : (part + 1) * width] = ref[0, at * block : (at + 1) * block]


def hand_out(flag_ref, g_ref, keep_ref, send_ref):
    core, block = flag_ref[0], keep_ref.shape[1] // 2
    for holder, ref in ((core, keep_ref), (1 - core, send_ref)):
        for at, place in enumerate(places(holder, block)):
            ref[0, at * block : (at + 1) * block] = g_ref[pl.ds(place, block), :]


def where_active(kernel):
    def guarded(flag_ref, *refs):
        @pl.when(flag_ref[1] == 1)
        def _():
            kernel(flag_ref, *refs)

    return guarded


def scaled_queries(q_ref, at, q_tile, q_half):
    queries = q_ref[0, at, q_tile * LANES : (q_tile + 1) * LANES] * 0.125
    return jnp.where(half_mask(queries.shape[0], q_half), queries, 0).astype(jnp.bfloat16)


def units_of(total, rows):
    return [
        (slice(part * rows, (part + 1) * rows), part, head)
        for part in range(total // rows)
        for head in range(len(HEADS))
    ]


def attend_block(causal, xq_ref, xkv_ref, w_ref, qx_ref, kx_ref, tri_ref, q_ref, kv_ref, c_ref, l_ref):
    q_ref[0] = mul(xq_ref[...], w_ref[:, : 2 * LANES]).astype(jnp.bfloat16)
    kv_ref[0] = mul(xkv_ref[...], w_ref[:, LANES : 5 * LANES]).astype(jnp.bfloat16)
    rows = TILE_ROWS
    low = half_mask(rows, 0)

    def scores_of(at, part, head):
        q_tile, k_tile, _, q_half, _ = HEADS[head]
        keys = kv_ref[0, :, k_tile * LANES : (k_tile + 1) * LANES]
        scores = mul_nt(
            jnp.concatenate([scaled_queries(q_ref, at, q_tile, q_half), qx_ref[at, :]], axis=1),
            jnp.concatenate([keys, kx_ref[...]], axis=1),
        )
        return with_triangle(scores, tri_ref[...], part) if causal else scores

    units = units_of(q_ref.shape[1], rows)
    ahead = scores_of(*units[0])
    contexts, totals = [], None
    for index, (at, part, head) in enumerate(units):
        scores = ahead
        if index + 1 < len(units):
            ahead = scores_of(*units[index + 1])
        v_tile = HEADS[head][2]
        values = kv_ref[0, :, v_tile * LANES : (v_tile + 1) * LANES]
        highest = jnp.max(scores, axis=1, keepdims=True)
        weights = jnp.exp(scores - highest)
        sums = jnp.sum(weights, axis=1, keepdims=True)
        contexts.append(mul(weights.astype(jnp.bfloat16), values) / sums)
        logs = jnp.broadcast_to(highest + jnp.log(sums), (rows, LANES))
        totals = logs if head == 0 else jnp.where(lane_ids(rows) == head, logs, totals)
        if head == len(HEADS) - 1:
            c_ref[0, at, :LANES] = jnp.where(low, 0, contexts[2]).astype(jnp.bfloat16)
            c_ref[0, at, LANES:] = jnp.where(low, contexts[0], contexts[1]).astype(jnp.bfloat16)
            l_ref[0, at, :] = totals
            contexts = []
    return mul_nt(c_ref[0], w_ref[:, 4 * LANES :])


def attend_kernel(causal, flag_ref, xq_ref, xkv_ref, own_ref, peer_ref, qx_ref, kx_ref, tri_ref, o_ref, *refs):
    q_ref, kv_ref, c_ref, l_ref, w_ref = refs
    assemble(flag_ref, [own_ref], [peer_ref], w_ref)
    out = attend_block(causal, xq_ref, xkv_ref, w_ref, qx_ref, kx_ref, tri_ref, q_ref, kv_ref, c_ref, l_ref)
    add_up(pl.program_id(0) == 0, o_ref, out)


def add_up(first, ref, value):
    @pl.when(first)
    def _():
        ref[...] = value

    @pl.when(jnp.logical_not(first))
    def _():
        ref[...] += value


def attend_back_block(causal, do_ref, xq_ref, xkv_ref, w_ref, qx_ref, kx_ref, tri_ref, kept, work):
    q_ref, kv_ref, c_ref, l_ref = kept
    sum_ref, dq_ref, dkv_ref, g_ref = work
    rows = TILE_ROWS
    d_context = mul(do_ref[...], w_ref[:, 4 * LANES :]).astype(jnp.bfloat16)
    low = half_mask(rows, 0)

    def products_of(at, part, head):
        q_tile, k_tile, v_tile, q_half, v_half = HEADS[head]
        c_tile = 0 if head == 2 else 1
        keys = kv_ref[0, :, k_tile * LANES : (k_tile + 1) * LANES]
        values = kv_ref[0, :, v_tile * LANES : (v_tile + 1) * LANES]
        queries = scaled_queries(q_ref, at, q_tile, q_half)
        d_rows = jnp.where(half_mask(rows, v_half), tile_of(d_context[at], c_tile), 0).astype(jnp.bfloat16)
        total = l_ref[0, at, head : head + 1]
        scores = mul_nt(
            jnp.concatenate([queries, in_parts(qx_ref[at, :].astype(jnp.float32), -total)], axis=1),
            jnp.concatenate([keys, kx_ref[...]], axis=1),
        )
        if causal:
            scores = with_triangle(scores, tri_ref[...], part)
        return scores, mul_nt(d_rows, values), queries, d_rows, keys

    units = units_of(q_ref.shape[1], rows)
    ahead = products_of(*units[0])
    d_queries = []
    for index, (at, part, head) in enumerate(units):
        scores, d_probs, queries, d_rows, keys = ahead
        if index + 1 < len(units):
            ahead = products_of(*units[index + 1])
        _, k_tile, v_tile, _, _ = HEADS[head]
        probs = jnp.exp(scores)
        inner = jnp.sum(probs * d_probs, axis=1, keepdims=True)
        d_scores = (probs * (d_probs - inner)).astype(jnp.bfloat16)
        d_values = mul_tn(probs.astype(jnp.bfloat16), d_rows)
        d_keys = mul_tn(d_scores, queries)
        d_queries.append(mul(d_scores, keys) * 0.125)
        k_at = slice(k_tile * LANES, (k_tile + 1) * LANES)
        v_at = slice(v_tile * LANES, (v_tile + 1) * LANES)
        if part == 0 and head != 1:
            sum_ref[:, k_at] = d_keys
            sum_ref[:, v_at] = d_values
        else:
            sum_ref[:, k_at] += d_keys
            sum_ref[:, v_at] += d_values
        if head == len(HEADS) - 1:
            dq_ref[at, :LANES] = jnp.where(low, d_queries[0], d_queries[1]).astype(jnp.bfloat16)
            dq_ref[at, LANES:] = jnp.where(low, d_queries[2], 0).astype(jnp.bfloat16)
            d_queries = []
    dkv_ref[...] = sum_ref[...].astype(jnp.bfloat16)
    d_xq = mul_nt(dq_ref[...], w_ref[:, : 2 * LANES])
    d_xkv = mul_nt(dkv_ref[...], w_ref[:, LANES : 5 * LANES])

    grad_q = mul_tn(xq_ref[...], dq_ref[...])
    grad_kv = mul_tn(xkv_ref[...], dkv_ref[...])
    grad_o = mul_tn(do_ref[...], c_ref[0])
    g_ref[:, :LANES] = grad_q[:, :LANES].astype(jnp.bfloat16)
    g_ref[:, LANES : 2 * LANES] = (grad_q[:, LANES:] + grad_kv[:, :LANES]).astype(jnp.bfloat16)
    g_ref[:, 2 * LANES : 4 * LANES] = grad_kv[:, LANES : 3 * LANES].astype(jnp.bfloat16)
    g_ref[:, 4 * LANES : 5 * LANES] = (grad_kv[:, 3 * LANES :] + grad_o[:, :LANES]).astype(jnp.bfloat16)
    g_ref[:, 5 * LANES :] = grad_o[:, LANES:].astype(jnp.bfloat16)
    return d_xq, d_xkv


def attend_back_kernel(causal, flag_ref, do_ref, xq_ref, xkv_ref, own_ref, peer_ref, *refs):
    kept, (qx_ref, kx_ref, tri_ref, dxq_ref, dxkv_ref, keep_ref, send_ref, w_ref) = refs[:4], refs[4:12]
    work = refs[12:]
    assemble(flag_ref, [own_ref], [peer_ref], w_ref)
    d_xq, d_xkv = attend_back_block(
        causal, do_ref, xq_ref, xkv_ref, w_ref, qx_ref, kx_ref, tri_ref, kept, work
    )
    add_up(pl.program_id(0) == 0, dxq_ref, d_xq)
    add_up(pl.program_id(0) == 0, dxkv_ref, d_xkv)
    hand_out(flag_ref, work[3], keep_ref, send_ref)


def whole(shape):
    return pl.BlockSpec(shape, lambda j, flag: (0,) * len(shape))


def held(shape):
    return pl.BlockSpec(shape, lambda j, flag: (0,) * len(shape), pipeline_mode=pl.Buffered(1))


def per_block(shape, first=0, gate=1):
    return pl.BlockSpec((1,) + shape, lambda j, flag: (first + j * flag[gate],) + (0,) * len(shape))


shape = jax.ShapeDtypeStruct


def call(kernel, name, micros, moved, grid, in_specs, out_specs, out_shape, scratch, *operands):
    return pl.pallas_call(
        where_active(kernel),
        grid_spec=pltpu.PrefetchScalarGridSpec(
            num_scalar_prefetch=1,
            grid=(grid,),
            in_specs=in_specs,
            out_specs=out_specs,
            scratch_shapes=scratch,
        ),
        out_shape=out_shape,
        compiler_params=pltpu.CompilerParams(
            vmem_limit_bytes=VMEM_BYTES if name == "decoder" else SMALL_VMEM_BYTES
        ),
        cost_estimate=cost(micros, moved),
        name=name,
    )(*operands)


def cost(micros, moved):
    return pl.CostEstimate(flops=int(micros * 1.15e9), bytes_accessed=int(moved), transcendentals=0)


def attend(flag, xq, xkv, weights, extras, causal):
    rows, width = xq.shape
    keys = xkv.shape[0]
    blocks = weights[0].shape[0]
    return call(
        functools.partial(attend_kernel, causal),
        "attend_self" if causal else "attend_cross",
        20,
        24 * 2**20,
        blocks,
        [held((rows, width)), held((keys, width))]
        + [per_block(part.shape[1:]) for part in weights]
        + [held(extra.shape) for extra in extras],
        [
            whole((rows, width)),
            per_block((rows, 2 * LANES)),
            per_block((keys, 4 * LANES)),
            per_block((rows, 2 * LANES)),
            per_block((rows, LANES)),
        ],
        [
            shape((rows, width), jnp.float32),
            shape((blocks, rows, 2 * LANES), jnp.bfloat16),
            shape((blocks, keys, 4 * LANES), jnp.bfloat16),
            shape((blocks, rows, 2 * LANES), jnp.bfloat16),
            shape((blocks, rows, LANES), jnp.float32),
        ],
        [pltpu.VMEM((width, 6 * LANES), jnp.bfloat16)],
        flag,
        xq,
        xkv,
        *weights,
        *extras,
    )


def attend_back(flag, d_out, xq, xkv, weights, kept, extras, causal, first, count):
    rows, width = xq.shape
    keys = xkv.shape[0]
    return call(
        functools.partial(attend_back_kernel, causal),
        "attend_self_back" if causal else "attend_cross_back",
        10 * count,
        6 * 2**20 * count,
        count,
        [held((rows, width)), held((rows, width)), held((keys, width))]
        + [per_block(part.shape[1:], first) for part in weights]
        + [
            per_block((rows, 2 * LANES), first),
            per_block((keys, 4 * LANES), first),
            per_block((rows, 2 * LANES), first),
            per_block((rows, LANES), first),
        ]
        + [held(extra.shape) for extra in extras],
        [whole((rows, width)), whole((keys, width))] + [per_block(part.shape[1:]) for part in weights],
        [shape((rows, width), jnp.float32), shape((keys, width), jnp.float32)]
        + [shape((count,) + part.shape[1:], jnp.bfloat16) for part in weights],
        [
            pltpu.VMEM((width, 6 * LANES), jnp.bfloat16),
            pltpu.VMEM((keys, 4 * LANES), jnp.float32),
            pltpu.VMEM((rows, 2 * LANES), jnp.bfloat16),
            pltpu.VMEM((keys, 4 * LANES), jnp.bfloat16),
            pltpu.VMEM((width, 6 * LANES), jnp.bfloat16),
        ],
        flag,
        d_out,
        xq,
        xkv,
        *weights,
        *kept,
        *extras,
    )


def ffn_block(x_ref, w_ref, units, g_ref, slope_ref, first, out_ref):
    inner = mul(x_ref[...], w_ref[:, :units])
    spread = 0.5 * (1.0 + lax.erf(inner * (0.5**0.5)))
    bell = jnp.exp(-0.5 * inner * inner) * 0.3989422804014327
    active = (inner * spread).astype(jnp.bfloat16)
    g_ref[0] = active
    slope_ref[0] = (spread + inner * bell).astype(jnp.bfloat16)
    add_up(first, out_ref, mul_nt(active, w_ref[:, units:]))


def ffn_kernel(flag_ref, x_ref, *refs):
    own_refs, peer_refs = refs[:PARTS], refs[PARTS : 2 * PARTS]
    z_ref, g_ref, slope_ref, w_ref = refs[2 * PARTS :]
    assemble(flag_ref, own_refs, peer_refs, w_ref)
    ffn_block(x_ref, w_ref, own_refs[0].shape[2], g_ref, slope_ref, pl.program_id(0) == 0, z_ref)


def feed_blocks(feed, index):
    half, units = feed[0].shape[1], feed[0].shape[2] // 2
    return [
        pl.BlockSpec((1, half, units), lambda j, flag, side=side: (index(j, flag), 0, side))
        for _ in feed
        for side in (0, 1)
    ]


def feed_operands(feed):
    return [part for part in feed for _ in (0, 1)]


def ffn(flag, x, feed):
    rows, width = x.shape
    blocks, units = feed[0].shape[0], feed[0].shape[2] // 2
    return call(
        ffn_kernel,
        "ffn",
        12,
        rows * units * blocks * 16,
        blocks,
        [held((rows, width))] + feed_blocks(feed, lambda j, flag: j * flag[1]),
        [whole((rows, width)), per_block((rows, units)), per_block((rows, units))],
        [
            shape((rows, width), jnp.float32),
            shape((blocks, rows, units), jnp.bfloat16),
            shape((blocks, rows, units), jnp.bfloat16),
        ],
        [pltpu.VMEM((width, 2 * units), jnp.bfloat16)],
        flag,
        x,
        *feed_operands(feed),
    )


def ffn_back_block(dz_ref, w_ref, units, slope_ref, dh_ref, first, out_ref):
    d_active = mul(dz_ref[...], w_ref[:, units:])
    d_inner = (d_active * slope_ref[0].astype(jnp.float32)).astype(jnp.bfloat16)
    dh_ref[0] = d_inner
    add_up(first, out_ref, mul_nt(d_inner, w_ref[:, :units]))


def layer_norm(values, gain_row, bias_row):
    average = jnp.mean(values, axis=-1, keepdims=True)
    centered = values - average
    variance = jnp.mean(centered * centered, axis=-1, keepdims=True)
    return centered * lax.rsqrt(variance + NORM_EPS) * gain_row + bias_row


def norm_back(values, gain_row, bias_row, upstream):
    _, pullback = jax.vjp(layer_norm, values, gain_row, bias_row)
    return pullback(upstream)


def norm_parts(values):
    average = jnp.mean(values, axis=1, keepdims=True)
    centered = values - average
    scale = lax.rsqrt(jnp.mean(centered * centered, axis=1, keepdims=True) + NORM_EPS)
    return centered * scale, scale


def norm_gradients(values, gain_row, upstream):
    shaped, scale = norm_parts(values)
    inner = upstream * gain_row
    mean_inner = jnp.mean(inner, axis=1, keepdims=True)
    mean_product = jnp.mean(inner * shaped, axis=1, keepdims=True)
    d_values = scale * (inner - mean_inner - shaped * mean_product)
    d_gain = jnp.sum(upstream * shaped, axis=0, keepdims=True)
    return d_values, d_gain, jnp.sum(upstream, axis=0, keepdims=True)


def enc_out_back_kernel(
    flag_ref, arrived_ref, cot_ref, total_ref, norms_ref, d_dec_ref, enc_ref, dec_ref, *refs
):
    d_total_ref, dz_ref, sums_ref, keep_ref, send_ref, g_ref, left_t_ref = refs

    @pl.when(jnp.logical_and(pl.program_id(0) == 0, flag_ref[2] == 1))
    def _():
        upstream = arrived_ref[...].astype(jnp.float32) + cot_ref[...].astype(jnp.float32)
        d_total, sums_ref[0:1, :], sums_ref[1:2, :] = norm_gradients(total_ref[...], norms_ref[2:3, :], upstream)
        d_total_ref[...] = d_total
        dz_ref[...] = d_total.astype(jnp.bfloat16)

    @pl.when(jnp.logical_and(pl.program_id(0) == 0, flag_ref[2] == 0))
    def _():
        dz_ref[...] = d_dec_ref[...]

    @pl.when(pl.program_id(0) == 0)
    def _():
        left_t_ref[...] = dz_ref[...].T

    right = jnp.where(flag_ref[2] == 1, enc_ref[0], dec_ref[0])
    g_ref[...] = mul(left_t_ref[...], right).astype(jnp.bfloat16)
    hand_out(flag_ref, g_ref, keep_ref, send_ref)


def enc_out_back(flag, arrived, cot, total, norms, d_dec, enc_active, dec_active, feed):
    rows, width = cot.shape
    blocks, _, units = enc_active.shape
    like = shape((blocks, feed[0].shape[1], units), jnp.bfloat16)
    full = shape((rows, width), jnp.float32)
    return call(
        enc_out_back_kernel,
        "enc_out_back",
        9,
        rows * units * blocks * 8,
        blocks,
        [held(item.shape) for item in (arrived, cot, total, norms, d_dec)]
        + [per_block((rows, units), 0, 2), per_block((rows, units), 0, 3)],
        [whole((rows, width))] * 2 + [whole((8, width))] + [per_block(like.shape[1:])] * 2,
        [full, shape((rows, width), jnp.bfloat16), shape((8, width), jnp.float32)]
        + [like] * 2,
        [pltpu.VMEM((width, units), jnp.bfloat16), pltpu.VMEM((width, rows), jnp.bfloat16)],
        flag,
        arrived,
        cot,
        total,
        norms,
        d_dec,
        enc_active,
        dec_active,
    )


def enc_in_back_kernel(
    flag_ref, dz_ref, d_enc_ref, d_middle_ref, total_ref, gain_ref, middle_ref, crossed_ref, *refs
):
    first_own_ref, second_own_ref, first_peer_ref, second_peer_ref, slope_ref, dec_inner_ref, *refs = refs
    d_total_ref, d_low_ref, sums_ref, keep_ref, send_ref, w_ref, inner_ref, out_ref, g_ref, left_t_ref = refs
    step = pl.program_id(0)
    phase, at = step // 4, step % 4
    on_encoder = flag_ref[2] == 1

    @pl.when(jnp.logical_and(phase == 0, on_encoder))
    def _():
        assemble(flag_ref, [first_own_ref, second_own_ref], [first_peer_ref, second_peer_ref], w_ref)
        ffn_back_block(
            dz_ref, w_ref, first_own_ref.shape[2], slope_ref, inner_ref.at[pl.ds(at, 1)], at == 0, out_ref
        )

    @pl.when(step == 3)
    def _():
        upstream = jnp.where(on_encoder, d_enc_ref[...] + out_ref[...], d_middle_ref[...])
        d_total, sums_ref[0:1, :], sums_ref[1:2, :] = norm_gradients(total_ref[...], gain_ref[0:1, :], upstream)
        d_total_ref[...] = d_total
        d_low_ref[...] = d_total.astype(jnp.bfloat16)
        left_t_ref[...] = jnp.where(on_encoder, middle_ref[...], crossed_ref[...]).T

    @pl.when(phase == 1)
    def _():
        right = jnp.where(on_encoder, inner_ref[at], dec_inner_ref[0])
        g_ref[...] = mul(left_t_ref[...], right).astype(jnp.bfloat16)
        hand_out(flag_ref, g_ref, keep_ref, send_ref)


def enc_in_back(flag, dz, d_enc, d_middle, total, gain, middle, crossed, feed, slope, dec_inner):
    rows, width = dz.shape
    blocks, half, units = feed[0].shape[0], feed[0].shape[1], feed[0].shape[2] // 2
    full = shape((rows, width), jnp.float32)

    def at_step(of, low, high, gate):
        def index(j, flag):
            return (jnp.where(j < 4, j if low == "up" else low, j - 4 if high == "up" else high) * flag[gate],) + (
                0,
            ) * len(of)

        return pl.BlockSpec((1,) + of, index)

    return call(
        enc_in_back_kernel,
        "enc_in_back",
        19,
        rows * units * blocks * 20,
        8,
        [held(item.shape) for item in (dz, d_enc, d_middle, total, gain, middle, crossed)]
        + feed_blocks(feed, lambda j, flag: jnp.where(j < 4, j, 3) * flag[2])
        + [at_step((rows, units), "up", 3, 2), at_step((rows, units), 0, "up", 3)],
        [whole((rows, width))] * 2 + [whole((8, width))] + [at_step((half, units), 0, "up", 1)] * 2,
        [full, shape((rows, width), jnp.bfloat16), shape((8, width), jnp.float32)]
        + [shape((blocks, half, units), jnp.bfloat16)] * 2,
        [
            pltpu.VMEM((width, 2 * units), jnp.bfloat16),
            pltpu.VMEM((blocks, rows, units), jnp.bfloat16),
            pltpu.VMEM((rows, width), jnp.float32),
            pltpu.VMEM((width, units), jnp.bfloat16),
            pltpu.VMEM((width, rows), jnp.bfloat16),
        ],
        flag,
        dz,
        d_enc,
        d_middle,
        total,
        gain,
        middle,
        crossed,
        *feed_operands(feed),
        slope,
        dec_inner,
    )


def decoder_kernel(
    flag_ref,
    h1_ref,
    mem_a_ref,
    mem_b_ref,
    peer_a_ref,
    peer_b_ref,
    cot_ref,
    qx_ref,
    kx_ref,
    norms_ref,
    own_ref,
    peer_ref,
    first_own_ref,
    second_own_ref,
    first_peer_ref,
    second_peer_ref,
    decoded_ref,
    crossed_ref,
    d_dec_ref,
    d_middle_ref,
    mine_ref,
    other_ref,
    sums_ref,
    active_ref,
    inner_ref,
    keep_ref,
    send_ref,
    xq_ref,
    xkv_ref,
    wx_ref,
    wf_ref,
    q_ref,
    kv_ref,
    c_ref,
    l_ref,
    slope_ref,
    out_ref,
    total_ref,
    do_ref,
    dxkv_ref,
    *work,
):
    step = pl.program_id(0)
    phase, at = step // 4, step % 4
    first, last = at == 0, at == 3
    rows = h1_ref.shape[0]
    units = first_own_ref.shape[2]
    gain = [norms_ref[row : row + 1, :] for row in range(3)]
    bias = [norms_ref[3 + row : 4 + row, :] for row in range(3)]

    def kept(block):
        return tuple(ref.at[pl.ds(block, 1)] for ref in (q_ref, kv_ref, c_ref, l_ref))

    @pl.when(step == 0)
    def _():
        xq_ref[...] = h1_ref[...].astype(jnp.bfloat16)
        for part, ref in enumerate((mem_a_ref, mem_b_ref, peer_a_ref, peer_b_ref)):
            xkv_ref[part * rows // 2 : (part + 1) * rows // 2] = ref[...]

    @pl.when(jnp.logical_or(phase == 0, phase == 3))
    def _():
        assemble(flag_ref, [own_ref], [peer_ref], wx_ref)

    @pl.when(jnp.logical_or(phase == 1, phase == 2))
    def _():
        assemble(flag_ref, [first_own_ref, second_own_ref], [first_peer_ref, second_peer_ref], wf_ref)

    @pl.when(phase == 0)
    def _():
        add_up(first, out_ref, attend_block(False, xq_ref, xkv_ref, wx_ref, qx_ref, kx_ref, None, *kept(at)))

    @pl.when(jnp.logical_and(phase == 0, last))
    def _():
        total = h1_ref[...] + out_ref[...]
        total_ref[...] = total
        crossed = norm_parts(total)[0] * gain[1] + bias[1]
        mine_ref[...] = crossed
        crossed_ref[...] = crossed.astype(jnp.bfloat16)

    @pl.when(phase == 1)
    def _():
        ffn_block(crossed_ref, wf_ref, units, active_ref, slope_ref.at[pl.ds(at, 1)], first, out_ref)

    @pl.when(jnp.logical_and(phase == 1, last))
    def _():
        total = mine_ref[...] + out_ref[...]
        decoded_ref[...] = (norm_parts(total)[0] * gain[2] + bias[2]).astype(jnp.bfloat16)
        d_total, sums_ref[0:1, :], sums_ref[1:2, :] = norm_gradients(
            total, gain[2], cot_ref[...].astype(jnp.float32)
        )
        d_middle_ref[...] = d_total
        d_dec_ref[...] = d_total.astype(jnp.bfloat16)

    @pl.when(phase == 2)
    def _():
        ffn_back_block(d_dec_ref, wf_ref, units, slope_ref.at[pl.ds(3 - at, 1)], inner_ref, first, out_ref)

    @pl.when(jnp.logical_and(phase == 2, last))
    def _():
        d_total, sums_ref[2:3, :], sums_ref[3:4, :] = norm_gradients(
            total_ref[...], gain[1], d_middle_ref[...] + out_ref[...]
        )
        d_middle_ref[...] = d_total
        do_ref[...] = d_total.astype(jnp.bfloat16)

    @pl.when(phase == 3)
    def _():
        d_xq, d_xkv = attend_back_block(
            False, do_ref, xq_ref, xkv_ref, wx_ref, qx_ref, kx_ref, None, kept(3 - at), work
        )
        add_up(first, out_ref, d_xq)
        add_up(first, dxkv_ref, d_xkv)
        hand_out(flag_ref, work[3], keep_ref, send_ref)

    @pl.when(jnp.logical_and(phase == 3, last))
    def _():
        d_middle_ref[...] += out_ref[...]
        mine_ref[...] = dxkv_ref[:rows]
        other_ref[...] = dxkv_ref[rows:].astype(jnp.bfloat16)


def decoder(flag, h1, memory, cot, extras, norms, cross, feed):
    rows, width = h1.shape
    blocks, half, _ = cross[0].shape
    units = feed[0].shape[2] // 2
    keys = 2 * rows
    qx, kx = extras

    def at_step(of, in_phase):
        def index(j, flag):
            at = j % 4
            choice = [{"up": at, "down": 3 - at}.get(way, way) for way in in_phase]
            chosen = choice[3]
            for phase in (2, 1, 0):
                chosen = jnp.where(j // 4 == phase, choice[phase], chosen)
            return (chosen * flag[1],) + (0,) * len(of)

        return pl.BlockSpec((1,) + of, index)

    part = (half, cross[0].shape[2])
    full = shape((rows, width), jnp.float32)
    rounded = shape((rows, width), jnp.bfloat16)
    return call(
        decoder_kernel,
        "decoder",
        90,
        40 * 2**20,
        16,
        [held(item.shape) for item in (h1, *memory, cot, qx, kx, norms)]
        + [at_step(part, ("up", 3, 3, "down"))] * 2
        + feed_blocks(feed, lambda j, flag: at_step((half, units), (0, "up", "down", 0)).index_map(j, flag)[0]),
        [whole((rows, width))] * 6
        + [whole((8, width))]
        + [
            at_step((rows, units), (0, "up", 3, 3)),
            at_step((rows, units), (3, 3, "down", 0)),
            at_step(part, (3, 3, 3, "down")),
            at_step(part, (3, 3, 3, "down")),
        ],
        [rounded, rounded, rounded, full, full, rounded, shape((8, width), jnp.float32)]
        + [shape((blocks, rows, units), jnp.bfloat16)] * 2
        + [shape(cross[0].shape, jnp.bfloat16)] * 2,
        [
            pltpu.VMEM((rows, width), jnp.bfloat16),
            pltpu.VMEM((keys, width), jnp.bfloat16),
            pltpu.VMEM((width, 6 * LANES), jnp.bfloat16),
            pltpu.VMEM((width, 2 * units), jnp.bfloat16),
            pltpu.VMEM((blocks, rows, 2 * LANES), jnp.bfloat16),
            pltpu.VMEM((blocks, keys, 4 * LANES), jnp.bfloat16),
            pltpu.VMEM((blocks, rows, 2 * LANES), jnp.bfloat16),
            pltpu.VMEM((blocks, rows, LANES), jnp.float32),
            pltpu.VMEM((blocks, rows, units), jnp.bfloat16),
            pltpu.VMEM((rows, width), jnp.float32),
            pltpu.VMEM((rows, width), jnp.float32),
            pltpu.VMEM((rows, width), jnp.bfloat16),
            pltpu.VMEM((keys, width), jnp.float32),
            pltpu.VMEM((keys, 4 * LANES), jnp.float32),
            pltpu.VMEM((rows, 2 * LANES), jnp.bfloat16),
            pltpu.VMEM((keys, 4 * LANES), jnp.bfloat16),
            pltpu.VMEM((width, 6 * LANES), jnp.bfloat16),
        ],
        flag,
        h1,
        *memory,
        cot,
        qx,
        kx,
        norms,
        *cross,
        *feed_operands(feed),
    )


def low(values):
    return values.astype(jnp.bfloat16)


def axes_of(count):
    return ("section", "zh", "zl") + tuple("e%d" % at for at in range(count)) + ("ty", "tx")


def layer_of(place):
    return 1 ^ place["zh"] ^ place["zl"]


def moved(x, names, to):
    names = [name for name in axes_of(8) if name in names]

    def index(place):
        return sum(place[name] << (len(names) - 1 - at) for at, name in enumerate(names))

    pairs = []
    for source in range(2 ** len(names)):
        place = {name: source >> (len(names) - 1 - at) & 1 for at, name in enumerate(names)}
        target = to(place)
        if target is not None:
            pairs.append((source, index(target)))
    return lax.ppermute(x, tuple(names), pairs)


def over(x, *axes, layer=None):
    def to(place):
        if layer is not None and layer_of(place) != layer:
            return None
        return {**place, **{axis: 1 - place[axis] for axis in axes}}

    return moved(x, axes if layer is None else axes + Z, to)


Z = ("zh", "zl")


def swapped(x):
    def to(place):
        if place["section"] == layer_of(place):
            return place
        return {"section": 1 - place["section"], "zh": place["zh"], "zl": 1 - place["zl"]}

    return moved(x, ("section",) + Z, to)


def turned(x):
    return moved(x, ("section", "ty"), lambda place: {"section": place["ty"], "ty": place["section"]})


def sent_home(x, other):
    def to(place):
        return {
            "section": layer_of(place),
            "zh": place["zh"],
            "zl": 1 ^ place["zh"] ^ place["ty"],
            "ty": place["section"],
            "tx": place["tx"] ^ other,
        }

    return moved(x, ("section",) + Z + ("ty", "tx"), to)


def cross_in(x, layer):
    def to(place):
        if place["section"] != layer:
            return None
        return {"section": layer_of(place), "zh": place["zh"], "zl": place["zh"]}

    return moved(x, ("section",) + Z, to)


def cross_out(x, layer):
    def to(place):
        if layer_of(place) != 1:
            return None
        return {"section": layer, "zh": place["zh"], "zl": 1 ^ place["zh"] ^ place["section"]}

    return moved(x, ("section",) + Z, to)


def in_order(x, flag, axis):
    return jnp.where(flag == 1, jnp.flip(x, axis), x)


def pack_heads(query, key, value, out):
    pair = 2 * HDIM
    return jnp.concatenate(
        [
            query,
            value[:, pair:],
            key[:, :pair],
            value[:, :pair],
            key[:, pair:],
            out[:, pair:],
            out[:, :pair],
        ],
        axis=1,
    )


def unpack_heads(packed):
    part = [packed[:, at * HDIM : (at + 1) * HDIM] for at in range(12)]
    query = jnp.concatenate(part[0:3], axis=1)
    key = jnp.concatenate([part[4], part[5], part[8]], axis=1)
    value = jnp.concatenate([part[6], part[7], part[3]], axis=1)
    out = jnp.concatenate([part[10], part[11], part[9]], axis=1)
    return query, key, value, out


def after(x, *earlier):
    return lax.optimization_barrier((x,) + earlier)[0]


def plane_gathered(x, until=(), **only):
    parts = [x, over(x, "tx", **only), over(x, "ty", **only), over(x, "ty", "tx", **only)]
    return jnp.stack([after(part, *until) for part in parts])


def plane_summed(x, until=(), raw=None, **only):
    terms = [x[0], over(x[1], "tx", **only), over(x[2], "ty", **only), over(x[3], "ty", "tx", **only)]
    if raw is not None:
        raw.extend(terms[1:])
    terms = [after(term, *until) for term in terms]
    return low(sum(term.astype(jnp.float32) for term in terms))


def rows_gathered(x, count, until=(), raw=None, **only):
    for axes in [("e%d" % at,) for at in reversed(range(count))] + [Z]:
        got = over(x, *axes, **only)
        if raw is not None:
            raw.append(got)
        parts = [after(part, *until) for part in (x, got)]
        both = in_order(jnp.stack(parts, axis=-3), lax.axis_index(axes[0]), x.ndim - 2)
        x = both.reshape(x.shape[:-2] + (2 * x.shape[-2], x.shape[-1]))
    return x


def rows_summed(x, count, until=(), raw=None, **only):
    for axes in [Z] + [("e%d" % at,) for at in range(count)]:
        halves = x.reshape(x.shape[:-2] + (2, x.shape[-2] // 2, x.shape[-1]))
        halves = in_order(halves, lax.axis_index(axes[0]), x.ndim - 2)
        got = over(halves[..., 1, :, :], *axes, **only)
        if raw is not None:
            raw.append(got)
        x = plus(halves[..., 0, :, :], after(got, *until))
    return x


def plus(first, second):
    return low(first.astype(jnp.float32) + second.astype(jnp.float32))


def from_cores(keep, send, raw=None, **only):
    got = over(send, "section", **only)
    if raw is not None:
        raw.append(got)
    return plus(keep, got)


def body(
    count,
    hidden,
    cotangent,
    segments,
    sa_qkv,
    sa_out,
    cross_one,
    cross_two,
    ffn_in,
    ffn_out,
    norm_gain,
    norm_bias,
):
    core = lax.axis_index("section")
    x_at, y_at, zh_at, zl_at = (lax.axis_index(name) for name in ("tx", "ty", "zh", "zl"))
    layer = 1 ^ zh_at ^ zl_at
    on_encoder = layer == 0
    quarter = hidden.shape[3]
    enc_flag = jnp.stack([core, 1 - layer, 1 - layer, layer])
    dec_flag = jnp.stack([core, layer, 1 - layer, layer])
    flag = jnp.stack([core, jnp.ones_like(core), 1 - layer, layer])

    def pick(first, second):
        return jnp.where(on_encoder, first, second)

    def of_one_row(x):
        both = in_order(x[0, :, 0], x_at, 0)
        return in_order(jnp.stack([both[0], over(both[1], "tx")]), x_at, 0).reshape(2 * quarter, -1)

    def rows_out(x, raw=None):
        mine, other = in_order(x.reshape(2, quarter, -1), x_at, 0)
        both = [sent_home(mine, 0), sent_home(other, 1)]
        if raw is not None:
            raw.extend(both)
        return in_order(jnp.stack(both), x_at, 0)[None, :, None]

    units = ffn_in.shape[2]
    width = cross_one.shape[2]
    packed_self = pack_heads(sa_qkv[0, :, 0], sa_qkv[0, :, 1], sa_qkv[0, :, 2], sa_out[0])
    packed_ffn = jnp.concatenate([ffn_in[0], ffn_out[0].T], axis=1)
    with jax.named_scope("norms_in"):
        norms = swapped(jnp.concatenate([norm_gain[0], norm_bias[0]], axis=0))
        gains, biases = norms[:3], norms[3:]
        seg_own = segments[:, :, 0].astype(jnp.float32)
        seg_here = jnp.where(zl_at == 1 ^ zh_at ^ y_at, seg_own, over(seg_own, "zl")).astype(jnp.int32)
    with jax.named_scope("hidden_in"):
        one_row = of_one_row(jnp.concatenate([hidden, cotangent], axis=-1))
    with jax.named_scope("self_weights"):
        shard_self = swapped(packed_self)
    with jax.named_scope("hidden_in"):
        one_row = swapped(after(one_row, shard_self))
    with jax.named_scope("ffn_weights"):
        shard_ffn = swapped(after(packed_ffn, one_row))

    def both_rows(x):
        for_enc = rows_gathered(x, count, layer=0)
        return pick(for_enc, rows_gathered(after(x, for_enc), count, layer=1))

    with jax.named_scope("self_weights"):
        rows_self = both_rows(shard_self)
        raw_ffn_rows = []
        rows_ffn_enc = rows_gathered(after(shard_ffn, rows_self), count, raw=raw_ffn_rows, layer=0)
        own_self = plane_gathered(rows_self, until=tuple(raw_ffn_rows))
        w_self = [own_self, over(own_self, "section")]
    with jax.named_scope("hidden_in"):
        rows_here = turned(one_row)
        rows_here, cot = rows_here[:, : hidden.shape[-1]], rows_here[:, hidden.shape[-1] :]
        rows_all = jnp.concatenate([rows_here, over(rows_here, "section")], axis=0)
    with jax.named_scope("cross_weights"):
        cross_low = after(jnp.concatenate([cross_one[0], cross_two[0]], axis=1), own_self)
        pair_kv, pair_qo = cross_in(cross_low, 0), cross_in(cross_low, 1)
        packed = pack_heads(pair_qo[:, :width], pair_kv[:, :width], pair_kv[:, width:], pair_qo[:, width:])
    with jax.named_scope("ffn_weights"):
        rows_ffn = pick(rows_ffn_enc, rows_gathered(after(shard_ffn, *raw_ffn_rows), count, layer=1))

    both_segments = in_order(seg_here, x_at, 1)[:, 0]
    ordered = in_order(both_segments.reshape(2, 2, 2 * quarter), core, 1).reshape(2, 4 * quarter)
    source_seg, target_seg = ordered[0], ordered[1]
    self_seg = pick(source_seg, target_seg)
    parts = jnp.arange(4)
    quarter_of = jnp.repeat(2 * ((parts // 2) ^ core) + parts % 2, quarter)
    lanes = jnp.arange(LANES)[None, :]

    def key_extras(seg):
        differs = jnp.logical_and(lanes < SEG_LANES, seg[:, None] != lanes)
        later = jnp.logical_and(
            jnp.logical_and(lanes >= SEG_LANES, lanes < PART_LANE),
            quarter_of[:, None] > lanes - SEG_LANES,
        )
        part = jnp.logical_and(lanes >= PART_LANE, lanes < PART_LANE + 3)
        return jnp.where(differs | later | part, 1.0, 0.0).astype(jnp.bfloat16)

    def query_extras(seg, causal):
        seg, at = seg[: 2 * quarter], quarter_of[: 2 * quarter]
        same = seg[:, None] == lanes
        here = jnp.logical_and(at[:, None] + SEG_LANES == lanes, causal)
        return jnp.where(same | here, MASKED, 0.0).astype(jnp.bfloat16)

    at_row = jnp.arange(quarter)
    later_key = jnp.logical_and(at_row[None, :] > at_row[:, None], jnp.logical_not(on_encoder))
    tri = jnp.where(later_key, MASKED, 0.0).astype(jnp.float32)
    self_extras = (query_extras(self_seg, jnp.logical_not(on_encoder)), key_extras(self_seg), tri)
    cross_extras = (query_extras(target_seg, False), key_extras(source_seg), tri)

    start = rows_all.astype(jnp.float32)
    start = pick(layer_norm(start, gains[0], biases[0]), start)
    start_here = start[: 2 * quarter]
    start_low = low(start)
    self_gain, self_bias = pick(gains[1], gains[0]), pick(biases[1], biases[0])
    raw_cross_rows = []
    with jax.named_scope("cross_weights"):
        rows_cross = rows_gathered(after(packed, rows_ffn), count, raw=raw_cross_rows, layer=1)
    self_out, *kept_self = attend(
        flag, start_low[: 2 * quarter], start_low, w_self, self_extras, True
    )
    with jax.named_scope("ffn_weights"):
        own_ffn = plane_gathered(after(rows_ffn, own_self), until=(self_out, *raw_cross_rows))
        feed = [own_ffn, over(own_ffn, "section")]
    self_total = start_here + after(self_out, *raw_cross_rows)
    middle = layer_norm(self_total, self_gain, self_bias)
    middle_low = low(middle)

    enc_out, enc_active, enc_slope = ffn(enc_flag, middle_low, feed)
    enc_total = middle + enc_out
    encoded = low(layer_norm(enc_total, gains[2], biases[2]))
    def across(x, layer):
        return moved(x, Z, lambda place: {**place, "zl": 1 - place["zl"]} if layer_of(place) == layer else None)

    with jax.named_scope("memory"):
        memory_here = [across(encoded[:quarter], 0), across(encoded[quarter:], 0)]
        memory_peer = [over(part, "section", layer=1) for part in memory_here]
    with jax.named_scope("cross_weights"):
        own_cross = plane_gathered(after(rows_cross, feed[1]), until=tuple(memory_here), layer=1)
        w_cross = [own_cross, over(own_cross, "section", layer=1)]
    (
        decoded,
        crossed_low,
        d_dec_low,
        d_middle_dec,
        d_memory_here,
        d_memory_other,
        dec_sums,
        dec_active,
        dec_inner,
        cross_keep,
        cross_send,
    ) = decoder(
        dec_flag, middle, memory_here + memory_peer, cot, cross_extras[:2], norms, w_cross, feed
    )
    with jax.named_scope("d_memory"):
        d_memory_here = d_memory_here + over(d_memory_other, "section", layer=1).astype(jnp.float32)
        d_memory_low = low(d_memory_here)
        arrived = across(d_memory_low, 1)
    with jax.named_scope("cross_sums"):
        cross_sum = from_cores(after(cross_keep, arrived), after(cross_send, arrived), layer=1)
        raw_cross = []
        cross_plane = plane_summed(cross_sum, raw=raw_cross, layer=1)

    raw_hidden = []
    with jax.named_scope("hidden_out"):
        hidden_out = rows_out(after(pick(encoded, decoded), arrived), raw_hidden)

    d_enc_total, dz_low, enc_sums, second_keep, second_send = enc_out_back(
        flag, arrived, cot, enc_total, norms, d_dec_low, enc_active, dec_active, feed
    )
    with jax.named_scope("ffn_sums"):
        raw_second_sum = []
        second_sum = from_cores(
            after(second_keep, *raw_hidden), after(second_send, *raw_hidden), raw=raw_second_sum
        )
    gain_row = jnp.broadcast_to(self_gain, (8, self_gain.shape[0]))
    d_self_total, d_self_low, self_norm, first_keep, first_send = enc_in_back(
        flag,
        after(dz_low, second_keep, cross_sum),
        d_enc_total,
        d_middle_dec,
        self_total,
        gain_row,
        middle_low,
        crossed_low,
        feed,
        enc_slope,
        dec_inner,
    )
    with jax.named_scope("ffn_sums"):
        gate = []
        second_plane = plane_summed(after(second_sum, d_self_low), raw=gate)
        first_sum = from_cores(after(first_keep, *raw_cross), after(first_send, *raw_cross), raw=gate)

    halves = []
    for first, earlier in ((0, ()), (2, gate)):
        halves.append(
            attend_back(
                flag,
                after(d_self_low, *earlier),
                start_low[: 2 * quarter],
                start_low,
                w_self,
                kept_self,
                self_extras,
                True,
                first,
                2,
            )
        )
    d_start_q = halves[0][0] + halves[1][0]
    with jax.named_scope("cross_sums"):
        share_cross = rows_summed(after(cross_plane, d_start_q), count, layer=1)
    with jax.named_scope("ffn_sums"):
        gate_later = []
        first_plane = plane_summed(after(first_sum, second_plane), raw=gate_later)
        second_share = rows_summed(second_plane, count, raw=gate_later)
    with jax.named_scope("self_sums"):
        (_, _, keep, send), (_, _, *later) = halves
        self_sum = [from_cores(after(keep, *gate), after(send, *gate), raw=gate_later)]
        raw_later = []
        self_sum.append(from_cores(*(after(part, *gate_later) for part in later), raw=raw_later))
        self_sum = jnp.concatenate(self_sum, axis=0)
    with jax.named_scope("d_start"):
        d_start_kv = after(halves[0][1], *raw_later) + halves[1][1]
        d_start = d_self_total + d_start_q + d_start_kv[: 2 * quarter]
        d_start = d_start + over(low(d_start_kv[2 * quarter :]), "section").astype(jnp.float32)
    d_source, gain_a, bias_a = norm_back(
        rows_here.astype(jnp.float32), gains[0], biases[0], d_start
    )

    rows_from = jnp.concatenate([enc_sums, self_norm, dec_sums, jnp.stack([gain_a, bias_a])], axis=0)
    enc_rows, dec_rows = jnp.array([24, 8, 0, 25, 9, 1]), jnp.array([8, 18, 16, 9, 19, 17])
    wanted = pick(enc_rows, dec_rows)[:, None] == jnp.arange(26)
    norm_sums = jnp.sum(jnp.where(wanted[:, :, None], rows_from[None], 0.0), axis=1)
    shards = 2**count
    sides = jnp.arange(2)
    held, outer = core ^ sides[:, None], sides[None, :]
    row_block = ((2 * outer + (1 ^ outer ^ held)) * shards)[:, :, None] + jnp.arange(shards)
    column_block = (2 * (y_at ^ sides)[:, None] + (x_at ^ sides)[None, :]).reshape(-1)
    order = (row_block.reshape(2, -1)[:, None, :] + 0) * 4 + column_block[:, None]
    norm_sums = jnp.take(norm_sums.reshape(6, 8 * 2 * shards, -1), order.reshape(-1), axis=1)
    norm_sums = norm_sums.reshape(6, 2, 4, 2 * shards, -1)
    with jax.named_scope("norm_sums"):
        norm_got = over(norm_sums[:, 1], "section")
        norm_sums = norm_sums[:, 0] + norm_got
    with jax.named_scope("self_sums"):
        self_plane = plane_summed(self_sum, until=(norm_got,))
    with jax.named_scope("norm_sums"):
        norm_blocks = after(norm_sums.transpose(1, 2, 0, 3).reshape(4, 2 * shards, -1), self_plane)
        norm_plane = norm_blocks[0] + over(norm_blocks[1], "tx") + over(norm_blocks[2], "ty")
        norm_plane = norm_plane + over(norm_blocks[3], "ty", "tx")
    norm_width = norm_plane.shape[1]
    with jax.named_scope("self_sums"):
        pad = ((0, 0), (0, 15), (0, self_plane.shape[1] - norm_width))
        both = jnp.concatenate(
            [
                self_plane.reshape(2 * shards, -1, self_plane.shape[1]),
                jnp.pad(low(norm_plane)[:, None], pad),
            ],
            axis=1,
        )
        raw_self = []
        share_self = rows_summed(both.reshape(-1, self_plane.shape[1]), count, raw=raw_self)
        share_self = swapped(share_self).astype(jnp.float32)
    norm_shares = share_self[-16, :norm_width].reshape(6, -1)
    share_self = share_self[:-16]
    with jax.named_scope("ffn_sums"):
        first_share = rows_summed(after(first_plane, *raw_later), count)
        share_ffn = swapped(jnp.concatenate([first_share, second_share], axis=1)).astype(jnp.float32)
    share_first, share_second = share_ffn[:, :units], share_ffn[:, units:].T
    with jax.named_scope("hidden_grad"):
        hidden_grad = rows_out(after(low(pick(d_source, d_start)), *raw_self)).astype(jnp.float32)
    g_query, g_key, g_value, g_out = unpack_heads(share_self)
    grad_qkv = jnp.stack([g_query, g_key, g_value], axis=1)
    c_query, c_key, c_value, c_out = unpack_heads(share_cross)
    with jax.named_scope("cross_out"):
        for_enc = cross_out(jnp.concatenate([c_key, c_value], axis=1), 0)
        for_dec = cross_out(jnp.concatenate([c_query, c_out], axis=1), 1)
    cross = jnp.where(core == 0, for_enc, for_dec).astype(jnp.float32)

    return (
        hidden_out,
        hidden_grad,
        grad_qkv[None],
        g_out[None],
        cross[None, :, :width],
        cross[None, :, width:],
        share_first[None],
        share_second[None],
        norm_shares[None, :3],
        norm_shares[None, 3:],
    )


def solution(mesh):
    _, dp_count, _ = mesh.devices.shape
    count = dp_count.bit_length() - 3
    names = axes_of(count)
    dp, tensor = names[1:-2], names[-2:]
    split = Mesh(mesh.devices.reshape((2,) * len(names)), names)
    rows = P("section", None, dp, tensor, None)
    in_specs = (
        rows,
        rows,
        P(None, None, dp, None),
        P("section", dp, None, tensor),
        P("section", dp, tensor),
        P("section", dp, tensor),
        P("section", dp, tensor),
        P("section", dp, tensor),
        P("section", tensor, dp),
        P("section", None, None),
        P("section", None, None),
    )
    out_specs = (
        rows,
        rows,
        P("section", dp, None, tensor),
        P("section", dp, tensor),
        P("section", dp, tensor),
        P("section", dp, tensor),
        P("section", dp, tensor),
        P("section", tensor, dp),
        P("section", None, dp + tensor),
        P("section", None, dp + tensor),
    )
    return jax.shard_map(
        functools.partial(body, count), mesh=split, in_specs=in_specs, out_specs=out_specs, check_vma=False
    )
```
